32 devices in a mesh: dp: 8 (over z, x), rep: 4 (over y, core).
Axes of the slice: x: 2, y: 2, z: 4, core: 2. Of those that a mesh axis runs over, the one named last changes fastest.
Arguments:
- images: bfloat16 [128, 14, 14, 1024], P(('dp', 'rep')), may hold values from -18 to 18, as said below
- out_grad: bfloat16 [128, 14, 14, 1024], P(('dp', 'rep')), may hold values from -18 to 18, as said below
- reduce_weight: float32 [1024, 256], P('dp'), may hold values from -0.1875 to 0.1875
- reduce_moment: float32 [1024, 256], P('dp'), may hold values from -224 to 224
- reduce_second: float32 [1024, 256], P('dp'), may hold values from 100.352 to 401.408
- conv_weight: float32 [2304, 256], P('dp'), may hold values from -0.1875 to 0.1875
- conv_moment: float32 [2304, 256], P('dp'), may hold values from -128 to 128
- conv_second: float32 [2304, 256], P('dp'), may hold values from 50.176 to 200.704
- squeeze_weight: float32 [256, 128], P('dp'), may hold values from -0.375 to 0.375
- squeeze_moment: float32 [256, 128], P('dp'), may hold values from -56 to 56
- squeeze_second: float32 [256, 128], P('dp'), may hold values from 6.272 to 25.088
- expand_weight: float32 [128, 512], P('dp'), may hold values from -1.5 to 1.5
- expand_moment: float32 [128, 512], P('dp'), may hold values from -56 to 56
- expand_second: float32 [128, 512], P('dp'), may hold values from 6.272 to 25.088
- project_weight: float32 [256, 1024], P('dp'), may hold values from -0.375 to 0.375
- project_moment: float32 [256, 1024], P('dp'), may hold values from -112 to 112
- project_second: float32 [256, 1024], P('dp'), may hold values from 30.1056 to 120.4224
- norm_params: float32 [4352], P('dp'), may hold values from -0.5 to 1.4, as said below
- norm_moment: float32 [4352], P('dp'), may hold values from -128 to 128
- norm_second: float32 [4352], P('dp'), may hold values from 35.1232 to 145.5104
Outputs:
- block_out: bfloat16 [128, 14, 14, 1024], P(('dp', 'rep'))
- images_grad: float32 [128, 14, 14, 1024], P(('dp', 'rep'))
- new_reduce_weight: float32 [1024, 256], P('dp')
- new_reduce_moment: float32 [1024, 256], P('dp')
- new_reduce_second: float32 [1024, 256], P('dp')
- new_conv_weight: float32 [2304, 256], P('dp')
- new_conv_moment: float32 [2304, 256], P('dp')
- new_conv_second: float32 [2304, 256], P('dp')
- new_squeeze_weight: float32 [256, 128], P('dp')
- new_squeeze_moment: float32 [256, 128], P('dp')
- new_squeeze_second: float32 [256, 128], P('dp')
- new_expand_weight: float32 [128, 512], P('dp')
- new_expand_moment: float32 [128, 512], P('dp')
- new_expand_second: float32 [128, 512], P('dp')
- new_project_weight: float32 [256, 1024], P('dp')
- new_project_moment: float32 [256, 1024], P('dp')
- new_project_second: float32 [256, 1024], P('dp')
- new_norm_params: float32 [4352], P('dp')
- new_norm_moment: float32 [4352], P('dp')
- new_norm_second: float32 [4352], P('dp')
The draws below stay inside these ranges and needn't reach their ends.
Inputs may be any that keep to these rules, and one draw needn't show every extreme that they name: `images`: entries drawn independently. `out_grad`: entries drawn independently. `norm_params`: gains lie near one, biases near zero.
All inputs are finite; a program needn't handle non-finite values.
Results may differ from the reference program's by a relative error of at most 0.0055.
The reference program's roundings to bfloat16 on the way (of `active` and `mixed`) count: a program that leaves them out, or rounds other values in their place, can miss the bound.
Values may be sent and summed in bfloat16 or wider, within the bound.
A program may use at most 128 MiB of HBM per device.

```python
import math
import jax
import jax.numpy as jnp
from jax import lax

CHANNELS = 1024
BOTTLE = 256
INNER = 128
RADIX = 2
SIDE = 14
MICRO = 2
STEP = 10
IMG_DEV = 4
IMAGES = 128
PIXELS = 25088
NORM_TOTAL = 4352
N_DP = 8
N_REP = 4


def device_ramp(base):
    owner = jnp.arange(IMAGES) // IMG_DEV
    along_dp = (owner // N_REP).astype(jnp.float32) / max(N_DP - 1, 1)
    along_rep = (owner % N_REP).astype(jnp.float32) / max(N_REP - 1, 1)
    return jnp.power(jnp.float32(base), 0.5 * (along_dp + along_rep))


def draw_images(key, part):
    key = jax.random.fold_in(key, 3)
    shape = (IMAGES, SIDE, SIDE, CHANNELS)
    values = jnp.clip(jax.random.normal(key, shape, jnp.float32), -6.0, 6.0) * device_ramp(3.0)[:, None, None, None]
    return values.astype(jnp.bfloat16)


def draw_out_grad(key, part):
    key = jax.random.fold_in(key, 4)
    shape = (IMAGES, SIDE, SIDE, CHANNELS)
    values = jnp.clip(jax.random.normal(key, shape, jnp.float32), -6.0, 6.0) * device_ramp(3.0)[:, None, None, None]
    return values.astype(jnp.bfloat16)


def draw_norm_params(key, part):
    key = jax.random.fold_in(key, 5)
    widths = (BOTTLE, BOTTLE, RADIX * BOTTLE, RADIX * BOTTLE, INNER, INNER, RADIX * BOTTLE, CHANNELS, CHANNELS)
    kinds = (1.0, 0.0, 1.0, 0.0, 1.0, 0.0, 0.0, 1.0, 0.0)
    is_gain = jnp.concatenate([jnp.full((segment,), flavor, jnp.float32) for segment, flavor in zip(widths, kinds)])
    values = jax.random.uniform(key, (NORM_TOTAL,), jnp.float32, -1.0, 1.0)
    return is_gain * (1.0 + 0.4 * values) + (1.0 - is_gain) * (0.5 * values)


def block_scale(rng, extent, cuts, least, high):
    def one(position, shards_of):
        draws = jax.random.uniform(jax.random.fold_in(jax.random.fold_in(rng, 6), position), (shards_of,), jnp.float32, least / len(cuts), high / len(cuts))
        return jnp.repeat(jnp.exp(draws), extent[position] // shards_of).reshape((-1,) + (1,) * (len(extent) - position - 1))

    level = one(*cuts[0])
    for cut in cuts[1:]:
        level = level * one(*cut)
    return level


def noise(rng, extent, scale, most, cuts=(), held_as=jnp.bfloat16):
    entries = scale * jax.random.normal(rng, extent, jnp.float32)
    if cuts:
        entries = entries * block_scale(rng, extent, cuts, -0.22, 0.18)
    return jnp.clip(entries, -most, most).astype(held_as)


def setup_inputs(seed: int = 0) -> dict:
    key_of = jax.random.split(jax.random.key(seed), 21)
    return {
        "images": draw_images(jax.random.fold_in(key_of[20], 71), 0),
        "out_grad": draw_out_grad(jax.random.fold_in(key_of[20], 71), 0),
        "reduce_weight": noise(key_of[2], (CHANNELS, BOTTLE), CHANNELS ** -0.5, 0.1875, ((0, 8),), jnp.float32),
        "reduce_moment": noise(key_of[3], (CHANNELS, BOTTLE), (0.22 * PIXELS ** 0.5), 224.0, ((0, 8),), jnp.float32),
        "reduce_second": jnp.clip(jnp.exp(math.log(401.408) - 1.3862944 * jax.random.uniform(key_of[4], (CHANNELS, BOTTLE), jnp.float32) ** block_scale(key_of[4], (CHANNELS, BOTTLE), ((0, 8),), -0.2, 0.2)), 100.352, 401.408),
        "conv_weight": noise(key_of[5], (9 * BOTTLE, BOTTLE), (9 * BOTTLE // RADIX) ** -0.5, 0.1875, ((0, 8),), jnp.float32),
        "conv_moment": noise(key_of[6], (9 * BOTTLE, BOTTLE), (0.155 * PIXELS ** 0.5), 128.0, ((0, 8),), jnp.float32),
        "conv_second": jnp.clip(jnp.exp(math.log(200.704) - 1.3862944 * jax.random.uniform(key_of[7], (9 * BOTTLE, BOTTLE), jnp.float32) ** block_scale(key_of[7], (9 * BOTTLE, BOTTLE), ((0, 8),), -0.2, 0.2)), 50.176, 200.704),
        "squeeze_weight": noise(key_of[8], (BOTTLE, INNER), BOTTLE ** -0.5, 0.375, ((0, 8),), jnp.float32),
        "squeeze_moment": noise(key_of[9], (BOTTLE, INNER), (0.055 * PIXELS ** 0.5), 56.0, ((0, 8),), jnp.float32),
        "squeeze_second": jnp.clip(jnp.exp(math.log(25.088) - 1.3862944 * jax.random.uniform(key_of[10], (BOTTLE, INNER), jnp.float32) ** block_scale(key_of[10], (BOTTLE, INNER), ((0, 8),), -0.2, 0.2)), 6.272, 25.088),
        "expand_weight": noise(key_of[11], (INNER, RADIX * BOTTLE), (INNER // 8) ** -0.5, 1.5, ((0, 8),), jnp.float32),
        "expand_moment": noise(key_of[12], (INNER, RADIX * BOTTLE), (0.055 * PIXELS ** 0.5), 56.0, ((0, 8),), jnp.float32),
        "expand_second": jnp.clip(jnp.exp(math.log(25.088) - 1.3862944 * jax.random.uniform(key_of[13], (INNER, RADIX * BOTTLE), jnp.float32) ** block_scale(key_of[13], (INNER, RADIX * BOTTLE), ((0, 8),), -0.2, 0.2)), 6.272, 25.088),
        "project_weight": noise(key_of[14], (BOTTLE, CHANNELS), BOTTLE ** -0.5, 0.375, ((0, 8),), jnp.float32),
        "project_moment": noise(key_of[15], (BOTTLE, CHANNELS), (0.12 * PIXELS ** 0.5), 112.0, ((0, 8),), jnp.float32),
        "project_second": jnp.clip(jnp.exp(math.log(120.4224) - 1.3862944 * jax.random.uniform(key_of[16], (BOTTLE, CHANNELS), jnp.float32) ** block_scale(key_of[16], (BOTTLE, CHANNELS), ((0, 8),), -0.2, 0.2)), 30.1056, 120.4224),
        "norm_params": draw_norm_params(jax.random.fold_in(key_of[20], 71), 0),
        "norm_moment": noise(key_of[18], (NORM_TOTAL,), (0.13 * PIXELS ** 0.5), 128.0, ((0, 8),), jnp.float32),
        "norm_second": jnp.clip(jnp.exp(math.log(145.5104) - 1.42138574 * jax.random.uniform(key_of[19], (NORM_TOTAL,), jnp.float32) ** block_scale(key_of[19], (NORM_TOTAL,), ((0, 8),), -0.2, 0.2)), 35.1232, 145.5104),
    }


EPSILON = 1e-05
PRECISE = lax.Precision.HIGHEST
BETA_ONE = 0.9
BETA_TWO = 0.999
ADAM_EPSILON = 1e-08
DECAY = 0.01
NORM_RATE = 0.8

@jax.custom_vjp
def low(v):
    return lax.optimization_barrier(v.astype(jnp.bfloat16)).astype(jnp.float32)

@jax.custom_vjp
def low_back(v):
    return v

def low_keep(v):
    return (low(v), None)

def low_pass(kept, grad):
    return (grad,)

def back_keep(v):
    return (v, None)

def back_low(kept, grad):
    return (low(grad),)
low.defvjp(low_keep, low_pass)
low_back.defvjp(back_keep, back_low)

def split_params(packed):
    widths = (BOTTLE, BOTTLE, RADIX * BOTTLE, RADIX * BOTTLE, INNER, INNER, RADIX * BOTTLE, CHANNELS, CHANNELS)
    pieces = []
    offset = 0
    for segment in widths:
        pieces.append(lax.slice_in_dim(packed, offset, offset + segment))
        offset = offset + segment
    return pieces

def normalize(values, gain, bias):
    reduce_axes = tuple(range(values.ndim - 1))
    center = lax.optimization_barrier(jnp.mean(values, axis=reduce_axes))
    spread = lax.optimization_barrier(jnp.mean(values * values, axis=reduce_axes)) - center * center
    return (values - center) * lax.rsqrt(spread + EPSILON) * gain + bias

def grouped_conv(active, kernel):
    filters = kernel.reshape(RADIX, 3, 3, BOTTLE // RADIX, BOTTLE).transpose(1, 2, 3, 0, 4)
    filters = filters.reshape(3, 3, BOTTLE // RADIX, RADIX * BOTTLE)
    return lax.conv_general_dilated(active, filters, (1, 1), ((1, 1), (1, 1)), dimension_numbers=('NHWC', 'HWIO', 'NHWC'), feature_group_count=RADIX, precision=PRECISE)

def micro_forward(batched, weights):
    first, conv, squeeze, expand, last, packed = weights
    gain_one, bias_one, gain_two, bias_two, gain_pool, bias_pool, bias_expand, gain_three, bias_three = split_params(packed)
    count = batched.shape[0]
    reduced = low_back(jnp.einsum('nhwc,cb->nhwb', batched, first, precision=PRECISE))
    active = low(jax.nn.silu(normalize(reduced, gain_one, bias_one)))
    widened = low_back(grouped_conv(active, conv))
    splits = jax.nn.silu(normalize(widened, gain_two, bias_two)).reshape(count, SIDE, SIDE, RADIX, BOTTLE)
    pooled = lax.optimization_barrier(jnp.mean(lax.optimization_barrier(jnp.sum(splits, axis=3)), axis=(1, 2)))
    hidden = jax.nn.silu(normalize(jnp.dot(pooled, squeeze, precision=PRECISE), gain_pool, bias_pool))
    logits = (jnp.dot(hidden, expand, precision=PRECISE) + bias_expand).reshape(count, RADIX, BOTTLE)
    attention = jax.nn.softmax(logits, axis=1)
    mixed = low(lax.optimization_barrier(jnp.sum(splits * attention[:, None, None], axis=3)))
    projected = low_back(jnp.einsum('nhwb,bc->nhwc', mixed, last, precision=PRECISE))
    return jax.nn.silu(batched + normalize(projected, gain_three, bias_three))

def forward(images_full, first, conv, squeeze, expand, last, packed):
    weights = (low(first), low(conv), low(squeeze), low(expand), low(last), low(packed))
    owners = IMAGES // IMG_DEV
    per_batch = IMG_DEV // MICRO
    grouped = images_full.reshape(owners, MICRO, per_batch, SIDE, SIDE, CHANNELS)
    outputs = []
    for number in range(MICRO):
        batched = grouped[:, number].reshape(owners * per_batch, SIDE, SIDE, CHANNELS)
        result = jax.checkpoint(micro_forward)(batched, weights)
        outputs.append(result.reshape(owners, 1, per_batch, SIDE, SIDE, CHANNELS))
    return jnp.concatenate(outputs, axis=1).reshape(IMAGES, SIDE, SIDE, CHANNELS)

def adamw(param, moment, second, gradient, rate, decay):
    moment_new = BETA_ONE * moment + (1.0 - BETA_ONE) * gradient
    second_new = BETA_TWO * second + (1.0 - BETA_TWO) * gradient * gradient
    ratio = moment_new / (1.0 - BETA_ONE ** STEP) / (jnp.sqrt(second_new / (1.0 - BETA_TWO ** STEP)) + ADAM_EPSILON)
    return (param - rate * (ratio + decay * param), moment_new, second_new)

def reference(images, out_grad, reduce_weight, reduce_moment, reduce_second, conv_weight, conv_moment, conv_second, squeeze_weight, squeeze_moment, squeeze_second, expand_weight, expand_moment, expand_second, project_weight, project_moment, project_second, norm_params, norm_moment, norm_second):
    result, pullback = jax.vjp(forward, images.astype(jnp.float32), reduce_weight, conv_weight, squeeze_weight, expand_weight, project_weight, norm_params)
    gradients = pullback(out_grad.astype(jnp.float32))
    reduce_new = adamw(reduce_weight, reduce_moment, reduce_second, gradients[1], 2.0 * CHANNELS ** (-0.5), DECAY)
    conv_new = adamw(conv_weight, conv_moment, conv_second, gradients[2], 2.0 * (9 * BOTTLE // RADIX) ** (-0.5), DECAY)
    squeeze_new = adamw(squeeze_weight, squeeze_moment, squeeze_second, gradients[3], 2.0 * BOTTLE ** (-0.5), DECAY)
    expand_new = adamw(expand_weight, expand_moment, expand_second, gradients[4], 2.0 * (INNER // 8) ** (-0.5), DECAY)
    project_new = adamw(project_weight, project_moment, project_second, gradients[5], 2.0 * BOTTLE ** (-0.5), DECAY)
    norm_new = adamw(norm_params, norm_moment, norm_second, gradients[6], NORM_RATE, 0.0)
    return (result.astype(jnp.bfloat16), gradients[0], reduce_new[0], reduce_new[1], reduce_new[2], conv_new[0], conv_new[1], conv_new[2], squeeze_new[0], squeeze_new[1], squeeze_new[2], expand_new[0], expand_new[1], expand_new[2], project_new[0], project_new[1], project_new[2], norm_new[0], norm_new[1], norm_new[2])
```

```python
import functools
import jax
import jax.numpy as jnp
from jax import lax
from jax.experimental import pallas as pl
from jax.experimental.pallas import tpu as pltpu
from jax.sharding import PartitionSpec as P

CHANNELS = 1024
BOTTLE = 256
INNER = 128
RADIX = 2
SIDE = 14
MICRO = 2
STEP = 10


EPSILON = 1e-05
PRECISE = lax.Precision.HIGHEST
BETA_ONE = 0.9
BETA_TWO = 0.999
ADAM_EPSILON = 1e-08
DECAY = 0.01
NORM_RATE = 0.8
ROWS = 4 * SIDE * SIDE
NORM_WIDTH = 4352


def split_params(packed):
    widths = (
        BOTTLE,
        BOTTLE,
        RADIX * BOTTLE,
        RADIX * BOTTLE,
        INNER,
        INNER,
        RADIX * BOTTLE,
        CHANNELS,
        CHANNELS,
    )
    pieces = []
    offset = 0
    for segment in widths:
        pieces.append(lax.slice_in_dim(packed, offset, offset + segment))
        offset = offset + segment
    return pieces


def silu_slope(values):
    logistic = jax.nn.sigmoid(values)
    return logistic * (1.0 + values * (1.0 - logistic))


def norm_forward(values, gain, bias, count):
    flat = values.reshape(-1, values.shape[-1])
    total, square = lax.psum((jnp.sum(flat, axis=0), jnp.sum(flat * flat, axis=0)), ("dp", "rep"))
    center = total / count
    scale = lax.rsqrt(square / count - center * center + EPSILON)
    normed = (values - center) * scale
    return (normed * gain + bias, normed, scale)


def norm_backward(upstream, normed, scale, gain, count):
    flat_up = upstream.reshape(-1, upstream.shape[-1])
    flat_norm = normed.reshape(-1, normed.shape[-1])
    bias_sum, gain_sum = lax.psum(
        (jnp.sum(flat_up, axis=0), jnp.sum(flat_up * flat_norm, axis=0)), ("dp", "rep")
    )
    downstream = gain * scale * (upstream - bias_sum / count - normed * (gain_sum / count))
    return (downstream, gain_sum, bias_sum)


def patches(active):
    padded = jnp.pad(active, ((0, 0), (1, 1), (1, 1), (0, 0), (0, 0)))
    shifted = [
        padded[:, down_step : down_step + SIDE, side_step : side_step + SIDE]
        for down_step in range(3)
        for side_step in range(3)
    ]
    return jnp.stack(shifted, axis=4)


def unpatch(columns):
    total = jnp.zeros(
        (columns.shape[0], SIDE + 2, SIDE + 2, columns.shape[3], columns.shape[5]), jnp.float32
    )
    for down_step in range(3):
        for side_step in range(3):
            piece = columns[:, :, :, :, 3 * down_step + side_step]
            total = total + jnp.pad(
                piece,
                ((0, 0), (down_step, 2 - down_step), (side_step, 2 - side_step), (0, 0), (0, 0)),
            )
    return total[:, 1 : SIDE + 1, 1 : SIDE + 1]


def adamw(param, moment, second, gradient, rate, decay):
    moment_new = BETA_ONE * moment + (1.0 - BETA_ONE) * gradient
    second_new = BETA_TWO * second + (1.0 - BETA_TWO) * gradient * gradient
    ratio = (
        moment_new
        / (1.0 - BETA_ONE**STEP)
        / (jnp.sqrt(second_new / (1.0 - BETA_TWO**STEP)) + ADAM_EPSILON)
    )
    return (param - rate * (ratio + decay * param), moment_new, second_new)


def per_device(
    images,
    out_grad,
    reduce_weight,
    reduce_moment,
    reduce_second,
    conv_weight,
    conv_moment,
    conv_second,
    squeeze_weight,
    squeeze_moment,
    squeeze_second,
    expand_weight,
    expand_moment,
    expand_second,
    project_weight,
    project_moment,
    project_second,
    norm_params,
    norm_moment,
    norm_second,
):
    bf16 = jnp.bfloat16
    low_reduce = reduce_weight.astype(bf16)
    low_conv = conv_weight.astype(bf16)
    low_squeeze = squeeze_weight.astype(bf16)
    low_expand = expand_weight.astype(bf16)
    low_project = project_weight.astype(bf16)
    low_norm = norm_params.astype(bf16)
    devices = lax.axis_size("dp") * lax.axis_size("rep")
    per_batch = images.shape[0] // MICRO
    pixel_count = float(per_batch * SIDE * SIDE * devices)
    image_count = float(per_batch * devices)
    group_in = BOTTLE // RADIX
    grad_first = jnp.zeros((CHANNELS, BOTTLE), jnp.float32)
    grad_conv = jnp.zeros((RADIX, 9 * group_in, BOTTLE), jnp.float32)
    grad_squeeze = jnp.zeros((BOTTLE, INNER), jnp.float32)
    grad_expand = jnp.zeros((INNER, RADIX * BOTTLE), jnp.float32)
    grad_last = jnp.zeros((BOTTLE, CHANNELS), jnp.float32)
    grad_norms = jnp.zeros(
        (2 * BOTTLE + 3 * RADIX * BOTTLE + 2 * INNER + 2 * CHANNELS,), jnp.float32
    )
    outputs = []
    input_grads = []
    for number in range(MICRO):
        forward_set = (
            lax.all_gather(low_reduce, "dp", axis=0, tiled=True),
            lax.all_gather(low_conv, "dp", axis=0, tiled=True),
            lax.all_gather(low_squeeze, "dp", axis=0, tiled=True),
            lax.all_gather(low_expand, "dp", axis=0, tiled=True),
            lax.all_gather(low_project, "dp", axis=0, tiled=True),
            lax.all_gather(low_norm, "dp", axis=0, tiled=True),
        )
        first, conv, squeeze, expand, last, packed = forward_set
        (
            gain_one,
            bias_one,
            gain_two,
            bias_two,
            gain_pool,
            bias_pool,
            bias_expand,
            gain_three,
            bias_three,
        ) = split_params(packed.astype(jnp.float32))
        batched = images[number * per_batch : (number + 1) * per_batch]
        cotangent = out_grad[number * per_batch : (number + 1) * per_batch]
        reduced = jnp.einsum("nhwc,cb->nhwb", batched, first, preferred_element_type=jnp.float32)
        norm_one, normed_one, scale_one = norm_forward(reduced, gain_one, bias_one, pixel_count)
        active = jax.nn.silu(norm_one).astype(bf16)
        columns = patches(active.reshape(per_batch, SIDE, SIDE, RADIX, group_in)).reshape(
            per_batch * SIDE * SIDE, RADIX, 9 * group_in
        )
        conv_grouped = conv.reshape(RADIX, 9 * group_in, BOTTLE)
        widened = jnp.einsum(
            "prk,rko->pro", columns, conv_grouped, preferred_element_type=jnp.float32
        )
        widened = widened.reshape(per_batch, SIDE, SIDE, RADIX * BOTTLE)
        norm_two, normed_two, scale_two = norm_forward(widened, gain_two, bias_two, pixel_count)
        splits = jax.nn.silu(norm_two).reshape(per_batch, SIDE, SIDE, RADIX, BOTTLE)
        pooled = jnp.sum(jnp.sum(splits, axis=3), axis=(1, 2)) / (SIDE * SIDE)
        squeeze_float = squeeze.astype(jnp.float32)
        expand_float = expand.astype(jnp.float32)
        pre_pool = jnp.dot(pooled, squeeze_float, precision=PRECISE)
        norm_pool, normed_pool, scale_pool = norm_forward(
            pre_pool, gain_pool, bias_pool, image_count
        )
        hidden = jax.nn.silu(norm_pool)
        logits = (jnp.dot(hidden, expand_float, precision=PRECISE) + bias_expand).reshape(
            per_batch, RADIX, BOTTLE
        )
        attention = jax.nn.softmax(logits, axis=1)
        mixed = jnp.sum(splits * attention[:, None, None], axis=3).astype(bf16)
        projected = jnp.einsum("nhwb,bc->nhwc", mixed, last, preferred_element_type=jnp.float32)
        norm_three, normed_three, scale_three = norm_forward(
            projected, gain_three, bias_three, pixel_count
        )
        summed = batched.astype(jnp.float32) + norm_three
        outputs.append(jax.nn.silu(summed).astype(bf16))
        backward_set = (
            lax.all_gather(low_reduce, "dp", axis=0, tiled=True),
            lax.all_gather(low_conv, "dp", axis=0, tiled=True),
            lax.all_gather(low_squeeze, "dp", axis=0, tiled=True),
            lax.all_gather(low_expand, "dp", axis=0, tiled=True),
            lax.all_gather(low_project, "dp", axis=0, tiled=True),
            lax.all_gather(low_norm, "dp", axis=0, tiled=True),
        )
        first, conv, squeeze, expand, last, packed = backward_set
        gains_back = split_params(packed.astype(jnp.float32))
        conv_grouped = conv.reshape(RADIX, 9 * group_in, BOTTLE)
        expand_float = expand.astype(jnp.float32)
        squeeze_float = squeeze.astype(jnp.float32)
        upstream = cotangent.astype(jnp.float32) * silu_slope(summed)
        d_projected, gain_three_grad, bias_three_grad = norm_backward(
            upstream, normed_three, scale_three, gains_back[7], pixel_count
        )
        d_projected_low = d_projected.astype(bf16)
        grad_last = grad_last + jnp.einsum(
            "nhwb,nhwc->bc", mixed, d_projected_low, preferred_element_type=jnp.float32
        )
        d_mixed = jnp.einsum(
            "nhwc,bc->nhwb", d_projected_low, last, preferred_element_type=jnp.float32
        )
        d_splits = d_mixed[:, :, :, None] * attention[:, None, None]
        d_attention = jnp.sum(d_mixed[:, :, :, None] * splits, axis=(1, 2))
        d_logits = attention * (
            d_attention - jnp.sum(attention * d_attention, axis=1, keepdims=True)
        )
        flat_logits = d_logits.reshape(per_batch, RADIX * BOTTLE)
        grad_expand = grad_expand + jnp.dot(hidden.T, flat_logits, precision=PRECISE)
        d_hidden = jnp.dot(flat_logits, expand_float.T, precision=PRECISE)
        d_pool_norm = d_hidden * silu_slope(norm_pool)
        pool_bias_sum, pool_gain_sum, expand_bias_sum = lax.psum(
            (
                jnp.sum(d_pool_norm, axis=0),
                jnp.sum(d_pool_norm * normed_pool, axis=0),
                jnp.sum(flat_logits, axis=0),
            ),
            ("dp", "rep"),
        )
        d_pre_pool = (
            gains_back[4]
            * scale_pool
            * (
                d_pool_norm
                - pool_bias_sum / image_count
                - normed_pool * (pool_gain_sum / image_count)
            )
        )
        grad_squeeze = grad_squeeze + jnp.dot(pooled.T, d_pre_pool, precision=PRECISE)
        d_pooled = jnp.dot(d_pre_pool, squeeze_float.T, precision=PRECISE)
        d_splits = d_splits + (d_pooled / (SIDE * SIDE))[:, None, None, None, :]
        d_norm_two = d_splits.reshape(per_batch, SIDE, SIDE, RADIX * BOTTLE) * silu_slope(norm_two)
        d_widened, gain_two_grad, bias_two_grad = norm_backward(
            d_norm_two, normed_two, scale_two, gains_back[2], pixel_count
        )
        d_widened_low = d_widened.astype(bf16).reshape(per_batch * SIDE * SIDE, RADIX, BOTTLE)
        grad_conv = grad_conv + jnp.einsum(
            "prk,pro->rko", columns, d_widened_low, preferred_element_type=jnp.float32
        )
        d_columns = jnp.einsum(
            "pro,rko->prk", d_widened_low, conv_grouped, preferred_element_type=jnp.float32
        )
        d_active = unpatch(d_columns.reshape(per_batch, SIDE, SIDE, RADIX, 9, group_in)).reshape(
            per_batch, SIDE, SIDE, BOTTLE
        )
        d_norm_one = d_active * silu_slope(norm_one)
        d_reduced, gain_one_grad, bias_one_grad = norm_backward(
            d_norm_one, normed_one, scale_one, gains_back[0], pixel_count
        )
        d_reduced_low = d_reduced.astype(bf16)
        grad_first = grad_first + jnp.einsum(
            "nhwc,nhwb->cb", batched, d_reduced_low, preferred_element_type=jnp.float32
        )
        input_grads.append(
            upstream
            + jnp.einsum("nhwb,cb->nhwc", d_reduced_low, first, preferred_element_type=jnp.float32)
        )
        grad_norms = grad_norms + jnp.concatenate(
            [
                gain_one_grad,
                bias_one_grad,
                gain_two_grad,
                bias_two_grad,
                pool_gain_sum,
                pool_bias_sum,
                expand_bias_sum,
                gain_three_grad,
                bias_three_grad,
            ]
        )
    grad_conv = grad_conv.reshape(9 * BOTTLE, BOTTLE)
    partial_value = (
        lax.psum_scatter(grad_first, "dp", scatter_dimension=0, tiled=True),
        lax.psum_scatter(grad_conv, "dp", scatter_dimension=0, tiled=True),
        lax.psum_scatter(grad_squeeze, "dp", scatter_dimension=0, tiled=True),
        lax.psum_scatter(grad_expand, "dp", scatter_dimension=0, tiled=True),
        lax.psum_scatter(grad_last, "dp", scatter_dimension=0, tiled=True),
    )
    owned = lax.psum(
        (partial_value[0], partial_value[1], partial_value[2], partial_value[3], partial_value[4]),
        "rep",
    )
    shard_length = norm_params.shape[0]
    norm_grad_owned = lax.dynamic_slice_in_dim(
        grad_norms, lax.axis_index("dp") * shard_length, shard_length
    )
    reduce_new = adamw(
        reduce_weight, reduce_moment, reduce_second, owned[0], 2.0 * CHANNELS ** (-0.5), DECAY
    )
    conv_new = adamw(
        conv_weight,
        conv_moment,
        conv_second,
        owned[1],
        2.0 * (9 * BOTTLE // RADIX) ** (-0.5),
        DECAY,
    )
    squeeze_new = adamw(
        squeeze_weight, squeeze_moment, squeeze_second, owned[2], 2.0 * BOTTLE ** (-0.5), DECAY
    )
    expand_new = adamw(
        expand_weight, expand_moment, expand_second, owned[3], 2.0 * (INNER // 8) ** (-0.5), DECAY
    )
    project_new = adamw(
        project_weight, project_moment, project_second, owned[4], 2.0 * BOTTLE ** (-0.5), DECAY
    )
    norm_new = adamw(norm_params, norm_moment, norm_second, norm_grad_owned, NORM_RATE, 0.0)
    return (
        jnp.concatenate(outputs, axis=0),
        jnp.concatenate(input_grads, axis=0),
        reduce_new[0],
        reduce_new[1],
        reduce_new[2],
        conv_new[0],
        conv_new[1],
        conv_new[2],
        squeeze_new[0],
        squeeze_new[1],
        squeeze_new[2],
        expand_new[0],
        expand_new[1],
        expand_new[2],
        project_new[0],
        project_new[1],
        project_new[2],
        norm_new[0],
        norm_new[1],
        norm_new[2],
    )


MESH = pl.DeviceIdType.MESH
PAD = 64
CHUNK = 112
F32 = jnp.float32
BF16 = jnp.bfloat16
STATS = ((8, 128), (8, 256), (8, 128), (8, 512), (8, 512), (16, 128), (8, 256), (8, 128))


def row_ids(width):
    return lax.broadcasted_iota(jnp.int32, (8, width), 0)


def image_sum(rows):
    return rows + pltpu.roll(rows, 4, 0)


def pair_sum(rows):
    even = row_ids(rows.shape[1]) % 2 == 0
    return rows + jnp.where(even, pltpu.roll(rows, 7, 0), pltpu.roll(rows, 1, 0))


def micro_sum(rows):
    return pair_sum(image_sum(rows))


def stack_sums(first, second):
    return jnp.where(row_ids(first.shape[1]) < 4, first, second)


def unstack_sums(stacked):
    upper = row_ids(stacked.shape[1]) < 4
    turned = pltpu.roll(stacked, 4, 0)
    return jnp.where(upper, stacked, turned), jnp.where(upper, turned, stacked)


def fold_lanes(stacked):
    half = stacked.shape[1] // 2
    even = row_ids(half) % 2 == 0
    return jnp.where(even, stacked[:, :half], stacked[:, half:])


def unfold_lanes(folded):
    even = row_ids(folded.shape[1]) % 2 == 0
    left = jnp.where(even, folded, pltpu.roll(folded, 1, 0))
    right = jnp.where(even, pltpu.roll(folded, 7, 0), folded)
    return jnp.concatenate([left, right], axis=1)


def norm_terms(total, square, gain, bias, count):
    center = total / count
    scale = lax.rsqrt(square / count - center * center + EPSILON)
    slope = scale * gain
    return center, scale, slope, bias - center * slope


def back_terms(center, scale, slope, bias_sum, gain_sum, count):
    by_value = -slope * scale * (gain_sum / count)
    constant = -slope * (bias_sum / count) - by_value * center
    return by_value, constant


def tdot(left, right):
    return lax.dot_general(left, right, (((0,), (0,)), ((), ())), preferred_element_type=F32)


def dot_t(left, right):
    return lax.dot_general(left, right, (((1,), (1,)), ((), ())), preferred_element_type=F32)


def block_kernel(
    n_dp,
    n_rep,
    x_hbm,
    gy_hbm,
    w1_own,
    wc_own,
    sq_own,
    ex_own,
    w3_own,
    np_own,
    bo_hbm,
    dx_hbm,
    f1_out,
    fc_out,
    f3_out,
    fe_out,
    gn_out,
    x_v,
    gy_v,
    fw1,
    fwc,
    fpe,
    pe_own,
    np_slots,
    np_full,
    red,
    act,
    columns,
    wid,
    splits,
    mixed,
    proj,
    up,
    bo_v,
    dproj,
    d_mixed,
    dn2,
    dwid,
    dcol,
    dn1,
    dred,
    g1,
    gc,
    g3,
    ge,
    *rest,
):
    n_ar = len(STATS)
    ar_src_a = rest[0:n_ar]
    ar_slots_a = rest[n_ar : 2 * n_ar]
    ar_src_b = rest[2 * n_ar : 3 * n_ar]
    ar_slots_b = rest[3 * n_ar : 4 * n_ar]
    rest = rest[4 * n_ar :]
    r1s, r2s, ks, r3s, own, fs = (rest[4 * i : 4 * i + 4] for i in range(6))
    rest = rest[24:]
    local_sem, ar_send_a, ar_recv_a, ar_send_b, ar_recv_b, np_sems, ws, wr, gs, gr = rest

    dp = lax.axis_index("dp")
    rep = lax.axis_index("rep")
    core = lax.rem(rep, 2)
    half_y = rep // 2
    planes = n_dp // 2
    plane_size = 2 * n_rep
    plane = dp // 2
    in_plane = lax.rem(dp, 2) * n_rep + rep
    sibling = (dp, half_y * 2 + (1 - core))
    across = (dp, (1 - half_y) * 2 + core)
    pixels = float(SIDE * SIDE * 2 * n_dp * n_rep)
    pictures = float(2 * n_dp * n_rep)

    def plane_peer(step):
        other = lax.rem(in_plane + step, plane_size)
        return (plane * 2 + other // n_rep, lax.rem(other, n_rep))

    def column_peer(step):
        return (lax.rem(plane + step, planes) * 2 + lax.rem(dp, 2), rep)

    def owner_peer(step):
        return (lax.rem(dp + step, n_dp), rep)

    def rep_peer(step):
        return (dp, lax.rem(rep + step, n_rep))

    def remote(src, dst, send_sem, recv_sem, device):
        return pltpu.make_async_remote_copy(
            src_ref=src,
            dst_ref=dst,
            send_sem=send_sem,
            recv_sem=recv_sem,
            device_id=device,
            device_id_type=MESH,
        )

    def send_all(src, dst, send_sem, recv_sem, peer, count):
        def one(step, carry):
            remote(src, dst, send_sem, recv_sem, peer(step)).start()
            return carry

        lax.fori_loop(1, count, one, 0)

    def wait_bytes(ref, sem):
        pltpu.make_async_copy(ref, ref, sem).wait()

    def over_rows(body, init):
        def step(index, carry):
            return body(pl.multiple_of(index * CHUNK, CHUNK), carry)

        return lax.fori_loop(0, ROWS // CHUNK, step, init)

    def grouped(values):
        return values.reshape(CHUNK // 8, 8, values.shape[-1])

    def flat(values):
        return values.reshape(CHUNK, values.shape[-1])

    x_copy = pltpu.make_async_copy(x_hbm, x_v, local_sem.at[0])
    gy_copy = pltpu.make_async_copy(gy_hbm, gy_v, local_sem.at[1])
    x_copy.start()
    gy_copy.start()
    barrier = pltpu.get_barrier_semaphore()

    def greet_plane(step, carry):
        pl.semaphore_signal(barrier, inc=1, device_id=plane_peer(step), device_id_type=MESH)
        return carry

    def greet_owner(step, carry):
        pl.semaphore_signal(barrier, inc=1, device_id=owner_peer(step), device_id_type=MESH)
        return carry

    lax.fori_loop(1, plane_size, greet_plane, 0)
    lax.fori_loop(1, n_dp, greet_owner, 0)

    part = core * 2 + half_y
    q1 = w1_own.shape[0] // 4
    fw1[dp, core, half_y] = w1_own[pl.ds(pl.multiple_of(part * q1, q1), q1), :].astype(BF16)
    qc = wc_own.shape[0] // 2
    core_lanes = pl.ds(pl.multiple_of(core * 128, 128), 128)
    fwc[dp, half_y, :, core_lanes] = wc_own[
        pl.ds(pl.multiple_of(half_y * qc, qc), qc), core_lanes
    ].astype(BF16)
    ex_rows = ex_own.shape[0]
    pe_own[:, 0:CHANNELS] = w3_own[...].astype(BF16)
    pe_own[:, 1024:1152] = sq_own[...].astype(BF16)
    pe_own[0:ex_rows, 1152:1408] = ex_own[:, 0:256].astype(BF16)
    pe_own[ex_rows : 2 * ex_rows, 1152:1408] = ex_own[:, 256:512].astype(BF16)
    pe_own[:, 1408:1536] = jnp.zeros((2 * ex_rows, 128), BF16)
    pe_lanes = pl.ds(pl.multiple_of(part * 384, 128), 384)
    fpe[dp, :, pe_lanes] = pe_own[:, pe_lanes]
    np_slots[dp] = np_own[...].astype(BF16).astype(F32)

    pl.semaphore_wait(barrier, plane_size + n_dp - 2)

    def quarter_w1(c, y):
        return fw1.at[:, c, y]

    def quarter_wc(c, y):
        return fwc.at[:, y, :, pl.ds(pl.multiple_of(c * 128, 128), 128)]

    def quarter_pe(c, y):
        return fpe.at[:, :, pl.ds(pl.multiple_of((c * 2 + y) * 384, 128), 384)]

    quarters = (quarter_w1, quarter_wc, quarter_pe)

    def piece(which, d):
        return (
            fw1.at[d, core, half_y],
            fwc.at[d, half_y, :, core_lanes],
            fpe.at[d, :, pe_lanes],
        )[which]

    def seven(which):
        return (
            fw1.at[pl.ds(0, n_dp - 1), core, half_y],
            fwc.at[pl.ds(0, n_dp - 1), half_y, :, core_lanes],
            fpe.at[pl.ds(0, n_dp - 1), :, pe_lanes],
        )[which]

    def gather_out(which):
        src = piece(which, dp)
        send_all(src, src, ws.at[which, 0], wr.at[which, 0], owner_peer, n_dp)

    def gather_turn(which):
        wait_bytes(seven(which), wr.at[which, 0])
        mine = quarters[which](core, half_y)
        remote(mine, mine, ws.at[which, 1], wr.at[which, 1], across).start()
        remote(mine, mine, ws.at[which, 2], wr.at[which, 2], sibling).start()

    def gather_hand(which):
        theirs = quarters[which](core, 1 - half_y)
        wait_bytes(theirs, wr.at[which, 1])
        remote(theirs, theirs, ws.at[which, 3], wr.at[which, 3], sibling).start()

    def gather_end(which):
        wait_bytes(quarters[which](1 - core, half_y), wr.at[which, 2])
        wait_bytes(quarters[which](1 - core, 1 - half_y), wr.at[which, 3])

    gather_out(0)
    send_all(np_slots.at[dp], np_slots.at[dp], np_sems.at[0], np_sems.at[1], owner_peer, n_dp)
    gather_out(1)
    gather_out(2)
    gather_turn(0)
    gather_hand(0)

    def sum_start(k, payload):
        ar_src_a[k][...] = payload
        ar_slots_a[k][in_plane] = payload
        send_all(
            ar_src_a[k],
            ar_slots_a[k].at[in_plane],
            ar_send_a.at[k],
            ar_recv_a.at[k],
            plane_peer,
            plane_size,
        )

    def sum_turn(k):
        wait_bytes(ar_slots_a[k].at[pl.ds(0, plane_size - 1)], ar_recv_a.at[k])
        part_sum = ar_slots_a[k][0]
        for slot in range(1, plane_size):
            part_sum = part_sum + ar_slots_a[k][slot]
        ar_src_b[k][...] = part_sum
        ar_slots_b[k][plane] = part_sum
        send_all(
            ar_src_b[k],
            ar_slots_b[k].at[plane],
            ar_send_b.at[k],
            ar_recv_b.at[k],
            column_peer,
            planes,
        )

    def sum_end(k):
        wait_bytes(ar_slots_b[k].at[pl.ds(0, planes - 1)], ar_recv_b.at[k])
        whole = ar_slots_b[k][0]
        for slot in range(1, planes):
            whole = whole + ar_slots_b[k][slot]
        return whole

    def lanes_of(index, width):
        return pl.ds(pl.multiple_of(index * width, 128), width)

    def half_of(which, ref, c):
        if which == 0:
            return ref.at[:, c]
        if which == 1:
            return ref.at[:, :, :, lanes_of(c, 128)]
        return ref.at[:, :, lanes_of(c, (512, 256)[which - 2])]

    def quarter_of(which, ref, c, y):
        if which == 0:
            return ref.at[:, c, y]
        if which == 1:
            return ref.at[:, y, :, lanes_of(c, 128)]
        return ref.at[:, :, lanes_of(c * 2 + y, (256, 128)[which - 2])]

    def final_part(which, c, y):
        if which == 0:
            return fs[0].at[c, y]
        if which == 1:
            return fs[1].at[y, :, lanes_of(c, 128)]
        return fs[which].at[:, lanes_of(c * 2 + y, (256, 128)[which - 2])]

    grads = (g1, gc, g3, ge)

    def reduce_core(which):
        remote(
            half_of(which, grads[which], 1 - core),
            r1s[which],
            gs.at[which, 0],
            gr.at[which, 0],
            sibling,
        ).start()

    def reduce_y(which):
        wait_bytes(r1s[which], gr.at[which, 0])
        mine = half_of(which, grads[which], core)

        def add(d, carry):
            mine[d] = mine[d] + r1s[which][d]
            return carry

        lax.fori_loop(0, n_dp, add, 0)
        remote(
            quarter_of(which, grads[which], core, 1 - half_y),
            r2s[which],
            gs.at[which, 1],
            gr.at[which, 1],
            across,
        ).start()

    def reduce_owner(which):
        wait_bytes(r2s[which], gr.at[which, 1])
        mine = quarter_of(which, grads[which], core, half_y)

        def add(d, carry):
            ks[which][d] = (mine[d] + r2s[which][d]).astype(ks[which].dtype)
            return carry

        lax.fori_loop(0, n_dp, add, 0)
        own[which][...] = mine[dp] + r2s[which][dp]
        r3s[which][dp] = jnp.zeros(own[which].shape, r3s[which].dtype)

        def one(step, carry):
            device = owner_peer(step)
            remote(
                ks[which].at[device[0]],
                r3s[which].at[dp],
                gs.at[which, 2],
                gr.at[which, 2],
                device,
            ).start()
            return carry

        lax.fori_loop(1, n_dp, one, 0)

    def reduce_spread(which):
        wait_bytes(r3s[which].at[pl.ds(0, n_dp - 1)], gr.at[which, 2])
        total = own[which][...]
        for slot in range(n_dp):
            total = total + r3s[which][slot].astype(F32)
        mine = final_part(which, core, half_y)
        mine[...] = total
        send_all(mine, mine, gs.at[which, 3], gr.at[which, 3], rep_peer, n_rep)

    def three_parts(which):
        return r2s[which].at[pl.ds(0, 3)]

    def reduce_end(which):
        wait_bytes(three_parts(which), gr.at[which, 3])

    zero_rows = jnp.zeros((PAD, BOTTLE), F32)
    for side in range(3):
        act[side, 0:PAD, :] = zero_rows
        act[side, PAD + ROWS : 2 * PAD + ROWS, :] = zero_rows
    for lane_block in range(9):
        dcol[0:PAD, lane_block * 256 : lane_block * 256 + 256] = zero_rows
        dcol[PAD + ROWS : 2 * PAD + ROWS, lane_block * 256 : lane_block * 256 + 256] = zero_rows

    x_copy.wait()
    gather_end(0)
    red[...] = jnp.dot(x_v[...], fw1[...].reshape(CHANNELS, BOTTLE), preferred_element_type=F32)

    def sums_of(ref, start, width):
        def body(row, carry):
            values = grouped(ref[pl.ds(row, CHUNK), start : start + width])
            return carry[0] + jnp.sum(values, axis=0), carry[1] + jnp.sum(values * values, axis=0)

        zero = jnp.zeros((8, width), F32)
        return over_rows(body, (zero, zero))

    def wide_sums(ref, width):
        found = [sums_of(ref, start, 256) for start in range(0, width, 256)]
        first = jnp.concatenate([item[0] for item in found], axis=1)
        second = jnp.concatenate([item[1] for item in found], axis=1)
        return fold_lanes(stack_sums(micro_sum(first), micro_sum(second)))

    sum_start(0, wide_sums(red, BOTTLE))

    wait_bytes(np_slots.at[pl.ds(0, n_dp - 1)], np_sems.at[1])
    np_full[...] = jnp.zeros(np_full.shape, F32)
    shard = NORM_WIDTH // n_dp
    for d in range(n_dp):
        at = shard * d // 128
        np_full[at : at + 8, :] = np_full[at : at + 8, :] + np_slots[d]

    def vector(at, width):
        rows = [np_full[at // 128 + k : at // 128 + k + 1, :] for k in range(width // 128)]
        return jnp.concatenate(rows, axis=1) if len(rows) > 1 else rows[0]

    gain_one, bias_one = vector(0, 256), vector(256, 256)
    gain_two, bias_two = vector(512, 512), vector(1024, 512)
    gain_pool, bias_pool = vector(1536, 128), vector(1664, 128)
    bias_expand = vector(1792, 512)
    gain_three, bias_three = vector(2304, 1024), vector(3328, 1024)

    gather_turn(1)
    sum_turn(0)
    gather_hand(1)
    total, square = unstack_sums(unfold_lanes(sum_end(0)))
    center1, scale1, mul1, add1 = norm_terms(total, square, gain_one, bias_one, pixels)

    def make_active(row, carry):
        turned = grouped(red[pl.ds(row, CHUNK), :]) * mul1 + add1
        act[1, pl.ds(PAD + row, CHUNK), :] = flat(turned * jax.nn.sigmoid(turned))
        return carry

    over_rows(make_active, 0)
    place = lax.rem(lax.broadcasted_iota(jnp.int32, (CHUNK, BOTTLE), 0) // 4, SIDE)
    not_last = place != SIDE - 1
    not_first = place != 0

    def beside(side, row, distance):
        near = act[side, pl.ds(PAD + row - 8, CHUNK + 16), :]
        return pltpu.roll(near, (CHUNK + 16 - distance) % (CHUNK + 16), 0)[8 : 8 + CHUNK]

    def shift_active(row, carry):
        act[2, pl.ds(PAD + row, CHUNK), :] = jnp.where(not_last, beside(1, row, 4), 0.0)
        act[0, pl.ds(PAD + row, CHUNK), :] = jnp.where(not_first, beside(1, row, -4), 0.0)
        return carry

    over_rows(shift_active, 0)

    def make_columns(row, carry):
        for tap in range(9):
            down, side = tap // 3 - 1, tap % 3
            values = act[side, pl.ds(PAD + row + 56 * down, CHUNK), :].astype(BF16)
            columns[0, pl.ds(row, CHUNK), tap * 128 : tap * 128 + 128] = values[:, 0:128]
            columns[1, pl.ds(row, CHUNK), tap * 128 : tap * 128 + 128] = values[:, 128:256]
        return carry

    over_rows(make_columns, 0)
    gather_end(1)
    own_half = n_dp // 2

    def filters(group):
        return fwc[group * own_half : (group + 1) * own_half].reshape(9 * 128, BOTTLE)

    for group in range(2):
        wid[:, group * 256 : group * 256 + 256] = jnp.dot(
            columns[group], filters(group), preferred_element_type=F32
        )
    sum_start(1, wide_sums(wid, 512))
    gather_turn(2)
    sum_turn(1)
    gather_hand(2)
    total, square = unstack_sums(unfold_lanes(sum_end(1)))
    center2, scale2, mul2, add2 = norm_terms(total, square, gain_two, bias_two, pixels)

    def make_splits(row, carry):
        found = []
        for group in range(2):
            lanes = slice(group * 256, group * 256 + 256)
            turned = grouped(wid[pl.ds(row, CHUNK), lanes]) * mul2[:, lanes] + add2[:, lanes]
            values = turned * jax.nn.sigmoid(turned)
            splits[pl.ds(row, CHUNK), lanes] = flat(values)
            found.append(jnp.sum(values, axis=0))
        return carry + found[0] + found[1]

    pooled = image_sum(over_rows(make_splits, jnp.zeros((8, BOTTLE), F32))) / (SIDE * SIDE)
    gather_end(2)
    last = fpe[:, :, 0:CHANNELS].reshape(BOTTLE, CHANNELS)
    squeeze = fpe[:, :, 1024:1152].reshape(BOTTLE, INNER).astype(F32)
    ex_both = fpe[:, :, 1152:1408]
    expand = jnp.concatenate(
        [
            ex_both[:, 0:ex_rows].reshape(INNER, 256),
            ex_both[:, ex_rows : 2 * ex_rows].reshape(INNER, 256),
        ],
        axis=1,
    ).astype(F32)
    pre_pool = jnp.dot(pooled, squeeze, precision=PRECISE, preferred_element_type=F32)
    sum_start(2, stack_sums(pair_sum(pre_pool), pair_sum(pre_pool * pre_pool)))
    sum_turn(2)
    total, square = unstack_sums(sum_end(2))
    center_p, scale_p, mul_p, add_p = norm_terms(total, square, gain_pool, bias_pool, pictures)
    normed_p = (pre_pool - center_p) * scale_p
    norm_p = pre_pool * mul_p + add_p
    gate_p = jax.nn.sigmoid(norm_p)
    hidden = norm_p * gate_p
    slope_p = gate_p * (1.0 + norm_p * (1.0 - gate_p))
    logits = jnp.dot(hidden, expand, precision=PRECISE, preferred_element_type=F32) + bias_expand
    left, right = logits[:, 0:256], logits[:, 256:512]
    most = jnp.maximum(left, right)
    left, right = jnp.exp(left - most), jnp.exp(right - most)
    att0 = left / (left + right)
    att1 = right / (left + right)

    def make_mixed(row, carry):
        rows = pl.ds(row, CHUNK)
        values = grouped(splits[rows, 0:256]) * att0 + grouped(splits[rows, 256:512]) * att1
        mixed[rows, :] = flat(values).astype(BF16)
        return carry

    over_rows(make_mixed, 0)
    proj[...] = jnp.dot(mixed[...], last, preferred_element_type=F32)
    sum_start(3, wide_sums(proj, CHANNELS))
    sum_turn(3)
    total, square = unstack_sums(unfold_lanes(sum_end(3)))
    center3, scale3, mul3, add3 = norm_terms(total, square, gain_three, bias_three, pixels)

    gy_copy.wait()
    found = []
    for start in range(0, CHANNELS, 256):
        lanes = slice(start, start + 256)
        m3, a3, c3, s3 = mul3[:, lanes], add3[:, lanes], center3[:, lanes], scale3[:, lanes]

        def make_out(row, carry):
            rows = pl.ds(row, CHUNK)
            values = grouped(proj[rows, lanes])
            summed = grouped(x_v[rows, lanes].astype(F32)) + (values * m3 + a3)
            gate = jax.nn.sigmoid(summed)
            bo_v[rows, lanes] = flat(summed * gate).astype(BF16)
            upstream = grouped(gy_v[rows, lanes].astype(F32)) * (
                gate * (1.0 + summed * (1.0 - gate))
            )
            up[rows, lanes] = flat(upstream)
            normed = (values - c3) * s3
            return carry[0] + jnp.sum(upstream, axis=0), carry[1] + jnp.sum(
                upstream * normed, axis=0
            )

        zero = jnp.zeros((8, 256), F32)
        found.append(over_rows(make_out, (zero, zero)))
    bias_sum = micro_sum(jnp.concatenate([item[0] for item in found], axis=1))
    gain_sum = micro_sum(jnp.concatenate([item[1] for item in found], axis=1))
    sum_start(4, fold_lanes(stack_sums(bias_sum, gain_sum)))
    bo_copy = pltpu.make_async_copy(bo_v, bo_hbm, local_sem.at[2])
    bo_copy.start()

    def write_norm(at, pattern):
        both = pattern[0:1, :] + pattern[2:3, :]
        for k in range(both.shape[1] // 128):
            gn_out[at // 128 + k : at // 128 + k + 1, :] = both[:, k * 128 : k * 128 + 128]

    gn_out[32:40, :] = jnp.zeros((8, 128), F32)
    sum_turn(4)
    bias_sum, gain_sum = unstack_sums(unfold_lanes(sum_end(4)))
    write_norm(2304, gain_sum)
    write_norm(3328, bias_sum)
    by_value, constant = back_terms(center3, scale3, mul3, bias_sum, gain_sum, pixels)
    for start in range(0, CHANNELS, 256):
        lanes = slice(start, start + 256)
        m3, v3, k3 = mul3[:, lanes], by_value[:, lanes], constant[:, lanes]

        def make_dproj(row, carry):
            rows = pl.ds(row, CHUNK)
            values = grouped(up[rows, lanes]) * m3 + grouped(proj[rows, lanes]) * v3 + k3
            dproj[rows, lanes] = flat(values).astype(BF16)
            return carry

        over_rows(make_dproj, 0)

    d_mixed[...] = dot_t(dproj[...], last)

    def attend(row, carry):
        rows = pl.ds(row, CHUNK)
        values = grouped(d_mixed[rows, :])
        return (
            carry[0] + jnp.sum(values * grouped(splits[rows, 0:256]), axis=0),
            carry[1] + jnp.sum(values * grouped(splits[rows, 256:512]), axis=0),
        )

    zero = jnp.zeros((8, 256), F32)
    d_att0, d_att1 = over_rows(attend, (zero, zero))
    d_att0, d_att1 = image_sum(d_att0), image_sum(d_att1)
    both = att0 * d_att0 + att1 * d_att1
    d_logits = jnp.concatenate([att0 * (d_att0 - both), att1 * (d_att1 - both)], axis=1)
    d_hidden = lax.dot_general(
        d_logits, expand, (((1,), (1,)), ((), ())), precision=PRECISE, preferred_element_type=F32
    )
    d_pool = d_hidden * slope_p
    per_micro = stack_sums(pair_sum(d_pool), pair_sum(d_pool * normed_p))
    ex_sum = pair_sum(d_logits)
    ex_sum = ex_sum + pltpu.roll(ex_sum, 2, 0)
    ids = row_ids(128)
    ex_rows_sum = jnp.where(ids == 0, ex_sum[:, 0:128], 0.0)
    for k in range(1, 4):
        ex_rows_sum = ex_rows_sum + jnp.where(ids == k, ex_sum[:, k * 128 : k * 128 + 128], 0.0)
    sum_start(5, jnp.concatenate([per_micro, ex_rows_sum], axis=0))

    once = row_ids(INNER) < 4
    grad_ex = lax.dot_general(
        jnp.where(once, hidden, 0.0),
        d_logits,
        (((0,), (0,)), ((), ())),
        precision=PRECISE,
        preferred_element_type=F32,
    )
    grad_ex = grad_ex.reshape(n_dp, ex_rows, 512)
    ge[:, 0:ex_rows, 128:384] = grad_ex[:, :, 0:256]
    ge[:, ex_rows : 2 * ex_rows, 128:384] = grad_ex[:, :, 256:512]
    ge[:, :, 384:512] = jnp.zeros((n_dp, 2 * ex_rows, 128), F32)
    for start in range(0, CHANNELS, 256):
        lanes = slice(start, start + 256)
        g3[:, :, lanes] = tdot(mixed[...], dproj[:, lanes]).reshape(n_dp, 2 * ex_rows, 256)
    reduce_core(2)
    sum_turn(5)
    whole = sum_end(5)
    pool_bias_sum, pool_gain_sum = unstack_sums(whole[0:8])
    write_norm(1536, pool_gain_sum)
    write_norm(1664, pool_bias_sum)
    gn_out[14:18, :] = whole[8:12]
    d_pre_pool = mul_p * (
        d_pool - pool_bias_sum / pictures - normed_p * (pool_gain_sum / pictures)
    )
    d_pooled = lax.dot_general(
        d_pre_pool, squeeze, (((1,), (1,)), ((), ())), precision=PRECISE, preferred_element_type=F32
    ) / (SIDE * SIDE)
    found = []
    for group, att in ((0, att0), (1, att1)):
        lanes = slice(group * 256, group * 256 + 256)
        m2, a2, c2, s2 = mul2[:, lanes], add2[:, lanes], center2[:, lanes], scale2[:, lanes]

        def make_dn2(row, carry):
            rows = pl.ds(row, CHUNK)
            values = grouped(wid[rows, lanes])
            turned = values * m2 + a2
            gate = jax.nn.sigmoid(turned)
            slope = gate * (1.0 + turned * (1.0 - gate))
            down = (grouped(d_mixed[rows, :]) * att + d_pooled) * slope
            dn2[rows, lanes] = flat(down)
            normed = (values - c2) * s2
            return carry[0] + jnp.sum(down, axis=0), carry[1] + jnp.sum(down * normed, axis=0)

        found.append(over_rows(make_dn2, (zero, zero)))
    bias_sum = micro_sum(jnp.concatenate([item[0] for item in found], axis=1))
    gain_sum = micro_sum(jnp.concatenate([item[1] for item in found], axis=1))
    sum_start(6, fold_lanes(stack_sums(bias_sum, gain_sum)))
    ge[:, :, 0:128] = lax.dot_general(
        jnp.where(row_ids(BOTTLE) < 4, pooled, 0.0),
        d_pre_pool,
        (((0,), (0,)), ((), ())),
        precision=PRECISE,
        preferred_element_type=F32,
    ).reshape(n_dp, 2 * ex_rows, 128)
    reduce_core(3)
    sum_turn(6)
    reduce_y(2)
    reduce_y(3)
    bias_sum, gain_sum = unstack_sums(unfold_lanes(sum_end(6)))
    write_norm(512, gain_sum)
    write_norm(1024, bias_sum)
    by_value, constant = back_terms(center2, scale2, mul2, bias_sum, gain_sum, pixels)

    for group in range(2):
        lanes = slice(group * 256, group * 256 + 256)
        m2, v2, k2 = mul2[:, lanes], by_value[:, lanes], constant[:, lanes]

        def make_dwid(row, carry):
            rows = pl.ds(row, CHUNK)
            values = grouped(dn2[rows, lanes]) * m2 + grouped(wid[rows, lanes]) * v2 + k2
            dwid[rows, lanes] = flat(values).astype(BF16)
            return carry

        over_rows(make_dwid, 0)
        dcol[PAD : PAD + ROWS, group * 1152 : group * 1152 + 1152] = dot_t(
            dwid[:, lanes], filters(group)
        )

    def gather_taps(row, carry):
        for side in range(3):
            for group in range(2):
                total = None
                for down in range(3):
                    at = group * 1152 + (3 * down + side) * 128
                    values = dcol[pl.ds(PAD + row - 56 * (down - 1), CHUNK), at : at + 128]
                    total = values if total is None else total + values
                act[side, pl.ds(PAD + row, CHUNK), group * 128 : group * 128 + 128] = total
        return carry

    over_rows(gather_taps, 0)

    def make_dn1(row, carry):
        rows = pl.ds(row, CHUNK)
        d_active = act[1, pl.ds(PAD + row, CHUNK), :]
        d_active = d_active + jnp.where(not_first, beside(2, row, -4), 0.0)
        d_active = d_active + jnp.where(not_last, beside(0, row, 4), 0.0)
        values = grouped(red[rows, :])
        turned = values * mul1 + add1
        gate = jax.nn.sigmoid(turned)
        slope = gate * (1.0 + turned * (1.0 - gate))
        down = grouped(d_active) * slope
        dn1[rows, :] = flat(down)
        normed = (values - center1) * scale1
        return carry[0] + jnp.sum(down, axis=0), carry[1] + jnp.sum(down * normed, axis=0)

    bias_sum, gain_sum = over_rows(make_dn1, (zero, zero))
    sum_start(7, fold_lanes(stack_sums(micro_sum(bias_sum), micro_sum(gain_sum))))
    reduce_owner(2)
    reduce_owner(3)
    for group in range(2):
        gc[group * own_half : (group + 1) * own_half] = tdot(
            columns[group], dwid[:, group * 256 : group * 256 + 256]
        ).reshape(own_half, 2, 9 * 128 // n_dp, BOTTLE)
    reduce_core(1)
    sum_turn(7)
    reduce_y(1)
    bias_sum, gain_sum = unstack_sums(unfold_lanes(sum_end(7)))
    write_norm(0, gain_sum)
    write_norm(256, bias_sum)
    by_value, constant = back_terms(center1, scale1, mul1, bias_sum, gain_sum, pixels)

    def make_dred(row, carry):
        rows = pl.ds(row, CHUNK)
        values = grouped(dn1[rows, :]) * mul1 + grouped(red[rows, :]) * by_value + constant
        dred[rows, :] = flat(values).astype(BF16)
        return carry

    over_rows(make_dred, 0)
    g1[...] = tdot(x_v[...], dred[...]).reshape(g1.shape)
    reduce_core(0)
    reduce_owner(1)
    up[...] = up[...] + dot_t(dred[...], fw1[...].reshape(CHANNELS, BOTTLE))
    dx_copy = pltpu.make_async_copy(up, dx_hbm, local_sem.at[3])
    dx_copy.start()
    reduce_y(0)
    reduce_spread(2)
    reduce_spread(3)
    reduce_owner(0)
    reduce_spread(1)
    reduce_spread(0)
    for which, out in ((2, f3_out), (3, fe_out), (1, fc_out), (0, f1_out)):
        reduce_end(which)
        out[...] = fs[which][...]

    bo_copy.wait()
    dx_copy.wait()
    for k in range(n_ar):
        wait_bytes(ar_slots_a[k].at[pl.ds(0, plane_size - 1)], ar_send_a.at[k])
        wait_bytes(ar_slots_b[k].at[pl.ds(0, planes - 1)], ar_send_b.at[k])
    wait_bytes(np_slots.at[pl.ds(0, n_dp - 1)], np_sems.at[0])
    for which in range(3):
        wait_bytes(seven(which), ws.at[which, 0])
        for stage in range(1, 4):
            wait_bytes(quarters[which](core, half_y), ws.at[which, stage])
    for which in range(4):
        wait_bytes(r1s[which], gs.at[which, 0])
        wait_bytes(r2s[which], gs.at[which, 1])
        wait_bytes(r3s[which].at[pl.ds(0, n_dp - 1)], gs.at[which, 2])
        wait_bytes(three_parts(which), gs.at[which, 3])


def update_kernel(*refs):
    grads, states, outs = refs[0:4], refs[4:19], refs[19:34]
    ex_rows = states[9].shape[0]
    found = (
        grads[0][...],
        grads[1][...],
        grads[3][:, 0:128],
        jnp.concatenate([grads[3][0:ex_rows, 128:384], grads[3][ex_rows:, 128:384]], axis=1),
        grads[2][...],
    )
    rates = (CHANNELS, 9 * BOTTLE // RADIX, BOTTLE, INNER // 8, BOTTLE)
    for k in range(5):
        new = adamw(
            states[3 * k][...],
            states[3 * k + 1][...],
            states[3 * k + 2][...],
            found[k],
            2.0 * rates[k] ** (-0.5),
            DECAY,
        )
        for j in range(3):
            outs[3 * k + j][...] = new[j]


def fused_device(
    images,
    out_grad,
    reduce_weight,
    reduce_moment,
    reduce_second,
    conv_weight,
    conv_moment,
    conv_second,
    squeeze_weight,
    squeeze_moment,
    squeeze_second,
    expand_weight,
    expand_moment,
    expand_second,
    project_weight,
    project_moment,
    project_second,
    norm_params,
    norm_moment,
    norm_second,
):
    n_dp, n_rep = lax.axis_size("dp"), lax.axis_size("rep")
    shard = norm_params.shape[0]
    offset = lax.axis_index("dp") * shard
    by_pixel = lambda values: jnp.transpose(values, (1, 2, 0, 3)).reshape(ROWS, CHANNELS)
    block = lax.dynamic_update_slice(
        jnp.zeros((1024,), F32), norm_params, (lax.rem(offset, 128),)
    ).reshape(8, 128)
    qc = conv_weight.shape[0] // 2
    q1 = reduce_weight.shape[0] // 4
    pe = squeeze_weight.shape[0]
    vmem = pltpu.VMEM
    scratch = [
        vmem((ROWS, CHANNELS), BF16),
        vmem((ROWS, CHANNELS), BF16),
        vmem((n_dp, 2, 2, q1, BOTTLE), BF16),
        vmem((n_dp, 2, qc, BOTTLE), BF16),
        vmem((n_dp, pe, 1536), BF16),
        vmem((pe, 1536), BF16),
        vmem((n_dp, 8, 128), F32),
        vmem((40, 128), F32),
        vmem((ROWS, BOTTLE), F32),
        vmem((3, ROWS + 2 * PAD, BOTTLE), F32),
        vmem((2, ROWS, 9 * 128), BF16),
        vmem((ROWS, 512), F32),
        vmem((ROWS, 512), F32),
        vmem((ROWS, BOTTLE), BF16),
        vmem((ROWS, CHANNELS), F32),
        vmem((ROWS, CHANNELS), F32),
        vmem((ROWS, CHANNELS), BF16),
        vmem((ROWS, CHANNELS), BF16),
        vmem((ROWS, BOTTLE), F32),
        vmem((ROWS, 512), F32),
        vmem((ROWS, 512), BF16),
        vmem((ROWS + 2 * PAD, 2 * 9 * 128), F32),
        vmem((ROWS, BOTTLE), F32),
        vmem((ROWS, BOTTLE), BF16),
        vmem((n_dp, 2, 2, q1, BOTTLE), F32),
        vmem((n_dp, 2, qc, BOTTLE), F32),
        vmem((n_dp, pe, CHANNELS), F32),
        vmem((n_dp, pe, 512), F32),
    ]
    scratch += [vmem(shape, F32) for shape in STATS]
    scratch += [vmem((2 * n_rep,) + shape, F32) for shape in STATS]
    scratch += [vmem(shape, F32) for shape in STATS]
    scratch += [vmem((n_dp // 2,) + shape, F32) for shape in STATS]
    half = [(n_dp, 2, q1, BOTTLE), (n_dp, 2, qc, 128), (n_dp, pe, 512), (n_dp, pe, 256)]
    quarter = [(n_dp, q1, BOTTLE), (n_dp, qc, 128), (n_dp, pe, 256), (n_dp, pe, 128)]
    final = [(2, 2, q1, BOTTLE), (2, qc, BOTTLE), (pe, CHANNELS), (pe, 512)]
    sent = [BF16, BF16, BF16, F32]
    scratch += [vmem(shape, F32) for shape in half + quarter]
    scratch += [vmem(shape, kind) for shape, kind in zip(quarter, sent)] * 2
    scratch += [vmem(shape[1:], F32) for shape in quarter]
    scratch += [vmem(shape, F32) for shape in final]
    dma = pltpu.SemaphoreType.DMA
    scratch += [dma((4,))] + [dma((len(STATS),))] * 4 + [dma((2,))] + [dma((3, 4))] * 2 + [dma((4, 4))] * 2
    any_space = pl.BlockSpec(memory_space=pl.ANY)
    in_vmem = pl.BlockSpec(memory_space=pltpu.VMEM)
    block_out, images_grad, sum1, sumc, sum3, sume, norm_grads = pl.pallas_call(
        functools.partial(block_kernel, n_dp, n_rep),
        out_shape=[
            jax.ShapeDtypeStruct((ROWS, CHANNELS), BF16),
            jax.ShapeDtypeStruct((ROWS, CHANNELS), F32),
            *[jax.ShapeDtypeStruct(shape, F32) for shape in final],
            jax.ShapeDtypeStruct((40, 128), F32),
        ],
        in_specs=[any_space] * 2 + [in_vmem] * 6,
        out_specs=[any_space] * 2 + [in_vmem] * 5,
        scratch_shapes=scratch,
        compiler_params=pltpu.CompilerParams(
            collective_id=0, has_side_effects=True, vmem_limit_bytes=63 * 1024 * 1024
        ),
    )(
        by_pixel(images),
        by_pixel(out_grad),
        reduce_weight,
        conv_weight,
        squeeze_weight,
        expand_weight,
        project_weight,
        block,
    )
    states = (
        reduce_weight,
        reduce_moment,
        reduce_second,
        conv_weight,
        conv_moment,
        conv_second,
        squeeze_weight,
        squeeze_moment,
        squeeze_second,
        expand_weight,
        expand_moment,
        expand_second,
        project_weight,
        project_moment,
        project_second,
    )
    updated = pl.pallas_call(
        update_kernel,
        out_shape=[jax.ShapeDtypeStruct(state.shape, F32) for state in states],
        in_specs=[in_vmem] * 19,
        out_specs=[in_vmem] * 15,
        compiler_params=pltpu.CompilerParams(vmem_limit_bytes=32 * 1024 * 1024),
    )(
        sum1.reshape(reduce_weight.shape),
        sumc.reshape(conv_weight.shape),
        sum3,
        sume,
        *states,
    )
    norm_owned = lax.dynamic_slice_in_dim(norm_grads.reshape(-1), offset, shard)
    norm_new = adamw(norm_params, norm_moment, norm_second, norm_owned, NORM_RATE, 0.0)
    by_image = lambda values: jnp.transpose(
        values.reshape(SIDE, SIDE, images.shape[0], CHANNELS), (2, 0, 1, 3)
    )
    return (by_image(block_out), by_image(images_grad), *updated, *norm_new)


def solution(mesh):
    placed = (
        P(("dp", "rep"), None, None, None),
        P(("dp", "rep"), None, None, None),
        P("dp", None),
        P("dp", None),
        P("dp", None),
        P("dp", None),
        P("dp", None),
        P("dp", None),
        P("dp", None),
        P("dp", None),
        P("dp", None),
        P("dp", None),
        P("dp", None),
        P("dp", None),
        P("dp", None),
        P("dp", None),
        P("dp", None),
        P("dp"),
        P("dp"),
        P("dp"),
    )
    n_dp, n_rep = mesh.shape["dp"], mesh.shape["rep"]
    whole_tiles = n_rep == 4 and n_dp % 2 == 0 and INNER % (16 * n_dp) == 0
    return jax.shard_map(
        fused_device if whole_tiles else per_device,
        mesh=mesh,
        in_specs=placed,
        out_specs=(
            P(("dp", "rep"), None, None, None),
            P(("dp", "rep"), None, None, None),
            P("dp", None),
            P("dp", None),
            P("dp", None),
            P("dp", None),
            P("dp", None),
            P("dp", None),
            P("dp", None),
            P("dp", None),
            P("dp", None),
            P("dp", None),
            P("dp", None),
            P("dp", None),
            P("dp", None),
            P("dp", None),
            P("dp", None),
            P("dp"),
            P("dp"),
            P("dp"),
        ),
        check_vma=False,
    )
```

```python
import functools
import jax
import jax.numpy as jnp
from jax import lax
from jax.experimental import pallas as pl
from jax.experimental.pallas import tpu as pltpu
from jax.sharding import PartitionSpec as P

CHANNELS = 1024
BOTTLE = 256
INNER = 128
RADIX = 2
SIDE = 14
MICRO = 2
STEP = 10


EPSILON = 1e-05
PRECISE = lax.Precision.HIGHEST
BETA_ONE = 0.9
BETA_TWO = 0.999
ADAM_EPSILON = 1e-08
DECAY = 0.01
NORM_RATE = 0.8
ROWS = 4 * SIDE * SIDE
NORM_WIDTH = 4352


def split_params(packed):
    widths = (
        BOTTLE,
        BOTTLE,
        RADIX * BOTTLE,
        RADIX * BOTTLE,
        INNER,
        INNER,
        RADIX * BOTTLE,
        CHANNELS,
        CHANNELS,
    )
    pieces = []
    offset = 0
    for segment in widths:
        pieces.append(lax.slice_in_dim(packed, offset, offset + segment))
        offset = offset + segment
    return pieces


def silu_slope(values):
    logistic = jax.nn.sigmoid(values)
    return logistic * (1.0 + values * (1.0 - logistic))


def norm_forward(values, gain, bias, count):
    flat = values.reshape(-1, values.shape[-1])
    total, square = lax.psum((jnp.sum(flat, axis=0), jnp.sum(flat * flat, axis=0)), ("dp", "rep"))
    center = total / count
    scale = lax.rsqrt(square / count - center * center + EPSILON)
    normed = (values - center) * scale
    return (normed * gain + bias, normed, scale)


def norm_backward(upstream, normed, scale, gain, count):
    flat_up = upstream.reshape(-1, upstream.shape[-1])
    flat_norm = normed.reshape(-1, normed.shape[-1])
    bias_sum, gain_sum = lax.psum(
        (jnp.sum(flat_up, axis=0), jnp.sum(flat_up * flat_norm, axis=0)), ("dp", "rep")
    )
    downstream = gain * scale * (upstream - bias_sum / count - normed * (gain_sum / count))
    return (downstream, gain_sum, bias_sum)


def patches(active):
    padded = jnp.pad(active, ((0, 0), (1, 1), (1, 1), (0, 0), (0, 0)))
    shifted = [
        padded[:, down_step : down_step + SIDE, side_step : side_step + SIDE]
        for down_step in range(3)
        for side_step in range(3)
    ]
    return jnp.stack(shifted, axis=4)


def unpatch(columns):
    total = jnp.zeros(
        (columns.shape[0], SIDE + 2, SIDE + 2, columns.shape[3], columns.shape[5]), jnp.float32
    )
    for down_step in range(3):
        for side_step in range(3):
            piece = columns[:, :, :, :, 3 * down_step + side_step]
            total = total + jnp.pad(
                piece,
                ((0, 0), (down_step, 2 - down_step), (side_step, 2 - side_step), (0, 0), (0, 0)),
            )
    return total[:, 1 : SIDE + 1, 1 : SIDE + 1]


def adamw(param, moment, second, gradient, rate, decay):
    moment_new = BETA_ONE * moment + (1.0 - BETA_ONE) * gradient
    second_new = BETA_TWO * second + (1.0 - BETA_TWO) * gradient * gradient
    ratio = (
        moment_new
        / (1.0 - BETA_ONE**STEP)
        / (jnp.sqrt(second_new / (1.0 - BETA_TWO**STEP)) + ADAM_EPSILON)
    )
    return (param - rate * (ratio + decay * param), moment_new, second_new)


def per_device(
    images,
    out_grad,
    reduce_weight,
    reduce_moment,
    reduce_second,
    conv_weight,
    conv_moment,
    conv_second,
    squeeze_weight,
    squeeze_moment,
    squeeze_second,
    expand_weight,
    expand_moment,
    expand_second,
    project_weight,
    project_moment,
    project_second,
    norm_params,
    norm_moment,
    norm_second,
):
    bf16 = jnp.bfloat16
    low_reduce = reduce_weight.astype(bf16)
    low_conv = conv_weight.astype(bf16)
    low_squeeze = squeeze_weight.astype(bf16)
    low_expand = expand_weight.astype(bf16)
    low_project = project_weight.astype(bf16)
    low_norm = norm_params.astype(bf16)
    devices = lax.axis_size("dp") * lax.axis_size("rep")
    per_batch = images.shape[0] // MICRO
    pixel_count = float(per_batch * SIDE * SIDE * devices)
    image_count = float(per_batch * devices)
    group_in = BOTTLE // RADIX
    grad_first = jnp.zeros((CHANNELS, BOTTLE), jnp.float32)
    grad_conv = jnp.zeros((RADIX, 9 * group_in, BOTTLE), jnp.float32)
    grad_squeeze = jnp.zeros((BOTTLE, INNER), jnp.float32)
    grad_expand = jnp.zeros((INNER, RADIX * BOTTLE), jnp.float32)
    grad_last = jnp.zeros((BOTTLE, CHANNELS), jnp.float32)
    grad_norms = jnp.zeros(
        (2 * BOTTLE + 3 * RADIX * BOTTLE + 2 * INNER + 2 * CHANNELS,), jnp.float32
    )
    outputs = []
    input_grads = []
    for number in range(MICRO):
        forward_set = (
            lax.all_gather(low_reduce, "dp", axis=0, tiled=True),
            lax.all_gather(low_conv, "dp", axis=0, tiled=True),
            lax.all_gather(low_squeeze, "dp", axis=0, tiled=True),
            lax.all_gather(low_expand, "dp", axis=0, tiled=True),
            lax.all_gather(low_project, "dp", axis=0, tiled=True),
            lax.all_gather(low_norm, "dp", axis=0, tiled=True),
        )
        first, conv, squeeze, expand, last, packed = forward_set
        (
            gain_one,
            bias_one,
            gain_two,
            bias_two,
            gain_pool,
            bias_pool,
            bias_expand,
            gain_three,
            bias_three,
        ) = split_params(packed.astype(jnp.float32))
        batched = images[number * per_batch : (number + 1) * per_batch]
        cotangent = out_grad[number * per_batch : (number + 1) * per_batch]
        reduced = jnp.einsum("nhwc,cb->nhwb", batched, first, preferred_element_type=jnp.float32)
        norm_one, normed_one, scale_one = norm_forward(reduced, gain_one, bias_one, pixel_count)
        active = jax.nn.silu(norm_one).astype(bf16)
        columns = patches(active.reshape(per_batch, SIDE, SIDE, RADIX, group_in)).reshape(
            per_batch * SIDE * SIDE, RADIX, 9 * group_in
        )
        conv_grouped = conv.reshape(RADIX, 9 * group_in, BOTTLE)
        widened = jnp.einsum(
            "prk,rko->pro", columns, conv_grouped, preferred_element_type=jnp.float32
        )
        widened = widened.reshape(per_batch, SIDE, SIDE, RADIX * BOTTLE)
        norm_two, normed_two, scale_two = norm_forward(widened, gain_two, bias_two, pixel_count)
        splits = jax.nn.silu(norm_two).reshape(per_batch, SIDE, SIDE, RADIX, BOTTLE)
        pooled = jnp.sum(jnp.sum(splits, axis=3), axis=(1, 2)) / (SIDE * SIDE)
        squeeze_float = squeeze.astype(jnp.float32)
        expand_float = expand.astype(jnp.float32)
        pre_pool = jnp.dot(pooled, squeeze_float, precision=PRECISE)
        norm_pool, normed_pool, scale_pool = norm_forward(
            pre_pool, gain_pool, bias_pool, image_count
        )
        hidden = jax.nn.silu(norm_pool)
        logits = (jnp.dot(hidden, expand_float, precision=PRECISE) + bias_expand).reshape(
            per_batch, RADIX, BOTTLE
        )
        attention = jax.nn.softmax(logits, axis=1)
        mixed = jnp.sum(splits * attention[:, None, None], axis=3).astype(bf16)
        projected = jnp.einsum("nhwb,bc->nhwc", mixed, last, preferred_element_type=jnp.float32)
        norm_three, normed_three, scale_three = norm_forward(
            projected, gain_three, bias_three, pixel_count
        )
        summed = batched.astype(jnp.float32) + norm_three
        outputs.append(jax.nn.silu(summed).astype(bf16))
        backward_set = (
            lax.all_gather(low_reduce, "dp", axis=0, tiled=True),
            lax.all_gather(low_conv, "dp", axis=0, tiled=True),
            lax.all_gather(low_squeeze, "dp", axis=0, tiled=True),
            lax.all_gather(low_expand, "dp", axis=0, tiled=True),
            lax.all_gather(low_project, "dp", axis=0, tiled=True),
            lax.all_gather(low_norm, "dp", axis=0, tiled=True),
        )
        first, conv, squeeze, expand, last, packed = backward_set
        gains_back = split_params(packed.astype(jnp.float32))
        conv_grouped = conv.reshape(RADIX, 9 * group_in, BOTTLE)
        expand_float = expand.astype(jnp.float32)
        squeeze_float = squeeze.astype(jnp.float32)
        upstream = cotangent.astype(jnp.float32) * silu_slope(summed)
        d_projected, gain_three_grad, bias_three_grad = norm_backward(
            upstream, normed_three, scale_three, gains_back[7], pixel_count
        )
        d_projected_low = d_projected.astype(bf16)
        grad_last = grad_last + jnp.einsum(
            "nhwb,nhwc->bc", mixed, d_projected_low, preferred_element_type=jnp.float32
        )
        d_mixed = jnp.einsum(
            "nhwc,bc->nhwb", d_projected_low, last, preferred_element_type=jnp.float32
        )
        d_splits = d_mixed[:, :, :, None] * attention[:, None, None]
        d_attention = jnp.sum(d_mixed[:, :, :, None] * splits, axis=(1, 2))
        d_logits = attention * (
            d_attention - jnp.sum(attention * d_attention, axis=1, keepdims=True)
        )
        flat_logits = d_logits.reshape(per_batch, RADIX * BOTTLE)
        grad_expand = grad_expand + jnp.dot(hidden.T, flat_logits, precision=PRECISE)
        d_hidden = jnp.dot(flat_logits, expand_float.T, precision=PRECISE)
        d_pool_norm = d_hidden * silu_slope(norm_pool)
        pool_bias_sum, pool_gain_sum, expand_bias_sum = lax.psum(
            (
                jnp.sum(d_pool_norm, axis=0),
                jnp.sum(d_pool_norm * normed_pool, axis=0),
                jnp.sum(flat_logits, axis=0),
            ),
            ("dp", "rep"),
        )
        d_pre_pool = (
            gains_back[4]
            * scale_pool
            * (
                d_pool_norm
                - pool_bias_sum / image_count
                - normed_pool * (pool_gain_sum / image_count)
            )
        )
        grad_squeeze = grad_squeeze + jnp.dot(pooled.T, d_pre_pool, precision=PRECISE)
        d_pooled = jnp.dot(d_pre_pool, squeeze_float.T, precision=PRECISE)
        d_splits = d_splits + (d_pooled / (SIDE * SIDE))[:, None, None, None, :]
        d_norm_two = d_splits.reshape(per_batch, SIDE, SIDE, RADIX * BOTTLE) * silu_slope(norm_two)
        d_widened, gain_two_grad, bias_two_grad = norm_backward(
            d_norm_two, normed_two, scale_two, gains_back[2], pixel_count
        )
        d_widened_low = d_widened.astype(bf16).reshape(per_batch * SIDE * SIDE, RADIX, BOTTLE)
        grad_conv = grad_conv + jnp.einsum(
            "prk,pro->rko", columns, d_widened_low, preferred_element_type=jnp.float32
        )
        d_columns = jnp.einsum(
            "pro,rko->prk", d_widened_low, conv_grouped, preferred_element_type=jnp.float32
        )
        d_active = unpatch(d_columns.reshape(per_batch, SIDE, SIDE, RADIX, 9, group_in)).reshape(
            per_batch, SIDE, SIDE, BOTTLE
        )
        d_norm_one = d_active * silu_slope(norm_one)
        d_reduced, gain_one_grad, bias_one_grad = norm_backward(
            d_norm_one, normed_one, scale_one, gains_back[0], pixel_count
        )
        d_reduced_low = d_reduced.astype(bf16)
        grad_first = grad_first + jnp.einsum(
            "nhwc,nhwb->cb", batched, d_reduced_low, preferred_element_type=jnp.float32
        )
        input_grads.append(
            upstream
            + jnp.einsum("nhwb,cb->nhwc", d_reduced_low, first, preferred_element_type=jnp.float32)
        )
        grad_norms = grad_norms + jnp.concatenate(
            [
                gain_one_grad,
                bias_one_grad,
                gain_two_grad,
                bias_two_grad,
                pool_gain_sum,
                pool_bias_sum,
                expand_bias_sum,
                gain_three_grad,
                bias_three_grad,
            ]
        )
    grad_conv = grad_conv.reshape(9 * BOTTLE, BOTTLE)
    partial_value = (
        lax.psum_scatter(grad_first, "dp", scatter_dimension=0, tiled=True),
        lax.psum_scatter(grad_conv, "dp", scatter_dimension=0, tiled=True),
        lax.psum_scatter(grad_squeeze, "dp", scatter_dimension=0, tiled=True),
        lax.psum_scatter(grad_expand, "dp", scatter_dimension=0, tiled=True),
        lax.psum_scatter(grad_last, "dp", scatter_dimension=0, tiled=True),
    )
    owned = lax.psum(
        (partial_value[0], partial_value[1], partial_value[2], partial_value[3], partial_value[4]),
        "rep",
    )
    shard_length = norm_params.shape[0]
    norm_grad_owned = lax.dynamic_slice_in_dim(
        grad_norms, lax.axis_index("dp") * shard_length, shard_length
    )
    reduce_new = adamw(
        reduce_weight, reduce_moment, reduce_second, owned[0], 2.0 * CHANNELS ** (-0.5), DECAY
    )
    conv_new = adamw(
        conv_weight,
        conv_moment,
        conv_second,
        owned[1],
        2.0 * (9 * BOTTLE // RADIX) ** (-0.5),
        DECAY,
    )
    squeeze_new = adamw(
        squeeze_weight, squeeze_moment, squeeze_second, owned[2], 2.0 * BOTTLE ** (-0.5), DECAY
    )
    expand_new = adamw(
        expand_weight, expand_moment, expand_second, owned[3], 2.0 * (INNER // 8) ** (-0.5), DECAY
    )
    project_new = adamw(
        project_weight, project_moment, project_second, owned[4], 2.0 * BOTTLE ** (-0.5), DECAY
    )
    norm_new = adamw(norm_params, norm_moment, norm_second, norm_grad_owned, NORM_RATE, 0.0)
    return (
        jnp.concatenate(outputs, axis=0),
        jnp.concatenate(input_grads, axis=0),
        reduce_new[0],
        reduce_new[1],
        reduce_new[2],
        conv_new[0],
        conv_new[1],
        conv_new[2],
        squeeze_new[0],
        squeeze_new[1],
        squeeze_new[2],
        expand_new[0],
        expand_new[1],
        expand_new[2],
        project_new[0],
        project_new[1],
        project_new[2],
        norm_new[0],
        norm_new[1],
        norm_new[2],
    )


MESH = pl.DeviceIdType.MESH
PAD = 64
CHUNK = 112
F32 = jnp.float32
BF16 = jnp.bfloat16
STATS = ((8, 128), (8, 256), (8, 128), (8, 512), (8, 512), (16, 128), (8, 256), (8, 128))


def sigmoid(values):
    return 0.5 * jnp.tanh(0.5 * values) + 0.5


def row_ids(width):
    return lax.broadcasted_iota(jnp.int32, (8, width), 0)


def image_sum(rows):
    return rows + pltpu.roll(rows, 4, 0)


def pair_sum(rows):
    even = row_ids(rows.shape[1]) % 2 == 0
    return rows + jnp.where(even, pltpu.roll(rows, 7, 0), pltpu.roll(rows, 1, 0))


def micro_sum(rows):
    return pair_sum(image_sum(rows))


def stack_sums(first, second):
    return jnp.where(row_ids(first.shape[1]) < 4, first, second)


def unstack_sums(stacked):
    upper = row_ids(stacked.shape[1]) < 4
    turned = pltpu.roll(stacked, 4, 0)
    return jnp.where(upper, stacked, turned), jnp.where(upper, turned, stacked)


def fold_lanes(stacked):
    half = stacked.shape[1] // 2
    even = row_ids(half) % 2 == 0
    return jnp.where(even, stacked[:, :half], stacked[:, half:])


def unfold_lanes(folded):
    even = row_ids(folded.shape[1]) % 2 == 0
    left = jnp.where(even, folded, pltpu.roll(folded, 1, 0))
    right = jnp.where(even, pltpu.roll(folded, 7, 0), folded)
    return jnp.concatenate([left, right], axis=1)


def norm_terms(total, square, gain, bias, count):
    center = total / count
    scale = lax.rsqrt(square / count - center * center + EPSILON)
    slope = scale * gain
    return center, scale, slope, bias - center * slope


def back_terms(center, scale, slope, bias_sum, gain_sum, count):
    by_value = -slope * scale * (gain_sum / count)
    constant = -slope * (bias_sum / count) - by_value * center
    return by_value, constant


def tdot(left, right):
    return lax.dot_general(left, right, (((0,), (0,)), ((), ())), preferred_element_type=F32)


def dot_t(left, right):
    return lax.dot_general(left, right, (((1,), (1,)), ((), ())), preferred_element_type=F32)


def block_kernel(
    n_dp,
    n_rep,
    x_hbm,
    gy_hbm,
    w1_own,
    wc_own,
    sq_own,
    ex_own,
    w3_own,
    np_own,
    bo_hbm,
    dx_hbm,
    f1_out,
    fc_out,
    f3_out,
    fe_out,
    gn_out,
    x4,
    gy4,
    x_v,
    gy_v,
    fw1,
    fwc,
    fpe,
    pe_own,
    np_slots,
    np_full,
    red,
    act,
    columns,
    wid,
    splits,
    mixed,
    proj,
    up,
    bo4,
    dx4,
    dproj,
    d_mixed,
    dn2,
    dwid,
    dcol,
    dn1,
    dred,
    g1,
    gc,
    g3,
    ge,
    *rest,
):
    n_ar = len(STATS)
    ar_slots_a = rest[0:n_ar]
    ar_slots_b = rest[n_ar : 2 * n_ar]
    rest = rest[2 * n_ar :]
    r1s, r2s, ks, r3s, own, fs = (rest[4 * i : 4 * i + 4] for i in range(6))
    rest = rest[24:]
    local_sem, ar_send_a, ar_recv_a, ar_send_b, ar_recv_b, np_sems, ws, wr, gs, gr = rest

    dp = lax.axis_index("dp")
    rep = lax.axis_index("rep")
    core = lax.rem(rep, 2)
    half_y = rep // 2
    planes = n_dp // 2
    plane_size = 2 * n_rep
    plane = dp // 2
    in_plane = lax.rem(dp, 2) * n_rep + rep
    sibling = (dp, half_y * 2 + (1 - core))
    across = (dp, (1 - half_y) * 2 + core)
    pixels = float(SIDE * SIDE * 2 * n_dp * n_rep)
    pictures = float(2 * n_dp * n_rep)

    in_planes = [lax.rem(in_plane + step, plane_size) for step in range(1, plane_size)]
    plane_peers = [(plane * 2 + other // n_rep, lax.rem(other, n_rep)) for other in in_planes]
    column_peers = [
        (lax.rem(plane + step, planes) * 2 + lax.rem(dp, 2), rep) for step in range(1, planes)
    ]
    owner_peers = [(lax.rem(dp + step, n_dp), rep) for step in range(1, n_dp)]
    rep_peers = [(dp, lax.rem(rep + step, n_rep)) for step in range(1, n_rep)]

    def remote(src, dst, send_sem, recv_sem, device):
        return pltpu.make_async_remote_copy(
            src_ref=src,
            dst_ref=dst,
            send_sem=send_sem,
            recv_sem=recv_sem,
            device_id=device,
            device_id_type=MESH,
        )

    def send_all(ref, send_sem, recv_sem, peers):
        for device in peers:
            remote(ref, ref, send_sem, recv_sem, device).start()

    def wait_bytes(ref, sem):
        pltpu.make_async_copy(ref, ref, sem).wait()

    def over_rows(body, init):
        def step(index, carry):
            return body(pl.multiple_of(index * CHUNK, CHUNK), carry)

        return lax.fori_loop(0, ROWS // CHUNK, step, init)

    def grouped(values):
        return values.reshape(CHUNK // 8, 8, values.shape[-1])

    def by_four(values):
        return flat(values).reshape(CHUNK // 4, 4, values.shape[-1])

    def flat(values):
        return values.reshape(CHUNK, values.shape[-1])

    x_copy = pltpu.make_async_copy(x_hbm, x4, local_sem.at[0])
    gy_copy = pltpu.make_async_copy(gy_hbm, gy4, local_sem.at[1])
    x_copy.start()
    barrier = pltpu.get_barrier_semaphore()
    for device in plane_peers + owner_peers:
        pl.semaphore_signal(barrier, inc=1, device_id=device, device_id_type=MESH)

    part = core * 2 + half_y
    q1 = w1_own.shape[0] // 4
    fw1[dp, core, half_y] = w1_own[pl.ds(pl.multiple_of(part * q1, q1), q1), :].astype(BF16)
    qc = wc_own.shape[0] // 2
    core_lanes = pl.ds(pl.multiple_of(core * 128, 128), 128)
    fwc[dp, half_y, :, core_lanes] = wc_own[
        pl.ds(pl.multiple_of(half_y * qc, qc), qc), core_lanes
    ].astype(BF16)
    ex_rows = ex_own.shape[0]
    pe_own[:, 0:CHANNELS] = w3_own[...].astype(BF16)
    pe_own[:, 1024:1152] = sq_own[...].astype(BF16)
    pe_own[0:ex_rows, 1152:1408] = ex_own[:, 0:256].astype(BF16)
    pe_own[ex_rows : 2 * ex_rows, 1152:1408] = ex_own[:, 256:512].astype(BF16)
    pe_own[:, 1408:1536] = jnp.zeros((2 * ex_rows, 128), BF16)
    pe_lanes = pl.ds(pl.multiple_of(part * 384, 128), 384)
    fpe[dp, :, pe_lanes] = pe_own[:, pe_lanes]
    shard = np_own.shape[1]
    lanes_id = lax.broadcasted_iota(jnp.int32, (8, 128), 1)
    turn = lax.rem(shard * dp, 128)
    full_rows = shard // 128
    flat_np = np_own[...].astype(BF16).astype(F32)
    np_rows = [flat_np[:, k * 128 : k * 128 + 128] for k in range(full_rows)]
    if shard % 128:
        tail = flat_np[:, full_rows * 128 : shard]
        np_rows.append(jnp.concatenate([tail, jnp.zeros((1, 128 - shard % 128), F32)], axis=1))
    np_rows.append(jnp.zeros((8 - len(np_rows), 128), F32))
    turned = pltpu.roll(jnp.concatenate(np_rows, axis=0), turn, 1)
    np_slots[dp] = jnp.where(lanes_id < turn, pltpu.roll(turned, 1, 0), turned)
    gy_copy.start()

    pl.semaphore_wait(barrier, plane_size + n_dp - 2)

    def quarter_w1(c, y):
        return fw1.at[:, c, y]

    def quarter_wc(c, y):
        return fwc.at[:, y, :, pl.ds(pl.multiple_of(c * 128, 128), 128)]

    def quarter_pe(c, y):
        return fpe.at[:, :, pl.ds(pl.multiple_of((c * 2 + y) * 384, 128), 384)]

    quarters = (quarter_w1, quarter_wc, quarter_pe)

    def piece(which, d):
        return (
            fw1.at[d, core, half_y],
            fwc.at[d, half_y, :, core_lanes],
            fpe.at[d, :, pe_lanes],
        )[which]

    def seven(which):
        return (
            fw1.at[pl.ds(0, n_dp - 1), core, half_y],
            fwc.at[pl.ds(0, n_dp - 1), half_y, :, core_lanes],
            fpe.at[pl.ds(0, n_dp - 1), :, pe_lanes],
        )[which]

    def gather_out(which):
        send_all(piece(which, dp), ws.at[which, 0], wr.at[which, 0], owner_peers)

    def gather_turn(which):
        wait_bytes(seven(which), wr.at[which, 0])
        mine = quarters[which](core, half_y)
        remote(mine, mine, ws.at[which, 1], wr.at[which, 1], across).start()
        remote(mine, mine, ws.at[which, 2], wr.at[which, 2], sibling).start()

    def gather_hand(which):
        theirs = quarters[which](core, 1 - half_y)
        wait_bytes(theirs, wr.at[which, 1])
        remote(theirs, theirs, ws.at[which, 3], wr.at[which, 3], sibling).start()

    def gather_end(which):
        wait_bytes(quarters[which](1 - core, half_y), wr.at[which, 2])
        wait_bytes(quarters[which](1 - core, 1 - half_y), wr.at[which, 3])

    def to_rows(source, target):
        def body(index, carry):
            values = source[pl.ds(index * (CHUNK // 4), CHUNK // 4)].astype(F32)
            row = pl.multiple_of(index * CHUNK, CHUNK)
            target[pl.ds(row, CHUNK), :] = values.reshape(CHUNK, CHANNELS).astype(BF16)
            return carry

        lax.fori_loop(0, ROWS // CHUNK, body, 0)

    gather_out(0)
    send_all(np_slots.at[dp], np_sems.at[0], np_sems.at[1], owner_peers)
    x_copy.wait()
    to_rows(x4, x_v)
    gather_turn(0)
    gather_out(1)
    zero_rows = jnp.zeros((PAD, BOTTLE), F32)
    for side in range(3):
        act[side, 0:PAD, :] = zero_rows
        act[side, PAD + ROWS : 2 * PAD + ROWS, :] = zero_rows
    for lane_block in range(9):
        dcol[0:PAD, lane_block * 256 : lane_block * 256 + 256] = zero_rows
        dcol[PAD + ROWS : 2 * PAD + ROWS, lane_block * 256 : lane_block * 256 + 256] = zero_rows
    gather_hand(0)

    def sum_start(k, payload):
        ar_slots_a[k][in_plane] = payload
        send_all(ar_slots_a[k].at[in_plane], ar_send_a.at[k], ar_recv_a.at[k], plane_peers)

    def sum_turn(k):
        wait_bytes(ar_slots_a[k].at[pl.ds(0, plane_size - 1)], ar_recv_a.at[k])
        part_sum = ar_slots_a[k][0]
        for slot in range(1, plane_size):
            part_sum = part_sum + ar_slots_a[k][slot]
        ar_slots_b[k][plane] = part_sum
        send_all(ar_slots_b[k].at[plane], ar_send_b.at[k], ar_recv_b.at[k], column_peers)

    def sum_end(k):
        wait_bytes(ar_slots_b[k].at[pl.ds(0, planes - 1)], ar_recv_b.at[k])
        whole = ar_slots_b[k][0]
        for slot in range(1, planes):
            whole = whole + ar_slots_b[k][slot]
        return whole

    def lanes_of(index, width):
        return pl.ds(pl.multiple_of(index * width, 128), width)

    def half_of(which, ref, c):
        if which == 0:
            return ref.at[:, c]
        if which == 1:
            return ref.at[:, :, :, lanes_of(c, 128)]
        return ref.at[:, :, lanes_of(c, (512, 256)[which - 2])]

    def quarter_of(which, ref, c, y):
        if which == 0:
            return ref.at[:, c, y]
        if which == 1:
            return ref.at[:, y, :, lanes_of(c, 128)]
        return ref.at[:, :, lanes_of(c * 2 + y, (256, 128)[which - 2])]

    def final_part(which, c, y):
        if which == 0:
            return fs[0].at[c, y]
        if which == 1:
            return fs[1].at[y, :, lanes_of(c, 128)]
        return fs[which].at[:, lanes_of(c * 2 + y, (256, 128)[which - 2])]

    grads = (g1, gc, g3, ge)

    def reduce_core(which):
        remote(
            half_of(which, grads[which], 1 - core),
            r1s[which],
            gs.at[which, 0],
            gr.at[which, 0],
            sibling,
        ).start()

    def reduce_y(which):
        wait_bytes(r1s[which], gr.at[which, 0])
        mine = half_of(which, grads[which], core)

        def add(d, carry):
            mine[d] = mine[d] + r1s[which][d]
            return carry

        lax.fori_loop(0, n_dp, add, 0)
        remote(
            quarter_of(which, grads[which], core, 1 - half_y),
            r2s[which],
            gs.at[which, 1],
            gr.at[which, 1],
            across,
        ).start()

    def reduce_owner(which):
        wait_bytes(r2s[which], gr.at[which, 1])
        mine = quarter_of(which, grads[which], core, half_y)

        def add(d, carry):
            ks[which][d] = (mine[d] + r2s[which][d]).astype(ks[which].dtype)
            return carry

        lax.fori_loop(0, n_dp, add, 0)
        own[which][...] = mine[dp] + r2s[which][dp]
        r3s[which][dp] = jnp.zeros(own[which].shape, r3s[which].dtype)

        for device in owner_peers:
            remote(
                ks[which].at[device[0]],
                r3s[which].at[dp],
                gs.at[which, 2],
                gr.at[which, 2],
                device,
            ).start()

    def reduce_spread(which):
        wait_bytes(r3s[which].at[pl.ds(0, n_dp - 1)], gr.at[which, 2])
        total = own[which][...]
        for slot in range(n_dp):
            total = total + r3s[which][slot].astype(F32)
        mine = final_part(which, core, half_y)
        mine[...] = total
        send_all(mine, gs.at[which, 3], gr.at[which, 3], rep_peers)

    def three_parts(which):
        return r2s[which].at[pl.ds(0, 3)]

    def reduce_end(which):
        wait_bytes(three_parts(which), gr.at[which, 3])

    gather_end(0)
    red[...] = jnp.dot(x_v[...], fw1[...].reshape(CHANNELS, BOTTLE), preferred_element_type=F32)

    def sums_of(ref, start, width):
        def body(row, carry):
            values = grouped(ref[pl.ds(row, CHUNK), start : start + width])
            return carry[0] + jnp.sum(values, axis=0), carry[1] + jnp.sum(values * values, axis=0)

        zero = jnp.zeros((8, width), F32)
        return over_rows(body, (zero, zero))

    def wide_sums(ref, width):
        found = [sums_of(ref, start, 256) for start in range(0, width, 256)]
        first = jnp.concatenate([item[0] for item in found], axis=1)
        second = jnp.concatenate([item[1] for item in found], axis=1)
        return fold_lanes(stack_sums(micro_sum(first), micro_sum(second)))

    sum_start(0, wide_sums(red, BOTTLE))

    gy_copy.wait()
    to_rows(gy4, gy_v)
    wait_bytes(np_slots.at[pl.ds(0, n_dp - 1)], np_sems.at[1])
    np_full[...] = jnp.zeros(np_full.shape, F32)
    for d in range(n_dp):
        at = shard * d // 128
        np_full[at : at + 8, :] = np_full[at : at + 8, :] + np_slots[d]

    def vector(at, width):
        rows = [np_full[at // 128 + k : at // 128 + k + 1, :] for k in range(width // 128)]
        return jnp.concatenate(rows, axis=1) if len(rows) > 1 else rows[0]

    gain_one, bias_one = vector(0, 256), vector(256, 256)
    gain_two, bias_two = vector(512, 512), vector(1024, 512)
    gain_pool, bias_pool = vector(1536, 128), vector(1664, 128)
    bias_expand = vector(1792, 512)
    gain_three, bias_three = vector(2304, 1024), vector(3328, 1024)

    sum_turn(0)
    gather_turn(1)
    gather_out(2)
    total, square = unstack_sums(unfold_lanes(sum_end(0)))
    center1, scale1, mul1, add1 = norm_terms(total, square, gain_one, bias_one, pixels)

    def make_active(row, carry):
        turned = grouped(red[pl.ds(row, CHUNK), :]) * mul1 + add1
        act[1, pl.ds(PAD + row, CHUNK), :] = flat(turned * sigmoid(turned))
        return carry

    over_rows(make_active, 0)
    gather_hand(1)
    place = lax.rem(lax.broadcasted_iota(jnp.int32, (CHUNK, BOTTLE), 0) // 4, SIDE)
    not_last = place != SIDE - 1
    not_first = place != 0

    def beside(side, row, distance):
        near = act[side, pl.ds(PAD + row - 8, CHUNK + 16), :]
        return pltpu.roll(near, (CHUNK + 16 - distance) % (CHUNK + 16), 0)[8 : 8 + CHUNK]

    def shift_active(row, carry):
        act[2, pl.ds(PAD + row, CHUNK), :] = jnp.where(not_last, beside(1, row, 4), 0.0)
        act[0, pl.ds(PAD + row, CHUNK), :] = jnp.where(not_first, beside(1, row, -4), 0.0)
        return carry

    over_rows(shift_active, 0)

    def make_columns(row, carry):
        for tap in range(9):
            down, side = tap // 3 - 1, tap % 3
            values = act[side, pl.ds(PAD + row + 56 * down, CHUNK), :].astype(BF16)
            columns[0, pl.ds(row, CHUNK), tap * 128 : tap * 128 + 128] = values[:, 0:128]
            columns[1, pl.ds(row, CHUNK), tap * 128 : tap * 128 + 128] = values[:, 128:256]
        return carry

    over_rows(make_columns, 0)
    gather_end(1)
    own_half = n_dp // 2

    def filters(group):
        return fwc[group * own_half : (group + 1) * own_half].reshape(9 * 128, BOTTLE)

    for group in range(2):
        wid[:, group * 256 : group * 256 + 256] = jnp.dot(
            columns[group], filters(group), preferred_element_type=F32
        )
    sum_start(1, wide_sums(wid, 512))
    gather_turn(2)
    sum_turn(1)
    gather_hand(2)
    total, square = unstack_sums(unfold_lanes(sum_end(1)))
    center2, scale2, mul2, add2 = norm_terms(total, square, gain_two, bias_two, pixels)

    def make_splits(row, carry):
        found = []
        for group in range(2):
            lanes = slice(group * 256, group * 256 + 256)
            turned = grouped(wid[pl.ds(row, CHUNK), lanes]) * mul2[:, lanes] + add2[:, lanes]
            values = turned * sigmoid(turned)
            splits[pl.ds(row, CHUNK), lanes] = flat(values)
            found.append(jnp.sum(values, axis=0))
        return carry + found[0] + found[1]

    pooled = image_sum(over_rows(make_splits, jnp.zeros((8, BOTTLE), F32))) / (SIDE * SIDE)
    gather_end(2)
    last = fpe[:, :, 0:CHANNELS].reshape(BOTTLE, CHANNELS)
    squeeze = fpe[:, :, 1024:1152].reshape(BOTTLE, INNER).astype(F32)
    ex_both = fpe[:, :, 1152:1408]
    expand = jnp.concatenate(
        [
            ex_both[:, 0:ex_rows].reshape(INNER, 256),
            ex_both[:, ex_rows : 2 * ex_rows].reshape(INNER, 256),
        ],
        axis=1,
    ).astype(F32)
    pre_pool = jnp.dot(pooled, squeeze, precision=PRECISE, preferred_element_type=F32)
    sum_start(2, stack_sums(pair_sum(pre_pool), pair_sum(pre_pool * pre_pool)))
    sum_turn(2)
    total, square = unstack_sums(sum_end(2))
    center_p, scale_p, mul_p, add_p = norm_terms(total, square, gain_pool, bias_pool, pictures)
    normed_p = (pre_pool - center_p) * scale_p
    norm_p = pre_pool * mul_p + add_p
    gate_p = sigmoid(norm_p)
    hidden = norm_p * gate_p
    slope_p = gate_p * (1.0 + norm_p * (1.0 - gate_p))
    logits = jnp.dot(hidden, expand, precision=PRECISE, preferred_element_type=F32) + bias_expand
    left, right = logits[:, 0:256], logits[:, 256:512]
    most = jnp.maximum(left, right)
    left, right = jnp.exp(left - most), jnp.exp(right - most)
    att0 = left / (left + right)
    att1 = right / (left + right)

    def make_mixed(row, carry):
        rows = pl.ds(row, CHUNK)
        values = grouped(splits[rows, 0:256]) * att0 + grouped(splits[rows, 256:512]) * att1
        mixed[rows, :] = flat(values).astype(BF16)
        return carry

    over_rows(make_mixed, 0)
    proj[...] = jnp.dot(mixed[...], last, preferred_element_type=F32)
    sum_start(3, wide_sums(proj, CHANNELS))
    sum_turn(3)
    total, square = unstack_sums(unfold_lanes(sum_end(3)))
    center3, scale3, mul3, add3 = norm_terms(total, square, gain_three, bias_three, pixels)

    found = []
    for start in range(0, CHANNELS, 256):
        lanes = slice(start, start + 256)
        m3, a3, c3, s3 = mul3[:, lanes], add3[:, lanes], center3[:, lanes], scale3[:, lanes]

        def make_out(row, carry):
            rows = pl.ds(row, CHUNK)
            values = grouped(proj[rows, lanes])
            summed = grouped(x_v[rows, lanes].astype(F32)) + (values * m3 + a3)
            gate = sigmoid(summed)
            bo4[pl.ds(row // 4, CHUNK // 4), :, lanes] = by_four(summed * gate).astype(BF16)
            upstream = grouped(gy_v[rows, lanes].astype(F32)) * (
                gate * (1.0 + summed * (1.0 - gate))
            )
            up[rows, lanes] = flat(upstream)
            normed = (values - c3) * s3
            return carry[0] + jnp.sum(upstream, axis=0), carry[1] + jnp.sum(
                upstream * normed, axis=0
            )

        zero = jnp.zeros((8, 256), F32)
        found.append(over_rows(make_out, (zero, zero)))
    bias_sum = micro_sum(jnp.concatenate([item[0] for item in found], axis=1))
    gain_sum = micro_sum(jnp.concatenate([item[1] for item in found], axis=1))
    sum_start(4, fold_lanes(stack_sums(bias_sum, gain_sum)))
    bo_copy = pltpu.make_async_copy(bo4, bo_hbm, local_sem.at[2])
    bo_copy.start()

    def write_norm(at, pattern):
        both = pattern[0:1, :] + pattern[2:3, :]
        for k in range(both.shape[1] // 128):
            np_full[at // 128 + k : at // 128 + k + 1, :] = both[:, k * 128 : k * 128 + 128]

    sum_turn(4)
    bias_sum, gain_sum = unstack_sums(unfold_lanes(sum_end(4)))
    write_norm(2304, gain_sum)
    write_norm(3328, bias_sum)
    by_value, constant = back_terms(center3, scale3, mul3, bias_sum, gain_sum, pixels)
    for start in range(0, CHANNELS, 256):
        lanes = slice(start, start + 256)
        m3, v3, k3 = mul3[:, lanes], by_value[:, lanes], constant[:, lanes]

        def make_dproj(row, carry):
            rows = pl.ds(row, CHUNK)
            values = grouped(up[rows, lanes]) * m3 + grouped(proj[rows, lanes]) * v3 + k3
            dproj[rows, lanes] = flat(values).astype(BF16)
            return carry

        over_rows(make_dproj, 0)

    d_mixed[...] = dot_t(dproj[...], last)

    def attend(row, carry):
        rows = pl.ds(row, CHUNK)
        values = grouped(d_mixed[rows, :])
        return (
            carry[0] + jnp.sum(values * grouped(splits[rows, 0:256]), axis=0),
            carry[1] + jnp.sum(values * grouped(splits[rows, 256:512]), axis=0),
        )

    zero = jnp.zeros((8, 256), F32)
    d_att0, d_att1 = over_rows(attend, (zero, zero))
    d_att0, d_att1 = image_sum(d_att0), image_sum(d_att1)
    both = att0 * d_att0 + att1 * d_att1
    d_logits = jnp.concatenate([att0 * (d_att0 - both), att1 * (d_att1 - both)], axis=1)
    d_hidden = lax.dot_general(
        d_logits, expand, (((1,), (1,)), ((), ())), precision=PRECISE, preferred_element_type=F32
    )
    d_pool = d_hidden * slope_p
    per_micro = stack_sums(pair_sum(d_pool), pair_sum(d_pool * normed_p))
    ex_sum = pair_sum(d_logits)
    ex_sum = ex_sum + pltpu.roll(ex_sum, 2, 0)
    ids = row_ids(128)
    ex_rows_sum = jnp.where(ids == 0, ex_sum[:, 0:128], 0.0)
    for k in range(1, 4):
        ex_rows_sum = ex_rows_sum + jnp.where(ids == k, ex_sum[:, k * 128 : k * 128 + 128], 0.0)
    sum_start(5, jnp.concatenate([per_micro, ex_rows_sum], axis=0))

    once = row_ids(INNER) < 4
    grad_ex = lax.dot_general(
        jnp.where(once, hidden, 0.0),
        d_logits,
        (((0,), (0,)), ((), ())),
        precision=PRECISE,
        preferred_element_type=F32,
    )
    grad_ex = grad_ex.reshape(n_dp, ex_rows, 512)
    ge[:, 0:ex_rows, 128:384] = grad_ex[:, :, 0:256]
    ge[:, ex_rows : 2 * ex_rows, 128:384] = grad_ex[:, :, 256:512]
    ge[:, :, 384:512] = jnp.zeros((n_dp, 2 * ex_rows, 128), F32)
    g3[...] = tdot(mixed[...], dproj[...]).reshape(g3.shape)
    reduce_core(2)
    sum_turn(5)
    whole = sum_end(5)
    pool_bias_sum, pool_gain_sum = unstack_sums(whole[0:8])
    write_norm(1536, pool_gain_sum)
    write_norm(1664, pool_bias_sum)
    np_full[14:18, :] = whole[8:12]
    d_pre_pool = mul_p * (
        d_pool - pool_bias_sum / pictures - normed_p * (pool_gain_sum / pictures)
    )
    d_pooled = lax.dot_general(
        d_pre_pool, squeeze, (((1,), (1,)), ((), ())), precision=PRECISE, preferred_element_type=F32
    ) / (SIDE * SIDE)
    found = []
    for group, att in ((0, att0), (1, att1)):
        lanes = slice(group * 256, group * 256 + 256)
        m2, a2, c2, s2 = mul2[:, lanes], add2[:, lanes], center2[:, lanes], scale2[:, lanes]

        def make_dn2(row, carry):
            rows = pl.ds(row, CHUNK)
            values = grouped(wid[rows, lanes])
            turned = values * m2 + a2
            gate = sigmoid(turned)
            slope = gate * (1.0 + turned * (1.0 - gate))
            down = (grouped(d_mixed[rows, :]) * att + d_pooled) * slope
            dn2[rows, lanes] = flat(down)
            normed = (values - c2) * s2
            return carry[0] + jnp.sum(down, axis=0), carry[1] + jnp.sum(down * normed, axis=0)

        found.append(over_rows(make_dn2, (zero, zero)))
    bias_sum = micro_sum(jnp.concatenate([item[0] for item in found], axis=1))
    gain_sum = micro_sum(jnp.concatenate([item[1] for item in found], axis=1))
    sum_start(6, fold_lanes(stack_sums(bias_sum, gain_sum)))
    ge[:, :, 0:128] = lax.dot_general(
        jnp.where(row_ids(BOTTLE) < 4, pooled, 0.0),
        d_pre_pool,
        (((0,), (0,)), ((), ())),
        precision=PRECISE,
        preferred_element_type=F32,
    ).reshape(n_dp, 2 * ex_rows, 128)
    reduce_core(3)
    sum_turn(6)
    reduce_y(2)
    reduce_y(3)
    bias_sum, gain_sum = unstack_sums(unfold_lanes(sum_end(6)))
    write_norm(512, gain_sum)
    write_norm(1024, bias_sum)
    by_value, constant = back_terms(center2, scale2, mul2, bias_sum, gain_sum, pixels)

    for group in range(2):
        lanes = slice(group * 256, group * 256 + 256)
        m2, v2, k2 = mul2[:, lanes], by_value[:, lanes], constant[:, lanes]

        def make_dwid(row, carry):
            rows = pl.ds(row, CHUNK)
            values = grouped(dn2[rows, lanes]) * m2 + grouped(wid[rows, lanes]) * v2 + k2
            dwid[rows, lanes] = flat(values).astype(BF16)
            return carry

        over_rows(make_dwid, 0)
        dcol[PAD : PAD + ROWS, group * 1152 : group * 1152 + 1152] = dot_t(
            dwid[:, lanes], filters(group)
        )

    def gather_taps(row, carry):
        for side in range(3):
            for group in range(2):
                total = None
                for down in range(3):
                    at = group * 1152 + (3 * down + side) * 128
                    values = dcol[pl.ds(PAD + row - 56 * (down - 1), CHUNK), at : at + 128]
                    total = values if total is None else total + values
                act[side, pl.ds(PAD + row, CHUNK), group * 128 : group * 128 + 128] = total
        return carry

    over_rows(gather_taps, 0)

    def make_dn1(row, carry):
        rows = pl.ds(row, CHUNK)
        d_active = act[1, pl.ds(PAD + row, CHUNK), :]
        d_active = d_active + jnp.where(not_first, beside(2, row, -4), 0.0)
        d_active = d_active + jnp.where(not_last, beside(0, row, 4), 0.0)
        values = grouped(red[rows, :])
        turned = values * mul1 + add1
        gate = sigmoid(turned)
        slope = gate * (1.0 + turned * (1.0 - gate))
        down = grouped(d_active) * slope
        dn1[rows, :] = flat(down)
        normed = (values - center1) * scale1
        return carry[0] + jnp.sum(down, axis=0), carry[1] + jnp.sum(down * normed, axis=0)

    bias_sum, gain_sum = over_rows(make_dn1, (zero, zero))
    sum_start(7, fold_lanes(stack_sums(micro_sum(bias_sum), micro_sum(gain_sum))))
    reduce_owner(2)
    reduce_owner(3)
    for group in range(2):
        gc[group * own_half : (group + 1) * own_half] = tdot(
            columns[group], dwid[:, group * 256 : group * 256 + 256]
        ).reshape(own_half, 2, 9 * 128 // n_dp, BOTTLE)
    reduce_core(1)
    sum_turn(7)
    reduce_y(1)
    bias_sum, gain_sum = unstack_sums(unfold_lanes(sum_end(7)))
    write_norm(0, gain_sum)
    write_norm(256, bias_sum)
    by_value, constant = back_terms(center1, scale1, mul1, bias_sum, gain_sum, pixels)
    norm_rows = np_full[0:8, :]
    for d in range(1, n_dp):
        at = shard * d // 128
        norm_rows = jnp.where(dp == d, np_full[at : at + 8, :], norm_rows)
    norm_rows = pltpu.roll(norm_rows, lax.rem(128 - turn, 128), 1)
    gn_out[...] = jnp.where(lanes_id < 128 - turn, norm_rows, pltpu.roll(norm_rows, 7, 0))

    def make_dred(row, carry):
        rows = pl.ds(row, CHUNK)
        values = grouped(dn1[rows, :]) * mul1 + grouped(red[rows, :]) * by_value + constant
        dred[rows, :] = flat(values).astype(BF16)
        return carry

    over_rows(make_dred, 0)
    g1[...] = tdot(x_v[...], dred[...]).reshape(g1.shape)
    reduce_core(0)
    reduce_owner(1)
    proj[...] = dot_t(dred[...], fw1[...].reshape(CHANNELS, BOTTLE))

    def make_dx(row, carry):
        for start in range(0, CHANNELS, 256):
            lanes = slice(start, start + 256)
            values = up[pl.ds(row, CHUNK), lanes] + proj[pl.ds(row, CHUNK), lanes]
            dx4[pl.ds(row // 4, CHUNK // 4), :, lanes] = values.reshape(CHUNK // 4, 4, 256)
        return carry

    over_rows(make_dx, 0)
    dx_copy = pltpu.make_async_copy(dx4, dx_hbm, local_sem.at[3])
    dx_copy.start()
    reduce_y(0)
    reduce_spread(2)
    reduce_spread(3)
    reduce_owner(0)
    reduce_spread(1)
    reduce_spread(0)
    for which, out in ((2, f3_out), (3, fe_out), (1, fc_out), (0, f1_out)):
        reduce_end(which)
        out[...] = fs[which][...]

    bo_copy.wait()
    dx_copy.wait()
    for k in range(n_ar):
        wait_bytes(ar_slots_a[k].at[pl.ds(0, plane_size - 1)], ar_send_a.at[k])
        wait_bytes(ar_slots_b[k].at[pl.ds(0, planes - 1)], ar_send_b.at[k])
    wait_bytes(np_slots.at[pl.ds(0, n_dp - 1)], np_sems.at[0])
    for which in range(3):
        wait_bytes(seven(which), ws.at[which, 0])
        for stage in range(1, 4):
            wait_bytes(quarters[which](core, half_y), ws.at[which, stage])
    for which in range(4):
        wait_bytes(r1s[which], gs.at[which, 0])
        wait_bytes(r2s[which], gs.at[which, 1])
        wait_bytes(r3s[which].at[pl.ds(0, n_dp - 1)], gs.at[which, 2])
        wait_bytes(three_parts(which), gs.at[which, 3])


def update_kernel(*refs):
    sources, grads, states = refs[0:2], refs[2:7], refs[7:25]
    targets, outs, sems = refs[25:27], refs[27:45], refs[45]
    part = SIDE * SIDE // 4
    copies = []
    for which in range(2):
        for k in range(4):
            rows = pl.ds(k * part, part)
            copies.append(
                pltpu.make_async_copy(
                    sources[which].at[rows], targets[which].at[rows], sems.at[which, k]
                )
            )
    for copy in copies:
        copy.start()
    ex_rows = states[9].shape[0]
    shard = states[15].shape[1]
    norm_rows = [grads[4][k : k + 1, :] for k in range(-(-shard // 128))]
    found = (
        grads[0][...],
        grads[1][...],
        grads[3][:, 0:128],
        jnp.concatenate([grads[3][0:ex_rows, 128:384], grads[3][ex_rows:, 128:384]], axis=1),
        grads[2][...],
        jnp.concatenate(norm_rows, axis=1)[:, 0:shard],
    )
    fans = (CHANNELS, 9 * BOTTLE // RADIX, BOTTLE, INNER // 8, BOTTLE)
    rates = [2.0 * fan ** (-0.5) for fan in fans] + [NORM_RATE]
    for k in range(6):
        new = adamw(
            states[3 * k][...],
            states[3 * k + 1][...],
            states[3 * k + 2][...],
            found[k],
            rates[k],
            DECAY if k < 5 else 0.0,
        )
        for j in range(3):
            outs[3 * k + j][...] = new[j]
    for copy in copies:
        copy.wait()


def fused_device(
    images,
    out_grad,
    reduce_weight,
    reduce_moment,
    reduce_second,
    conv_weight,
    conv_moment,
    conv_second,
    squeeze_weight,
    squeeze_moment,
    squeeze_second,
    expand_weight,
    expand_moment,
    expand_second,
    project_weight,
    project_moment,
    project_second,
    norm_params,
    norm_moment,
    norm_second,
):
    n_dp, n_rep = lax.axis_size("dp"), lax.axis_size("rep")
    shard = norm_params.shape[0]
    by_pixel = lambda values: jnp.transpose(values, (1, 2, 0, 3)).reshape(-1, 4, CHANNELS)
    qc = conv_weight.shape[0] // 2
    q1 = reduce_weight.shape[0] // 4
    pe = squeeze_weight.shape[0]
    vmem = pltpu.VMEM
    pixel_form = (SIDE * SIDE, 4, CHANNELS)
    scratch = [
        vmem(pixel_form, BF16),
        vmem(pixel_form, BF16),
        vmem((ROWS, CHANNELS), BF16),
        vmem((ROWS, CHANNELS), BF16),
        vmem((n_dp, 2, 2, q1, BOTTLE), BF16),
        vmem((n_dp, 2, qc, BOTTLE), BF16),
        vmem((n_dp, pe, 1536), BF16),
        vmem((pe, 1536), BF16),
        vmem((n_dp, 8, 128), F32),
        vmem((40, 128), F32),
        vmem((ROWS, BOTTLE), F32),
        vmem((3, ROWS + 2 * PAD, BOTTLE), F32),
        vmem((2, ROWS, 9 * 128), BF16),
        vmem((ROWS, 512), F32),
        vmem((ROWS, 512), F32),
        vmem((ROWS, BOTTLE), BF16),
        vmem((ROWS, CHANNELS), F32),
        vmem((ROWS, CHANNELS), F32),
        vmem(pixel_form, BF16),
        vmem(pixel_form, F32),
        vmem((ROWS, CHANNELS), BF16),
        vmem((ROWS, BOTTLE), F32),
        vmem((ROWS, 512), F32),
        vmem((ROWS, 512), BF16),
        vmem((ROWS + 2 * PAD, 2 * 9 * 128), F32),
        vmem((ROWS, BOTTLE), F32),
        vmem((ROWS, BOTTLE), BF16),
        vmem((n_dp, 2, 2, q1, BOTTLE), F32),
        vmem((n_dp, 2, qc, BOTTLE), F32),
        vmem((n_dp, pe, CHANNELS), F32),
        vmem((n_dp, pe, 512), F32),
    ]
    scratch += [vmem((2 * n_rep,) + shape, F32) for shape in STATS]
    scratch += [vmem((n_dp // 2,) + shape, F32) for shape in STATS]
    half = [(n_dp, 2, q1, BOTTLE), (n_dp, 2, qc, 128), (n_dp, pe, 512), (n_dp, pe, 256)]
    quarter = [(n_dp, q1, BOTTLE), (n_dp, qc, 128), (n_dp, pe, 256), (n_dp, pe, 128)]
    final = [(2, 2, q1, BOTTLE), (2, qc, BOTTLE), (pe, CHANNELS), (pe, 512)]
    sent = [BF16, BF16, BF16, F32]
    scratch += [vmem(shape, F32) for shape in half + quarter]
    scratch += [vmem(shape, kind) for shape, kind in zip(quarter, sent)] * 2
    scratch += [vmem(shape[1:], F32) for shape in quarter]
    scratch += [vmem(shape, F32) for shape in final]
    dma = pltpu.SemaphoreType.DMA
    scratch += [dma((4,))] + [dma((len(STATS),))] * 4 + [dma((2,))] + [dma((3, 4))] * 2 + [dma((4, 4))] * 2
    any_space = pl.BlockSpec(memory_space=pl.ANY)
    in_vmem = pl.BlockSpec(memory_space=pltpu.VMEM)
    block_out, images_grad, sum1, sumc, sum3, sume, norm_grads = pl.pallas_call(
        functools.partial(block_kernel, n_dp, n_rep),
        out_shape=[
            jax.ShapeDtypeStruct(pixel_form, BF16),
            jax.ShapeDtypeStruct(pixel_form, F32),
            *[jax.ShapeDtypeStruct(shape, F32) for shape in final],
            jax.ShapeDtypeStruct((8, 128), F32),
        ],
        in_specs=[any_space] * 2 + [in_vmem] * 6,
        out_specs=[any_space] * 2 + [in_vmem] * 5,
        scratch_shapes=scratch,
        compiler_params=pltpu.CompilerParams(
            collective_id=0, has_side_effects=True, vmem_limit_bytes=63 * 1024 * 1024
        ),
    )(
        by_pixel(images),
        by_pixel(out_grad),
        reduce_weight,
        conv_weight,
        squeeze_weight,
        expand_weight,
        project_weight,
        norm_params.reshape(1, shard),
    )
    states = (
        reduce_weight,
        reduce_moment,
        reduce_second,
        conv_weight,
        conv_moment,
        conv_second,
        squeeze_weight,
        squeeze_moment,
        squeeze_second,
        expand_weight,
        expand_moment,
        expand_second,
        project_weight,
        project_moment,
        project_second,
    )
    norms = [values.reshape(1, shard) for values in (norm_params, norm_moment, norm_second)]
    block_out, images_grad, *updated = pl.pallas_call(
        update_kernel,
        out_shape=[
            jax.ShapeDtypeStruct(pixel_form, BF16),
            jax.ShapeDtypeStruct(pixel_form, F32),
            *[jax.ShapeDtypeStruct(state.shape, F32) for state in (*states, *norms)],
        ],
        in_specs=[any_space] * 2 + [in_vmem] * 23,
        out_specs=[any_space] * 2 + [in_vmem] * 18,
        scratch_shapes=[dma((2, 4))],
        compiler_params=pltpu.CompilerParams(vmem_limit_bytes=32 * 1024 * 1024),
    )(
        block_out,
        images_grad,
        sum1.reshape(reduce_weight.shape),
        sumc.reshape(conv_weight.shape),
        sum3,
        sume,
        norm_grads,
        *states,
        *norms,
    )
    by_image = lambda values: jnp.transpose(
        values.reshape(SIDE, SIDE, images.shape[0], CHANNELS), (2, 0, 1, 3)
    )
    return (
        by_image(block_out),
        by_image(images_grad),
        *updated[:15],
        *[values.reshape(shard) for values in updated[15:]],
    )


def solution(mesh):
    placed = (
        P(("dp", "rep"), None, None, None),
        P(("dp", "rep"), None, None, None),
        P("dp", None),
        P("dp", None),
        P("dp", None),
        P("dp", None),
        P("dp", None),
        P("dp", None),
        P("dp", None),
        P("dp", None),
        P("dp", None),
        P("dp", None),
        P("dp", None),
        P("dp", None),
        P("dp", None),
        P("dp", None),
        P("dp", None),
        P("dp"),
        P("dp"),
        P("dp"),
    )
    n_dp, n_rep = mesh.shape["dp"], mesh.shape["rep"]
    whole_tiles = n_rep == 4 and n_dp % 2 == 0 and INNER % (16 * n_dp) == 0
    return jax.shard_map(
        fused_device if whole_tiles else per_device,
        mesh=mesh,
        in_specs=placed,
        out_specs=(
            P(("dp", "rep"), None, None, None),
            P(("dp", "rep"), None, None, None),
            P("dp", None),
            P("dp", None),
            P("dp", None),
            P("dp", None),
            P("dp", None),
            P("dp", None),
            P("dp", None),
            P("dp", None),
            P("dp", None),
            P("dp", None),
            P("dp", None),
            P("dp", None),
            P("dp", None),
            P("dp", None),
            P("dp", None),
            P("dp"),
            P("dp"),
            P("dp"),
        ),
        check_vma=False,
    )
```

```python
import functools
import jax
import jax.numpy as jnp
from jax import lax
from jax.experimental import pallas as pl
from jax.experimental.pallas import tpu as pltpu
from jax.sharding import PartitionSpec as P

CHANNELS = 1024
BOTTLE = 256
INNER = 128
RADIX = 2
SIDE = 14
MICRO = 2
STEP = 10


EPSILON = 1e-05
PRECISE = lax.Precision.HIGHEST
BETA_ONE = 0.9
BETA_TWO = 0.999
ADAM_EPSILON = 1e-08
DECAY = 0.01
NORM_RATE = 0.8
ROWS = 4 * SIDE * SIDE
NORM_WIDTH = 4352


def split_params(packed):
    widths = (
        BOTTLE,
        BOTTLE,
        RADIX * BOTTLE,
        RADIX * BOTTLE,
        INNER,
        INNER,
        RADIX * BOTTLE,
        CHANNELS,
        CHANNELS,
    )
    pieces = []
    offset = 0
    for segment in widths:
        pieces.append(lax.slice_in_dim(packed, offset, offset + segment))
        offset = offset + segment
    return pieces


def silu_slope(values):
    logistic = jax.nn.sigmoid(values)
    return logistic * (1.0 + values * (1.0 - logistic))


def norm_forward(values, gain, bias, count):
    flat = values.reshape(-1, values.shape[-1])
    total, square = lax.psum((jnp.sum(flat, axis=0), jnp.sum(flat * flat, axis=0)), ("dp", "rep"))
    center = total / count
    scale = lax.rsqrt(square / count - center * center + EPSILON)
    normed = (values - center) * scale
    return (normed * gain + bias, normed, scale)


def norm_backward(upstream, normed, scale, gain, count):
    flat_up = upstream.reshape(-1, upstream.shape[-1])
    flat_norm = normed.reshape(-1, normed.shape[-1])
    bias_sum, gain_sum = lax.psum(
        (jnp.sum(flat_up, axis=0), jnp.sum(flat_up * flat_norm, axis=0)), ("dp", "rep")
    )
    downstream = gain * scale * (upstream - bias_sum / count - normed * (gain_sum / count))
    return (downstream, gain_sum, bias_sum)


def patches(active):
    padded = jnp.pad(active, ((0, 0), (1, 1), (1, 1), (0, 0), (0, 0)))
    shifted = [
        padded[:, down_step : down_step + SIDE, side_step : side_step + SIDE]
        for down_step in range(3)
        for side_step in range(3)
    ]
    return jnp.stack(shifted, axis=4)


def unpatch(columns):
    total = jnp.zeros(
        (columns.shape[0], SIDE + 2, SIDE + 2, columns.shape[3], columns.shape[5]), jnp.float32
    )
    for down_step in range(3):
        for side_step in range(3):
            piece = columns[:, :, :, :, 3 * down_step + side_step]
            total = total + jnp.pad(
                piece,
                ((0, 0), (down_step, 2 - down_step), (side_step, 2 - side_step), (0, 0), (0, 0)),
            )
    return total[:, 1 : SIDE + 1, 1 : SIDE + 1]


def adamw(param, moment, second, gradient, rate, decay):
    moment_new = BETA_ONE * moment + (1.0 - BETA_ONE) * gradient
    second_new = BETA_TWO * second + (1.0 - BETA_TWO) * gradient * gradient
    ratio = (
        moment_new
        / (1.0 - BETA_ONE**STEP)
        / (jnp.sqrt(second_new / (1.0 - BETA_TWO**STEP)) + ADAM_EPSILON)
    )
    return (param - rate * (ratio + decay * param), moment_new, second_new)


def per_device(
    images,
    out_grad,
    reduce_weight,
    reduce_moment,
    reduce_second,
    conv_weight,
    conv_moment,
    conv_second,
    squeeze_weight,
    squeeze_moment,
    squeeze_second,
    expand_weight,
    expand_moment,
    expand_second,
    project_weight,
    project_moment,
    project_second,
    norm_params,
    norm_moment,
    norm_second,
):
    bf16 = jnp.bfloat16
    low_reduce = reduce_weight.astype(bf16)
    low_conv = conv_weight.astype(bf16)
    low_squeeze = squeeze_weight.astype(bf16)
    low_expand = expand_weight.astype(bf16)
    low_project = project_weight.astype(bf16)
    low_norm = norm_params.astype(bf16)
    devices = lax.axis_size("dp") * lax.axis_size("rep")
    per_batch = images.shape[0] // MICRO
    pixel_count = float(per_batch * SIDE * SIDE * devices)
    image_count = float(per_batch * devices)
    group_in = BOTTLE // RADIX
    grad_first = jnp.zeros((CHANNELS, BOTTLE), jnp.float32)
    grad_conv = jnp.zeros((RADIX, 9 * group_in, BOTTLE), jnp.float32)
    grad_squeeze = jnp.zeros((BOTTLE, INNER), jnp.float32)
    grad_expand = jnp.zeros((INNER, RADIX * BOTTLE), jnp.float32)
    grad_last = jnp.zeros((BOTTLE, CHANNELS), jnp.float32)
    grad_norms = jnp.zeros(
        (2 * BOTTLE + 3 * RADIX * BOTTLE + 2 * INNER + 2 * CHANNELS,), jnp.float32
    )
    outputs = []
    input_grads = []
    for number in range(MICRO):
        forward_set = (
            lax.all_gather(low_reduce, "dp", axis=0, tiled=True),
            lax.all_gather(low_conv, "dp", axis=0, tiled=True),
            lax.all_gather(low_squeeze, "dp", axis=0, tiled=True),
            lax.all_gather(low_expand, "dp", axis=0, tiled=True),
            lax.all_gather(low_project, "dp", axis=0, tiled=True),
            lax.all_gather(low_norm, "dp", axis=0, tiled=True),
        )
        first, conv, squeeze, expand, last, packed = forward_set
        (
            gain_one,
            bias_one,
            gain_two,
            bias_two,
            gain_pool,
            bias_pool,
            bias_expand,
            gain_three,
            bias_three,
        ) = split_params(packed.astype(jnp.float32))
        batched = images[number * per_batch : (number + 1) * per_batch]
        cotangent = out_grad[number * per_batch : (number + 1) * per_batch]
        reduced = jnp.einsum("nhwc,cb->nhwb", batched, first, preferred_element_type=jnp.float32)
        norm_one, normed_one, scale_one = norm_forward(reduced, gain_one, bias_one, pixel_count)
        active = jax.nn.silu(norm_one).astype(bf16)
        columns = patches(active.reshape(per_batch, SIDE, SIDE, RADIX, group_in)).reshape(
            per_batch * SIDE * SIDE, RADIX, 9 * group_in
        )
        conv_grouped = conv.reshape(RADIX, 9 * group_in, BOTTLE)
        widened = jnp.einsum(
            "prk,rko->pro", columns, conv_grouped, preferred_element_type=jnp.float32
        )
        widened = widened.reshape(per_batch, SIDE, SIDE, RADIX * BOTTLE)
        norm_two, normed_two, scale_two = norm_forward(widened, gain_two, bias_two, pixel_count)
        splits = jax.nn.silu(norm_two).reshape(per_batch, SIDE, SIDE, RADIX, BOTTLE)
        pooled = jnp.sum(jnp.sum(splits, axis=3), axis=(1, 2)) / (SIDE * SIDE)
        squeeze_float = squeeze.astype(jnp.float32)
        expand_float = expand.astype(jnp.float32)
        pre_pool = jnp.dot(pooled, squeeze_float, precision=PRECISE)
        norm_pool, normed_pool, scale_pool = norm_forward(
            pre_pool, gain_pool, bias_pool, image_count
        )
        hidden = jax.nn.silu(norm_pool)
        logits = (jnp.dot(hidden, expand_float, precision=PRECISE) + bias_expand).reshape(
            per_batch, RADIX, BOTTLE
        )
        attention = jax.nn.softmax(logits, axis=1)
        mixed = jnp.sum(splits * attention[:, None, None], axis=3).astype(bf16)
        projected = jnp.einsum("nhwb,bc->nhwc", mixed, last, preferred_element_type=jnp.float32)
        norm_three, normed_three, scale_three = norm_forward(
            projected, gain_three, bias_three, pixel_count
        )
        summed = batched.astype(jnp.float32) + norm_three
        outputs.append(jax.nn.silu(summed).astype(bf16))
        backward_set = (
            lax.all_gather(low_reduce, "dp", axis=0, tiled=True),
            lax.all_gather(low_conv, "dp", axis=0, tiled=True),
            lax.all_gather(low_squeeze, "dp", axis=0, tiled=True),
            lax.all_gather(low_expand, "dp", axis=0, tiled=True),
            lax.all_gather(low_project, "dp", axis=0, tiled=True),
            lax.all_gather(low_norm, "dp", axis=0, tiled=True),
        )
        first, conv, squeeze, expand, last, packed = backward_set
        gains_back = split_params(packed.astype(jnp.float32))
        conv_grouped = conv.reshape(RADIX, 9 * group_in, BOTTLE)
        expand_float = expand.astype(jnp.float32)
        squeeze_float = squeeze.astype(jnp.float32)
        upstream = cotangent.astype(jnp.float32) * silu_slope(summed)
        d_projected, gain_three_grad, bias_three_grad = norm_backward(
            upstream, normed_three, scale_three, gains_back[7], pixel_count
        )
        d_projected_low = d_projected.astype(bf16)
        grad_last = grad_last + jnp.einsum(
            "nhwb,nhwc->bc", mixed, d_projected_low, preferred_element_type=jnp.float32
        )
        d_mixed = jnp.einsum(
            "nhwc,bc->nhwb", d_projected_low, last, preferred_element_type=jnp.float32
        )
        d_splits = d_mixed[:, :, :, None] * attention[:, None, None]
        d_attention = jnp.sum(d_mixed[:, :, :, None] * splits, axis=(1, 2))
        d_logits = attention * (
            d_attention - jnp.sum(attention * d_attention, axis=1, keepdims=True)
        )
        flat_logits = d_logits.reshape(per_batch, RADIX * BOTTLE)
        grad_expand = grad_expand + jnp.dot(hidden.T, flat_logits, precision=PRECISE)
        d_hidden = jnp.dot(flat_logits, expand_float.T, precision=PRECISE)
        d_pool_norm = d_hidden * silu_slope(norm_pool)
        pool_bias_sum, pool_gain_sum, expand_bias_sum = lax.psum(
            (
                jnp.sum(d_pool_norm, axis=0),
                jnp.sum(d_pool_norm * normed_pool, axis=0),
                jnp.sum(flat_logits, axis=0),
            ),
            ("dp", "rep"),
        )
        d_pre_pool = (
            gains_back[4]
            * scale_pool
            * (
                d_pool_norm
                - pool_bias_sum / image_count
                - normed_pool * (pool_gain_sum / image_count)
            )
        )
        grad_squeeze = grad_squeeze + jnp.dot(pooled.T, d_pre_pool, precision=PRECISE)
        d_pooled = jnp.dot(d_pre_pool, squeeze_float.T, precision=PRECISE)
        d_splits = d_splits + (d_pooled / (SIDE * SIDE))[:, None, None, None, :]
        d_norm_two = d_splits.reshape(per_batch, SIDE, SIDE, RADIX * BOTTLE) * silu_slope(norm_two)
        d_widened, gain_two_grad, bias_two_grad = norm_backward(
            d_norm_two, normed_two, scale_two, gains_back[2], pixel_count
        )
        d_widened_low = d_widened.astype(bf16).reshape(per_batch * SIDE * SIDE, RADIX, BOTTLE)
        grad_conv = grad_conv + jnp.einsum(
            "prk,pro->rko", columns, d_widened_low, preferred_element_type=jnp.float32
        )
        d_columns = jnp.einsum(
            "pro,rko->prk", d_widened_low, conv_grouped, preferred_element_type=jnp.float32
        )
        d_active = unpatch(d_columns.reshape(per_batch, SIDE, SIDE, RADIX, 9, group_in)).reshape(
            per_batch, SIDE, SIDE, BOTTLE
        )
        d_norm_one = d_active * silu_slope(norm_one)
        d_reduced, gain_one_grad, bias_one_grad = norm_backward(
            d_norm_one, normed_one, scale_one, gains_back[0], pixel_count
        )
        d_reduced_low = d_reduced.astype(bf16)
        grad_first = grad_first + jnp.einsum(
            "nhwc,nhwb->cb", batched, d_reduced_low, preferred_element_type=jnp.float32
        )
        input_grads.append(
            upstream
            + jnp.einsum("nhwb,cb->nhwc", d_reduced_low, first, preferred_element_type=jnp.float32)
        )
        grad_norms = grad_norms + jnp.concatenate(
            [
                gain_one_grad,
                bias_one_grad,
                gain_two_grad,
                bias_two_grad,
                pool_gain_sum,
                pool_bias_sum,
                expand_bias_sum,
                gain_three_grad,
                bias_three_grad,
            ]
        )
    grad_conv = grad_conv.reshape(9 * BOTTLE, BOTTLE)
    partial_value = (
        lax.psum_scatter(grad_first, "dp", scatter_dimension=0, tiled=True),
        lax.psum_scatter(grad_conv, "dp", scatter_dimension=0, tiled=True),
        lax.psum_scatter(grad_squeeze, "dp", scatter_dimension=0, tiled=True),
        lax.psum_scatter(grad_expand, "dp", scatter_dimension=0, tiled=True),
        lax.psum_scatter(grad_last, "dp", scatter_dimension=0, tiled=True),
    )
    owned = lax.psum(
        (partial_value[0], partial_value[1], partial_value[2], partial_value[3], partial_value[4]),
        "rep",
    )
    shard_length = norm_params.shape[0]
    norm_grad_owned = lax.dynamic_slice_in_dim(
        grad_norms, lax.axis_index("dp") * shard_length, shard_length
    )
    reduce_new = adamw(
        reduce_weight, reduce_moment, reduce_second, owned[0], 2.0 * CHANNELS ** (-0.5), DECAY
    )
    conv_new = adamw(
        conv_weight,
        conv_moment,
        conv_second,
        owned[1],
        2.0 * (9 * BOTTLE // RADIX) ** (-0.5),
        DECAY,
    )
    squeeze_new = adamw(
        squeeze_weight, squeeze_moment, squeeze_second, owned[2], 2.0 * BOTTLE ** (-0.5), DECAY
    )
    expand_new = adamw(
        expand_weight, expand_moment, expand_second, owned[3], 2.0 * (INNER // 8) ** (-0.5), DECAY
    )
    project_new = adamw(
        project_weight, project_moment, project_second, owned[4], 2.0 * BOTTLE ** (-0.5), DECAY
    )
    norm_new = adamw(norm_params, norm_moment, norm_second, norm_grad_owned, NORM_RATE, 0.0)
    return (
        jnp.concatenate(outputs, axis=0),
        jnp.concatenate(input_grads, axis=0),
        reduce_new[0],
        reduce_new[1],
        reduce_new[2],
        conv_new[0],
        conv_new[1],
        conv_new[2],
        squeeze_new[0],
        squeeze_new[1],
        squeeze_new[2],
        expand_new[0],
        expand_new[1],
        expand_new[2],
        project_new[0],
        project_new[1],
        project_new[2],
        norm_new[0],
        norm_new[1],
        norm_new[2],
    )


MESH = pl.DeviceIdType.MESH
PAD = 64
CHUNK = 112
F32 = jnp.float32
BF16 = jnp.bfloat16
STATS = ((8, 128), (8, 256), (8, 128), (8, 512), (8, 512), (16, 128), (8, 256), (8, 128))


def sigmoid(values):
    return 0.5 * jnp.tanh(0.5 * values) + 0.5


def row_ids(width):
    return lax.broadcasted_iota(jnp.int32, (8, width), 0)


def image_sum(rows):
    return rows + pltpu.roll(rows, 4, 0)


def pair_sum(rows):
    even = row_ids(rows.shape[1]) % 2 == 0
    return rows + jnp.where(even, pltpu.roll(rows, 7, 0), pltpu.roll(rows, 1, 0))


def micro_sum(rows):
    return pair_sum(image_sum(rows))


def stack_sums(first, second):
    return jnp.where(row_ids(first.shape[1]) < 4, first, second)


def unstack_sums(stacked):
    upper = row_ids(stacked.shape[1]) < 4
    turned = pltpu.roll(stacked, 4, 0)
    return jnp.where(upper, stacked, turned), jnp.where(upper, turned, stacked)


def fold_lanes(stacked):
    half = stacked.shape[1] // 2
    even = row_ids(half) % 2 == 0
    return jnp.where(even, stacked[:, :half], stacked[:, half:])


def unfold_lanes(folded):
    even = row_ids(folded.shape[1]) % 2 == 0
    left = jnp.where(even, folded, pltpu.roll(folded, 1, 0))
    right = jnp.where(even, pltpu.roll(folded, 7, 0), folded)
    return jnp.concatenate([left, right], axis=1)


def norm_terms(total, square, gain, bias, count):
    center = total / count
    scale = lax.rsqrt(square / count - center * center + EPSILON)
    slope = scale * gain
    return center, scale, slope, bias - center * slope


def back_terms(center, scale, slope, bias_sum, gain_sum, count):
    by_value = -slope * scale * (gain_sum / count)
    constant = -slope * (bias_sum / count) - by_value * center
    return by_value, constant


def tdot(left, right):
    return lax.dot_general(left, right, (((0,), (0,)), ((), ())), preferred_element_type=F32)


def dot_t(left, right):
    return lax.dot_general(left, right, (((1,), (1,)), ((), ())), preferred_element_type=F32)


def in_parts(values, parts):
    found = []
    for _ in range(parts):
        rounded = values.astype(BF16).astype(F32)
        found.append(rounded)
        values = values - rounded
    return found


def exact_dot(left, right, transposed):
    stacked = jnp.concatenate(in_parts(left, 3), axis=0).astype(BF16)
    wide = dot_t(stacked, right) if transposed else jnp.dot(stacked, right, preferred_element_type=F32)
    return wide[0:8] + wide[8:16] + wide[16:24]


def image_dot(left, right):
    once = row_ids(left.shape[1]) < 4
    high, low = in_parts(jnp.where(once, left, 0.0), 2)
    other_high, other_low = in_parts(right, 2)
    return tdot(
        jnp.concatenate([high, high, low, low], axis=0).astype(BF16),
        jnp.concatenate([other_high, other_low, other_high, other_low], axis=0).astype(BF16),
    )


def block_kernel(
    n_dp,
    n_rep,
    x_hbm,
    gy_hbm,
    w1_hbm,
    wc_hbm,
    sq_hbm,
    ex_hbm,
    w3_hbm,
    np_hbm,
    bo_hbm,
    dx_hbm,
    f1_hbm,
    fc_hbm,
    f3_hbm,
    fe_hbm,
    gn_hbm,
    w1_own,
    wc_own,
    sq_own,
    ex_own,
    w3_own,
    np_own,
    gn_out,
    x4,
    gy4,
    x_v,
    gy_v,
    fw1,
    fwc,
    fpe,
    pe_own,
    np_slots,
    np_full,
    red,
    act,
    columns,
    wid,
    splits,
    mixed,
    proj,
    up,
    bo4,
    dx4,
    dproj,
    d_mixed,
    dn2,
    dwid,
    dcol,
    dn1,
    dred,
    g1,
    gc,
    g3,
    ge,
    *rest,
):
    n_ar = len(STATS)
    ar_slots_a = rest[0:n_ar]
    ar_slots_b = rest[n_ar : 2 * n_ar]
    rest = rest[2 * n_ar :]
    r1s, ys, r2s, ks, r3s, own = (rest[5 * i : 5 * i + 5] for i in range(6))
    fs = rest[30:34]
    rest = rest[34:]
    local_sem, ar_send_a, ar_recv_a, ar_send_b, ar_recv_b, np_sems, ws, wr, gs, gr = rest

    dp = lax.axis_index("dp")
    rep = lax.axis_index("rep")
    core = lax.rem(rep, 2)
    half_y = rep // 2
    planes = n_dp // 2
    plane_size = 2 * n_rep
    plane = dp // 2
    in_plane = lax.rem(dp, 2) * n_rep + rep
    sibling = (dp, half_y * 2 + (1 - core))
    across = (dp, (1 - half_y) * 2 + core)
    pixels = float(SIDE * SIDE * 2 * n_dp * n_rep)
    pictures = float(2 * n_dp * n_rep)

    in_planes = [lax.rem(in_plane + step, plane_size) for step in range(1, plane_size)]
    plane_peers = [(plane * 2 + other // n_rep, lax.rem(other, n_rep)) for other in in_planes]
    column_peers = [
        (lax.rem(plane + step, planes) * 2 + lax.rem(dp, 2), rep) for step in range(1, planes)
    ]
    owner_peers = [(lax.rem(dp + step, n_dp), rep) for step in range(1, n_dp)]
    rep_peers = [(dp, lax.rem(rep + step, n_rep)) for step in range(1, n_rep)]

    def remote(src, dst, send_sem, recv_sem, device):
        return pltpu.make_async_remote_copy(
            src_ref=src,
            dst_ref=dst,
            send_sem=send_sem,
            recv_sem=recv_sem,
            device_id=device,
            device_id_type=MESH,
        )

    def send_all(ref, send_sem, recv_sem, peers):
        for device in peers:
            remote(ref, ref, send_sem, recv_sem, device).start()

    def wait_bytes(ref, sem):
        pltpu.make_async_copy(ref, ref, sem).wait()

    def over_rows(body, init):
        def step(index, carry):
            return body(pl.multiple_of(index * CHUNK, CHUNK), carry)

        return lax.fori_loop(0, ROWS // CHUNK, step, init)

    def grouped(values):
        return values.reshape(CHUNK // 8, 8, values.shape[-1])

    def by_four(values):
        return flat(values).reshape(CHUNK // 4, 4, values.shape[-1])

    def flat(values):
        return values.reshape(CHUNK, values.shape[-1])

    own_copies = [
        pltpu.make_async_copy(source, target, local_sem.at[4 + k])
        for k, (source, target) in enumerate(
            (
                (w1_hbm, w1_own),
                (np_hbm, np_own),
                (wc_hbm, wc_own),
                (w3_hbm, w3_own),
                (sq_hbm, sq_own),
                (ex_hbm, ex_own),
            )
        )
    ]
    for copy in own_copies:
        copy.start()
    x_copy = pltpu.make_async_copy(x_hbm, x4, local_sem.at[0])
    gy_copy = pltpu.make_async_copy(gy_hbm, gy4, local_sem.at[1])
    x_copy.start()
    barrier = pltpu.get_barrier_semaphore()
    for device in plane_peers + owner_peers:
        pl.semaphore_signal(barrier, inc=1, device_id=device, device_id_type=MESH)

    part = core * 2 + half_y
    own_copies[0].wait()
    q1 = w1_own.shape[0] // 4
    fw1[dp, core, half_y] = w1_own[pl.ds(pl.multiple_of(part * q1, q1), q1), :].astype(BF16)
    core_lanes = pl.ds(pl.multiple_of(core * 128, 128), 128)
    pe_lanes = pl.ds(pl.multiple_of(part * 384, 128), 384)

    pl.semaphore_wait(barrier, plane_size + n_dp - 2)

    def quarter_w1(c, y):
        return fw1.at[:, c, y]

    def quarter_wc(c, y):
        return fwc.at[:, y, :, pl.ds(pl.multiple_of(c * 128, 128), 128)]

    def quarter_pe(c, y):
        return fpe.at[:, :, pl.ds(pl.multiple_of((c * 2 + y) * 384, 128), 384)]

    quarters = (quarter_w1, quarter_wc, quarter_pe)

    def piece(which, d):
        return (
            fw1.at[d, core, half_y],
            fwc.at[d, half_y, :, core_lanes],
            fpe.at[d, :, pe_lanes],
        )[which]

    def seven(which):
        return (
            fw1.at[pl.ds(0, n_dp - 1), core, half_y],
            fwc.at[pl.ds(0, n_dp - 1), half_y, :, core_lanes],
            fpe.at[pl.ds(0, n_dp - 1), :, pe_lanes],
        )[which]

    def gather_out(which):
        send_all(piece(which, dp), ws.at[which, 0], wr.at[which, 0], owner_peers)

    def gather_turn(which):
        wait_bytes(seven(which), wr.at[which, 0])
        mine = quarters[which](core, half_y)
        remote(mine, mine, ws.at[which, 1], wr.at[which, 1], across).start()
        remote(mine, mine, ws.at[which, 2], wr.at[which, 2], sibling).start()

    def gather_hand(which):
        theirs = quarters[which](core, 1 - half_y)
        wait_bytes(theirs, wr.at[which, 1])
        remote(theirs, theirs, ws.at[which, 3], wr.at[which, 3], sibling).start()

    def gather_end(which):
        wait_bytes(quarters[which](1 - core, half_y), wr.at[which, 2])
        wait_bytes(quarters[which](1 - core, 1 - half_y), wr.at[which, 3])

    def to_rows(source, target):
        def body(index, carry):
            values = source[pl.ds(index * (CHUNK // 4), CHUNK // 4)].astype(F32)
            row = pl.multiple_of(index * CHUNK, CHUNK)
            target[pl.ds(row, CHUNK), :] = values.reshape(CHUNK, CHANNELS).astype(BF16)
            return carry

        lax.fori_loop(0, ROWS // CHUNK, body, 0)

    gather_out(0)

    own_copies[1].wait()
    shard = np_own.shape[0]
    lanes_id = lax.broadcasted_iota(jnp.int32, (8, 128), 1)
    turn = lax.rem(shard * dp, 128)
    np_rows = []
    for at in range(0, shard, 128):
        width = min(128, shard - at)
        piece_row = np_own[pl.ds(at, width)].reshape(1, width)
        if width < 128:
            piece_row = jnp.concatenate([piece_row, jnp.zeros((1, 128 - width), F32)], axis=1)
        np_rows.append(piece_row)
    np_rows.append(jnp.zeros((8 - len(np_rows), 128), F32))
    np_turned = jnp.concatenate(np_rows, axis=0).astype(BF16).astype(F32)
    np_turned = pltpu.roll(np_turned, turn, 1)
    np_slots[dp] = jnp.where(lanes_id < turn, pltpu.roll(np_turned, 1, 0), np_turned)
    send_all(np_slots.at[dp], np_sems.at[0], np_sems.at[1], owner_peers)
    own_copies[2].wait()
    qc = wc_own.shape[0] // 2
    fwc[dp, half_y, :, core_lanes] = wc_own[
        pl.ds(pl.multiple_of(half_y * qc, qc), qc), core_lanes
    ].astype(BF16)
    for copy in own_copies[3:]:
        copy.wait()
    ex_rows = ex_own.shape[0]
    pe_own[:, 0:CHANNELS] = w3_own[...].astype(BF16)
    pe_own[:, 1024:1152] = sq_own[...].astype(BF16)
    pe_own[0:ex_rows, 1152:1408] = ex_own[:, 0:256].astype(BF16)
    pe_own[ex_rows : 2 * ex_rows, 1152:1408] = ex_own[:, 256:512].astype(BF16)
    pe_own[:, 1408:1536] = jnp.zeros((2 * ex_rows, 128), BF16)
    fpe[dp, :, pe_lanes] = pe_own[:, pe_lanes]
    gy_copy.start()
    x_copy.wait()
    to_rows(x4, x_v)
    gather_turn(0)
    gather_out(1)
    zero_rows = jnp.zeros((PAD, BOTTLE), F32)
    for side in range(3):
        act[side, 0:PAD, :] = zero_rows
        act[side, PAD + ROWS : 2 * PAD + ROWS, :] = zero_rows
    for lane_block in range(9):
        dcol[0:PAD, lane_block * 256 : lane_block * 256 + 256] = zero_rows
        dcol[PAD + ROWS : 2 * PAD + ROWS, lane_block * 256 : lane_block * 256 + 256] = zero_rows
    gather_hand(0)

    def sum_start(k, payload):
        ar_slots_a[k][in_plane] = payload
        send_all(ar_slots_a[k].at[in_plane], ar_send_a.at[k], ar_recv_a.at[k], plane_peers)

    def sum_turn(k):
        wait_bytes(ar_slots_a[k].at[pl.ds(0, plane_size - 1)], ar_recv_a.at[k])
        part_sum = ar_slots_a[k][0]
        for slot in range(1, plane_size):
            part_sum = part_sum + ar_slots_a[k][slot]
        ar_slots_b[k][plane] = part_sum
        send_all(ar_slots_b[k].at[plane], ar_send_b.at[k], ar_recv_b.at[k], column_peers)

    def sum_end(k):
        wait_bytes(ar_slots_b[k].at[pl.ds(0, planes - 1)], ar_recv_b.at[k])
        whole = ar_slots_b[k][0]
        for slot in range(1, planes):
            whole = whole + ar_slots_b[k][slot]
        return whole

    def lanes_of(index, width):
        return pl.ds(pl.multiple_of(index * width, 128), width)

    cut = 64
    conv_rows = {1: pl.ds(0, cut), 2: pl.ds(cut, gc.shape[2] - cut)}
    grads = (g1, gc, gc, g3, ge)

    def half_of(which, c):
        ref = grads[which]
        if which == 0:
            return ref.at[:, c]
        if which in conv_rows:
            return ref.at[:, :, conv_rows[which], lanes_of(c, 128)]
        return ref.at[:, :, lanes_of(c, (512, 256)[which - 3])]

    def y_part(which, ref, y):
        if which < 3:
            return ref.at[:, y]
        return ref.at[:, :, lanes_of(y, (256, 128)[which - 3])]

    def quarter_of(which, c, y):
        ref = grads[which]
        if which == 0:
            return ref.at[:, c, y]
        if which in conv_rows:
            return ref.at[:, y, conv_rows[which], lanes_of(c, 128)]
        return ref.at[:, :, lanes_of(c * 2 + y, (256, 128)[which - 3])]

    def final_part(which, c, y):
        if which == 0:
            return fs[0].at[c, y]
        if which in conv_rows:
            return fs[1].at[y, conv_rows[which], lanes_of(c, 128)]
        return fs[which - 1].at[:, lanes_of(c * 2 + y, (256, 128)[which - 3])]

    def reduce_core(which):
        remote(
            half_of(which, 1 - core), r1s[which], gs.at[which, 0], gr.at[which, 0], sibling
        ).start()

    def reduce_y(which):
        wait_bytes(r1s[which], gr.at[which, 0])
        away = quarter_of(which, core, 1 - half_y)
        mine = quarter_of(which, core, half_y)
        there = y_part(which, r1s[which], 1 - half_y)
        here = y_part(which, r1s[which], half_y)

        def add_away(d, carry):
            ys[which][d] = (away[d] + there[d]).astype(ys[which].dtype)
            return carry

        lax.fori_loop(0, n_dp, add_away, 0)
        remote(ys[which], r2s[which], gs.at[which, 1], gr.at[which, 1], across).start()

        def add_mine(d, carry):
            mine[d] = mine[d] + here[d]
            return carry

        lax.fori_loop(0, n_dp, add_mine, 0)

    def reduce_owner(which):
        wait_bytes(r2s[which], gr.at[which, 1])
        mine = quarter_of(which, core, half_y)

        def add(d, carry):
            ks[which][d] = (mine[d] + r2s[which][d].astype(F32)).astype(ks[which].dtype)
            return carry

        lax.fori_loop(0, n_dp, add, 0)
        for device in owner_peers:
            remote(
                ks[which].at[device[0]],
                r3s[which].at[dp],
                gs.at[which, 2],
                gr.at[which, 2],
                device,
            ).start()
        own[which][...] = mine[dp] + r2s[which][dp].astype(F32)
        r3s[which][dp] = jnp.zeros(own[which].shape, r3s[which].dtype)

    def reduce_spread(which):
        wait_bytes(r3s[which].at[pl.ds(0, n_dp - 1)], gr.at[which, 2])
        total = own[which][...]
        for slot in range(n_dp):
            total = total + r3s[which][slot].astype(F32)
        mine = final_part(which, core, half_y)
        mine[...] = total
        send_all(mine, gs.at[which, 3], gr.at[which, 3], rep_peers)

    def three_parts(which):
        return r1s[which].at[pl.ds(0, 3), 0] if which < 3 else y_part(which, r1s[which], 0).at[pl.ds(0, 3)]

    def reduce_end(which):
        wait_bytes(three_parts(which), gr.at[which, 3])

    gather_end(0)
    red[...] = jnp.dot(x_v[...], fw1[...].reshape(CHANNELS, BOTTLE), preferred_element_type=F32)

    def sums_of(ref, start, width):
        def body(row, carry):
            values = grouped(ref[pl.ds(row, CHUNK), start : start + width])
            return carry[0] + jnp.sum(values, axis=0), carry[1] + jnp.sum(values * values, axis=0)

        zero = jnp.zeros((8, width), F32)
        return over_rows(body, (zero, zero))

    def wide_sums(ref, width):
        found = [sums_of(ref, start, 256) for start in range(0, width, 256)]
        first = jnp.concatenate([item[0] for item in found], axis=1)
        second = jnp.concatenate([item[1] for item in found], axis=1)
        return fold_lanes(stack_sums(micro_sum(first), micro_sum(second)))

    sum_start(0, wide_sums(red, BOTTLE))

    gy_copy.wait()
    to_rows(gy4, gy_v)
    wait_bytes(np_slots.at[pl.ds(0, n_dp - 1)], np_sems.at[1])
    np_full[...] = jnp.zeros(np_full.shape, F32)
    for d in range(n_dp):
        at = shard * d // 128
        np_full[at : at + 8, :] = np_full[at : at + 8, :] + np_slots[d]

    def vector(at, width):
        rows = [np_full[at // 128 + k : at // 128 + k + 1, :] for k in range(width // 128)]
        return jnp.concatenate(rows, axis=1) if len(rows) > 1 else rows[0]

    gain_one, bias_one = vector(0, 256), vector(256, 256)
    gain_two, bias_two = vector(512, 512), vector(1024, 512)
    gain_pool, bias_pool = vector(1536, 128), vector(1664, 128)
    bias_expand = vector(1792, 512)
    gain_three, bias_three = vector(2304, 1024), vector(3328, 1024)

    sum_turn(0)
    gather_turn(1)
    gather_out(2)
    total, square = unstack_sums(unfold_lanes(sum_end(0)))
    center1, scale1, mul1, add1 = norm_terms(total, square, gain_one, bias_one, pixels)

    def make_active(row, carry):
        turned = grouped(red[pl.ds(row, CHUNK), :]) * mul1 + add1
        act[1, pl.ds(PAD + row, CHUNK), :] = flat(turned * sigmoid(turned))
        return carry

    over_rows(make_active, 0)
    gather_hand(1)
    place = lax.rem(lax.broadcasted_iota(jnp.int32, (CHUNK, BOTTLE), 0) // 4, SIDE)
    not_last = place != SIDE - 1
    not_first = place != 0

    def beside(side, row, distance):
        near = act[side, pl.ds(PAD + row - 8, CHUNK + 16), :]
        return pltpu.roll(near, (CHUNK + 16 - distance) % (CHUNK + 16), 0)[8 : 8 + CHUNK]

    def shift_active(row, carry):
        act[2, pl.ds(PAD + row, CHUNK), :] = jnp.where(not_last, beside(1, row, 4), 0.0)
        act[0, pl.ds(PAD + row, CHUNK), :] = jnp.where(not_first, beside(1, row, -4), 0.0)
        return carry

    over_rows(shift_active, 0)

    def make_columns(row, carry):
        for tap in range(9):
            down, side = tap // 3 - 1, tap % 3
            values = act[side, pl.ds(PAD + row + 56 * down, CHUNK), :].astype(BF16)
            columns[0, pl.ds(row, CHUNK), tap * 128 : tap * 128 + 128] = values[:, 0:128]
            columns[1, pl.ds(row, CHUNK), tap * 128 : tap * 128 + 128] = values[:, 128:256]
        return carry

    over_rows(make_columns, 0)
    gather_end(1)
    own_half = n_dp // 2

    def filters(group):
        return fwc[group * own_half : (group + 1) * own_half].reshape(9 * 128, BOTTLE)

    for group in range(2):
        wid[:, group * 256 : group * 256 + 256] = jnp.dot(
            columns[group], filters(group), preferred_element_type=F32
        )
    sum_start(1, wide_sums(wid, 512))
    gather_turn(2)
    sum_turn(1)
    gather_hand(2)
    total, square = unstack_sums(unfold_lanes(sum_end(1)))
    center2, scale2, mul2, add2 = norm_terms(total, square, gain_two, bias_two, pixels)

    def make_splits(row, carry):
        found = []
        for group in range(2):
            lanes = slice(group * 256, group * 256 + 256)
            turned = grouped(wid[pl.ds(row, CHUNK), lanes]) * mul2[:, lanes] + add2[:, lanes]
            values = turned * sigmoid(turned)
            splits[pl.ds(row, CHUNK), lanes] = flat(values)
            found.append(jnp.sum(values, axis=0))
        return carry + found[0] + found[1]

    pooled = image_sum(over_rows(make_splits, jnp.zeros((8, BOTTLE), F32))) / (SIDE * SIDE)
    gather_end(2)
    last = fpe[:, :, 0:CHANNELS].reshape(BOTTLE, CHANNELS)
    squeeze = fpe[:, :, 1024:1152].reshape(BOTTLE, INNER)
    ex_both = fpe[:, :, 1152:1408]
    expand = jnp.concatenate(
        [
            ex_both[:, 0:ex_rows].reshape(INNER, 256),
            ex_both[:, ex_rows : 2 * ex_rows].reshape(INNER, 256),
        ],
        axis=1,
    )
    pre_pool = exact_dot(pooled, squeeze, False)
    sum_start(2, stack_sums(pair_sum(pre_pool), pair_sum(pre_pool * pre_pool)))
    sum_turn(2)
    total, square = unstack_sums(sum_end(2))
    center_p, scale_p, mul_p, add_p = norm_terms(total, square, gain_pool, bias_pool, pictures)
    normed_p = (pre_pool - center_p) * scale_p
    norm_p = pre_pool * mul_p + add_p
    gate_p = sigmoid(norm_p)
    hidden = norm_p * gate_p
    slope_p = gate_p * (1.0 + norm_p * (1.0 - gate_p))
    logits = exact_dot(hidden, expand, False) + bias_expand
    left, right = logits[:, 0:256], logits[:, 256:512]
    most = jnp.maximum(left, right)
    left, right = jnp.exp(left - most), jnp.exp(right - most)
    att0 = left / (left + right)
    att1 = right / (left + right)

    def make_mixed(row, carry):
        rows = pl.ds(row, CHUNK)
        values = grouped(splits[rows, 0:256]) * att0 + grouped(splits[rows, 256:512]) * att1
        mixed[rows, :] = flat(values).astype(BF16)
        return carry

    over_rows(make_mixed, 0)
    proj[...] = jnp.dot(mixed[...], last, preferred_element_type=F32)
    sum_start(3, wide_sums(proj, CHANNELS))
    sum_turn(3)
    total, square = unstack_sums(unfold_lanes(sum_end(3)))
    center3, scale3, mul3, add3 = norm_terms(total, square, gain_three, bias_three, pixels)

    found = []
    for start in range(0, CHANNELS, 256):
        lanes = slice(start, start + 256)
        m3, a3, c3, s3 = mul3[:, lanes], add3[:, lanes], center3[:, lanes], scale3[:, lanes]

        def make_out(row, carry):
            rows = pl.ds(row, CHUNK)
            values = grouped(proj[rows, lanes])
            summed = grouped(x_v[rows, lanes].astype(F32)) + (values * m3 + a3)
            gate = sigmoid(summed)
            bo4[pl.ds(row // 4, CHUNK // 4), :, lanes] = by_four(summed * gate).astype(BF16)
            upstream = grouped(gy_v[rows, lanes].astype(F32)) * (
                gate * (1.0 + summed * (1.0 - gate))
            )
            up[rows, lanes] = flat(upstream)
            normed = (values - c3) * s3
            return carry[0] + jnp.sum(upstream, axis=0), carry[1] + jnp.sum(
                upstream * normed, axis=0
            )

        zero = jnp.zeros((8, 256), F32)
        found.append(over_rows(make_out, (zero, zero)))
    bias_sum = micro_sum(jnp.concatenate([item[0] for item in found], axis=1))
    gain_sum = micro_sum(jnp.concatenate([item[1] for item in found], axis=1))
    sum_start(4, fold_lanes(stack_sums(bias_sum, gain_sum)))
    bo_copy = pltpu.make_async_copy(bo4, bo_hbm, local_sem.at[2])
    bo_copy.start()

    def write_norm(at, pattern):
        both = pattern[0:1, :] + pattern[2:3, :]
        for k in range(both.shape[1] // 128):
            np_full[at // 128 + k : at // 128 + k + 1, :] = both[:, k * 128 : k * 128 + 128]

    sum_turn(4)
    bias_sum, gain_sum = unstack_sums(unfold_lanes(sum_end(4)))
    write_norm(2304, gain_sum)
    write_norm(3328, bias_sum)
    by_value, constant = back_terms(center3, scale3, mul3, bias_sum, gain_sum, pixels)
    for start in range(0, CHANNELS, 256):
        lanes = slice(start, start + 256)
        m3, v3, k3 = mul3[:, lanes], by_value[:, lanes], constant[:, lanes]

        def make_dproj(row, carry):
            rows = pl.ds(row, CHUNK)
            values = grouped(up[rows, lanes]) * m3 + grouped(proj[rows, lanes]) * v3 + k3
            dproj[rows, lanes] = flat(values).astype(BF16)
            return carry

        over_rows(make_dproj, 0)

    d_mixed[...] = dot_t(dproj[...], last)

    def attend(row, carry):
        rows = pl.ds(row, CHUNK)
        values = grouped(d_mixed[rows, :])
        return (
            carry[0] + jnp.sum(values * grouped(splits[rows, 0:256]), axis=0),
            carry[1] + jnp.sum(values * grouped(splits[rows, 256:512]), axis=0),
        )

    zero = jnp.zeros((8, 256), F32)
    d_att0, d_att1 = over_rows(attend, (zero, zero))
    d_att0, d_att1 = image_sum(d_att0), image_sum(d_att1)
    both = att0 * d_att0 + att1 * d_att1
    d_logits = jnp.concatenate([att0 * (d_att0 - both), att1 * (d_att1 - both)], axis=1)
    d_hidden = exact_dot(d_logits, expand, True)
    d_pool = d_hidden * slope_p
    per_micro = stack_sums(pair_sum(d_pool), pair_sum(d_pool * normed_p))
    ex_sum = pair_sum(d_logits)
    ex_sum = ex_sum + pltpu.roll(ex_sum, 2, 0)
    ids = row_ids(128)
    ex_rows_sum = jnp.where(ids == 0, ex_sum[:, 0:128], 0.0)
    for k in range(1, 4):
        ex_rows_sum = ex_rows_sum + jnp.where(ids == k, ex_sum[:, k * 128 : k * 128 + 128], 0.0)
    sum_start(5, jnp.concatenate([per_micro, ex_rows_sum], axis=0))

    grad_ex = image_dot(hidden, d_logits)
    grad_ex = grad_ex.reshape(n_dp, ex_rows, 512)
    ge[:, 0:ex_rows, 128:384] = grad_ex[:, :, 0:256]
    ge[:, ex_rows : 2 * ex_rows, 128:384] = grad_ex[:, :, 256:512]
    ge[:, :, 384:512] = jnp.zeros((n_dp, 2 * ex_rows, 128), F32)
    g3[...] = tdot(mixed[...], dproj[...]).reshape(g3.shape)
    reduce_core(3)
    sum_turn(5)
    whole = sum_end(5)
    pool_bias_sum, pool_gain_sum = unstack_sums(whole[0:8])
    write_norm(1536, pool_gain_sum)
    write_norm(1664, pool_bias_sum)
    np_full[14:18, :] = whole[8:12]
    d_pre_pool = mul_p * (
        d_pool - pool_bias_sum / pictures - normed_p * (pool_gain_sum / pictures)
    )
    d_pooled = exact_dot(d_pre_pool, squeeze, True) / (SIDE * SIDE)
    found = []
    for group, att in ((0, att0), (1, att1)):
        lanes = slice(group * 256, group * 256 + 256)
        m2, a2, c2, s2 = mul2[:, lanes], add2[:, lanes], center2[:, lanes], scale2[:, lanes]

        def make_dn2(row, carry):
            rows = pl.ds(row, CHUNK)
            values = grouped(wid[rows, lanes])
            turned = values * m2 + a2
            gate = sigmoid(turned)
            slope = gate * (1.0 + turned * (1.0 - gate))
            down = (grouped(d_mixed[rows, :]) * att + d_pooled) * slope
            dn2[rows, lanes] = flat(down)
            normed = (values - c2) * s2
            return carry[0] + jnp.sum(down, axis=0), carry[1] + jnp.sum(down * normed, axis=0)

        found.append(over_rows(make_dn2, (zero, zero)))
    bias_sum = micro_sum(jnp.concatenate([item[0] for item in found], axis=1))
    gain_sum = micro_sum(jnp.concatenate([item[1] for item in found], axis=1))
    sum_start(6, fold_lanes(stack_sums(bias_sum, gain_sum)))
    ge[:, :, 0:128] = image_dot(pooled, d_pre_pool).reshape(n_dp, 2 * ex_rows, 128)
    reduce_core(4)
    sum_turn(6)
    reduce_y(3)
    reduce_y(4)
    bias_sum, gain_sum = unstack_sums(unfold_lanes(sum_end(6)))
    write_norm(512, gain_sum)
    write_norm(1024, bias_sum)
    by_value, constant = back_terms(center2, scale2, mul2, bias_sum, gain_sum, pixels)

    for group in range(2):
        lanes = slice(group * 256, group * 256 + 256)
        m2, v2, k2 = mul2[:, lanes], by_value[:, lanes], constant[:, lanes]

        def make_dwid(row, carry):
            rows = pl.ds(row, CHUNK)
            values = grouped(dn2[rows, lanes]) * m2 + grouped(wid[rows, lanes]) * v2 + k2
            dwid[rows, lanes] = flat(values).astype(BF16)
            return carry

        over_rows(make_dwid, 0)
        dcol[PAD : PAD + ROWS, group * 1152 : group * 1152 + 1152] = dot_t(
            dwid[:, lanes], filters(group)
        )

    def gather_taps(row, carry):
        for side in range(3):
            for group in range(2):
                total = None
                for down in range(3):
                    at = group * 1152 + (3 * down + side) * 128
                    values = dcol[pl.ds(PAD + row - 56 * (down - 1), CHUNK), at : at + 128]
                    total = values if total is None else total + values
                act[side, pl.ds(PAD + row, CHUNK), group * 128 : group * 128 + 128] = total
        return carry

    over_rows(gather_taps, 0)

    def make_dn1(row, carry):
        rows = pl.ds(row, CHUNK)
        d_active = act[1, pl.ds(PAD + row, CHUNK), :]
        d_active = d_active + jnp.where(not_first, beside(2, row, -4), 0.0)
        d_active = d_active + jnp.where(not_last, beside(0, row, 4), 0.0)
        values = grouped(red[rows, :])
        turned = values * mul1 + add1
        gate = sigmoid(turned)
        slope = gate * (1.0 + turned * (1.0 - gate))
        down = grouped(d_active) * slope
        dn1[rows, :] = flat(down)
        normed = (values - center1) * scale1
        return carry[0] + jnp.sum(down, axis=0), carry[1] + jnp.sum(down * normed, axis=0)

    bias_sum, gain_sum = over_rows(make_dn1, (zero, zero))
    sum_start(7, fold_lanes(stack_sums(micro_sum(bias_sum), micro_sum(gain_sum))))
    reduce_owner(3)
    reduce_owner(4)

    def grad_conv(group):
        gc[group * own_half : (group + 1) * own_half] = tdot(
            columns[group], dwid[:, group * 256 : group * 256 + 256]
        ).reshape(own_half, 2, 9 * 128 // own_half // 2, BOTTLE)

    grad_conv(0)
    sum_turn(7)
    grad_conv(1)
    reduce_core(1)
    reduce_core(2)
    bias_sum, gain_sum = unstack_sums(unfold_lanes(sum_end(7)))
    write_norm(0, gain_sum)
    write_norm(256, bias_sum)
    by_value, constant = back_terms(center1, scale1, mul1, bias_sum, gain_sum, pixels)
    norm_rows = np_full[0:8, :]
    for d in range(1, n_dp):
        at = shard * d // 128
        norm_rows = jnp.where(dp == d, np_full[at : at + 8, :], norm_rows)
    norm_rows = pltpu.roll(norm_rows, lax.rem(128 - turn, 128), 1)
    gn_out[...] = jnp.where(lanes_id < 128 - turn, norm_rows, pltpu.roll(norm_rows, 7, 0))

    def make_dred(row, carry):
        rows = pl.ds(row, CHUNK)
        values = grouped(dn1[rows, :]) * mul1 + grouped(red[rows, :]) * by_value + constant
        dred[rows, :] = flat(values).astype(BF16)
        return carry

    over_rows(make_dred, 0)
    g1[...] = tdot(x_v[...], dred[...]).reshape(g1.shape)
    reduce_core(0)
    reduce_y(1)
    reduce_y(2)
    proj[...] = dot_t(dred[...], fw1[...].reshape(CHANNELS, BOTTLE))
    reduce_y(0)
    reduce_spread(3)
    reduce_spread(4)
    reduce_owner(1)

    def make_dx(row, carry):
        for start in range(0, CHANNELS, 256):
            lanes = slice(start, start + 256)
            values = up[pl.ds(row, CHUNK), lanes] + proj[pl.ds(row, CHUNK), lanes]
            dx4[pl.ds(row // 4, CHUNK // 4), :, lanes] = values.reshape(CHUNK // 4, 4, 256)
        return carry

    over_rows(make_dx, 0)
    dx_copy = pltpu.make_async_copy(dx4, dx_hbm, local_sem.at[3])
    dx_copy.start()
    reduce_owner(2)
    reduce_owner(0)
    reduce_spread(1)
    reduce_spread(2)
    reduce_spread(0)
    out_copies = [
        pltpu.make_async_copy(source, target, local_sem.at[10 + k])
        for k, (source, target) in enumerate(
            (
                (gn_out, gn_hbm),
                (fs[2], f3_hbm),
                (fs[3], fe_hbm),
                (fs[1], fc_hbm),
                (fs[0], f1_hbm),
            )
        )
    ]
    out_copies[0].start()
    for which in (3, 4, 1, 2, 0):
        reduce_end(which)
        if which != 1:
            out_copies[{3: 1, 4: 2, 2: 3, 0: 4}[which]].start()

    bo_copy.wait()
    dx_copy.wait()
    for copy in out_copies:
        copy.wait()
    for k in range(n_ar):
        wait_bytes(ar_slots_a[k].at[pl.ds(0, plane_size - 1)], ar_send_a.at[k])
        wait_bytes(ar_slots_b[k].at[pl.ds(0, planes - 1)], ar_send_b.at[k])
    wait_bytes(np_slots.at[pl.ds(0, n_dp - 1)], np_sems.at[0])
    for which in range(3):
        wait_bytes(seven(which), ws.at[which, 0])
        for stage in range(1, 4):
            wait_bytes(quarters[which](core, half_y), ws.at[which, stage])
    for which in range(5):
        wait_bytes(r1s[which], gs.at[which, 0])
        wait_bytes(r2s[which], gs.at[which, 1])
        wait_bytes(r3s[which].at[pl.ds(0, n_dp - 1)], gs.at[which, 2])
        wait_bytes(three_parts(which), gs.at[which, 3])


def update_kernel(*refs):
    sources, targets = refs[0:25], refs[25:45]
    inputs, outs, pass_sems, in_sems, out_sems = refs[45:68], refs[68:86], *refs[86:89]
    coming = [
        pltpu.make_async_copy(source, held, in_sems.at[k])
        for k, (source, held) in enumerate(zip(sources[2:], inputs))
    ]
    for copy in coming:
        copy.start()
    part = SIDE * SIDE // 4
    passing = []
    for which in range(2):
        for k in range(4):
            rows = pl.ds(k * part, part)
            passing.append(
                pltpu.make_async_copy(
                    sources[which].at[rows], targets[which].at[rows], pass_sems.at[which, k]
                )
            )
    for copy in passing:
        copy.start()
    grads, states = inputs[0:5], inputs[5:23]
    going = [
        pltpu.make_async_copy(held, target, out_sems.at[k])
        for k, (held, target) in enumerate(zip(outs, targets[2:]))
    ]
    ex_rows = states[9].shape[0]
    shard = states[15].shape[0]
    fans = (CHANNELS, 9 * BOTTLE // RADIX, BOTTLE, INNER // 8, BOTTLE)
    for copy in coming[0:5]:
        copy.wait()
    found = (
        grads[0][...],
        grads[1][...],
        grads[3][:, 0:128],
        jnp.concatenate([grads[3][0:ex_rows, 128:384], grads[3][ex_rows:, 128:384]], axis=1),
        grads[2][...],
    )
    for k in (1, 0, 4, 3, 2):
        for copy in coming[5 + 3 * k : 8 + 3 * k]:
            copy.wait()
        new = adamw(
            states[3 * k][...],
            states[3 * k + 1][...],
            states[3 * k + 2][...],
            found[k],
            2.0 * fans[k] ** (-0.5),
            DECAY,
        )
        for j in range(3):
            outs[3 * k + j][...] = new[j]
            going[3 * k + j].start()
    for copy in coming[20:23]:
        copy.wait()
    for at in range(0, shard, 128):
        width = min(128, shard - at)
        lanes = pl.ds(at, width)
        new = adamw(
            *[states[15 + j][lanes].reshape(1, width) for j in range(3)],
            grads[4][at // 128 : at // 128 + 1, 0:width],
            NORM_RATE,
            0.0,
        )
        for j in range(3):
            outs[15 + j][lanes] = new[j].reshape(width)
    for copy in going[15:18]:
        copy.start()
    for copy in passing + going:
        copy.wait()


def fused_device(
    images,
    out_grad,
    reduce_weight,
    reduce_moment,
    reduce_second,
    conv_weight,
    conv_moment,
    conv_second,
    squeeze_weight,
    squeeze_moment,
    squeeze_second,
    expand_weight,
    expand_moment,
    expand_second,
    project_weight,
    project_moment,
    project_second,
    norm_params,
    norm_moment,
    norm_second,
):
    n_dp, n_rep = lax.axis_size("dp"), lax.axis_size("rep")
    by_pixel = lambda values: jnp.transpose(values, (1, 2, 0, 3)).reshape(-1, 4, CHANNELS)
    qc = conv_weight.shape[0] // 2
    q1 = reduce_weight.shape[0] // 4
    pe = squeeze_weight.shape[0]
    vmem = pltpu.VMEM
    pixel_form = (SIDE * SIDE, 4, CHANNELS)
    scratch = [
        *[
            vmem(values.shape, F32)
            for values in (
                reduce_weight,
                conv_weight,
                squeeze_weight,
                expand_weight,
                project_weight,
                norm_params,
            )
        ],
        vmem((8, 128), F32),
        vmem(pixel_form, BF16),
        vmem(pixel_form, BF16),
        vmem((ROWS, CHANNELS), BF16),
        vmem((ROWS, CHANNELS), BF16),
        vmem((n_dp, 2, 2, q1, BOTTLE), BF16),
        vmem((n_dp, 2, qc, BOTTLE), BF16),
        vmem((n_dp, pe, 1536), BF16),
        vmem((pe, 1536), BF16),
        vmem((n_dp, 8, 128), F32),
        vmem((40, 128), F32),
        vmem((ROWS, BOTTLE), F32),
        vmem((3, ROWS + 2 * PAD, BOTTLE), F32),
        vmem((2, ROWS, 9 * 128), BF16),
        vmem((ROWS, 512), F32),
        vmem((ROWS, 512), F32),
        vmem((ROWS, BOTTLE), BF16),
        vmem((ROWS, CHANNELS), F32),
        vmem((ROWS, CHANNELS), F32),
        vmem(pixel_form, BF16),
        vmem(pixel_form, F32),
        vmem((ROWS, CHANNELS), BF16),
        vmem((ROWS, BOTTLE), F32),
        vmem((ROWS, 512), F32),
        vmem((ROWS, 512), BF16),
        vmem((ROWS + 2 * PAD, 2 * 9 * 128), F32),
        vmem((ROWS, BOTTLE), F32),
        vmem((ROWS, BOTTLE), BF16),
        vmem((n_dp, 2, 2, q1, BOTTLE), F32),
        vmem((n_dp, 2, qc, BOTTLE), F32),
        vmem((n_dp, pe, CHANNELS), F32),
        vmem((n_dp, pe, 512), F32),
    ]
    scratch += [vmem((2 * n_rep,) + shape, F32) for shape in STATS]
    scratch += [vmem((n_dp // 2,) + shape, F32) for shape in STATS]
    cut = 64
    half = [
        (n_dp, 2, q1, BOTTLE),
        (n_dp, 2, cut, 128),
        (n_dp, 2, qc - cut, 128),
        (n_dp, pe, 512),
        (n_dp, pe, 256),
    ]
    quarter = [
        (n_dp, q1, BOTTLE),
        (n_dp, cut, 128),
        (n_dp, qc - cut, 128),
        (n_dp, pe, 256),
        (n_dp, pe, 128),
    ]
    final = [(2, 2, q1, BOTTLE), (2, qc, BOTTLE), (pe, CHANNELS), (pe, 512)]
    sent = [BF16, BF16, BF16, BF16, F32]
    scratch += [vmem(shape, F32) for shape in half]
    scratch += [vmem(shape, kind) for shape, kind in zip(quarter, sent)] * 4
    scratch += [vmem(shape[1:], F32) for shape in quarter]
    scratch += [vmem(shape, F32) for shape in final]
    dma = pltpu.SemaphoreType.DMA
    scratch += [dma((15,))] + [dma((len(STATS),))] * 4 + [dma((2,))] + [dma((3, 4))] * 2 + [dma((5, 4))] * 2
    any_space = pl.BlockSpec(memory_space=pl.ANY)
    block_out, images_grad, sum1, sumc, sum3, sume, norm_grads = pl.pallas_call(
        functools.partial(block_kernel, n_dp, n_rep),
        out_shape=[
            jax.ShapeDtypeStruct(pixel_form, BF16),
            jax.ShapeDtypeStruct(pixel_form, F32),
            *[jax.ShapeDtypeStruct(shape, F32) for shape in final],
            jax.ShapeDtypeStruct((8, 128), F32),
        ],
        in_specs=[any_space] * 8,
        out_specs=[any_space] * 7,
        scratch_shapes=scratch,
        compiler_params=pltpu.CompilerParams(
            collective_id=0, has_side_effects=True, vmem_limit_bytes=63 * 1024 * 1024
        ),
    )(
        by_pixel(images),
        by_pixel(out_grad),
        reduce_weight,
        conv_weight,
        squeeze_weight,
        expand_weight,
        project_weight,
        norm_params,
    )
    states = (
        reduce_weight,
        reduce_moment,
        reduce_second,
        conv_weight,
        conv_moment,
        conv_second,
        squeeze_weight,
        squeeze_moment,
        squeeze_second,
        expand_weight,
        expand_moment,
        expand_second,
        project_weight,
        project_moment,
        project_second,
    )
    held = (*states, norm_params, norm_moment, norm_second)
    sums = (
        sum1.reshape(reduce_weight.shape),
        sumc.reshape(conv_weight.shape),
        sum3,
        sume,
        norm_grads,
    )
    block_out, images_grad, *updated = pl.pallas_call(
        update_kernel,
        out_shape=[
            jax.ShapeDtypeStruct(pixel_form, BF16),
            jax.ShapeDtypeStruct(pixel_form, F32),
            *[jax.ShapeDtypeStruct(state.shape, F32) for state in held],
        ],
        in_specs=[any_space] * 25,
        out_specs=[any_space] * 20,
        scratch_shapes=[vmem(values.shape, F32) for values in (*sums, *held, *held)]
        + [dma((2, 4)), dma((23,)), dma((18,))],
        compiler_params=pltpu.CompilerParams(vmem_limit_bytes=63 * 1024 * 1024),
    )(block_out, images_grad, *sums, *held)
    by_image = lambda values: jnp.transpose(
        values.reshape(SIDE, SIDE, images.shape[0], CHANNELS), (2, 0, 1, 3)
    )
    return (
        by_image(block_out),
        by_image(images_grad),
        *updated,
    )


def solution(mesh):
    placed = (
        P(("dp", "rep"), None, None, None),
        P(("dp", "rep"), None, None, None),
        P("dp", None),
        P("dp", None),
        P("dp", None),
        P("dp", None),
        P("dp", None),
        P("dp", None),
        P("dp", None),
        P("dp", None),
        P("dp", None),
        P("dp", None),
        P("dp", None),
        P("dp", None),
        P("dp", None),
        P("dp", None),
        P("dp", None),
        P("dp"),
        P("dp"),
        P("dp"),
    )
    n_dp, n_rep = mesh.shape["dp"], mesh.shape["rep"]
    whole_tiles = n_rep == 4 and n_dp % 2 == 0 and INNER % (16 * n_dp) == 0
    return jax.shard_map(
        fused_device if whole_tiles else per_device,
        mesh=mesh,
        in_specs=placed,
        out_specs=(
            P(("dp", "rep"), None, None, None),
            P(("dp", "rep"), None, None, None),
            P("dp", None),
            P("dp", None),
            P("dp", None),
            P("dp", None),
            P("dp", None),
            P("dp", None),
            P("dp", None),
            P("dp", None),
            P("dp", None),
            P("dp", None),
            P("dp", None),
            P("dp", None),
            P("dp", None),
            P("dp", None),
            P("dp", None),
            P("dp"),
            P("dp"),
            P("dp"),
        ),
        check_vma=False,
    )
```

```python
import functools
import jax
import jax.numpy as jnp
from jax import lax
from jax.experimental import pallas as pl
from jax.experimental.pallas import tpu as pltpu
from jax.sharding import PartitionSpec as P

CHANNELS = 1024
BOTTLE = 256
INNER = 128
RADIX = 2
SIDE = 14
MICRO = 2
STEP = 10


EPSILON = 1e-05
PRECISE = lax.Precision.HIGHEST
BETA_ONE = 0.9
BETA_TWO = 0.999
ADAM_EPSILON = 1e-08
DECAY = 0.01
NORM_RATE = 0.8
ROWS = 4 * SIDE * SIDE
NORM_WIDTH = 4352


def split_params(packed):
    widths = (
        BOTTLE,
        BOTTLE,
        RADIX * BOTTLE,
        RADIX * BOTTLE,
        INNER,
        INNER,
        RADIX * BOTTLE,
        CHANNELS,
        CHANNELS,
    )
    pieces = []
    offset = 0
    for segment in widths:
        pieces.append(lax.slice_in_dim(packed, offset, offset + segment))
        offset = offset + segment
    return pieces


def silu_slope(values):
    logistic = jax.nn.sigmoid(values)
    return logistic * (1.0 + values * (1.0 - logistic))


def norm_forward(values, gain, bias, count):
    flat = values.reshape(-1, values.shape[-1])
    total, square = lax.psum((jnp.sum(flat, axis=0), jnp.sum(flat * flat, axis=0)), ("dp", "rep"))
    center = total / count
    scale = lax.rsqrt(square / count - center * center + EPSILON)
    normed = (values - center) * scale
    return (normed * gain + bias, normed, scale)


def norm_backward(upstream, normed, scale, gain, count):
    flat_up = upstream.reshape(-1, upstream.shape[-1])
    flat_norm = normed.reshape(-1, normed.shape[-1])
    bias_sum, gain_sum = lax.psum(
        (jnp.sum(flat_up, axis=0), jnp.sum(flat_up * flat_norm, axis=0)), ("dp", "rep")
    )
    downstream = gain * scale * (upstream - bias_sum / count - normed * (gain_sum / count))
    return (downstream, gain_sum, bias_sum)


def patches(active):
    padded = jnp.pad(active, ((0, 0), (1, 1), (1, 1), (0, 0), (0, 0)))
    shifted = [
        padded[:, down_step : down_step + SIDE, side_step : side_step + SIDE]
        for down_step in range(3)
        for side_step in range(3)
    ]
    return jnp.stack(shifted, axis=4)


def unpatch(columns):
    total = jnp.zeros(
        (columns.shape[0], SIDE + 2, SIDE + 2, columns.shape[3], columns.shape[5]), jnp.float32
    )
    for down_step in range(3):
        for side_step in range(3):
            piece = columns[:, :, :, :, 3 * down_step + side_step]
            total = total + jnp.pad(
                piece,
                ((0, 0), (down_step, 2 - down_step), (side_step, 2 - side_step), (0, 0), (0, 0)),
            )
    return total[:, 1 : SIDE + 1, 1 : SIDE + 1]


def adamw(param, moment, second, gradient, rate, decay):
    moment_new = BETA_ONE * moment + (1.0 - BETA_ONE) * gradient
    second_new = BETA_TWO * second + (1.0 - BETA_TWO) * gradient * gradient
    ratio = (
        moment_new
        / (1.0 - BETA_ONE**STEP)
        / (jnp.sqrt(second_new / (1.0 - BETA_TWO**STEP)) + ADAM_EPSILON)
    )
    return (param - rate * (ratio + decay * param), moment_new, second_new)


def per_device(
    images,
    out_grad,
    reduce_weight,
    reduce_moment,
    reduce_second,
    conv_weight,
    conv_moment,
    conv_second,
    squeeze_weight,
    squeeze_moment,
    squeeze_second,
    expand_weight,
    expand_moment,
    expand_second,
    project_weight,
    project_moment,
    project_second,
    norm_params,
    norm_moment,
    norm_second,
):
    bf16 = jnp.bfloat16
    low_reduce = reduce_weight.astype(bf16)
    low_conv = conv_weight.astype(bf16)
    low_squeeze = squeeze_weight.astype(bf16)
    low_expand = expand_weight.astype(bf16)
    low_project = project_weight.astype(bf16)
    low_norm = norm_params.astype(bf16)
    devices = lax.axis_size("dp") * lax.axis_size("rep")
    per_batch = images.shape[0] // MICRO
    pixel_count = float(per_batch * SIDE * SIDE * devices)
    image_count = float(per_batch * devices)
    group_in = BOTTLE // RADIX
    grad_first = jnp.zeros((CHANNELS, BOTTLE), jnp.float32)
    grad_conv = jnp.zeros((RADIX, 9 * group_in, BOTTLE), jnp.float32)
    grad_squeeze = jnp.zeros((BOTTLE, INNER), jnp.float32)
    grad_expand = jnp.zeros((INNER, RADIX * BOTTLE), jnp.float32)
    grad_last = jnp.zeros((BOTTLE, CHANNELS), jnp.float32)
    grad_norms = jnp.zeros(
        (2 * BOTTLE + 3 * RADIX * BOTTLE + 2 * INNER + 2 * CHANNELS,), jnp.float32
    )
    outputs = []
    input_grads = []
    for number in range(MICRO):
        forward_set = (
            lax.all_gather(low_reduce, "dp", axis=0, tiled=True),
            lax.all_gather(low_conv, "dp", axis=0, tiled=True),
            lax.all_gather(low_squeeze, "dp", axis=0, tiled=True),
            lax.all_gather(low_expand, "dp", axis=0, tiled=True),
            lax.all_gather(low_project, "dp", axis=0, tiled=True),
            lax.all_gather(low_norm, "dp", axis=0, tiled=True),
        )
        first, conv, squeeze, expand, last, packed = forward_set
        (
            gain_one,
            bias_one,
            gain_two,
            bias_two,
            gain_pool,
            bias_pool,
            bias_expand,
            gain_three,
            bias_three,
        ) = split_params(packed.astype(jnp.float32))
        batched = images[number * per_batch : (number + 1) * per_batch]
        cotangent = out_grad[number * per_batch : (number + 1) * per_batch]
        reduced = jnp.einsum("nhwc,cb->nhwb", batched, first, preferred_element_type=jnp.float32)
        norm_one, normed_one, scale_one = norm_forward(reduced, gain_one, bias_one, pixel_count)
        active = jax.nn.silu(norm_one).astype(bf16)
        columns = patches(active.reshape(per_batch, SIDE, SIDE, RADIX, group_in)).reshape(
            per_batch * SIDE * SIDE, RADIX, 9 * group_in
        )
        conv_grouped = conv.reshape(RADIX, 9 * group_in, BOTTLE)
        widened = jnp.einsum(
            "prk,rko->pro", columns, conv_grouped, preferred_element_type=jnp.float32
        )
        widened = widened.reshape(per_batch, SIDE, SIDE, RADIX * BOTTLE)
        norm_two, normed_two, scale_two = norm_forward(widened, gain_two, bias_two, pixel_count)
        splits = jax.nn.silu(norm_two).reshape(per_batch, SIDE, SIDE, RADIX, BOTTLE)
        pooled = jnp.sum(jnp.sum(splits, axis=3), axis=(1, 2)) / (SIDE * SIDE)
        squeeze_float = squeeze.astype(jnp.float32)
        expand_float = expand.astype(jnp.float32)
        pre_pool = jnp.dot(pooled, squeeze_float, precision=PRECISE)
        norm_pool, normed_pool, scale_pool = norm_forward(
            pre_pool, gain_pool, bias_pool, image_count
        )
        hidden = jax.nn.silu(norm_pool)
        logits = (jnp.dot(hidden, expand_float, precision=PRECISE) + bias_expand).reshape(
            per_batch, RADIX, BOTTLE
        )
        attention = jax.nn.softmax(logits, axis=1)
        mixed = jnp.sum(splits * attention[:, None, None], axis=3).astype(bf16)
        projected = jnp.einsum("nhwb,bc->nhwc", mixed, last, preferred_element_type=jnp.float32)
        norm_three, normed_three, scale_three = norm_forward(
            projected, gain_three, bias_three, pixel_count
        )
        summed = batched.astype(jnp.float32) + norm_three
        outputs.append(jax.nn.silu(summed).astype(bf16))
        backward_set = (
            lax.all_gather(low_reduce, "dp", axis=0, tiled=True),
            lax.all_gather(low_conv, "dp", axis=0, tiled=True),
            lax.all_gather(low_squeeze, "dp", axis=0, tiled=True),
            lax.all_gather(low_expand, "dp", axis=0, tiled=True),
            lax.all_gather(low_project, "dp", axis=0, tiled=True),
            lax.all_gather(low_norm, "dp", axis=0, tiled=True),
        )
        first, conv, squeeze, expand, last, packed = backward_set
        gains_back = split_params(packed.astype(jnp.float32))
        conv_grouped = conv.reshape(RADIX, 9 * group_in, BOTTLE)
        expand_float = expand.astype(jnp.float32)
        squeeze_float = squeeze.astype(jnp.float32)
        upstream = cotangent.astype(jnp.float32) * silu_slope(summed)
        d_projected, gain_three_grad, bias_three_grad = norm_backward(
            upstream, normed_three, scale_three, gains_back[7], pixel_count
        )
        d_projected_low = d_projected.astype(bf16)
        grad_last = grad_last + jnp.einsum(
            "nhwb,nhwc->bc", mixed, d_projected_low, preferred_element_type=jnp.float32
        )
        d_mixed = jnp.einsum(
            "nhwc,bc->nhwb", d_projected_low, last, preferred_element_type=jnp.float32
        )
        d_splits = d_mixed[:, :, :, None] * attention[:, None, None]
        d_attention = jnp.sum(d_mixed[:, :, :, None] * splits, axis=(1, 2))
        d_logits = attention * (
            d_attention - jnp.sum(attention * d_attention, axis=1, keepdims=True)
        )
        flat_logits = d_logits.reshape(per_batch, RADIX * BOTTLE)
        grad_expand = grad_expand + jnp.dot(hidden.T, flat_logits, precision=PRECISE)
        d_hidden = jnp.dot(flat_logits, expand_float.T, precision=PRECISE)
        d_pool_norm = d_hidden * silu_slope(norm_pool)
        pool_bias_sum, pool_gain_sum, expand_bias_sum = lax.psum(
            (
                jnp.sum(d_pool_norm, axis=0),
                jnp.sum(d_pool_norm * normed_pool, axis=0),
                jnp.sum(flat_logits, axis=0),
            ),
            ("dp", "rep"),
        )
        d_pre_pool = (
            gains_back[4]
            * scale_pool
            * (
                d_pool_norm
                - pool_bias_sum / image_count
                - normed_pool * (pool_gain_sum / image_count)
            )
        )
        grad_squeeze = grad_squeeze + jnp.dot(pooled.T, d_pre_pool, precision=PRECISE)
        d_pooled = jnp.dot(d_pre_pool, squeeze_float.T, precision=PRECISE)
        d_splits = d_splits + (d_pooled / (SIDE * SIDE))[:, None, None, None, :]
        d_norm_two = d_splits.reshape(per_batch, SIDE, SIDE, RADIX * BOTTLE) * silu_slope(norm_two)
        d_widened, gain_two_grad, bias_two_grad = norm_backward(
            d_norm_two, normed_two, scale_two, gains_back[2], pixel_count
        )
        d_widened_low = d_widened.astype(bf16).reshape(per_batch * SIDE * SIDE, RADIX, BOTTLE)
        grad_conv = grad_conv + jnp.einsum(
            "prk,pro->rko", columns, d_widened_low, preferred_element_type=jnp.float32
        )
        d_columns = jnp.einsum(
            "pro,rko->prk", d_widened_low, conv_grouped, preferred_element_type=jnp.float32
        )
        d_active = unpatch(d_columns.reshape(per_batch, SIDE, SIDE, RADIX, 9, group_in)).reshape(
            per_batch, SIDE, SIDE, BOTTLE
        )
        d_norm_one = d_active * silu_slope(norm_one)
        d_reduced, gain_one_grad, bias_one_grad = norm_backward(
            d_norm_one, normed_one, scale_one, gains_back[0], pixel_count
        )
        d_reduced_low = d_reduced.astype(bf16)
        grad_first = grad_first + jnp.einsum(
            "nhwc,nhwb->cb", batched, d_reduced_low, preferred_element_type=jnp.float32
        )
        input_grads.append(
            upstream
            + jnp.einsum("nhwb,cb->nhwc", d_reduced_low, first, preferred_element_type=jnp.float32)
        )
        grad_norms = grad_norms + jnp.concatenate(
            [
                gain_one_grad,
                bias_one_grad,
                gain_two_grad,
                bias_two_grad,
                pool_gain_sum,
                pool_bias_sum,
                expand_bias_sum,
                gain_three_grad,
                bias_three_grad,
            ]
        )
    grad_conv = grad_conv.reshape(9 * BOTTLE, BOTTLE)
    partial_value = (
        lax.psum_scatter(grad_first, "dp", scatter_dimension=0, tiled=True),
        lax.psum_scatter(grad_conv, "dp", scatter_dimension=0, tiled=True),
        lax.psum_scatter(grad_squeeze, "dp", scatter_dimension=0, tiled=True),
        lax.psum_scatter(grad_expand, "dp", scatter_dimension=0, tiled=True),
        lax.psum_scatter(grad_last, "dp", scatter_dimension=0, tiled=True),
    )
    owned = lax.psum(
        (partial_value[0], partial_value[1], partial_value[2], partial_value[3], partial_value[4]),
        "rep",
    )
    shard_length = norm_params.shape[0]
    norm_grad_owned = lax.dynamic_slice_in_dim(
        grad_norms, lax.axis_index("dp") * shard_length, shard_length
    )
    reduce_new = adamw(
        reduce_weight, reduce_moment, reduce_second, owned[0], 2.0 * CHANNELS ** (-0.5), DECAY
    )
    conv_new = adamw(
        conv_weight,
        conv_moment,
        conv_second,
        owned[1],
        2.0 * (9 * BOTTLE // RADIX) ** (-0.5),
        DECAY,
    )
    squeeze_new = adamw(
        squeeze_weight, squeeze_moment, squeeze_second, owned[2], 2.0 * BOTTLE ** (-0.5), DECAY
    )
    expand_new = adamw(
        expand_weight, expand_moment, expand_second, owned[3], 2.0 * (INNER // 8) ** (-0.5), DECAY
    )
    project_new = adamw(
        project_weight, project_moment, project_second, owned[4], 2.0 * BOTTLE ** (-0.5), DECAY
    )
    norm_new = adamw(norm_params, norm_moment, norm_second, norm_grad_owned, NORM_RATE, 0.0)
    return (
        jnp.concatenate(outputs, axis=0),
        jnp.concatenate(input_grads, axis=0),
        reduce_new[0],
        reduce_new[1],
        reduce_new[2],
        conv_new[0],
        conv_new[1],
        conv_new[2],
        squeeze_new[0],
        squeeze_new[1],
        squeeze_new[2],
        expand_new[0],
        expand_new[1],
        expand_new[2],
        project_new[0],
        project_new[1],
        project_new[2],
        norm_new[0],
        norm_new[1],
        norm_new[2],
    )


MESH = pl.DeviceIdType.MESH
PAD = 64
CHUNK = 112
F32 = jnp.float32
BF16 = jnp.bfloat16
STATS = ((8, 128), (8, 256), (8, 128), (8, 512), (8, 512), (8, 128), (16, 256), (8, 128))
DIRECT = (0, 2, 5, 7)


def sigmoid(values):
    return 0.5 * jnp.tanh(0.5 * values) + 0.5


def row_ids(width):
    return lax.broadcasted_iota(jnp.int32, (8, width), 0)


def image_sum(rows):
    return rows + pltpu.roll(rows, 4, 0)


def pair_sum(rows):
    even = row_ids(rows.shape[1]) % 2 == 0
    return rows + jnp.where(even, pltpu.roll(rows, 7, 0), pltpu.roll(rows, 1, 0))


def micro_sum(rows):
    return pair_sum(image_sum(rows))


def stack_sums(first, second):
    return jnp.where(row_ids(first.shape[1]) < 4, first, second)


def unstack_sums(stacked):
    upper = row_ids(stacked.shape[1]) < 4
    turned = pltpu.roll(stacked, 4, 0)
    return jnp.where(upper, stacked, turned), jnp.where(upper, turned, stacked)


def fold_lanes(stacked):
    half = stacked.shape[1] // 2
    even = row_ids(half) % 2 == 0
    return jnp.where(even, stacked[:, :half], stacked[:, half:])


def unfold_lanes(folded):
    even = row_ids(folded.shape[1]) % 2 == 0
    left = jnp.where(even, folded, pltpu.roll(folded, 1, 0))
    right = jnp.where(even, pltpu.roll(folded, 7, 0), folded)
    return jnp.concatenate([left, right], axis=1)


def norm_terms(total, square, gain, bias, count):
    center = total / count
    scale = lax.rsqrt(square / count - center * center + EPSILON)
    slope = scale * gain
    return center, scale, slope, bias - center * slope


def back_terms(center, scale, slope, bias_sum, gain_sum, count):
    by_value = -slope * scale * (gain_sum / count)
    constant = -slope * (bias_sum / count) - by_value * center
    return by_value, constant


def tdot(left, right):
    return lax.dot_general(left, right, (((0,), (0,)), ((), ())), preferred_element_type=F32)


def dot_t(left, right):
    return lax.dot_general(left, right, (((1,), (1,)), ((), ())), preferred_element_type=F32)


def in_parts(values, parts):
    found = []
    for _ in range(parts):
        rounded = values.astype(BF16).astype(F32)
        found.append(rounded)
        values = values - rounded
    return found


def exact_dot(left, right, transposed):
    stacked = jnp.concatenate(in_parts(left, 3), axis=0).astype(BF16)
    wide = dot_t(stacked, right) if transposed else jnp.dot(stacked, right, preferred_element_type=F32)
    return wide[0:8] + wide[8:16] + wide[16:24]


def image_dot(left, right):
    once = row_ids(left.shape[1]) < 4
    high, low = in_parts(jnp.where(once, left, 0.0), 2)
    other_high, other_low = in_parts(right, 2)
    return tdot(
        jnp.concatenate([high, high, low, low], axis=0).astype(BF16),
        jnp.concatenate([other_high, other_low, other_high, other_low], axis=0).astype(BF16),
    )


def block_kernel(
    n_dp,
    n_rep,
    x_hbm,
    gy_hbm,
    w1_hbm,
    wc_hbm,
    sq_hbm,
    ex_hbm,
    w3_hbm,
    np_hbm,
    bo_hbm,
    dx_hbm,
    f1_hbm,
    fc_hbm,
    f3_hbm,
    fe_hbm,
    gn_hbm,
    w1_own,
    wc_own,
    sq_own,
    ex_own,
    w3_own,
    np_own,
    gn_out,
    x4,
    gy4,
    x_v,
    gy_v,
    fw1,
    fwc,
    fpe,
    pe_own,
    np_slots,
    np_full,
    red,
    act,
    columns,
    wid,
    splits,
    mixed,
    proj,
    up,
    bo4,
    dx4,
    dproj,
    d_mixed,
    dn2,
    dwid,
    dcol,
    dn1,
    dred,
    g1,
    gc,
    g3,
    ge,
    *rest,
):
    n_ar = len(STATS)
    ar_slots_a = rest[0:n_ar]
    ar_slots_b = rest[n_ar : 2 * n_ar]
    rest = rest[2 * n_ar :]
    r1s, ys, r2s, ks, r3s, own = (rest[5 * i : 5 * i + 5] for i in range(6))
    fs = rest[30:34]
    rest = rest[34:]
    local_sem, ar_send_a, ar_recv_a, ar_send_b, ar_recv_b, np_sems, ws, wr, gs, gr = rest

    dp = lax.axis_index("dp")
    rep = lax.axis_index("rep")
    core = lax.rem(rep, 2)
    half_y = lax.div(rep, 2)
    planes = n_dp // 2
    plane_size = 2 * n_rep
    plane = lax.div(dp, 2)
    in_plane = lax.rem(dp, 2) * n_rep + rep
    sibling = (dp, half_y * 2 + (1 - core))
    across = (dp, (1 - half_y) * 2 + core)
    pixels = float(SIDE * SIDE * 2 * n_dp * n_rep)
    pictures = float(2 * n_dp * n_rep)

    in_planes = [lax.rem(in_plane + step, plane_size) for step in range(1, plane_size)]
    plane_peers = [
        (plane * 2 + lax.div(other, n_rep), lax.rem(other, n_rep)) for other in in_planes
    ]
    column_peers = [
        (lax.rem(plane + step, planes) * 2 + lax.rem(dp, 2), rep) for step in range(1, planes)
    ]
    owner_peers = [(lax.rem(dp + step, n_dp), rep) for step in range(1, n_dp)]
    me, everyone = dp * n_rep + rep, n_dp * n_rep
    others = [lax.rem(me + step, everyone) for step in range(1, everyone)]
    all_peers = [(lax.div(other, n_rep), lax.rem(other, n_rep)) for other in others]
    rep_peers = [(dp, lax.rem(rep + step, n_rep)) for step in range(1, n_rep)]

    def remote(src, dst, send_sem, recv_sem, device):
        return pltpu.make_async_remote_copy(
            src_ref=src,
            dst_ref=dst,
            send_sem=send_sem,
            recv_sem=recv_sem,
            device_id=device,
            device_id_type=MESH,
        )

    def send_all(ref, send_sem, recv_sem, peers):
        for device in peers:
            remote(ref, ref, send_sem, recv_sem, device).start()

    def wait_bytes(ref, sem):
        pltpu.make_async_copy(ref, ref, sem).wait()

    def over_rows(body, init):
        def step(index, carry):
            return body(pl.multiple_of(index * CHUNK, CHUNK), carry)

        return lax.fori_loop(0, ROWS // CHUNK, step, init)

    def grouped(values):
        return values.reshape(CHUNK // 8, 8, values.shape[-1])

    def by_four(values):
        return flat(values).reshape(CHUNK // 4, 4, values.shape[-1])

    def flat(values):
        return values.reshape(CHUNK, values.shape[-1])

    own_copies = [
        pltpu.make_async_copy(source, target, local_sem.at[4 + k])
        for k, (source, target) in enumerate(
            (
                (w1_hbm, w1_own),
                (np_hbm, np_own),
                (wc_hbm, wc_own),
                (w3_hbm, w3_own),
                (sq_hbm, sq_own),
                (ex_hbm, ex_own),
            )
        )
    ]
    for copy in own_copies:
        copy.start()
    x_copy = pltpu.make_async_copy(x_hbm, x4, local_sem.at[0])
    gy_copy = pltpu.make_async_copy(gy_hbm, gy4, local_sem.at[1])
    x_copy.start()
    barrier = pltpu.get_barrier_semaphore()
    for device in all_peers:
        pl.semaphore_signal(barrier, inc=1, device_id=device, device_id_type=MESH)

    part = core * 2 + half_y
    own_copies[0].wait()
    q1 = w1_own.shape[0] // 4
    fw1[dp, core, half_y] = w1_own[pl.ds(pl.multiple_of(part * q1, q1), q1), :].astype(BF16)
    core_lanes = pl.ds(pl.multiple_of(core * 128, 128), 128)
    pe_lanes = pl.ds(pl.multiple_of(part * 384, 128), 384)

    pl.semaphore_wait(barrier, everyone - 1)

    def quarter_w1(c, y):
        return fw1.at[:, c, y]

    def quarter_wc(c, y):
        return fwc.at[:, y, :, pl.ds(pl.multiple_of(c * 128, 128), 128)]

    def quarter_pe(c, y):
        return fpe.at[:, :, pl.ds(pl.multiple_of((c * 2 + y) * 384, 128), 384)]

    quarters = (quarter_w1, quarter_wc, quarter_pe)

    def piece(which, d):
        return (
            fw1.at[d, core, half_y],
            fwc.at[d, half_y, :, core_lanes],
            fpe.at[d, :, pe_lanes],
        )[which]

    def seven(which):
        return (
            fw1.at[pl.ds(0, n_dp - 1), core, half_y],
            fwc.at[pl.ds(0, n_dp - 1), half_y, :, core_lanes],
            fpe.at[pl.ds(0, n_dp - 1), :, pe_lanes],
        )[which]

    def gather_out(which):
        send_all(piece(which, dp), ws.at[which, 0], wr.at[which, 0], owner_peers)

    def gather_turn(which):
        wait_bytes(seven(which), wr.at[which, 0])
        mine = quarters[which](core, half_y)
        remote(mine, mine, ws.at[which, 1], wr.at[which, 1], across).start()
        remote(mine, mine, ws.at[which, 2], wr.at[which, 2], sibling).start()

    def gather_hand(which):
        theirs = quarters[which](core, 1 - half_y)
        wait_bytes(theirs, wr.at[which, 1])
        remote(theirs, theirs, ws.at[which, 3], wr.at[which, 3], sibling).start()

    def gather_end(which):
        wait_bytes(quarters[which](1 - core, half_y), wr.at[which, 2])
        wait_bytes(quarters[which](1 - core, 1 - half_y), wr.at[which, 3])

    def to_rows(source, target):
        def body(index, carry):
            values = source[pl.ds(index * (CHUNK // 4), CHUNK // 4)].astype(F32)
            row = pl.multiple_of(index * CHUNK, CHUNK)
            target[pl.ds(row, CHUNK), :] = values.reshape(CHUNK, CHANNELS).astype(BF16)
            return carry

        lax.fori_loop(0, ROWS // CHUNK, body, 0)

    gather_out(0)

    own_copies[1].wait()
    shard = np_own.shape[0]
    lanes_id = lax.broadcasted_iota(jnp.int32, (8, 128), 1)
    turn = lax.rem(shard * dp, 128)
    np_rows = []
    for at in range(0, shard, 128):
        width = min(128, shard - at)
        piece_row = np_own[pl.ds(at, width)].reshape(1, width)
        if width < 128:
            piece_row = jnp.concatenate([piece_row, jnp.zeros((1, 128 - width), F32)], axis=1)
        np_rows.append(piece_row)
    np_rows.append(jnp.zeros((8 - len(np_rows), 128), F32))
    np_turned = jnp.concatenate(np_rows, axis=0).astype(BF16).astype(F32)
    np_turned = pltpu.roll(np_turned, turn, 1)
    np_slots[dp] = jnp.where(lanes_id < turn, pltpu.roll(np_turned, 1, 0), np_turned)
    send_all(np_slots.at[dp], np_sems.at[0], np_sems.at[1], owner_peers)
    own_copies[2].wait()
    qc = wc_own.shape[0] // 2
    fwc[dp, half_y, :, core_lanes] = wc_own[
        pl.ds(pl.multiple_of(half_y * qc, qc), qc), core_lanes
    ].astype(BF16)
    for copy in own_copies[3:]:
        copy.wait()
    ex_rows = ex_own.shape[0]
    pe_own[:, 0:CHANNELS] = w3_own[...].astype(BF16)
    pe_own[:, 1024:1152] = sq_own[...].astype(BF16)
    pe_own[0:ex_rows, 1152:1408] = ex_own[:, 0:256].astype(BF16)
    pe_own[ex_rows : 2 * ex_rows, 1152:1408] = ex_own[:, 256:512].astype(BF16)
    pe_own[:, 1408:1536] = jnp.zeros((2 * ex_rows, 128), BF16)
    fpe[dp, :, pe_lanes] = pe_own[:, pe_lanes]
    gy_copy.start()
    x_copy.wait()
    to_rows(x4, x_v)
    gather_turn(0)
    gather_out(1)
    zero_rows = jnp.zeros((PAD, BOTTLE), F32)
    for side in range(3):
        act[side, 0:PAD, :] = zero_rows
        act[side, PAD + ROWS : 2 * PAD + ROWS, :] = zero_rows
    for lane_block in range(9):
        dcol[0:PAD, lane_block * 256 : lane_block * 256 + 256] = zero_rows
        dcol[PAD + ROWS : 2 * PAD + ROWS, lane_block * 256 : lane_block * 256 + 256] = zero_rows
    gather_hand(0)

    def sum_start(k, payload):
        if k in DIRECT:
            ar_slots_a[k][me] = payload
            send_all(ar_slots_a[k].at[me], ar_send_a.at[k], ar_recv_a.at[k], all_peers)
        else:
            ar_slots_a[k][in_plane] = payload
            send_all(ar_slots_a[k].at[in_plane], ar_send_a.at[k], ar_recv_a.at[k], plane_peers)

    def sum_slots(slots, count):
        sums = [slots[slot] for slot in range(count)]
        while len(sums) > 1:
            sums = [sums[i] + sums[i + 1] for i in range(0, len(sums), 2)]
        return sums[0]

    def sum_turn(k):
        if k in DIRECT:
            return
        wait_bytes(ar_slots_a[k].at[pl.ds(0, plane_size - 1)], ar_recv_a.at[k])
        ar_slots_b[k][plane] = sum_slots(ar_slots_a[k], plane_size)
        send_all(ar_slots_b[k].at[plane], ar_send_b.at[k], ar_recv_b.at[k], column_peers)

    def sum_end(k):
        if k in DIRECT:
            wait_bytes(ar_slots_a[k].at[pl.ds(0, everyone - 1)], ar_recv_a.at[k])
            return sum_slots(ar_slots_a[k], everyone)
        wait_bytes(ar_slots_b[k].at[pl.ds(0, planes - 1)], ar_recv_b.at[k])
        return sum_slots(ar_slots_b[k], planes)

    def lanes_of(index, width):
        return pl.ds(pl.multiple_of(index * width, 128), width)

    cut = 64
    conv_rows = {1: pl.ds(0, cut), 2: pl.ds(cut, gc.shape[2] - cut)}
    grads = (g1, gc, gc, g3, ge)

    def half_of(which, c):
        ref = grads[which]
        if which == 0:
            return ref.at[:, c]
        if which in conv_rows:
            return ref.at[:, :, conv_rows[which], lanes_of(c, 128)]
        return ref.at[:, :, lanes_of(c, (512, 256)[which - 3])]

    def y_part(which, ref, y):
        if which < 3:
            return ref.at[:, y]
        return ref.at[:, :, lanes_of(y, (256, 128)[which - 3])]

    def quarter_of(which, c, y):
        ref = grads[which]
        if which == 0:
            return ref.at[:, c, y]
        if which in conv_rows:
            return ref.at[:, y, conv_rows[which], lanes_of(c, 128)]
        return ref.at[:, :, lanes_of(c * 2 + y, (256, 128)[which - 3])]

    def final_part(which, c, y):
        if which == 0:
            return fs[0].at[c, y]
        if which in conv_rows:
            return fs[1].at[y, conv_rows[which], lanes_of(c, 128)]
        return fs[which - 1].at[:, lanes_of(c * 2 + y, (256, 128)[which - 3])]

    def reduce_core(which):
        remote(
            half_of(which, 1 - core), r1s[which], gs.at[which, 0], gr.at[which, 0], sibling
        ).start()

    def reduce_y(which):
        wait_bytes(r1s[which], gr.at[which, 0])
        away = quarter_of(which, core, 1 - half_y)
        mine = quarter_of(which, core, half_y)
        there = y_part(which, r1s[which], 1 - half_y)
        here = y_part(which, r1s[which], half_y)

        def add_away(d, carry):
            ys[which][d] = (away[d] + there[d]).astype(ys[which].dtype)
            return carry

        lax.fori_loop(0, n_dp, add_away, 0)
        remote(ys[which], r2s[which], gs.at[which, 1], gr.at[which, 1], across).start()

        def add_mine(d, carry):
            mine[d] = mine[d] + here[d]
            return carry

        lax.fori_loop(0, n_dp, add_mine, 0)

    def reduce_owner(which):
        wait_bytes(r2s[which], gr.at[which, 1])
        mine = quarter_of(which, core, half_y)

        def add(d, carry):
            ks[which][d] = (mine[d] + r2s[which][d].astype(F32)).astype(ks[which].dtype)
            return carry

        lax.fori_loop(0, n_dp, add, 0)
        for device in owner_peers:
            remote(
                ks[which].at[device[0]],
                r3s[which].at[dp],
                gs.at[which, 2],
                gr.at[which, 2],
                device,
            ).start()
        own[which][...] = mine[dp] + r2s[which][dp].astype(F32)
        r3s[which][dp] = jnp.zeros(own[which].shape, r3s[which].dtype)

    def reduce_spread(which):
        wait_bytes(r3s[which].at[pl.ds(0, n_dp - 1)], gr.at[which, 2])
        total = own[which][...]
        for slot in range(n_dp):
            total = total + r3s[which][slot].astype(F32)
        mine = final_part(which, core, half_y)
        mine[...] = total
        send_all(mine, gs.at[which, 3], gr.at[which, 3], rep_peers)

    def three_parts(which):
        return r1s[which].at[pl.ds(0, 3), 0] if which < 3 else y_part(which, r1s[which], 0).at[pl.ds(0, 3)]

    def reduce_end(which):
        wait_bytes(three_parts(which), gr.at[which, 3])

    gather_end(0)
    red[...] = jnp.dot(x_v[...], fw1[...].reshape(CHANNELS, BOTTLE), preferred_element_type=F32)

    def sums_of(ref, start, width):
        def body(row, carry):
            values = grouped(ref[pl.ds(row, CHUNK), start : start + width])
            return carry[0] + jnp.sum(values, axis=0), carry[1] + jnp.sum(values * values, axis=0)

        zero = jnp.zeros((8, width), F32)
        return over_rows(body, (zero, zero))

    def wide_sums(ref, width):
        found = [sums_of(ref, start, 256) for start in range(0, width, 256)]
        first = jnp.concatenate([item[0] for item in found], axis=1)
        second = jnp.concatenate([item[1] for item in found], axis=1)
        return fold_lanes(stack_sums(micro_sum(first), micro_sum(second)))

    sum_start(0, wide_sums(red, BOTTLE))

    gy_copy.wait()
    to_rows(gy4, gy_v)
    wait_bytes(np_slots.at[pl.ds(0, n_dp - 1)], np_sems.at[1])
    np_full[...] = jnp.zeros(np_full.shape, F32)
    for d in range(n_dp):
        at = shard * d // 128
        np_full[at : at + 8, :] = np_full[at : at + 8, :] + np_slots[d]

    def vector(at, width):
        rows = [np_full[at // 128 + k : at // 128 + k + 1, :] for k in range(width // 128)]
        return jnp.concatenate(rows, axis=1) if len(rows) > 1 else rows[0]

    gain_one, bias_one = vector(0, 256), vector(256, 256)
    gain_two, bias_two = vector(512, 512), vector(1024, 512)
    gain_pool, bias_pool = vector(1536, 128), vector(1664, 128)
    bias_expand = vector(1792, 512)
    gain_three, bias_three = vector(2304, 1024), vector(3328, 1024)

    sum_turn(0)
    gather_turn(1)
    gather_out(2)
    total, square = unstack_sums(unfold_lanes(sum_end(0)))
    center1, scale1, mul1, add1 = norm_terms(total, square, gain_one, bias_one, pixels)

    def make_active(row, carry):
        turned = grouped(red[pl.ds(row, CHUNK), :]) * mul1 + add1
        act[1, pl.ds(PAD + row, CHUNK), :] = flat(turned * sigmoid(turned))
        return carry

    over_rows(make_active, 0)
    gather_hand(1)
    place = lax.rem(lax.broadcasted_iota(jnp.int32, (CHUNK, BOTTLE), 0) // 4, SIDE)
    not_last = place != SIDE - 1
    not_first = place != 0

    def beside(side, row, distance):
        near = act[side, pl.ds(PAD + row - 8, CHUNK + 16), :]
        return pltpu.roll(near, (CHUNK + 16 - distance) % (CHUNK + 16), 0)[8 : 8 + CHUNK]

    def shift_active(row, carry):
        act[2, pl.ds(PAD + row, CHUNK), :] = jnp.where(not_last, beside(1, row, 4), 0.0)
        act[0, pl.ds(PAD + row, CHUNK), :] = jnp.where(not_first, beside(1, row, -4), 0.0)
        return carry

    over_rows(shift_active, 0)

    def make_columns(row, carry):
        for tap in range(9):
            down, side = tap // 3 - 1, tap % 3
            values = act[side, pl.ds(PAD + row + 56 * down, CHUNK), :].astype(BF16)
            columns[0, pl.ds(row, CHUNK), tap * 128 : tap * 128 + 128] = values[:, 0:128]
            columns[1, pl.ds(row, CHUNK), tap * 128 : tap * 128 + 128] = values[:, 128:256]
        return carry

    over_rows(make_columns, 0)
    gather_end(1)
    own_half = n_dp // 2

    def filters(group):
        return fwc[group * own_half : (group + 1) * own_half].reshape(9 * 128, BOTTLE)

    for group in range(2):
        wid[:, group * 256 : group * 256 + 256] = jnp.dot(
            columns[group], filters(group), preferred_element_type=F32
        )
    sum_start(1, wide_sums(wid, 512))
    gather_turn(2)
    sum_turn(1)
    gather_hand(2)
    total, square = unstack_sums(unfold_lanes(sum_end(1)))
    center2, scale2, mul2, add2 = norm_terms(total, square, gain_two, bias_two, pixels)

    def make_splits(row, carry):
        found = []
        for group in range(2):
            lanes = slice(group * 256, group * 256 + 256)
            turned = grouped(wid[pl.ds(row, CHUNK), lanes]) * mul2[:, lanes] + add2[:, lanes]
            values = turned * sigmoid(turned)
            splits[pl.ds(row, CHUNK), lanes] = flat(values)
            found.append(jnp.sum(values, axis=0))
        return carry + found[0] + found[1]

    pooled = image_sum(over_rows(make_splits, jnp.zeros((8, BOTTLE), F32))) / (SIDE * SIDE)
    gather_end(2)
    last = fpe[:, :, 0:CHANNELS].reshape(BOTTLE, CHANNELS)
    squeeze = fpe[:, :, 1024:1152].reshape(BOTTLE, INNER)
    ex_both = fpe[:, :, 1152:1408]
    expand = jnp.concatenate(
        [
            ex_both[:, 0:ex_rows].reshape(INNER, 256),
            ex_both[:, ex_rows : 2 * ex_rows].reshape(INNER, 256),
        ],
        axis=1,
    )
    pre_pool = exact_dot(pooled, squeeze, False)
    sum_start(2, stack_sums(pair_sum(pre_pool), pair_sum(pre_pool * pre_pool)))
    sum_turn(2)
    total, square = unstack_sums(sum_end(2))
    center_p, scale_p, mul_p, add_p = norm_terms(total, square, gain_pool, bias_pool, pictures)
    normed_p = (pre_pool - center_p) * scale_p
    norm_p = pre_pool * mul_p + add_p
    gate_p = sigmoid(norm_p)
    hidden = norm_p * gate_p
    slope_p = gate_p * (1.0 + norm_p * (1.0 - gate_p))
    logits = exact_dot(hidden, expand, False) + bias_expand
    left, right = logits[:, 0:256], logits[:, 256:512]
    most = jnp.maximum(left, right)
    left, right = jnp.exp(left - most), jnp.exp(right - most)
    att0 = left / (left + right)
    att1 = right / (left + right)

    def make_mixed(row, carry):
        rows = pl.ds(row, CHUNK)
        values = grouped(splits[rows, 0:256]) * att0 + grouped(splits[rows, 256:512]) * att1
        mixed[rows, :] = flat(values).astype(BF16)
        return carry

    over_rows(make_mixed, 0)
    proj[...] = jnp.dot(mixed[...], last, preferred_element_type=F32)
    sum_start(3, wide_sums(proj, CHANNELS))
    sum_turn(3)
    total, square = unstack_sums(unfold_lanes(sum_end(3)))
    center3, scale3, mul3, add3 = norm_terms(total, square, gain_three, bias_three, pixels)

    found = []
    for start in range(0, CHANNELS, 256):
        lanes = slice(start, start + 256)
        m3, a3, c3, s3 = mul3[:, lanes], add3[:, lanes], center3[:, lanes], scale3[:, lanes]

        def make_out(row, carry):
            rows = pl.ds(row, CHUNK)
            values = grouped(proj[rows, lanes])
            summed = grouped(x_v[rows, lanes].astype(F32)) + (values * m3 + a3)
            gate = sigmoid(summed)
            bo4[pl.ds(row // 4, CHUNK // 4), :, lanes] = by_four(summed * gate).astype(BF16)
            upstream = grouped(gy_v[rows, lanes].astype(F32)) * (
                gate * (1.0 + summed * (1.0 - gate))
            )
            up[rows, lanes] = flat(upstream)
            normed = (values - c3) * s3
            return carry[0] + jnp.sum(upstream, axis=0), carry[1] + jnp.sum(
                upstream * normed, axis=0
            )

        zero = jnp.zeros((8, 256), F32)
        found.append(over_rows(make_out, (zero, zero)))
    bias_sum = micro_sum(jnp.concatenate([item[0] for item in found], axis=1))
    gain_sum = micro_sum(jnp.concatenate([item[1] for item in found], axis=1))
    sum_start(4, fold_lanes(stack_sums(bias_sum, gain_sum)))
    bo_copy = pltpu.make_async_copy(bo4, bo_hbm, local_sem.at[2])
    bo_copy.start()

    def write_norm(at, pattern):
        both = pattern[0:1, :] + pattern[2:3, :]
        for k in range(both.shape[1] // 128):
            np_full[at // 128 + k : at // 128 + k + 1, :] = both[:, k * 128 : k * 128 + 128]

    sum_turn(4)
    bias_sum, gain_sum = unstack_sums(unfold_lanes(sum_end(4)))
    write_norm(2304, gain_sum)
    write_norm(3328, bias_sum)
    by_value, constant = back_terms(center3, scale3, mul3, bias_sum, gain_sum, pixels)
    for start in range(0, CHANNELS, 256):
        lanes = slice(start, start + 256)
        m3, v3, k3 = mul3[:, lanes], by_value[:, lanes], constant[:, lanes]

        def make_dproj(row, carry):
            rows = pl.ds(row, CHUNK)
            values = grouped(up[rows, lanes]) * m3 + grouped(proj[rows, lanes]) * v3 + k3
            dproj[rows, lanes] = flat(values).astype(BF16)
            return carry

        over_rows(make_dproj, 0)

    d_mixed[...] = dot_t(dproj[...], last)

    def attend(row, carry):
        rows = pl.ds(row, CHUNK)
        values = grouped(d_mixed[rows, :])
        return (
            carry[0] + jnp.sum(values * grouped(splits[rows, 0:256]), axis=0),
            carry[1] + jnp.sum(values * grouped(splits[rows, 256:512]), axis=0),
        )

    zero = jnp.zeros((8, 256), F32)
    d_att0, d_att1 = over_rows(attend, (zero, zero))
    d_att0, d_att1 = image_sum(d_att0), image_sum(d_att1)
    both = att0 * d_att0 + att1 * d_att1
    d_logits = jnp.concatenate([att0 * (d_att0 - both), att1 * (d_att1 - both)], axis=1)
    d_hidden = exact_dot(d_logits, expand, True)
    d_pool = d_hidden * slope_p
    per_micro = stack_sums(pair_sum(d_pool), pair_sum(d_pool * normed_p))
    sum_start(5, per_micro)
    ex_sum = pair_sum(d_logits)
    ex_sum = ex_sum + pltpu.roll(ex_sum, 2, 0)
    ex_sum = jnp.where(row_ids(256) % 2 == 0, ex_sum[:, 0:256], ex_sum[:, 256:512])

    grad_ex = image_dot(hidden, d_logits)
    grad_ex = grad_ex.reshape(n_dp, ex_rows, 512)
    ge[:, 0:ex_rows, 128:384] = grad_ex[:, :, 0:256]
    ge[:, ex_rows : 2 * ex_rows, 128:384] = grad_ex[:, :, 256:512]
    ge[:, :, 384:512] = jnp.zeros((n_dp, 2 * ex_rows, 128), F32)
    g3[...] = tdot(mixed[...], dproj[...]).reshape(g3.shape)
    reduce_core(3)
    sum_turn(5)
    pool_bias_sum, pool_gain_sum = unstack_sums(sum_end(5))
    write_norm(1536, pool_gain_sum)
    write_norm(1664, pool_bias_sum)
    d_pre_pool = mul_p * (
        d_pool - pool_bias_sum / pictures - normed_p * (pool_gain_sum / pictures)
    )
    d_pooled = exact_dot(d_pre_pool, squeeze, True) / (SIDE * SIDE)
    found = []
    for group, att in ((0, att0), (1, att1)):
        lanes = slice(group * 256, group * 256 + 256)
        m2, a2, c2, s2 = mul2[:, lanes], add2[:, lanes], center2[:, lanes], scale2[:, lanes]

        def make_dn2(row, carry):
            rows = pl.ds(row, CHUNK)
            values = grouped(wid[rows, lanes])
            turned = values * m2 + a2
            gate = sigmoid(turned)
            slope = gate * (1.0 + turned * (1.0 - gate))
            down = (grouped(d_mixed[rows, :]) * att + d_pooled) * slope
            dn2[rows, lanes] = flat(down)
            normed = (values - c2) * s2
            return carry[0] + jnp.sum(down, axis=0), carry[1] + jnp.sum(down * normed, axis=0)

        found.append(over_rows(make_dn2, (zero, zero)))
    bias_sum = micro_sum(jnp.concatenate([item[0] for item in found], axis=1))
    gain_sum = micro_sum(jnp.concatenate([item[1] for item in found], axis=1))
    sum_start(6, jnp.concatenate([fold_lanes(stack_sums(bias_sum, gain_sum)), ex_sum], axis=0))
    ge[:, :, 0:128] = image_dot(pooled, d_pre_pool).reshape(n_dp, 2 * ex_rows, 128)
    reduce_core(4)
    sum_turn(6)
    reduce_y(3)
    reduce_y(4)
    whole = sum_end(6)
    for k in range(4):
        np_full[14 + k : 15 + k, :] = whole[8 + k // 2 : 9 + k // 2, k % 2 * 128 : k % 2 * 128 + 128]
    bias_sum, gain_sum = unstack_sums(unfold_lanes(whole[0:8]))
    write_norm(512, gain_sum)
    write_norm(1024, bias_sum)
    by_value, constant = back_terms(center2, scale2, mul2, bias_sum, gain_sum, pixels)

    for group in range(2):
        lanes = slice(group * 256, group * 256 + 256)
        m2, v2, k2 = mul2[:, lanes], by_value[:, lanes], constant[:, lanes]

        def make_dwid(row, carry):
            rows = pl.ds(row, CHUNK)
            values = grouped(dn2[rows, lanes]) * m2 + grouped(wid[rows, lanes]) * v2 + k2
            dwid[rows, lanes] = flat(values).astype(BF16)
            return carry

        over_rows(make_dwid, 0)
        dcol[PAD : PAD + ROWS, group * 1152 : group * 1152 + 1152] = dot_t(
            dwid[:, lanes], filters(group)
        )

    def gather_taps(row, carry):
        for side in range(3):
            for group in range(2):
                total = None
                for down in range(3):
                    at = group * 1152 + (3 * down + side) * 128
                    values = dcol[pl.ds(PAD + row - 56 * (down - 1), CHUNK), at : at + 128]
                    total = values if total is None else total + values
                act[side, pl.ds(PAD + row, CHUNK), group * 128 : group * 128 + 128] = total
        return carry

    over_rows(gather_taps, 0)

    def make_dn1(row, carry):
        rows = pl.ds(row, CHUNK)
        d_active = act[1, pl.ds(PAD + row, CHUNK), :]
        d_active = d_active + jnp.where(not_first, beside(2, row, -4), 0.0)
        d_active = d_active + jnp.where(not_last, beside(0, row, 4), 0.0)
        values = grouped(red[rows, :])
        turned = values * mul1 + add1
        gate = sigmoid(turned)
        slope = gate * (1.0 + turned * (1.0 - gate))
        down = grouped(d_active) * slope
        dn1[rows, :] = flat(down)
        normed = (values - center1) * scale1
        return carry[0] + jnp.sum(down, axis=0), carry[1] + jnp.sum(down * normed, axis=0)

    bias_sum, gain_sum = over_rows(make_dn1, (zero, zero))
    sum_start(7, fold_lanes(stack_sums(micro_sum(bias_sum), micro_sum(gain_sum))))
    reduce_owner(3)
    reduce_owner(4)

    def grad_conv(group):
        gc[group * own_half : (group + 1) * own_half] = tdot(
            columns[group], dwid[:, group * 256 : group * 256 + 256]
        ).reshape(own_half, 2, 9 * 128 // own_half // 2, BOTTLE)

    grad_conv(0)
    sum_turn(7)
    grad_conv(1)
    reduce_core(1)
    reduce_core(2)
    bias_sum, gain_sum = unstack_sums(unfold_lanes(sum_end(7)))
    write_norm(0, gain_sum)
    write_norm(256, bias_sum)
    by_value, constant = back_terms(center1, scale1, mul1, bias_sum, gain_sum, pixels)
    norm_rows = np_full[0:8, :]
    for d in range(1, n_dp):
        at = shard * d // 128
        norm_rows = jnp.where(dp == d, np_full[at : at + 8, :], norm_rows)
    norm_rows = pltpu.roll(norm_rows, lax.rem(128 - turn, 128), 1)
    gn_out[...] = jnp.where(lanes_id < 128 - turn, norm_rows, pltpu.roll(norm_rows, 7, 0))

    def make_dred(row, carry):
        rows = pl.ds(row, CHUNK)
        values = grouped(dn1[rows, :]) * mul1 + grouped(red[rows, :]) * by_value + constant
        dred[rows, :] = flat(values).astype(BF16)
        return carry

    over_rows(make_dred, 0)
    g1[...] = tdot(x_v[...], dred[...]).reshape(g1.shape)
    reduce_core(0)
    reduce_y(1)
    reduce_y(2)
    proj[...] = dot_t(dred[...], fw1[...].reshape(CHANNELS, BOTTLE))
    reduce_y(0)
    reduce_spread(3)
    reduce_spread(4)
    reduce_owner(1)

    def make_dx(row, carry):
        for start in range(0, CHANNELS, 256):
            lanes = slice(start, start + 256)
            values = up[pl.ds(row, CHUNK), lanes] + proj[pl.ds(row, CHUNK), lanes]
            dx4[pl.ds(row // 4, CHUNK // 4), :, lanes] = values.reshape(CHUNK // 4, 4, 256)
        return carry

    over_rows(make_dx, 0)
    dx_copy = pltpu.make_async_copy(dx4, dx_hbm, local_sem.at[3])
    dx_copy.start()
    reduce_owner(2)
    reduce_owner(0)
    reduce_spread(1)
    reduce_spread(2)
    reduce_spread(0)
    out_copies = [
        pltpu.make_async_copy(source, target, local_sem.at[10 + k])
        for k, (source, target) in enumerate(
            (
                (gn_out, gn_hbm),
                (fs[2], f3_hbm),
                (fs[3], fe_hbm),
                (fs[1], fc_hbm),
                (fs[0], f1_hbm),
            )
        )
    ]
    out_copies[0].start()
    for which in (3, 4, 1, 2, 0):
        reduce_end(which)
        if which != 1:
            out_copies[{3: 1, 4: 2, 2: 3, 0: 4}[which]].start()

    bo_copy.wait()
    dx_copy.wait()
    for copy in out_copies:
        copy.wait()
    for k in range(n_ar):
        if k in DIRECT:
            wait_bytes(ar_slots_a[k].at[pl.ds(0, everyone - 1)], ar_send_a.at[k])
        else:
            wait_bytes(ar_slots_a[k].at[pl.ds(0, plane_size - 1)], ar_send_a.at[k])
            wait_bytes(ar_slots_b[k].at[pl.ds(0, planes - 1)], ar_send_b.at[k])
    wait_bytes(np_slots.at[pl.ds(0, n_dp - 1)], np_sems.at[0])
    for which in range(3):
        wait_bytes(seven(which), ws.at[which, 0])
        for stage in range(1, 4):
            wait_bytes(quarters[which](core, half_y), ws.at[which, stage])
    for which in range(5):
        wait_bytes(r1s[which], gs.at[which, 0])
        wait_bytes(r2s[which], gs.at[which, 1])
        wait_bytes(r3s[which].at[pl.ds(0, n_dp - 1)], gs.at[which, 2])
        wait_bytes(three_parts(which), gs.at[which, 3])


def update_kernel(*refs):
    sources, targets = refs[0:25], refs[25:45]
    inputs, outs, through = refs[45:68], refs[68:86], refs[86:88]
    pass_sems, in_sems, out_sems = refs[88:91]
    coming = [
        pltpu.make_async_copy(source, held, in_sems.at[k])
        for k, (source, held) in enumerate(zip(sources[2:], inputs))
    ]
    for copy in coming:
        copy.start()
    part = SIDE * SIDE // 4
    fetching, passing = [], []
    for k in range(4):
        rows = pl.ds(k * part, part)
        for which in range(2):
            fetching.append(
                pltpu.make_async_copy(
                    sources[which].at[rows], through[which].at[rows], pass_sems.at[0, which, k]
                )
            )
            passing.append(
                pltpu.make_async_copy(
                    through[which].at[rows], targets[which].at[rows], pass_sems.at[1, which, k]
                )
            )
    for copy in fetching:
        copy.start()
    grads, states = inputs[0:5], inputs[5:23]
    going = [
        pltpu.make_async_copy(held, target, out_sems.at[k])
        for k, (held, target) in enumerate(zip(outs, targets[2:]))
    ]
    ex_rows = states[9].shape[0]
    shard = states[15].shape[0]
    fans = (CHANNELS, 9 * BOTTLE // RADIX, BOTTLE, INNER // 8, BOTTLE)
    for copy in coming[0:5]:
        copy.wait()
    found = (
        grads[0][...],
        grads[1][...],
        grads[3][:, 0:128],
        jnp.concatenate([grads[3][0:ex_rows, 128:384], grads[3][ex_rows:, 128:384]], axis=1),
        grads[2][...],
    )
    for order, k in enumerate((3, 2, 4, 0, 1)):
        for copy in coming[5 + 3 * k : 8 + 3 * k]:
            copy.wait()
        new = adamw(
            states[3 * k][...],
            states[3 * k + 1][...],
            states[3 * k + 2][...],
            found[k],
            2.0 * fans[k] ** (-0.5),
            DECAY,
        )
        for j in range(3):
            outs[3 * k + j][...] = new[j]
            going[3 * k + j].start()
        for copy in range(2 * order, min(2 * order + 2, 8)):
            fetching[copy].wait()
            passing[copy].start()
    for copy in coming[20:23]:
        copy.wait()
    for at in range(0, shard, 128):
        width = min(128, shard - at)
        lanes = pl.ds(at, width)
        new = adamw(
            *[states[15 + j][lanes].reshape(1, width) for j in range(3)],
            grads[4][at // 128 : at // 128 + 1, 0:width],
            NORM_RATE,
            0.0,
        )
        for j in range(3):
            outs[15 + j][lanes] = new[j].reshape(width)
    for copy in going[15:18]:
        copy.start()
    for copy in passing + going:
        copy.wait()


def fused_device(
    images,
    out_grad,
    reduce_weight,
    reduce_moment,
    reduce_second,
    conv_weight,
    conv_moment,
    conv_second,
    squeeze_weight,
    squeeze_moment,
    squeeze_second,
    expand_weight,
    expand_moment,
    expand_second,
    project_weight,
    project_moment,
    project_second,
    norm_params,
    norm_moment,
    norm_second,
):
    n_dp, n_rep = lax.axis_size("dp"), lax.axis_size("rep")
    by_pixel = lambda values: jnp.transpose(values, (1, 2, 0, 3)).reshape(-1, 4, CHANNELS)
    qc = conv_weight.shape[0] // 2
    q1 = reduce_weight.shape[0] // 4
    pe = squeeze_weight.shape[0]
    vmem = pltpu.VMEM
    pixel_form = (SIDE * SIDE, 4, CHANNELS)
    scratch = [
        *[
            vmem(values.shape, F32)
            for values in (
                reduce_weight,
                conv_weight,
                squeeze_weight,
                expand_weight,
                project_weight,
                norm_params,
            )
        ],
        vmem((8, 128), F32),
        vmem(pixel_form, BF16),
        vmem(pixel_form, BF16),
        vmem((ROWS, CHANNELS), BF16),
        vmem((ROWS, CHANNELS), BF16),
        vmem((n_dp, 2, 2, q1, BOTTLE), BF16),
        vmem((n_dp, 2, qc, BOTTLE), BF16),
        vmem((n_dp, pe, 1536), BF16),
        vmem((pe, 1536), BF16),
        vmem((n_dp, 8, 128), F32),
        vmem((40, 128), F32),
        vmem((ROWS, BOTTLE), F32),
        vmem((3, ROWS + 2 * PAD, BOTTLE), F32),
        vmem((2, ROWS, 9 * 128), BF16),
        vmem((ROWS, 512), F32),
        vmem((ROWS, 512), F32),
        vmem((ROWS, BOTTLE), BF16),
        vmem((ROWS, CHANNELS), F32),
        vmem((ROWS, CHANNELS), F32),
        vmem(pixel_form, BF16),
        vmem(pixel_form, F32),
        vmem((ROWS, CHANNELS), BF16),
        vmem((ROWS, BOTTLE), F32),
        vmem((ROWS, 512), F32),
        vmem((ROWS, 512), BF16),
        vmem((ROWS + 2 * PAD, 2 * 9 * 128), F32),
        vmem((ROWS, BOTTLE), F32),
        vmem((ROWS, BOTTLE), BF16),
        vmem((n_dp, 2, 2, q1, BOTTLE), F32),
        vmem((n_dp, 2, qc, BOTTLE), F32),
        vmem((n_dp, pe, CHANNELS), F32),
        vmem((n_dp, pe, 512), F32),
    ]
    direct = n_dp * n_rep
    scratch += [
        vmem((direct if k in DIRECT else 2 * n_rep,) + shape, F32) for k, shape in enumerate(STATS)
    ]
    scratch += [vmem((n_dp // 2,) + shape, F32) for shape in STATS]
    cut = 64
    half = [
        (n_dp, 2, q1, BOTTLE),
        (n_dp, 2, cut, 128),
        (n_dp, 2, qc - cut, 128),
        (n_dp, pe, 512),
        (n_dp, pe, 256),
    ]
    quarter = [
        (n_dp, q1, BOTTLE),
        (n_dp, cut, 128),
        (n_dp, qc - cut, 128),
        (n_dp, pe, 256),
        (n_dp, pe, 128),
    ]
    final = [(2, 2, q1, BOTTLE), (2, qc, BOTTLE), (pe, CHANNELS), (pe, 512)]
    sent = [BF16, BF16, BF16, BF16, F32]
    scratch += [vmem(shape, F32) for shape in half]
    scratch += [vmem(shape, kind) for shape, kind in zip(quarter, sent)] * 4
    scratch += [vmem(shape[1:], F32) for shape in quarter]
    scratch += [vmem(shape, F32) for shape in final]
    dma = pltpu.SemaphoreType.DMA
    scratch += [dma((15,))] + [dma((len(STATS),))] * 4 + [dma((2,))] + [dma((3, 4))] * 2 + [dma((5, 4))] * 2
    any_space = pl.BlockSpec(memory_space=pl.ANY)
    block_out, images_grad, sum1, sumc, sum3, sume, norm_grads = pl.pallas_call(
        functools.partial(block_kernel, n_dp, n_rep),
        out_shape=[
            jax.ShapeDtypeStruct(pixel_form, BF16),
            jax.ShapeDtypeStruct(pixel_form, F32),
            *[jax.ShapeDtypeStruct(shape, F32) for shape in final],
            jax.ShapeDtypeStruct((8, 128), F32),
        ],
        in_specs=[any_space] * 8,
        out_specs=[any_space] * 7,
        scratch_shapes=scratch,
        compiler_params=pltpu.CompilerParams(
            collective_id=0, has_side_effects=True, vmem_limit_bytes=63 * 1024 * 1024
        ),
    )(
        by_pixel(images),
        by_pixel(out_grad),
        reduce_weight,
        conv_weight,
        squeeze_weight,
        expand_weight,
        project_weight,
        norm_params,
    )
    states = (
        reduce_weight,
        reduce_moment,
        reduce_second,
        conv_weight,
        conv_moment,
        conv_second,
        squeeze_weight,
        squeeze_moment,
        squeeze_second,
        expand_weight,
        expand_moment,
        expand_second,
        project_weight,
        project_moment,
        project_second,
    )
    held = (*states, norm_params, norm_moment, norm_second)
    sums = (
        sum1.reshape(reduce_weight.shape),
        sumc.reshape(conv_weight.shape),
        sum3,
        sume,
        norm_grads,
    )
    block_out, images_grad, *updated = pl.pallas_call(
        update_kernel,
        out_shape=[
            jax.ShapeDtypeStruct(pixel_form, BF16),
            jax.ShapeDtypeStruct(pixel_form, F32),
            *[jax.ShapeDtypeStruct(state.shape, F32) for state in held],
        ],
        in_specs=[any_space] * 25,
        out_specs=[any_space] * 20,
        scratch_shapes=[vmem(values.shape, F32) for values in (*sums, *held, *held)]
        + [vmem(pixel_form, BF16), vmem(pixel_form, F32)]
        + [dma((2, 2, 4)), dma((23,)), dma((18,))],
        compiler_params=pltpu.CompilerParams(vmem_limit_bytes=63 * 1024 * 1024),
    )(block_out, images_grad, *sums, *held)
    by_image = lambda values: jnp.transpose(
        values.reshape(SIDE, SIDE, images.shape[0], CHANNELS), (2, 0, 1, 3)
    )
    return (
        by_image(block_out),
        by_image(images_grad),
        *updated,
    )


def solution(mesh):
    placed = (
        P(("dp", "rep"), None, None, None),
        P(("dp", "rep"), None, None, None),
        P("dp", None),
        P("dp", None),
        P("dp", None),
        P("dp", None),
        P("dp", None),
        P("dp", None),
        P("dp", None),
        P("dp", None),
        P("dp", None),
        P("dp", None),
        P("dp", None),
        P("dp", None),
        P("dp", None),
        P("dp", None),
        P("dp", None),
        P("dp"),
        P("dp"),
        P("dp"),
    )
    n_dp, n_rep = mesh.shape["dp"], mesh.shape["rep"]
    whole_tiles = n_rep == 4 and n_dp % 2 == 0 and INNER % (16 * n_dp) == 0
    return jax.shard_map(
        fused_device if whole_tiles else per_device,
        mesh=mesh,
        in_specs=placed,
        out_specs=(
            P(("dp", "rep"), None, None, None),
            P(("dp", "rep"), None, None, None),
            P("dp", None),
            P("dp", None),
            P("dp", None),
            P("dp", None),
            P("dp", None),
            P("dp", None),
            P("dp", None),
            P("dp", None),
            P("dp", None),
            P("dp", None),
            P("dp", None),
            P("dp", None),
            P("dp", None),
            P("dp", None),
            P("dp", None),
            P("dp"),
            P("dp"),
            P("dp"),
        ),
        check_vma=False,
    )
```

```python
import functools
import jax
import jax.numpy as jnp
from jax import lax
from jax.experimental import pallas as pl
from jax.experimental.pallas import tpu as pltpu
from jax.sharding import PartitionSpec as P

CHANNELS = 1024
BOTTLE = 256
INNER = 128
RADIX = 2
SIDE = 14
MICRO = 2
STEP = 10


EPSILON = 1e-05
PRECISE = lax.Precision.HIGHEST
BETA_ONE = 0.9
BETA_TWO = 0.999
ADAM_EPSILON = 1e-08
DECAY = 0.01
NORM_RATE = 0.8
ROWS = 4 * SIDE * SIDE
NORM_WIDTH = 4352


def split_params(packed):
    widths = (
        BOTTLE,
        BOTTLE,
        RADIX * BOTTLE,
        RADIX * BOTTLE,
        INNER,
        INNER,
        RADIX * BOTTLE,
        CHANNELS,
        CHANNELS,
    )
    pieces = []
    offset = 0
    for segment in widths:
        pieces.append(lax.slice_in_dim(packed, offset, offset + segment))
        offset = offset + segment
    return pieces


def silu_slope(values):
    logistic = jax.nn.sigmoid(values)
    return logistic * (1.0 + values * (1.0 - logistic))


def norm_forward(values, gain, bias, count):
    flat = values.reshape(-1, values.shape[-1])
    total, square = lax.psum((jnp.sum(flat, axis=0), jnp.sum(flat * flat, axis=0)), ("dp", "rep"))
    center = total / count
    scale = lax.rsqrt(square / count - center * center + EPSILON)
    normed = (values - center) * scale
    return (normed * gain + bias, normed, scale)


def norm_backward(upstream, normed, scale, gain, count):
    flat_up = upstream.reshape(-1, upstream.shape[-1])
    flat_norm = normed.reshape(-1, normed.shape[-1])
    bias_sum, gain_sum = lax.psum(
        (jnp.sum(flat_up, axis=0), jnp.sum(flat_up * flat_norm, axis=0)), ("dp", "rep")
    )
    downstream = gain * scale * (upstream - bias_sum / count - normed * (gain_sum / count))
    return (downstream, gain_sum, bias_sum)


def patches(active):
    padded = jnp.pad(active, ((0, 0), (1, 1), (1, 1), (0, 0), (0, 0)))
    shifted = [
        padded[:, down_step : down_step + SIDE, side_step : side_step + SIDE]
        for down_step in range(3)
        for side_step in range(3)
    ]
    return jnp.stack(shifted, axis=4)


def unpatch(columns):
    total = jnp.zeros(
        (columns.shape[0], SIDE + 2, SIDE + 2, columns.shape[3], columns.shape[5]), jnp.float32
    )
    for down_step in range(3):
        for side_step in range(3):
            piece = columns[:, :, :, :, 3 * down_step + side_step]
            total = total + jnp.pad(
                piece,
                ((0, 0), (down_step, 2 - down_step), (side_step, 2 - side_step), (0, 0), (0, 0)),
            )
    return total[:, 1 : SIDE + 1, 1 : SIDE + 1]


def adamw(param, moment, second, gradient, rate, decay):
    moment_new = BETA_ONE * moment + (1.0 - BETA_ONE) * gradient
    second_new = BETA_TWO * second + (1.0 - BETA_TWO) * gradient * gradient
    ratio = (
        moment_new
        / (1.0 - BETA_ONE**STEP)
        / (jnp.sqrt(second_new / (1.0 - BETA_TWO**STEP)) + ADAM_EPSILON)
    )
    return (param - rate * (ratio + decay * param), moment_new, second_new)


def per_device(
    images,
    out_grad,
    reduce_weight,
    reduce_moment,
    reduce_second,
    conv_weight,
    conv_moment,
    conv_second,
    squeeze_weight,
    squeeze_moment,
    squeeze_second,
    expand_weight,
    expand_moment,
    expand_second,
    project_weight,
    project_moment,
    project_second,
    norm_params,
    norm_moment,
    norm_second,
):
    bf16 = jnp.bfloat16
    low_reduce = reduce_weight.astype(bf16)
    low_conv = conv_weight.astype(bf16)
    low_squeeze = squeeze_weight.astype(bf16)
    low_expand = expand_weight.astype(bf16)
    low_project = project_weight.astype(bf16)
    low_norm = norm_params.astype(bf16)
    devices = lax.axis_size("dp") * lax.axis_size("rep")
    per_batch = images.shape[0] // MICRO
    pixel_count = float(per_batch * SIDE * SIDE * devices)
    image_count = float(per_batch * devices)
    group_in = BOTTLE // RADIX
    grad_first = jnp.zeros((CHANNELS, BOTTLE), jnp.float32)
    grad_conv = jnp.zeros((RADIX, 9 * group_in, BOTTLE), jnp.float32)
    grad_squeeze = jnp.zeros((BOTTLE, INNER), jnp.float32)
    grad_expand = jnp.zeros((INNER, RADIX * BOTTLE), jnp.float32)
    grad_last = jnp.zeros((BOTTLE, CHANNELS), jnp.float32)
    grad_norms = jnp.zeros(
        (2 * BOTTLE + 3 * RADIX * BOTTLE + 2 * INNER + 2 * CHANNELS,), jnp.float32
    )
    outputs = []
    input_grads = []
    for number in range(MICRO):
        forward_set = (
            lax.all_gather(low_reduce, "dp", axis=0, tiled=True),
            lax.all_gather(low_conv, "dp", axis=0, tiled=True),
            lax.all_gather(low_squeeze, "dp", axis=0, tiled=True),
            lax.all_gather(low_expand, "dp", axis=0, tiled=True),
            lax.all_gather(low_project, "dp", axis=0, tiled=True),
            lax.all_gather(low_norm, "dp", axis=0, tiled=True),
        )
        first, conv, squeeze, expand, last, packed = forward_set
        (
            gain_one,
            bias_one,
            gain_two,
            bias_two,
            gain_pool,
            bias_pool,
            bias_expand,
            gain_three,
            bias_three,
        ) = split_params(packed.astype(jnp.float32))
        batched = images[number * per_batch : (number + 1) * per_batch]
        cotangent = out_grad[number * per_batch : (number + 1) * per_batch]
        reduced = jnp.einsum("nhwc,cb->nhwb", batched, first, preferred_element_type=jnp.float32)
        norm_one, normed_one, scale_one = norm_forward(reduced, gain_one, bias_one, pixel_count)
        active = jax.nn.silu(norm_one).astype(bf16)
        columns = patches(active.reshape(per_batch, SIDE, SIDE, RADIX, group_in)).reshape(
            per_batch * SIDE * SIDE, RADIX, 9 * group_in
        )
        conv_grouped = conv.reshape(RADIX, 9 * group_in, BOTTLE)
        widened = jnp.einsum(
            "prk,rko->pro", columns, conv_grouped, preferred_element_type=jnp.float32
        )
        widened = widened.reshape(per_batch, SIDE, SIDE, RADIX * BOTTLE)
        norm_two, normed_two, scale_two = norm_forward(widened, gain_two, bias_two, pixel_count)
        splits = jax.nn.silu(norm_two).reshape(per_batch, SIDE, SIDE, RADIX, BOTTLE)
        pooled = jnp.sum(jnp.sum(splits, axis=3), axis=(1, 2)) / (SIDE * SIDE)
        squeeze_float = squeeze.astype(jnp.float32)
        expand_float = expand.astype(jnp.float32)
        pre_pool = jnp.dot(pooled, squeeze_float, precision=PRECISE)
        norm_pool, normed_pool, scale_pool = norm_forward(
            pre_pool, gain_pool, bias_pool, image_count
        )
        hidden = jax.nn.silu(norm_pool)
        logits = (jnp.dot(hidden, expand_float, precision=PRECISE) + bias_expand).reshape(
            per_batch, RADIX, BOTTLE
        )
        attention = jax.nn.softmax(logits, axis=1)
        mixed = jnp.sum(splits * attention[:, None, None], axis=3).astype(bf16)
        projected = jnp.einsum("nhwb,bc->nhwc", mixed, last, preferred_element_type=jnp.float32)
        norm_three, normed_three, scale_three = norm_forward(
            projected, gain_three, bias_three, pixel_count
        )
        summed = batched.astype(jnp.float32) + norm_three
        outputs.append(jax.nn.silu(summed).astype(bf16))
        backward_set = (
            lax.all_gather(low_reduce, "dp", axis=0, tiled=True),
            lax.all_gather(low_conv, "dp", axis=0, tiled=True),
            lax.all_gather(low_squeeze, "dp", axis=0, tiled=True),
            lax.all_gather(low_expand, "dp", axis=0, tiled=True),
            lax.all_gather(low_project, "dp", axis=0, tiled=True),
            lax.all_gather(low_norm, "dp", axis=0, tiled=True),
        )
        first, conv, squeeze, expand, last, packed = backward_set
        gains_back = split_params(packed.astype(jnp.float32))
        conv_grouped = conv.reshape(RADIX, 9 * group_in, BOTTLE)
        expand_float = expand.astype(jnp.float32)
        squeeze_float = squeeze.astype(jnp.float32)
        upstream = cotangent.astype(jnp.float32) * silu_slope(summed)
        d_projected, gain_three_grad, bias_three_grad = norm_backward(
            upstream, normed_three, scale_three, gains_back[7], pixel_count
        )
        d_projected_low = d_projected.astype(bf16)
        grad_last = grad_last + jnp.einsum(
            "nhwb,nhwc->bc", mixed, d_projected_low, preferred_element_type=jnp.float32
        )
        d_mixed = jnp.einsum(
            "nhwc,bc->nhwb", d_projected_low, last, preferred_element_type=jnp.float32
        )
        d_splits = d_mixed[:, :, :, None] * attention[:, None, None]
        d_attention = jnp.sum(d_mixed[:, :, :, None] * splits, axis=(1, 2))
        d_logits = attention * (
            d_attention - jnp.sum(attention * d_attention, axis=1, keepdims=True)
        )
        flat_logits = d_logits.reshape(per_batch, RADIX * BOTTLE)
        grad_expand = grad_expand + jnp.dot(hidden.T, flat_logits, precision=PRECISE)
        d_hidden = jnp.dot(flat_logits, expand_float.T, precision=PRECISE)
        d_pool_norm = d_hidden * silu_slope(norm_pool)
        pool_bias_sum, pool_gain_sum, expand_bias_sum = lax.psum(
            (
                jnp.sum(d_pool_norm, axis=0),
                jnp.sum(d_pool_norm * normed_pool, axis=0),
                jnp.sum(flat_logits, axis=0),
            ),
            ("dp", "rep"),
        )
        d_pre_pool = (
            gains_back[4]
            * scale_pool
            * (
                d_pool_norm
                - pool_bias_sum / image_count
                - normed_pool * (pool_gain_sum / image_count)
            )
        )
        grad_squeeze = grad_squeeze + jnp.dot(pooled.T, d_pre_pool, precision=PRECISE)
        d_pooled = jnp.dot(d_pre_pool, squeeze_float.T, precision=PRECISE)
        d_splits = d_splits + (d_pooled / (SIDE * SIDE))[:, None, None, None, :]
        d_norm_two = d_splits.reshape(per_batch, SIDE, SIDE, RADIX * BOTTLE) * silu_slope(norm_two)
        d_widened, gain_two_grad, bias_two_grad = norm_backward(
            d_norm_two, normed_two, scale_two, gains_back[2], pixel_count
        )
        d_widened_low = d_widened.astype(bf16).reshape(per_batch * SIDE * SIDE, RADIX, BOTTLE)
        grad_conv = grad_conv + jnp.einsum(
            "prk,pro->rko", columns, d_widened_low, preferred_element_type=jnp.float32
        )
        d_columns = jnp.einsum(
            "pro,rko->prk", d_widened_low, conv_grouped, preferred_element_type=jnp.float32
        )
        d_active = unpatch(d_columns.reshape(per_batch, SIDE, SIDE, RADIX, 9, group_in)).reshape(
            per_batch, SIDE, SIDE, BOTTLE
        )
        d_norm_one = d_active * silu_slope(norm_one)
        d_reduced, gain_one_grad, bias_one_grad = norm_backward(
            d_norm_one, normed_one, scale_one, gains_back[0], pixel_count
        )
        d_reduced_low = d_reduced.astype(bf16)
        grad_first = grad_first + jnp.einsum(
            "nhwc,nhwb->cb", batched, d_reduced_low, preferred_element_type=jnp.float32
        )
        input_grads.append(
            upstream
            + jnp.einsum("nhwb,cb->nhwc", d_reduced_low, first, preferred_element_type=jnp.float32)
        )
        grad_norms = grad_norms + jnp.concatenate(
            [
                gain_one_grad,
                bias_one_grad,
                gain_two_grad,
                bias_two_grad,
                pool_gain_sum,
                pool_bias_sum,
                expand_bias_sum,
                gain_three_grad,
                bias_three_grad,
            ]
        )
    grad_conv = grad_conv.reshape(9 * BOTTLE, BOTTLE)
    partial_value = (
        lax.psum_scatter(grad_first, "dp", scatter_dimension=0, tiled=True),
        lax.psum_scatter(grad_conv, "dp", scatter_dimension=0, tiled=True),
        lax.psum_scatter(grad_squeeze, "dp", scatter_dimension=0, tiled=True),
        lax.psum_scatter(grad_expand, "dp", scatter_dimension=0, tiled=True),
        lax.psum_scatter(grad_last, "dp", scatter_dimension=0, tiled=True),
    )
    owned = lax.psum(
        (partial_value[0], partial_value[1], partial_value[2], partial_value[3], partial_value[4]),
        "rep",
    )
    shard_length = norm_params.shape[0]
    norm_grad_owned = lax.dynamic_slice_in_dim(
        grad_norms, lax.axis_index("dp") * shard_length, shard_length
    )
    reduce_new = adamw(
        reduce_weight, reduce_moment, reduce_second, owned[0], 2.0 * CHANNELS ** (-0.5), DECAY
    )
    conv_new = adamw(
        conv_weight,
        conv_moment,
        conv_second,
        owned[1],
        2.0 * (9 * BOTTLE // RADIX) ** (-0.5),
        DECAY,
    )
    squeeze_new = adamw(
        squeeze_weight, squeeze_moment, squeeze_second, owned[2], 2.0 * BOTTLE ** (-0.5), DECAY
    )
    expand_new = adamw(
        expand_weight, expand_moment, expand_second, owned[3], 2.0 * (INNER // 8) ** (-0.5), DECAY
    )
    project_new = adamw(
        project_weight, project_moment, project_second, owned[4], 2.0 * BOTTLE ** (-0.5), DECAY
    )
    norm_new = adamw(norm_params, norm_moment, norm_second, norm_grad_owned, NORM_RATE, 0.0)
    return (
        jnp.concatenate(outputs, axis=0),
        jnp.concatenate(input_grads, axis=0),
        reduce_new[0],
        reduce_new[1],
        reduce_new[2],
        conv_new[0],
        conv_new[1],
        conv_new[2],
        squeeze_new[0],
        squeeze_new[1],
        squeeze_new[2],
        expand_new[0],
        expand_new[1],
        expand_new[2],
        project_new[0],
        project_new[1],
        project_new[2],
        norm_new[0],
        norm_new[1],
        norm_new[2],
    )


MESH = pl.DeviceIdType.MESH
PAD = 64
CHUNK = 112
F32 = jnp.float32
BF16 = jnp.bfloat16
STATS = {
    "reduced": (8, 128),
    "widened0": (8, 128),
    "widened1": (8, 128),
    "pool": (8, 128),
    "projected0": (8, 256),
    "projected1": (8, 256),
    "back_projected0": (8, 256),
    "back_projected1": (8, 256),
    "back_pool": (8, 128),
    "back_widened0": (8, 128),
    "back_widened1": (16, 128),
    "back_reduced0": (8, 128),
    "back_reduced1": (8, 128),
}
DIRECT = ("reduced", "pool", "back_pool")


def sigmoid(values):
    return 0.5 * jnp.tanh(0.5 * values) + 0.5


def row_ids(width):
    return lax.broadcasted_iota(jnp.int32, (8, width), 0)


def image_sum(rows):
    return rows + pltpu.roll(rows, 4, 0)


def pair_sum(rows):
    even = row_ids(rows.shape[1]) % 2 == 0
    return rows + jnp.where(even, pltpu.roll(rows, 7, 0), pltpu.roll(rows, 1, 0))


def micro_sum(rows):
    return pair_sum(image_sum(rows))


def stack_sums(first, second):
    return jnp.where(row_ids(first.shape[1]) < 4, first, second)


def unstack_sums(stacked):
    upper = row_ids(stacked.shape[1]) < 4
    turned = pltpu.roll(stacked, 4, 0)
    return jnp.where(upper, stacked, turned), jnp.where(upper, turned, stacked)


def fold_lanes(stacked):
    half = stacked.shape[1] // 2
    even = row_ids(half) % 2 == 0
    return jnp.where(even, stacked[:, :half], stacked[:, half:])


def unfold_lanes(folded):
    even = row_ids(folded.shape[1]) % 2 == 0
    left = jnp.where(even, folded, pltpu.roll(folded, 1, 0))
    right = jnp.where(even, pltpu.roll(folded, 7, 0), folded)
    return jnp.concatenate([left, right], axis=1)


def norm_terms(total, square, gain, bias, count):
    center = total * (1.0 / count)
    scale = lax.rsqrt(square * (1.0 / count) - center * center + EPSILON)
    slope = scale * gain
    return center, scale, slope, bias - center * slope


def back_terms(center, scale, slope, bias_sum, gain_sum, count):
    by_value = -slope * scale * (gain_sum * (1.0 / count))
    constant = -slope * (bias_sum * (1.0 / count)) - by_value * center
    return by_value, constant


def tdot(left, right):
    return lax.dot_general(left, right, (((0,), (0,)), ((), ())), preferred_element_type=F32)


def dot_t(left, right):
    return lax.dot_general(left, right, (((1,), (1,)), ((), ())), preferred_element_type=F32)


def in_parts(values, parts):
    found = []
    for _ in range(parts):
        rounded = values.astype(BF16).astype(F32)
        found.append(rounded)
        values = values - rounded
    return found


def exact_dot(left, right, transposed):
    stacked = jnp.concatenate(in_parts(left, 3), axis=0).astype(BF16)
    wide = dot_t(stacked, right) if transposed else jnp.dot(stacked, right, preferred_element_type=F32)
    return wide[0:8] + wide[8:16] + wide[16:24]


def image_dot(left, right):
    once = row_ids(left.shape[1]) < 4
    high, low = in_parts(jnp.where(once, left, 0.0), 2)
    other_high, other_low = in_parts(right, 2)
    return tdot(
        jnp.concatenate([high, high, low, low], axis=0).astype(BF16),
        jnp.concatenate([other_high, other_low, other_high, other_low], axis=0).astype(BF16),
    )


def block_kernel(
    n_dp,
    n_rep,
    x_hbm,
    gy_hbm,
    w1_hbm,
    wc_hbm,
    sq_hbm,
    ex_hbm,
    w3_hbm,
    np_hbm,
    bo_hbm,
    dx_hbm,
    f1_hbm,
    fc_hbm,
    f3_hbm,
    fe_hbm,
    gn_hbm,
    w1_own,
    wc_own,
    sq_own,
    ex_own,
    w3_own,
    np_own,
    gn_out,
    x4,
    gy4,
    x_v,
    gy_v,
    fw1,
    fwc,
    fpe,
    pe_own,
    np_slots,
    np_full,
    red,
    act,
    columns,
    wid,
    splits,
    mixed,
    proj,
    up,
    bo4,
    dx4,
    dproj,
    d_mixed,
    dn2,
    dwid,
    dcol,
    dn1,
    dred,
    g1,
    gc,
    g3,
    ge,
    *rest,
):
    n_ar = len(STATS)
    order = {name: k for k, name in enumerate(STATS)}
    ar_slots_a = dict(zip(STATS, rest[0:n_ar]))
    ar_slots_b = dict(zip(STATS, rest[n_ar : 2 * n_ar]))
    rest = rest[2 * n_ar :]
    r1s, ys, r2s, ks, r3s, own = (rest[5 * i : 5 * i + 5] for i in range(6))
    fs = rest[30:34]
    rest = rest[34:]
    local_sem, ar_send_a, ar_recv_a, ar_send_b, ar_recv_b, np_sems, ws, wr, gs, gr = rest

    dp = lax.axis_index("dp")
    rep = lax.axis_index("rep")
    core = lax.rem(rep, 2)
    half_y = lax.div(rep, 2)
    planes = n_dp // 2
    plane_size = 2 * n_rep
    plane = lax.div(dp, 2)
    in_plane = lax.rem(dp, 2) * n_rep + rep
    sibling = (dp, half_y * 2 + (1 - core))
    across = (dp, (1 - half_y) * 2 + core)
    pixels = float(SIDE * SIDE * 2 * n_dp * n_rep)
    pictures = float(2 * n_dp * n_rep)

    in_planes = [lax.rem(in_plane + step, plane_size) for step in range(1, plane_size)]
    plane_peers = [
        (plane * 2 + lax.div(other, n_rep), lax.rem(other, n_rep)) for other in in_planes
    ]
    column_peers = [
        (lax.rem(plane + step, planes) * 2 + lax.rem(dp, 2), rep) for step in range(1, planes)
    ]
    owner_peers = [(lax.rem(dp + step, n_dp), rep) for step in range(1, n_dp)]
    me, everyone = dp * n_rep + rep, n_dp * n_rep
    others = [lax.rem(me + step, everyone) for step in range(1, everyone)]
    all_peers = [(lax.div(other, n_rep), lax.rem(other, n_rep)) for other in others]
    rep_peers = [(dp, lax.rem(rep + step, n_rep)) for step in range(1, n_rep)]

    def remote(src, dst, send_sem, recv_sem, device):
        return pltpu.make_async_remote_copy(
            src_ref=src,
            dst_ref=dst,
            send_sem=send_sem,
            recv_sem=recv_sem,
            device_id=device,
            device_id_type=MESH,
        )

    def send_all(ref, send_sem, recv_sem, peers):
        for device in peers:
            remote(ref, ref, send_sem, recv_sem, device).start()

    def wait_bytes(ref, sem):
        pltpu.make_async_copy(ref, ref, sem).wait()

    def over_rows(body, init):
        def step(index, carry):
            return body(pl.multiple_of(index * CHUNK, CHUNK), carry)

        return lax.fori_loop(0, ROWS // CHUNK, step, init)

    def grouped(values):
        return values.reshape(CHUNK // 8, 8, values.shape[-1])

    def by_four(values):
        return flat(values).reshape(CHUNK // 4, 4, values.shape[-1])

    def flat(values):
        return values.reshape(CHUNK, values.shape[-1])

    own_copies = [
        pltpu.make_async_copy(source, target, local_sem.at[4 + k])
        for k, (source, target) in enumerate(
            (
                (w1_hbm, w1_own),
                (np_hbm, np_own),
                (wc_hbm, wc_own),
                (w3_hbm, w3_own),
                (sq_hbm, sq_own),
                (ex_hbm, ex_own),
            )
        )
    ]
    for copy in own_copies:
        copy.start()
    x_copy = pltpu.make_async_copy(x_hbm, x4, local_sem.at[0])
    gy_copy = pltpu.make_async_copy(gy_hbm, gy4, local_sem.at[1])
    x_copy.start()
    barrier = pltpu.get_barrier_semaphore()
    for device in all_peers:
        pl.semaphore_signal(barrier, inc=1, device_id=device, device_id_type=MESH)

    part = core * 2 + half_y
    own_copies[0].wait()
    q1 = w1_own.shape[0] // 4
    fw1[dp, core, half_y] = w1_own[pl.ds(pl.multiple_of(part * q1, q1), q1), :].astype(BF16)
    core_lanes = pl.ds(pl.multiple_of(core * 128, 128), 128)
    pe_lanes = pl.ds(pl.multiple_of(part * 384, 128), 384)

    pl.semaphore_wait(barrier, everyone - 1)

    def quarter_w1(c, y):
        return fw1.at[:, c, y]

    def quarter_wc(c, y):
        return fwc.at[:, y, :, pl.ds(pl.multiple_of(c * 128, 128), 128)]

    def quarter_pe(c, y):
        return fpe.at[:, :, pl.ds(pl.multiple_of((c * 2 + y) * 384, 128), 384)]

    quarters = (quarter_w1, quarter_wc, quarter_pe)

    def piece(which, d):
        return (
            fw1.at[d, core, half_y],
            fwc.at[d, half_y, :, core_lanes],
            fpe.at[d, :, pe_lanes],
        )[which]

    def seven(which):
        return (
            fw1.at[pl.ds(0, n_dp - 1), core, half_y],
            fwc.at[pl.ds(0, n_dp - 1), half_y, :, core_lanes],
            fpe.at[pl.ds(0, n_dp - 1), :, pe_lanes],
        )[which]

    def gather_out(which):
        send_all(piece(which, dp), ws.at[which, 0], wr.at[which, 0], owner_peers)

    def gather_turn(which):
        wait_bytes(seven(which), wr.at[which, 0])
        mine = quarters[which](core, half_y)
        remote(mine, mine, ws.at[which, 1], wr.at[which, 1], across).start()
        remote(mine, mine, ws.at[which, 2], wr.at[which, 2], sibling).start()

    def gather_hand(which):
        theirs = quarters[which](core, 1 - half_y)
        wait_bytes(theirs, wr.at[which, 1])
        remote(theirs, theirs, ws.at[which, 3], wr.at[which, 3], sibling).start()

    def gather_end(which):
        wait_bytes(quarters[which](1 - core, half_y), wr.at[which, 2])
        wait_bytes(quarters[which](1 - core, 1 - half_y), wr.at[which, 3])

    def to_rows(source, target):
        def body(index, carry):
            values = source[pl.ds(index * (CHUNK // 4), CHUNK // 4)].astype(F32)
            row = pl.multiple_of(index * CHUNK, CHUNK)
            target[pl.ds(row, CHUNK), :] = values.reshape(CHUNK, CHANNELS).astype(BF16)
            return carry

        lax.fori_loop(0, ROWS // CHUNK, body, 0)

    gather_out(0)

    own_copies[1].wait()
    shard = np_own.shape[0]
    lanes_id = lax.broadcasted_iota(jnp.int32, (8, 128), 1)
    turn = lax.rem(shard * dp, 128)
    np_rows = []
    for at in range(0, shard, 128):
        width = min(128, shard - at)
        piece_row = np_own[pl.ds(at, width)].reshape(1, width)
        if width < 128:
            piece_row = jnp.concatenate([piece_row, jnp.zeros((1, 128 - width), F32)], axis=1)
        np_rows.append(piece_row)
    np_rows.append(jnp.zeros((8 - len(np_rows), 128), F32))
    np_turned = jnp.concatenate(np_rows, axis=0).astype(BF16).astype(F32)
    np_turned = pltpu.roll(np_turned, turn, 1)
    np_slots[dp] = jnp.where(lanes_id < turn, pltpu.roll(np_turned, 1, 0), np_turned)
    send_all(np_slots.at[dp], np_sems.at[0], np_sems.at[1], owner_peers)
    own_copies[2].wait()
    qc = wc_own.shape[0] // 2
    fwc[dp, half_y, :, core_lanes] = wc_own[
        pl.ds(pl.multiple_of(half_y * qc, qc), qc), core_lanes
    ].astype(BF16)
    for copy in own_copies[3:]:
        copy.wait()
    ex_rows = ex_own.shape[0]
    pe_own[:, 0:CHANNELS] = w3_own[...].astype(BF16)
    pe_own[:, 1024:1152] = sq_own[...].astype(BF16)
    pe_own[0:ex_rows, 1152:1408] = ex_own[:, 0:256].astype(BF16)
    pe_own[ex_rows : 2 * ex_rows, 1152:1408] = ex_own[:, 256:512].astype(BF16)
    pe_own[:, 1408:1536] = jnp.zeros((2 * ex_rows, 128), BF16)
    fpe[dp, :, pe_lanes] = pe_own[:, pe_lanes]
    gy_copy.start()
    x_copy.wait()
    to_rows(x4, x_v)
    gather_turn(0)
    gather_out(1)
    zero_rows = jnp.zeros((PAD, BOTTLE), F32)
    for side in range(3):
        act[side, 0:PAD, :] = zero_rows
        act[side, PAD + ROWS : 2 * PAD + ROWS, :] = zero_rows
    for lane_block in range(9):
        dcol[0:PAD, lane_block * 256 : lane_block * 256 + 256] = zero_rows
        dcol[PAD + ROWS : 2 * PAD + ROWS, lane_block * 256 : lane_block * 256 + 256] = zero_rows
    gather_hand(0)

    def sum_start(k, payload):
        if k in DIRECT:
            ar_slots_a[k][me] = payload
            send_all(ar_slots_a[k].at[me], ar_send_a.at[order[k]], ar_recv_a.at[order[k]], all_peers)
        else:
            ar_slots_a[k][in_plane] = payload
            send_all(ar_slots_a[k].at[in_plane], ar_send_a.at[order[k]], ar_recv_a.at[order[k]], plane_peers)

    def sum_slots(slots, count):
        sums = [slots[slot] for slot in range(count)]
        while len(sums) > 1:
            sums = [sums[i] + sums[i + 1] for i in range(0, len(sums), 2)]
        return sums[0]

    def sum_turn(k):
        if k in DIRECT:
            return
        wait_bytes(ar_slots_a[k].at[pl.ds(0, plane_size - 1)], ar_recv_a.at[order[k]])
        ar_slots_b[k][plane] = sum_slots(ar_slots_a[k], plane_size)
        send_all(ar_slots_b[k].at[plane], ar_send_b.at[order[k]], ar_recv_b.at[order[k]], column_peers)

    def sum_end(k):
        if k in DIRECT:
            wait_bytes(ar_slots_a[k].at[pl.ds(0, everyone - 1)], ar_recv_a.at[order[k]])
            return sum_slots(ar_slots_a[k], everyone)
        wait_bytes(ar_slots_b[k].at[pl.ds(0, planes - 1)], ar_recv_b.at[order[k]])
        return sum_slots(ar_slots_b[k], planes)

    def lanes_of(index, width):
        return pl.ds(pl.multiple_of(index * width, 128), width)

    cut = 64
    conv_rows = {1: pl.ds(0, cut), 2: pl.ds(cut, gc.shape[2] - cut)}
    grads = (g1, gc, gc, g3, ge)

    def half_of(which, c):
        ref = grads[which]
        if which == 0:
            return ref.at[c]
        if which in conv_rows:
            return ref.at[:, :, conv_rows[which], lanes_of(c, 128)]
        return ref.at[:, :, lanes_of(c, (512, 256)[which - 3])]

    def y_part(which, ref, y):
        if which == 0:
            return ref.at[y]
        if which < 3:
            return ref.at[:, y]
        return ref.at[:, :, lanes_of(y, (256, 128)[which - 3])]

    def quarter_of(which, c, y):
        ref = grads[which]
        if which == 0:
            return ref.at[c, y]
        if which in conv_rows:
            return ref.at[:, y, conv_rows[which], lanes_of(c, 128)]
        return ref.at[:, :, lanes_of(c * 2 + y, (256, 128)[which - 3])]

    def final_part(which, c, y):
        if which == 0:
            return fs[0].at[c, y]
        if which in conv_rows:
            return fs[1].at[y, conv_rows[which], lanes_of(c, 128)]
        return fs[which - 1].at[:, lanes_of(c * 2 + y, (256, 128)[which - 3])]

    def of_owner(which, ref, d):
        return ref.at[:, lanes_of(d, CHANNELS // n_dp)] if which == 0 else ref.at[d]

    def in_blocks(which, body):
        if which == 0:
            count = 4
            rows = g1.shape[2] // count
            block = lambda index: pl.ds(pl.multiple_of(index * rows, rows), rows)
        else:
            count, block = n_dp, lambda index: index

        def step(index, carry):
            body(block(index))
            return carry

        lax.fori_loop(0, count, step, 0)

    def reduce_core(which):
        remote(
            half_of(which, 1 - core), r1s[which], gs.at[which, 0], gr.at[which, 0], sibling
        ).start()

    def reduce_y(which):
        wait_bytes(r1s[which], gr.at[which, 0])
        away = quarter_of(which, core, 1 - half_y)
        mine = quarter_of(which, core, half_y)
        there = y_part(which, r1s[which], 1 - half_y)
        here = y_part(which, r1s[which], half_y)

        def add_away(at):
            ys[which][at] = (away[at] + there[at]).astype(ys[which].dtype)

        in_blocks(which, add_away)
        remote(ys[which], r2s[which], gs.at[which, 1], gr.at[which, 1], across).start()

        def add_mine(at):
            mine[at] = mine[at] + here[at]

        in_blocks(which, add_mine)

    def reduce_owner(which):
        wait_bytes(r2s[which], gr.at[which, 1])
        mine = quarter_of(which, core, half_y)

        def add(at):
            ks[which][at] = (mine[at] + r2s[which][at].astype(F32)).astype(ks[which].dtype)

        in_blocks(which, add)
        for device in owner_peers:
            remote(
                of_owner(which, ks[which], device[0]),
                r3s[which].at[dp],
                gs.at[which, 2],
                gr.at[which, 2],
                device,
            ).start()
        own[which][...] = of_owner(which, mine, dp)[...] + of_owner(which, r2s[which], dp)[...].astype(F32)
        r3s[which][dp] = jnp.zeros(own[which].shape, r3s[which].dtype)

    def reduce_spread(which):
        wait_bytes(r3s[which].at[pl.ds(0, n_dp - 1)], gr.at[which, 2])
        total = own[which][...]
        for slot in range(n_dp):
            total = total + r3s[which][slot].astype(F32)
        mine = final_part(which, core, half_y)
        mine[...] = total
        send_all(mine, gs.at[which, 3], gr.at[which, 3], rep_peers)

    def three_parts(which):
        if which == 0:
            return r1s[0].at[0, :, pl.ds(0, 3 * CHANNELS // n_dp)]
        return r1s[which].at[pl.ds(0, 3), 0] if which < 3 else y_part(which, r1s[which], 0).at[pl.ds(0, 3)]

    def reduce_end(which):
        wait_bytes(three_parts(which), gr.at[which, 3])

    gather_end(0)
    red[...] = jnp.dot(x_v[...], fw1[...].reshape(CHANNELS, BOTTLE), preferred_element_type=F32)

    def sums_of(ref, start, width):
        def body(row, carry):
            values = grouped(ref[pl.ds(row, CHUNK), start : start + width])
            return carry[0] + jnp.sum(values, axis=0), carry[1] + jnp.sum(values * values, axis=0)

        zero = jnp.zeros((8, width), F32)
        return over_rows(body, (zero, zero))

    def joined(found):
        both = [jnp.concatenate(item, axis=1) for item in zip(*found)]
        return fold_lanes(stack_sums(micro_sum(both[0]), micro_sum(both[1])))

    def both_sums(name):
        return unstack_sums(unfold_lanes(sum_end(name)))

    sum_start("reduced", joined([sums_of(red, 0, 256)]))

    gy_copy.wait()
    to_rows(gy4, gy_v)
    wait_bytes(np_slots.at[pl.ds(0, n_dp - 1)], np_sems.at[1])
    np_full[...] = jnp.zeros(np_full.shape, F32)
    for d in range(n_dp):
        at = shard * d // 128
        np_full[at : at + 8, :] = np_full[at : at + 8, :] + np_slots[d]

    def vector(at, width):
        rows = [np_full[at // 128 + k : at // 128 + k + 1, :] for k in range(width // 128)]
        return jnp.concatenate(rows, axis=1) if len(rows) > 1 else rows[0]

    gain_one, bias_one = vector(0, 256), vector(256, 256)
    gain_two, bias_two = vector(512, 512), vector(1024, 512)
    gain_pool, bias_pool = vector(1536, 128), vector(1664, 128)
    bias_expand = vector(1792, 512)
    gain_three, bias_three = vector(2304, 1024), vector(3328, 1024)

    gather_turn(1)
    gather_out(2)
    total, square = both_sums("reduced")
    center1, scale1, mul1, add1 = norm_terms(total, square, gain_one, bias_one, pixels)

    def make_active(row, carry):
        turned = grouped(red[pl.ds(row, CHUNK), :]) * mul1 + add1
        act[1, pl.ds(PAD + row, CHUNK), :] = flat(turned * sigmoid(turned))
        return carry

    over_rows(make_active, 0)
    gather_hand(1)
    place = lax.rem(lax.broadcasted_iota(jnp.int32, (CHUNK, BOTTLE), 0) // 4, SIDE)
    not_last = place != SIDE - 1
    not_first = place != 0

    def beside(side, row, distance, lanes=slice(0, BOTTLE)):
        near = act[side, pl.ds(PAD + row - 8, CHUNK + 16), lanes]
        return pltpu.roll(near, (CHUNK + 16 - distance) % (CHUNK + 16), 0)[8 : 8 + CHUNK]

    def shift_active(row, carry):
        act[2, pl.ds(PAD + row, CHUNK), :] = jnp.where(not_last, beside(1, row, 4), 0.0)
        act[0, pl.ds(PAD + row, CHUNK), :] = jnp.where(not_first, beside(1, row, -4), 0.0)
        return carry

    over_rows(shift_active, 0)

    def make_columns(row, carry):
        for tap in range(9):
            down, side = tap // 3 - 1, tap % 3
            values = act[side, pl.ds(PAD + row + 56 * down, CHUNK), :].astype(BF16)
            columns[0, pl.ds(row, CHUNK), tap * 128 : tap * 128 + 128] = values[:, 0:128]
            columns[1, pl.ds(row, CHUNK), tap * 128 : tap * 128 + 128] = values[:, 128:256]
        return carry

    over_rows(make_columns, 0)
    gather_end(1)
    own_half = n_dp // 2

    def filters(group):
        return fwc[group * own_half : (group + 1) * own_half].reshape(9 * 128, BOTTLE)

    halves2 = (slice(0, 256), slice(256, 512))
    for group, lanes in enumerate(halves2):
        wid[:, lanes] = jnp.dot(columns[group], filters(group), preferred_element_type=F32)
        sum_start(f"widened{group}", joined([sums_of(wid, group * 256, 256)]))
    gather_turn(2)
    sum_turn("widened0")
    sum_turn("widened1")
    gather_hand(2)

    norm2 = []
    pooled = jnp.zeros((8, BOTTLE), F32)
    for group, lanes in enumerate(halves2):
        total, square = both_sums(f"widened{group}")
        norm2.append(norm_terms(total, square, gain_two[:, lanes], bias_two[:, lanes], pixels))
        m2, a2 = norm2[group][2:4]

        def make_splits(row, carry):
            turned = grouped(wid[pl.ds(row, CHUNK), lanes]) * m2 + a2
            values = turned * sigmoid(turned)
            splits[pl.ds(row, CHUNK), lanes] = flat(values)
            return carry + jnp.sum(values, axis=0)

        pooled = over_rows(make_splits, pooled)
    pooled = image_sum(pooled) * (1.0 / (SIDE * SIDE))
    gather_end(2)
    last = fpe[:, :, 0:CHANNELS].reshape(BOTTLE, CHANNELS)
    squeeze = fpe[:, :, 1024:1152].reshape(BOTTLE, INNER)
    ex_both = fpe[:, :, 1152:1408]
    expand = jnp.concatenate(
        [
            ex_both[:, 0:ex_rows].reshape(INNER, 256),
            ex_both[:, ex_rows : 2 * ex_rows].reshape(INNER, 256),
        ],
        axis=1,
    )
    pre_pool = exact_dot(pooled, squeeze, False)
    sum_start("pool", stack_sums(pair_sum(pre_pool), pair_sum(pre_pool * pre_pool)))
    total, square = unstack_sums(sum_end("pool"))
    center_p, scale_p, mul_p, add_p = norm_terms(total, square, gain_pool, bias_pool, pictures)
    normed_p = (pre_pool - center_p) * scale_p
    norm_p = pre_pool * mul_p + add_p
    gate_p = sigmoid(norm_p)
    hidden = norm_p * gate_p
    slope_p = gate_p * (1.0 + norm_p * (1.0 - gate_p))
    logits = exact_dot(hidden, expand, False) + bias_expand
    left, right = logits[:, 0:256], logits[:, 256:512]
    most = jnp.maximum(left, right)
    left, right = jnp.exp(left - most), jnp.exp(right - most)
    att0 = left / (left + right)
    att1 = right / (left + right)

    def make_mixed(row, carry):
        rows = pl.ds(row, CHUNK)
        values = grouped(splits[rows, 0:256]) * att0 + grouped(splits[rows, 256:512]) * att1
        mixed[rows, :] = flat(values).astype(BF16)
        return carry

    over_rows(make_mixed, 0)
    halves3 = (slice(0, 512), slice(512, 1024))
    blocks3 = [[slice(512 * h + k, 512 * h + k + 256) for k in (0, 256)] for h in range(2)]
    for half, lanes in enumerate(halves3):
        proj[:, lanes] = jnp.dot(mixed[...], last[:, lanes], preferred_element_type=F32)
        sum_start(
            f"projected{half}", joined([sums_of(proj, 512 * half + k, 256) for k in (0, 256)])
        )
    sum_turn("projected0")
    sum_turn("projected1")

    norm3 = []
    zero = jnp.zeros((8, 256), F32)
    for half, lanes in enumerate(halves3):
        total, square = both_sums(f"projected{half}")
        norm3.append(norm_terms(total, square, gain_three[:, lanes], bias_three[:, lanes], pixels))
        found = []
        for k, block in enumerate(blocks3[half]):
            c3, s3, m3, a3 = (item[:, k * 256 : k * 256 + 256] for item in norm3[half])

            def make_out(row, carry):
                rows = pl.ds(row, CHUNK)
                values = grouped(proj[rows, block])
                summed = grouped(x_v[rows, block].astype(F32)) + (values * m3 + a3)
                gate = sigmoid(summed)
                bo4[pl.ds(row // 4, CHUNK // 4), :, block] = by_four(summed * gate).astype(BF16)
                upstream = grouped(gy_v[rows, block].astype(F32)) * (
                    gate * (1.0 + summed * (1.0 - gate))
                )
                up[rows, block] = flat(upstream)
                normed = (values - c3) * s3
                return carry[0] + jnp.sum(upstream, axis=0), carry[1] + jnp.sum(
                    upstream * normed, axis=0
                )

            found.append(over_rows(make_out, (zero, zero)))
        sum_start(f"back_projected{half}", joined(found))
    bo_copy = pltpu.make_async_copy(bo4, bo_hbm, local_sem.at[2])
    bo_copy.start()

    def write_norm(at, pattern):
        at = at // 128
        both = pattern[0:1, :] + pattern[2:3, :]
        for k in range(both.shape[1] // 128):
            np_full[at + k : at + k + 1, :] = both[:, k * 128 : k * 128 + 128]

    sum_turn("back_projected0")
    sum_turn("back_projected1")

    for half, lanes in enumerate(halves3):
        bias_sum, gain_sum = both_sums(f"back_projected{half}")
        write_norm(2304 + 512 * half, gain_sum)
        write_norm(3328 + 512 * half, bias_sum)
        by_value, constant = back_terms(*norm3[half][0:3], bias_sum, gain_sum, pixels)
        for k, block in enumerate(blocks3[half]):
            m3, v3, k3 = (
                item[:, k * 256 : k * 256 + 256] for item in (norm3[half][2], by_value, constant)
            )

            def make_dproj(row, carry):
                rows = pl.ds(row, CHUNK)
                values = grouped(up[rows, block]) * m3 + grouped(proj[rows, block]) * v3 + k3
                dproj[rows, block] = flat(values).astype(BF16)
                return carry

            over_rows(make_dproj, 0)
        part_mixed = dot_t(dproj[:, lanes], last[:, lanes])
        d_mixed[...] = part_mixed if half == 0 else d_mixed[...] + part_mixed

    def attend(row, carry):
        rows = pl.ds(row, CHUNK)
        values = grouped(d_mixed[rows, :])
        return (
            carry[0] + jnp.sum(values * grouped(splits[rows, 0:256]), axis=0),
            carry[1] + jnp.sum(values * grouped(splits[rows, 256:512]), axis=0),
        )

    d_att0, d_att1 = over_rows(attend, (zero, zero))
    d_att0, d_att1 = image_sum(d_att0), image_sum(d_att1)
    both = att0 * d_att0 + att1 * d_att1
    d_logits = jnp.concatenate([att0 * (d_att0 - both), att1 * (d_att1 - both)], axis=1)
    d_hidden = exact_dot(d_logits, expand, True)
    d_pool = d_hidden * slope_p
    per_micro = stack_sums(pair_sum(d_pool), pair_sum(d_pool * normed_p))
    sum_start("back_pool", per_micro)
    ex_sum = pair_sum(d_logits)
    ex_sum = ex_sum + pltpu.roll(ex_sum, 2, 0)
    ex_rows_sum = ex_sum[:, 0:128]
    for k in range(1, 4):
        ex_rows_sum = jnp.where(row_ids(128) == k, ex_sum[:, k * 128 : k * 128 + 128], ex_rows_sum)

    grad_ex = image_dot(hidden, d_logits)
    grad_ex = grad_ex.reshape(n_dp, ex_rows, 512)
    ge[:, 0:ex_rows, 128:384] = grad_ex[:, :, 0:256]
    ge[:, ex_rows : 2 * ex_rows, 128:384] = grad_ex[:, :, 256:512]
    ge[:, :, 384:512] = jnp.zeros((n_dp, 2 * ex_rows, 128), F32)
    g3[...] = tdot(mixed[...], dproj[...]).reshape(g3.shape)
    reduce_core(3)
    pool_bias_sum, pool_gain_sum = unstack_sums(sum_end("back_pool"))
    write_norm(1536, pool_gain_sum)
    write_norm(1664, pool_bias_sum)
    d_pre_pool = mul_p * (
        d_pool - pool_bias_sum * (1.0 / pictures) - normed_p * (pool_gain_sum * (1.0 / pictures))
    )
    d_pooled = exact_dot(d_pre_pool, squeeze, True) * (1.0 / (SIDE * SIDE))
    for group, att in ((0, att0), (1, att1)):
        lanes = halves2[group]
        c2, s2, m2, a2 = norm2[group]

        def make_dn2(row, carry):
            rows = pl.ds(row, CHUNK)
            values = grouped(wid[rows, lanes])
            turned = values * m2 + a2
            gate = sigmoid(turned)
            slope = gate * (1.0 + turned * (1.0 - gate))
            down = (grouped(d_mixed[rows, :]) * att + d_pooled) * slope
            dn2[rows, lanes] = flat(down)
            normed = (values - c2) * s2
            return carry[0] + jnp.sum(down, axis=0), carry[1] + jnp.sum(down * normed, axis=0)

        payload = joined([over_rows(make_dn2, (zero, zero))])
        if group == 1:
            payload = jnp.concatenate([payload, ex_rows_sum], axis=0)
        sum_start(f"back_widened{group}", payload)
    ge[:, :, 0:128] = image_dot(pooled, d_pre_pool).reshape(n_dp, 2 * ex_rows, 128)
    reduce_core(4)
    sum_turn("back_widened0")
    sum_turn("back_widened1")
    reduce_y(3)
    reduce_y(4)

    small_zero = jnp.zeros((8, 128), F32)
    for group, lanes in enumerate(halves2):
        whole = sum_end(f"back_widened{group}")
        if group == 1:
            np_full[14:18, :] = whole[8:12]
        bias_sum, gain_sum = unstack_sums(unfold_lanes(whole[0:8]))
        write_norm(512 + 256 * group, gain_sum)
        write_norm(1024 + 256 * group, bias_sum)
        m2 = norm2[group][2]
        v2, k2 = back_terms(*norm2[group][0:3], bias_sum, gain_sum, pixels)

        def make_dwid(row, carry):
            rows = pl.ds(row, CHUNK)
            values = grouped(dn2[rows, lanes]) * m2 + grouped(wid[rows, lanes]) * v2 + k2
            dwid[rows, lanes] = flat(values).astype(BF16)
            return carry

        over_rows(make_dwid, 0)
        dcol[PAD : PAD + ROWS, group * 1152 : group * 1152 + 1152] = dot_t(
            dwid[:, lanes], filters(group)
        )
        inner = slice(group * 128, group * 128 + 128)

        def gather_taps(row, carry):
            for side in range(3):
                total = None
                for down in range(3):
                    at = group * 1152 + (3 * down + side) * 128
                    values = dcol[pl.ds(PAD + row - 56 * (down - 1), CHUNK), at : at + 128]
                    total = values if total is None else total + values
                act[side, pl.ds(PAD + row, CHUNK), inner] = total
            return carry

        over_rows(gather_taps, 0)
        c1, s1, m1, a1 = (item[:, inner] for item in (center1, scale1, mul1, add1))
        not_first1, not_last1 = not_first[:, inner], not_last[:, inner]

        def make_dn1(row, carry):
            rows = pl.ds(row, CHUNK)
            d_active = act[1, pl.ds(PAD + row, CHUNK), inner]
            d_active = d_active + jnp.where(not_first1, beside(2, row, -4, inner), 0.0)
            d_active = d_active + jnp.where(not_last1, beside(0, row, 4, inner), 0.0)
            values = grouped(red[rows, inner])
            turned = values * m1 + a1
            gate = sigmoid(turned)
            slope = gate * (1.0 + turned * (1.0 - gate))
            down = grouped(d_active) * slope
            dn1[rows, inner] = flat(down)
            normed = (values - c1) * s1
            return carry[0] + jnp.sum(down, axis=0), carry[1] + jnp.sum(down * normed, axis=0)

        bias_sum, gain_sum = over_rows(make_dn1, (small_zero, small_zero))
        sum_start(
            f"back_reduced{group}", stack_sums(micro_sum(bias_sum), micro_sum(gain_sum))
        )
    reduce_owner(3)
    reduce_owner(4)

    def grad_conv(group):
        gc[group * own_half : (group + 1) * own_half] = tdot(
            columns[group], dwid[:, halves2[group]]
        ).reshape(own_half, 2, 9 * 128 // own_half // 2, BOTTLE)

    grad_conv(0)
    sum_turn("back_reduced0")
    sum_turn("back_reduced1")
    grad_conv(1)
    reduce_core(1)
    reduce_core(2)
    found = [unstack_sums(sum_end(f"back_reduced{group}")) for group in range(2)]
    bias_sum, gain_sum = (jnp.concatenate(item, axis=1) for item in zip(*found))
    write_norm(0, gain_sum)
    write_norm(256, bias_sum)
    by_value, constant = back_terms(center1, scale1, mul1, bias_sum, gain_sum, pixels)
    def make_dred(row, carry):
        rows = pl.ds(row, CHUNK)
        values = grouped(dn1[rows, :]) * mul1 + grouped(red[rows, :]) * by_value + constant
        dred[rows, :] = flat(values).astype(BF16)
        return carry

    over_rows(make_dred, 0)
    g1[...] = tdot(dred[...], x_v[...]).reshape(g1.shape)
    reduce_core(0)
    reduce_y(1)
    reduce_y(2)
    proj[...] = dot_t(dred[...], fw1[...].reshape(CHANNELS, BOTTLE))
    reduce_y(0)
    reduce_spread(3)
    reduce_spread(4)
    reduce_owner(1)

    def make_dx(row, carry):
        for start in range(0, CHANNELS, 256):
            lanes = slice(start, start + 256)
            values = up[pl.ds(row, CHUNK), lanes] + proj[pl.ds(row, CHUNK), lanes]
            dx4[pl.ds(row // 4, CHUNK // 4), :, lanes] = values.reshape(CHUNK // 4, 4, 256)
        return carry

    over_rows(make_dx, 0)
    dx_copy = pltpu.make_async_copy(dx4, dx_hbm, local_sem.at[3])
    dx_copy.start()
    norm_rows = np_full[0:8, :]
    for d in range(1, n_dp):
        at = shard * d // 128
        norm_rows = jnp.where(dp == d, np_full[at : at + 8, :], norm_rows)
    norm_rows = pltpu.roll(norm_rows, lax.rem(128 - turn, 128), 1)
    gn_out[...] = jnp.where(lanes_id < 128 - turn, norm_rows, pltpu.roll(norm_rows, 7, 0))
    reduce_owner(2)
    reduce_owner(0)
    reduce_spread(1)
    reduce_spread(2)
    reduce_spread(0)
    out_copies = [
        pltpu.make_async_copy(source, target, local_sem.at[10 + k])
        for k, (source, target) in enumerate(
            (
                (gn_out, gn_hbm),
                (fs[2], f3_hbm),
                (fs[3], fe_hbm),
                (fs[1], fc_hbm),
                (fs[0], f1_hbm),
            )
        )
    ]
    out_copies[0].start()
    for which in (3, 4, 1, 2, 0):
        reduce_end(which)
        if which != 1:
            out_copies[{3: 1, 4: 2, 2: 3, 0: 4}[which]].start()

    bo_copy.wait()
    dx_copy.wait()
    for copy in out_copies:
        copy.wait()
    for k in STATS:
        if k in DIRECT:
            wait_bytes(ar_slots_a[k].at[pl.ds(0, everyone - 1)], ar_send_a.at[order[k]])
        else:
            wait_bytes(ar_slots_a[k].at[pl.ds(0, plane_size - 1)], ar_send_a.at[order[k]])
            wait_bytes(ar_slots_b[k].at[pl.ds(0, planes - 1)], ar_send_b.at[order[k]])
    wait_bytes(np_slots.at[pl.ds(0, n_dp - 1)], np_sems.at[0])
    for which in range(3):
        wait_bytes(seven(which), ws.at[which, 0])
        for stage in range(1, 4):
            wait_bytes(quarters[which](core, half_y), ws.at[which, stage])
    for which in range(5):
        wait_bytes(r1s[which], gs.at[which, 0])
        wait_bytes(r2s[which], gs.at[which, 1])
        wait_bytes(r3s[which].at[pl.ds(0, n_dp - 1)], gs.at[which, 2])
        wait_bytes(three_parts(which), gs.at[which, 3])


def update_kernel(*refs):
    sources, targets = refs[0:25], refs[25:45]
    inputs, outs, through = refs[45:68], refs[68:86], refs[86:88]
    pass_sems, in_sems, out_sems = refs[88:91]
    part = SIDE * SIDE // 4
    fetching, passing = [], []
    for k in range(4):
        rows = pl.ds(k * part, part)
        for which in range(2):
            fetching.append(
                pltpu.make_async_copy(
                    sources[which].at[rows], through[which].at[rows], pass_sems.at[0, which, k]
                )
            )
            passing.append(
                pltpu.make_async_copy(
                    through[which].at[rows], targets[which].at[rows], pass_sems.at[1, which, k]
                )
            )
    for copy in fetching:
        copy.start()
    coming = [
        pltpu.make_async_copy(source, held, in_sems.at[k])
        for k, (source, held) in enumerate(zip(sources[2:], inputs))
    ]
    for copy in coming:
        copy.start()
    grads, states = inputs[0:5], inputs[5:23]
    going = [
        pltpu.make_async_copy(held, target, out_sems.at[k])
        for k, (held, target) in enumerate(zip(outs, targets[2:]))
    ]
    ex_rows = states[9].shape[0]
    shard = states[15].shape[0]
    fans = (CHANNELS, 9 * BOTTLE // RADIX, BOTTLE, INNER // 8, BOTTLE)
    for copy in coming[0:5]:
        copy.wait()
    found = (
        grads[0][...].T,
        grads[1][...],
        grads[3][:, 0:128],
        jnp.concatenate([grads[3][0:ex_rows, 128:384], grads[3][ex_rows:, 128:384]], axis=1),
        grads[2][...],
    )
    for order, k in enumerate((3, 2, 4, 0, 1)):
        for copy in coming[5 + 3 * k : 8 + 3 * k]:
            copy.wait()
        new = adamw(
            states[3 * k][...],
            states[3 * k + 1][...],
            states[3 * k + 2][...],
            found[k],
            2.0 * fans[k] ** (-0.5),
            DECAY,
        )
        for j in range(3):
            outs[3 * k + j][...] = new[j]
            going[3 * k + j].start()
        for copy in range(2 * order, min(2 * order + 2, 8)):
            fetching[copy].wait()
            passing[copy].start()
    for copy in coming[20:23]:
        copy.wait()
    for at in range(0, shard, 128):
        width = min(128, shard - at)
        lanes = pl.ds(at, width)
        new = adamw(
            *[states[15 + j][lanes].reshape(1, width) for j in range(3)],
            grads[4][at // 128 : at // 128 + 1, 0:width],
            NORM_RATE,
            0.0,
        )
        for j in range(3):
            outs[15 + j][lanes] = new[j].reshape(width)
    for copy in going[15:18]:
        copy.start()
    for copy in passing + going:
        copy.wait()


def fused_device(
    images,
    out_grad,
    reduce_weight,
    reduce_moment,
    reduce_second,
    conv_weight,
    conv_moment,
    conv_second,
    squeeze_weight,
    squeeze_moment,
    squeeze_second,
    expand_weight,
    expand_moment,
    expand_second,
    project_weight,
    project_moment,
    project_second,
    norm_params,
    norm_moment,
    norm_second,
):
    n_dp, n_rep = lax.axis_size("dp"), lax.axis_size("rep")
    by_pixel = lambda values: jnp.transpose(values, (1, 2, 0, 3)).reshape(-1, 4, CHANNELS)
    qc = conv_weight.shape[0] // 2
    q1 = reduce_weight.shape[0] // 4
    pe = squeeze_weight.shape[0]
    vmem = pltpu.VMEM
    pixel_form = (SIDE * SIDE, 4, CHANNELS)
    scratch = [
        *[
            vmem(values.shape, F32)
            for values in (
                reduce_weight,
                conv_weight,
                squeeze_weight,
                expand_weight,
                project_weight,
                norm_params,
            )
        ],
        vmem((8, 128), F32),
        vmem(pixel_form, BF16),
        vmem(pixel_form, BF16),
        vmem((ROWS, CHANNELS), BF16),
        vmem((ROWS, CHANNELS), BF16),
        vmem((n_dp, 2, 2, q1, BOTTLE), BF16),
        vmem((n_dp, 2, qc, BOTTLE), BF16),
        vmem((n_dp, pe, 1536), BF16),
        vmem((pe, 1536), BF16),
        vmem((n_dp, 8, 128), F32),
        vmem((40, 128), F32),
        vmem((ROWS, BOTTLE), F32),
        vmem((3, ROWS + 2 * PAD, BOTTLE), F32),
        vmem((2, ROWS, 9 * 128), BF16),
        vmem((ROWS, 512), F32),
        vmem((ROWS, 512), F32),
        vmem((ROWS, BOTTLE), BF16),
        vmem((ROWS, CHANNELS), F32),
        vmem((ROWS, CHANNELS), F32),
        vmem(pixel_form, BF16),
        vmem(pixel_form, F32),
        vmem((ROWS, CHANNELS), BF16),
        vmem((ROWS, BOTTLE), F32),
        vmem((ROWS, 512), F32),
        vmem((ROWS, 512), BF16),
        vmem((ROWS + 2 * PAD, 2 * 9 * 128), F32),
        vmem((ROWS, BOTTLE), F32),
        vmem((ROWS, BOTTLE), BF16),
        vmem((2, 2, BOTTLE // 4, CHANNELS), F32),
        vmem((n_dp, 2, qc, BOTTLE), F32),
        vmem((n_dp, pe, CHANNELS), F32),
        vmem((n_dp, pe, 512), F32),
    ]
    direct = n_dp * n_rep
    scratch += [
        vmem((direct if k in DIRECT else 2 * n_rep,) + shape, F32) for k, shape in STATS.items()
    ]
    scratch += [vmem((n_dp // 2,) + shape, F32) for shape in STATS.values()]
    cut = 64
    lanes1 = CHANNELS // n_dp
    half = [
        (2, BOTTLE // 4, CHANNELS),
        (n_dp, 2, cut, 128),
        (n_dp, 2, qc - cut, 128),
        (n_dp, pe, 512),
        (n_dp, pe, 256),
    ]
    quarter = [
        (BOTTLE // 4, CHANNELS),
        (n_dp, cut, 128),
        (n_dp, qc - cut, 128),
        (n_dp, pe, 256),
        (n_dp, pe, 128),
    ]
    final = [(2, 2, BOTTLE // 4, lanes1), (2, qc, BOTTLE), (pe, CHANNELS), (pe, 512)]
    sent = [BF16, BF16, BF16, BF16, F32]
    scratch += [vmem(shape, F32) for shape in half]
    scratch += [vmem(shape, kind) for shape, kind in zip(quarter, sent)] * 3
    owned = [(BOTTLE // 4, lanes1)] + [shape[1:] for shape in quarter[1:]]
    scratch += [vmem((n_dp,) + shape, kind) for shape, kind in zip(owned, sent)]
    scratch += [vmem(shape, F32) for shape in owned]
    scratch += [vmem(shape, F32) for shape in final]
    dma = pltpu.SemaphoreType.DMA
    scratch += [dma((15,))] + [dma((len(STATS),))] * 4 + [dma((2,))] + [dma((3, 4))] * 2 + [dma((5, 4))] * 2
    any_space = pl.BlockSpec(memory_space=pl.ANY)
    block_out, images_grad, sum1, sumc, sum3, sume, norm_grads = pl.pallas_call(
        functools.partial(block_kernel, n_dp, n_rep),
        out_shape=[
            jax.ShapeDtypeStruct(pixel_form, BF16),
            jax.ShapeDtypeStruct(pixel_form, F32),
            *[jax.ShapeDtypeStruct(shape, F32) for shape in final],
            jax.ShapeDtypeStruct((8, 128), F32),
        ],
        in_specs=[any_space] * 8,
        out_specs=[any_space] * 7,
        scratch_shapes=scratch,
        compiler_params=pltpu.CompilerParams(
            collective_id=0, has_side_effects=True, vmem_limit_bytes=63 * 1024 * 1024
        ),
    )(
        by_pixel(images),
        by_pixel(out_grad),
        reduce_weight,
        conv_weight,
        squeeze_weight,
        expand_weight,
        project_weight,
        norm_params,
    )
    states = (
        reduce_weight,
        reduce_moment,
        reduce_second,
        conv_weight,
        conv_moment,
        conv_second,
        squeeze_weight,
        squeeze_moment,
        squeeze_second,
        expand_weight,
        expand_moment,
        expand_second,
        project_weight,
        project_moment,
        project_second,
    )
    held = (*states, norm_params, norm_moment, norm_second)
    sums = (
        sum1.reshape(BOTTLE, lanes1),
        sumc.reshape(conv_weight.shape),
        sum3,
        sume,
        norm_grads,
    )
    block_out, images_grad, *updated = pl.pallas_call(
        update_kernel,
        out_shape=[
            jax.ShapeDtypeStruct(pixel_form, BF16),
            jax.ShapeDtypeStruct(pixel_form, F32),
            *[jax.ShapeDtypeStruct(state.shape, F32) for state in held],
        ],
        in_specs=[any_space] * 25,
        out_specs=[any_space] * 20,
        scratch_shapes=[vmem(values.shape, F32) for values in (*sums, *held, *held)]
        + [vmem(pixel_form, BF16), vmem(pixel_form, F32)]
        + [dma((2, 2, 4)), dma((23,)), dma((18,))],
        compiler_params=pltpu.CompilerParams(vmem_limit_bytes=63 * 1024 * 1024),
    )(block_out, images_grad, *sums, *held)
    by_image = lambda values: jnp.transpose(
        values.reshape(SIDE, SIDE, images.shape[0], CHANNELS), (2, 0, 1, 3)
    )
    return (
        by_image(block_out),
        by_image(images_grad),
        *updated,
    )


def solution(mesh):
    placed = (
        P(("dp", "rep"), None, None, None),
        P(("dp", "rep"), None, None, None),
        P("dp", None),
        P("dp", None),
        P("dp", None),
        P("dp", None),
        P("dp", None),
        P("dp", None),
        P("dp", None),
        P("dp", None),
        P("dp", None),
        P("dp", None),
        P("dp", None),
        P("dp", None),
        P("dp", None),
        P("dp", None),
        P("dp", None),
        P("dp"),
        P("dp"),
        P("dp"),
    )
    n_dp, n_rep = mesh.shape["dp"], mesh.shape["rep"]
    whole_tiles = n_rep == 4 and n_dp % 2 == 0 and INNER % (16 * n_dp) == 0
    return jax.shard_map(
        fused_device if whole_tiles else per_device,
        mesh=mesh,
        in_specs=placed,
        out_specs=(
            P(("dp", "rep"), None, None, None),
            P(("dp", "rep"), None, None, None),
            P("dp", None),
            P("dp", None),
            P("dp", None),
            P("dp", None),
            P("dp", None),
            P("dp", None),
            P("dp", None),
            P("dp", None),
            P("dp", None),
            P("dp", None),
            P("dp", None),
            P("dp", None),
            P("dp", None),
            P("dp", None),
            P("dp", None),
            P("dp"),
            P("dp"),
            P("dp"),
        ),
        check_vma=False,
    )
```

```python
import functools
import jax
import jax.numpy as jnp
from jax import lax
from jax.experimental import pallas as pl
from jax.experimental.pallas import tpu as pltpu
from jax.sharding import PartitionSpec as P

CHANNELS = 1024
BOTTLE = 256
INNER = 128
RADIX = 2
SIDE = 14
MICRO = 2
STEP = 10


EPSILON = 1e-05
PRECISE = lax.Precision.HIGHEST
BETA_ONE = 0.9
BETA_TWO = 0.999
ADAM_EPSILON = 1e-08
DECAY = 0.01
NORM_RATE = 0.8
ROWS = 4 * SIDE * SIDE
NORM_WIDTH = 4352


def split_params(packed):
    widths = (
        BOTTLE,
        BOTTLE,
        RADIX * BOTTLE,
        RADIX * BOTTLE,
        INNER,
        INNER,
        RADIX * BOTTLE,
        CHANNELS,
        CHANNELS,
    )
    pieces = []
    offset = 0
    for segment in widths:
        pieces.append(lax.slice_in_dim(packed, offset, offset + segment))
        offset = offset + segment
    return pieces


def silu_slope(values):
    logistic = jax.nn.sigmoid(values)
    return logistic * (1.0 + values * (1.0 - logistic))


def norm_forward(values, gain, bias, count):
    flat = values.reshape(-1, values.shape[-1])
    total, square = lax.psum((jnp.sum(flat, axis=0), jnp.sum(flat * flat, axis=0)), ("dp", "rep"))
    center = total / count
    scale = lax.rsqrt(square / count - center * center + EPSILON)
    normed = (values - center) * scale
    return (normed * gain + bias, normed, scale)


def norm_backward(upstream, normed, scale, gain, count):
    flat_up = upstream.reshape(-1, upstream.shape[-1])
    flat_norm = normed.reshape(-1, normed.shape[-1])
    bias_sum, gain_sum = lax.psum(
        (jnp.sum(flat_up, axis=0), jnp.sum(flat_up * flat_norm, axis=0)), ("dp", "rep")
    )
    downstream = gain * scale * (upstream - bias_sum / count - normed * (gain_sum / count))
    return (downstream, gain_sum, bias_sum)


def patches(active):
    padded = jnp.pad(active, ((0, 0), (1, 1), (1, 1), (0, 0), (0, 0)))
    shifted = [
        padded[:, down_step : down_step + SIDE, side_step : side_step + SIDE]
        for down_step in range(3)
        for side_step in range(3)
    ]
    return jnp.stack(shifted, axis=4)


def unpatch(columns):
    total = jnp.zeros(
        (columns.shape[0], SIDE + 2, SIDE + 2, columns.shape[3], columns.shape[5]), jnp.float32
    )
    for down_step in range(3):
        for side_step in range(3):
            piece = columns[:, :, :, :, 3 * down_step + side_step]
            total = total + jnp.pad(
                piece,
                ((0, 0), (down_step, 2 - down_step), (side_step, 2 - side_step), (0, 0), (0, 0)),
            )
    return total[:, 1 : SIDE + 1, 1 : SIDE + 1]


def adamw(param, moment, second, gradient, rate, decay):
    moment_new = BETA_ONE * moment + (1.0 - BETA_ONE) * gradient
    second_new = BETA_TWO * second + (1.0 - BETA_TWO) * gradient * gradient
    ratio = (
        moment_new
        / (1.0 - BETA_ONE**STEP)
        / (jnp.sqrt(second_new / (1.0 - BETA_TWO**STEP)) + ADAM_EPSILON)
    )
    return (param - rate * (ratio + decay * param), moment_new, second_new)


def per_device(
    images,
    out_grad,
    reduce_weight,
    reduce_moment,
    reduce_second,
    conv_weight,
    conv_moment,
    conv_second,
    squeeze_weight,
    squeeze_moment,
    squeeze_second,
    expand_weight,
    expand_moment,
    expand_second,
    project_weight,
    project_moment,
    project_second,
    norm_params,
    norm_moment,
    norm_second,
):
    bf16 = jnp.bfloat16
    low_reduce = reduce_weight.astype(bf16)
    low_conv = conv_weight.astype(bf16)
    low_squeeze = squeeze_weight.astype(bf16)
    low_expand = expand_weight.astype(bf16)
    low_project = project_weight.astype(bf16)
    low_norm = norm_params.astype(bf16)
    devices = lax.axis_size("dp") * lax.axis_size("rep")
    per_batch = images.shape[0] // MICRO
    pixel_count = float(per_batch * SIDE * SIDE * devices)
    image_count = float(per_batch * devices)
    group_in = BOTTLE // RADIX
    grad_first = jnp.zeros((CHANNELS, BOTTLE), jnp.float32)
    grad_conv = jnp.zeros((RADIX, 9 * group_in, BOTTLE), jnp.float32)
    grad_squeeze = jnp.zeros((BOTTLE, INNER), jnp.float32)
    grad_expand = jnp.zeros((INNER, RADIX * BOTTLE), jnp.float32)
    grad_last = jnp.zeros((BOTTLE, CHANNELS), jnp.float32)
    grad_norms = jnp.zeros(
        (2 * BOTTLE + 3 * RADIX * BOTTLE + 2 * INNER + 2 * CHANNELS,), jnp.float32
    )
    outputs = []
    input_grads = []
    for number in range(MICRO):
        forward_set = (
            lax.all_gather(low_reduce, "dp", axis=0, tiled=True),
            lax.all_gather(low_conv, "dp", axis=0, tiled=True),
            lax.all_gather(low_squeeze, "dp", axis=0, tiled=True),
            lax.all_gather(low_expand, "dp", axis=0, tiled=True),
            lax.all_gather(low_project, "dp", axis=0, tiled=True),
            lax.all_gather(low_norm, "dp", axis=0, tiled=True),
        )
        first, conv, squeeze, expand, last, packed = forward_set
        (
            gain_one,
            bias_one,
            gain_two,
            bias_two,
            gain_pool,
            bias_pool,
            bias_expand,
            gain_three,
            bias_three,
        ) = split_params(packed.astype(jnp.float32))
        batched = images[number * per_batch : (number + 1) * per_batch]
        cotangent = out_grad[number * per_batch : (number + 1) * per_batch]
        reduced = jnp.einsum("nhwc,cb->nhwb", batched, first, preferred_element_type=jnp.float32)
        norm_one, normed_one, scale_one = norm_forward(reduced, gain_one, bias_one, pixel_count)
        active = jax.nn.silu(norm_one).astype(bf16)
        columns = patches(active.reshape(per_batch, SIDE, SIDE, RADIX, group_in)).reshape(
            per_batch * SIDE * SIDE, RADIX, 9 * group_in
        )
        conv_grouped = conv.reshape(RADIX, 9 * group_in, BOTTLE)
        widened = jnp.einsum(
            "prk,rko->pro", columns, conv_grouped, preferred_element_type=jnp.float32
        )
        widened = widened.reshape(per_batch, SIDE, SIDE, RADIX * BOTTLE)
        norm_two, normed_two, scale_two = norm_forward(widened, gain_two, bias_two, pixel_count)
        splits = jax.nn.silu(norm_two).reshape(per_batch, SIDE, SIDE, RADIX, BOTTLE)
        pooled = jnp.sum(jnp.sum(splits, axis=3), axis=(1, 2)) / (SIDE * SIDE)
        squeeze_float = squeeze.astype(jnp.float32)
        expand_float = expand.astype(jnp.float32)
        pre_pool = jnp.dot(pooled, squeeze_float, precision=PRECISE)
        norm_pool, normed_pool, scale_pool = norm_forward(
            pre_pool, gain_pool, bias_pool, image_count
        )
        hidden = jax.nn.silu(norm_pool)
        logits = (jnp.dot(hidden, expand_float, precision=PRECISE) + bias_expand).reshape(
            per_batch, RADIX, BOTTLE
        )
        attention = jax.nn.softmax(logits, axis=1)
        mixed = jnp.sum(splits * attention[:, None, None], axis=3).astype(bf16)
        projected = jnp.einsum("nhwb,bc->nhwc", mixed, last, preferred_element_type=jnp.float32)
        norm_three, normed_three, scale_three = norm_forward(
            projected, gain_three, bias_three, pixel_count
        )
        summed = batched.astype(jnp.float32) + norm_three
        outputs.append(jax.nn.silu(summed).astype(bf16))
        backward_set = (
            lax.all_gather(low_reduce, "dp", axis=0, tiled=True),
            lax.all_gather(low_conv, "dp", axis=0, tiled=True),
            lax.all_gather(low_squeeze, "dp", axis=0, tiled=True),
            lax.all_gather(low_expand, "dp", axis=0, tiled=True),
            lax.all_gather(low_project, "dp", axis=0, tiled=True),
            lax.all_gather(low_norm, "dp", axis=0, tiled=True),
        )
        first, conv, squeeze, expand, last, packed = backward_set
        gains_back = split_params(packed.astype(jnp.float32))
        conv_grouped = conv.reshape(RADIX, 9 * group_in, BOTTLE)
        expand_float = expand.astype(jnp.float32)
        squeeze_float = squeeze.astype(jnp.float32)
        upstream = cotangent.astype(jnp.float32) * silu_slope(summed)
        d_projected, gain_three_grad, bias_three_grad = norm_backward(
            upstream, normed_three, scale_three, gains_back[7], pixel_count
        )
        d_projected_low = d_projected.astype(bf16)
        grad_last = grad_last + jnp.einsum(
            "nhwb,nhwc->bc", mixed, d_projected_low, preferred_element_type=jnp.float32
        )
        d_mixed = jnp.einsum(
            "nhwc,bc->nhwb", d_projected_low, last, preferred_element_type=jnp.float32
        )
        d_splits = d_mixed[:, :, :, None] * attention[:, None, None]
        d_attention = jnp.sum(d_mixed[:, :, :, None] * splits, axis=(1, 2))
        d_logits = attention * (
            d_attention - jnp.sum(attention * d_attention, axis=1, keepdims=True)
        )
        flat_logits = d_logits.reshape(per_batch, RADIX * BOTTLE)
        grad_expand = grad_expand + jnp.dot(hidden.T, flat_logits, precision=PRECISE)
        d_hidden = jnp.dot(flat_logits, expand_float.T, precision=PRECISE)
        d_pool_norm = d_hidden * silu_slope(norm_pool)
        pool_bias_sum, pool_gain_sum, expand_bias_sum = lax.psum(
            (
                jnp.sum(d_pool_norm, axis=0),
                jnp.sum(d_pool_norm * normed_pool, axis=0),
                jnp.sum(flat_logits, axis=0),
            ),
            ("dp", "rep"),
        )
        d_pre_pool = (
            gains_back[4]
            * scale_pool
            * (
                d_pool_norm
                - pool_bias_sum / image_count
                - normed_pool * (pool_gain_sum / image_count)
            )
        )
        grad_squeeze = grad_squeeze + jnp.dot(pooled.T, d_pre_pool, precision=PRECISE)
        d_pooled = jnp.dot(d_pre_pool, squeeze_float.T, precision=PRECISE)
        d_splits = d_splits + (d_pooled / (SIDE * SIDE))[:, None, None, None, :]
        d_norm_two = d_splits.reshape(per_batch, SIDE, SIDE, RADIX * BOTTLE) * silu_slope(norm_two)
        d_widened, gain_two_grad, bias_two_grad = norm_backward(
            d_norm_two, normed_two, scale_two, gains_back[2], pixel_count
        )
        d_widened_low = d_widened.astype(bf16).reshape(per_batch * SIDE * SIDE, RADIX, BOTTLE)
        grad_conv = grad_conv + jnp.einsum(
            "prk,pro->rko", columns, d_widened_low, preferred_element_type=jnp.float32
        )
        d_columns = jnp.einsum(
            "pro,rko->prk", d_widened_low, conv_grouped, preferred_element_type=jnp.float32
        )
        d_active = unpatch(d_columns.reshape(per_batch, SIDE, SIDE, RADIX, 9, group_in)).reshape(
            per_batch, SIDE, SIDE, BOTTLE
        )
        d_norm_one = d_active * silu_slope(norm_one)
        d_reduced, gain_one_grad, bias_one_grad = norm_backward(
            d_norm_one, normed_one, scale_one, gains_back[0], pixel_count
        )
        d_reduced_low = d_reduced.astype(bf16)
        grad_first = grad_first + jnp.einsum(
            "nhwc,nhwb->cb", batched, d_reduced_low, preferred_element_type=jnp.float32
        )
        input_grads.append(
            upstream
            + jnp.einsum("nhwb,cb->nhwc", d_reduced_low, first, preferred_element_type=jnp.float32)
        )
        grad_norms = grad_norms + jnp.concatenate(
            [
                gain_one_grad,
                bias_one_grad,
                gain_two_grad,
                bias_two_grad,
                pool_gain_sum,
                pool_bias_sum,
                expand_bias_sum,
                gain_three_grad,
                bias_three_grad,
            ]
        )
    grad_conv = grad_conv.reshape(9 * BOTTLE, BOTTLE)
    partial_value = (
        lax.psum_scatter(grad_first, "dp", scatter_dimension=0, tiled=True),
        lax.psum_scatter(grad_conv, "dp", scatter_dimension=0, tiled=True),
        lax.psum_scatter(grad_squeeze, "dp", scatter_dimension=0, tiled=True),
        lax.psum_scatter(grad_expand, "dp", scatter_dimension=0, tiled=True),
        lax.psum_scatter(grad_last, "dp", scatter_dimension=0, tiled=True),
    )
    owned = lax.psum(
        (partial_value[0], partial_value[1], partial_value[2], partial_value[3], partial_value[4]),
        "rep",
    )
    shard_length = norm_params.shape[0]
    norm_grad_owned = lax.dynamic_slice_in_dim(
        grad_norms, lax.axis_index("dp") * shard_length, shard_length
    )
    reduce_new = adamw(
        reduce_weight, reduce_moment, reduce_second, owned[0], 2.0 * CHANNELS ** (-0.5), DECAY
    )
    conv_new = adamw(
        conv_weight,
        conv_moment,
        conv_second,
        owned[1],
        2.0 * (9 * BOTTLE // RADIX) ** (-0.5),
        DECAY,
    )
    squeeze_new = adamw(
        squeeze_weight, squeeze_moment, squeeze_second, owned[2], 2.0 * BOTTLE ** (-0.5), DECAY
    )
    expand_new = adamw(
        expand_weight, expand_moment, expand_second, owned[3], 2.0 * (INNER // 8) ** (-0.5), DECAY
    )
    project_new = adamw(
        project_weight, project_moment, project_second, owned[4], 2.0 * BOTTLE ** (-0.5), DECAY
    )
    norm_new = adamw(norm_params, norm_moment, norm_second, norm_grad_owned, NORM_RATE, 0.0)
    return (
        jnp.concatenate(outputs, axis=0),
        jnp.concatenate(input_grads, axis=0),
        reduce_new[0],
        reduce_new[1],
        reduce_new[2],
        conv_new[0],
        conv_new[1],
        conv_new[2],
        squeeze_new[0],
        squeeze_new[1],
        squeeze_new[2],
        expand_new[0],
        expand_new[1],
        expand_new[2],
        project_new[0],
        project_new[1],
        project_new[2],
        norm_new[0],
        norm_new[1],
        norm_new[2],
    )


MESH = pl.DeviceIdType.MESH
PAD = 64
CHUNK = 112
F32 = jnp.float32
BF16 = jnp.bfloat16
STATS = {
    "reduced": (8, 128),
    "widened0": (8, 128),
    "widened1": (8, 128),
    "pool": (8, 128),
    "images": (16, 128),
    "projected0": (8, 256),
    "projected1": (8, 256),
    "back_projected0": (8, 256),
    "back_projected1": (8, 256),
    "back_pool": (8, 128),
    "back_widened0": (8, 128),
    "back_widened1": (16, 128),
    "back_reduced0": (8, 128),
    "back_reduced1": (8, 128),
}
DIRECT = ("reduced", "pool", "back_pool")


def sigmoid(values):
    return 0.5 * jnp.tanh(0.5 * values) + 0.5


def row_ids(width):
    return lax.broadcasted_iota(jnp.int32, (8, width), 0)


def image_sum(rows):
    return rows + pltpu.roll(rows, 4, 0)


def pair_sum(rows):
    even = row_ids(rows.shape[1]) % 2 == 0
    return rows + jnp.where(even, pltpu.roll(rows, 7, 0), pltpu.roll(rows, 1, 0))


def micro_sum(rows):
    return pair_sum(image_sum(rows))


def stack_sums(first, second):
    return jnp.where(row_ids(first.shape[1]) < 4, first, second)


def unstack_sums(stacked):
    upper = row_ids(stacked.shape[1]) < 4
    turned = pltpu.roll(stacked, 4, 0)
    return jnp.where(upper, stacked, turned), jnp.where(upper, turned, stacked)


def fold_lanes(stacked):
    half = stacked.shape[1] // 2
    even = row_ids(half) % 2 == 0
    return jnp.where(even, stacked[:, :half], stacked[:, half:])


def unfold_lanes(folded):
    even = row_ids(folded.shape[1]) % 2 == 0
    left = jnp.where(even, folded, pltpu.roll(folded, 1, 0))
    right = jnp.where(even, pltpu.roll(folded, 7, 0), folded)
    return jnp.concatenate([left, right], axis=1)


def norm_terms(total, square, gain, bias, count):
    center = total * (1.0 / count)
    scale = lax.rsqrt(square * (1.0 / count) - center * center + EPSILON)
    slope = scale * gain
    return center, scale, slope, bias - center * slope


def back_terms(center, scale, slope, bias_sum, gain_sum, count):
    by_value = -slope * scale * (gain_sum * (1.0 / count))
    constant = -slope * (bias_sum * (1.0 / count)) - by_value * center
    return by_value, constant


def tdot(left, right):
    return lax.dot_general(left, right, (((0,), (0,)), ((), ())), preferred_element_type=F32)


def dot_t(left, right):
    return lax.dot_general(left, right, (((1,), (1,)), ((), ())), preferred_element_type=F32)


def in_parts(values, parts):
    found = []
    for _ in range(parts):
        rounded = values.astype(BF16).astype(F32)
        found.append(rounded)
        values = values - rounded
    return found


def exact_dot(left, right, transposed):
    stacked = jnp.concatenate(in_parts(left, 3), axis=0).astype(BF16)
    wide = dot_t(stacked, right) if transposed else jnp.dot(stacked, right, preferred_element_type=F32)
    return wide[0:8] + wide[8:16] + wide[16:24]


def row_dot(left, right):
    high, low = in_parts(left, 2)
    other_high, other_low = in_parts(right, 2)
    return tdot(
        jnp.concatenate([high, high, low, low], axis=0).astype(BF16),
        jnp.concatenate([other_high, other_low, other_high, other_low], axis=0).astype(BF16),
    )


def image_dot(left, right):
    return row_dot(jnp.where(row_ids(left.shape[1]) < 4, left, 0.0), right)


def block_kernel(
    n_dp,
    n_rep,
    x_hbm,
    gy_hbm,
    w1_hbm,
    wc_hbm,
    sq_hbm,
    ex_hbm,
    w3_hbm,
    np_hbm,
    bo_hbm,
    dx_hbm,
    f1_hbm,
    fc_hbm,
    f3_hbm,
    fe_hbm,
    gn_hbm,
    w1_own,
    wc_own,
    sq_own,
    ex_own,
    w3_own,
    np_own,
    gn_out,
    x4,
    gy4,
    x_v,
    gy_v,
    fw1,
    fwc,
    fpe,
    pe_own,
    np_slots,
    np_full,
    red,
    act,
    columns,
    wid,
    splits,
    mixed,
    proj,
    up,
    bo4,
    dx4,
    dproj,
    d_mixed,
    dn2,
    dwid,
    dcol,
    dn1,
    dred,
    g1,
    gc,
    g3,
    ge,
    gb,
    fix,
    back_own,
    *rest,
):
    n_ar = len(STATS)
    order = {name: k for k, name in enumerate(STATS)}
    ar_slots_a = dict(zip(STATS, rest[0:n_ar]))
    ar_slots_b = dict(zip(STATS, rest[n_ar : 2 * n_ar]))
    rest = rest[2 * n_ar :]
    r1s, ys, r2s, ks, r3s, own = (rest[6 * i : 6 * i + 6] for i in range(6))
    fs = rest[36:40]
    rest = rest[40:]
    local_sem, ar_send_a, ar_recv_a, ar_send_b, ar_recv_b, np_sems, ws, wr, gs, gr = rest

    dp = lax.axis_index("dp")
    rep = lax.axis_index("rep")
    core = lax.rem(rep, 2)
    half_y = lax.div(rep, 2)
    planes = n_dp // 2
    plane_size = 2 * n_rep
    plane = lax.div(dp, 2)
    in_plane = lax.rem(dp, 2) * n_rep + rep
    sibling = (dp, half_y * 2 + (1 - core))
    across = (dp, (1 - half_y) * 2 + core)
    pixels = float(SIDE * SIDE * 2 * n_dp * n_rep)
    pictures = float(2 * n_dp * n_rep)

    x = lax.rem(dp, 2)
    if planes == 4:
        upper = lax.div(plane, 2)
        other_planes = [3 - 3 * upper, 2 - upper, 1 - plane + 4 * upper]
    else:
        other_planes = [lax.rem(plane + step, planes) for step in range(1, planes)]
    flips = ((1, 1, 1), (1, 1, 0), (1, 0, 1), (1, 0, 0), (0, 1, 1), (0, 1, 0), (0, 0, 1), (0, 0, 0))

    def of_flip(z, flip):
        there = [1 - own if turn else own for own, turn in zip((x, half_y, core), flip)]
        return (z * 2 + there[0], there[1] * 2 + there[2])

    plane_peers = [of_flip(plane, flip) for flip in flips[:-1]]
    column_peers = [of_flip(z, flips[-1]) for z in other_planes]
    owner_peers = [of_flip(z, flip) for z in other_planes for flip in (flips[3], flips[7])]
    owner_peers += [of_flip(plane, flips[3])]
    all_peers = [of_flip(z, flip) for z in other_planes for flip in flips] + plane_peers
    me, everyone = dp * n_rep + rep, n_dp * n_rep
    rep_peers = [(dp, lax.rem(rep + step, n_rep)) for step in range(1, n_rep)]

    def remote(src, dst, send_sem, recv_sem, device):
        return pltpu.make_async_remote_copy(
            src_ref=src,
            dst_ref=dst,
            send_sem=send_sem,
            recv_sem=recv_sem,
            device_id=device,
            device_id_type=MESH,
        )

    def send_all(ref, send_sem, recv_sem, peers):
        for device in peers:
            remote(ref, ref, send_sem, recv_sem, device).start()

    def wait_bytes(ref, sem):
        pltpu.make_async_copy(ref, ref, sem).wait()

    def over_rows(body, init):
        def step(index, carry):
            return body(pl.multiple_of(index * CHUNK, CHUNK), carry)

        return lax.fori_loop(0, ROWS // CHUNK, step, init)

    def grouped(values):
        return values.reshape(CHUNK // 8, 8, values.shape[-1])

    def by_four(values):
        return flat(values).reshape(CHUNK // 4, 4, values.shape[-1])

    def flat(values):
        return values.reshape(CHUNK, values.shape[-1])

    own_copies = [
        pltpu.make_async_copy(source, target, local_sem.at[4 + k])
        for k, (source, target) in enumerate(
            (
                (w1_hbm, w1_own),
                (np_hbm, np_own),
                (wc_hbm, wc_own),
                (w3_hbm, w3_own),
                (sq_hbm, sq_own),
                (ex_hbm, ex_own),
            )
        )
    ]
    for copy in own_copies:
        copy.start()
    x_copy = pltpu.make_async_copy(x_hbm, x4, local_sem.at[0])
    gy_copy = pltpu.make_async_copy(gy_hbm, gy4, local_sem.at[1])
    x_copy.start()
    barrier = pltpu.get_barrier_semaphore()
    for device in all_peers:
        pl.semaphore_signal(barrier, inc=1, device_id=device, device_id_type=MESH)

    part = core * 2 + half_y
    own_copies[0].wait()
    q1 = w1_own.shape[0] // 4
    fw1[dp, core, half_y] = w1_own[pl.ds(pl.multiple_of(part * q1, q1), q1), :].astype(BF16)
    core_lanes = pl.ds(pl.multiple_of(core * 128, 128), 128)
    pe_lanes = pl.ds(pl.multiple_of(part * 384, 128), 384)

    pl.semaphore_wait(barrier, everyone - 1)

    def quarter_w1(c, y):
        return fw1.at[:, c, y]

    def quarter_wc(c, y):
        return fwc.at[:, y, :, pl.ds(pl.multiple_of(c * 128, 128), 128)]

    def quarter_pe(c, y):
        return fpe.at[:, :, pl.ds(pl.multiple_of((c * 2 + y) * 384, 128), 384)]

    quarters = (quarter_w1, quarter_wc, quarter_pe)

    def piece(which, d):
        return (
            fw1.at[d, core, half_y],
            fwc.at[d, half_y, :, core_lanes],
            fpe.at[d, :, pe_lanes],
        )[which]

    def seven(which):
        return (
            fw1.at[pl.ds(0, n_dp - 1), core, half_y],
            fwc.at[pl.ds(0, n_dp - 1), half_y, :, core_lanes],
            fpe.at[pl.ds(0, n_dp - 1), :, pe_lanes],
        )[which]

    def gather_out(which):
        send_all(piece(which, dp), ws.at[which, 0], wr.at[which, 0], owner_peers)

    def gather_turn(which):
        wait_bytes(seven(which), wr.at[which, 0])
        mine = quarters[which](core, half_y)
        remote(mine, mine, ws.at[which, 1], wr.at[which, 1], across).start()
        remote(mine, mine, ws.at[which, 2], wr.at[which, 2], sibling).start()

    def gather_hand(which):
        theirs = quarters[which](core, 1 - half_y)
        wait_bytes(theirs, wr.at[which, 1])
        remote(theirs, theirs, ws.at[which, 3], wr.at[which, 3], sibling).start()

    def gather_end(which):
        wait_bytes(quarters[which](1 - core, half_y), wr.at[which, 2])
        wait_bytes(quarters[which](1 - core, 1 - half_y), wr.at[which, 3])

    def to_rows(source, target):
        def body(index, carry):
            values = source[pl.ds(index * (CHUNK // 4), CHUNK // 4)].astype(F32)
            row = pl.multiple_of(index * CHUNK, CHUNK)
            target[pl.ds(row, CHUNK), :] = values.reshape(CHUNK, CHANNELS).astype(BF16)
            return carry

        lax.fori_loop(0, ROWS // CHUNK, body, 0)

    gather_out(0)

    own_copies[1].wait()
    shard = np_own.shape[0]
    lanes_id = lax.broadcasted_iota(jnp.int32, (8, 128), 1)
    turn = lax.rem(shard * dp, 128)
    np_rows = []
    for at in range(0, shard, 128):
        width = min(128, shard - at)
        piece_row = np_own[pl.ds(at, width)].reshape(1, width)
        if width < 128:
            piece_row = jnp.concatenate([piece_row, jnp.zeros((1, 128 - width), F32)], axis=1)
        np_rows.append(piece_row)
    np_rows.append(jnp.zeros((8 - len(np_rows), 128), F32))
    np_turned = jnp.concatenate(np_rows, axis=0).astype(BF16).astype(F32)
    np_turned = pltpu.roll(np_turned, turn, 1)
    np_slots[dp] = jnp.where(lanes_id < turn, pltpu.roll(np_turned, 1, 0), np_turned)
    send_all(np_slots.at[dp], np_sems.at[0], np_sems.at[1], owner_peers)
    own_copies[2].wait()
    qc = wc_own.shape[0] // 2
    fwc[dp, half_y, :, core_lanes] = wc_own[
        pl.ds(pl.multiple_of(half_y * qc, qc), qc), core_lanes
    ].astype(BF16)
    for copy in own_copies[3:]:
        copy.wait()
    ex_rows = ex_own.shape[0]
    pe_own[:, 0:CHANNELS] = w3_own[...].astype(BF16)
    pe_own[:, 1024:1152] = sq_own[...].astype(BF16)
    pe_own[0:ex_rows, 1152:1408] = ex_own[:, 0:256].astype(BF16)
    pe_own[ex_rows : 2 * ex_rows, 1152:1408] = ex_own[:, 256:512].astype(BF16)
    pe_own[:, 1408:1536] = jnp.zeros((2 * ex_rows, 128), BF16)
    fpe[dp, :, pe_lanes] = pe_own[:, pe_lanes]
    gy_copy.start()
    x_copy.wait()
    to_rows(x4, x_v)
    gather_turn(0)
    gather_out(1)
    zero_rows = jnp.zeros((PAD, BOTTLE), F32)
    for side in range(3):
        act[side, 0:PAD, :] = zero_rows
        act[side, PAD + ROWS : 2 * PAD + ROWS, :] = zero_rows
    for lane_block in range(9):
        dcol[0:PAD, lane_block * 256 : lane_block * 256 + 256] = zero_rows
        dcol[PAD + ROWS : 2 * PAD + ROWS, lane_block * 256 : lane_block * 256 + 256] = zero_rows
    gather_hand(0)

    def sum_start(k, payload):
        if k in DIRECT:
            ar_slots_a[k][me] = payload
            send_all(ar_slots_a[k].at[me], ar_send_a.at[order[k]], ar_recv_a.at[order[k]], all_peers)
        else:
            ar_slots_a[k][in_plane] = payload
            send_all(ar_slots_a[k].at[in_plane], ar_send_a.at[order[k]], ar_recv_a.at[order[k]], plane_peers)

    def sum_slots(slots, count):
        sums = [slots[slot] for slot in range(count)]
        while len(sums) > 1:
            sums = [sums[i] + sums[i + 1] for i in range(0, len(sums), 2)]
        return sums[0]

    def sum_turn(k):
        if k in DIRECT:
            return
        wait_bytes(ar_slots_a[k].at[pl.ds(0, plane_size - 1)], ar_recv_a.at[order[k]])
        ar_slots_b[k][plane] = sum_slots(ar_slots_a[k], plane_size)
        send_all(ar_slots_b[k].at[plane], ar_send_b.at[order[k]], ar_recv_b.at[order[k]], column_peers)

    def sum_end(k):
        if k in DIRECT:
            wait_bytes(ar_slots_a[k].at[pl.ds(0, everyone - 1)], ar_recv_a.at[order[k]])
            return sum_slots(ar_slots_a[k], everyone)
        wait_bytes(ar_slots_b[k].at[pl.ds(0, planes - 1)], ar_recv_b.at[order[k]])
        return sum_slots(ar_slots_b[k], planes)

    def lanes_of(index, width):
        return pl.ds(pl.multiple_of(index * width, 128), width)

    cut = 64
    conv_rows = {1: pl.ds(0, cut), 2: pl.ds(cut, gc.shape[2] - cut)}
    grads = (g1, gc, gc, g3, ge, gb)
    turned_kinds = (0, 5)

    def half_of(which, c):
        ref = grads[which]
        if which in turned_kinds:
            return ref.at[c]
        if which in conv_rows:
            return ref.at[:, :, conv_rows[which], lanes_of(c, 128)]
        return ref.at[:, :, lanes_of(c, (512, 256)[which - 3])]

    def y_part(which, ref, y):
        if which in turned_kinds:
            return ref.at[y]
        if which < 3:
            return ref.at[:, y]
        return ref.at[:, :, lanes_of(y, (256, 128)[which - 3])]

    def quarter_of(which, c, y):
        ref = grads[which]
        if which in turned_kinds:
            return ref.at[c, y]
        if which in conv_rows:
            return ref.at[:, y, conv_rows[which], lanes_of(c, 128)]
        return ref.at[:, :, lanes_of(c * 2 + y, (256, 128)[which - 3])]

    def final_part(which, c, y):
        if which == 0:
            return fs[0].at[c, y]
        if which in conv_rows:
            return fs[1].at[y, conv_rows[which], lanes_of(c, 128)]
        return fs[which - 1].at[:, lanes_of(c * 2 + y, (256, 128)[which - 3])]

    def of_owner(which, ref, d):
        return ref.at[:, lanes_of(d, CHANNELS // n_dp)] if which in turned_kinds else ref.at[d]

    def in_blocks(which, body):
        if which in turned_kinds:
            count = 4
            rows = grads[which].shape[2] // count
            block = lambda index: pl.ds(pl.multiple_of(index * rows, rows), rows)
        else:
            count, block = n_dp, lambda index: index

        def step(index, carry):
            body(block(index))
            return carry

        lax.fori_loop(0, count, step, 0)

    def reduce_core(which):
        remote(
            half_of(which, 1 - core), r1s[which], gs.at[which, 0], gr.at[which, 0], sibling
        ).start()

    def reduce_y(which):
        wait_bytes(r1s[which], gr.at[which, 0])
        away = quarter_of(which, core, 1 - half_y)
        mine = quarter_of(which, core, half_y)
        there = y_part(which, r1s[which], 1 - half_y)
        here = y_part(which, r1s[which], half_y)

        def add_away(at):
            ys[which][at] = (away[at].astype(F32) + there[at].astype(F32)).astype(
                ys[which].dtype
            )

        in_blocks(which, add_away)
        remote(ys[which], r2s[which], gs.at[which, 1], gr.at[which, 1], across).start()

        def add_mine(at):
            mine[at] = (mine[at].astype(F32) + here[at].astype(F32)).astype(mine.dtype)

        in_blocks(which, add_mine)

    def reduce_owner(which):
        wait_bytes(r2s[which], gr.at[which, 1])
        mine = quarter_of(which, core, half_y)

        def add(at):
            ks[which][at] = (mine[at].astype(F32) + r2s[which][at].astype(F32)).astype(
                ks[which].dtype
            )

        in_blocks(which, add)
        for device in owner_peers:
            remote(
                of_owner(which, ks[which], device[0]),
                r3s[which].at[dp],
                gs.at[which, 2],
                gr.at[which, 2],
                device,
            ).start()
        own[which][...] = of_owner(which, mine, dp)[...].astype(F32) + of_owner(
            which, r2s[which], dp
        )[...].astype(F32)
        r3s[which][dp] = jnp.zeros(own[which].shape, r3s[which].dtype)

    def owner_total(which):
        wait_bytes(r3s[which].at[pl.ds(0, n_dp - 1)], gr.at[which, 2])
        total = own[which][...]
        for slot in range(n_dp):
            total = total + r3s[which][slot].astype(F32)
        return total

    def reduce_spread(which):
        total = owner_total(which)
        if which == 0:
            rows = pl.ds(pl.multiple_of(part * (BOTTLE // 4), BOTTLE // 4), BOTTLE // 4)
            total = total - fix[0, rows, :]
            for m in range(2):
                total = total - fix[1 + m, rows, :] * back_own[m]
        mine = final_part(which, core, half_y)
        mine[...] = total
        send_all(mine, gs.at[which, 3], gr.at[which, 3], rep_peers)

    def three_parts(which):
        if which == 0:
            return r1s[0].at[0, :, pl.ds(0, 3 * CHANNELS // n_dp)]
        return r1s[which].at[pl.ds(0, 3), 0] if which < 3 else y_part(which, r1s[which], 0).at[pl.ds(0, 3)]

    def reduce_end(which):
        wait_bytes(three_parts(which), gr.at[which, 3])

    gather_end(0)
    red[...] = jnp.dot(x_v[...], fw1[...].reshape(CHANNELS, BOTTLE), preferred_element_type=F32)

    def sums_of(ref, start, width):
        def body(row, carry):
            values = grouped(ref[pl.ds(row, CHUNK), start : start + width])
            return carry[0] + jnp.sum(values, axis=0), carry[1] + jnp.sum(values * values, axis=0)

        zero = jnp.zeros((8, width), F32)
        return over_rows(body, (zero, zero))

    def joined(found):
        both = [jnp.concatenate(item, axis=1) for item in zip(*found)]
        return fold_lanes(stack_sums(micro_sum(both[0]), micro_sum(both[1])))

    def both_sums(name):
        return unstack_sums(unfold_lanes(sum_end(name)))

    sum_start("reduced", joined([sums_of(red, 0, 256)]))

    gy_copy.wait()
    to_rows(gy4, gy_v)
    wait_bytes(np_slots.at[pl.ds(0, n_dp - 1)], np_sems.at[1])
    np_full[...] = jnp.zeros(np_full.shape, F32)
    for d in range(n_dp):
        at = shard * d // 128
        np_full[at : at + 8, :] = np_full[at : at + 8, :] + np_slots[d]

    def vector(at, width):
        rows = [np_full[at // 128 + k : at // 128 + k + 1, :] for k in range(width // 128)]
        return jnp.concatenate(rows, axis=1) if len(rows) > 1 else rows[0]

    gain_one, bias_one = vector(0, 256), vector(256, 256)
    gain_two, bias_two = vector(512, 512), vector(1024, 512)
    gain_pool, bias_pool = vector(1536, 128), vector(1664, 128)
    bias_expand = vector(1792, 512)
    gain_three, bias_three = vector(2304, 1024), vector(3328, 1024)

    gather_turn(1)
    gather_out(2)
    total, square = both_sums("reduced")
    center1, scale1, mul1, add1 = norm_terms(total, square, gain_one, bias_one, pixels)

    def make_active(row, carry):
        turned = grouped(red[pl.ds(row, CHUNK), :]) * mul1 + add1
        act[1, pl.ds(PAD + row, CHUNK), :] = flat(turned * sigmoid(turned))
        return carry

    over_rows(make_active, 0)
    gather_hand(1)
    place = lax.rem(lax.broadcasted_iota(jnp.int32, (CHUNK, BOTTLE), 0) // 4, SIDE)
    not_last = place != SIDE - 1
    not_first = place != 0

    def beside(side, row, distance, lanes=slice(0, BOTTLE)):
        near = act[side, pl.ds(PAD + row - 8, CHUNK + 16), lanes]
        return pltpu.roll(near, (CHUNK + 16 - distance) % (CHUNK + 16), 0)[8 : 8 + CHUNK]

    def shift_active(row, carry):
        act[2, pl.ds(PAD + row, CHUNK), :] = jnp.where(not_last, beside(1, row, 4), 0.0)
        act[0, pl.ds(PAD + row, CHUNK), :] = jnp.where(not_first, beside(1, row, -4), 0.0)
        return carry

    over_rows(shift_active, 0)

    def make_columns(row, carry):
        for tap in range(9):
            down, side = tap // 3 - 1, tap % 3
            values = act[side, pl.ds(PAD + row + 56 * down, CHUNK), :].astype(BF16)
            columns[0, pl.ds(row, CHUNK), tap * 128 : tap * 128 + 128] = values[:, 0:128]
            columns[1, pl.ds(row, CHUNK), tap * 128 : tap * 128 + 128] = values[:, 128:256]
        return carry

    over_rows(make_columns, 0)
    gather_end(1)
    own_half = n_dp // 2

    def filters(group):
        return fwc[group * own_half : (group + 1) * own_half].reshape(9 * 128, BOTTLE)

    halves2 = (slice(0, 256), slice(256, 512))
    for group, lanes in enumerate(halves2):
        wid[:, lanes] = jnp.dot(columns[group], filters(group), preferred_element_type=F32)
        sum_start(f"widened{group}", joined([sums_of(wid, group * 256, 256)]))
    gather_turn(2)
    sum_turn("widened0")
    sum_turn("widened1")
    gather_hand(2)

    norm2 = []
    pooled = jnp.zeros((8, BOTTLE), F32)
    for group, lanes in enumerate(halves2):
        total, square = both_sums(f"widened{group}")
        norm2.append(norm_terms(total, square, gain_two[:, lanes], bias_two[:, lanes], pixels))
        m2, a2 = norm2[group][2:4]

        def make_splits(row, carry):
            turned = grouped(wid[pl.ds(row, CHUNK), lanes]) * m2 + a2
            values = turned * sigmoid(turned)
            splits[pl.ds(row, CHUNK), lanes] = flat(values)
            return carry + jnp.sum(values, axis=0)

        pooled = over_rows(make_splits, pooled)
    pooled = image_sum(pooled) * (1.0 / (SIDE * SIDE))
    gather_end(2)
    last = fpe[:, :, 0:CHANNELS].reshape(BOTTLE, CHANNELS)
    squeeze = fpe[:, :, 1024:1152].reshape(BOTTLE, INNER)
    ex_both = fpe[:, :, 1152:1408]
    expand = jnp.concatenate(
        [
            ex_both[:, 0:ex_rows].reshape(INNER, 256),
            ex_both[:, ex_rows : 2 * ex_rows].reshape(INNER, 256),
        ],
        axis=1,
    )
    pre_pool = exact_dot(pooled, squeeze, False)
    sum_start("pool", stack_sums(pair_sum(pre_pool), pair_sum(pre_pool * pre_pool)))
    first_micro = lax.rem(row_ids(BOTTLE), 4) < 2

    def make_normed(row, carry):
        rows = pl.ds(row, CHUNK)
        normed = (grouped(red[rows, :]) - center1) * scale1
        dwid[rows, 0:256] = flat(jnp.where(first_micro, normed, 0.0)).astype(BF16)
        dwid[rows, 256:512] = flat(jnp.where(first_micro, 0.0, normed)).astype(BF16)
        return carry + jnp.sum(grouped(x_v[rows, :].astype(F32)), axis=0)

    image_sums = micro_sum(over_rows(make_normed, jnp.zeros((8, CHANNELS), F32)))
    sum_start(
        "images",
        jnp.concatenate(
            [
                image_sums[2 * m : 2 * m + 1, at : at + 128]
                for m in range(2)
                for at in range(0, CHANNELS, 128)
            ],
            axis=0,
        ),
    )
    normed_images = tdot(dwid[...], x_v[...]).astype(BF16)
    normed_images = normed_images.reshape(2, 2, 2, BOTTLE // 4, CHANNELS)
    for m in range(2):
        gb[:, :, m * (BOTTLE // 4) : (m + 1) * (BOTTLE // 4)] = normed_images[m]
    reduce_core(5)
    total, square = unstack_sums(sum_end("pool"))
    center_p, scale_p, mul_p, add_p = norm_terms(total, square, gain_pool, bias_pool, pictures)
    normed_p = (pre_pool - center_p) * scale_p
    norm_p = pre_pool * mul_p + add_p
    gate_p = sigmoid(norm_p)
    hidden = norm_p * gate_p
    slope_p = gate_p * (1.0 + norm_p * (1.0 - gate_p))
    logits = exact_dot(hidden, expand, False) + bias_expand
    left, right = logits[:, 0:256], logits[:, 256:512]
    most = jnp.maximum(left, right)
    left, right = jnp.exp(left - most), jnp.exp(right - most)
    att0 = left / (left + right)
    att1 = right / (left + right)

    def make_mixed(row, carry):
        rows = pl.ds(row, CHUNK)
        values = grouped(splits[rows, 0:256]) * att0 + grouped(splits[rows, 256:512]) * att1
        mixed[rows, :] = flat(values).astype(BF16)
        return carry

    over_rows(make_mixed, 0)
    halves3 = (slice(0, 512), slice(512, 1024))
    blocks3 = [[slice(512 * h + k, 512 * h + k + 256) for k in (0, 256)] for h in range(2)]
    for half, lanes in enumerate(halves3):
        proj[:, lanes] = jnp.dot(mixed[...], last[:, lanes], preferred_element_type=F32)
        sum_start(
            f"projected{half}", joined([sums_of(proj, 512 * half + k, 256) for k in (0, 256)])
        )
    sum_turn("projected0")
    sum_turn("projected1")
    sum_turn("images")
    reduce_y(5)

    norm3 = []
    zero = jnp.zeros((8, 256), F32)
    for half, lanes in enumerate(halves3):
        total, square = both_sums(f"projected{half}")
        norm3.append(norm_terms(total, square, gain_three[:, lanes], bias_three[:, lanes], pixels))
        found = []
        for k, block in enumerate(blocks3[half]):
            c3, s3, m3, a3 = (item[:, k * 256 : k * 256 + 256] for item in norm3[half])

            def make_out(row, carry):
                rows = pl.ds(row, CHUNK)
                values = grouped(proj[rows, block])
                summed = grouped(x_v[rows, block].astype(F32)) + (values * m3 + a3)
                gate = sigmoid(summed)
                bo4[pl.ds(row // 4, CHUNK // 4), :, block] = by_four(summed * gate).astype(BF16)
                upstream = grouped(gy_v[rows, block].astype(F32)) * (
                    gate * (1.0 + summed * (1.0 - gate))
                )
                up[rows, block] = flat(upstream)
                normed = (values - c3) * s3
                return carry[0] + jnp.sum(upstream, axis=0), carry[1] + jnp.sum(
                    upstream * normed, axis=0
                )

            found.append(over_rows(make_out, (zero, zero)))
        sum_start(f"back_projected{half}", joined(found))
    bo_copy = pltpu.make_async_copy(bo4, bo_hbm, local_sem.at[2])
    bo_copy.start()

    def write_norm(at, pattern):
        at = at // 128
        both = pattern[0:1, :] + pattern[2:3, :]
        for k in range(both.shape[1] // 128):
            np_full[at + k : at + k + 1, :] = both[:, k * 128 : k * 128 + 128]

    sum_turn("back_projected0")
    sum_turn("back_projected1")
    reduce_owner(5)

    for half, lanes in enumerate(halves3):
        bias_sum, gain_sum = both_sums(f"back_projected{half}")
        write_norm(2304 + 512 * half, gain_sum)
        write_norm(3328 + 512 * half, bias_sum)
        by_value, constant = back_terms(*norm3[half][0:3], bias_sum, gain_sum, pixels)
        for k, block in enumerate(blocks3[half]):
            m3, v3, k3 = (
                item[:, k * 256 : k * 256 + 256] for item in (norm3[half][2], by_value, constant)
            )

            def make_dproj(row, carry):
                rows = pl.ds(row, CHUNK)
                values = grouped(up[rows, block]) * m3 + grouped(proj[rows, block]) * v3 + k3
                dproj[rows, block] = flat(values).astype(BF16)
                return carry

            over_rows(make_dproj, 0)
        part_mixed = dot_t(dproj[:, lanes], last[:, lanes])
        d_mixed[...] = part_mixed if half == 0 else d_mixed[...] + part_mixed

    def attend(row, carry):
        rows = pl.ds(row, CHUNK)
        values = grouped(d_mixed[rows, :])
        return (
            carry[0] + jnp.sum(values * grouped(splits[rows, 0:256]), axis=0),
            carry[1] + jnp.sum(values * grouped(splits[rows, 256:512]), axis=0),
        )

    d_att0, d_att1 = over_rows(attend, (zero, zero))
    d_att0, d_att1 = image_sum(d_att0), image_sum(d_att1)
    both = att0 * d_att0 + att1 * d_att1
    d_logits = jnp.concatenate([att0 * (d_att0 - both), att1 * (d_att1 - both)], axis=1)
    d_hidden = exact_dot(d_logits, expand, True)
    d_pool = d_hidden * slope_p
    per_micro = stack_sums(pair_sum(d_pool), pair_sum(d_pool * normed_p))
    sum_start("back_pool", per_micro)
    ex_sum = pair_sum(d_logits)
    ex_sum = ex_sum + pltpu.roll(ex_sum, 2, 0)
    ex_rows_sum = ex_sum[:, 0:128]
    for k in range(1, 4):
        ex_rows_sum = jnp.where(row_ids(128) == k, ex_sum[:, k * 128 : k * 128 + 128], ex_rows_sum)

    grad_ex = image_dot(hidden, d_logits)
    grad_ex = grad_ex.reshape(n_dp, ex_rows, 512)
    ge[:, 0:ex_rows, 128:384] = grad_ex[:, :, 0:256]
    ge[:, ex_rows : 2 * ex_rows, 128:384] = grad_ex[:, :, 256:512]
    ge[:, :, 384:512] = jnp.zeros((n_dp, 2 * ex_rows, 128), F32)
    g3[...] = tdot(mixed[...], dproj[...]).reshape(g3.shape)
    reduce_core(3)
    held = []
    for group, att in ((0, att0), (1, att1)):
        lanes = halves2[group]
        c2, s2, m2, a2 = norm2[group]

        def make_dn2(row, carry):
            rows = pl.ds(row, CHUNK)
            values = grouped(wid[rows, lanes])
            turned = values * m2 + a2
            gate = sigmoid(turned)
            slope = gate * (1.0 + turned * (1.0 - gate))
            down = grouped(d_mixed[rows, :]) * att * slope
            dn2[rows, lanes] = flat(down)
            splits[rows, lanes] = flat(slope)
            normed = (values - c2) * s2
            terms = (down, down * normed, slope, slope * normed)
            return tuple(item + jnp.sum(term, axis=0) for item, term in zip(carry, terms))

        held.append([image_sum(item) for item in over_rows(make_dn2, (zero,) * 4)])
    pool_bias_sum, pool_gain_sum = unstack_sums(sum_end("back_pool"))
    write_norm(1536, pool_gain_sum)
    write_norm(1664, pool_bias_sum)
    d_pre_pool = mul_p * (
        d_pool - pool_bias_sum * (1.0 / pictures) - normed_p * (pool_gain_sum * (1.0 / pictures))
    )
    d_pooled = exact_dot(d_pre_pool, squeeze, True) * (1.0 / (SIDE * SIDE))
    for group in range(2):
        down, down_normed, slope, slope_normed = held[group]
        payload = fold_lanes(
            stack_sums(
                pair_sum(down + d_pooled * slope), pair_sum(down_normed + d_pooled * slope_normed)
            )
        )
        if group == 1:
            payload = jnp.concatenate([payload, ex_rows_sum], axis=0)
        sum_start(f"back_widened{group}", payload)
    ge[:, :, 0:128] = image_dot(pooled, d_pre_pool).reshape(n_dp, 2 * ex_rows, 128)
    reduce_core(4)
    sum_turn("back_widened0")
    sum_turn("back_widened1")
    reduce_y(3)
    reduce_y(4)
    back_total = owner_total(5)
    back_own[0] = back_total[0 : BOTTLE // 4]
    back_own[1] = back_total[BOTTLE // 4 :]

    small_zero = jnp.zeros((8, 128), F32)
    for group, lanes in enumerate(halves2):
        whole = sum_end(f"back_widened{group}")
        if group == 1:
            np_full[14:18, :] = whole[8:12]
        bias_sum, gain_sum = unstack_sums(unfold_lanes(whole[0:8]))
        write_norm(512 + 256 * group, gain_sum)
        write_norm(1024 + 256 * group, bias_sum)
        m2 = norm2[group][2]
        v2, k2 = back_terms(*norm2[group][0:3], bias_sum, gain_sum, pixels)
        pooled_m2 = d_pooled * m2

        def make_dwid(row, carry):
            rows = pl.ds(row, CHUNK)
            values = grouped(dn2[rows, lanes]) * m2 + grouped(splits[rows, lanes]) * pooled_m2
            values = values + grouped(wid[rows, lanes]) * v2 + k2
            dwid[rows, lanes] = flat(values).astype(BF16)
            return carry

        over_rows(make_dwid, 0)
        gc[group * own_half : (group + 1) * own_half] = tdot(
            columns[group], dwid[:, lanes]
        ).reshape(own_half, 2, 9 * 128 // own_half // 2, BOTTLE)
    reduce_core(1)
    reduce_core(2)
    for group, lanes in enumerate(halves2):
        dcol[PAD : PAD + ROWS, group * 1152 : group * 1152 + 1152] = dot_t(
            dwid[:, lanes], filters(group)
        )
        inner = slice(group * 128, group * 128 + 128)

        def gather_taps(row, carry):
            for side in range(3):
                total = None
                for down in range(3):
                    at = group * 1152 + (3 * down + side) * 128
                    values = dcol[pl.ds(PAD + row - 56 * (down - 1), CHUNK), at : at + 128]
                    total = values if total is None else total + values
                act[side, pl.ds(PAD + row, CHUNK), inner] = total
            return carry

        over_rows(gather_taps, 0)
        c1, s1, m1, a1 = (item[:, inner] for item in (center1, scale1, mul1, add1))
        not_first1, not_last1 = not_first[:, inner], not_last[:, inner]

        def make_dn1(row, carry):
            rows = pl.ds(row, CHUNK)
            d_active = act[1, pl.ds(PAD + row, CHUNK), inner]
            d_active = d_active + jnp.where(not_first1, beside(2, row, -4, inner), 0.0)
            d_active = d_active + jnp.where(not_last1, beside(0, row, 4, inner), 0.0)
            values = grouped(red[rows, inner])
            turned = values * m1 + a1
            gate = sigmoid(turned)
            slope = gate * (1.0 + turned * (1.0 - gate))
            down = grouped(d_active) * slope
            dn1[rows, inner] = flat(down)
            mixed[rows, inner] = flat(down * m1).astype(BF16)
            normed = (values - c1) * s1
            return carry[0] + jnp.sum(down, axis=0), carry[1] + jnp.sum(down * normed, axis=0)

        bias_sum, gain_sum = over_rows(make_dn1, (small_zero, small_zero))
        sum_start(f"back_reduced{group}", stack_sums(micro_sum(bias_sum), micro_sum(gain_sum)))
        if group == 0:
            reduce_owner(3)
            reduce_owner(4)
            reduce_y(1)
    reduce_y(2)
    sum_turn("back_reduced0")
    sum_turn("back_reduced1")
    g1[...] = tdot(mixed[...], x_v[...]).reshape(g1.shape)
    reduce_core(0)
    found = [unstack_sums(sum_end(f"back_reduced{group}")) for group in range(2)]
    bias_sum, gain_sum = (jnp.concatenate(item, axis=1) for item in zip(*found))
    write_norm(0, gain_sum)
    write_norm(256, bias_sum)
    by_value, constant = back_terms(center1, scale1, mul1, bias_sum, gain_sum, pixels)
    def make_dred(row, carry):
        rows = pl.ds(row, CHUNK)
        values = grouped(dn1[rows, :]) * mul1 + grouped(red[rows, :]) * by_value + constant
        dred[rows, :] = flat(values).astype(BF16)
        return carry

    over_rows(make_dred, 0)
    reduce_owner(1)
    proj[...] = dot_t(dred[...], fw1[...].reshape(CHANNELS, BOTTLE))
    reduce_y(0)

    by_bias = mul1 * bias_sum * (1.0 / pixels)
    by_gain = mul1 * gain_sum * (1.0 / pixels)
    image_sums = sum_end("images")
    ids = lax.broadcasted_iota(jnp.int32, (16, 128), 0)
    own_sums = [
        jnp.sum(jnp.where(ids == m * n_dp + dp, image_sums, 0.0), axis=0, keepdims=True)
        for m in range(2)
    ]
    ids = row_ids(128)
    fix[0] = row_dot(by_bias, jnp.where(ids == 0, own_sums[0], jnp.where(ids == 2, own_sums[1], 0.0)))
    for m in range(2):
        fix[1 + m] = row_dot(by_gain, jnp.where(ids == 2 * m, 1.0, 0.0))
    reduce_spread(3)
    reduce_spread(4)

    def make_dx(row, carry):
        for start in range(0, CHANNELS, 256):
            lanes = slice(start, start + 256)
            values = up[pl.ds(row, CHUNK), lanes] + proj[pl.ds(row, CHUNK), lanes]
            dx4[pl.ds(row // 4, CHUNK // 4), :, lanes] = values.reshape(CHUNK // 4, 4, 256)
        return carry

    over_rows(make_dx, 0)
    dx_copy = pltpu.make_async_copy(dx4, dx_hbm, local_sem.at[3])
    dx_copy.start()
    norm_rows = np_full[0:8, :]
    for d in range(1, n_dp):
        at = shard * d // 128
        norm_rows = jnp.where(dp == d, np_full[at : at + 8, :], norm_rows)
    norm_rows = pltpu.roll(norm_rows, lax.rem(128 - turn, 128), 1)
    gn_out[...] = jnp.where(lanes_id < 128 - turn, norm_rows, pltpu.roll(norm_rows, 7, 0))
    reduce_owner(2)
    reduce_owner(0)
    reduce_spread(1)
    reduce_spread(2)
    reduce_spread(0)
    out_copies = [
        pltpu.make_async_copy(source, target, local_sem.at[10 + k])
        for k, (source, target) in enumerate(
            (
                (gn_out, gn_hbm),
                (fs[2], f3_hbm),
                (fs[3], fe_hbm),
                (fs[1], fc_hbm),
                (fs[0], f1_hbm),
            )
        )
    ]
    out_copies[0].start()
    for which in (3, 4, 1, 2, 0):
        reduce_end(which)
        if which != 1:
            out_copies[{3: 1, 4: 2, 2: 3, 0: 4}[which]].start()

    bo_copy.wait()
    dx_copy.wait()
    for copy in out_copies:
        copy.wait()
    for k in STATS:
        if k in DIRECT:
            wait_bytes(ar_slots_a[k].at[pl.ds(0, everyone - 1)], ar_send_a.at[order[k]])
        else:
            wait_bytes(ar_slots_a[k].at[pl.ds(0, plane_size - 1)], ar_send_a.at[order[k]])
            wait_bytes(ar_slots_b[k].at[pl.ds(0, planes - 1)], ar_send_b.at[order[k]])
    wait_bytes(np_slots.at[pl.ds(0, n_dp - 1)], np_sems.at[0])
    for which in range(3):
        wait_bytes(seven(which), ws.at[which, 0])
        for stage in range(1, 4):
            wait_bytes(quarters[which](core, half_y), ws.at[which, stage])
    for which in range(6):
        wait_bytes(r1s[which], gs.at[which, 0])
        wait_bytes(r2s[which], gs.at[which, 1])
        wait_bytes(r3s[which].at[pl.ds(0, n_dp - 1)], gs.at[which, 2])
        if which < 5:
            wait_bytes(three_parts(which), gs.at[which, 3])


def update_kernel(*refs):
    sources, targets = refs[0:25], refs[25:45]
    inputs, outs, through = refs[45:68], refs[68:86], refs[86:88]
    pass_sems, in_sems, out_sems = refs[88:91]
    part = SIDE * SIDE // 4
    fetching, passing = [], []
    for k in range(4):
        rows = pl.ds(k * part, part)
        for which in range(2):
            fetching.append(
                pltpu.make_async_copy(
                    sources[which].at[rows], through[which].at[rows], pass_sems.at[0, which, k]
                )
            )
            passing.append(
                pltpu.make_async_copy(
                    through[which].at[rows], targets[which].at[rows], pass_sems.at[1, which, k]
                )
            )
    for copy in fetching:
        copy.start()
    coming = [
        pltpu.make_async_copy(source, held, in_sems.at[k])
        for k, (source, held) in enumerate(zip(sources[2:], inputs))
    ]
    for copy in coming:
        copy.start()
    grads, states = inputs[0:5], inputs[5:23]
    going = [
        pltpu.make_async_copy(held, target, out_sems.at[k])
        for k, (held, target) in enumerate(zip(outs, targets[2:]))
    ]
    ex_rows = states[9].shape[0]
    shard = states[15].shape[0]
    fans = (CHANNELS, 9 * BOTTLE // RADIX, BOTTLE, INNER // 8, BOTTLE)
    for copy in coming[0:5]:
        copy.wait()
    found = (
        grads[0][...].T,
        grads[1][...],
        grads[3][:, 0:128],
        jnp.concatenate([grads[3][0:ex_rows, 128:384], grads[3][ex_rows:, 128:384]], axis=1),
        grads[2][...],
    )
    for order, k in enumerate((3, 2, 4, 0, 1)):
        for copy in coming[5 + 3 * k : 8 + 3 * k]:
            copy.wait()
        new = adamw(
            states[3 * k][...],
            states[3 * k + 1][...],
            states[3 * k + 2][...],
            found[k],
            2.0 * fans[k] ** (-0.5),
            DECAY,
        )
        for j in range(3):
            outs[3 * k + j][...] = new[j]
            going[3 * k + j].start()
        for copy in range(2 * order, min(2 * order + 2, 8)):
            fetching[copy].wait()
            passing[copy].start()
    for copy in coming[20:23]:
        copy.wait()
    for at in range(0, shard, 128):
        width = min(128, shard - at)
        lanes = pl.ds(at, width)
        new = adamw(
            *[states[15 + j][lanes].reshape(1, width) for j in range(3)],
            grads[4][at // 128 : at // 128 + 1, 0:width],
            NORM_RATE,
            0.0,
        )
        for j in range(3):
            outs[15 + j][lanes] = new[j].reshape(width)
    for copy in going[15:18]:
        copy.start()
    for copy in passing + going:
        copy.wait()


def fused_device(
    images,
    out_grad,
    reduce_weight,
    reduce_moment,
    reduce_second,
    conv_weight,
    conv_moment,
    conv_second,
    squeeze_weight,
    squeeze_moment,
    squeeze_second,
    expand_weight,
    expand_moment,
    expand_second,
    project_weight,
    project_moment,
    project_second,
    norm_params,
    norm_moment,
    norm_second,
):
    n_dp, n_rep = lax.axis_size("dp"), lax.axis_size("rep")
    by_pixel = lambda values: jnp.transpose(values, (1, 2, 0, 3)).reshape(-1, 4, CHANNELS)
    qc = conv_weight.shape[0] // 2
    q1 = reduce_weight.shape[0] // 4
    pe = squeeze_weight.shape[0]
    vmem = pltpu.VMEM
    pixel_form = (SIDE * SIDE, 4, CHANNELS)
    scratch = [
        *[
            vmem(values.shape, F32)
            for values in (
                reduce_weight,
                conv_weight,
                squeeze_weight,
                expand_weight,
                project_weight,
                norm_params,
            )
        ],
        vmem((8, 128), F32),
        vmem(pixel_form, BF16),
        vmem(pixel_form, BF16),
        vmem((ROWS, CHANNELS), BF16),
        vmem((ROWS, CHANNELS), BF16),
        vmem((n_dp, 2, 2, q1, BOTTLE), BF16),
        vmem((n_dp, 2, qc, BOTTLE), BF16),
        vmem((n_dp, pe, 1536), BF16),
        vmem((pe, 1536), BF16),
        vmem((n_dp, 8, 128), F32),
        vmem((40, 128), F32),
        vmem((ROWS, BOTTLE), F32),
        vmem((3, ROWS + 2 * PAD, BOTTLE), F32),
        vmem((2, ROWS, 9 * 128), BF16),
        vmem((ROWS, 512), F32),
        vmem((ROWS, 512), F32),
        vmem((ROWS, BOTTLE), BF16),
        vmem((ROWS, CHANNELS), F32),
        vmem((ROWS, CHANNELS), F32),
        vmem(pixel_form, BF16),
        vmem(pixel_form, F32),
        vmem((ROWS, CHANNELS), BF16),
        vmem((ROWS, BOTTLE), F32),
        vmem((ROWS, 512), F32),
        vmem((ROWS, 512), BF16),
        vmem((ROWS + 2 * PAD, 2 * 9 * 128), F32),
        vmem((ROWS, BOTTLE), F32),
        vmem((ROWS, BOTTLE), BF16),
        vmem((2, 2, BOTTLE // 4, CHANNELS), F32),
        vmem((n_dp, 2, qc, BOTTLE), F32),
        vmem((n_dp, pe, CHANNELS), F32),
        vmem((n_dp, pe, 512), F32),
        vmem((2, 2, BOTTLE // 2, CHANNELS), BF16),
        vmem((3, BOTTLE, CHANNELS // n_dp), F32),
        vmem((2, BOTTLE // 4, CHANNELS // n_dp), F32),
    ]
    direct = n_dp * n_rep
    scratch += [
        vmem((direct if k in DIRECT else 2 * n_rep,) + shape, F32) for k, shape in STATS.items()
    ]
    scratch += [vmem((n_dp // 2,) + shape, F32) for shape in STATS.values()]
    cut = 64
    lanes1 = CHANNELS // n_dp
    half = [
        (2, BOTTLE // 4, CHANNELS),
        (n_dp, 2, cut, 128),
        (n_dp, 2, qc - cut, 128),
        (n_dp, pe, 512),
        (n_dp, pe, 256),
        (2, BOTTLE // 2, CHANNELS),
    ]
    quarter = [
        (BOTTLE // 4, CHANNELS),
        (n_dp, cut, 128),
        (n_dp, qc - cut, 128),
        (n_dp, pe, 256),
        (n_dp, pe, 128),
        (BOTTLE // 2, CHANNELS),
    ]
    final = [(2, 2, BOTTLE // 4, lanes1), (2, qc, BOTTLE), (pe, CHANNELS), (pe, 512)]
    sent = [BF16, BF16, BF16, BF16, F32, BF16]
    scratch += [vmem(shape, F32) for shape in half[:-1]] + [vmem(half[-1], BF16)]
    scratch += [vmem(shape, kind) for shape, kind in zip(quarter, sent)] * 3
    owned = [(BOTTLE // 4, lanes1)] + [shape[1:] for shape in quarter[1:-1]]
    owned += [(BOTTLE // 2, lanes1)]
    scratch += [vmem((n_dp,) + shape, kind) for shape, kind in zip(owned, sent)]
    scratch += [vmem(shape, F32) for shape in owned]
    scratch += [vmem(shape, F32) for shape in final]
    dma = pltpu.SemaphoreType.DMA
    scratch += [dma((15,))] + [dma((len(STATS),))] * 4 + [dma((2,))] + [dma((3, 4))] * 2 + [dma((6, 4))] * 2
    any_space = pl.BlockSpec(memory_space=pl.ANY)
    block_out, images_grad, sum1, sumc, sum3, sume, norm_grads = pl.pallas_call(
        functools.partial(block_kernel, n_dp, n_rep),
        out_shape=[
            jax.ShapeDtypeStruct(pixel_form, BF16),
            jax.ShapeDtypeStruct(pixel_form, F32),
            *[jax.ShapeDtypeStruct(shape, F32) for shape in final],
            jax.ShapeDtypeStruct((8, 128), F32),
        ],
        in_specs=[any_space] * 8,
        out_specs=[any_space] * 7,
        scratch_shapes=scratch,
        compiler_params=pltpu.CompilerParams(
            collective_id=0, has_side_effects=True, vmem_limit_bytes=63 * 1024 * 1024
        ),
    )(
        by_pixel(images),
        by_pixel(out_grad),
        reduce_weight,
        conv_weight,
        squeeze_weight,
        expand_weight,
        project_weight,
        norm_params,
    )
    states = (
        reduce_weight,
        reduce_moment,
        reduce_second,
        conv_weight,
        conv_moment,
        conv_second,
        squeeze_weight,
        squeeze_moment,
        squeeze_second,
        expand_weight,
        expand_moment,
        expand_second,
        project_weight,
        project_moment,
        project_second,
    )
    held = (*states, norm_params, norm_moment, norm_second)
    sums = (
        sum1.reshape(BOTTLE, lanes1),
        sumc.reshape(conv_weight.shape),
        sum3,
        sume,
        norm_grads,
    )
    block_out, images_grad, *updated = pl.pallas_call(
        update_kernel,
        out_shape=[
            jax.ShapeDtypeStruct(pixel_form, BF16),
            jax.ShapeDtypeStruct(pixel_form, F32),
            *[jax.ShapeDtypeStruct(state.shape, F32) for state in held],
        ],
        in_specs=[any_space] * 25,
        out_specs=[any_space] * 20,
        scratch_shapes=[vmem(values.shape, F32) for values in (*sums, *held, *held)]
        + [vmem(pixel_form, BF16), vmem(pixel_form, F32)]
        + [dma((2, 2, 4)), dma((23,)), dma((18,))],
        compiler_params=pltpu.CompilerParams(vmem_limit_bytes=63 * 1024 * 1024),
    )(block_out, images_grad, *sums, *held)
    by_image = lambda values: jnp.transpose(
        values.reshape(SIDE, SIDE, images.shape[0], CHANNELS), (2, 0, 1, 3)
    )
    return (
        by_image(block_out),
        by_image(images_grad),
        *updated,
    )


def solution(mesh):
    placed = (
        P(("dp", "rep"), None, None, None),
        P(("dp", "rep"), None, None, None),
        P("dp", None),
        P("dp", None),
        P("dp", None),
        P("dp", None),
        P("dp", None),
        P("dp", None),
        P("dp", None),
        P("dp", None),
        P("dp", None),
        P("dp", None),
        P("dp", None),
        P("dp", None),
        P("dp", None),
        P("dp", None),
        P("dp", None),
        P("dp"),
        P("dp"),
        P("dp"),
    )
    n_dp, n_rep = mesh.shape["dp"], mesh.shape["rep"]
    whole_tiles = n_rep == 4 and n_dp % 2 == 0 and INNER % (16 * n_dp) == 0
    return jax.shard_map(
        fused_device if whole_tiles else per_device,
        mesh=mesh,
        in_specs=placed,
        out_specs=(
            P(("dp", "rep"), None, None, None),
            P(("dp", "rep"), None, None, None),
            P("dp", None),
            P("dp", None),
            P("dp", None),
            P("dp", None),
            P("dp", None),
            P("dp", None),
            P("dp", None),
            P("dp", None),
            P("dp", None),
            P("dp", None),
            P("dp", None),
            P("dp", None),
            P("dp", None),
            P("dp", None),
            P("dp", None),
            P("dp"),
            P("dp"),
            P("dp"),
        ),
        check_vma=False,
    )
```

```python
import functools
import jax
import jax.numpy as jnp
from jax import lax
from jax.experimental import pallas as pl
from jax.experimental.pallas import tpu as pltpu
from jax.sharding import PartitionSpec as P

CHANNELS = 1024
BOTTLE = 256
INNER = 128
RADIX = 2
SIDE = 14
MICRO = 2
STEP = 10


EPSILON = 1e-05
PRECISE = lax.Precision.HIGHEST
BETA_ONE = 0.9
BETA_TWO = 0.999
ADAM_EPSILON = 1e-08
DECAY = 0.01
NORM_RATE = 0.8
ROWS = 4 * SIDE * SIDE
NORM_WIDTH = 4352


def split_params(packed):
    widths = (
        BOTTLE,
        BOTTLE,
        RADIX * BOTTLE,
        RADIX * BOTTLE,
        INNER,
        INNER,
        RADIX * BOTTLE,
        CHANNELS,
        CHANNELS,
    )
    pieces = []
    offset = 0
    for segment in widths:
        pieces.append(lax.slice_in_dim(packed, offset, offset + segment))
        offset = offset + segment
    return pieces


def silu_slope(values):
    logistic = jax.nn.sigmoid(values)
    return logistic * (1.0 + values * (1.0 - logistic))


def norm_forward(values, gain, bias, count):
    flat = values.reshape(-1, values.shape[-1])
    total, square = lax.psum((jnp.sum(flat, axis=0), jnp.sum(flat * flat, axis=0)), ("dp", "rep"))
    center = total / count
    scale = lax.rsqrt(square / count - center * center + EPSILON)
    normed = (values - center) * scale
    return (normed * gain + bias, normed, scale)


def norm_backward(upstream, normed, scale, gain, count):
    flat_up = upstream.reshape(-1, upstream.shape[-1])
    flat_norm = normed.reshape(-1, normed.shape[-1])
    bias_sum, gain_sum = lax.psum(
        (jnp.sum(flat_up, axis=0), jnp.sum(flat_up * flat_norm, axis=0)), ("dp", "rep")
    )
    downstream = gain * scale * (upstream - bias_sum / count - normed * (gain_sum / count))
    return (downstream, gain_sum, bias_sum)


def patches(active):
    padded = jnp.pad(active, ((0, 0), (1, 1), (1, 1), (0, 0), (0, 0)))
    shifted = [
        padded[:, down_step : down_step + SIDE, side_step : side_step + SIDE]
        for down_step in range(3)
        for side_step in range(3)
    ]
    return jnp.stack(shifted, axis=4)


def unpatch(columns):
    total = jnp.zeros(
        (columns.shape[0], SIDE + 2, SIDE + 2, columns.shape[3], columns.shape[5]), jnp.float32
    )
    for down_step in range(3):
        for side_step in range(3):
            piece = columns[:, :, :, :, 3 * down_step + side_step]
            total = total + jnp.pad(
                piece,
                ((0, 0), (down_step, 2 - down_step), (side_step, 2 - side_step), (0, 0), (0, 0)),
            )
    return total[:, 1 : SIDE + 1, 1 : SIDE + 1]


def adamw(param, moment, second, gradient, rate, decay):
    moment_new = BETA_ONE * moment + (1.0 - BETA_ONE) * gradient
    second_new = BETA_TWO * second + (1.0 - BETA_TWO) * gradient * gradient
    ratio = (
        moment_new
        / (1.0 - BETA_ONE**STEP)
        / (jnp.sqrt(second_new / (1.0 - BETA_TWO**STEP)) + ADAM_EPSILON)
    )
    return (param - rate * (ratio + decay * param), moment_new, second_new)


def per_device(
    images,
    out_grad,
    reduce_weight,
    reduce_moment,
    reduce_second,
    conv_weight,
    conv_moment,
    conv_second,
    squeeze_weight,
    squeeze_moment,
    squeeze_second,
    expand_weight,
    expand_moment,
    expand_second,
    project_weight,
    project_moment,
    project_second,
    norm_params,
    norm_moment,
    norm_second,
):
    bf16 = jnp.bfloat16
    low_reduce = reduce_weight.astype(bf16)
    low_conv = conv_weight.astype(bf16)
    low_squeeze = squeeze_weight.astype(bf16)
    low_expand = expand_weight.astype(bf16)
    low_project = project_weight.astype(bf16)
    low_norm = norm_params.astype(bf16)
    devices = lax.axis_size("dp") * lax.axis_size("rep")
    per_batch = images.shape[0] // MICRO
    pixel_count = float(per_batch * SIDE * SIDE * devices)
    image_count = float(per_batch * devices)
    group_in = BOTTLE // RADIX
    grad_first = jnp.zeros((CHANNELS, BOTTLE), jnp.float32)
    grad_conv = jnp.zeros((RADIX, 9 * group_in, BOTTLE), jnp.float32)
    grad_squeeze = jnp.zeros((BOTTLE, INNER), jnp.float32)
    grad_expand = jnp.zeros((INNER, RADIX * BOTTLE), jnp.float32)
    grad_last = jnp.zeros((BOTTLE, CHANNELS), jnp.float32)
    grad_norms = jnp.zeros(
        (2 * BOTTLE + 3 * RADIX * BOTTLE + 2 * INNER + 2 * CHANNELS,), jnp.float32
    )
    outputs = []
    input_grads = []
    for number in range(MICRO):
        forward_set = (
            lax.all_gather(low_reduce, "dp", axis=0, tiled=True),
            lax.all_gather(low_conv, "dp", axis=0, tiled=True),
            lax.all_gather(low_squeeze, "dp", axis=0, tiled=True),
            lax.all_gather(low_expand, "dp", axis=0, tiled=True),
            lax.all_gather(low_project, "dp", axis=0, tiled=True),
            lax.all_gather(low_norm, "dp", axis=0, tiled=True),
        )
        first, conv, squeeze, expand, last, packed = forward_set
        (
            gain_one,
            bias_one,
            gain_two,
            bias_two,
            gain_pool,
            bias_pool,
            bias_expand,
            gain_three,
            bias_three,
        ) = split_params(packed.astype(jnp.float32))
        batched = images[number * per_batch : (number + 1) * per_batch]
        cotangent = out_grad[number * per_batch : (number + 1) * per_batch]
        reduced = jnp.einsum("nhwc,cb->nhwb", batched, first, preferred_element_type=jnp.float32)
        norm_one, normed_one, scale_one = norm_forward(reduced, gain_one, bias_one, pixel_count)
        active = jax.nn.silu(norm_one).astype(bf16)
        columns = patches(active.reshape(per_batch, SIDE, SIDE, RADIX, group_in)).reshape(
            per_batch * SIDE * SIDE, RADIX, 9 * group_in
        )
        conv_grouped = conv.reshape(RADIX, 9 * group_in, BOTTLE)
        widened = jnp.einsum(
            "prk,rko->pro", columns, conv_grouped, preferred_element_type=jnp.float32
        )
        widened = widened.reshape(per_batch, SIDE, SIDE, RADIX * BOTTLE)
        norm_two, normed_two, scale_two = norm_forward(widened, gain_two, bias_two, pixel_count)
        splits = jax.nn.silu(norm_two).reshape(per_batch, SIDE, SIDE, RADIX, BOTTLE)
        pooled = jnp.sum(jnp.sum(splits, axis=3), axis=(1, 2)) / (SIDE * SIDE)
        squeeze_float = squeeze.astype(jnp.float32)
        expand_float = expand.astype(jnp.float32)
        pre_pool = jnp.dot(pooled, squeeze_float, precision=PRECISE)
        norm_pool, normed_pool, scale_pool = norm_forward(
            pre_pool, gain_pool, bias_pool, image_count
        )
        hidden = jax.nn.silu(norm_pool)
        logits = (jnp.dot(hidden, expand_float, precision=PRECISE) + bias_expand).reshape(
            per_batch, RADIX, BOTTLE
        )
        attention = jax.nn.softmax(logits, axis=1)
        mixed = jnp.sum(splits * attention[:, None, None], axis=3).astype(bf16)
        projected = jnp.einsum("nhwb,bc->nhwc", mixed, last, preferred_element_type=jnp.float32)
        norm_three, normed_three, scale_three = norm_forward(
            projected, gain_three, bias_three, pixel_count
        )
        summed = batched.astype(jnp.float32) + norm_three
        outputs.append(jax.nn.silu(summed).astype(bf16))
        backward_set = (
            lax.all_gather(low_reduce, "dp", axis=0, tiled=True),
            lax.all_gather(low_conv, "dp", axis=0, tiled=True),
            lax.all_gather(low_squeeze, "dp", axis=0, tiled=True),
            lax.all_gather(low_expand, "dp", axis=0, tiled=True),
            lax.all_gather(low_project, "dp", axis=0, tiled=True),
            lax.all_gather(low_norm, "dp", axis=0, tiled=True),
        )
        first, conv, squeeze, expand, last, packed = backward_set
        gains_back = split_params(packed.astype(jnp.float32))
        conv_grouped = conv.reshape(RADIX, 9 * group_in, BOTTLE)
        expand_float = expand.astype(jnp.float32)
        squeeze_float = squeeze.astype(jnp.float32)
        upstream = cotangent.astype(jnp.float32) * silu_slope(summed)
        d_projected, gain_three_grad, bias_three_grad = norm_backward(
            upstream, normed_three, scale_three, gains_back[7], pixel_count
        )
        d_projected_low = d_projected.astype(bf16)
        grad_last = grad_last + jnp.einsum(
            "nhwb,nhwc->bc", mixed, d_projected_low, preferred_element_type=jnp.float32
        )
        d_mixed = jnp.einsum(
            "nhwc,bc->nhwb", d_projected_low, last, preferred_element_type=jnp.float32
        )
        d_splits = d_mixed[:, :, :, None] * attention[:, None, None]
        d_attention = jnp.sum(d_mixed[:, :, :, None] * splits, axis=(1, 2))
        d_logits = attention * (
            d_attention - jnp.sum(attention * d_attention, axis=1, keepdims=True)
        )
        flat_logits = d_logits.reshape(per_batch, RADIX * BOTTLE)
        grad_expand = grad_expand + jnp.dot(hidden.T, flat_logits, precision=PRECISE)
        d_hidden = jnp.dot(flat_logits, expand_float.T, precision=PRECISE)
        d_pool_norm = d_hidden * silu_slope(norm_pool)
        pool_bias_sum, pool_gain_sum, expand_bias_sum = lax.psum(
            (
                jnp.sum(d_pool_norm, axis=0),
                jnp.sum(d_pool_norm * normed_pool, axis=0),
                jnp.sum(flat_logits, axis=0),
            ),
            ("dp", "rep"),
        )
        d_pre_pool = (
            gains_back[4]
            * scale_pool
            * (
                d_pool_norm
                - pool_bias_sum / image_count
                - normed_pool * (pool_gain_sum / image_count)
            )
        )
        grad_squeeze = grad_squeeze + jnp.dot(pooled.T, d_pre_pool, precision=PRECISE)
        d_pooled = jnp.dot(d_pre_pool, squeeze_float.T, precision=PRECISE)
        d_splits = d_splits + (d_pooled / (SIDE * SIDE))[:, None, None, None, :]
        d_norm_two = d_splits.reshape(per_batch, SIDE, SIDE, RADIX * BOTTLE) * silu_slope(norm_two)
        d_widened, gain_two_grad, bias_two_grad = norm_backward(
            d_norm_two, normed_two, scale_two, gains_back[2], pixel_count
        )
        d_widened_low = d_widened.astype(bf16).reshape(per_batch * SIDE * SIDE, RADIX, BOTTLE)
        grad_conv = grad_conv + jnp.einsum(
            "prk,pro->rko", columns, d_widened_low, preferred_element_type=jnp.float32
        )
        d_columns = jnp.einsum(
            "pro,rko->prk", d_widened_low, conv_grouped, preferred_element_type=jnp.float32
        )
        d_active = unpatch(d_columns.reshape(per_batch, SIDE, SIDE, RADIX, 9, group_in)).reshape(
            per_batch, SIDE, SIDE, BOTTLE
        )
        d_norm_one = d_active * silu_slope(norm_one)
        d_reduced, gain_one_grad, bias_one_grad = norm_backward(
            d_norm_one, normed_one, scale_one, gains_back[0], pixel_count
        )
        d_reduced_low = d_reduced.astype(bf16)
        grad_first = grad_first + jnp.einsum(
            "nhwc,nhwb->cb", batched, d_reduced_low, preferred_element_type=jnp.float32
        )
        input_grads.append(
            upstream
            + jnp.einsum("nhwb,cb->nhwc", d_reduced_low, first, preferred_element_type=jnp.float32)
        )
        grad_norms = grad_norms + jnp.concatenate(
            [
                gain_one_grad,
                bias_one_grad,
                gain_two_grad,
                bias_two_grad,
                pool_gain_sum,
                pool_bias_sum,
                expand_bias_sum,
                gain_three_grad,
                bias_three_grad,
            ]
        )
    grad_conv = grad_conv.reshape(9 * BOTTLE, BOTTLE)
    partial_value = (
        lax.psum_scatter(grad_first, "dp", scatter_dimension=0, tiled=True),
        lax.psum_scatter(grad_conv, "dp", scatter_dimension=0, tiled=True),
        lax.psum_scatter(grad_squeeze, "dp", scatter_dimension=0, tiled=True),
        lax.psum_scatter(grad_expand, "dp", scatter_dimension=0, tiled=True),
        lax.psum_scatter(grad_last, "dp", scatter_dimension=0, tiled=True),
    )
    owned = lax.psum(
        (partial_value[0], partial_value[1], partial_value[2], partial_value[3], partial_value[4]),
        "rep",
    )
    shard_length = norm_params.shape[0]
    norm_grad_owned = lax.dynamic_slice_in_dim(
        grad_norms, lax.axis_index("dp") * shard_length, shard_length
    )
    reduce_new = adamw(
        reduce_weight, reduce_moment, reduce_second, owned[0], 2.0 * CHANNELS ** (-0.5), DECAY
    )
    conv_new = adamw(
        conv_weight,
        conv_moment,
        conv_second,
        owned[1],
        2.0 * (9 * BOTTLE // RADIX) ** (-0.5),
        DECAY,
    )
    squeeze_new = adamw(
        squeeze_weight, squeeze_moment, squeeze_second, owned[2], 2.0 * BOTTLE ** (-0.5), DECAY
    )
    expand_new = adamw(
        expand_weight, expand_moment, expand_second, owned[3], 2.0 * (INNER // 8) ** (-0.5), DECAY
    )
    project_new = adamw(
        project_weight, project_moment, project_second, owned[4], 2.0 * BOTTLE ** (-0.5), DECAY
    )
    norm_new = adamw(norm_params, norm_moment, norm_second, norm_grad_owned, NORM_RATE, 0.0)
    return (
        jnp.concatenate(outputs, axis=0),
        jnp.concatenate(input_grads, axis=0),
        reduce_new[0],
        reduce_new[1],
        reduce_new[2],
        conv_new[0],
        conv_new[1],
        conv_new[2],
        squeeze_new[0],
        squeeze_new[1],
        squeeze_new[2],
        expand_new[0],
        expand_new[1],
        expand_new[2],
        project_new[0],
        project_new[1],
        project_new[2],
        norm_new[0],
        norm_new[1],
        norm_new[2],
    )


MESH = pl.DeviceIdType.MESH
PAD = 64
CHUNK = 112
F32 = jnp.float32
BF16 = jnp.bfloat16
STATS = {
    "reduced": (4, 256),
    "widened0": (4, 256),
    "widened1": (4, 256),
    "pool": (4, 128),
    "images": (16, 128),
    "projected0": (4, 512),
    "projected1": (4, 512),
    "back_projected0": (4, 512),
    "back_projected1": (4, 512),
    "back_pool": (4, 128),
    "back_widened": (8, 512),
    "back_reduced0": (4, 128),
    "back_reduced1": (4, 128),
}
DIRECT = ("reduced", "pool", "back_pool", "back_reduced0", "back_reduced1")


def sigmoid(values):
    return 0.5 * jnp.tanh(0.5 * values) + 0.5


def row_ids(width):
    return lax.broadcasted_iota(jnp.int32, (8, width), 0)


def image_sum(rows):
    return rows + pltpu.roll(rows, 4, 0)


def pair_sum(rows):
    even = row_ids(rows.shape[1]) % 2 == 0
    return rows + jnp.where(even, pltpu.roll(rows, 7, 0), pltpu.roll(rows, 1, 0))


def micro_sum(rows):
    return pair_sum(image_sum(rows))


def stack_sums(first, second):
    rows = (first[0:1], first[2:3], second[0:1], second[2:3])
    return jnp.concatenate(rows, axis=0)


def unstack_sums(stacked):
    earlier = lax.rem(row_ids(stacked.shape[1]), 4) < 2
    return tuple(jnp.where(earlier, stacked[k : k + 1], stacked[k + 1 : k + 2]) for k in (0, 2))


def norm_terms(total, square, gain, bias, count):
    center = total * (1.0 / count)
    scale = lax.rsqrt(square * (1.0 / count) - center * center + EPSILON)
    slope = scale * gain
    return center, scale, slope, bias - center * slope


def back_terms(center, scale, slope, bias_sum, gain_sum, count):
    by_value = -slope * scale * (gain_sum * (1.0 / count))
    constant = -slope * (bias_sum * (1.0 / count)) - by_value * center
    return by_value, constant


def tdot(left, right):
    return lax.dot_general(left, right, (((0,), (0,)), ((), ())), preferred_element_type=F32)


def dot_t(left, right):
    return lax.dot_general(left, right, (((1,), (1,)), ((), ())), preferred_element_type=F32)


def in_parts(values, parts):
    found = []
    for _ in range(parts):
        rounded = values.astype(BF16).astype(F32)
        found.append(rounded)
        values = values - rounded
    return found


def exact_dot(left, right, transposed):
    stacked = jnp.concatenate(in_parts(left, 3), axis=0).astype(BF16)
    wide = dot_t(stacked, right) if transposed else jnp.dot(stacked, right, preferred_element_type=F32)
    return wide[0:8] + wide[8:16] + wide[16:24]


def row_dot(left, right):
    high, low = in_parts(left, 2)
    other_high, other_low = in_parts(right, 2)
    return tdot(
        jnp.concatenate([high, high, low, low], axis=0).astype(BF16),
        jnp.concatenate([other_high, other_low, other_high, other_low], axis=0).astype(BF16),
    )


def image_dot(left, right):
    return row_dot(jnp.where(row_ids(left.shape[1]) < 4, left, 0.0), right)


def block_kernel(
    n_dp,
    n_rep,
    x_hbm,
    gy_hbm,
    w1_hbm,
    wc_hbm,
    sq_hbm,
    ex_hbm,
    w3_hbm,
    np_hbm,
    bo_hbm,
    dx_hbm,
    f1_hbm,
    fc_hbm,
    f3_hbm,
    fe_hbm,
    gn_hbm,
    w1_own,
    wc_own,
    sq_own,
    ex_own,
    w3_own,
    np_own,
    gn_out,
    x4,
    gy4,
    x_v,
    gy_v,
    fw1,
    fwc,
    fpe,
    pe_own,
    np_slots,
    np_full,
    red,
    act,
    columns,
    wid,
    splits,
    mixed,
    proj,
    up,
    bo4,
    dx4,
    dproj,
    d_mixed,
    dn2,
    dwid,
    dcol,
    dn1,
    dred,
    g1,
    gc,
    g3,
    ge,
    gb,
    fix,
    back_own,
    *rest,
):
    n_ar = len(STATS)
    order = {name: k for k, name in enumerate(STATS)}
    ar_slots_a = dict(zip(STATS, rest[0:n_ar]))
    ar_slots_b = dict(zip(STATS, rest[n_ar : 2 * n_ar]))
    rest = rest[2 * n_ar :]
    r1s, ys, r2s, ks, r3s, own = (rest[6 * i : 6 * i + 6] for i in range(6))
    fs = rest[36:40]
    rest = rest[40:]
    w1_recv, local_sem, ar_send_a, ar_recv_a, ar_send_b, ar_recv_b, np_sems, ws, wr, gs, gr = rest

    dp = lax.axis_index("dp")
    rep = lax.axis_index("rep")
    core = lax.rem(rep, 2)
    half_y = lax.div(rep, 2)
    planes = n_dp // 2
    plane_size = 2 * n_rep
    plane = lax.div(dp, 2)
    in_plane = lax.rem(dp, 2) * n_rep + rep
    sibling = (dp, half_y * 2 + (1 - core))
    across = (dp, (1 - half_y) * 2 + core)
    pixels = float(SIDE * SIDE * 2 * n_dp * n_rep)
    pictures = float(2 * n_dp * n_rep)

    x = lax.rem(dp, 2)
    if planes == 4:
        upper = lax.div(plane, 2)
        other_planes = [3 - 3 * upper, 2 - upper, 1 - plane + 4 * upper]
    else:
        other_planes = [lax.rem(plane + step, planes) for step in range(1, planes)]
    flips = ((1, 1, 1), (1, 1, 0), (1, 0, 1), (1, 0, 0), (0, 1, 1), (0, 1, 0), (0, 0, 1), (0, 0, 0))

    def of_flip(z, flip):
        there = [1 - own if turn else own for own, turn in zip((x, half_y, core), flip)]
        return (z * 2 + there[0], there[1] * 2 + there[2])

    plane_peers = [of_flip(plane, flip) for flip in flips[:-1]]
    column_peers = [of_flip(z, flips[-1]) for z in other_planes]
    owner_peers = [of_flip(z, flip) for z in other_planes for flip in (flips[3], flips[7])]
    owner_peers += [of_flip(plane, flips[3])]
    all_peers = [of_flip(z, flip) for z in other_planes for flip in flips] + plane_peers
    me, everyone = dp * n_rep + rep, n_dp * n_rep
    rep_peers = [(dp, lax.rem(rep + step, n_rep)) for step in range(1, n_rep)]

    def remote(src, dst, send_sem, recv_sem, device):
        return pltpu.make_async_remote_copy(
            src_ref=src,
            dst_ref=dst,
            send_sem=send_sem,
            recv_sem=recv_sem,
            device_id=device,
            device_id_type=MESH,
        )

    def send_all(ref, send_sem, recv_sem, peers):
        for device in peers:
            remote(ref, ref, send_sem, recv_sem, device).start()

    def wait_bytes(ref, sem):
        pltpu.make_async_copy(ref, ref, sem).wait()

    def over_rows(body, init):
        def step(index, carry):
            return body(pl.multiple_of(index * CHUNK, CHUNK), carry)

        return lax.fori_loop(0, ROWS // CHUNK, step, init)

    def grouped(values):
        return values.reshape(CHUNK // 8, 8, values.shape[-1])

    def by_four(values):
        return flat(values).reshape(CHUNK // 4, 4, values.shape[-1])

    def flat(values):
        return values.reshape(CHUNK, values.shape[-1])

    own_copies = [
        pltpu.make_async_copy(source, target, local_sem.at[4 + k])
        for k, (source, target) in enumerate(
            (
                (w1_hbm, w1_own),
                (np_hbm, np_own),
                (wc_hbm, wc_own),
                (w3_hbm, w3_own),
                (sq_hbm, sq_own),
                (ex_hbm, ex_own),
            )
        )
    ]
    for copy in own_copies:
        copy.start()
    x_copy = pltpu.make_async_copy(x_hbm, x4, local_sem.at[0])
    gy_copy = pltpu.make_async_copy(gy_hbm, gy4, local_sem.at[1])
    x_copy.start()
    barrier = pltpu.get_barrier_semaphore()
    for device in all_peers:
        pl.semaphore_signal(barrier, inc=1, device_id=device, device_id_type=MESH)

    part = core * 2 + half_y
    own_copies[0].wait()
    h1 = w1_own.shape[0] // 2
    fw1[dp, core] = w1_own[pl.ds(pl.multiple_of(core * h1, h1), h1), :].astype(BF16)
    core_lanes = pl.ds(pl.multiple_of(core * 128, 128), 128)
    pe_lanes = pl.ds(pl.multiple_of(part * 384, 128), 384)

    pl.semaphore_wait(barrier, everyone - 1)

    def quarter_wc(c, y):
        return fwc.at[:, y, :, pl.ds(pl.multiple_of(c * 128, 128), 128)]

    def quarter_pe(c, y):
        return fpe.at[:, :, pl.ds(pl.multiple_of((c * 2 + y) * 384, 128), 384)]

    quarters = (None, quarter_wc, quarter_pe)

    def piece(which, d):
        return (
            fw1.at[d, core],
            fwc.at[d, half_y, :, core_lanes],
            fpe.at[d, :, pe_lanes],
        )[which]

    def seven(which):
        return (
            fw1.at[pl.ds(0, n_dp - 1), core],
            fwc.at[pl.ds(0, n_dp - 1), half_y, :, core_lanes],
            fpe.at[pl.ds(0, n_dp - 1), :, pe_lanes],
        )[which]

    def gather_out(which):
        send_all(piece(which, dp), ws.at[which, 0], wr.at[which, 0], owner_peers)

    def first_out():
        for device in owner_peers:
            remote(piece(0, dp), piece(0, dp), ws.at[0, 0], w1_recv.at[plane], device).start()

    def of_plane(z, c):
        return fw1.at[pl.ds(2 * z, 2), c]

    near_planes = [plane] + other_planes[::-1]

    def first_turn():
        for z in near_planes:
            awaited = of_plane(z, core) if z is not plane else fw1.at[pl.ds(dp, 1), core]
            wait_bytes(awaited, w1_recv.at[z])
            mine = of_plane(z, core)
            remote(mine, mine, ws.at[0, 1], wr.at[0, 1], sibling).start()

    def first_end():
        wait_bytes(fw1.at[:, 1 - core], wr.at[0, 1])

    def gather_turn(which):
        wait_bytes(seven(which), wr.at[which, 0])
        mine = quarters[which](core, half_y)
        remote(mine, mine, ws.at[which, 1], wr.at[which, 1], across).start()
        remote(mine, mine, ws.at[which, 2], wr.at[which, 2], sibling).start()

    def gather_hand(which):
        theirs = quarters[which](core, 1 - half_y)
        wait_bytes(theirs, wr.at[which, 1])
        remote(theirs, theirs, ws.at[which, 3], wr.at[which, 3], sibling).start()

    def gather_end(which):
        wait_bytes(quarters[which](1 - core, half_y), wr.at[which, 2])
        wait_bytes(quarters[which](1 - core, 1 - half_y), wr.at[which, 3])

    def to_rows(source, target):
        def body(index, carry):
            values = source[pl.ds(index * (CHUNK // 4), CHUNK // 4)].astype(F32)
            row = pl.multiple_of(index * CHUNK, CHUNK)
            target[pl.ds(row, CHUNK), :] = values.reshape(CHUNK, CHANNELS).astype(BF16)
            return carry

        lax.fori_loop(0, ROWS // CHUNK, body, 0)

    first_out()

    own_copies[1].wait()
    shard = np_own.shape[0]
    lanes_id = lax.broadcasted_iota(jnp.int32, (8, 128), 1)
    turn = lax.rem(shard * dp, 128)
    np_rows = []
    for at in range(0, shard, 128):
        width = min(128, shard - at)
        piece_row = np_own[pl.ds(at, width)].reshape(1, width)
        if width < 128:
            piece_row = jnp.concatenate([piece_row, jnp.zeros((1, 128 - width), F32)], axis=1)
        np_rows.append(piece_row)
    np_rows.append(jnp.zeros((8 - len(np_rows), 128), F32))
    np_turned = jnp.concatenate(np_rows, axis=0).astype(BF16).astype(F32)
    np_turned = pltpu.roll(np_turned, turn, 1)
    np_slots[dp] = jnp.where(lanes_id < turn, pltpu.roll(np_turned, 1, 0), np_turned)
    send_all(np_slots.at[dp], np_sems.at[0], np_sems.at[1], owner_peers)
    own_copies[2].wait()
    qc = wc_own.shape[0] // 2
    fwc[dp, half_y, :, core_lanes] = wc_own[
        pl.ds(pl.multiple_of(half_y * qc, qc), qc), core_lanes
    ].astype(BF16)
    for copy in own_copies[3:]:
        copy.wait()
    ex_rows = ex_own.shape[0]
    pe_own[:, 0:CHANNELS] = w3_own[...].astype(BF16)
    pe_own[:, 1024:1152] = sq_own[...].astype(BF16)
    pe_own[0:ex_rows, 1152:1408] = ex_own[:, 0:256].astype(BF16)
    pe_own[ex_rows : 2 * ex_rows, 1152:1408] = ex_own[:, 256:512].astype(BF16)
    pe_own[:, 1408:1536] = jnp.zeros((2 * ex_rows, 128), BF16)
    fpe[dp, :, pe_lanes] = pe_own[:, pe_lanes]
    gy_copy.start()
    x_copy.wait()
    to_rows(x4, x_v)
    gather_out(1)
    first_turn()
    zero_rows = jnp.zeros((PAD, BOTTLE), F32)
    for side in range(3):
        act[side, 0:PAD, :] = zero_rows
        act[side, PAD + ROWS : 2 * PAD + ROWS, :] = zero_rows
    for lane_block in range(9):
        dcol[0:PAD, lane_block * 256 : lane_block * 256 + 256] = zero_rows
        dcol[PAD + ROWS : 2 * PAD + ROWS, lane_block * 256 : lane_block * 256 + 256] = zero_rows

    def sum_start(k, payload):
        if k in DIRECT:
            ar_slots_a[k][me] = payload
            send_all(ar_slots_a[k].at[me], ar_send_a.at[order[k]], ar_recv_a.at[order[k]], all_peers)
        else:
            ar_slots_a[k][in_plane] = payload
            send_all(ar_slots_a[k].at[in_plane], ar_send_a.at[order[k]], ar_recv_a.at[order[k]], plane_peers)

    def sum_slots(slots, count):
        sums = [slots[slot] for slot in range(count)]
        while len(sums) > 1:
            sums = [sums[i] + sums[i + 1] for i in range(0, len(sums), 2)]
        return sums[0]

    def sum_turn(k):
        if k in DIRECT:
            return
        wait_bytes(ar_slots_a[k].at[pl.ds(0, plane_size - 1)], ar_recv_a.at[order[k]])
        ar_slots_b[k][plane] = sum_slots(ar_slots_a[k], plane_size)
        send_all(ar_slots_b[k].at[plane], ar_send_b.at[order[k]], ar_recv_b.at[order[k]], column_peers)

    def sum_end(k):
        if k in DIRECT:
            wait_bytes(ar_slots_a[k].at[pl.ds(0, everyone - 1)], ar_recv_a.at[order[k]])
            return sum_slots(ar_slots_a[k], everyone)
        wait_bytes(ar_slots_b[k].at[pl.ds(0, planes - 1)], ar_recv_b.at[order[k]])
        return sum_slots(ar_slots_b[k], planes)

    def lanes_of(index, width):
        return pl.ds(pl.multiple_of(index * width, 128), width)

    cut = 64
    conv_rows = {1: pl.ds(0, cut), 2: pl.ds(cut, gc.shape[2] - cut)}
    grads = (g1, gc, gc, g3, ge, gb)
    turned_kinds = (0, 5)

    def half_of(which, c):
        ref = grads[which]
        if which in turned_kinds:
            return ref.at[c]
        if which in conv_rows:
            return ref.at[:, :, conv_rows[which], lanes_of(c, 128)]
        return ref.at[:, :, lanes_of(c, (512, 256)[which - 3])]

    def y_part(which, ref, y):
        if which in turned_kinds:
            return ref.at[y]
        if which < 3:
            return ref.at[:, y]
        return ref.at[:, :, lanes_of(y, (256, 128)[which - 3])]

    def quarter_of(which, c, y):
        ref = grads[which]
        if which in turned_kinds:
            return ref.at[c, y]
        if which in conv_rows:
            return ref.at[:, y, conv_rows[which], lanes_of(c, 128)]
        return ref.at[:, :, lanes_of(c * 2 + y, (256, 128)[which - 3])]

    def final_part(which, c, y):
        if which == 0:
            return fs[0].at[c, y]
        if which in conv_rows:
            return fs[1].at[y, conv_rows[which], lanes_of(c, 128)]
        return fs[which - 1].at[:, lanes_of(c * 2 + y, (256, 128)[which - 3])]

    def of_owner(which, ref, d):
        return ref.at[:, lanes_of(d, CHANNELS // n_dp)] if which in turned_kinds else ref.at[d]

    def in_blocks(which, body):
        if which in turned_kinds:
            count = 4
            rows = grads[which].shape[2] // count
            block = lambda index: pl.ds(pl.multiple_of(index * rows, rows), rows)
        else:
            count, block = n_dp, lambda index: index

        def step(index, carry):
            body(block(index))
            return carry

        lax.fori_loop(0, count, step, 0)

    def reduce_core(which):
        remote(
            half_of(which, 1 - core), r1s[which], gs.at[which, 0], gr.at[which, 0], sibling
        ).start()

    def reduce_y(which):
        wait_bytes(r1s[which], gr.at[which, 0])
        away = quarter_of(which, core, 1 - half_y)
        mine = quarter_of(which, core, half_y)
        there = y_part(which, r1s[which], 1 - half_y)
        here = y_part(which, r1s[which], half_y)

        def add_away(at):
            ys[which][at] = (away[at].astype(F32) + there[at].astype(F32)).astype(
                ys[which].dtype
            )

        in_blocks(which, add_away)
        remote(ys[which], r2s[which], gs.at[which, 1], gr.at[which, 1], across).start()

        def add_mine(at):
            mine[at] = (mine[at].astype(F32) + here[at].astype(F32)).astype(mine.dtype)

        in_blocks(which, add_mine)

    def reduce_owner(which):
        wait_bytes(r2s[which], gr.at[which, 1])
        mine = quarter_of(which, core, half_y)

        def add(at):
            ks[which][at] = (mine[at].astype(F32) + r2s[which][at].astype(F32)).astype(
                ks[which].dtype
            )

        in_blocks(which, add)
        for device in owner_peers:
            remote(
                of_owner(which, ks[which], device[0]),
                r3s[which].at[dp],
                gs.at[which, 2],
                gr.at[which, 2],
                device,
            ).start()
        own[which][...] = of_owner(which, mine, dp)[...].astype(F32) + of_owner(
            which, r2s[which], dp
        )[...].astype(F32)
        r3s[which][dp] = jnp.zeros(own[which].shape, r3s[which].dtype)

    def owner_total(which):
        wait_bytes(r3s[which].at[pl.ds(0, n_dp - 1)], gr.at[which, 2])
        total = own[which][...]
        for slot in range(n_dp):
            total = total + r3s[which][slot].astype(F32)
        return total

    def reduce_spread(which):
        total = owner_total(which)
        if which == 0:
            rows = pl.ds(pl.multiple_of(part * (BOTTLE // 4), BOTTLE // 4), BOTTLE // 4)
            total = total - fix[0, rows, :]
            for m in range(2):
                total = total - fix[1 + m, rows, :] * back_own[m]
        mine = final_part(which, core, half_y)
        mine[...] = total
        send_all(mine, gs.at[which, 3], gr.at[which, 3], rep_peers)

    def three_parts(which):
        if which == 0:
            return r1s[0].at[0, :, pl.ds(0, 3 * CHANNELS // n_dp)]
        return r1s[which].at[pl.ds(0, 3), 0] if which < 3 else y_part(which, r1s[which], 0).at[pl.ds(0, 3)]

    def reduce_end(which):
        wait_bytes(three_parts(which), gr.at[which, 3])

    first_end()
    red[...] = jnp.dot(x_v[...], fw1[...].reshape(CHANNELS, BOTTLE), preferred_element_type=F32)

    def sums_of(ref, start, width):
        def body(row, carry):
            values = grouped(ref[pl.ds(row, CHUNK), start : start + width])
            return carry[0] + jnp.sum(values, axis=0), carry[1] + jnp.sum(values * values, axis=0)

        zero = jnp.zeros((8, width), F32)
        return over_rows(body, (zero, zero))

    def joined(found):
        both = [jnp.concatenate(item, axis=1) for item in zip(*found)]
        return stack_sums(micro_sum(both[0]), micro_sum(both[1]))

    def both_sums(name):
        return unstack_sums(sum_end(name))

    sum_start("reduced", joined([sums_of(red, 0, 256)]))

    gy_copy.wait()
    to_rows(gy4, gy_v)
    wait_bytes(np_slots.at[pl.ds(0, n_dp - 1)], np_sems.at[1])
    np_full[...] = jnp.zeros(np_full.shape, F32)
    for d in range(n_dp):
        at = shard * d // 128
        np_full[at : at + 8, :] = np_full[at : at + 8, :] + np_slots[d]

    def vector(at, width):
        rows = [np_full[at // 128 + k : at // 128 + k + 1, :] for k in range(width // 128)]
        return jnp.concatenate(rows, axis=1) if len(rows) > 1 else rows[0]

    gain_one, bias_one = vector(0, 256), vector(256, 256)
    gain_two, bias_two = vector(512, 512), vector(1024, 512)
    gain_pool, bias_pool = vector(1536, 128), vector(1664, 128)
    bias_expand = vector(1792, 512)
    gain_three, bias_three = vector(2304, 1024), vector(3328, 1024)

    gather_turn(1)
    gather_out(2)
    total, square = both_sums("reduced")
    center1, scale1, mul1, add1 = norm_terms(total, square, gain_one, bias_one, pixels)

    def make_active(row, carry):
        turned = grouped(red[pl.ds(row, CHUNK), :]) * mul1 + add1
        act[1, pl.ds(PAD + row, CHUNK), :] = flat(turned * sigmoid(turned))
        return carry

    over_rows(make_active, 0)
    gather_hand(1)
    place = lax.rem(lax.broadcasted_iota(jnp.int32, (CHUNK, BOTTLE), 0) // 4, SIDE)
    not_last = place != SIDE - 1
    not_first = place != 0

    def beside(side, row, distance, lanes=slice(0, BOTTLE)):
        near = act[side, pl.ds(PAD + row - 8, CHUNK + 16), lanes]
        return pltpu.roll(near, (CHUNK + 16 - distance) % (CHUNK + 16), 0)[8 : 8 + CHUNK]

    def shift_active(row, carry):
        act[2, pl.ds(PAD + row, CHUNK), :] = jnp.where(not_last, beside(1, row, 4), 0.0)
        act[0, pl.ds(PAD + row, CHUNK), :] = jnp.where(not_first, beside(1, row, -4), 0.0)
        return carry

    over_rows(shift_active, 0)

    def make_columns(row, carry):
        for tap in range(9):
            down, side = tap // 3 - 1, tap % 3
            values = act[side, pl.ds(PAD + row + 56 * down, CHUNK), :].astype(BF16)
            columns[0, pl.ds(row, CHUNK), tap * 128 : tap * 128 + 128] = values[:, 0:128]
            columns[1, pl.ds(row, CHUNK), tap * 128 : tap * 128 + 128] = values[:, 128:256]
        return carry

    over_rows(make_columns, 0)
    gather_end(1)
    own_half = n_dp // 2

    def filters(group):
        return fwc[group * own_half : (group + 1) * own_half].reshape(9 * 128, BOTTLE)

    halves2 = (slice(0, 256), slice(256, 512))
    for group, lanes in enumerate(halves2):
        wid[:, lanes] = jnp.dot(columns[group], filters(group), preferred_element_type=F32)
        sum_start(f"widened{group}", joined([sums_of(wid, group * 256, 256)]))
    gather_turn(2)
    sum_turn("widened0")
    sum_turn("widened1")
    gather_hand(2)

    norm2 = []
    pooled = jnp.zeros((8, BOTTLE), F32)
    for group, lanes in enumerate(halves2):
        total, square = both_sums(f"widened{group}")
        norm2.append(norm_terms(total, square, gain_two[:, lanes], bias_two[:, lanes], pixels))
        m2, a2 = norm2[group][2:4]

        def make_splits(row, carry):
            turned = grouped(wid[pl.ds(row, CHUNK), lanes]) * m2 + a2
            values = turned * sigmoid(turned)
            splits[pl.ds(row, CHUNK), lanes] = flat(values)
            return carry + jnp.sum(values, axis=0)

        pooled = over_rows(make_splits, pooled)
    pooled = image_sum(pooled) * (1.0 / (SIDE * SIDE))
    gather_end(2)
    last = fpe[:, :, 0:CHANNELS].reshape(BOTTLE, CHANNELS)
    squeeze = fpe[:, :, 1024:1152].reshape(BOTTLE, INNER)
    ex_both = fpe[:, :, 1152:1408]
    expand = jnp.concatenate(
        [
            ex_both[:, 0:ex_rows].reshape(INNER, 256),
            ex_both[:, ex_rows : 2 * ex_rows].reshape(INNER, 256),
        ],
        axis=1,
    )
    pre_pool = exact_dot(pooled, squeeze, False)
    sum_start("pool", stack_sums(pair_sum(pre_pool), pair_sum(pre_pool * pre_pool)))
    first_micro = lax.rem(row_ids(BOTTLE), 4) < 2

    def make_normed(row, carry):
        rows = pl.ds(row, CHUNK)
        normed = (grouped(red[rows, :]) - center1) * scale1
        dwid[rows, 0:256] = flat(jnp.where(first_micro, normed, 0.0)).astype(BF16)
        dwid[rows, 256:512] = flat(jnp.where(first_micro, 0.0, normed)).astype(BF16)
        return carry + jnp.sum(grouped(x_v[rows, :].astype(F32)), axis=0)

    image_sums = micro_sum(over_rows(make_normed, jnp.zeros((8, CHANNELS), F32)))
    sum_start(
        "images",
        jnp.concatenate(
            [
                image_sums[2 * m : 2 * m + 1, at : at + 128]
                for m in range(2)
                for at in range(0, CHANNELS, 128)
            ],
            axis=0,
        ),
    )
    normed_images = tdot(dwid[...], x_v[...]).astype(BF16)
    normed_images = normed_images.reshape(2, 2, 2, BOTTLE // 4, CHANNELS)
    for m in range(2):
        gb[:, :, m * (BOTTLE // 4) : (m + 1) * (BOTTLE // 4)] = normed_images[m]
    reduce_core(5)
    total, square = unstack_sums(sum_end("pool"))
    center_p, scale_p, mul_p, add_p = norm_terms(total, square, gain_pool, bias_pool, pictures)
    normed_p = (pre_pool - center_p) * scale_p
    norm_p = pre_pool * mul_p + add_p
    gate_p = sigmoid(norm_p)
    hidden = norm_p * gate_p
    slope_p = gate_p * (1.0 + norm_p * (1.0 - gate_p))
    logits = exact_dot(hidden, expand, False) + bias_expand
    left, right = logits[:, 0:256], logits[:, 256:512]
    most = jnp.maximum(left, right)
    left, right = jnp.exp(left - most), jnp.exp(right - most)
    att0 = left / (left + right)
    att1 = right / (left + right)

    def make_mixed(row, carry):
        rows = pl.ds(row, CHUNK)
        values = grouped(splits[rows, 0:256]) * att0 + grouped(splits[rows, 256:512]) * att1
        mixed[rows, :] = flat(values).astype(BF16)
        return carry

    over_rows(make_mixed, 0)
    halves3 = (slice(0, 512), slice(512, 1024))
    blocks3 = [[slice(512 * h + k, 512 * h + k + 256) for k in (0, 256)] for h in range(2)]
    for half, lanes in enumerate(halves3):
        proj[:, lanes] = jnp.dot(mixed[...], last[:, lanes], preferred_element_type=F32)
        sum_start(
            f"projected{half}", joined([sums_of(proj, 512 * half + k, 256) for k in (0, 256)])
        )
    sum_turn("projected0")
    sum_turn("projected1")
    sum_turn("images")
    reduce_y(5)

    norm3 = []
    zero = jnp.zeros((8, 256), F32)
    for half, lanes in enumerate(halves3):
        total, square = both_sums(f"projected{half}")
        norm3.append(norm_terms(total, square, gain_three[:, lanes], bias_three[:, lanes], pixels))
        found = []
        for k, block in enumerate(blocks3[half]):
            c3, s3, m3, a3 = (item[:, k * 256 : k * 256 + 256] for item in norm3[half])

            def make_out(row, carry):
                rows = pl.ds(row, CHUNK)
                values = grouped(proj[rows, block])
                summed = grouped(x_v[rows, block].astype(F32)) + (values * m3 + a3)
                gate = sigmoid(summed)
                bo4[pl.ds(row // 4, CHUNK // 4), :, block] = by_four(summed * gate).astype(BF16)
                upstream = grouped(gy_v[rows, block].astype(F32)) * (
                    gate * (1.0 + summed * (1.0 - gate))
                )
                up[rows, block] = flat(upstream)
                normed = (values - c3) * s3
                return carry[0] + jnp.sum(upstream, axis=0), carry[1] + jnp.sum(
                    upstream * normed, axis=0
                )

            found.append(over_rows(make_out, (zero, zero)))
        sum_start(f"back_projected{half}", joined(found))
    bo_copy = pltpu.make_async_copy(bo4, bo_hbm, local_sem.at[2])
    bo_copy.start()

    def write_norm(at, pattern):
        at = at // 128
        both = pattern[0:1, :] + pattern[2:3, :]
        for k in range(both.shape[1] // 128):
            np_full[at + k : at + k + 1, :] = both[:, k * 128 : k * 128 + 128]

    sum_turn("back_projected0")
    sum_turn("back_projected1")
    reduce_owner(5)

    for half, lanes in enumerate(halves3):
        bias_sum, gain_sum = both_sums(f"back_projected{half}")
        write_norm(2304 + 512 * half, gain_sum)
        write_norm(3328 + 512 * half, bias_sum)
        by_value, constant = back_terms(*norm3[half][0:3], bias_sum, gain_sum, pixels)
        for k, block in enumerate(blocks3[half]):
            m3, v3, k3 = (
                item[:, k * 256 : k * 256 + 256] for item in (norm3[half][2], by_value, constant)
            )

            def make_dproj(row, carry):
                rows = pl.ds(row, CHUNK)
                values = grouped(up[rows, block]) * m3 + grouped(proj[rows, block]) * v3 + k3
                dproj[rows, block] = flat(values).astype(BF16)
                return carry

            over_rows(make_dproj, 0)
        part_mixed = dot_t(dproj[:, lanes], last[:, lanes])
        d_mixed[...] = part_mixed if half == 0 else d_mixed[...] + part_mixed

    def attend(row, carry):
        rows = pl.ds(row, CHUNK)
        values = grouped(d_mixed[rows, :])
        return (
            carry[0] + jnp.sum(values * grouped(splits[rows, 0:256]), axis=0),
            carry[1] + jnp.sum(values * grouped(splits[rows, 256:512]), axis=0),
        )

    d_att0, d_att1 = over_rows(attend, (zero, zero))
    d_att0, d_att1 = image_sum(d_att0), image_sum(d_att1)
    both = att0 * d_att0 + att1 * d_att1
    d_logits = jnp.concatenate([att0 * (d_att0 - both), att1 * (d_att1 - both)], axis=1)
    d_hidden = exact_dot(d_logits, expand, True)
    d_pool = d_hidden * slope_p
    per_micro = stack_sums(pair_sum(d_pool), pair_sum(d_pool * normed_p))
    sum_start("back_pool", per_micro)
    ex_sum = pair_sum(d_logits)
    ex_sum = ex_sum + pltpu.roll(ex_sum, 2, 0)

    grad_ex = image_dot(hidden, d_logits)
    grad_ex = grad_ex.reshape(n_dp, ex_rows, 512)
    ge[:, 0:ex_rows, 128:384] = grad_ex[:, :, 0:256]
    ge[:, ex_rows : 2 * ex_rows, 128:384] = grad_ex[:, :, 256:512]
    ge[:, :, 384:512] = jnp.zeros((n_dp, 2 * ex_rows, 128), F32)
    g3[...] = tdot(mixed[...], dproj[...]).reshape(g3.shape)
    reduce_core(3)
    held = []
    for group, att in ((0, att0), (1, att1)):
        lanes = halves2[group]
        c2, s2, m2, a2 = norm2[group]

        def make_dn2(row, carry):
            rows = pl.ds(row, CHUNK)
            values = grouped(wid[rows, lanes])
            turned = values * m2 + a2
            gate = sigmoid(turned)
            slope = gate * (1.0 + turned * (1.0 - gate))
            down = grouped(d_mixed[rows, :]) * att * slope
            dn2[rows, lanes] = flat(down)
            splits[rows, lanes] = flat(slope)
            normed = (values - c2) * s2
            terms = (down, down * normed, slope, slope * normed)
            return tuple(item + jnp.sum(term, axis=0) for item, term in zip(carry, terms))

        held.append([image_sum(item) for item in over_rows(make_dn2, (zero,) * 4)])
    pool_bias_sum, pool_gain_sum = unstack_sums(sum_end("back_pool"))
    write_norm(1536, pool_gain_sum)
    write_norm(1664, pool_bias_sum)
    d_pre_pool = mul_p * (
        d_pool - pool_bias_sum * (1.0 / pictures) - normed_p * (pool_gain_sum * (1.0 / pictures))
    )
    d_pooled = exact_dot(d_pre_pool, squeeze, True) * (1.0 / (SIDE * SIDE))
    found = []
    for down, down_normed, slope, slope_normed in held:
        first, second = down + d_pooled * slope, down_normed + d_pooled * slope_normed
        found.append(stack_sums(pair_sum(first), pair_sum(second)))
    sum_start(
        "back_widened", jnp.concatenate([jnp.concatenate(found, axis=1), ex_sum[0:4]], axis=0)
    )
    ge[:, :, 0:128] = image_dot(pooled, d_pre_pool).reshape(n_dp, 2 * ex_rows, 128)
    reduce_core(4)
    sum_turn("back_widened")
    reduce_y(3)
    reduce_y(4)
    back_total = owner_total(5)
    back_own[0] = back_total[0 : BOTTLE // 4]
    back_own[1] = back_total[BOTTLE // 4 :]

    small_zero = jnp.zeros((8, 128), F32)
    for group, lanes in enumerate(halves2):
        if group == 0:
            whole = sum_end("back_widened")
            for k in range(4):
                np_full[14 + k : 15 + k, :] = whole[4:5, k * 128 : k * 128 + 128]
        bias_sum, gain_sum = unstack_sums(whole[0:4, lanes])
        write_norm(512 + 256 * group, gain_sum)
        write_norm(1024 + 256 * group, bias_sum)
        m2 = norm2[group][2]
        v2, k2 = back_terms(*norm2[group][0:3], bias_sum, gain_sum, pixels)
        pooled_m2 = d_pooled * m2

        def make_dwid(row, carry):
            rows = pl.ds(row, CHUNK)
            values = grouped(dn2[rows, lanes]) * m2 + grouped(splits[rows, lanes]) * pooled_m2
            values = values + grouped(wid[rows, lanes]) * v2 + k2
            dwid[rows, lanes] = flat(values).astype(BF16)
            return carry

        over_rows(make_dwid, 0)
        gc[group * own_half : (group + 1) * own_half] = tdot(
            columns[group], dwid[:, lanes]
        ).reshape(own_half, 2, 9 * 128 // own_half // 2, BOTTLE)
    reduce_core(1)
    reduce_core(2)
    for group, lanes in enumerate(halves2):
        dcol[PAD : PAD + ROWS, group * 1152 : group * 1152 + 1152] = dot_t(
            dwid[:, lanes], filters(group)
        )
        inner = slice(group * 128, group * 128 + 128)

        def gather_taps(row, carry):
            for side in range(3):
                total = None
                for down in range(3):
                    at = group * 1152 + (3 * down + side) * 128
                    values = dcol[pl.ds(PAD + row - 56 * (down - 1), CHUNK), at : at + 128]
                    total = values if total is None else total + values
                act[side, pl.ds(PAD + row, CHUNK), inner] = total
            return carry

        over_rows(gather_taps, 0)
        c1, s1, m1, a1 = (item[:, inner] for item in (center1, scale1, mul1, add1))
        not_first1, not_last1 = not_first[:, inner], not_last[:, inner]

        def make_dn1(row, carry):
            rows = pl.ds(row, CHUNK)
            d_active = act[1, pl.ds(PAD + row, CHUNK), inner]
            d_active = d_active + jnp.where(not_first1, beside(2, row, -4, inner), 0.0)
            d_active = d_active + jnp.where(not_last1, beside(0, row, 4, inner), 0.0)
            values = grouped(red[rows, inner])
            turned = values * m1 + a1
            gate = sigmoid(turned)
            slope = gate * (1.0 + turned * (1.0 - gate))
            down = grouped(d_active) * slope
            dn1[rows, inner] = flat(down)
            mixed[rows, inner] = flat(down * m1).astype(BF16)
            normed = (values - c1) * s1
            return carry[0] + jnp.sum(down, axis=0), carry[1] + jnp.sum(down * normed, axis=0)

        bias_sum, gain_sum = over_rows(make_dn1, (small_zero, small_zero))
        sum_start(f"back_reduced{group}", stack_sums(micro_sum(bias_sum), micro_sum(gain_sum)))
        if group == 0:
            reduce_owner(3)
            reduce_owner(4)
            reduce_y(1)
    reduce_y(2)
    sum_turn("back_reduced0")
    sum_turn("back_reduced1")
    g1[...] = tdot(mixed[...], x_v[...]).reshape(g1.shape)
    reduce_core(0)
    found = [unstack_sums(sum_end(f"back_reduced{group}")) for group in range(2)]
    bias_sum, gain_sum = (jnp.concatenate(item, axis=1) for item in zip(*found))
    write_norm(0, gain_sum)
    write_norm(256, bias_sum)
    by_value, constant = back_terms(center1, scale1, mul1, bias_sum, gain_sum, pixels)
    def make_dred(row, carry):
        rows = pl.ds(row, CHUNK)
        values = grouped(dn1[rows, :]) * mul1 + grouped(red[rows, :]) * by_value + constant
        dred[rows, :] = flat(values).astype(BF16)
        return carry

    over_rows(make_dred, 0)
    reduce_owner(1)
    proj[...] = dot_t(dred[...], fw1[...].reshape(CHANNELS, BOTTLE))
    reduce_y(0)

    by_bias = mul1 * bias_sum * (1.0 / pixels)
    by_gain = mul1 * gain_sum * (1.0 / pixels)
    image_sums = sum_end("images")
    ids = lax.broadcasted_iota(jnp.int32, (16, 128), 0)
    own_sums = [
        jnp.sum(jnp.where(ids == m * n_dp + dp, image_sums, 0.0), axis=0, keepdims=True)
        for m in range(2)
    ]
    ids = row_ids(128)
    fix[0] = row_dot(by_bias, jnp.where(ids == 0, own_sums[0], jnp.where(ids == 2, own_sums[1], 0.0)))
    for m in range(2):
        fix[1 + m] = row_dot(by_gain, jnp.where(ids == 2 * m, 1.0, 0.0))
    reduce_spread(3)
    reduce_spread(4)

    def make_dx(row, carry):
        for start in range(0, CHANNELS, 256):
            lanes = slice(start, start + 256)
            values = up[pl.ds(row, CHUNK), lanes] + proj[pl.ds(row, CHUNK), lanes]
            dx4[pl.ds(row // 4, CHUNK // 4), :, lanes] = values.reshape(CHUNK // 4, 4, 256)
        return carry

    over_rows(make_dx, 0)
    dx_copy = pltpu.make_async_copy(dx4, dx_hbm, local_sem.at[3])
    dx_copy.start()
    norm_rows = np_full[0:8, :]
    for d in range(1, n_dp):
        at = shard * d // 128
        norm_rows = jnp.where(dp == d, np_full[at : at + 8, :], norm_rows)
    norm_rows = pltpu.roll(norm_rows, lax.rem(128 - turn, 128), 1)
    gn_out[...] = jnp.where(lanes_id < 128 - turn, norm_rows, pltpu.roll(norm_rows, 7, 0))
    reduce_owner(2)
    reduce_owner(0)
    reduce_spread(1)
    reduce_spread(2)
    reduce_spread(0)
    out_copies = [
        pltpu.make_async_copy(source, target, local_sem.at[10 + k])
        for k, (source, target) in enumerate(
            (
                (gn_out, gn_hbm),
                (fs[2], f3_hbm),
                (fs[3], fe_hbm),
                (fs[1], fc_hbm),
                (fs[0], f1_hbm),
            )
        )
    ]
    out_copies[0].start()
    for which in (3, 4, 1, 2, 0):
        reduce_end(which)
        if which != 1:
            out_copies[{3: 1, 4: 2, 2: 3, 0: 4}[which]].start()

    bo_copy.wait()
    dx_copy.wait()
    for copy in out_copies:
        copy.wait()
    for k in STATS:
        if k in DIRECT:
            wait_bytes(ar_slots_a[k].at[pl.ds(0, everyone - 1)], ar_send_a.at[order[k]])
        else:
            wait_bytes(ar_slots_a[k].at[pl.ds(0, plane_size - 1)], ar_send_a.at[order[k]])
            wait_bytes(ar_slots_b[k].at[pl.ds(0, planes - 1)], ar_send_b.at[order[k]])
    wait_bytes(np_slots.at[pl.ds(0, n_dp - 1)], np_sems.at[0])
    wait_bytes(seven(0), ws.at[0, 0])
    wait_bytes(fw1.at[:, core], ws.at[0, 1])
    for which in range(1, 3):
        wait_bytes(seven(which), ws.at[which, 0])
        for stage in range(1, 4):
            wait_bytes(quarters[which](core, half_y), ws.at[which, stage])
    for which in range(6):
        wait_bytes(r1s[which], gs.at[which, 0])
        wait_bytes(r2s[which], gs.at[which, 1])
        wait_bytes(r3s[which].at[pl.ds(0, n_dp - 1)], gs.at[which, 2])
        if which < 5:
            wait_bytes(three_parts(which), gs.at[which, 3])


def update_kernel(*refs):
    sources, targets = refs[0:25], refs[25:45]
    inputs, outs, through = refs[45:68], refs[68:86], refs[86:88]
    pass_sems, in_sems, out_sems = refs[88:91]
    part = SIDE * SIDE // 4
    fetching, passing = [], []
    for k in range(4):
        rows = pl.ds(k * part, part)
        for which in range(2):
            fetching.append(
                pltpu.make_async_copy(
                    sources[which].at[rows], through[which].at[rows], pass_sems.at[0, which, k]
                )
            )
            passing.append(
                pltpu.make_async_copy(
                    through[which].at[rows], targets[which].at[rows], pass_sems.at[1, which, k]
                )
            )
    for copy in fetching:
        copy.start()
    coming = [
        pltpu.make_async_copy(source, held, in_sems.at[k])
        for k, (source, held) in enumerate(zip(sources[2:], inputs))
    ]
    for copy in coming:
        copy.start()
    grads, states = inputs[0:5], inputs[5:23]
    going = [
        pltpu.make_async_copy(held, target, out_sems.at[k])
        for k, (held, target) in enumerate(zip(outs, targets[2:]))
    ]
    ex_rows = states[9].shape[0]
    shard = states[15].shape[0]
    fans = (CHANNELS, 9 * BOTTLE // RADIX, BOTTLE, INNER // 8, BOTTLE)
    for copy in coming[0:5]:
        copy.wait()
    found = (
        grads[0][...].T,
        grads[1][...],
        grads[3][:, 0:128],
        jnp.concatenate([grads[3][0:ex_rows, 128:384], grads[3][ex_rows:, 128:384]], axis=1),
        grads[2][...],
    )
    for order, k in enumerate((3, 2, 4, 0, 1)):
        for copy in coming[5 + 3 * k : 8 + 3 * k]:
            copy.wait()
        new = adamw(
            states[3 * k][...],
            states[3 * k + 1][...],
            states[3 * k + 2][...],
            found[k],
            2.0 * fans[k] ** (-0.5),
            DECAY,
        )
        for j in range(3):
            outs[3 * k + j][...] = new[j]
            going[3 * k + j].start()
        for copy in range(2 * order, min(2 * order + 2, 8)):
            fetching[copy].wait()
            passing[copy].start()
    for copy in coming[20:23]:
        copy.wait()
    for at in range(0, shard, 128):
        width = min(128, shard - at)
        lanes = pl.ds(at, width)
        new = adamw(
            *[states[15 + j][lanes].reshape(1, width) for j in range(3)],
            grads[4][at // 128 : at // 128 + 1, 0:width],
            NORM_RATE,
            0.0,
        )
        for j in range(3):
            outs[15 + j][lanes] = new[j].reshape(width)
    for copy in going[15:18]:
        copy.start()
    for copy in passing + going:
        copy.wait()


def fused_device(
    images,
    out_grad,
    reduce_weight,
    reduce_moment,
    reduce_second,
    conv_weight,
    conv_moment,
    conv_second,
    squeeze_weight,
    squeeze_moment,
    squeeze_second,
    expand_weight,
    expand_moment,
    expand_second,
    project_weight,
    project_moment,
    project_second,
    norm_params,
    norm_moment,
    norm_second,
):
    n_dp, n_rep = lax.axis_size("dp"), lax.axis_size("rep")
    by_pixel = lambda values: jnp.transpose(values, (1, 2, 0, 3)).reshape(-1, 4, CHANNELS)
    qc = conv_weight.shape[0] // 2
    h1 = reduce_weight.shape[0] // 2
    pe = squeeze_weight.shape[0]
    vmem = pltpu.VMEM
    pixel_form = (SIDE * SIDE, 4, CHANNELS)
    scratch = [
        *[
            vmem(values.shape, F32)
            for values in (
                reduce_weight,
                conv_weight,
                squeeze_weight,
                expand_weight,
                project_weight,
                norm_params,
            )
        ],
        vmem((8, 128), F32),
        vmem(pixel_form, BF16),
        vmem(pixel_form, BF16),
        vmem((ROWS, CHANNELS), BF16),
        vmem((ROWS, CHANNELS), BF16),
        vmem((n_dp, 2, h1, BOTTLE), BF16),
        vmem((n_dp, 2, qc, BOTTLE), BF16),
        vmem((n_dp, pe, 1536), BF16),
        vmem((pe, 1536), BF16),
        vmem((n_dp, 8, 128), F32),
        vmem((40, 128), F32),
        vmem((ROWS, BOTTLE), F32),
        vmem((3, ROWS + 2 * PAD, BOTTLE), F32),
        vmem((2, ROWS, 9 * 128), BF16),
        vmem((ROWS, 512), F32),
        vmem((ROWS, 512), F32),
        vmem((ROWS, BOTTLE), BF16),
        vmem((ROWS, CHANNELS), F32),
        vmem((ROWS, CHANNELS), F32),
        vmem(pixel_form, BF16),
        vmem(pixel_form, F32),
        vmem((ROWS, CHANNELS), BF16),
        vmem((ROWS, BOTTLE), F32),
        vmem((ROWS, 512), F32),
        vmem((ROWS, 512), BF16),
        vmem((ROWS + 2 * PAD, 2 * 9 * 128), F32),
        vmem((ROWS, BOTTLE), F32),
        vmem((ROWS, BOTTLE), BF16),
        vmem((2, 2, BOTTLE // 4, CHANNELS), F32),
        vmem((n_dp, 2, qc, BOTTLE), F32),
        vmem((n_dp, pe, CHANNELS), F32),
        vmem((n_dp, pe, 512), F32),
        vmem((2, 2, BOTTLE // 2, CHANNELS), BF16),
        vmem((3, BOTTLE, CHANNELS // n_dp), F32),
        vmem((2, BOTTLE // 4, CHANNELS // n_dp), F32),
    ]
    direct = n_dp * n_rep
    scratch += [
        vmem((direct if k in DIRECT else 2 * n_rep,) + shape, F32) for k, shape in STATS.items()
    ]
    scratch += [vmem((n_dp // 2,) + shape, F32) for shape in STATS.values()]
    cut = 64
    lanes1 = CHANNELS // n_dp
    half = [
        (2, BOTTLE // 4, CHANNELS),
        (n_dp, 2, cut, 128),
        (n_dp, 2, qc - cut, 128),
        (n_dp, pe, 512),
        (n_dp, pe, 256),
        (2, BOTTLE // 2, CHANNELS),
    ]
    quarter = [
        (BOTTLE // 4, CHANNELS),
        (n_dp, cut, 128),
        (n_dp, qc - cut, 128),
        (n_dp, pe, 256),
        (n_dp, pe, 128),
        (BOTTLE // 2, CHANNELS),
    ]
    final = [(2, 2, BOTTLE // 4, lanes1), (2, qc, BOTTLE), (pe, CHANNELS), (pe, 512)]
    sent = [BF16, BF16, BF16, BF16, F32, BF16]
    scratch += [vmem(shape, F32) for shape in half[:-1]] + [vmem(half[-1], BF16)]
    scratch += [vmem(shape, kind) for shape, kind in zip(quarter, sent)] * 3
    owned = [(BOTTLE // 4, lanes1)] + [shape[1:] for shape in quarter[1:-1]]
    owned += [(BOTTLE // 2, lanes1)]
    scratch += [vmem((n_dp,) + shape, kind) for shape, kind in zip(owned, sent)]
    scratch += [vmem(shape, F32) for shape in owned]
    scratch += [vmem(shape, F32) for shape in final]
    dma = pltpu.SemaphoreType.DMA
    scratch += [dma((n_dp // 2,)), dma((15,))] + [dma((len(STATS),))] * 4 + [dma((2,))] + [dma((3, 4))] * 2 + [dma((6, 4))] * 2
    any_space = pl.BlockSpec(memory_space=pl.ANY)
    block_out, images_grad, sum1, sumc, sum3, sume, norm_grads = pl.pallas_call(
        functools.partial(block_kernel, n_dp, n_rep),
        out_shape=[
            jax.ShapeDtypeStruct(pixel_form, BF16),
            jax.ShapeDtypeStruct(pixel_form, F32),
            *[jax.ShapeDtypeStruct(shape, F32) for shape in final],
            jax.ShapeDtypeStruct((8, 128), F32),
        ],
        in_specs=[any_space] * 8,
        out_specs=[any_space] * 7,
        scratch_shapes=scratch,
        compiler_params=pltpu.CompilerParams(
            collective_id=0, has_side_effects=True, vmem_limit_bytes=63 * 1024 * 1024
        ),
    )(
        by_pixel(images),
        by_pixel(out_grad),
        reduce_weight,
        conv_weight,
        squeeze_weight,
        expand_weight,
        project_weight,
        norm_params,
    )
    states = (
        reduce_weight,
        reduce_moment,
        reduce_second,
        conv_weight,
        conv_moment,
        conv_second,
        squeeze_weight,
        squeeze_moment,
        squeeze_second,
        expand_weight,
        expand_moment,
        expand_second,
        project_weight,
        project_moment,
        project_second,
    )
    held = (*states, norm_params, norm_moment, norm_second)
    sums = (
        sum1.reshape(BOTTLE, lanes1),
        sumc.reshape(conv_weight.shape),
        sum3,
        sume,
        norm_grads,
    )
    block_out, images_grad, *updated = pl.pallas_call(
        update_kernel,
        out_shape=[
            jax.ShapeDtypeStruct(pixel_form, BF16),
            jax.ShapeDtypeStruct(pixel_form, F32),
            *[jax.ShapeDtypeStruct(state.shape, F32) for state in held],
        ],
        in_specs=[any_space] * 25,
        out_specs=[any_space] * 20,
        scratch_shapes=[vmem(values.shape, F32) for values in (*sums, *held, *held)]
        + [vmem(pixel_form, BF16), vmem(pixel_form, F32)]
        + [dma((2, 2, 4)), dma((23,)), dma((18,))],
        compiler_params=pltpu.CompilerParams(vmem_limit_bytes=63 * 1024 * 1024),
    )(block_out, images_grad, *sums, *held)
    by_image = lambda values: jnp.transpose(
        values.reshape(SIDE, SIDE, images.shape[0], CHANNELS), (2, 0, 1, 3)
    )
    return (
        by_image(block_out),
        by_image(images_grad),
        *updated,
    )


def solution(mesh):
    placed = (
        P(("dp", "rep"), None, None, None),
        P(("dp", "rep"), None, None, None),
        P("dp", None),
        P("dp", None),
        P("dp", None),
        P("dp", None),
        P("dp", None),
        P("dp", None),
        P("dp", None),
        P("dp", None),
        P("dp", None),
        P("dp", None),
        P("dp", None),
        P("dp", None),
        P("dp", None),
        P("dp", None),
        P("dp", None),
        P("dp"),
        P("dp"),
        P("dp"),
    )
    n_dp, n_rep = mesh.shape["dp"], mesh.shape["rep"]
    whole_tiles = n_rep == 4 and n_dp % 2 == 0 and INNER % (16 * n_dp) == 0
    return jax.shard_map(
        fused_device if whole_tiles else per_device,
        mesh=mesh,
        in_specs=placed,
        out_specs=(
            P(("dp", "rep"), None, None, None),
            P(("dp", "rep"), None, None, None),
            P("dp", None),
            P("dp", None),
            P("dp", None),
            P("dp", None),
            P("dp", None),
            P("dp", None),
            P("dp", None),
            P("dp", None),
            P("dp", None),
            P("dp", None),
            P("dp", None),
            P("dp", None),
            P("dp", None),
            P("dp", None),
            P("dp", None),
            P("dp"),
            P("dp"),
            P("dp"),
        ),
        check_vma=False,
    )
```

```python
import functools
import jax
import jax.numpy as jnp
from jax import lax
from jax.experimental import pallas as pl
from jax.experimental.pallas import tpu as pltpu
from jax.sharding import PartitionSpec as P

CHANNELS = 1024
BOTTLE = 256
INNER = 128
RADIX = 2
SIDE = 14
MICRO = 2
STEP = 10


EPSILON = 1e-05
PRECISE = lax.Precision.HIGHEST
BETA_ONE = 0.9
BETA_TWO = 0.999
ADAM_EPSILON = 1e-08
DECAY = 0.01
NORM_RATE = 0.8
ROWS = 4 * SIDE * SIDE
NORM_WIDTH = 4352


def split_params(packed):
    widths = (
        BOTTLE,
        BOTTLE,
        RADIX * BOTTLE,
        RADIX * BOTTLE,
        INNER,
        INNER,
        RADIX * BOTTLE,
        CHANNELS,
        CHANNELS,
    )
    pieces = []
    offset = 0
    for segment in widths:
        pieces.append(lax.slice_in_dim(packed, offset, offset + segment))
        offset = offset + segment
    return pieces


def silu_slope(values):
    logistic = jax.nn.sigmoid(values)
    return logistic * (1.0 + values * (1.0 - logistic))


def norm_forward(values, gain, bias, count):
    flat = values.reshape(-1, values.shape[-1])
    total, square = lax.psum((jnp.sum(flat, axis=0), jnp.sum(flat * flat, axis=0)), ("dp", "rep"))
    center = total / count
    scale = lax.rsqrt(square / count - center * center + EPSILON)
    normed = (values - center) * scale
    return (normed * gain + bias, normed, scale)


def norm_backward(upstream, normed, scale, gain, count):
    flat_up = upstream.reshape(-1, upstream.shape[-1])
    flat_norm = normed.reshape(-1, normed.shape[-1])
    bias_sum, gain_sum = lax.psum(
        (jnp.sum(flat_up, axis=0), jnp.sum(flat_up * flat_norm, axis=0)), ("dp", "rep")
    )
    downstream = gain * scale * (upstream - bias_sum / count - normed * (gain_sum / count))
    return (downstream, gain_sum, bias_sum)


def patches(active):
    padded = jnp.pad(active, ((0, 0), (1, 1), (1, 1), (0, 0), (0, 0)))
    shifted = [
        padded[:, down_step : down_step + SIDE, side_step : side_step + SIDE]
        for down_step in range(3)
        for side_step in range(3)
    ]
    return jnp.stack(shifted, axis=4)


def unpatch(columns):
    total = jnp.zeros(
        (columns.shape[0], SIDE + 2, SIDE + 2, columns.shape[3], columns.shape[5]), jnp.float32
    )
    for down_step in range(3):
        for side_step in range(3):
            piece = columns[:, :, :, :, 3 * down_step + side_step]
            total = total + jnp.pad(
                piece,
                ((0, 0), (down_step, 2 - down_step), (side_step, 2 - side_step), (0, 0), (0, 0)),
            )
    return total[:, 1 : SIDE + 1, 1 : SIDE + 1]


def adamw(param, moment, second, gradient, rate, decay):
    moment_new = BETA_ONE * moment + (1.0 - BETA_ONE) * gradient
    second_new = BETA_TWO * second + (1.0 - BETA_TWO) * gradient * gradient
    ratio = (
        moment_new
        / (1.0 - BETA_ONE**STEP)
        / (jnp.sqrt(second_new / (1.0 - BETA_TWO**STEP)) + ADAM_EPSILON)
    )
    return (param - rate * (ratio + decay * param), moment_new, second_new)


def per_device(
    images,
    out_grad,
    reduce_weight,
    reduce_moment,
    reduce_second,
    conv_weight,
    conv_moment,
    conv_second,
    squeeze_weight,
    squeeze_moment,
    squeeze_second,
    expand_weight,
    expand_moment,
    expand_second,
    project_weight,
    project_moment,
    project_second,
    norm_params,
    norm_moment,
    norm_second,
):
    bf16 = jnp.bfloat16
    low_reduce = reduce_weight.astype(bf16)
    low_conv = conv_weight.astype(bf16)
    low_squeeze = squeeze_weight.astype(bf16)
    low_expand = expand_weight.astype(bf16)
    low_project = project_weight.astype(bf16)
    low_norm = norm_params.astype(bf16)
    devices = lax.axis_size("dp") * lax.axis_size("rep")
    per_batch = images.shape[0] // MICRO
    pixel_count = float(per_batch * SIDE * SIDE * devices)
    image_count = float(per_batch * devices)
    group_in = BOTTLE // RADIX
    grad_first = jnp.zeros((CHANNELS, BOTTLE), jnp.float32)
    grad_conv = jnp.zeros((RADIX, 9 * group_in, BOTTLE), jnp.float32)
    grad_squeeze = jnp.zeros((BOTTLE, INNER), jnp.float32)
    grad_expand = jnp.zeros((INNER, RADIX * BOTTLE), jnp.float32)
    grad_last = jnp.zeros((BOTTLE, CHANNELS), jnp.float32)
    grad_norms = jnp.zeros(
        (2 * BOTTLE + 3 * RADIX * BOTTLE + 2 * INNER + 2 * CHANNELS,), jnp.float32
    )
    outputs = []
    input_grads = []
    for number in range(MICRO):
        forward_set = (
            lax.all_gather(low_reduce, "dp", axis=0, tiled=True),
            lax.all_gather(low_conv, "dp", axis=0, tiled=True),
            lax.all_gather(low_squeeze, "dp", axis=0, tiled=True),
            lax.all_gather(low_expand, "dp", axis=0, tiled=True),
            lax.all_gather(low_project, "dp", axis=0, tiled=True),
            lax.all_gather(low_norm, "dp", axis=0, tiled=True),
        )
        first, conv, squeeze, expand, last, packed = forward_set
        (
            gain_one,
            bias_one,
            gain_two,
            bias_two,
            gain_pool,
            bias_pool,
            bias_expand,
            gain_three,
            bias_three,
        ) = split_params(packed.astype(jnp.float32))
        batched = images[number * per_batch : (number + 1) * per_batch]
        cotangent = out_grad[number * per_batch : (number + 1) * per_batch]
        reduced = jnp.einsum("nhwc,cb->nhwb", batched, first, preferred_element_type=jnp.float32)
        norm_one, normed_one, scale_one = norm_forward(reduced, gain_one, bias_one, pixel_count)
        active = jax.nn.silu(norm_one).astype(bf16)
        columns = patches(active.reshape(per_batch, SIDE, SIDE, RADIX, group_in)).reshape(
            per_batch * SIDE * SIDE, RADIX, 9 * group_in
        )
        conv_grouped = conv.reshape(RADIX, 9 * group_in, BOTTLE)
        widened = jnp.einsum(
            "prk,rko->pro", columns, conv_grouped, preferred_element_type=jnp.float32
        )
        widened = widened.reshape(per_batch, SIDE, SIDE, RADIX * BOTTLE)
        norm_two, normed_two, scale_two = norm_forward(widened, gain_two, bias_two, pixel_count)
        splits = jax.nn.silu(norm_two).reshape(per_batch, SIDE, SIDE, RADIX, BOTTLE)
        pooled = jnp.sum(jnp.sum(splits, axis=3), axis=(1, 2)) / (SIDE * SIDE)
        squeeze_float = squeeze.astype(jnp.float32)
        expand_float = expand.astype(jnp.float32)
        pre_pool = jnp.dot(pooled, squeeze_float, precision=PRECISE)
        norm_pool, normed_pool, scale_pool = norm_forward(
            pre_pool, gain_pool, bias_pool, image_count
        )
        hidden = jax.nn.silu(norm_pool)
        logits = (jnp.dot(hidden, expand_float, precision=PRECISE) + bias_expand).reshape(
            per_batch, RADIX, BOTTLE
        )
        attention = jax.nn.softmax(logits, axis=1)
        mixed = jnp.sum(splits * attention[:, None, None], axis=3).astype(bf16)
        projected = jnp.einsum("nhwb,bc->nhwc", mixed, last, preferred_element_type=jnp.float32)
        norm_three, normed_three, scale_three = norm_forward(
            projected, gain_three, bias_three, pixel_count
        )
        summed = batched.astype(jnp.float32) + norm_three
        outputs.append(jax.nn.silu(summed).astype(bf16))
        backward_set = (
            lax.all_gather(low_reduce, "dp", axis=0, tiled=True),
            lax.all_gather(low_conv, "dp", axis=0, tiled=True),
            lax.all_gather(low_squeeze, "dp", axis=0, tiled=True),
            lax.all_gather(low_expand, "dp", axis=0, tiled=True),
            lax.all_gather(low_project, "dp", axis=0, tiled=True),
            lax.all_gather(low_norm, "dp", axis=0, tiled=True),
        )
        first, conv, squeeze, expand, last, packed = backward_set
        gains_back = split_params(packed.astype(jnp.float32))
        conv_grouped = conv.reshape(RADIX, 9 * group_in, BOTTLE)
        expand_float = expand.astype(jnp.float32)
        squeeze_float = squeeze.astype(jnp.float32)
        upstream = cotangent.astype(jnp.float32) * silu_slope(summed)
        d_projected, gain_three_grad, bias_three_grad = norm_backward(
            upstream, normed_three, scale_three, gains_back[7], pixel_count
        )
        d_projected_low = d_projected.astype(bf16)
        grad_last = grad_last + jnp.einsum(
            "nhwb,nhwc->bc", mixed, d_projected_low, preferred_element_type=jnp.float32
        )
        d_mixed = jnp.einsum(
            "nhwc,bc->nhwb", d_projected_low, last, preferred_element_type=jnp.float32
        )
        d_splits = d_mixed[:, :, :, None] * attention[:, None, None]
        d_attention = jnp.sum(d_mixed[:, :, :, None] * splits, axis=(1, 2))
        d_logits = attention * (
            d_attention - jnp.sum(attention * d_attention, axis=1, keepdims=True)
        )
        flat_logits = d_logits.reshape(per_batch, RADIX * BOTTLE)
        grad_expand = grad_expand + jnp.dot(hidden.T, flat_logits, precision=PRECISE)
        d_hidden = jnp.dot(flat_logits, expand_float.T, precision=PRECISE)
        d_pool_norm = d_hidden * silu_slope(norm_pool)
        pool_bias_sum, pool_gain_sum, expand_bias_sum = lax.psum(
            (
                jnp.sum(d_pool_norm, axis=0),
                jnp.sum(d_pool_norm * normed_pool, axis=0),
                jnp.sum(flat_logits, axis=0),
            ),
            ("dp", "rep"),
        )
        d_pre_pool = (
            gains_back[4]
            * scale_pool
            * (
                d_pool_norm
                - pool_bias_sum / image_count
                - normed_pool * (pool_gain_sum / image_count)
            )
        )
        grad_squeeze = grad_squeeze + jnp.dot(pooled.T, d_pre_pool, precision=PRECISE)
        d_pooled = jnp.dot(d_pre_pool, squeeze_float.T, precision=PRECISE)
        d_splits = d_splits + (d_pooled / (SIDE * SIDE))[:, None, None, None, :]
        d_norm_two = d_splits.reshape(per_batch, SIDE, SIDE, RADIX * BOTTLE) * silu_slope(norm_two)
        d_widened, gain_two_grad, bias_two_grad = norm_backward(
            d_norm_two, normed_two, scale_two, gains_back[2], pixel_count
        )
        d_widened_low = d_widened.astype(bf16).reshape(per_batch * SIDE * SIDE, RADIX, BOTTLE)
        grad_conv = grad_conv + jnp.einsum(
            "prk,pro->rko", columns, d_widened_low, preferred_element_type=jnp.float32
        )
        d_columns = jnp.einsum(
            "pro,rko->prk", d_widened_low, conv_grouped, preferred_element_type=jnp.float32
        )
        d_active = unpatch(d_columns.reshape(per_batch, SIDE, SIDE, RADIX, 9, group_in)).reshape(
            per_batch, SIDE, SIDE, BOTTLE
        )
        d_norm_one = d_active * silu_slope(norm_one)
        d_reduced, gain_one_grad, bias_one_grad = norm_backward(
            d_norm_one, normed_one, scale_one, gains_back[0], pixel_count
        )
        d_reduced_low = d_reduced.astype(bf16)
        grad_first = grad_first + jnp.einsum(
            "nhwc,nhwb->cb", batched, d_reduced_low, preferred_element_type=jnp.float32
        )
        input_grads.append(
            upstream
            + jnp.einsum("nhwb,cb->nhwc", d_reduced_low, first, preferred_element_type=jnp.float32)
        )
        grad_norms = grad_norms + jnp.concatenate(
            [
                gain_one_grad,
                bias_one_grad,
                gain_two_grad,
                bias_two_grad,
                pool_gain_sum,
                pool_bias_sum,
                expand_bias_sum,
                gain_three_grad,
                bias_three_grad,
            ]
        )
    grad_conv = grad_conv.reshape(9 * BOTTLE, BOTTLE)
    partial_value = (
        lax.psum_scatter(grad_first, "dp", scatter_dimension=0, tiled=True),
        lax.psum_scatter(grad_conv, "dp", scatter_dimension=0, tiled=True),
        lax.psum_scatter(grad_squeeze, "dp", scatter_dimension=0, tiled=True),
        lax.psum_scatter(grad_expand, "dp", scatter_dimension=0, tiled=True),
        lax.psum_scatter(grad_last, "dp", scatter_dimension=0, tiled=True),
    )
    owned = lax.psum(
        (partial_value[0], partial_value[1], partial_value[2], partial_value[3], partial_value[4]),
        "rep",
    )
    shard_length = norm_params.shape[0]
    norm_grad_owned = lax.dynamic_slice_in_dim(
        grad_norms, lax.axis_index("dp") * shard_length, shard_length
    )
    reduce_new = adamw(
        reduce_weight, reduce_moment, reduce_second, owned[0], 2.0 * CHANNELS ** (-0.5), DECAY
    )
    conv_new = adamw(
        conv_weight,
        conv_moment,
        conv_second,
        owned[1],
        2.0 * (9 * BOTTLE // RADIX) ** (-0.5),
        DECAY,
    )
    squeeze_new = adamw(
        squeeze_weight, squeeze_moment, squeeze_second, owned[2], 2.0 * BOTTLE ** (-0.5), DECAY
    )
    expand_new = adamw(
        expand_weight, expand_moment, expand_second, owned[3], 2.0 * (INNER // 8) ** (-0.5), DECAY
    )
    project_new = adamw(
        project_weight, project_moment, project_second, owned[4], 2.0 * BOTTLE ** (-0.5), DECAY
    )
    norm_new = adamw(norm_params, norm_moment, norm_second, norm_grad_owned, NORM_RATE, 0.0)
    return (
        jnp.concatenate(outputs, axis=0),
        jnp.concatenate(input_grads, axis=0),
        reduce_new[0],
        reduce_new[1],
        reduce_new[2],
        conv_new[0],
        conv_new[1],
        conv_new[2],
        squeeze_new[0],
        squeeze_new[1],
        squeeze_new[2],
        expand_new[0],
        expand_new[1],
        expand_new[2],
        project_new[0],
        project_new[1],
        project_new[2],
        norm_new[0],
        norm_new[1],
        norm_new[2],
    )


MESH = pl.DeviceIdType.MESH
PAD = 64
CHUNK = 112
F32 = jnp.float32
BF16 = jnp.bfloat16
STATS = {
    "reduced": (4, 256),
    "widened0": (4, 256),
    "widened1": (4, 256),
    "pool": (4, 128),
    "images": (16, 128),
    "projected0": (4, 512),
    "projected1": (4, 512),
    "back_projected0": (4, 512),
    "back_projected1": (4, 512),
    "back_pool": (4, 128),
    "back_widened": (8, 512),
    "back_reduced0": (4, 128),
    "back_reduced1": (4, 128),
}
DIRECT = ("reduced", "pool", "back_pool", "back_reduced0", "back_reduced1")


def sigmoid(values):
    return 0.5 * jnp.tanh(0.5 * values) + 0.5


def row_ids(width):
    return lax.broadcasted_iota(jnp.int32, (8, width), 0)


def image_sum(rows):
    return rows + pltpu.roll(rows, 4, 0)


def pair_sum(rows):
    even = row_ids(rows.shape[1]) % 2 == 0
    return rows + jnp.where(even, pltpu.roll(rows, 7, 0), pltpu.roll(rows, 1, 0))


def micro_sum(rows):
    return pair_sum(image_sum(rows))


def stack_sums(first, second):
    rows = (first[0:1], first[2:3], second[0:1], second[2:3])
    return jnp.concatenate(rows, axis=0)


def unstack_sums(stacked):
    earlier = lax.rem(row_ids(stacked.shape[1]), 4) < 2
    return tuple(jnp.where(earlier, stacked[k : k + 1], stacked[k + 1 : k + 2]) for k in (0, 2))


def norm_terms(total, square, gain, bias, count):
    center = total * (1.0 / count)
    scale = lax.rsqrt(square * (1.0 / count) - center * center + EPSILON)
    slope = scale * gain
    return center, scale, slope, bias - center * slope


def back_terms(center, scale, slope, bias_sum, gain_sum, count):
    by_value = -slope * scale * (gain_sum * (1.0 / count))
    constant = -slope * (bias_sum * (1.0 / count)) - by_value * center
    return by_value, constant


def tdot(left, right):
    return lax.dot_general(left, right, (((0,), (0,)), ((), ())), preferred_element_type=F32)


def dot_t(left, right):
    return lax.dot_general(left, right, (((1,), (1,)), ((), ())), preferred_element_type=F32)


def in_parts(values, parts):
    found = []
    for _ in range(parts):
        rounded = values.astype(BF16).astype(F32)
        found.append(rounded)
        values = values - rounded
    return found


def exact_dot(left, right, transposed):
    stacked = jnp.concatenate(in_parts(left, 3), axis=0).astype(BF16)
    wide = dot_t(stacked, right) if transposed else jnp.dot(stacked, right, preferred_element_type=F32)
    return wide[0:8] + wide[8:16] + wide[16:24]


def row_dot(left, right):
    high, low = in_parts(left, 2)
    other_high, other_low = in_parts(right, 2)
    return tdot(
        jnp.concatenate([high, high, low, low], axis=0).astype(BF16),
        jnp.concatenate([other_high, other_low, other_high, other_low], axis=0).astype(BF16),
    )


def image_dot(left, right):
    return row_dot(jnp.where(row_ids(left.shape[1]) < 4, left, 0.0), right)


def block_kernel(
    n_dp,
    n_rep,
    x_hbm,
    gy_hbm,
    w1_hbm,
    wc_hbm,
    sq_hbm,
    ex_hbm,
    w3_hbm,
    np_hbm,
    bo_hbm,
    dx_hbm,
    f1_hbm,
    fc_hbm,
    f3_hbm,
    fe_hbm,
    gn_hbm,
    w1_own,
    wc_own,
    sq_own,
    ex_own,
    w3_own,
    np_own,
    gn_out,
    x4,
    gy4,
    x_v,
    gy_v,
    fw1,
    fwc,
    fpe,
    pe_own,
    np_slots,
    np_full,
    red,
    act,
    columns,
    wid,
    splits,
    mixed,
    proj,
    up,
    bo4,
    dx4,
    dproj,
    d_mixed,
    dn2,
    dwid,
    dcol,
    dn1,
    dred,
    g1,
    gc,
    g3,
    ge,
    gb,
    fix,
    back_own,
    *rest,
):
    n_ar = len(STATS)
    order = {name: k for k, name in enumerate(STATS)}
    ar_slots_a = dict(zip(STATS, rest[0:n_ar]))
    ar_slots_b = dict(zip(STATS, rest[n_ar : 2 * n_ar]))
    rest = rest[2 * n_ar :]
    r1s, xs, xr, acc, zs, zr = (rest[6 * i : 6 * i + 6] for i in range(6))
    ys, r2s, hr, hs, fs = rest[36:39], rest[39:42], rest[42:45], rest[45:47], rest[47:51]
    rest = rest[51:]
    local_sem, ar_send_a, ar_recv_a, ar_send_b, ar_recv_b, np_sems, ws, wr, gs, gr = rest

    dp = lax.axis_index("dp")
    rep = lax.axis_index("rep")
    core = lax.rem(rep, 2)
    half_y = lax.div(rep, 2)
    planes = n_dp // 2
    plane_size = 2 * n_rep
    plane = lax.div(dp, 2)
    in_plane = lax.rem(dp, 2) * n_rep + rep
    sibling = (dp, half_y * 2 + (1 - core))
    across = (dp, (1 - half_y) * 2 + core)
    pixels = float(SIDE * SIDE * 2 * n_dp * n_rep)
    pictures = float(2 * n_dp * n_rep)

    x = lax.rem(dp, 2)
    if planes == 4:
        upper = lax.div(plane, 2)
        other_planes = [3 - 3 * upper, 2 - upper, 1 - plane + 4 * upper]
    else:
        other_planes = [lax.rem(plane + step, planes) for step in range(1, planes)]
    flips = ((1, 1, 1), (1, 1, 0), (1, 0, 1), (1, 0, 0), (0, 1, 1), (0, 1, 0), (0, 0, 1), (0, 0, 0))

    def of_flip(z, flip):
        there = [1 - own if turn else own for own, turn in zip((x, half_y, core), flip)]
        return (z * 2 + there[0], there[1] * 2 + there[2])

    plane_peers = [of_flip(plane, flip) for flip in flips[:-1]]
    column_peers = [of_flip(z, flips[-1]) for z in other_planes]
    owner_peers = [of_flip(z, flip) for z in other_planes for flip in (flips[3], flips[7])]
    owner_peers += [of_flip(plane, flips[3])]
    all_peers = [of_flip(z, flip) for z in other_planes for flip in flips] + plane_peers
    me, everyone = dp * n_rep + rep, n_dp * n_rep
    x_peer = of_flip(plane, flips[3])

    def remote(src, dst, send_sem, recv_sem, device):
        return pltpu.make_async_remote_copy(
            src_ref=src,
            dst_ref=dst,
            send_sem=send_sem,
            recv_sem=recv_sem,
            device_id=device,
            device_id_type=MESH,
        )

    def send_all(ref, send_sem, recv_sem, peers):
        for device in peers:
            remote(ref, ref, send_sem, recv_sem, device).start()

    def wait_bytes(ref, sem):
        pltpu.make_async_copy(ref, ref, sem).wait()

    def over_rows(body, init):
        def step(index, carry):
            return body(pl.multiple_of(index * CHUNK, CHUNK), carry)

        return lax.fori_loop(0, ROWS // CHUNK, step, init)

    def grouped(values):
        return values.reshape(CHUNK // 8, 8, values.shape[-1])

    def by_four(values):
        return flat(values).reshape(CHUNK // 4, 4, values.shape[-1])

    def flat(values):
        return values.reshape(CHUNK, values.shape[-1])

    own_copies = [
        pltpu.make_async_copy(source, target, local_sem.at[4 + k])
        for k, (source, target) in enumerate(
            (
                (w1_hbm, w1_own),
                (np_hbm, np_own),
                (wc_hbm, wc_own),
                (w3_hbm, w3_own),
                (sq_hbm, sq_own),
                (ex_hbm, ex_own),
            )
        )
    ]
    for copy in own_copies:
        copy.start()
    x_copy = pltpu.make_async_copy(x_hbm, x4, local_sem.at[0])
    gy_copy = pltpu.make_async_copy(gy_hbm, gy4, local_sem.at[1])
    x_copy.start()
    barrier = pltpu.get_barrier_semaphore()
    for device in all_peers:
        pl.semaphore_signal(barrier, inc=1, device_id=device, device_id_type=MESH)

    def lanes_of(index, width):
        return pl.ds(pl.multiple_of(index * width, 128), width)

    part = core * 2 + half_y
    own_copies[0].wait()
    q1 = w1_own.shape[0] // 4
    fw1[plane, x, core, half_y] = w1_own[pl.ds(pl.multiple_of(part * q1, q1), q1), :].astype(BF16)

    pl.semaphore_wait(barrier, everyone - 1)

    def region(which, z, xs, c, y):
        return (
            lambda: fw1.at[z, xs, c, y],
            lambda: fwc.at[z, xs, y, :, lanes_of(c, 128)],
            lambda: fpe.at[z, xs, :, lanes_of(c, fpe.shape[3] // 2)],
        )[which]()

    both_x = pl.ds(0, 2)
    near_planes = [plane] + other_planes[::-1]
    split_over_y = (True, True, False)

    def pass_on(which, ref, stage, z, device):
        remote(ref, ref, ws.at[which, stage], wr.at[which, stage, z], device).start()

    def gather_out(which):
        mine = region(which, plane, x, core, half_y)
        for device in column_peers:
            pass_on(which, mine, 0, plane, device)
        pass_on(which, mine, 1, plane, x_peer)

    def gather_x(which, k):
        z = near_planes[k]
        mine = region(which, z, x, core, half_y)
        wait_bytes(mine, wr.at[which, 0, z])
        pass_on(which, mine, 1, z, x_peer)

    def gather_y(which, k):
        z = near_planes[k]
        wait_bytes(region(which, z, 1 - x, core, half_y), wr.at[which, 1, z])
        mine = region(which, z, both_x, core, half_y)
        if split_over_y[which]:
            pass_on(which, mine, 2, z, across)
        pass_on(which, mine, 3, z, sibling)

    def gather_hand(which, k):
        z = near_planes[k]
        theirs = region(which, z, both_x, core, 1 - half_y)
        wait_bytes(theirs, wr.at[which, 2, z])
        pass_on(which, theirs, 4, z, sibling)

    def gather_end(which):
        for z in near_planes:
            wait_bytes(region(which, z, both_x, 1 - core, half_y), wr.at[which, 3, z])
            if split_over_y[which]:
                wait_bytes(region(which, z, both_x, 1 - core, 1 - half_y), wr.at[which, 4, z])

    def gather_sent(which):
        wait_bytes(region(which, pl.ds(0, planes - 1), x, core, half_y), ws.at[which, 0])
        wait_bytes(region(which, pl.ds(0, planes), x, core, half_y), ws.at[which, 1])
        for stage in (2, 3, 4) if split_over_y[which] else (3,):
            wait_bytes(region(which, pl.ds(0, planes), both_x, core, half_y), ws.at[which, stage])

    def to_rows(source, target):
        def body(index, carry):
            values = source[pl.ds(index * (CHUNK // 4), CHUNK // 4)].astype(F32)
            row = pl.multiple_of(index * CHUNK, CHUNK)
            target[pl.ds(row, CHUNK), :] = values.reshape(CHUNK, CHANNELS).astype(BF16)
            return carry

        lax.fori_loop(0, ROWS // CHUNK, body, 0)

    gather_out(0)

    own_copies[1].wait()
    shard = np_own.shape[0]
    lanes_id = lax.broadcasted_iota(jnp.int32, (8, 128), 1)
    turn = lax.rem(shard * dp, 128)
    np_rows = []
    for at in range(0, shard, 128):
        width = min(128, shard - at)
        piece_row = np_own[pl.ds(at, width)].reshape(1, width)
        if width < 128:
            piece_row = jnp.concatenate([piece_row, jnp.zeros((1, 128 - width), F32)], axis=1)
        np_rows.append(piece_row)
    np_rows.append(jnp.zeros((8 - len(np_rows), 128), F32))
    np_turned = jnp.concatenate(np_rows, axis=0).astype(BF16).astype(F32)
    np_turned = pltpu.roll(np_turned, turn, 1)
    np_slots[dp] = jnp.where(lanes_id < turn, pltpu.roll(np_turned, 1, 0), np_turned)
    send_all(np_slots.at[dp], np_sems.at[0], np_sems.at[1], owner_peers)
    own_copies[2].wait()
    qc = wc_own.shape[0] // 2
    fwc[plane, x, half_y, :, lanes_of(core, 128)] = wc_own[
        pl.ds(pl.multiple_of(half_y * qc, qc), qc), lanes_of(core, 128)
    ].astype(BF16)
    gather_out(1)
    for copy in own_copies[3:]:
        copy.wait()
    ex_rows = ex_own.shape[0]
    pe_own[:, 0:CHANNELS] = w3_own[...].astype(BF16)
    pe_own[:, 1024:1152] = sq_own[...].astype(BF16)
    pe_own[0:ex_rows, 1152:1408] = ex_own[:, 0:256].astype(BF16)
    pe_own[ex_rows : 2 * ex_rows, 1152:1408] = ex_own[:, 256:512].astype(BF16)
    pe_own[:, 1408:1536] = jnp.zeros((2 * ex_rows, 128), BF16)
    fpe[plane, x, :, lanes_of(core, 768)] = pe_own[:, lanes_of(core, 768)]
    gather_x(0, 1)
    gather_y(0, 0)
    gather_x(0, 2)
    gather_y(0, 1)
    gy_copy.start()
    x_copy.wait()
    to_rows(x4, x_v)
    gather_hand(0, 0)
    gather_x(0, 3)
    gather_y(0, 2)
    gather_hand(0, 1)
    gather_y(0, 3)
    gather_x(1, 1)
    gather_x(1, 2)
    gather_x(1, 3)
    gather_out(2)
    zero_rows = jnp.zeros((PAD, BOTTLE), F32)
    for side in range(3):
        act[side, 0:PAD, :] = zero_rows
        act[side, PAD + ROWS : 2 * PAD + ROWS, :] = zero_rows
    for lane_block in range(9):
        dcol[0:PAD, lane_block * 256 : lane_block * 256 + 256] = zero_rows
        dcol[PAD + ROWS : 2 * PAD + ROWS, lane_block * 256 : lane_block * 256 + 256] = zero_rows

    gather_hand(0, 2)
    gather_hand(0, 3)
    for k in range(4):
        gather_y(1, k)

    def sum_start(k, payload):
        if k in DIRECT:
            ar_slots_a[k][me] = payload
            send_all(ar_slots_a[k].at[me], ar_send_a.at[order[k]], ar_recv_a.at[order[k]], all_peers)
        else:
            ar_slots_a[k][in_plane] = payload
            send_all(ar_slots_a[k].at[in_plane], ar_send_a.at[order[k]], ar_recv_a.at[order[k]], plane_peers)

    def sum_slots(slots, count):
        sums = [slots[slot] for slot in range(count)]
        while len(sums) > 1:
            sums = [sums[i] + sums[i + 1] for i in range(0, len(sums), 2)]
        return sums[0]

    def sum_turn(k):
        if k in DIRECT:
            return
        wait_bytes(ar_slots_a[k].at[pl.ds(0, plane_size - 1)], ar_recv_a.at[order[k]])
        ar_slots_b[k][plane] = sum_slots(ar_slots_a[k], plane_size)
        send_all(ar_slots_b[k].at[plane], ar_send_b.at[order[k]], ar_recv_b.at[order[k]], column_peers)

    def sum_end(k):
        if k in DIRECT:
            wait_bytes(ar_slots_a[k].at[pl.ds(0, everyone - 1)], ar_recv_a.at[order[k]])
            return sum_slots(ar_slots_a[k], everyone)
        wait_bytes(ar_slots_b[k].at[pl.ds(0, planes - 1)], ar_recv_b.at[order[k]])
        return sum_slots(ar_slots_b[k], planes)

    cut = 64
    conv_rows = {1: pl.ds(0, cut), 2: pl.ds(cut, gc.shape[2] - cut)}
    grads = (g1, gc, gc, g3, ge, gb)
    turned_kinds = (0, 5)
    split_kinds = (0, 1, 2)

    def half_of(which, c):
        ref = grads[which]
        if which in turned_kinds:
            return ref.at[c]
        if which in conv_rows:
            return ref.at[:, :, conv_rows[which], lanes_of(c, 128)]
        return ref.at[:, :, lanes_of(c, (512, 256)[which - 3])]

    def y_part(which, ref, y):
        return ref.at[y] if which == 0 else ref.at[:, y]

    def of_owner(which, ref, d):
        if which == 0:
            return ref.at[:, lanes_of(d, CHANNELS // n_dp)]
        if which == 5:
            return ref.at[:, :, lanes_of(d, CHANNELS // n_dp)]
        return ref.at[d]

    def in_blocks(which, body):
        if which == 0:
            count = 4
            rows = g1.shape[2] // count
            block = lambda index: pl.ds(pl.multiple_of(index * rows, rows), rows)
        else:
            count, block = n_dp, lambda index: index

        def step(index, carry):
            body(block(index))
            return carry

        lax.fori_loop(0, count, step, 0)

    def stage(which, number, src, dst, device):
        remote(src, dst, gs.at[which, number], gr.at[which, number], device).start()

    def reduce_core(which):
        stage(which, 0, half_of(which, 1 - core), r1s[which], sibling)

    def reduce_y(which):
        wait_bytes(r1s[which], gr.at[which, 0])
        half = half_of(which, core)
        away, mine = y_part(which, half, 1 - half_y), y_part(which, half, half_y)
        there, here = y_part(which, r1s[which], 1 - half_y), y_part(which, r1s[which], half_y)

        def add_away(at):
            ys[which][at] = (away[at] + there[at]).astype(BF16)

        in_blocks(which, add_away)
        stage(which, 1, ys[which], r2s[which], across)

        def add_mine(at):
            mine[at] = mine[at] + here[at]

        in_blocks(which, add_mine)

    def reduce_x(which):
        if which in split_kinds:
            wait_bytes(r2s[which], gr.at[which, 1])
            mine = y_part(which, half_of(which, core), half_y)
            other = r2s[which]
        else:
            wait_bytes(r1s[which], gr.at[which, 0])
            mine, other = half_of(which, core), r1s[which]

        def summed(d):
            first, second = of_owner(which, mine, d), of_owner(which, other, d)
            return first[...].astype(F32) + second[...].astype(F32)

        for z in range(planes):
            xs[which][z] = summed(2 * z + 1 - x).astype(xs[which].dtype)
        stage(which, 2, xs[which], xr[which], x_peer)
        for z in range(planes):
            acc[which][z] = summed(2 * z + x)

    def reduce_z(which):
        wait_bytes(xr[which], gr.at[which, 2])
        for z in range(planes):
            total = acc[which][z] + xr[which][z].astype(F32)
            acc[which][z] = total
            zs[which][z] = total.astype(zs[which].dtype)
        zr[which][plane] = jnp.zeros(zr[which].shape[1:], zr[which].dtype)
        for z, device in zip(other_planes, column_peers):
            stage(which, 3, zs[which].at[z], zr[which].at[plane], device)

    def owner_total(which):
        wait_bytes(zr[which].at[pl.ds(0, planes - 1)], gr.at[which, 3])
        total = acc[which][plane]
        for z in range(planes):
            total = total + zr[which][z].astype(F32)
        return total

    def final_part(which, c, y):
        if which == 0:
            return fs[0].at[c, y]
        if which in conv_rows:
            return fs[1].at[y, conv_rows[which], lanes_of(c, 128)]
        return fs[which - 1].at[:, lanes_of(c, (512, 256)[which - 3])]

    def reduce_across(which):
        total = owner_total(which)
        if which == 5:
            back_own[...] = total
            stage(which, 4, back_own.at[1 - half_y], hr[which - 3], across)
        else:
            hs[which - 3][...] = total
            stage(which, 4, hs[which - 3], hr[which - 3], across)

    def reduce_spread(which):
        if which in split_kinds:
            total = owner_total(which)
        else:
            wait_bytes(hr[which - 3], gr.at[which, 4])
            total = hs[which - 3][...] + hr[which - 3][...]
        if which == 0:
            wait_bytes(hr[2], gr.at[5, 4])
            back = back_own[half_y] + hr[2][...]
            rows = pl.ds(pl.multiple_of(part * (BOTTLE // 4), BOTTLE // 4), BOTTLE // 4)
            total = total - fix[0, rows, :]
            for m in range(2):
                own_back = back[m * (BOTTLE // 4) : (m + 1) * (BOTTLE // 4)]
                total = total - fix[1 + m, rows, :] * own_back
        mine = final_part(which, core, half_y)
        mine[...] = total
        if which in split_kinds:
            stage(which, 4, mine, mine, across)
        stage(which, 5, mine, mine, sibling)

    def reduce_hand(which):
        theirs = final_part(which, core, 1 - half_y)
        wait_bytes(theirs, gr.at[which, 4])
        stage(which, 6, theirs, theirs, sibling)

    def reduce_end(which):
        wait_bytes(final_part(which, 1 - core, half_y), gr.at[which, 5])
        if which in split_kinds:
            wait_bytes(final_part(which, 1 - core, 1 - half_y), gr.at[which, 6])

    def reduce_sent(which):
        wait_bytes(r1s[which], gs.at[which, 0])
        wait_bytes(xs[which], gs.at[which, 2])
        wait_bytes(zs[which].at[pl.ds(0, planes - 1)], gs.at[which, 3])
        if which in split_kinds:
            wait_bytes(ys[which], gs.at[which, 1])
            for number in (4, 5, 6):
                wait_bytes(final_part(which, core, half_y), gs.at[which, number])
        else:
            wait_bytes(hr[which - 3], gs.at[which, 4])
            if which != 5:
                wait_bytes(final_part(which, core, half_y), gs.at[which, 5])

    gather_end(0)
    red[...] = jnp.dot(x_v[...], fw1[...].reshape(CHANNELS, BOTTLE), preferred_element_type=F32)

    def sums_of(ref, start, width):
        def body(row, carry):
            values = grouped(ref[pl.ds(row, CHUNK), start : start + width])
            return carry[0] + jnp.sum(values, axis=0), carry[1] + jnp.sum(values * values, axis=0)

        zero = jnp.zeros((8, width), F32)
        return over_rows(body, (zero, zero))

    def joined(found):
        both = [jnp.concatenate(item, axis=1) for item in zip(*found)]
        return stack_sums(micro_sum(both[0]), micro_sum(both[1]))

    def both_sums(name):
        return unstack_sums(sum_end(name))

    sum_start("reduced", joined([sums_of(red, 0, 256)]))

    gy_copy.wait()
    to_rows(gy4, gy_v)
    wait_bytes(np_slots.at[pl.ds(0, n_dp - 1)], np_sems.at[1])
    np_full[...] = jnp.zeros(np_full.shape, F32)
    for d in range(n_dp):
        at = shard * d // 128
        np_full[at : at + 8, :] = np_full[at : at + 8, :] + np_slots[d]

    def vector(at, width):
        rows = [np_full[at // 128 + k : at // 128 + k + 1, :] for k in range(width // 128)]
        return jnp.concatenate(rows, axis=1) if len(rows) > 1 else rows[0]

    gain_one, bias_one = vector(0, 256), vector(256, 256)
    gain_two, bias_two = vector(512, 512), vector(1024, 512)
    gain_pool, bias_pool = vector(1536, 128), vector(1664, 128)
    bias_expand = vector(1792, 512)
    gain_three, bias_three = vector(2304, 1024), vector(3328, 1024)

    for k in range(1, 4):
        gather_x(2, k)
    total, square = both_sums("reduced")
    center1, scale1, mul1, add1 = norm_terms(total, square, gain_one, bias_one, pixels)

    def make_active(row, carry):
        turned = grouped(red[pl.ds(row, CHUNK), :]) * mul1 + add1
        act[1, pl.ds(PAD + row, CHUNK), :] = flat(turned * sigmoid(turned))
        return carry

    over_rows(make_active, 0)
    for k in range(4):
        gather_hand(1, k)
    place = lax.rem(lax.broadcasted_iota(jnp.int32, (CHUNK, BOTTLE), 0) // 4, SIDE)
    not_last = place != SIDE - 1
    not_first = place != 0

    def beside(side, row, distance, lanes=slice(0, BOTTLE)):
        near = act[side, pl.ds(PAD + row - 8, CHUNK + 16), lanes]
        return pltpu.roll(near, (CHUNK + 16 - distance) % (CHUNK + 16), 0)[8 : 8 + CHUNK]

    def shift_active(row, carry):
        act[2, pl.ds(PAD + row, CHUNK), :] = jnp.where(not_last, beside(1, row, 4), 0.0)
        act[0, pl.ds(PAD + row, CHUNK), :] = jnp.where(not_first, beside(1, row, -4), 0.0)
        return carry

    over_rows(shift_active, 0)

    def make_columns(row, carry):
        for tap in range(9):
            down, side = tap // 3 - 1, tap % 3
            values = act[side, pl.ds(PAD + row + 56 * down, CHUNK), :].astype(BF16)
            columns[0, pl.ds(row, CHUNK), tap * 128 : tap * 128 + 128] = values[:, 0:128]
            columns[1, pl.ds(row, CHUNK), tap * 128 : tap * 128 + 128] = values[:, 128:256]
        return carry

    over_rows(make_columns, 0)
    gather_end(1)
    own_half = n_dp // 2
    own_planes = planes // 2

    def filters(group):
        return fwc[group * own_planes : (group + 1) * own_planes].reshape(9 * 128, BOTTLE)

    halves2 = (slice(0, 256), slice(256, 512))
    for group, lanes in enumerate(halves2):
        wid[:, lanes] = jnp.dot(columns[group], filters(group), preferred_element_type=F32)
        sum_start(f"widened{group}", joined([sums_of(wid, group * 256, 256)]))
    for k in range(4):
        gather_y(2, k)
    sum_turn("widened0")
    sum_turn("widened1")

    norm2 = []
    pooled = jnp.zeros((8, BOTTLE), F32)
    for group, lanes in enumerate(halves2):
        total, square = both_sums(f"widened{group}")
        norm2.append(norm_terms(total, square, gain_two[:, lanes], bias_two[:, lanes], pixels))
        m2, a2 = norm2[group][2:4]

        def make_splits(row, carry):
            turned = grouped(wid[pl.ds(row, CHUNK), lanes]) * m2 + a2
            values = turned * sigmoid(turned)
            splits[pl.ds(row, CHUNK), lanes] = flat(values)
            return carry + jnp.sum(values, axis=0)

        pooled = over_rows(make_splits, pooled)
    pooled = image_sum(pooled) * (1.0 / (SIDE * SIDE))
    gather_end(2)
    last = fpe[:, :, :, 0:CHANNELS].reshape(BOTTLE, CHANNELS)
    squeeze = fpe[:, :, :, 1024:1152].reshape(BOTTLE, INNER)
    ex_both = fpe[:, :, :, 1152:1408]
    expand = jnp.concatenate(
        [
            ex_both[:, :, 0:ex_rows].reshape(INNER, 256),
            ex_both[:, :, ex_rows : 2 * ex_rows].reshape(INNER, 256),
        ],
        axis=1,
    )
    pre_pool = exact_dot(pooled, squeeze, False)
    sum_start("pool", stack_sums(pair_sum(pre_pool), pair_sum(pre_pool * pre_pool)))
    first_micro = lax.rem(row_ids(BOTTLE), 4) < 2

    def make_normed(row, carry):
        rows = pl.ds(row, CHUNK)
        normed = (grouped(red[rows, :]) - center1) * scale1
        dwid[rows, 0:256] = flat(jnp.where(first_micro, normed, 0.0)).astype(BF16)
        dwid[rows, 256:512] = flat(jnp.where(first_micro, 0.0, normed)).astype(BF16)
        return carry + jnp.sum(grouped(x_v[rows, :].astype(F32)), axis=0)

    image_sums = micro_sum(over_rows(make_normed, jnp.zeros((8, CHANNELS), F32)))
    sum_start(
        "images",
        jnp.concatenate(
            [
                image_sums[2 * m : 2 * m + 1, at : at + 128]
                for m in range(2)
                for at in range(0, CHANNELS, 128)
            ],
            axis=0,
        ),
    )
    normed_images = tdot(dwid[...], x_v[...]).astype(BF16)
    normed_images = normed_images.reshape(2, 2, 2, BOTTLE // 4, CHANNELS)
    for m in range(2):
        gb[:, :, m * (BOTTLE // 4) : (m + 1) * (BOTTLE // 4)] = normed_images[m]
    reduce_core(5)
    total, square = unstack_sums(sum_end("pool"))
    center_p, scale_p, mul_p, add_p = norm_terms(total, square, gain_pool, bias_pool, pictures)
    normed_p = (pre_pool - center_p) * scale_p
    norm_p = pre_pool * mul_p + add_p
    gate_p = sigmoid(norm_p)
    hidden = norm_p * gate_p
    slope_p = gate_p * (1.0 + norm_p * (1.0 - gate_p))
    logits = exact_dot(hidden, expand, False) + bias_expand
    left, right = logits[:, 0:256], logits[:, 256:512]
    most = jnp.maximum(left, right)
    left, right = jnp.exp(left - most), jnp.exp(right - most)
    att0 = left / (left + right)
    att1 = right / (left + right)

    def make_mixed(row, carry):
        rows = pl.ds(row, CHUNK)
        values = grouped(splits[rows, 0:256]) * att0 + grouped(splits[rows, 256:512]) * att1
        mixed[rows, :] = flat(values).astype(BF16)
        return carry

    over_rows(make_mixed, 0)
    halves3 = (slice(0, 512), slice(512, 1024))
    blocks3 = [[slice(512 * h + k, 512 * h + k + 256) for k in (0, 256)] for h in range(2)]
    for half, lanes in enumerate(halves3):
        proj[:, lanes] = jnp.dot(mixed[...], last[:, lanes], preferred_element_type=F32)
        sum_start(
            f"projected{half}", joined([sums_of(proj, 512 * half + k, 256) for k in (0, 256)])
        )
    sum_turn("projected0")
    sum_turn("projected1")
    sum_turn("images")
    reduce_x(5)

    norm3 = []
    zero = jnp.zeros((8, 256), F32)
    for half, lanes in enumerate(halves3):
        total, square = both_sums(f"projected{half}")
        norm3.append(norm_terms(total, square, gain_three[:, lanes], bias_three[:, lanes], pixels))
        found = []
        for k, block in enumerate(blocks3[half]):
            c3, s3, m3, a3 = (item[:, k * 256 : k * 256 + 256] for item in norm3[half])

            def make_out(row, carry):
                rows = pl.ds(row, CHUNK)
                values = grouped(proj[rows, block])
                summed = grouped(x_v[rows, block].astype(F32)) + (values * m3 + a3)
                gate = sigmoid(summed)
                bo4[pl.ds(row // 4, CHUNK // 4), :, block] = by_four(summed * gate).astype(BF16)
                upstream = grouped(gy_v[rows, block].astype(F32)) * (
                    gate * (1.0 + summed * (1.0 - gate))
                )
                up[rows, block] = flat(upstream)
                normed = (values - c3) * s3
                return carry[0] + jnp.sum(upstream, axis=0), carry[1] + jnp.sum(
                    upstream * normed, axis=0
                )

            found.append(over_rows(make_out, (zero, zero)))
        sum_start(f"back_projected{half}", joined(found))
    bo_copy = pltpu.make_async_copy(bo4, bo_hbm, local_sem.at[2])
    bo_copy.start()

    def write_norm(at, pattern):
        at = at // 128
        both = pattern[0:1, :] + pattern[2:3, :]
        for k in range(both.shape[1] // 128):
            np_full[at + k : at + k + 1, :] = both[:, k * 128 : k * 128 + 128]

    sum_turn("back_projected0")
    sum_turn("back_projected1")
    reduce_z(5)

    for half, lanes in enumerate(halves3):
        bias_sum, gain_sum = both_sums(f"back_projected{half}")
        write_norm(2304 + 512 * half, gain_sum)
        write_norm(3328 + 512 * half, bias_sum)
        by_value, constant = back_terms(*norm3[half][0:3], bias_sum, gain_sum, pixels)
        for k, block in enumerate(blocks3[half]):
            m3, v3, k3 = (
                item[:, k * 256 : k * 256 + 256] for item in (norm3[half][2], by_value, constant)
            )

            def make_dproj(row, carry):
                rows = pl.ds(row, CHUNK)
                values = grouped(up[rows, block]) * m3 + grouped(proj[rows, block]) * v3 + k3
                dproj[rows, block] = flat(values).astype(BF16)
                return carry

            over_rows(make_dproj, 0)
        part_mixed = dot_t(dproj[:, lanes], last[:, lanes])
        d_mixed[...] = part_mixed if half == 0 else d_mixed[...] + part_mixed

    def attend(row, carry):
        rows = pl.ds(row, CHUNK)
        values = grouped(d_mixed[rows, :])
        return (
            carry[0] + jnp.sum(values * grouped(splits[rows, 0:256]), axis=0),
            carry[1] + jnp.sum(values * grouped(splits[rows, 256:512]), axis=0),
        )

    d_att0, d_att1 = over_rows(attend, (zero, zero))
    d_att0, d_att1 = image_sum(d_att0), image_sum(d_att1)
    both = att0 * d_att0 + att1 * d_att1
    d_logits = jnp.concatenate([att0 * (d_att0 - both), att1 * (d_att1 - both)], axis=1)
    d_hidden = exact_dot(d_logits, expand, True)
    d_pool = d_hidden * slope_p
    per_micro = stack_sums(pair_sum(d_pool), pair_sum(d_pool * normed_p))
    sum_start("back_pool", per_micro)
    ex_sum = pair_sum(d_logits)
    ex_sum = ex_sum + pltpu.roll(ex_sum, 2, 0)

    grad_ex = image_dot(hidden, d_logits)
    grad_ex = grad_ex.reshape(n_dp, ex_rows, 512)
    ge[:, 0:ex_rows, 128:384] = grad_ex[:, :, 0:256]
    ge[:, ex_rows : 2 * ex_rows, 128:384] = grad_ex[:, :, 256:512]
    ge[:, :, 384:512] = jnp.zeros((n_dp, 2 * ex_rows, 128), F32)
    g3[...] = tdot(mixed[...], dproj[...]).reshape(g3.shape)
    reduce_core(3)
    held = []
    for group, att in ((0, att0), (1, att1)):
        lanes = halves2[group]
        c2, s2, m2, a2 = norm2[group]

        def make_dn2(row, carry):
            rows = pl.ds(row, CHUNK)
            values = grouped(wid[rows, lanes])
            turned = values * m2 + a2
            gate = sigmoid(turned)
            slope = gate * (1.0 + turned * (1.0 - gate))
            down = grouped(d_mixed[rows, :]) * att * slope
            dn2[rows, lanes] = flat(down)
            splits[rows, lanes] = flat(slope)
            normed = (values - c2) * s2
            terms = (down, down * normed, slope, slope * normed)
            return tuple(item + jnp.sum(term, axis=0) for item, term in zip(carry, terms))

        held.append([image_sum(item) for item in over_rows(make_dn2, (zero,) * 4)])
    pool_bias_sum, pool_gain_sum = unstack_sums(sum_end("back_pool"))
    write_norm(1536, pool_gain_sum)
    write_norm(1664, pool_bias_sum)
    d_pre_pool = mul_p * (
        d_pool - pool_bias_sum * (1.0 / pictures) - normed_p * (pool_gain_sum * (1.0 / pictures))
    )
    d_pooled = exact_dot(d_pre_pool, squeeze, True) * (1.0 / (SIDE * SIDE))
    found = []
    for down, down_normed, slope, slope_normed in held:
        first, second = down + d_pooled * slope, down_normed + d_pooled * slope_normed
        found.append(stack_sums(pair_sum(first), pair_sum(second)))
    sum_start(
        "back_widened", jnp.concatenate([jnp.concatenate(found, axis=1), ex_sum[0:4]], axis=0)
    )
    ge[:, :, 0:128] = image_dot(pooled, d_pre_pool).reshape(n_dp, 2 * ex_rows, 128)
    reduce_core(4)
    sum_turn("back_widened")
    reduce_across(5)
    reduce_x(3)
    reduce_x(4)

    small_zero = jnp.zeros((8, 128), F32)
    for group, lanes in enumerate(halves2):
        if group == 0:
            whole = sum_end("back_widened")
            for k in range(4):
                np_full[14 + k : 15 + k, :] = whole[4:5, k * 128 : k * 128 + 128]
        bias_sum, gain_sum = unstack_sums(whole[0:4, lanes])
        write_norm(512 + 256 * group, gain_sum)
        write_norm(1024 + 256 * group, bias_sum)
        m2 = norm2[group][2]
        v2, k2 = back_terms(*norm2[group][0:3], bias_sum, gain_sum, pixels)
        pooled_m2 = d_pooled * m2

        def make_dwid(row, carry):
            rows = pl.ds(row, CHUNK)
            values = grouped(dn2[rows, lanes]) * m2 + grouped(splits[rows, lanes]) * pooled_m2
            values = values + grouped(wid[rows, lanes]) * v2 + k2
            dwid[rows, lanes] = flat(values).astype(BF16)
            return carry

        over_rows(make_dwid, 0)
        gc[group * own_half : (group + 1) * own_half] = tdot(
            columns[group], dwid[:, lanes]
        ).reshape(own_half, 2, 9 * 128 // own_half // 2, BOTTLE)
    reduce_core(1)
    reduce_core(2)
    for group, lanes in enumerate(halves2):
        dcol[PAD : PAD + ROWS, group * 1152 : group * 1152 + 1152] = dot_t(
            dwid[:, lanes], filters(group)
        )
        inner = slice(group * 128, group * 128 + 128)

        def gather_taps(row, carry):
            for side in range(3):
                total = None
                for down in range(3):
                    at = group * 1152 + (3 * down + side) * 128
                    values = dcol[pl.ds(PAD + row - 56 * (down - 1), CHUNK), at : at + 128]
                    total = values if total is None else total + values
                act[side, pl.ds(PAD + row, CHUNK), inner] = total
            return carry

        over_rows(gather_taps, 0)
        c1, s1, m1, a1 = (item[:, inner] for item in (center1, scale1, mul1, add1))
        not_first1, not_last1 = not_first[:, inner], not_last[:, inner]

        def make_dn1(row, carry):
            rows = pl.ds(row, CHUNK)
            d_active = act[1, pl.ds(PAD + row, CHUNK), inner]
            d_active = d_active + jnp.where(not_first1, beside(2, row, -4, inner), 0.0)
            d_active = d_active + jnp.where(not_last1, beside(0, row, 4, inner), 0.0)
            values = grouped(red[rows, inner])
            turned = values * m1 + a1
            gate = sigmoid(turned)
            slope = gate * (1.0 + turned * (1.0 - gate))
            down = grouped(d_active) * slope
            dn1[rows, inner] = flat(down)
            mixed[rows, inner] = flat(down * m1).astype(BF16)
            normed = (values - c1) * s1
            return carry[0] + jnp.sum(down, axis=0), carry[1] + jnp.sum(down * normed, axis=0)

        bias_sum, gain_sum = over_rows(make_dn1, (small_zero, small_zero))
        sum_start(f"back_reduced{group}", stack_sums(micro_sum(bias_sum), micro_sum(gain_sum)))
        if group == 0:
            reduce_y(1)
            reduce_z(3)
            reduce_z(4)
    reduce_y(2)
    sum_turn("back_reduced0")
    sum_turn("back_reduced1")
    g1[...] = tdot(mixed[...], x_v[...]).reshape(g1.shape)
    reduce_core(0)
    reduce_x(1)
    reduce_across(3)
    reduce_across(4)
    found = [unstack_sums(sum_end(f"back_reduced{group}")) for group in range(2)]
    bias_sum, gain_sum = (jnp.concatenate(item, axis=1) for item in zip(*found))
    write_norm(0, gain_sum)
    write_norm(256, bias_sum)
    by_value, constant = back_terms(center1, scale1, mul1, bias_sum, gain_sum, pixels)
    def make_dred(row, carry):
        rows = pl.ds(row, CHUNK)
        values = grouped(dn1[rows, :]) * mul1 + grouped(red[rows, :]) * by_value + constant
        dred[rows, :] = flat(values).astype(BF16)
        return carry

    over_rows(make_dred, 0)
    reduce_x(2)
    reduce_z(1)
    proj[...] = dot_t(dred[...], fw1[...].reshape(CHANNELS, BOTTLE))
    reduce_y(0)

    by_bias = mul1 * bias_sum * (1.0 / pixels)
    by_gain = mul1 * gain_sum * (1.0 / pixels)
    image_sums = sum_end("images")
    ids = lax.broadcasted_iota(jnp.int32, (16, 128), 0)
    own_sums = [
        jnp.sum(jnp.where(ids == m * n_dp + dp, image_sums, 0.0), axis=0, keepdims=True)
        for m in range(2)
    ]
    ids = row_ids(128)
    fix[0] = row_dot(by_bias, jnp.where(ids == 0, own_sums[0], jnp.where(ids == 2, own_sums[1], 0.0)))
    for m in range(2):
        fix[1 + m] = row_dot(by_gain, jnp.where(ids == 2 * m, 1.0, 0.0))
    reduce_spread(3)
    reduce_spread(4)

    def make_dx(row, carry):
        for start in range(0, CHANNELS, 256):
            lanes = slice(start, start + 256)
            values = up[pl.ds(row, CHUNK), lanes] + proj[pl.ds(row, CHUNK), lanes]
            dx4[pl.ds(row // 4, CHUNK // 4), :, lanes] = values.reshape(CHUNK // 4, 4, 256)
        return carry

    over_rows(make_dx, 0)
    dx_copy = pltpu.make_async_copy(dx4, dx_hbm, local_sem.at[3])
    dx_copy.start()
    norm_rows = np_full[0:8, :]
    for d in range(1, n_dp):
        at = shard * d // 128
        norm_rows = jnp.where(dp == d, np_full[at : at + 8, :], norm_rows)
    norm_rows = pltpu.roll(norm_rows, lax.rem(128 - turn, 128), 1)
    gn_out[...] = jnp.where(lanes_id < 128 - turn, norm_rows, pltpu.roll(norm_rows, 7, 0))
    reduce_z(2)
    reduce_x(0)
    reduce_spread(1)
    reduce_z(0)
    reduce_spread(2)
    reduce_hand(1)
    reduce_spread(0)
    reduce_hand(2)
    reduce_hand(0)
    out_copies = [
        pltpu.make_async_copy(source, target, local_sem.at[10 + k])
        for k, (source, target) in enumerate(
            (
                (gn_out, gn_hbm),
                (fs[2], f3_hbm),
                (fs[3], fe_hbm),
                (fs[1], fc_hbm),
                (fs[0], f1_hbm),
            )
        )
    ]
    out_copies[0].start()
    for which in (3, 4, 1, 2, 0):
        reduce_end(which)
        if which != 1:
            out_copies[{3: 1, 4: 2, 2: 3, 0: 4}[which]].start()

    bo_copy.wait()
    dx_copy.wait()
    for copy in out_copies:
        copy.wait()
    for k in STATS:
        if k in DIRECT:
            wait_bytes(ar_slots_a[k].at[pl.ds(0, everyone - 1)], ar_send_a.at[order[k]])
        else:
            wait_bytes(ar_slots_a[k].at[pl.ds(0, plane_size - 1)], ar_send_a.at[order[k]])
            wait_bytes(ar_slots_b[k].at[pl.ds(0, planes - 1)], ar_send_b.at[order[k]])
    wait_bytes(np_slots.at[pl.ds(0, n_dp - 1)], np_sems.at[0])
    for which in range(3):
        gather_sent(which)
    for which in range(6):
        reduce_sent(which)


def update_kernel(*refs):
    sources, targets = refs[0:25], refs[25:45]
    inputs, outs, through = refs[45:68], refs[68:86], refs[86:88]
    pass_sems, in_sems, out_sems = refs[88:91]
    part = SIDE * SIDE // 4
    fetching, passing = [], []
    for k in range(4):
        rows = pl.ds(k * part, part)
        for which in range(2):
            fetching.append(
                pltpu.make_async_copy(
                    sources[which].at[rows], through[which].at[rows], pass_sems.at[0, which, k]
                )
            )
            passing.append(
                pltpu.make_async_copy(
                    through[which].at[rows], targets[which].at[rows], pass_sems.at[1, which, k]
                )
            )
    for copy in fetching:
        copy.start()
    coming = [
        pltpu.make_async_copy(source, held, in_sems.at[k])
        for k, (source, held) in enumerate(zip(sources[2:], inputs))
    ]
    for copy in coming:
        copy.start()
    grads, states = inputs[0:5], inputs[5:23]
    going = [
        pltpu.make_async_copy(held, target, out_sems.at[k])
        for k, (held, target) in enumerate(zip(outs, targets[2:]))
    ]
    ex_rows = states[9].shape[0]
    shard = states[15].shape[0]
    fans = (CHANNELS, 9 * BOTTLE // RADIX, BOTTLE, INNER // 8, BOTTLE)
    for copy in coming[0:5]:
        copy.wait()
    found = (
        grads[0][...].T,
        grads[1][...],
        grads[3][:, 0:128],
        jnp.concatenate([grads[3][0:ex_rows, 128:384], grads[3][ex_rows:, 128:384]], axis=1),
        grads[2][...],
    )
    for order, k in enumerate((3, 2, 4, 0, 1)):
        for copy in coming[5 + 3 * k : 8 + 3 * k]:
            copy.wait()
        new = adamw(
            states[3 * k][...],
            states[3 * k + 1][...],
            states[3 * k + 2][...],
            found[k],
            2.0 * fans[k] ** (-0.5),
            DECAY,
        )
        for j in range(3):
            outs[3 * k + j][...] = new[j]
            going[3 * k + j].start()
        for copy in range(2 * order, min(2 * order + 2, 8)):
            fetching[copy].wait()
            passing[copy].start()
    for copy in coming[20:23]:
        copy.wait()
    for at in range(0, shard, 128):
        width = min(128, shard - at)
        lanes = pl.ds(at, width)
        new = adamw(
            *[states[15 + j][lanes].reshape(1, width) for j in range(3)],
            grads[4][at // 128 : at // 128 + 1, 0:width],
            NORM_RATE,
            0.0,
        )
        for j in range(3):
            outs[15 + j][lanes] = new[j].reshape(width)
    for copy in going[15:18]:
        copy.start()
    for copy in passing + going:
        copy.wait()


def fused_device(
    images,
    out_grad,
    reduce_weight,
    reduce_moment,
    reduce_second,
    conv_weight,
    conv_moment,
    conv_second,
    squeeze_weight,
    squeeze_moment,
    squeeze_second,
    expand_weight,
    expand_moment,
    expand_second,
    project_weight,
    project_moment,
    project_second,
    norm_params,
    norm_moment,
    norm_second,
):
    n_dp, n_rep = lax.axis_size("dp"), lax.axis_size("rep")
    by_pixel = lambda values: jnp.transpose(values, (1, 2, 0, 3)).reshape(-1, 4, CHANNELS)
    qc = conv_weight.shape[0] // 2
    q1 = reduce_weight.shape[0] // 4
    pe = squeeze_weight.shape[0]
    vmem = pltpu.VMEM
    pixel_form = (SIDE * SIDE, 4, CHANNELS)
    scratch = [
        *[
            vmem(values.shape, F32)
            for values in (
                reduce_weight,
                conv_weight,
                squeeze_weight,
                expand_weight,
                project_weight,
                norm_params,
            )
        ],
        vmem((8, 128), F32),
        vmem(pixel_form, BF16),
        vmem(pixel_form, BF16),
        vmem((ROWS, CHANNELS), BF16),
        vmem((ROWS, CHANNELS), BF16),
        vmem((n_dp // 2, 2, 2, 2, q1, BOTTLE), BF16),
        vmem((n_dp // 2, 2, 2, qc, BOTTLE), BF16),
        vmem((n_dp // 2, 2, pe, 1536), BF16),
        vmem((pe, 1536), BF16),
        vmem((n_dp, 8, 128), F32),
        vmem((40, 128), F32),
        vmem((ROWS, BOTTLE), F32),
        vmem((3, ROWS + 2 * PAD, BOTTLE), F32),
        vmem((2, ROWS, 9 * 128), BF16),
        vmem((ROWS, 512), F32),
        vmem((ROWS, 512), F32),
        vmem((ROWS, BOTTLE), BF16),
        vmem((ROWS, CHANNELS), F32),
        vmem((ROWS, CHANNELS), F32),
        vmem(pixel_form, BF16),
        vmem(pixel_form, F32),
        vmem((ROWS, CHANNELS), BF16),
        vmem((ROWS, BOTTLE), F32),
        vmem((ROWS, 512), F32),
        vmem((ROWS, 512), BF16),
        vmem((ROWS + 2 * PAD, 2 * 9 * 128), F32),
        vmem((ROWS, BOTTLE), F32),
        vmem((ROWS, BOTTLE), BF16),
        vmem((2, 2, BOTTLE // 4, CHANNELS), F32),
        vmem((n_dp, 2, qc, BOTTLE), F32),
        vmem((n_dp, pe, CHANNELS), F32),
        vmem((n_dp, pe, 512), F32),
        vmem((2, 2, BOTTLE // 2, CHANNELS), BF16),
        vmem((3, BOTTLE, CHANNELS // n_dp), F32),
        vmem((2, BOTTLE // 2, CHANNELS // n_dp), F32),
    ]
    direct = n_dp * n_rep
    scratch += [
        vmem((direct if k in DIRECT else 2 * n_rep,) + shape, F32) for k, shape in STATS.items()
    ]
    scratch += [vmem((n_dp // 2,) + shape, F32) for shape in STATS.values()]
    cut = 64
    lanes1 = CHANNELS // n_dp
    half = [
        (2, BOTTLE // 4, CHANNELS),
        (n_dp, 2, cut, 128),
        (n_dp, 2, qc - cut, 128),
        (n_dp, pe, 512),
        (n_dp, pe, 256),
        (2, BOTTLE // 2, CHANNELS),
    ]
    quarter = [
        (BOTTLE // 4, CHANNELS),
        (n_dp, cut, 128),
        (n_dp, qc - cut, 128),
    ]
    owned = [
        (BOTTLE // 4, lanes1),
        (cut, 128),
        (qc - cut, 128),
        (pe, 512),
        (pe, 256),
        (2, BOTTLE // 2, lanes1),
    ]
    final = [(2, 2, BOTTLE // 4, lanes1), (2, qc, BOTTLE), (pe, CHANNELS), (pe, 512)]
    sent = [BF16, BF16, BF16, BF16, F32, BF16]
    scratch += [vmem(shape, F32) for shape in half[:-1]] + [vmem(half[-1], BF16)]
    for kinds in (sent, sent, [F32] * 6, sent, sent):
        scratch += [vmem((n_dp // 2,) + shape, kind) for shape, kind in zip(owned, kinds)]
    scratch += [vmem(shape, BF16) for shape in quarter] * 2
    scratch += [vmem(shape, F32) for shape in (*owned[3:5], owned[5][1:], *owned[3:5])]
    scratch += [vmem(shape, F32) for shape in final]
    dma = pltpu.SemaphoreType.DMA
    scratch += [dma((15,))] + [dma((len(STATS),))] * 4 + [dma((2,))] + [dma((3, 5)), dma((3, 5, n_dp // 2))] + [dma((6, 7))] * 2
    any_space = pl.BlockSpec(memory_space=pl.ANY)
    block_out, images_grad, sum1, sumc, sum3, sume, norm_grads = pl.pallas_call(
        functools.partial(block_kernel, n_dp, n_rep),
        out_shape=[
            jax.ShapeDtypeStruct(pixel_form, BF16),
            jax.ShapeDtypeStruct(pixel_form, F32),
            *[jax.ShapeDtypeStruct(shape, F32) for shape in final],
            jax.ShapeDtypeStruct((8, 128), F32),
        ],
        in_specs=[any_space] * 8,
        out_specs=[any_space] * 7,
        scratch_shapes=scratch,
        compiler_params=pltpu.CompilerParams(
            collective_id=0, has_side_effects=True, vmem_limit_bytes=63 * 1024 * 1024
        ),
    )(
        by_pixel(images),
        by_pixel(out_grad),
        reduce_weight,
        conv_weight,
        squeeze_weight,
        expand_weight,
        project_weight,
        norm_params,
    )
    states = (
        reduce_weight,
        reduce_moment,
        reduce_second,
        conv_weight,
        conv_moment,
        conv_second,
        squeeze_weight,
        squeeze_moment,
        squeeze_second,
        expand_weight,
        expand_moment,
        expand_second,
        project_weight,
        project_moment,
        project_second,
    )
    held = (*states, norm_params, norm_moment, norm_second)
    sums = (
        sum1.reshape(BOTTLE, lanes1),
        sumc.reshape(conv_weight.shape),
        sum3,
        sume,
        norm_grads,
    )
    block_out, images_grad, *updated = pl.pallas_call(
        update_kernel,
        out_shape=[
            jax.ShapeDtypeStruct(pixel_form, BF16),
            jax.ShapeDtypeStruct(pixel_form, F32),
            *[jax.ShapeDtypeStruct(state.shape, F32) for state in held],
        ],
        in_specs=[any_space] * 25,
        out_specs=[any_space] * 20,
        scratch_shapes=[vmem(values.shape, F32) for values in (*sums, *held, *held)]
        + [vmem(pixel_form, BF16), vmem(pixel_form, F32)]
        + [dma((2, 2, 4)), dma((23,)), dma((18,))],
        compiler_params=pltpu.CompilerParams(vmem_limit_bytes=63 * 1024 * 1024),
    )(block_out, images_grad, *sums, *held)
    by_image = lambda values: jnp.transpose(
        values.reshape(SIDE, SIDE, images.shape[0], CHANNELS), (2, 0, 1, 3)
    )
    return (
        by_image(block_out),
        by_image(images_grad),
        *updated,
    )


def solution(mesh):
    placed = (
        P(("dp", "rep"), None, None, None),
        P(("dp", "rep"), None, None, None),
        P("dp", None),
        P("dp", None),
        P("dp", None),
        P("dp", None),
        P("dp", None),
        P("dp", None),
        P("dp", None),
        P("dp", None),
        P("dp", None),
        P("dp", None),
        P("dp", None),
        P("dp", None),
        P("dp", None),
        P("dp", None),
        P("dp", None),
        P("dp"),
        P("dp"),
        P("dp"),
    )
    n_dp, n_rep = mesh.shape["dp"], mesh.shape["rep"]
    whole_tiles = n_rep == 4 and n_dp % 2 == 0 and INNER % (16 * n_dp) == 0
    return jax.shard_map(
        fused_device if whole_tiles else per_device,
        mesh=mesh,
        in_specs=placed,
        out_specs=(
            P(("dp", "rep"), None, None, None),
            P(("dp", "rep"), None, None, None),
            P("dp", None),
            P("dp", None),
            P("dp", None),
            P("dp", None),
            P("dp", None),
            P("dp", None),
            P("dp", None),
            P("dp", None),
            P("dp", None),
            P("dp", None),
            P("dp", None),
            P("dp", None),
            P("dp", None),
            P("dp", None),
            P("dp", None),
            P("dp"),
            P("dp"),
            P("dp"),
        ),
        check_vma=False,
    )
```

```python
import functools
import jax
import jax.numpy as jnp
from jax import lax
from jax.experimental import pallas as pl
from jax.experimental.pallas import tpu as pltpu
from jax.sharding import PartitionSpec as P

CHANNELS = 1024
BOTTLE = 256
INNER = 128
RADIX = 2
SIDE = 14
MICRO = 2
STEP = 10


EPSILON = 1e-05
PRECISE = lax.Precision.HIGHEST
BETA_ONE = 0.9
BETA_TWO = 0.999
ADAM_EPSILON = 1e-08
DECAY = 0.01
NORM_RATE = 0.8
ROWS = 4 * SIDE * SIDE
NORM_WIDTH = 4352


def split_params(packed):
    widths = (
        BOTTLE,
        BOTTLE,
        RADIX * BOTTLE,
        RADIX * BOTTLE,
        INNER,
        INNER,
        RADIX * BOTTLE,
        CHANNELS,
        CHANNELS,
    )
    pieces = []
    offset = 0
    for segment in widths:
        pieces.append(lax.slice_in_dim(packed, offset, offset + segment))
        offset = offset + segment
    return pieces


def silu_slope(values):
    logistic = jax.nn.sigmoid(values)
    return logistic * (1.0 + values * (1.0 - logistic))


def norm_forward(values, gain, bias, count):
    flat = values.reshape(-1, values.shape[-1])
    total, square = lax.psum((jnp.sum(flat, axis=0), jnp.sum(flat * flat, axis=0)), ("dp", "rep"))
    center = total / count
    scale = lax.rsqrt(square / count - center * center + EPSILON)
    normed = (values - center) * scale
    return (normed * gain + bias, normed, scale)


def norm_backward(upstream, normed, scale, gain, count):
    flat_up = upstream.reshape(-1, upstream.shape[-1])
    flat_norm = normed.reshape(-1, normed.shape[-1])
    bias_sum, gain_sum = lax.psum(
        (jnp.sum(flat_up, axis=0), jnp.sum(flat_up * flat_norm, axis=0)), ("dp", "rep")
    )
    downstream = gain * scale * (upstream - bias_sum / count - normed * (gain_sum / count))
    return (downstream, gain_sum, bias_sum)


def patches(active):
    padded = jnp.pad(active, ((0, 0), (1, 1), (1, 1), (0, 0), (0, 0)))
    shifted = [
        padded[:, down_step : down_step + SIDE, side_step : side_step + SIDE]
        for down_step in range(3)
        for side_step in range(3)
    ]
    return jnp.stack(shifted, axis=4)


def unpatch(columns):
    total = jnp.zeros(
        (columns.shape[0], SIDE + 2, SIDE + 2, columns.shape[3], columns.shape[5]), jnp.float32
    )
    for down_step in range(3):
        for side_step in range(3):
            piece = columns[:, :, :, :, 3 * down_step + side_step]
            total = total + jnp.pad(
                piece,
                ((0, 0), (down_step, 2 - down_step), (side_step, 2 - side_step), (0, 0), (0, 0)),
            )
    return total[:, 1 : SIDE + 1, 1 : SIDE + 1]


def adamw(param, moment, second, gradient, rate, decay):
    moment_new = BETA_ONE * moment + (1.0 - BETA_ONE) * gradient
    second_new = BETA_TWO * second + (1.0 - BETA_TWO) * gradient * gradient
    ratio = (
        moment_new
        / (1.0 - BETA_ONE**STEP)
        / (jnp.sqrt(second_new / (1.0 - BETA_TWO**STEP)) + ADAM_EPSILON)
    )
    return (param - rate * (ratio + decay * param), moment_new, second_new)


def per_device(
    images,
    out_grad,
    reduce_weight,
    reduce_moment,
    reduce_second,
    conv_weight,
    conv_moment,
    conv_second,
    squeeze_weight,
    squeeze_moment,
    squeeze_second,
    expand_weight,
    expand_moment,
    expand_second,
    project_weight,
    project_moment,
    project_second,
    norm_params,
    norm_moment,
    norm_second,
):
    bf16 = jnp.bfloat16
    low_reduce = reduce_weight.astype(bf16)
    low_conv = conv_weight.astype(bf16)
    low_squeeze = squeeze_weight.astype(bf16)
    low_expand = expand_weight.astype(bf16)
    low_project = project_weight.astype(bf16)
    low_norm = norm_params.astype(bf16)
    devices = lax.axis_size("dp") * lax.axis_size("rep")
    per_batch = images.shape[0] // MICRO
    pixel_count = float(per_batch * SIDE * SIDE * devices)
    image_count = float(per_batch * devices)
    group_in = BOTTLE // RADIX
    grad_first = jnp.zeros((CHANNELS, BOTTLE), jnp.float32)
    grad_conv = jnp.zeros((RADIX, 9 * group_in, BOTTLE), jnp.float32)
    grad_squeeze = jnp.zeros((BOTTLE, INNER), jnp.float32)
    grad_expand = jnp.zeros((INNER, RADIX * BOTTLE), jnp.float32)
    grad_last = jnp.zeros((BOTTLE, CHANNELS), jnp.float32)
    grad_norms = jnp.zeros(
        (2 * BOTTLE + 3 * RADIX * BOTTLE + 2 * INNER + 2 * CHANNELS,), jnp.float32
    )
    outputs = []
    input_grads = []
    for number in range(MICRO):
        forward_set = (
            lax.all_gather(low_reduce, "dp", axis=0, tiled=True),
            lax.all_gather(low_conv, "dp", axis=0, tiled=True),
            lax.all_gather(low_squeeze, "dp", axis=0, tiled=True),
            lax.all_gather(low_expand, "dp", axis=0, tiled=True),
            lax.all_gather(low_project, "dp", axis=0, tiled=True),
            lax.all_gather(low_norm, "dp", axis=0, tiled=True),
        )
        first, conv, squeeze, expand, last, packed = forward_set
        (
            gain_one,
            bias_one,
            gain_two,
            bias_two,
            gain_pool,
            bias_pool,
            bias_expand,
            gain_three,
            bias_three,
        ) = split_params(packed.astype(jnp.float32))
        batched = images[number * per_batch : (number + 1) * per_batch]
        cotangent = out_grad[number * per_batch : (number + 1) * per_batch]
        reduced = jnp.einsum("nhwc,cb->nhwb", batched, first, preferred_element_type=jnp.float32)
        norm_one, normed_one, scale_one = norm_forward(reduced, gain_one, bias_one, pixel_count)
        active = jax.nn.silu(norm_one).astype(bf16)
        columns = patches(active.reshape(per_batch, SIDE, SIDE, RADIX, group_in)).reshape(
            per_batch * SIDE * SIDE, RADIX, 9 * group_in
        )
        conv_grouped = conv.reshape(RADIX, 9 * group_in, BOTTLE)
        widened = jnp.einsum(
            "prk,rko->pro", columns, conv_grouped, preferred_element_type=jnp.float32
        )
        widened = widened.reshape(per_batch, SIDE, SIDE, RADIX * BOTTLE)
        norm_two, normed_two, scale_two = norm_forward(widened, gain_two, bias_two, pixel_count)
        splits = jax.nn.silu(norm_two).reshape(per_batch, SIDE, SIDE, RADIX, BOTTLE)
        pooled = jnp.sum(jnp.sum(splits, axis=3), axis=(1, 2)) / (SIDE * SIDE)
        squeeze_float = squeeze.astype(jnp.float32)
        expand_float = expand.astype(jnp.float32)
        pre_pool = jnp.dot(pooled, squeeze_float, precision=PRECISE)
        norm_pool, normed_pool, scale_pool = norm_forward(
            pre_pool, gain_pool, bias_pool, image_count
        )
        hidden = jax.nn.silu(norm_pool)
        logits = (jnp.dot(hidden, expand_float, precision=PRECISE) + bias_expand).reshape(
            per_batch, RADIX, BOTTLE
        )
        attention = jax.nn.softmax(logits, axis=1)
        mixed = jnp.sum(splits * attention[:, None, None], axis=3).astype(bf16)
        projected = jnp.einsum("nhwb,bc->nhwc", mixed, last, preferred_element_type=jnp.float32)
        norm_three, normed_three, scale_three = norm_forward(
            projected, gain_three, bias_three, pixel_count
        )
        summed = batched.astype(jnp.float32) + norm_three
        outputs.append(jax.nn.silu(summed).astype(bf16))
        backward_set = (
            lax.all_gather(low_reduce, "dp", axis=0, tiled=True),
            lax.all_gather(low_conv, "dp", axis=0, tiled=True),
            lax.all_gather(low_squeeze, "dp", axis=0, tiled=True),
            lax.all_gather(low_expand, "dp", axis=0, tiled=True),
            lax.all_gather(low_project, "dp", axis=0, tiled=True),
            lax.all_gather(low_norm, "dp", axis=0, tiled=True),
        )
        first, conv, squeeze, expand, last, packed = backward_set
        gains_back = split_params(packed.astype(jnp.float32))
        conv_grouped = conv.reshape(RADIX, 9 * group_in, BOTTLE)
        expand_float = expand.astype(jnp.float32)
        squeeze_float = squeeze.astype(jnp.float32)
        upstream = cotangent.astype(jnp.float32) * silu_slope(summed)
        d_projected, gain_three_grad, bias_three_grad = norm_backward(
            upstream, normed_three, scale_three, gains_back[7], pixel_count
        )
        d_projected_low = d_projected.astype(bf16)
        grad_last = grad_last + jnp.einsum(
            "nhwb,nhwc->bc", mixed, d_projected_low, preferred_element_type=jnp.float32
        )
        d_mixed = jnp.einsum(
            "nhwc,bc->nhwb", d_projected_low, last, preferred_element_type=jnp.float32
        )
        d_splits = d_mixed[:, :, :, None] * attention[:, None, None]
        d_attention = jnp.sum(d_mixed[:, :, :, None] * splits, axis=(1, 2))
        d_logits = attention * (
            d_attention - jnp.sum(attention * d_attention, axis=1, keepdims=True)
        )
        flat_logits = d_logits.reshape(per_batch, RADIX * BOTTLE)
        grad_expand = grad_expand + jnp.dot(hidden.T, flat_logits, precision=PRECISE)
        d_hidden = jnp.dot(flat_logits, expand_float.T, precision=PRECISE)
        d_pool_norm = d_hidden * silu_slope(norm_pool)
        pool_bias_sum, pool_gain_sum, expand_bias_sum = lax.psum(
            (
                jnp.sum(d_pool_norm, axis=0),
                jnp.sum(d_pool_norm * normed_pool, axis=0),
                jnp.sum(flat_logits, axis=0),
            ),
            ("dp", "rep"),
        )
        d_pre_pool = (
            gains_back[4]
            * scale_pool
            * (
                d_pool_norm
                - pool_bias_sum / image_count
                - normed_pool * (pool_gain_sum / image_count)
            )
        )
        grad_squeeze = grad_squeeze + jnp.dot(pooled.T, d_pre_pool, precision=PRECISE)
        d_pooled = jnp.dot(d_pre_pool, squeeze_float.T, precision=PRECISE)
        d_splits = d_splits + (d_pooled / (SIDE * SIDE))[:, None, None, None, :]
        d_norm_two = d_splits.reshape(per_batch, SIDE, SIDE, RADIX * BOTTLE) * silu_slope(norm_two)
        d_widened, gain_two_grad, bias_two_grad = norm_backward(
            d_norm_two, normed_two, scale_two, gains_back[2], pixel_count
        )
        d_widened_low = d_widened.astype(bf16).reshape(per_batch * SIDE * SIDE, RADIX, BOTTLE)
        grad_conv = grad_conv + jnp.einsum(
            "prk,pro->rko", columns, d_widened_low, preferred_element_type=jnp.float32
        )
        d_columns = jnp.einsum(
            "pro,rko->prk", d_widened_low, conv_grouped, preferred_element_type=jnp.float32
        )
        d_active = unpatch(d_columns.reshape(per_batch, SIDE, SIDE, RADIX, 9, group_in)).reshape(
            per_batch, SIDE, SIDE, BOTTLE
        )
        d_norm_one = d_active * silu_slope(norm_one)
        d_reduced, gain_one_grad, bias_one_grad = norm_backward(
            d_norm_one, normed_one, scale_one, gains_back[0], pixel_count
        )
        d_reduced_low = d_reduced.astype(bf16)
        grad_first = grad_first + jnp.einsum(
            "nhwc,nhwb->cb", batched, d_reduced_low, preferred_element_type=jnp.float32
        )
        input_grads.append(
            upstream
            + jnp.einsum("nhwb,cb->nhwc", d_reduced_low, first, preferred_element_type=jnp.float32)
        )
        grad_norms = grad_norms + jnp.concatenate(
            [
                gain_one_grad,
                bias_one_grad,
                gain_two_grad,
                bias_two_grad,
                pool_gain_sum,
                pool_bias_sum,
                expand_bias_sum,
                gain_three_grad,
                bias_three_grad,
            ]
        )
    grad_conv = grad_conv.reshape(9 * BOTTLE, BOTTLE)
    partial_value = (
        lax.psum_scatter(grad_first, "dp", scatter_dimension=0, tiled=True),
        lax.psum_scatter(grad_conv, "dp", scatter_dimension=0, tiled=True),
        lax.psum_scatter(grad_squeeze, "dp", scatter_dimension=0, tiled=True),
        lax.psum_scatter(grad_expand, "dp", scatter_dimension=0, tiled=True),
        lax.psum_scatter(grad_last, "dp", scatter_dimension=0, tiled=True),
    )
    owned = lax.psum(
        (partial_value[0], partial_value[1], partial_value[2], partial_value[3], partial_value[4]),
        "rep",
    )
    shard_length = norm_params.shape[0]
    norm_grad_owned = lax.dynamic_slice_in_dim(
        grad_norms, lax.axis_index("dp") * shard_length, shard_length
    )
    reduce_new = adamw(
        reduce_weight, reduce_moment, reduce_second, owned[0], 2.0 * CHANNELS ** (-0.5), DECAY
    )
    conv_new = adamw(
        conv_weight,
        conv_moment,
        conv_second,
        owned[1],
        2.0 * (9 * BOTTLE // RADIX) ** (-0.5),
        DECAY,
    )
    squeeze_new = adamw(
        squeeze_weight, squeeze_moment, squeeze_second, owned[2], 2.0 * BOTTLE ** (-0.5), DECAY
    )
    expand_new = adamw(
        expand_weight, expand_moment, expand_second, owned[3], 2.0 * (INNER // 8) ** (-0.5), DECAY
    )
    project_new = adamw(
        project_weight, project_moment, project_second, owned[4], 2.0 * BOTTLE ** (-0.5), DECAY
    )
    norm_new = adamw(norm_params, norm_moment, norm_second, norm_grad_owned, NORM_RATE, 0.0)
    return (
        jnp.concatenate(outputs, axis=0),
        jnp.concatenate(input_grads, axis=0),
        reduce_new[0],
        reduce_new[1],
        reduce_new[2],
        conv_new[0],
        conv_new[1],
        conv_new[2],
        squeeze_new[0],
        squeeze_new[1],
        squeeze_new[2],
        expand_new[0],
        expand_new[1],
        expand_new[2],
        project_new[0],
        project_new[1],
        project_new[2],
        norm_new[0],
        norm_new[1],
        norm_new[2],
    )


MESH = pl.DeviceIdType.MESH
PAD = 64
CHUNK = 112
F32 = jnp.float32
BF16 = jnp.bfloat16
STATS = {
    "reduced": (4, 256),
    "widened0": (4, 256),
    "widened1": (4, 256),
    "pool": (4, 128),
    "images": (16, 128),
    "projected0": (4, 512),
    "projected1": (4, 512),
    "back_projected0": (4, 512),
    "back_projected1": (4, 512),
    "back_pool": (4, 128),
    "back_widened": (8, 512),
    "back_reduced0": (4, 128),
    "back_reduced1": (4, 128),
}
DIRECT = ("reduced", "pool", "back_pool", "back_reduced0", "back_reduced1")


def sigmoid(values):
    return 0.5 * jnp.tanh(0.5 * values) + 0.5


def row_ids(width):
    return lax.broadcasted_iota(jnp.int32, (8, width), 0)


def image_sum(rows):
    return rows + pltpu.roll(rows, 4, 0)


def pair_sum(rows):
    even = row_ids(rows.shape[1]) % 2 == 0
    return rows + jnp.where(even, pltpu.roll(rows, 7, 0), pltpu.roll(rows, 1, 0))


def micro_sum(rows):
    return pair_sum(image_sum(rows))


def stack_sums(first, second):
    rows = (first[0:1], first[2:3], second[0:1], second[2:3])
    return jnp.concatenate(rows, axis=0)


def unstack_sums(stacked):
    earlier = lax.rem(row_ids(stacked.shape[1]), 4) < 2
    return tuple(jnp.where(earlier, stacked[k : k + 1], stacked[k + 1 : k + 2]) for k in (0, 2))


def norm_terms(total, square, gain, bias, count):
    center = total * (1.0 / count)
    scale = lax.rsqrt(square * (1.0 / count) - center * center + EPSILON)
    slope = scale * gain
    return center, scale, slope, bias - center * slope


def back_terms(center, scale, slope, bias_sum, gain_sum, count):
    by_value = -slope * scale * (gain_sum * (1.0 / count))
    constant = -slope * (bias_sum * (1.0 / count)) - by_value * center
    return by_value, constant


def tdot(left, right):
    return lax.dot_general(left, right, (((0,), (0,)), ((), ())), preferred_element_type=F32)


def dot_t(left, right):
    return lax.dot_general(left, right, (((1,), (1,)), ((), ())), preferred_element_type=F32)


def in_parts(values, parts):
    found = []
    for _ in range(parts):
        rounded = values.astype(BF16).astype(F32)
        found.append(rounded)
        values = values - rounded
    return found


def exact_dot(left, right, transposed):
    stacked = jnp.concatenate(in_parts(left, 3), axis=0).astype(BF16)
    wide = dot_t(stacked, right) if transposed else jnp.dot(stacked, right, preferred_element_type=F32)
    return wide[0:8] + wide[8:16] + wide[16:24]


def row_dot(left, right):
    high, low = in_parts(left, 2)
    other_high, other_low = in_parts(right, 2)
    return tdot(
        jnp.concatenate([high, high, low, low], axis=0).astype(BF16),
        jnp.concatenate([other_high, other_low, other_high, other_low], axis=0).astype(BF16),
    )


def image_dot(left, right):
    return row_dot(jnp.where(row_ids(left.shape[1]) < 4, left, 0.0), right)


def block_kernel(
    n_dp,
    n_rep,
    x_hbm,
    gy_hbm,
    w1_hbm,
    wc_hbm,
    sq_hbm,
    ex_hbm,
    w3_hbm,
    np_hbm,
    bo_hbm,
    dx_hbm,
    f1_hbm,
    fc_hbm,
    f3_hbm,
    fe_hbm,
    gn_hbm,
    w1_own,
    wc_own,
    sq_own,
    ex_own,
    w3_own,
    np_own,
    gn_out,
    x4,
    gy4,
    x_v,
    gy_v,
    fw1,
    fwc,
    fpe,
    pe_own,
    np_slots,
    np_full,
    red,
    act,
    columns,
    wid,
    splits,
    mixed,
    proj,
    up,
    bo4,
    dx4,
    dproj,
    d_mixed,
    dn2,
    dwid,
    dcol,
    dn1,
    dred,
    g1,
    filters,
    gc_flat,
    g3,
    ge,
    gb,
    fix,
    back_own,
    *rest,
):
    n_ar = len(STATS)
    order = {name: k for k, name in enumerate(STATS)}
    ar_slots_a = dict(zip(STATS, rest[0:n_ar]))
    ar_slots_b = dict(zip(STATS, rest[n_ar : 2 * n_ar]))
    rest = rest[2 * n_ar :]
    r1s, xs, xr, acc, zs, zr = (rest[6 * i : 6 * i + 6] for i in range(6))
    ys, r2s, hr, hs, fs = rest[36:39], rest[39:42], rest[42:45], rest[45:47], rest[47:51]
    rest = rest[51:]
    local_sem, ar_send_a, ar_recv_a, ar_send_b, ar_recv_b, np_sems, ws, wr, gs, gr = rest

    dp = lax.axis_index("dp")
    rep = lax.axis_index("rep")
    core = lax.rem(rep, 2)
    half_y = lax.div(rep, 2)
    planes = n_dp // 2
    plane_size = 2 * n_rep
    plane = lax.div(dp, 2)
    in_plane = lax.rem(dp, 2) * n_rep + rep
    sibling = (dp, half_y * 2 + (1 - core))
    across = (dp, (1 - half_y) * 2 + core)
    pixels = float(SIDE * SIDE * 2 * n_dp * n_rep)
    pictures = float(2 * n_dp * n_rep)

    x = lax.rem(dp, 2)
    if planes == 4:
        upper = lax.div(plane, 2)
        other_planes = [3 - 3 * upper, 2 - upper, 1 - plane + 4 * upper]
    else:
        other_planes = [lax.rem(plane + step, planes) for step in range(1, planes)]
    flips = ((1, 1, 1), (1, 1, 0), (1, 0, 1), (1, 0, 0), (0, 1, 1), (0, 1, 0), (0, 0, 1), (0, 0, 0))

    def of_flip(z, flip):
        there = [1 - own if turn else own for own, turn in zip((x, half_y, core), flip)]
        return (z * 2 + there[0], there[1] * 2 + there[2])

    plane_peers = [of_flip(plane, flip) for flip in flips[:-1]]
    column_peers = [of_flip(z, flips[-1]) for z in other_planes]
    owner_peers = [of_flip(z, flip) for z in other_planes for flip in (flips[3], flips[7])]
    owner_peers += [of_flip(plane, flips[3])]
    all_peers = [of_flip(z, flip) for z in other_planes for flip in flips] + plane_peers
    me, everyone = dp * n_rep + rep, n_dp * n_rep
    x_peer = of_flip(plane, flips[3])

    def remote(src, dst, send_sem, recv_sem, device):
        return pltpu.make_async_remote_copy(
            src_ref=src,
            dst_ref=dst,
            send_sem=send_sem,
            recv_sem=recv_sem,
            device_id=device,
            device_id_type=MESH,
        )

    def send_all(ref, send_sem, recv_sem, peers):
        for device in peers:
            remote(ref, ref, send_sem, recv_sem, device).start()

    def wait_bytes(ref, sem):
        pltpu.make_async_copy(ref, ref, sem).wait()

    def over_rows(body, init):
        def step(index, carry):
            return body(pl.multiple_of(index * CHUNK, CHUNK), carry)

        return lax.fori_loop(0, ROWS // CHUNK, step, init)

    def over_blocks(count, width, body):
        def step(index, carry):
            body(index, pl.ds(pl.multiple_of(index * width, width), width))
            return carry

        lax.fori_loop(0, count, step, 0)

    def grouped(values):
        return values.reshape(CHUNK // 8, 8, values.shape[-1])

    def by_four(values):
        return flat(values).reshape(CHUNK // 4, 4, values.shape[-1])

    def flat(values):
        return values.reshape(CHUNK, values.shape[-1])

    own_copies = [
        pltpu.make_async_copy(source, target, local_sem.at[4 + k])
        for k, (source, target) in enumerate(
            (
                (w1_hbm, w1_own),
                (np_hbm, np_own),
                (wc_hbm, wc_own),
                (w3_hbm, w3_own),
                (sq_hbm, sq_own),
                (ex_hbm, ex_own),
            )
        )
    ]
    for copy in own_copies:
        copy.start()
    x_copy = pltpu.make_async_copy(x_hbm, x4, local_sem.at[0])
    gy_copy = pltpu.make_async_copy(gy_hbm, gy4, local_sem.at[1])
    x_copy.start()
    barrier = pltpu.get_barrier_semaphore()
    for device in all_peers:
        pl.semaphore_signal(barrier, inc=1, device_id=device, device_id_type=MESH)

    def lanes_of(index, width):
        return pl.ds(pl.multiple_of(index * width, 128), width)

    part = core * 2 + half_y
    own_copies[0].wait()
    q1 = w1_own.shape[0] // 4
    fw1[plane, x, core, half_y] = w1_own[pl.ds(pl.multiple_of(part * q1, q1), q1), :].astype(BF16)

    pl.semaphore_wait(barrier, everyone - 1)

    def region(which, z, xs, c, y):
        return (
            lambda: fw1.at[z, xs, c, y],
            lambda: fwc.at[z, xs, y, :, lanes_of(c, 128)],
            lambda: fpe.at[z, xs, :, lanes_of(c, fpe.shape[3] // 2)],
        )[which]()

    both_x = pl.ds(0, 2)
    near_planes = [plane] + other_planes[::-1]
    split_over_y = (True, True, False)

    def pass_on(which, ref, stage, z, device):
        remote(ref, ref, ws.at[which, stage], wr.at[which, stage, z], device).start()

    def gather_out(which):
        mine = region(which, plane, x, core, half_y)
        for device in column_peers:
            pass_on(which, mine, 0, plane, device)
        pass_on(which, mine, 1, plane, x_peer)

    def gather_x(which, k):
        z = near_planes[k]
        mine = region(which, z, x, core, half_y)
        wait_bytes(mine, wr.at[which, 0, z])
        pass_on(which, mine, 1, z, x_peer)

    def gather_y(which, k):
        z = near_planes[k]
        wait_bytes(region(which, z, 1 - x, core, half_y), wr.at[which, 1, z])
        mine = region(which, z, both_x, core, half_y)
        if split_over_y[which]:
            pass_on(which, mine, 2, z, across)
        pass_on(which, mine, 3, z, sibling)

    def gather_hand(which, k):
        z = near_planes[k]
        theirs = region(which, z, both_x, core, 1 - half_y)
        wait_bytes(theirs, wr.at[which, 2, z])
        pass_on(which, theirs, 4, z, sibling)

    def gather_end(which):
        for z in near_planes:
            wait_bytes(region(which, z, both_x, 1 - core, half_y), wr.at[which, 3, z])
            if split_over_y[which]:
                wait_bytes(region(which, z, both_x, 1 - core, 1 - half_y), wr.at[which, 4, z])

    def gather_sent(which):
        wait_bytes(region(which, pl.ds(0, planes - 1), x, core, half_y), ws.at[which, 0])
        wait_bytes(region(which, pl.ds(0, planes), x, core, half_y), ws.at[which, 1])
        for stage in (2, 3, 4) if split_over_y[which] else (3,):
            wait_bytes(region(which, pl.ds(0, planes), both_x, core, half_y), ws.at[which, stage])

    def to_rows(source, target):
        def body(index, carry):
            values = source[pl.ds(index * (CHUNK // 4), CHUNK // 4)].astype(F32)
            row = pl.multiple_of(index * CHUNK, CHUNK)
            target[pl.ds(row, CHUNK), :] = values.reshape(CHUNK, CHANNELS).astype(BF16)
            return carry

        lax.fori_loop(0, ROWS // CHUNK, body, 0)

    gather_out(0)

    own_copies[1].wait()
    shard = np_own.shape[0]
    lanes_id = lax.broadcasted_iota(jnp.int32, (8, 128), 1)
    turn = lax.rem(shard * dp, 128)
    np_rows = []
    for at in range(0, shard, 128):
        width = min(128, shard - at)
        piece_row = np_own[pl.ds(at, width)].reshape(1, width)
        if width < 128:
            piece_row = jnp.concatenate([piece_row, jnp.zeros((1, 128 - width), F32)], axis=1)
        np_rows.append(piece_row)
    np_rows.append(jnp.zeros((8 - len(np_rows), 128), F32))
    np_turned = jnp.concatenate(np_rows, axis=0).astype(BF16).astype(F32)
    np_turned = pltpu.roll(np_turned, turn, 1)
    np_slots[dp] = jnp.where(lanes_id < turn, pltpu.roll(np_turned, 1, 0), np_turned)
    send_all(np_slots.at[dp], np_sems.at[0], np_sems.at[1], owner_peers)
    own_copies[2].wait()
    qc = wc_own.shape[0] // 2
    fwc[plane, x, half_y, :, lanes_of(core, 128)] = wc_own[
        pl.ds(pl.multiple_of(half_y * qc, qc), qc), lanes_of(core, 128)
    ].astype(BF16)
    gather_out(1)
    for copy in own_copies[3:]:
        copy.wait()
    ex_rows = ex_own.shape[0]
    pe_own[:, 0:CHANNELS] = w3_own[...].astype(BF16)
    pe_own[:, 1024:1152] = sq_own[...].astype(BF16)
    pe_own[0:ex_rows, 1152:1408] = ex_own[:, 0:256].astype(BF16)
    pe_own[ex_rows : 2 * ex_rows, 1152:1408] = ex_own[:, 256:512].astype(BF16)
    pe_own[:, 1408:1536] = jnp.zeros((2 * ex_rows, 128), BF16)
    fpe[plane, x, :, lanes_of(core, 768)] = pe_own[:, lanes_of(core, 768)]
    gather_x(0, 1)
    gather_y(0, 0)
    gather_x(0, 2)
    gather_y(0, 1)
    gy_copy.start()
    x_copy.wait()
    to_rows(x4, x_v)
    gather_hand(0, 0)
    gather_x(0, 3)
    gather_y(0, 2)
    gather_hand(0, 1)
    gather_y(0, 3)
    gather_x(1, 1)
    gather_x(1, 2)
    gather_x(1, 3)
    gather_out(2)
    zero_rows = jnp.zeros((PAD, BOTTLE), F32)
    for side in range(3):
        act[side, 0:PAD, :] = zero_rows
        act[side, PAD + ROWS : 2 * PAD + ROWS, :] = zero_rows
    for lane_block in range(9):
        dcol[0:PAD, lane_block * 256 : lane_block * 256 + 256] = zero_rows
        dcol[PAD + ROWS : 2 * PAD + ROWS, lane_block * 256 : lane_block * 256 + 256] = zero_rows

    gather_hand(0, 2)
    gather_hand(0, 3)
    for k in range(4):
        gather_y(1, k)

    def sum_start(k, payload):
        if k in DIRECT:
            ar_slots_a[k][me] = payload
            send_all(ar_slots_a[k].at[me], ar_send_a.at[order[k]], ar_recv_a.at[order[k]], all_peers)
        else:
            ar_slots_a[k][in_plane] = payload
            send_all(ar_slots_a[k].at[in_plane], ar_send_a.at[order[k]], ar_recv_a.at[order[k]], plane_peers)

    def sum_slots(slots, count):
        sums = [slots[slot] for slot in range(count)]
        while len(sums) > 1:
            sums = [sums[i] + sums[i + 1] for i in range(0, len(sums), 2)]
        return sums[0]

    def sum_turn(k):
        if k in DIRECT:
            return
        wait_bytes(ar_slots_a[k].at[pl.ds(0, plane_size - 1)], ar_recv_a.at[order[k]])
        ar_slots_b[k][plane] = sum_slots(ar_slots_a[k], plane_size)
        send_all(ar_slots_b[k].at[plane], ar_send_b.at[order[k]], ar_recv_b.at[order[k]], column_peers)

    def sum_end(k):
        if k in DIRECT:
            wait_bytes(ar_slots_a[k].at[pl.ds(0, everyone - 1)], ar_recv_a.at[order[k]])
            return sum_slots(ar_slots_a[k], everyone)
        wait_bytes(ar_slots_b[k].at[pl.ds(0, planes - 1)], ar_recv_b.at[order[k]])
        return sum_slots(ar_slots_b[k], planes)

    gc = gc_flat.reshape(n_dp, 2, gc_flat.shape[0] // n_dp // 2, BOTTLE)
    cut = 64
    conv_rows = {1: pl.ds(0, cut), 2: pl.ds(cut, gc.shape[2] - cut)}
    grads = (g1, gc, gc, g3, ge, gb)
    turned_kinds = (0, 5)
    split_kinds = (0, 1, 2)

    def half_of(which, c):
        ref = grads[which]
        if which in turned_kinds:
            return ref.at[c]
        if which in conv_rows:
            return ref.at[:, :, conv_rows[which], lanes_of(c, 128)]
        return ref.at[:, :, lanes_of(c, (512, 256)[which - 3])]

    def y_part(which, ref, y):
        return ref.at[y] if which == 0 else ref.at[:, y]

    def of_owner(which, ref, d):
        if which == 0:
            return ref.at[:, lanes_of(d, CHANNELS // n_dp)]
        if which == 5:
            return ref.at[:, :, lanes_of(d, CHANNELS // n_dp)]
        return ref.at[d]

    def in_blocks(which, body):
        if which == 0:
            count = 4
            rows = g1.shape[2] // count
            block = lambda index: pl.ds(pl.multiple_of(index * rows, rows), rows)
        else:
            count, block = n_dp, lambda index: index

        def step(index, carry):
            body(block(index))
            return carry

        lax.fori_loop(0, count, step, 0)

    def stage(which, number, src, dst, device):
        remote(src, dst, gs.at[which, number], gr.at[which, number], device).start()

    def reduce_core(which):
        stage(which, 0, half_of(which, 1 - core), r1s[which], sibling)

    def reduce_y(which):
        wait_bytes(r1s[which], gr.at[which, 0])
        half = half_of(which, core)
        away, mine = y_part(which, half, 1 - half_y), y_part(which, half, half_y)
        there, here = y_part(which, r1s[which], 1 - half_y), y_part(which, r1s[which], half_y)

        def add_away(at):
            ys[which][at] = (away[at] + there[at]).astype(BF16)

        in_blocks(which, add_away)
        stage(which, 1, ys[which], r2s[which], across)

        def add_mine(at):
            mine[at] = mine[at] + here[at]

        in_blocks(which, add_mine)

    def reduce_x(which):
        if which in split_kinds:
            wait_bytes(r2s[which], gr.at[which, 1])
            mine = y_part(which, half_of(which, core), half_y)
            other = r2s[which]
        else:
            wait_bytes(r1s[which], gr.at[which, 0])
            mine, other = half_of(which, core), r1s[which]

        def summed(d):
            first, second = of_owner(which, mine, d), of_owner(which, other, d)
            return first[...].astype(F32) + second[...].astype(F32)

        def send_one(z, carry):
            xs[which][z] = summed(2 * z + 1 - x).astype(xs[which].dtype)
            return carry

        def keep_one(z, carry):
            acc[which][z] = summed(2 * z + x)
            return carry

        lax.fori_loop(0, planes, send_one, 0)
        stage(which, 2, xs[which], xr[which], x_peer)
        lax.fori_loop(0, planes, keep_one, 0)

    def reduce_z(which):
        wait_bytes(xr[which], gr.at[which, 2])
        def add_one(z, carry):
            total = acc[which][z] + xr[which][z].astype(F32)
            acc[which][z] = total
            zs[which][z] = total.astype(zs[which].dtype)
            return carry

        lax.fori_loop(0, planes, add_one, 0)
        zr[which][plane] = jnp.zeros(zr[which].shape[1:], zr[which].dtype)
        for z, device in zip(other_planes, column_peers):
            stage(which, 3, zs[which].at[z], zr[which].at[plane], device)

    def owner_total(which):
        wait_bytes(zr[which].at[pl.ds(0, planes - 1)], gr.at[which, 3])
        total = acc[which][plane]
        for z in range(planes):
            total = total + zr[which][z].astype(F32)
        return total

    def final_part(which, c, y):
        if which == 0:
            return fs[0].at[c, y]
        if which in conv_rows:
            return fs[1].at[y, conv_rows[which], lanes_of(c, 128)]
        return fs[which - 1].at[:, lanes_of(c, (512, 256)[which - 3])]

    def reduce_across(which):
        total = owner_total(which)
        if which == 5:
            back_own[...] = total
            stage(which, 4, back_own.at[1 - half_y], hr[which - 3], across)
        else:
            hs[which - 3][...] = total
            stage(which, 4, hs[which - 3], hr[which - 3], across)

    def reduce_spread(which):
        if which in split_kinds:
            total = owner_total(which)
        else:
            wait_bytes(hr[which - 3], gr.at[which, 4])
            total = hs[which - 3][...] + hr[which - 3][...]
        if which == 0:
            wait_bytes(hr[2], gr.at[5, 4])
            back = back_own[half_y] + hr[2][...]
            rows = pl.ds(pl.multiple_of(part * (BOTTLE // 4), BOTTLE // 4), BOTTLE // 4)
            total = total - fix[0, rows, :]
            for m in range(2):
                own_back = back[m * (BOTTLE // 4) : (m + 1) * (BOTTLE // 4)]
                total = total - fix[1 + m, rows, :] * own_back
        mine = final_part(which, core, half_y)
        mine[...] = total
        if which in split_kinds:
            stage(which, 4, mine, mine, across)
        stage(which, 5, mine, mine, sibling)

    def reduce_hand(which):
        theirs = final_part(which, core, 1 - half_y)
        wait_bytes(theirs, gr.at[which, 4])
        stage(which, 6, theirs, theirs, sibling)

    def reduce_end(which):
        wait_bytes(final_part(which, 1 - core, half_y), gr.at[which, 5])
        if which in split_kinds:
            wait_bytes(final_part(which, 1 - core, 1 - half_y), gr.at[which, 6])

    def reduce_sent(which):
        wait_bytes(r1s[which], gs.at[which, 0])
        wait_bytes(xs[which], gs.at[which, 2])
        wait_bytes(zs[which].at[pl.ds(0, planes - 1)], gs.at[which, 3])
        if which in split_kinds:
            wait_bytes(ys[which], gs.at[which, 1])
            for number in (4, 5, 6):
                wait_bytes(final_part(which, core, half_y), gs.at[which, number])
        else:
            wait_bytes(hr[which - 3], gs.at[which, 4])
            if which != 5:
                wait_bytes(final_part(which, core, half_y), gs.at[which, 5])

    gather_end(0)
    depth = CHANNELS // planes
    red[...] = jnp.zeros(red.shape, F32)

    def reduce_block(z, at):
        red[...] += jnp.dot(
            x_v[:, at], fw1[z].reshape(depth, BOTTLE), preferred_element_type=F32
        )

    over_blocks(planes, depth, reduce_block)

    def sums_of(ref, start, width):
        def body(row, carry):
            values = grouped(ref[pl.ds(row, CHUNK), start : start + width])
            return carry[0] + jnp.sum(values, axis=0), carry[1] + jnp.sum(values * values, axis=0)

        zero = jnp.zeros((8, width), F32)
        return over_rows(body, (zero, zero))

    def joined(found):
        both = [jnp.concatenate(item, axis=1) for item in zip(*found)]
        return stack_sums(micro_sum(both[0]), micro_sum(both[1]))

    def both_sums(name):
        return unstack_sums(sum_end(name))

    sum_start("reduced", joined([sums_of(red, 0, 256)]))

    gy_copy.wait()
    to_rows(gy4, gy_v)
    wait_bytes(np_slots.at[pl.ds(0, n_dp - 1)], np_sems.at[1])
    np_full[...] = jnp.zeros(np_full.shape, F32)
    for d in range(n_dp):
        at = shard * d // 128
        np_full[at : at + 8, :] = np_full[at : at + 8, :] + np_slots[d]

    def vector(at, width):
        rows = [np_full[at // 128 + k : at // 128 + k + 1, :] for k in range(width // 128)]
        return jnp.concatenate(rows, axis=1) if len(rows) > 1 else rows[0]

    gain_one, bias_one = vector(0, 256), vector(256, 256)
    gain_two, bias_two = vector(512, 512), vector(1024, 512)
    gain_pool, bias_pool = vector(1536, 128), vector(1664, 128)
    bias_expand = vector(1792, 512)
    gain_three, bias_three = vector(2304, 1024), vector(3328, 1024)

    for k in range(1, 4):
        gather_x(2, k)
    total, square = both_sums("reduced")
    center1, scale1, mul1, add1 = norm_terms(total, square, gain_one, bias_one, pixels)

    def make_active(row, carry):
        turned = grouped(red[pl.ds(row, CHUNK), :]) * mul1 + add1
        act[1, pl.ds(PAD + row, CHUNK), :] = flat(turned * sigmoid(turned))
        return carry

    over_rows(make_active, 0)
    for k in range(4):
        gather_hand(1, k)
    place = lax.rem(lax.broadcasted_iota(jnp.int32, (CHUNK, BOTTLE), 0) // 4, SIDE)
    not_last = place != SIDE - 1
    not_first = place != 0

    def beside(side, row, distance, lanes=slice(0, BOTTLE)):
        near = act[side, pl.ds(PAD + row - 8, CHUNK + 16), lanes]
        return pltpu.roll(near, (CHUNK + 16 - distance) % (CHUNK + 16), 0)[8 : 8 + CHUNK]

    def shift_active(row, carry):
        act[2, pl.ds(PAD + row, CHUNK), :] = jnp.where(not_last, beside(1, row, 4), 0.0)
        act[0, pl.ds(PAD + row, CHUNK), :] = jnp.where(not_first, beside(1, row, -4), 0.0)
        return carry

    over_rows(shift_active, 0)

    def make_columns(row, carry):
        for tap in range(9):
            down, side = tap // 3 - 1, tap % 3
            values = act[side, pl.ds(PAD + row + 56 * down, CHUNK), :].astype(BF16)
            columns[0, pl.ds(row, CHUNK), tap * 128 : tap * 128 + 128] = values[:, 0:128]
            columns[1, pl.ds(row, CHUNK), tap * 128 : tap * 128 + 128] = values[:, 128:256]
        return carry

    over_rows(make_columns, 0)
    gather_end(1)
    own_half = n_dp // 2
    own_planes = planes // 2

    for group in range(2):
        filters[group] = fwc[group * own_planes : (group + 1) * own_planes].reshape(9 * 128, BOTTLE)
    halves2 = (slice(0, 256), slice(256, 512))
    for group, lanes in enumerate(halves2):
        wid[:, lanes] = jnp.zeros((ROWS, 256), F32)

        def conv_block(k, at):
            wid[:, lanes] += jnp.dot(
                columns[group, :, at], filters[group, at, :], preferred_element_type=F32
            )

        over_blocks(3, 384, conv_block)
        sum_start(f"widened{group}", joined([sums_of(wid, group * 256, 256)]))
    for k in range(4):
        gather_y(2, k)
    sum_turn("widened0")
    sum_turn("widened1")

    norm2 = []
    pooled = jnp.zeros((8, BOTTLE), F32)
    for group, lanes in enumerate(halves2):
        total, square = both_sums(f"widened{group}")
        norm2.append(norm_terms(total, square, gain_two[:, lanes], bias_two[:, lanes], pixels))
        m2, a2 = norm2[group][2:4]

        def make_splits(row, carry):
            turned = grouped(wid[pl.ds(row, CHUNK), lanes]) * m2 + a2
            values = turned * sigmoid(turned)
            splits[pl.ds(row, CHUNK), lanes] = flat(values)
            return carry + jnp.sum(values, axis=0)

        pooled = over_rows(make_splits, pooled)
    pooled = image_sum(pooled) * (1.0 / (SIDE * SIDE))
    gather_end(2)
    last = fpe[:, :, :, 0:CHANNELS].reshape(BOTTLE, CHANNELS)
    squeeze = fpe[:, :, :, 1024:1152].reshape(BOTTLE, INNER)
    ex_both = fpe[:, :, :, 1152:1408]
    expand = jnp.concatenate(
        [
            ex_both[:, :, 0:ex_rows].reshape(INNER, 256),
            ex_both[:, :, ex_rows : 2 * ex_rows].reshape(INNER, 256),
        ],
        axis=1,
    )
    pre_pool = exact_dot(pooled, squeeze, False)
    sum_start("pool", stack_sums(pair_sum(pre_pool), pair_sum(pre_pool * pre_pool)))
    first_micro = lax.rem(row_ids(BOTTLE), 4) < 2

    def make_normed(row, carry):
        rows = pl.ds(row, CHUNK)
        normed = (grouped(red[rows, :]) - center1) * scale1
        dwid[rows, 0:256] = flat(jnp.where(first_micro, normed, 0.0)).astype(BF16)
        dwid[rows, 256:512] = flat(jnp.where(first_micro, 0.0, normed)).astype(BF16)
        return carry + jnp.sum(grouped(x_v[rows, :].astype(F32)), axis=0)

    image_sums = micro_sum(over_rows(make_normed, jnp.zeros((8, CHANNELS), F32)))
    sum_start(
        "images",
        jnp.concatenate(
            [
                image_sums[2 * m : 2 * m + 1, at : at + 128]
                for m in range(2)
                for at in range(0, CHANNELS, 128)
            ],
            axis=0,
        ),
    )
    def normed_block(m, at):
        found = tdot(dwid[:, at], x_v[...]).astype(BF16)
        rows = pl.ds(pl.multiple_of(m * (BOTTLE // 4), BOTTLE // 4), BOTTLE // 4)
        gb[:, :, rows, :] = found.reshape(2, 2, BOTTLE // 4, CHANNELS)

    over_blocks(2, 256, normed_block)
    reduce_core(5)
    total, square = unstack_sums(sum_end("pool"))
    center_p, scale_p, mul_p, add_p = norm_terms(total, square, gain_pool, bias_pool, pictures)
    normed_p = (pre_pool - center_p) * scale_p
    norm_p = pre_pool * mul_p + add_p
    gate_p = sigmoid(norm_p)
    hidden = norm_p * gate_p
    slope_p = gate_p * (1.0 + norm_p * (1.0 - gate_p))
    logits = exact_dot(hidden, expand, False) + bias_expand
    left, right = logits[:, 0:256], logits[:, 256:512]
    most = jnp.maximum(left, right)
    left, right = jnp.exp(left - most), jnp.exp(right - most)
    att0 = left / (left + right)
    att1 = right / (left + right)

    def make_mixed(row, carry):
        rows = pl.ds(row, CHUNK)
        values = grouped(splits[rows, 0:256]) * att0 + grouped(splits[rows, 256:512]) * att1
        mixed[rows, :] = flat(values).astype(BF16)
        return carry

    over_rows(make_mixed, 0)
    halves3 = (slice(0, 512), slice(512, 1024))
    blocks3 = [[slice(512 * h + k, 512 * h + k + 256) for k in (0, 256)] for h in range(2)]
    for half, lanes in enumerate(halves3):
        def project_block(k, at):
            at = pl.ds(pl.multiple_of(512 * half + 256 * k, 256), 256)
            proj[:, at] = jnp.dot(
                mixed[...], fpe[:, :, :, at].reshape(BOTTLE, 256), preferred_element_type=F32
            )

        over_blocks(2, 256, project_block)
        sum_start(
            f"projected{half}", joined([sums_of(proj, 512 * half + k, 256) for k in (0, 256)])
        )
    sum_turn("projected0")
    sum_turn("projected1")
    sum_turn("images")
    reduce_x(5)

    norm3 = []
    zero = jnp.zeros((8, 256), F32)
    for half, lanes in enumerate(halves3):
        total, square = both_sums(f"projected{half}")
        norm3.append(norm_terms(total, square, gain_three[:, lanes], bias_three[:, lanes], pixels))
        found = []
        for k, block in enumerate(blocks3[half]):
            c3, s3, m3, a3 = (item[:, k * 256 : k * 256 + 256] for item in norm3[half])

            def make_out(row, carry):
                rows = pl.ds(row, CHUNK)
                values = grouped(proj[rows, block])
                summed = grouped(x_v[rows, block].astype(F32)) + (values * m3 + a3)
                gate = sigmoid(summed)
                bo4[pl.ds(row // 4, CHUNK // 4), :, block] = by_four(summed * gate).astype(BF16)
                upstream = grouped(gy_v[rows, block].astype(F32)) * (
                    gate * (1.0 + summed * (1.0 - gate))
                )
                up[rows, block] = flat(upstream)
                normed = (values - c3) * s3
                return carry[0] + jnp.sum(upstream, axis=0), carry[1] + jnp.sum(
                    upstream * normed, axis=0
                )

            found.append(over_rows(make_out, (zero, zero)))
        sum_start(f"back_projected{half}", joined(found))
    bo_copy = pltpu.make_async_copy(bo4, bo_hbm, local_sem.at[2])
    bo_copy.start()

    def write_norm(at, pattern):
        at = at // 128
        both = pattern[0:1, :] + pattern[2:3, :]
        for k in range(both.shape[1] // 128):
            np_full[at + k : at + k + 1, :] = both[:, k * 128 : k * 128 + 128]

    sum_turn("back_projected0")
    sum_turn("back_projected1")
    reduce_z(5)

    for half, lanes in enumerate(halves3):
        bias_sum, gain_sum = both_sums(f"back_projected{half}")
        write_norm(2304 + 512 * half, gain_sum)
        write_norm(3328 + 512 * half, bias_sum)
        by_value, constant = back_terms(*norm3[half][0:3], bias_sum, gain_sum, pixels)
        for k, block in enumerate(blocks3[half]):
            m3, v3, k3 = (
                item[:, k * 256 : k * 256 + 256] for item in (norm3[half][2], by_value, constant)
            )

            def make_dproj(row, carry):
                rows = pl.ds(row, CHUNK)
                values = grouped(up[rows, block]) * m3 + grouped(proj[rows, block]) * v3 + k3
                dproj[rows, block] = flat(values).astype(BF16)
                return carry

            over_rows(make_dproj, 0)
        part_mixed = dot_t(dproj[:, lanes], last[:, lanes])
        d_mixed[...] = part_mixed if half == 0 else d_mixed[...] + part_mixed

    def attend(row, carry):
        rows = pl.ds(row, CHUNK)
        values = grouped(d_mixed[rows, :])
        return (
            carry[0] + jnp.sum(values * grouped(splits[rows, 0:256]), axis=0),
            carry[1] + jnp.sum(values * grouped(splits[rows, 256:512]), axis=0),
        )

    d_att0, d_att1 = over_rows(attend, (zero, zero))
    d_att0, d_att1 = image_sum(d_att0), image_sum(d_att1)
    both = att0 * d_att0 + att1 * d_att1
    d_logits = jnp.concatenate([att0 * (d_att0 - both), att1 * (d_att1 - both)], axis=1)
    d_hidden = exact_dot(d_logits, expand, True)
    d_pool = d_hidden * slope_p
    per_micro = stack_sums(pair_sum(d_pool), pair_sum(d_pool * normed_p))
    sum_start("back_pool", per_micro)
    ex_sum = pair_sum(d_logits)
    ex_sum = ex_sum + pltpu.roll(ex_sum, 2, 0)

    grad_ex = image_dot(hidden, d_logits)
    grad_ex = grad_ex.reshape(n_dp, ex_rows, 512)
    ge[:, 0:ex_rows, 128:384] = grad_ex[:, :, 0:256]
    ge[:, ex_rows : 2 * ex_rows, 128:384] = grad_ex[:, :, 256:512]
    ge[:, :, 384:512] = jnp.zeros((n_dp, 2 * ex_rows, 128), F32)
    def last_block(k, at):
        g3[:, :, at] = tdot(mixed[...], dproj[:, at]).reshape(n_dp, 2 * ex_rows, 512)

    over_blocks(2, 512, last_block)
    reduce_core(3)
    held = []
    for group, att in ((0, att0), (1, att1)):
        lanes = halves2[group]
        c2, s2, m2, a2 = norm2[group]

        def make_dn2(row, carry):
            rows = pl.ds(row, CHUNK)
            values = grouped(wid[rows, lanes])
            turned = values * m2 + a2
            gate = sigmoid(turned)
            slope = gate * (1.0 + turned * (1.0 - gate))
            down = grouped(d_mixed[rows, :]) * att * slope
            dn2[rows, lanes] = flat(down)
            splits[rows, lanes] = flat(slope)
            normed = (values - c2) * s2
            terms = (down, down * normed, slope, slope * normed)
            return tuple(item + jnp.sum(term, axis=0) for item, term in zip(carry, terms))

        held.append([image_sum(item) for item in over_rows(make_dn2, (zero,) * 4)])
    pool_bias_sum, pool_gain_sum = unstack_sums(sum_end("back_pool"))
    write_norm(1536, pool_gain_sum)
    write_norm(1664, pool_bias_sum)
    d_pre_pool = mul_p * (
        d_pool - pool_bias_sum * (1.0 / pictures) - normed_p * (pool_gain_sum * (1.0 / pictures))
    )
    d_pooled = exact_dot(d_pre_pool, squeeze, True) * (1.0 / (SIDE * SIDE))
    found = []
    for down, down_normed, slope, slope_normed in held:
        first, second = down + d_pooled * slope, down_normed + d_pooled * slope_normed
        found.append(stack_sums(pair_sum(first), pair_sum(second)))
    sum_start(
        "back_widened", jnp.concatenate([jnp.concatenate(found, axis=1), ex_sum[0:4]], axis=0)
    )
    ge[:, :, 0:128] = image_dot(pooled, d_pre_pool).reshape(n_dp, 2 * ex_rows, 128)
    reduce_core(4)
    sum_turn("back_widened")
    reduce_across(5)
    reduce_x(3)
    reduce_x(4)

    small_zero = jnp.zeros((8, 128), F32)
    for group, lanes in enumerate(halves2):
        if group == 0:
            whole = sum_end("back_widened")
            for k in range(4):
                np_full[14 + k : 15 + k, :] = whole[4:5, k * 128 : k * 128 + 128]
        bias_sum, gain_sum = unstack_sums(whole[0:4, lanes])
        write_norm(512 + 256 * group, gain_sum)
        write_norm(1024 + 256 * group, bias_sum)
        m2 = norm2[group][2]
        v2, k2 = back_terms(*norm2[group][0:3], bias_sum, gain_sum, pixels)
        pooled_m2 = d_pooled * m2

        def make_dwid(row, carry):
            rows = pl.ds(row, CHUNK)
            values = grouped(dn2[rows, lanes]) * m2 + grouped(splits[rows, lanes]) * pooled_m2
            values = values + grouped(wid[rows, lanes]) * v2 + k2
            dwid[rows, lanes] = flat(values).astype(BF16)
            return carry

        over_rows(make_dwid, 0)
        def grad_block(k, at):
            rows = pl.ds(pl.multiple_of(group * 1152 + k * 384, 384), 384)
            gc_flat[rows, :] = tdot(columns[group, :, at], dwid[:, lanes])

        over_blocks(3, 384, grad_block)
    reduce_core(1)
    reduce_core(2)
    for group, lanes in enumerate(halves2):
        def dcol_block(k, at):
            to = pl.ds(pl.multiple_of(group * 1152 + k * 384, 384), 384)
            dcol[PAD : PAD + ROWS, to] = dot_t(dwid[:, lanes], filters[group, at, :])

        over_blocks(3, 384, dcol_block)
        inner = slice(group * 128, group * 128 + 128)

        def gather_taps(row, carry):
            for side in range(3):
                total = None
                for down in range(3):
                    at = group * 1152 + (3 * down + side) * 128
                    values = dcol[pl.ds(PAD + row - 56 * (down - 1), CHUNK), at : at + 128]
                    total = values if total is None else total + values
                act[side, pl.ds(PAD + row, CHUNK), inner] = total
            return carry

        over_rows(gather_taps, 0)
        c1, s1, m1, a1 = (item[:, inner] for item in (center1, scale1, mul1, add1))
        not_first1, not_last1 = not_first[:, inner], not_last[:, inner]

        def make_dn1(row, carry):
            rows = pl.ds(row, CHUNK)
            d_active = act[1, pl.ds(PAD + row, CHUNK), inner]
            d_active = d_active + jnp.where(not_first1, beside(2, row, -4, inner), 0.0)
            d_active = d_active + jnp.where(not_last1, beside(0, row, 4, inner), 0.0)
            values = grouped(red[rows, inner])
            turned = values * m1 + a1
            gate = sigmoid(turned)
            slope = gate * (1.0 + turned * (1.0 - gate))
            down = grouped(d_active) * slope
            dn1[rows, inner] = flat(down)
            mixed[rows, inner] = flat(down * m1).astype(BF16)
            normed = (values - c1) * s1
            return carry[0] + jnp.sum(down, axis=0), carry[1] + jnp.sum(down * normed, axis=0)

        bias_sum, gain_sum = over_rows(make_dn1, (small_zero, small_zero))
        sum_start(f"back_reduced{group}", stack_sums(micro_sum(bias_sum), micro_sum(gain_sum)))
        if group == 0:
            reduce_y(1)
            reduce_z(3)
            reduce_z(4)
    reduce_y(2)
    sum_turn("back_reduced0")
    sum_turn("back_reduced1")
    g1[...] = tdot(mixed[...], x_v[...]).reshape(g1.shape)
    reduce_core(0)
    reduce_x(1)
    reduce_across(3)
    reduce_across(4)
    found = [unstack_sums(sum_end(f"back_reduced{group}")) for group in range(2)]
    bias_sum, gain_sum = (jnp.concatenate(item, axis=1) for item in zip(*found))
    write_norm(0, gain_sum)
    write_norm(256, bias_sum)
    by_value, constant = back_terms(center1, scale1, mul1, bias_sum, gain_sum, pixels)
    def make_dred(row, carry):
        rows = pl.ds(row, CHUNK)
        values = grouped(dn1[rows, :]) * mul1 + grouped(red[rows, :]) * by_value + constant
        dred[rows, :] = flat(values).astype(BF16)
        return carry

    over_rows(make_dred, 0)
    reduce_x(2)
    reduce_z(1)
    def dx_block(z, at):
        proj[:, at] = dot_t(dred[...], fw1[z].reshape(depth, BOTTLE))

    over_blocks(planes, depth, dx_block)
    reduce_y(0)

    by_bias = mul1 * bias_sum * (1.0 / pixels)
    by_gain = mul1 * gain_sum * (1.0 / pixels)
    image_sums = sum_end("images")
    ids = lax.broadcasted_iota(jnp.int32, (16, 128), 0)
    own_sums = [
        jnp.sum(jnp.where(ids == m * n_dp + dp, image_sums, 0.0), axis=0, keepdims=True)
        for m in range(2)
    ]
    ids = row_ids(128)
    fix[0] = row_dot(by_bias, jnp.where(ids == 0, own_sums[0], jnp.where(ids == 2, own_sums[1], 0.0)))
    for m in range(2):
        fix[1 + m] = row_dot(by_gain, jnp.where(ids == 2 * m, 1.0, 0.0))
    reduce_spread(3)
    reduce_spread(4)

    def make_dx(row, carry):
        for start in range(0, CHANNELS, 256):
            lanes = slice(start, start + 256)
            values = up[pl.ds(row, CHUNK), lanes] + proj[pl.ds(row, CHUNK), lanes]
            dx4[pl.ds(row // 4, CHUNK // 4), :, lanes] = values.reshape(CHUNK // 4, 4, 256)
        return carry

    over_rows(make_dx, 0)
    dx_copy = pltpu.make_async_copy(dx4, dx_hbm, local_sem.at[3])
    dx_copy.start()
    norm_rows = np_full[0:8, :]
    for d in range(1, n_dp):
        at = shard * d // 128
        norm_rows = jnp.where(dp == d, np_full[at : at + 8, :], norm_rows)
    norm_rows = pltpu.roll(norm_rows, lax.rem(128 - turn, 128), 1)
    gn_out[...] = jnp.where(lanes_id < 128 - turn, norm_rows, pltpu.roll(norm_rows, 7, 0))
    reduce_z(2)
    reduce_x(0)
    reduce_spread(1)
    reduce_z(0)
    reduce_spread(2)
    reduce_hand(1)
    reduce_spread(0)
    reduce_hand(2)
    reduce_hand(0)
    out_copies = [
        pltpu.make_async_copy(source, target, local_sem.at[10 + k])
        for k, (source, target) in enumerate(
            (
                (gn_out, gn_hbm),
                (fs[2], f3_hbm),
                (fs[3], fe_hbm),
                (fs[1], fc_hbm),
                (fs[0], f1_hbm),
            )
        )
    ]
    out_copies[0].start()
    for which in (3, 4, 1, 2, 0):
        reduce_end(which)
        if which != 1:
            out_copies[{3: 1, 4: 2, 2: 3, 0: 4}[which]].start()

    bo_copy.wait()
    dx_copy.wait()
    for copy in out_copies:
        copy.wait()
    for k in STATS:
        if k in DIRECT:
            wait_bytes(ar_slots_a[k].at[pl.ds(0, everyone - 1)], ar_send_a.at[order[k]])
        else:
            wait_bytes(ar_slots_a[k].at[pl.ds(0, plane_size - 1)], ar_send_a.at[order[k]])
            wait_bytes(ar_slots_b[k].at[pl.ds(0, planes - 1)], ar_send_b.at[order[k]])
    wait_bytes(np_slots.at[pl.ds(0, n_dp - 1)], np_sems.at[0])
    for which in range(3):
        gather_sent(which)
    for which in range(6):
        reduce_sent(which)


def update_kernel(*refs):
    sources, targets = refs[0:25], refs[25:45]
    inputs, outs, through = refs[45:68], refs[68:86], refs[86:88]
    pass_sems, in_sems, out_sems = refs[88:91]
    part = SIDE * SIDE // 4
    fetching, passing = [], []
    for k in range(4):
        rows = pl.ds(k * part, part)
        for which in range(2):
            fetching.append(
                pltpu.make_async_copy(
                    sources[which].at[rows], through[which].at[rows], pass_sems.at[0, which, k]
                )
            )
            passing.append(
                pltpu.make_async_copy(
                    through[which].at[rows], targets[which].at[rows], pass_sems.at[1, which, k]
                )
            )
    for copy in fetching:
        copy.start()
    coming = [
        pltpu.make_async_copy(source, held, in_sems.at[k])
        for k, (source, held) in enumerate(zip(sources[2:], inputs))
    ]
    for copy in coming:
        copy.start()
    grads, states = inputs[0:5], inputs[5:23]
    going = [
        pltpu.make_async_copy(held, target, out_sems.at[k])
        for k, (held, target) in enumerate(zip(outs, targets[2:]))
    ]
    ex_rows = states[9].shape[0]
    shard = states[15].shape[0]
    fans = (CHANNELS, 9 * BOTTLE // RADIX, BOTTLE, INNER // 8, BOTTLE)
    for copy in coming[0:5]:
        copy.wait()
    found = (
        grads[0][...].T,
        grads[1][...],
        grads[3][:, 0:128],
        jnp.concatenate([grads[3][0:ex_rows, 128:384], grads[3][ex_rows:, 128:384]], axis=1),
        grads[2][...],
    )
    for order, k in enumerate((3, 2, 4, 0, 1)):
        for copy in coming[5 + 3 * k : 8 + 3 * k]:
            copy.wait()
        new = adamw(
            states[3 * k][...],
            states[3 * k + 1][...],
            states[3 * k + 2][...],
            found[k],
            2.0 * fans[k] ** (-0.5),
            DECAY,
        )
        for j in range(3):
            outs[3 * k + j][...] = new[j]
            going[3 * k + j].start()
        for copy in range(2 * order, min(2 * order + 2, 8)):
            fetching[copy].wait()
            passing[copy].start()
    for copy in coming[20:23]:
        copy.wait()
    for at in range(0, shard, 128):
        width = min(128, shard - at)
        lanes = pl.ds(at, width)
        new = adamw(
            *[states[15 + j][lanes].reshape(1, width) for j in range(3)],
            grads[4][at // 128 : at // 128 + 1, 0:width],
            NORM_RATE,
            0.0,
        )
        for j in range(3):
            outs[15 + j][lanes] = new[j].reshape(width)
    for copy in going[15:18]:
        copy.start()
    for copy in passing + going:
        copy.wait()


def fused_device(
    images,
    out_grad,
    reduce_weight,
    reduce_moment,
    reduce_second,
    conv_weight,
    conv_moment,
    conv_second,
    squeeze_weight,
    squeeze_moment,
    squeeze_second,
    expand_weight,
    expand_moment,
    expand_second,
    project_weight,
    project_moment,
    project_second,
    norm_params,
    norm_moment,
    norm_second,
):
    n_dp, n_rep = lax.axis_size("dp"), lax.axis_size("rep")
    by_pixel = lambda values: jnp.transpose(values, (1, 2, 0, 3)).reshape(-1, 4, CHANNELS)
    qc = conv_weight.shape[0] // 2
    q1 = reduce_weight.shape[0] // 4
    pe = squeeze_weight.shape[0]
    vmem = pltpu.VMEM
    pixel_form = (SIDE * SIDE, 4, CHANNELS)
    scratch = [
        *[
            vmem(values.shape, F32)
            for values in (
                reduce_weight,
                conv_weight,
                squeeze_weight,
                expand_weight,
                project_weight,
                norm_params,
            )
        ],
        vmem((8, 128), F32),
        vmem(pixel_form, BF16),
        vmem(pixel_form, BF16),
        vmem((ROWS, CHANNELS), BF16),
        vmem((ROWS, CHANNELS), BF16),
        vmem((n_dp // 2, 2, 2, 2, q1, BOTTLE), BF16),
        vmem((n_dp // 2, 2, 2, qc, BOTTLE), BF16),
        vmem((n_dp // 2, 2, pe, 1536), BF16),
        vmem((pe, 1536), BF16),
        vmem((n_dp, 8, 128), F32),
        vmem((40, 128), F32),
        vmem((ROWS, BOTTLE), F32),
        vmem((3, ROWS + 2 * PAD, BOTTLE), F32),
        vmem((2, ROWS, 9 * 128), BF16),
        vmem((ROWS, 512), F32),
        vmem((ROWS, 512), F32),
        vmem((ROWS, BOTTLE), BF16),
        vmem((ROWS, CHANNELS), F32),
        vmem((ROWS, CHANNELS), F32),
        vmem(pixel_form, BF16),
        vmem(pixel_form, F32),
        vmem((ROWS, CHANNELS), BF16),
        vmem((ROWS, BOTTLE), F32),
        vmem((ROWS, 512), F32),
        vmem((ROWS, 512), BF16),
        vmem((ROWS + 2 * PAD, 2 * 9 * 128), F32),
        vmem((ROWS, BOTTLE), F32),
        vmem((ROWS, BOTTLE), BF16),
        vmem((2, 2, BOTTLE // 4, CHANNELS), F32),
        vmem((2, 9 * 128, BOTTLE), BF16),
        vmem((n_dp * 2 * qc, BOTTLE), F32),
        vmem((n_dp, pe, CHANNELS), F32),
        vmem((n_dp, pe, 512), F32),
        vmem((2, 2, BOTTLE // 2, CHANNELS), BF16),
        vmem((3, BOTTLE, CHANNELS // n_dp), F32),
        vmem((2, BOTTLE // 2, CHANNELS // n_dp), F32),
    ]
    direct = n_dp * n_rep
    scratch += [
        vmem((direct if k in DIRECT else 2 * n_rep,) + shape, F32) for k, shape in STATS.items()
    ]
    scratch += [vmem((n_dp // 2,) + shape, F32) for shape in STATS.values()]
    cut = 64
    lanes1 = CHANNELS // n_dp
    half = [
        (2, BOTTLE // 4, CHANNELS),
        (n_dp, 2, cut, 128),
        (n_dp, 2, qc - cut, 128),
        (n_dp, pe, 512),
        (n_dp, pe, 256),
        (2, BOTTLE // 2, CHANNELS),
    ]
    quarter = [
        (BOTTLE // 4, CHANNELS),
        (n_dp, cut, 128),
        (n_dp, qc - cut, 128),
    ]
    owned = [
        (BOTTLE // 4, lanes1),
        (cut, 128),
        (qc - cut, 128),
        (pe, 512),
        (pe, 256),
        (2, BOTTLE // 2, lanes1),
    ]
    final = [(2, 2, BOTTLE // 4, lanes1), (2, qc, BOTTLE), (pe, CHANNELS), (pe, 512)]
    sent = [BF16, BF16, BF16, BF16, F32, BF16]
    scratch += [vmem(shape, F32) for shape in half[:-1]] + [vmem(half[-1], BF16)]
    for kinds in (sent, sent, [F32] * 6, sent, sent):
        scratch += [vmem((n_dp // 2,) + shape, kind) for shape, kind in zip(owned, kinds)]
    scratch += [vmem(shape, BF16) for shape in quarter] * 2
    scratch += [vmem(shape, F32) for shape in (*owned[3:5], owned[5][1:], *owned[3:5])]
    scratch += [vmem(shape, F32) for shape in final]
    dma = pltpu.SemaphoreType.DMA
    scratch += [dma((15,))] + [dma((len(STATS),))] * 4 + [dma((2,))] + [dma((3, 5)), dma((3, 5, n_dp // 2))] + [dma((6, 7))] * 2
    any_space = pl.BlockSpec(memory_space=pl.ANY)
    block_out, images_grad, sum1, sumc, sum3, sume, norm_grads = pl.pallas_call(
        functools.partial(block_kernel, n_dp, n_rep),
        out_shape=[
            jax.ShapeDtypeStruct(pixel_form, BF16),
            jax.ShapeDtypeStruct(pixel_form, F32),
            *[jax.ShapeDtypeStruct(shape, F32) for shape in final],
            jax.ShapeDtypeStruct((8, 128), F32),
        ],
        in_specs=[any_space] * 8,
        out_specs=[any_space] * 7,
        scratch_shapes=scratch,
        compiler_params=pltpu.CompilerParams(
            collective_id=0, has_side_effects=True, vmem_limit_bytes=63 * 1024 * 1024
        ),
    )(
        by_pixel(images),
        by_pixel(out_grad),
        reduce_weight,
        conv_weight,
        squeeze_weight,
        expand_weight,
        project_weight,
        norm_params,
    )
    states = (
        reduce_weight,
        reduce_moment,
        reduce_second,
        conv_weight,
        conv_moment,
        conv_second,
        squeeze_weight,
        squeeze_moment,
        squeeze_second,
        expand_weight,
        expand_moment,
        expand_second,
        project_weight,
        project_moment,
        project_second,
    )
    held = (*states, norm_params, norm_moment, norm_second)
    sums = (
        sum1.reshape(BOTTLE, lanes1),
        sumc.reshape(conv_weight.shape),
        sum3,
        sume,
        norm_grads,
    )
    block_out, images_grad, *updated = pl.pallas_call(
        update_kernel,
        out_shape=[
            jax.ShapeDtypeStruct(pixel_form, BF16),
            jax.ShapeDtypeStruct(pixel_form, F32),
            *[jax.ShapeDtypeStruct(state.shape, F32) for state in held],
        ],
        in_specs=[any_space] * 25,
        out_specs=[any_space] * 20,
        scratch_shapes=[vmem(values.shape, F32) for values in (*sums, *held, *held)]
        + [vmem(pixel_form, BF16), vmem(pixel_form, F32)]
        + [dma((2, 2, 4)), dma((23,)), dma((18,))],
        compiler_params=pltpu.CompilerParams(vmem_limit_bytes=63 * 1024 * 1024),
    )(block_out, images_grad, *sums, *held)
    by_image = lambda values: jnp.transpose(
        values.reshape(SIDE, SIDE, images.shape[0], CHANNELS), (2, 0, 1, 3)
    )
    return (
        by_image(block_out),
        by_image(images_grad),
        *updated,
    )


def solution(mesh):
    placed = (
        P(("dp", "rep"), None, None, None),
        P(("dp", "rep"), None, None, None),
        P("dp", None),
        P("dp", None),
        P("dp", None),
        P("dp", None),
        P("dp", None),
        P("dp", None),
        P("dp", None),
        P("dp", None),
        P("dp", None),
        P("dp", None),
        P("dp", None),
        P("dp", None),
        P("dp", None),
        P("dp", None),
        P("dp", None),
        P("dp"),
        P("dp"),
        P("dp"),
    )
    n_dp, n_rep = mesh.shape["dp"], mesh.shape["rep"]
    whole_tiles = n_rep == 4 and n_dp % 2 == 0 and INNER % (16 * n_dp) == 0
    return jax.shard_map(
        fused_device if whole_tiles else per_device,
        mesh=mesh,
        in_specs=placed,
        out_specs=(
            P(("dp", "rep"), None, None, None),
            P(("dp", "rep"), None, None, None),
            P("dp", None),
            P("dp", None),
            P("dp", None),
            P("dp", None),
            P("dp", None),
            P("dp", None),
            P("dp", None),
            P("dp", None),
            P("dp", None),
            P("dp", None),
            P("dp", None),
            P("dp", None),
            P("dp", None),
            P("dp", None),
            P("dp", None),
            P("dp"),
            P("dp"),
            P("dp"),
        ),
        check_vma=False,
    )
```

```python
import functools
import jax
import jax.numpy as jnp
from jax import lax
from jax.experimental import pallas as pl
from jax.experimental.pallas import tpu as pltpu
from jax.sharding import PartitionSpec as P

CHANNELS = 1024
BOTTLE = 256
INNER = 128
RADIX = 2
SIDE = 14
MICRO = 2
STEP = 10


EPSILON = 1e-05
PRECISE = lax.Precision.HIGHEST
BETA_ONE = 0.9
BETA_TWO = 0.999
ADAM_EPSILON = 1e-08
DECAY = 0.01
NORM_RATE = 0.8
ROWS = 4 * SIDE * SIDE
NORM_WIDTH = 4352


def split_params(packed):
    widths = (
        BOTTLE,
        BOTTLE,
        RADIX * BOTTLE,
        RADIX * BOTTLE,
        INNER,
        INNER,
        RADIX * BOTTLE,
        CHANNELS,
        CHANNELS,
    )
    pieces = []
    offset = 0
    for segment in widths:
        pieces.append(lax.slice_in_dim(packed, offset, offset + segment))
        offset = offset + segment
    return pieces


def silu_slope(values):
    logistic = jax.nn.sigmoid(values)
    return logistic * (1.0 + values * (1.0 - logistic))


def norm_forward(values, gain, bias, count):
    flat = values.reshape(-1, values.shape[-1])
    total, square = lax.psum((jnp.sum(flat, axis=0), jnp.sum(flat * flat, axis=0)), ("dp", "rep"))
    center = total / count
    scale = lax.rsqrt(square / count - center * center + EPSILON)
    normed = (values - center) * scale
    return (normed * gain + bias, normed, scale)


def norm_backward(upstream, normed, scale, gain, count):
    flat_up = upstream.reshape(-1, upstream.shape[-1])
    flat_norm = normed.reshape(-1, normed.shape[-1])
    bias_sum, gain_sum = lax.psum(
        (jnp.sum(flat_up, axis=0), jnp.sum(flat_up * flat_norm, axis=0)), ("dp", "rep")
    )
    downstream = gain * scale * (upstream - bias_sum / count - normed * (gain_sum / count))
    return (downstream, gain_sum, bias_sum)


def patches(active):
    padded = jnp.pad(active, ((0, 0), (1, 1), (1, 1), (0, 0), (0, 0)))
    shifted = [
        padded[:, down_step : down_step + SIDE, side_step : side_step + SIDE]
        for down_step in range(3)
        for side_step in range(3)
    ]
    return jnp.stack(shifted, axis=4)


def unpatch(columns):
    total = jnp.zeros(
        (columns.shape[0], SIDE + 2, SIDE + 2, columns.shape[3], columns.shape[5]), jnp.float32
    )
    for down_step in range(3):
        for side_step in range(3):
            piece = columns[:, :, :, :, 3 * down_step + side_step]
            total = total + jnp.pad(
                piece,
                ((0, 0), (down_step, 2 - down_step), (side_step, 2 - side_step), (0, 0), (0, 0)),
            )
    return total[:, 1 : SIDE + 1, 1 : SIDE + 1]


def adamw(param, moment, second, gradient, rate, decay):
    moment_new = BETA_ONE * moment + (1.0 - BETA_ONE) * gradient
    second_new = BETA_TWO * second + (1.0 - BETA_TWO) * gradient * gradient
    ratio = (
        moment_new
        / (1.0 - BETA_ONE**STEP)
        / (jnp.sqrt(second_new / (1.0 - BETA_TWO**STEP)) + ADAM_EPSILON)
    )
    return (param - rate * (ratio + decay * param), moment_new, second_new)


def per_device(
    images,
    out_grad,
    reduce_weight,
    reduce_moment,
    reduce_second,
    conv_weight,
    conv_moment,
    conv_second,
    squeeze_weight,
    squeeze_moment,
    squeeze_second,
    expand_weight,
    expand_moment,
    expand_second,
    project_weight,
    project_moment,
    project_second,
    norm_params,
    norm_moment,
    norm_second,
):
    bf16 = jnp.bfloat16
    low_reduce = reduce_weight.astype(bf16)
    low_conv = conv_weight.astype(bf16)
    low_squeeze = squeeze_weight.astype(bf16)
    low_expand = expand_weight.astype(bf16)
    low_project = project_weight.astype(bf16)
    low_norm = norm_params.astype(bf16)
    devices = lax.axis_size("dp") * lax.axis_size("rep")
    per_batch = images.shape[0] // MICRO
    pixel_count = float(per_batch * SIDE * SIDE * devices)
    image_count = float(per_batch * devices)
    group_in = BOTTLE // RADIX
    grad_first = jnp.zeros((CHANNELS, BOTTLE), jnp.float32)
    grad_conv = jnp.zeros((RADIX, 9 * group_in, BOTTLE), jnp.float32)
    grad_squeeze = jnp.zeros((BOTTLE, INNER), jnp.float32)
    grad_expand = jnp.zeros((INNER, RADIX * BOTTLE), jnp.float32)
    grad_last = jnp.zeros((BOTTLE, CHANNELS), jnp.float32)
    grad_norms = jnp.zeros(
        (2 * BOTTLE + 3 * RADIX * BOTTLE + 2 * INNER + 2 * CHANNELS,), jnp.float32
    )
    outputs = []
    input_grads = []
    for number in range(MICRO):
        forward_set = (
            lax.all_gather(low_reduce, "dp", axis=0, tiled=True),
            lax.all_gather(low_conv, "dp", axis=0, tiled=True),
            lax.all_gather(low_squeeze, "dp", axis=0, tiled=True),
            lax.all_gather(low_expand, "dp", axis=0, tiled=True),
            lax.all_gather(low_project, "dp", axis=0, tiled=True),
            lax.all_gather(low_norm, "dp", axis=0, tiled=True),
        )
        first, conv, squeeze, expand, last, packed = forward_set
        (
            gain_one,
            bias_one,
            gain_two,
            bias_two,
            gain_pool,
            bias_pool,
            bias_expand,
            gain_three,
            bias_three,
        ) = split_params(packed.astype(jnp.float32))
        batched = images[number * per_batch : (number + 1) * per_batch]
        cotangent = out_grad[number * per_batch : (number + 1) * per_batch]
        reduced = jnp.einsum("nhwc,cb->nhwb", batched, first, preferred_element_type=jnp.float32)
        norm_one, normed_one, scale_one = norm_forward(reduced, gain_one, bias_one, pixel_count)
        active = jax.nn.silu(norm_one).astype(bf16)
        columns = patches(active.reshape(per_batch, SIDE, SIDE, RADIX, group_in)).reshape(
            per_batch * SIDE * SIDE, RADIX, 9 * group_in
        )
        conv_grouped = conv.reshape(RADIX, 9 * group_in, BOTTLE)
        widened = jnp.einsum(
            "prk,rko->pro", columns, conv_grouped, preferred_element_type=jnp.float32
        )
        widened = widened.reshape(per_batch, SIDE, SIDE, RADIX * BOTTLE)
        norm_two, normed_two, scale_two = norm_forward(widened, gain_two, bias_two, pixel_count)
        splits = jax.nn.silu(norm_two).reshape(per_batch, SIDE, SIDE, RADIX, BOTTLE)
        pooled = jnp.sum(jnp.sum(splits, axis=3), axis=(1, 2)) / (SIDE * SIDE)
        squeeze_float = squeeze.astype(jnp.float32)
        expand_float = expand.astype(jnp.float32)
        pre_pool = jnp.dot(pooled, squeeze_float, precision=PRECISE)
        norm_pool, normed_pool, scale_pool = norm_forward(
            pre_pool, gain_pool, bias_pool, image_count
        )
        hidden = jax.nn.silu(norm_pool)
        logits = (jnp.dot(hidden, expand_float, precision=PRECISE) + bias_expand).reshape(
            per_batch, RADIX, BOTTLE
        )
        attention = jax.nn.softmax(logits, axis=1)
        mixed = jnp.sum(splits * attention[:, None, None], axis=3).astype(bf16)
        projected = jnp.einsum("nhwb,bc->nhwc", mixed, last, preferred_element_type=jnp.float32)
        norm_three, normed_three, scale_three = norm_forward(
            projected, gain_three, bias_three, pixel_count
        )
        summed = batched.astype(jnp.float32) + norm_three
        outputs.append(jax.nn.silu(summed).astype(bf16))
        backward_set = (
            lax.all_gather(low_reduce, "dp", axis=0, tiled=True),
            lax.all_gather(low_conv, "dp", axis=0, tiled=True),
            lax.all_gather(low_squeeze, "dp", axis=0, tiled=True),
            lax.all_gather(low_expand, "dp", axis=0, tiled=True),
            lax.all_gather(low_project, "dp", axis=0, tiled=True),
            lax.all_gather(low_norm, "dp", axis=0, tiled=True),
        )
        first, conv, squeeze, expand, last, packed = backward_set
        gains_back = split_params(packed.astype(jnp.float32))
        conv_grouped = conv.reshape(RADIX, 9 * group_in, BOTTLE)
        expand_float = expand.astype(jnp.float32)
        squeeze_float = squeeze.astype(jnp.float32)
        upstream = cotangent.astype(jnp.float32) * silu_slope(summed)
        d_projected, gain_three_grad, bias_three_grad = norm_backward(
            upstream, normed_three, scale_three, gains_back[7], pixel_count
        )
        d_projected_low = d_projected.astype(bf16)
        grad_last = grad_last + jnp.einsum(
            "nhwb,nhwc->bc", mixed, d_projected_low, preferred_element_type=jnp.float32
        )
        d_mixed = jnp.einsum(
            "nhwc,bc->nhwb", d_projected_low, last, preferred_element_type=jnp.float32
        )
        d_splits = d_mixed[:, :, :, None] * attention[:, None, None]
        d_attention = jnp.sum(d_mixed[:, :, :, None] * splits, axis=(1, 2))
        d_logits = attention * (
            d_attention - jnp.sum(attention * d_attention, axis=1, keepdims=True)
        )
        flat_logits = d_logits.reshape(per_batch, RADIX * BOTTLE)
        grad_expand = grad_expand + jnp.dot(hidden.T, flat_logits, precision=PRECISE)
        d_hidden = jnp.dot(flat_logits, expand_float.T, precision=PRECISE)
        d_pool_norm = d_hidden * silu_slope(norm_pool)
        pool_bias_sum, pool_gain_sum, expand_bias_sum = lax.psum(
            (
                jnp.sum(d_pool_norm, axis=0),
                jnp.sum(d_pool_norm * normed_pool, axis=0),
                jnp.sum(flat_logits, axis=0),
            ),
            ("dp", "rep"),
        )
        d_pre_pool = (
            gains_back[4]
            * scale_pool
            * (
                d_pool_norm
                - pool_bias_sum / image_count
                - normed_pool * (pool_gain_sum / image_count)
            )
        )
        grad_squeeze = grad_squeeze + jnp.dot(pooled.T, d_pre_pool, precision=PRECISE)
        d_pooled = jnp.dot(d_pre_pool, squeeze_float.T, precision=PRECISE)
        d_splits = d_splits + (d_pooled / (SIDE * SIDE))[:, None, None, None, :]
        d_norm_two = d_splits.reshape(per_batch, SIDE, SIDE, RADIX * BOTTLE) * silu_slope(norm_two)
        d_widened, gain_two_grad, bias_two_grad = norm_backward(
            d_norm_two, normed_two, scale_two, gains_back[2], pixel_count
        )
        d_widened_low = d_widened.astype(bf16).reshape(per_batch * SIDE * SIDE, RADIX, BOTTLE)
        grad_conv = grad_conv + jnp.einsum(
            "prk,pro->rko", columns, d_widened_low, preferred_element_type=jnp.float32
        )
        d_columns = jnp.einsum(
            "pro,rko->prk", d_widened_low, conv_grouped, preferred_element_type=jnp.float32
        )
        d_active = unpatch(d_columns.reshape(per_batch, SIDE, SIDE, RADIX, 9, group_in)).reshape(
            per_batch, SIDE, SIDE, BOTTLE
        )
        d_norm_one = d_active * silu_slope(norm_one)
        d_reduced, gain_one_grad, bias_one_grad = norm_backward(
            d_norm_one, normed_one, scale_one, gains_back[0], pixel_count
        )
        d_reduced_low = d_reduced.astype(bf16)
        grad_first = grad_first + jnp.einsum(
            "nhwc,nhwb->cb", batched, d_reduced_low, preferred_element_type=jnp.float32
        )
        input_grads.append(
            upstream
            + jnp.einsum("nhwb,cb->nhwc", d_reduced_low, first, preferred_element_type=jnp.float32)
        )
        grad_norms = grad_norms + jnp.concatenate(
            [
                gain_one_grad,
                bias_one_grad,
                gain_two_grad,
                bias_two_grad,
                pool_gain_sum,
                pool_bias_sum,
                expand_bias_sum,
                gain_three_grad,
                bias_three_grad,
            ]
        )
    grad_conv = grad_conv.reshape(9 * BOTTLE, BOTTLE)
    partial_value = (
        lax.psum_scatter(grad_first, "dp", scatter_dimension=0, tiled=True),
        lax.psum_scatter(grad_conv, "dp", scatter_dimension=0, tiled=True),
        lax.psum_scatter(grad_squeeze, "dp", scatter_dimension=0, tiled=True),
        lax.psum_scatter(grad_expand, "dp", scatter_dimension=0, tiled=True),
        lax.psum_scatter(grad_last, "dp", scatter_dimension=0, tiled=True),
    )
    owned = lax.psum(
        (partial_value[0], partial_value[1], partial_value[2], partial_value[3], partial_value[4]),
        "rep",
    )
    shard_length = norm_params.shape[0]
    norm_grad_owned = lax.dynamic_slice_in_dim(
        grad_norms, lax.axis_index("dp") * shard_length, shard_length
    )
    reduce_new = adamw(
        reduce_weight, reduce_moment, reduce_second, owned[0], 2.0 * CHANNELS ** (-0.5), DECAY
    )
    conv_new = adamw(
        conv_weight,
        conv_moment,
        conv_second,
        owned[1],
        2.0 * (9 * BOTTLE // RADIX) ** (-0.5),
        DECAY,
    )
    squeeze_new = adamw(
        squeeze_weight, squeeze_moment, squeeze_second, owned[2], 2.0 * BOTTLE ** (-0.5), DECAY
    )
    expand_new = adamw(
        expand_weight, expand_moment, expand_second, owned[3], 2.0 * (INNER // 8) ** (-0.5), DECAY
    )
    project_new = adamw(
        project_weight, project_moment, project_second, owned[4], 2.0 * BOTTLE ** (-0.5), DECAY
    )
    norm_new = adamw(norm_params, norm_moment, norm_second, norm_grad_owned, NORM_RATE, 0.0)
    return (
        jnp.concatenate(outputs, axis=0),
        jnp.concatenate(input_grads, axis=0),
        reduce_new[0],
        reduce_new[1],
        reduce_new[2],
        conv_new[0],
        conv_new[1],
        conv_new[2],
        squeeze_new[0],
        squeeze_new[1],
        squeeze_new[2],
        expand_new[0],
        expand_new[1],
        expand_new[2],
        project_new[0],
        project_new[1],
        project_new[2],
        norm_new[0],
        norm_new[1],
        norm_new[2],
    )


MESH = pl.DeviceIdType.MESH
PAD = 64
CHUNK = 112
F32 = jnp.float32
BF16 = jnp.bfloat16
STATS = {
    "reduced": (8, 128),
    "widened0": (8, 128),
    "widened1": (8, 128),
    "pool": (8, 128),
    "projected0": (16, 256),
    "projected1": (8, 256),
    "back_projected0": (8, 256),
    "back_projected1": (8, 256),
    "back_pool": (8, 128),
    "back_widened0": (8, 128),
    "back_widened1": (16, 128),
    "back_reduced": (8, 128),
}
DIRECT = ("reduced", "pool", "back_pool", "back_reduced")


def sigmoid(values):
    return 0.5 * jnp.tanh(0.5 * values) + 0.5


def row_ids(width):
    return lax.broadcasted_iota(jnp.int32, (8, width), 0)


def image_sum(rows):
    return rows + pltpu.roll(rows, 4, 0)


def pair_sum(rows):
    even = row_ids(rows.shape[1]) % 2 == 0
    return rows + jnp.where(even, pltpu.roll(rows, 7, 0), pltpu.roll(rows, 1, 0))


def micro_sum(rows):
    return pair_sum(image_sum(rows))


def stack_sums(first, second):
    return jnp.where(row_ids(first.shape[1]) < 4, first, second)


def unstack_sums(stacked):
    upper = row_ids(stacked.shape[1]) < 4
    turned = pltpu.roll(stacked, 4, 0)
    return jnp.where(upper, stacked, turned), jnp.where(upper, turned, stacked)


def fold_lanes(stacked):
    half = stacked.shape[1] // 2
    even = row_ids(half) % 2 == 0
    return jnp.where(even, stacked[:, :half], stacked[:, half:])


def unfold_lanes(folded):
    even = row_ids(folded.shape[1]) % 2 == 0
    left = jnp.where(even, folded, pltpu.roll(folded, 1, 0))
    right = jnp.where(even, pltpu.roll(folded, 7, 0), folded)
    return jnp.concatenate([left, right], axis=1)


def norm_terms(total, square, gain, bias, count):
    center = total * (1.0 / count)
    scale = lax.rsqrt(square * (1.0 / count) - center * center + EPSILON)
    slope = scale * gain
    return center, scale, slope, bias - center * slope


def back_terms(center, scale, slope, bias_sum, gain_sum, count):
    by_value = -slope * scale * (gain_sum * (1.0 / count))
    constant = -slope * (bias_sum * (1.0 / count)) - by_value * center
    return by_value, constant


def tdot(left, right):
    return lax.dot_general(left, right, (((0,), (0,)), ((), ())), preferred_element_type=F32)


def dot_t(left, right):
    return lax.dot_general(left, right, (((1,), (1,)), ((), ())), preferred_element_type=F32)


def in_parts(values, parts):
    found = []
    for _ in range(parts):
        rounded = values.astype(BF16).astype(F32)
        found.append(rounded)
        values = values - rounded
    return found


def exact_dot(left, right, transposed):
    stacked = jnp.concatenate(in_parts(left, 3), axis=0).astype(BF16)
    wide = dot_t(stacked, right) if transposed else jnp.dot(stacked, right, preferred_element_type=F32)
    return wide[0:8] + wide[8:16] + wide[16:24]


def row_dot(left, right):
    high, low = in_parts(left, 2)
    other_high, other_low = in_parts(right, 2)
    return tdot(
        jnp.concatenate([high, high, low, low], axis=0).astype(BF16),
        jnp.concatenate([other_high, other_low, other_high, other_low], axis=0).astype(BF16),
    )


def image_dot(left, right):
    return row_dot(jnp.where(row_ids(left.shape[1]) < 4, left, 0.0), right)


def block_kernel(
    n_dp,
    n_rep,
    x_hbm,
    gy_hbm,
    w1_hbm,
    wc_hbm,
    sq_hbm,
    ex_hbm,
    w3_hbm,
    np_hbm,
    bo_hbm,
    dx_hbm,
    f1_hbm,
    fc_hbm,
    f3_hbm,
    fe_hbm,
    gn_hbm,
    w1_own,
    wc_own,
    sq_own,
    ex_own,
    w3_own,
    np_own,
    gn_out,
    x4,
    gy4,
    x_v,
    gy_v,
    fw1,
    fwc,
    fpe,
    pe_own,
    np_slots,
    np_full,
    red,
    act,
    columns,
    wid,
    splits,
    mixed,
    proj,
    up,
    bo4,
    dx4,
    dproj,
    d_mixed,
    dn2,
    dwid,
    dcol,
    dn1,
    dred,
    g1,
    gc,
    g3,
    ge,
    gb,
    fix,
    back_own,
    *rest,
):
    n_ar = len(STATS)
    order = {name: k for k, name in enumerate(STATS)}
    ar_slots_a = dict(zip(STATS, rest[0:n_ar]))
    ar_slots_b = dict(zip(STATS, rest[n_ar : 2 * n_ar]))
    rest = rest[2 * n_ar :]
    r1s, ys, r2s, ks, r3s, own = (rest[6 * i : 6 * i + 6] for i in range(6))
    fs = rest[36:40]
    rest = rest[40:]
    local_sem, ar_send_a, ar_recv_a, ar_send_b, ar_recv_b, np_sems, ws, wr, gs, gr = rest

    dp = lax.axis_index("dp")
    rep = lax.axis_index("rep")
    core = lax.rem(rep, 2)
    half_y = lax.div(rep, 2)
    planes = n_dp // 2
    plane_size = 2 * n_rep
    plane = lax.div(dp, 2)
    in_plane = lax.rem(dp, 2) * n_rep + rep
    sibling = (dp, half_y * 2 + (1 - core))
    across = (dp, (1 - half_y) * 2 + core)
    pixels = float(SIDE * SIDE * 2 * n_dp * n_rep)
    pictures = float(2 * n_dp * n_rep)

    x = lax.rem(dp, 2)
    if planes == 4:
        upper = lax.div(plane, 2)
        other_planes = [3 - 3 * upper, 2 - upper, 1 - plane + 4 * upper]
    else:
        other_planes = [lax.rem(plane + step, planes) for step in range(1, planes)]
    flips = ((1, 1, 1), (1, 1, 0), (1, 0, 1), (1, 0, 0), (0, 1, 1), (0, 1, 0), (0, 0, 1), (0, 0, 0))

    def of_flip(z, flip):
        there = [1 - own if turn else own for own, turn in zip((x, half_y, core), flip)]
        return (z * 2 + there[0], there[1] * 2 + there[2])

    plane_peers = [of_flip(plane, flip) for flip in flips[:-1]]
    column_peers = [of_flip(z, flips[-1]) for z in other_planes]
    owner_peers = [of_flip(z, flip) for z in other_planes for flip in (flips[3], flips[7])]
    owner_peers += [of_flip(plane, flips[3])]
    all_peers = [of_flip(z, flip) for z in other_planes for flip in flips] + plane_peers
    me, everyone = dp * n_rep + rep, n_dp * n_rep
    rep_peers = [(dp, lax.rem(rep + step, n_rep)) for step in range(1, n_rep)]

    def remote(src, dst, send_sem, recv_sem, device):
        return pltpu.make_async_remote_copy(
            src_ref=src,
            dst_ref=dst,
            send_sem=send_sem,
            recv_sem=recv_sem,
            device_id=device,
            device_id_type=MESH,
        )

    def send_all(ref, send_sem, recv_sem, peers):
        for device in peers:
            remote(ref, ref, send_sem, recv_sem, device).start()

    def wait_bytes(ref, sem):
        pltpu.make_async_copy(ref, ref, sem).wait()

    def over_rows(body, init):
        def step(index, carry):
            return body(pl.multiple_of(index * CHUNK, CHUNK), carry)

        return lax.fori_loop(0, ROWS // CHUNK, step, init)

    def grouped(values):
        return values.reshape(CHUNK // 8, 8, values.shape[-1])

    def by_four(values):
        return flat(values).reshape(CHUNK // 4, 4, values.shape[-1])

    def flat(values):
        return values.reshape(CHUNK, values.shape[-1])

    own_copies = [
        pltpu.make_async_copy(source, target, local_sem.at[4 + k])
        for k, (source, target) in enumerate(
            (
                (w1_hbm, w1_own),
                (np_hbm, np_own),
                (wc_hbm, wc_own),
                (w3_hbm, w3_own),
                (sq_hbm, sq_own),
                (ex_hbm, ex_own),
            )
        )
    ]
    for copy in own_copies:
        copy.start()
    x_copy = pltpu.make_async_copy(x_hbm, x4, local_sem.at[0])
    gy_copy = pltpu.make_async_copy(gy_hbm, gy4, local_sem.at[1])
    x_copy.start()
    barrier = pltpu.get_barrier_semaphore()
    for device in all_peers:
        pl.semaphore_signal(barrier, inc=1, device_id=device, device_id_type=MESH)

    part = core * 2 + half_y
    own_copies[0].wait()
    q1 = w1_own.shape[0] // 4
    fw1[dp, core, half_y] = w1_own[pl.ds(pl.multiple_of(part * q1, q1), q1), :].astype(BF16)
    core_lanes = pl.ds(pl.multiple_of(core * 128, 128), 128)
    pe_lanes = pl.ds(pl.multiple_of(part * 384, 128), 384)

    pl.semaphore_wait(barrier, everyone - 1)

    def quarter_w1(c, y):
        return fw1.at[:, c, y]

    def quarter_wc(c, y):
        return fwc.at[:, y, :, pl.ds(pl.multiple_of(c * 128, 128), 128)]

    def quarter_pe(c, y):
        return fpe.at[:, :, pl.ds(pl.multiple_of((c * 2 + y) * 384, 128), 384)]

    quarters = (quarter_w1, quarter_wc, quarter_pe)

    def piece(which, d):
        return (
            fw1.at[d, core, half_y],
            fwc.at[d, half_y, :, core_lanes],
            fpe.at[d, :, pe_lanes],
        )[which]

    def seven(which):
        return (
            fw1.at[pl.ds(0, n_dp - 1), core, half_y],
            fwc.at[pl.ds(0, n_dp - 1), half_y, :, core_lanes],
            fpe.at[pl.ds(0, n_dp - 1), :, pe_lanes],
        )[which]

    def gather_out(which):
        send_all(piece(which, dp), ws.at[which, 0], wr.at[which, 0], owner_peers)

    def gather_turn(which):
        wait_bytes(seven(which), wr.at[which, 0])
        mine = quarters[which](core, half_y)
        remote(mine, mine, ws.at[which, 1], wr.at[which, 1], across).start()
        remote(mine, mine, ws.at[which, 2], wr.at[which, 2], sibling).start()

    def gather_hand(which):
        theirs = quarters[which](core, 1 - half_y)
        wait_bytes(theirs, wr.at[which, 1])
        remote(theirs, theirs, ws.at[which, 3], wr.at[which, 3], sibling).start()

    def gather_end(which):
        wait_bytes(quarters[which](1 - core, half_y), wr.at[which, 2])
        wait_bytes(quarters[which](1 - core, 1 - half_y), wr.at[which, 3])

    def to_rows(source, target):
        def body(index, carry):
            values = source[pl.ds(index * (CHUNK // 4), CHUNK // 4)].astype(F32)
            row = pl.multiple_of(index * CHUNK, CHUNK)
            target[pl.ds(row, CHUNK), :] = values.reshape(CHUNK, CHANNELS).astype(BF16)
            return carry

        lax.fori_loop(0, ROWS // CHUNK, body, 0)

    gather_out(0)

    own_copies[1].wait()
    shard = np_own.shape[0]
    lanes_id = lax.broadcasted_iota(jnp.int32, (8, 128), 1)
    turn = lax.rem(shard * dp, 128)
    np_rows = []
    for at in range(0, shard, 128):
        width = min(128, shard - at)
        piece_row = np_own[pl.ds(at, width)].reshape(1, width)
        if width < 128:
            piece_row = jnp.concatenate([piece_row, jnp.zeros((1, 128 - width), F32)], axis=1)
        np_rows.append(piece_row)
    np_rows.append(jnp.zeros((8 - len(np_rows), 128), F32))
    np_turned = jnp.concatenate(np_rows, axis=0).astype(BF16).astype(F32)
    np_turned = pltpu.roll(np_turned, turn, 1)
    np_slots[dp] = jnp.where(lanes_id < turn, pltpu.roll(np_turned, 1, 0), np_turned)
    send_all(np_slots.at[dp], np_sems.at[0], np_sems.at[1], owner_peers)
    own_copies[2].wait()
    qc = wc_own.shape[0] // 2
    fwc[dp, half_y, :, core_lanes] = wc_own[
        pl.ds(pl.multiple_of(half_y * qc, qc), qc), core_lanes
    ].astype(BF16)
    for copy in own_copies[3:]:
        copy.wait()
    ex_rows = ex_own.shape[0]
    pe_own[:, 0:CHANNELS] = w3_own[...].astype(BF16)
    pe_own[:, 1024:1152] = sq_own[...].astype(BF16)
    pe_own[0:ex_rows, 1152:1408] = ex_own[:, 0:256].astype(BF16)
    pe_own[ex_rows : 2 * ex_rows, 1152:1408] = ex_own[:, 256:512].astype(BF16)
    pe_own[:, 1408:1536] = jnp.zeros((2 * ex_rows, 128), BF16)
    fpe[dp, :, pe_lanes] = pe_own[:, pe_lanes]
    gy_copy.start()
    x_copy.wait()
    to_rows(x4, x_v)
    gather_turn(0)
    gather_out(1)
    zero_rows = jnp.zeros((PAD, BOTTLE), F32)
    for side in range(3):
        act[side, 0:PAD, :] = zero_rows
        act[side, PAD + ROWS : 2 * PAD + ROWS, :] = zero_rows
    for lane_block in range(9):
        dcol[0:PAD, lane_block * 256 : lane_block * 256 + 256] = zero_rows
        dcol[PAD + ROWS : 2 * PAD + ROWS, lane_block * 256 : lane_block * 256 + 256] = zero_rows
    gather_hand(0)

    def sum_start(k, payload):
        if k in DIRECT:
            ar_slots_a[k][me] = payload
            send_all(ar_slots_a[k].at[me], ar_send_a.at[order[k]], ar_recv_a.at[order[k]], all_peers)
        else:
            ar_slots_a[k][in_plane] = payload
            send_all(ar_slots_a[k].at[in_plane], ar_send_a.at[order[k]], ar_recv_a.at[order[k]], plane_peers)

    def sum_slots(slots, count):
        sums = [slots[slot] for slot in range(count)]
        while len(sums) > 1:
            sums = [sums[i] + sums[i + 1] for i in range(0, len(sums), 2)]
        return sums[0]

    def sum_turn(k):
        if k in DIRECT:
            return
        wait_bytes(ar_slots_a[k].at[pl.ds(0, plane_size - 1)], ar_recv_a.at[order[k]])
        ar_slots_b[k][plane] = sum_slots(ar_slots_a[k], plane_size)
        send_all(ar_slots_b[k].at[plane], ar_send_b.at[order[k]], ar_recv_b.at[order[k]], column_peers)

    def sum_end(k):
        if k in DIRECT:
            wait_bytes(ar_slots_a[k].at[pl.ds(0, everyone - 1)], ar_recv_a.at[order[k]])
            return sum_slots(ar_slots_a[k], everyone)
        wait_bytes(ar_slots_b[k].at[pl.ds(0, planes - 1)], ar_recv_b.at[order[k]])
        return sum_slots(ar_slots_b[k], planes)

    def lanes_of(index, width):
        return pl.ds(pl.multiple_of(index * width, 128), width)

    cut = 64
    conv_rows = {1: pl.ds(0, cut), 2: pl.ds(cut, gc.shape[2] - cut)}
    grads = (g1, gc, gc, g3, ge, gb)
    turned_kinds = (0, 5)

    def half_of(which, c):
        ref = grads[which]
        if which in turned_kinds:
            return ref.at[c]
        if which in conv_rows:
            return ref.at[:, :, conv_rows[which], lanes_of(c, 128)]
        return ref.at[:, :, lanes_of(c, (512, 256)[which - 3])]

    def y_part(which, ref, y):
        if which in turned_kinds:
            return ref.at[y]
        if which < 3:
            return ref.at[:, y]
        return ref.at[:, :, lanes_of(y, (256, 128)[which - 3])]

    def quarter_of(which, c, y):
        ref = grads[which]
        if which in turned_kinds:
            return ref.at[c, y]
        if which in conv_rows:
            return ref.at[:, y, conv_rows[which], lanes_of(c, 128)]
        return ref.at[:, :, lanes_of(c * 2 + y, (256, 128)[which - 3])]

    def final_part(which, c, y):
        if which == 0:
            return fs[0].at[c, y]
        if which in conv_rows:
            return fs[1].at[y, conv_rows[which], lanes_of(c, 128)]
        return fs[which - 1].at[:, lanes_of(c * 2 + y, (256, 128)[which - 3])]

    def of_owner(which, ref, d):
        return ref.at[:, lanes_of(d, CHANNELS // n_dp)] if which in turned_kinds else ref.at[d]

    def in_blocks(which, body):
        if which in turned_kinds:
            count = 4
            rows = grads[which].shape[2] // count
            block = lambda index: pl.ds(pl.multiple_of(index * rows, rows), rows)
        else:
            count, block = n_dp, lambda index: index

        def step(index, carry):
            body(block(index))
            return carry

        lax.fori_loop(0, count, step, 0)

    def reduce_core(which):
        remote(
            half_of(which, 1 - core), r1s[which], gs.at[which, 0], gr.at[which, 0], sibling
        ).start()

    def reduce_y(which):
        wait_bytes(r1s[which], gr.at[which, 0])
        away = quarter_of(which, core, 1 - half_y)
        mine = quarter_of(which, core, half_y)
        there = y_part(which, r1s[which], 1 - half_y)
        here = y_part(which, r1s[which], half_y)

        def add_away(at):
            ys[which][at] = (away[at].astype(F32) + there[at].astype(F32)).astype(
                ys[which].dtype
            )

        in_blocks(which, add_away)
        remote(ys[which], r2s[which], gs.at[which, 1], gr.at[which, 1], across).start()

        def add_mine(at):
            mine[at] = (mine[at].astype(F32) + here[at].astype(F32)).astype(mine.dtype)

        in_blocks(which, add_mine)

    def reduce_owner(which):
        wait_bytes(r2s[which], gr.at[which, 1])
        mine = quarter_of(which, core, half_y)

        def add(at):
            ks[which][at] = (mine[at].astype(F32) + r2s[which][at].astype(F32)).astype(
                ks[which].dtype
            )

        in_blocks(which, add)
        for device in owner_peers:
            remote(
                of_owner(which, ks[which], device[0]),
                r3s[which].at[dp],
                gs.at[which, 2],
                gr.at[which, 2],
                device,
            ).start()
        own[which][...] = of_owner(which, mine, dp)[...].astype(F32) + of_owner(
            which, r2s[which], dp
        )[...].astype(F32)
        r3s[which][dp] = jnp.zeros(own[which].shape, r3s[which].dtype)

    def owner_total(which):
        wait_bytes(r3s[which].at[pl.ds(0, n_dp - 1)], gr.at[which, 2])
        total = own[which][...]
        for slot in range(n_dp):
            total = total + r3s[which][slot].astype(F32)
        return total

    def reduce_spread(which):
        total = owner_total(which)
        if which == 0:
            rows = pl.ds(pl.multiple_of(part * (BOTTLE // 4), BOTTLE // 4), BOTTLE // 4)
            total = total - fix[0, rows, :]
            for m in range(2):
                total = total - fix[1 + m, rows, :] * back_own[m]
        mine = final_part(which, core, half_y)
        mine[...] = total
        send_all(mine, gs.at[which, 3], gr.at[which, 3], rep_peers)

    def three_parts(which):
        if which == 0:
            return r1s[0].at[0, :, pl.ds(0, 3 * CHANNELS // n_dp)]
        return r1s[which].at[pl.ds(0, 3), 0] if which < 3 else y_part(which, r1s[which], 0).at[pl.ds(0, 3)]

    def reduce_end(which):
        wait_bytes(three_parts(which), gr.at[which, 3])

    gather_end(0)
    red[...] = jnp.dot(x_v[...], fw1[...].reshape(CHANNELS, BOTTLE), preferred_element_type=F32)

    def sums_of(ref, start, width):
        def body(row, carry):
            values = grouped(ref[pl.ds(row, CHUNK), start : start + width])
            return carry[0] + jnp.sum(values, axis=0), carry[1] + jnp.sum(values * values, axis=0)

        zero = jnp.zeros((8, width), F32)
        return over_rows(body, (zero, zero))

    def joined(found):
        both = [jnp.concatenate(item, axis=1) for item in zip(*found)]
        return fold_lanes(stack_sums(micro_sum(both[0]), micro_sum(both[1])))

    def both_sums(name):
        return unstack_sums(unfold_lanes(sum_end(name)))

    sum_start("reduced", joined([sums_of(red, 0, 256)]))

    gy_copy.wait()
    to_rows(gy4, gy_v)
    wait_bytes(np_slots.at[pl.ds(0, n_dp - 1)], np_sems.at[1])
    np_full[...] = jnp.zeros(np_full.shape, F32)
    for d in range(n_dp):
        at = shard * d // 128
        np_full[at : at + 8, :] = np_full[at : at + 8, :] + np_slots[d]

    def vector(at, width):
        rows = [np_full[at // 128 + k : at // 128 + k + 1, :] for k in range(width // 128)]
        return jnp.concatenate(rows, axis=1) if len(rows) > 1 else rows[0]

    gain_one, bias_one = vector(0, 256), vector(256, 256)
    gain_two, bias_two = vector(512, 512), vector(1024, 512)
    gain_pool, bias_pool = vector(1536, 128), vector(1664, 128)
    bias_expand = vector(1792, 512)
    gain_three, bias_three = vector(2304, 1024), vector(3328, 1024)

    gather_turn(1)
    gather_out(2)
    total, square = both_sums("reduced")
    center1, scale1, mul1, add1 = norm_terms(total, square, gain_one, bias_one, pixels)

    def make_active(row, carry):
        turned = grouped(red[pl.ds(row, CHUNK), :]) * mul1 + add1
        act[1, pl.ds(PAD + row, CHUNK), :] = flat(turned * sigmoid(turned))
        return carry

    over_rows(make_active, 0)
    gather_hand(1)
    place = lax.rem(lax.broadcasted_iota(jnp.int32, (CHUNK, BOTTLE), 0) // 4, SIDE)
    not_last = place != SIDE - 1
    not_first = place != 0

    def beside(side, row, distance, lanes=slice(0, BOTTLE)):
        near = act[side, pl.ds(PAD + row - 8, CHUNK + 16), lanes]
        return pltpu.roll(near, (CHUNK + 16 - distance) % (CHUNK + 16), 0)[8 : 8 + CHUNK]

    def shift_active(row, carry):
        act[2, pl.ds(PAD + row, CHUNK), :] = jnp.where(not_last, beside(1, row, 4), 0.0)
        act[0, pl.ds(PAD + row, CHUNK), :] = jnp.where(not_first, beside(1, row, -4), 0.0)
        return carry

    over_rows(shift_active, 0)

    def make_columns(row, carry):
        for tap in range(9):
            down, side = tap // 3 - 1, tap % 3
            values = act[side, pl.ds(PAD + row + 56 * down, CHUNK), :].astype(BF16)
            columns[0, pl.ds(row, CHUNK), tap * 128 : tap * 128 + 128] = values[:, 0:128]
            columns[1, pl.ds(row, CHUNK), tap * 128 : tap * 128 + 128] = values[:, 128:256]
        return carry

    over_rows(make_columns, 0)
    gather_end(1)
    own_half = n_dp // 2

    def filters(group):
        return fwc[group * own_half : (group + 1) * own_half].reshape(9 * 128, BOTTLE)

    halves2 = (slice(0, 256), slice(256, 512))
    for group, lanes in enumerate(halves2):
        wid[:, lanes] = jnp.dot(columns[group], filters(group), preferred_element_type=F32)
        sum_start(f"widened{group}", joined([sums_of(wid, group * 256, 256)]))
    gather_turn(2)
    sum_turn("widened0")
    sum_turn("widened1")
    gather_hand(2)

    norm2 = []
    pooled = jnp.zeros((8, BOTTLE), F32)
    for group, lanes in enumerate(halves2):
        total, square = both_sums(f"widened{group}")
        norm2.append(norm_terms(total, square, gain_two[:, lanes], bias_two[:, lanes], pixels))
        m2, a2 = norm2[group][2:4]

        def make_splits(row, carry):
            turned = grouped(wid[pl.ds(row, CHUNK), lanes]) * m2 + a2
            values = turned * sigmoid(turned)
            splits[pl.ds(row, CHUNK), lanes] = flat(values)
            return carry + jnp.sum(values, axis=0)

        pooled = over_rows(make_splits, pooled)
    pooled = image_sum(pooled) * (1.0 / (SIDE * SIDE))
    gather_end(2)
    last = fpe[:, :, 0:CHANNELS].reshape(BOTTLE, CHANNELS)
    squeeze = fpe[:, :, 1024:1152].reshape(BOTTLE, INNER)
    ex_both = fpe[:, :, 1152:1408]
    expand = jnp.concatenate(
        [
            ex_both[:, 0:ex_rows].reshape(INNER, 256),
            ex_both[:, ex_rows : 2 * ex_rows].reshape(INNER, 256),
        ],
        axis=1,
    )
    pre_pool = exact_dot(pooled, squeeze, False)
    sum_start("pool", stack_sums(pair_sum(pre_pool), pair_sum(pre_pool * pre_pool)))
    first_micro = lax.rem(row_ids(BOTTLE), 4) < 2

    def make_normed(row, carry):
        rows = pl.ds(row, CHUNK)
        normed = (grouped(red[rows, :]) - center1) * scale1
        dwid[rows, 0:256] = flat(jnp.where(first_micro, normed, 0.0)).astype(BF16)
        dwid[rows, 256:512] = flat(jnp.where(first_micro, 0.0, normed)).astype(BF16)
        return carry + jnp.sum(grouped(x_v[rows, :].astype(F32)), axis=0)

    image_sums = micro_sum(over_rows(make_normed, jnp.zeros((8, CHANNELS), F32)))
    image_sums = fold_lanes(image_sums)
    image_sums = jnp.where(row_ids(512) < 4, image_sums, pltpu.roll(image_sums, 4, 0))
    image_sums = jnp.where(row_ids(256) < 4, image_sums[:, 0:256], image_sums[:, 256:512])
    normed_images = tdot(dwid[...], x_v[...]).astype(BF16)
    normed_images = normed_images.reshape(2, 2, 2, BOTTLE // 4, CHANNELS)
    for m in range(2):
        gb[:, :, m * (BOTTLE // 4) : (m + 1) * (BOTTLE // 4)] = normed_images[m]
    reduce_core(5)
    total, square = unstack_sums(sum_end("pool"))
    center_p, scale_p, mul_p, add_p = norm_terms(total, square, gain_pool, bias_pool, pictures)
    normed_p = (pre_pool - center_p) * scale_p
    norm_p = pre_pool * mul_p + add_p
    gate_p = sigmoid(norm_p)
    hidden = norm_p * gate_p
    slope_p = gate_p * (1.0 + norm_p * (1.0 - gate_p))
    logits = exact_dot(hidden, expand, False) + bias_expand
    left, right = logits[:, 0:256], logits[:, 256:512]
    most = jnp.maximum(left, right)
    left, right = jnp.exp(left - most), jnp.exp(right - most)
    att0 = left / (left + right)
    att1 = right / (left + right)

    def make_mixed(row, carry):
        rows = pl.ds(row, CHUNK)
        values = grouped(splits[rows, 0:256]) * att0 + grouped(splits[rows, 256:512]) * att1
        mixed[rows, :] = flat(values).astype(BF16)
        return carry

    over_rows(make_mixed, 0)
    halves3 = (slice(0, 512), slice(512, 1024))
    blocks3 = [[slice(512 * h + k, 512 * h + k + 256) for k in (0, 256)] for h in range(2)]
    for half, lanes in enumerate(halves3):
        proj[:, lanes] = jnp.dot(mixed[...], last[:, lanes], preferred_element_type=F32)
        payload = joined([sums_of(proj, 512 * half + k, 256) for k in (0, 256)])
        if half == 0:
            payload = jnp.concatenate([payload, image_sums], axis=0)
        sum_start(f"projected{half}", payload)
    sum_turn("projected0")
    sum_turn("projected1")
    reduce_y(5)

    norm3 = []
    zero = jnp.zeros((8, 256), F32)
    for half, lanes in enumerate(halves3):
        whole = sum_end(f"projected{half}")
        if half == 0:
            image_sums = whole[8:16]
        total, square = unstack_sums(unfold_lanes(whole[0:8]))
        norm3.append(norm_terms(total, square, gain_three[:, lanes], bias_three[:, lanes], pixels))
        found = []
        for k, block in enumerate(blocks3[half]):
            c3, s3, m3, a3 = (item[:, k * 256 : k * 256 + 256] for item in norm3[half])

            def make_out(row, carry):
                rows = pl.ds(row, CHUNK)
                values = grouped(proj[rows, block])
                summed = grouped(x_v[rows, block].astype(F32)) + (values * m3 + a3)
                gate = sigmoid(summed)
                bo4[pl.ds(row // 4, CHUNK // 4), :, block] = by_four(summed * gate).astype(BF16)
                upstream = grouped(gy_v[rows, block].astype(F32)) * (
                    gate * (1.0 + summed * (1.0 - gate))
                )
                up[rows, block] = flat(upstream)
                normed = (values - c3) * s3
                return carry[0] + jnp.sum(upstream, axis=0), carry[1] + jnp.sum(
                    upstream * normed, axis=0
                )

            found.append(over_rows(make_out, (zero, zero)))
        sum_start(f"back_projected{half}", joined(found))
    bo_copy = pltpu.make_async_copy(bo4, bo_hbm, local_sem.at[2])
    bo_copy.start()

    def write_norm(at, pattern):
        at = at // 128
        both = pattern[0:1, :] + pattern[2:3, :]
        for k in range(both.shape[1] // 128):
            np_full[at + k : at + k + 1, :] = both[:, k * 128 : k * 128 + 128]

    sum_turn("back_projected0")
    sum_turn("back_projected1")
    reduce_owner(5)

    for half, lanes in enumerate(halves3):
        bias_sum, gain_sum = both_sums(f"back_projected{half}")
        write_norm(2304 + 512 * half, gain_sum)
        write_norm(3328 + 512 * half, bias_sum)
        by_value, constant = back_terms(*norm3[half][0:3], bias_sum, gain_sum, pixels)
        for k, block in enumerate(blocks3[half]):
            m3, v3, k3 = (
                item[:, k * 256 : k * 256 + 256] for item in (norm3[half][2], by_value, constant)
            )

            def make_dproj(row, carry):
                rows = pl.ds(row, CHUNK)
                values = grouped(up[rows, block]) * m3 + grouped(proj[rows, block]) * v3 + k3
                dproj[rows, block] = flat(values).astype(BF16)
                return carry

            over_rows(make_dproj, 0)
        part_mixed = dot_t(dproj[:, lanes], last[:, lanes])
        d_mixed[...] = part_mixed if half == 0 else d_mixed[...] + part_mixed

    def attend(row, carry):
        rows = pl.ds(row, CHUNK)
        values = grouped(d_mixed[rows, :])
        return (
            carry[0] + jnp.sum(values * grouped(splits[rows, 0:256]), axis=0),
            carry[1] + jnp.sum(values * grouped(splits[rows, 256:512]), axis=0),
        )

    d_att0, d_att1 = over_rows(attend, (zero, zero))
    d_att0, d_att1 = image_sum(d_att0), image_sum(d_att1)
    both = att0 * d_att0 + att1 * d_att1
    d_logits = jnp.concatenate([att0 * (d_att0 - both), att1 * (d_att1 - both)], axis=1)
    d_hidden = exact_dot(d_logits, expand, True)
    d_pool = d_hidden * slope_p
    per_micro = stack_sums(pair_sum(d_pool), pair_sum(d_pool * normed_p))
    sum_start("back_pool", per_micro)
    ex_sum = pair_sum(d_logits)
    ex_sum = ex_sum + pltpu.roll(ex_sum, 2, 0)
    ex_rows_sum = ex_sum[:, 0:128]
    for k in range(1, 4):
        ex_rows_sum = jnp.where(row_ids(128) == k, ex_sum[:, k * 128 : k * 128 + 128], ex_rows_sum)

    grad_ex = image_dot(hidden, d_logits)
    grad_ex = grad_ex.reshape(n_dp, ex_rows, 512)
    ge[:, 0:ex_rows, 128:384] = grad_ex[:, :, 0:256]
    ge[:, ex_rows : 2 * ex_rows, 128:384] = grad_ex[:, :, 256:512]
    ge[:, :, 384:512] = jnp.zeros((n_dp, 2 * ex_rows, 128), F32)
    g3[...] = tdot(mixed[...], dproj[...]).reshape(g3.shape)
    reduce_core(3)
    held = []
    for group, att in ((0, att0), (1, att1)):
        lanes = halves2[group]
        c2, s2, m2, a2 = norm2[group]

        def make_dn2(row, carry):
            rows = pl.ds(row, CHUNK)
            values = grouped(wid[rows, lanes])
            turned = values * m2 + a2
            gate = sigmoid(turned)
            slope = gate * (1.0 + turned * (1.0 - gate))
            down = grouped(d_mixed[rows, :]) * att * slope
            dn2[rows, lanes] = flat(down)
            splits[rows, lanes] = flat(slope)
            normed = (values - c2) * s2
            terms = (down, down * normed, slope, slope * normed)
            return tuple(item + jnp.sum(term, axis=0) for item, term in zip(carry, terms))

        held.append([image_sum(item) for item in over_rows(make_dn2, (zero,) * 4)])
    pool_bias_sum, pool_gain_sum = unstack_sums(sum_end("back_pool"))
    write_norm(1536, pool_gain_sum)
    write_norm(1664, pool_bias_sum)
    d_pre_pool = mul_p * (
        d_pool - pool_bias_sum * (1.0 / pictures) - normed_p * (pool_gain_sum * (1.0 / pictures))
    )
    d_pooled = exact_dot(d_pre_pool, squeeze, True) * (1.0 / (SIDE * SIDE))
    for group in range(2):
        down, down_normed, slope, slope_normed = held[group]
        payload = fold_lanes(
            stack_sums(
                pair_sum(down + d_pooled * slope), pair_sum(down_normed + d_pooled * slope_normed)
            )
        )
        if group == 1:
            payload = jnp.concatenate([payload, ex_rows_sum], axis=0)
        sum_start(f"back_widened{group}", payload)
    ge[:, :, 0:128] = image_dot(pooled, d_pre_pool).reshape(n_dp, 2 * ex_rows, 128)
    reduce_core(4)
    sum_turn("back_widened0")
    sum_turn("back_widened1")
    reduce_y(3)
    reduce_y(4)
    back_total = owner_total(5)
    back_own[0] = back_total[0 : BOTTLE // 4]
    back_own[1] = back_total[BOTTLE // 4 :]

    small_zero = jnp.zeros((8, 128), F32)
    found = []
    for group, lanes in enumerate(halves2):
        whole = sum_end(f"back_widened{group}")
        if group == 1:
            np_full[14:18, :] = whole[8:12]
        bias_sum, gain_sum = unstack_sums(unfold_lanes(whole[0:8]))
        write_norm(512 + 256 * group, gain_sum)
        write_norm(1024 + 256 * group, bias_sum)
        m2 = norm2[group][2]
        v2, k2 = back_terms(*norm2[group][0:3], bias_sum, gain_sum, pixels)
        pooled_m2 = d_pooled * m2

        def make_dwid(row, carry):
            rows = pl.ds(row, CHUNK)
            values = grouped(dn2[rows, lanes]) * m2 + grouped(splits[rows, lanes]) * pooled_m2
            values = values + grouped(wid[rows, lanes]) * v2 + k2
            dwid[rows, lanes] = flat(values).astype(BF16)
            return carry

        over_rows(make_dwid, 0)
        gc[group * own_half : (group + 1) * own_half] = tdot(
            columns[group], dwid[:, lanes]
        ).reshape(own_half, 2, 9 * 128 // own_half // 2, BOTTLE)
    reduce_core(1)
    reduce_core(2)
    for group, lanes in enumerate(halves2):
        dcol[PAD : PAD + ROWS, group * 1152 : group * 1152 + 1152] = dot_t(
            dwid[:, lanes], filters(group)
        )
        inner = slice(group * 128, group * 128 + 128)

        def gather_taps(row, carry):
            for side in range(3):
                total = None
                for down in range(3):
                    at = group * 1152 + (3 * down + side) * 128
                    values = dcol[pl.ds(PAD + row - 56 * (down - 1), CHUNK), at : at + 128]
                    total = values if total is None else total + values
                act[side, pl.ds(PAD + row, CHUNK), inner] = total
            return carry

        over_rows(gather_taps, 0)
        c1, s1, m1, a1 = (item[:, inner] for item in (center1, scale1, mul1, add1))
        not_first1, not_last1 = not_first[:, inner], not_last[:, inner]

        def make_dn1(row, carry):
            rows = pl.ds(row, CHUNK)
            d_active = act[1, pl.ds(PAD + row, CHUNK), inner]
            d_active = d_active + jnp.where(not_first1, beside(2, row, -4, inner), 0.0)
            d_active = d_active + jnp.where(not_last1, beside(0, row, 4, inner), 0.0)
            values = grouped(red[rows, inner])
            turned = values * m1 + a1
            gate = sigmoid(turned)
            slope = gate * (1.0 + turned * (1.0 - gate))
            down = grouped(d_active) * slope
            dn1[rows, inner] = flat(down)
            mixed[rows, inner] = flat(down * m1).astype(BF16)
            normed = (values - c1) * s1
            return carry[0] + jnp.sum(down, axis=0), carry[1] + jnp.sum(down * normed, axis=0)

        bias_sum, gain_sum = over_rows(make_dn1, (small_zero, small_zero))
        found.append((bias_sum, gain_sum))
        if group == 1:
            sum_start("back_reduced", joined(found))
        if group == 0:
            reduce_owner(3)
            reduce_owner(4)
            reduce_y(1)
    reduce_y(2)
    g1[...] = tdot(mixed[...], x_v[...]).reshape(g1.shape)
    reduce_core(0)
    bias_sum, gain_sum = both_sums("back_reduced")
    write_norm(0, gain_sum)
    write_norm(256, bias_sum)
    by_value, constant = back_terms(center1, scale1, mul1, bias_sum, gain_sum, pixels)
    def make_dred(row, carry):
        rows = pl.ds(row, CHUNK)
        values = grouped(dn1[rows, :]) * mul1 + grouped(red[rows, :]) * by_value + constant
        dred[rows, :] = flat(values).astype(BF16)
        return carry

    over_rows(make_dred, 0)
    reduce_owner(1)
    proj[...] = dot_t(dred[...], fw1[...].reshape(CHANNELS, BOTTLE))
    reduce_y(0)

    by_bias = mul1 * bias_sum * (1.0 / pixels)
    by_gain = mul1 * gain_sum * (1.0 / pixels)
    quarter_lanes = CHANNELS // 4 // (n_dp // 4)
    own_rows = image_sums[:, 0:quarter_lanes]
    for k in range(1, n_dp // 4):
        there = image_sums[:, k * quarter_lanes : (k + 1) * quarter_lanes]
        own_rows = jnp.where(lax.rem(dp, n_dp // 4) == k, there, own_rows)
    own_quarter = lax.div(dp, n_dp // 4)
    ids = row_ids(quarter_lanes)
    in_quarter = lax.div(ids, 4) + 2 * lax.rem(ids, 2) == own_quarter
    own_sums = [
        jnp.sum(
            jnp.where(in_quarter & (lax.div(lax.rem(ids, 4), 2) == m), own_rows, 0.0),
            axis=0,
            keepdims=True,
        )
        for m in range(2)
    ]
    ids = row_ids(128)
    fix[0] = row_dot(by_bias, jnp.where(ids == 0, own_sums[0], jnp.where(ids == 2, own_sums[1], 0.0)))
    for m in range(2):
        fix[1 + m] = row_dot(by_gain, jnp.where(ids == 2 * m, 1.0, 0.0))
    reduce_spread(3)
    reduce_spread(4)

    def make_dx(row, carry):
        for start in range(0, CHANNELS, 256):
            lanes = slice(start, start + 256)
            values = up[pl.ds(row, CHUNK), lanes] + proj[pl.ds(row, CHUNK), lanes]
            dx4[pl.ds(row // 4, CHUNK // 4), :, lanes] = values.reshape(CHUNK // 4, 4, 256)
        return carry

    over_rows(make_dx, 0)
    dx_copy = pltpu.make_async_copy(dx4, dx_hbm, local_sem.at[3])
    dx_copy.start()
    norm_rows = np_full[0:8, :]
    for d in range(1, n_dp):
        at = shard * d // 128
        norm_rows = jnp.where(dp == d, np_full[at : at + 8, :], norm_rows)
    norm_rows = pltpu.roll(norm_rows, lax.rem(128 - turn, 128), 1)
    gn_out[...] = jnp.where(lanes_id < 128 - turn, norm_rows, pltpu.roll(norm_rows, 7, 0))
    reduce_owner(2)
    reduce_owner(0)
    reduce_spread(1)
    reduce_spread(2)
    reduce_spread(0)
    out_copies = [
        pltpu.make_async_copy(source, target, local_sem.at[10 + k])
        for k, (source, target) in enumerate(
            (
                (gn_out, gn_hbm),
                (fs[2], f3_hbm),
                (fs[3], fe_hbm),
                (fs[1], fc_hbm),
                (fs[0], f1_hbm),
            )
        )
    ]
    out_copies[0].start()
    for which in (3, 4, 1, 2, 0):
        reduce_end(which)
        if which != 1:
            out_copies[{3: 1, 4: 2, 2: 3, 0: 4}[which]].start()

    bo_copy.wait()
    dx_copy.wait()
    for copy in out_copies:
        copy.wait()
    for k in STATS:
        if k in DIRECT:
            wait_bytes(ar_slots_a[k].at[pl.ds(0, everyone - 1)], ar_send_a.at[order[k]])
        else:
            wait_bytes(ar_slots_a[k].at[pl.ds(0, plane_size - 1)], ar_send_a.at[order[k]])
            wait_bytes(ar_slots_b[k].at[pl.ds(0, planes - 1)], ar_send_b.at[order[k]])
    wait_bytes(np_slots.at[pl.ds(0, n_dp - 1)], np_sems.at[0])
    for which in range(3):
        wait_bytes(seven(which), ws.at[which, 0])
        for stage in range(1, 4):
            wait_bytes(quarters[which](core, half_y), ws.at[which, stage])
    for which in range(6):
        wait_bytes(r1s[which], gs.at[which, 0])
        wait_bytes(r2s[which], gs.at[which, 1])
        wait_bytes(r3s[which].at[pl.ds(0, n_dp - 1)], gs.at[which, 2])
        if which < 5:
            wait_bytes(three_parts(which), gs.at[which, 3])


def update_kernel(*refs):
    sources, targets = refs[0:25], refs[25:45]
    inputs, outs, through = refs[45:68], refs[68:86], refs[86:88]
    pass_sems, in_sems, out_sems = refs[88:91]
    fetching, passing = [], []
    half = SIDE * SIDE // 2
    for number, (which, at, count) in enumerate(((1, 0, half), (1, half, half), (0, 0, 2 * half))):
        rows = pl.ds(at, count)
        fetching.append(
            pltpu.make_async_copy(
                sources[which].at[rows], through[which].at[rows], pass_sems.at[0, number]
            )
        )
        passing.append(
            pltpu.make_async_copy(
                through[which].at[rows], targets[which].at[rows], pass_sems.at[1, number]
            )
        )
    for copy in fetching:
        copy.start()
    coming = [
        pltpu.make_async_copy(source, held, in_sems.at[k])
        for k, (source, held) in enumerate(zip(sources[2:], inputs))
    ]
    for copy in coming:
        copy.start()
    grads, states = inputs[0:5], inputs[5:23]
    going = [
        pltpu.make_async_copy(held, target, out_sems.at[k])
        for k, (held, target) in enumerate(zip(outs, targets[2:]))
    ]
    ex_rows = states[9].shape[0]
    shard = states[15].shape[0]
    fans = (CHANNELS, 9 * BOTTLE // RADIX, BOTTLE, INNER // 8, BOTTLE)
    for copy in coming[0:5]:
        copy.wait()
    found = (
        grads[0][...].T,
        grads[1][...],
        grads[3][:, 0:128],
        jnp.concatenate([grads[3][0:ex_rows, 128:384], grads[3][ex_rows:, 128:384]], axis=1),
        grads[2][...],
    )
    for order, k in enumerate((3, 2, 4, 0, 1)):
        for copy in coming[5 + 3 * k : 8 + 3 * k]:
            copy.wait()
        new = adamw(
            states[3 * k][...],
            states[3 * k + 1][...],
            states[3 * k + 2][...],
            found[k],
            2.0 * fans[k] ** (-0.5),
            DECAY,
        )
        for j in range(3):
            outs[3 * k + j][...] = new[j]
            going[3 * k + j].start()
        if order < 3:
            fetching[order].wait()
            passing[order].start()
    for copy in coming[20:23]:
        copy.wait()
    for at in range(0, shard, 128):
        width = min(128, shard - at)
        lanes = pl.ds(at, width)
        new = adamw(
            *[states[15 + j][lanes].reshape(1, width) for j in range(3)],
            grads[4][at // 128 : at // 128 + 1, 0:width],
            NORM_RATE,
            0.0,
        )
        for j in range(3):
            outs[15 + j][lanes] = new[j].reshape(width)
    for copy in going[15:18]:
        copy.start()
    for copy in passing + going:
        copy.wait()


def fused_device(
    images,
    out_grad,
    reduce_weight,
    reduce_moment,
    reduce_second,
    conv_weight,
    conv_moment,
    conv_second,
    squeeze_weight,
    squeeze_moment,
    squeeze_second,
    expand_weight,
    expand_moment,
    expand_second,
    project_weight,
    project_moment,
    project_second,
    norm_params,
    norm_moment,
    norm_second,
):
    n_dp, n_rep = lax.axis_size("dp"), lax.axis_size("rep")
    by_pixel = lambda values: jnp.transpose(values, (1, 2, 0, 3)).reshape(-1, 4, CHANNELS)
    qc = conv_weight.shape[0] // 2
    q1 = reduce_weight.shape[0] // 4
    pe = squeeze_weight.shape[0]
    vmem = pltpu.VMEM
    pixel_form = (SIDE * SIDE, 4, CHANNELS)
    scratch = [
        *[
            vmem(values.shape, F32)
            for values in (
                reduce_weight,
                conv_weight,
                squeeze_weight,
                expand_weight,
                project_weight,
                norm_params,
            )
        ],
        vmem((8, 128), F32),
        vmem(pixel_form, BF16),
        vmem(pixel_form, BF16),
        vmem((ROWS, CHANNELS), BF16),
        vmem((ROWS, CHANNELS), BF16),
        vmem((n_dp, 2, 2, q1, BOTTLE), BF16),
        vmem((n_dp, 2, qc, BOTTLE), BF16),
        vmem((n_dp, pe, 1536), BF16),
        vmem((pe, 1536), BF16),
        vmem((n_dp, 8, 128), F32),
        vmem((40, 128), F32),
        vmem((ROWS, BOTTLE), F32),
        vmem((3, ROWS + 2 * PAD, BOTTLE), F32),
        vmem((2, ROWS, 9 * 128), BF16),
        vmem((ROWS, 512), F32),
        vmem((ROWS, 512), F32),
        vmem((ROWS, BOTTLE), BF16),
        vmem((ROWS, CHANNELS), F32),
        vmem((ROWS, CHANNELS), F32),
        vmem(pixel_form, BF16),
        vmem(pixel_form, F32),
        vmem((ROWS, CHANNELS), BF16),
        vmem((ROWS, BOTTLE), F32),
        vmem((ROWS, 512), F32),
        vmem((ROWS, 512), BF16),
        vmem((ROWS + 2 * PAD, 2 * 9 * 128), F32),
        vmem((ROWS, BOTTLE), F32),
        vmem((ROWS, BOTTLE), BF16),
        vmem((2, 2, BOTTLE // 4, CHANNELS), F32),
        vmem((n_dp, 2, qc, BOTTLE), F32),
        vmem((n_dp, pe, CHANNELS), F32),
        vmem((n_dp, pe, 512), F32),
        vmem((2, 2, BOTTLE // 2, CHANNELS), BF16),
        vmem((3, BOTTLE, CHANNELS // n_dp), F32),
        vmem((2, BOTTLE // 4, CHANNELS // n_dp), F32),
    ]
    direct = n_dp * n_rep
    scratch += [
        vmem((direct if k in DIRECT else 2 * n_rep,) + shape, F32) for k, shape in STATS.items()
    ]
    scratch += [vmem((n_dp // 2,) + shape, F32) for shape in STATS.values()]
    cut = 64
    lanes1 = CHANNELS // n_dp
    half = [
        (2, BOTTLE // 4, CHANNELS),
        (n_dp, 2, cut, 128),
        (n_dp, 2, qc - cut, 128),
        (n_dp, pe, 512),
        (n_dp, pe, 256),
        (2, BOTTLE // 2, CHANNELS),
    ]
    quarter = [
        (BOTTLE // 4, CHANNELS),
        (n_dp, cut, 128),
        (n_dp, qc - cut, 128),
        (n_dp, pe, 256),
        (n_dp, pe, 128),
        (BOTTLE // 2, CHANNELS),
    ]
    final = [(2, 2, BOTTLE // 4, lanes1), (2, qc, BOTTLE), (pe, CHANNELS), (pe, 512)]
    sent = [BF16, BF16, BF16, BF16, F32, BF16]
    scratch += [vmem(shape, F32) for shape in half[:-1]] + [vmem(half[-1], BF16)]
    scratch += [vmem(shape, kind) for shape, kind in zip(quarter, sent)] * 3
    owned = [(BOTTLE // 4, lanes1)] + [shape[1:] for shape in quarter[1:-1]]
    owned += [(BOTTLE // 2, lanes1)]
    scratch += [vmem((n_dp,) + shape, kind) for shape, kind in zip(owned, sent)]
    scratch += [vmem(shape, F32) for shape in owned]
    scratch += [vmem(shape, F32) for shape in final]
    dma = pltpu.SemaphoreType.DMA
    scratch += [dma((15,))] + [dma((len(STATS),))] * 4 + [dma((2,))] + [dma((3, 4))] * 2 + [dma((6, 4))] * 2
    any_space = pl.BlockSpec(memory_space=pl.ANY)
    block_out, images_grad, sum1, sumc, sum3, sume, norm_grads = pl.pallas_call(
        functools.partial(block_kernel, n_dp, n_rep),
        out_shape=[
            jax.ShapeDtypeStruct(pixel_form, BF16),
            jax.ShapeDtypeStruct(pixel_form, F32),
            *[jax.ShapeDtypeStruct(shape, F32) for shape in final],
            jax.ShapeDtypeStruct((8, 128), F32),
        ],
        in_specs=[any_space] * 8,
        out_specs=[any_space] * 7,
        scratch_shapes=scratch,
        compiler_params=pltpu.CompilerParams(
            collective_id=0, has_side_effects=True, vmem_limit_bytes=63 * 1024 * 1024
        ),
    )(
        by_pixel(images),
        by_pixel(out_grad),
        reduce_weight,
        conv_weight,
        squeeze_weight,
        expand_weight,
        project_weight,
        norm_params,
    )
    states = (
        reduce_weight,
        reduce_moment,
        reduce_second,
        conv_weight,
        conv_moment,
        conv_second,
        squeeze_weight,
        squeeze_moment,
        squeeze_second,
        expand_weight,
        expand_moment,
        expand_second,
        project_weight,
        project_moment,
        project_second,
    )
    held = (*states, norm_params, norm_moment, norm_second)
    sums = (
        sum1.reshape(BOTTLE, lanes1),
        sumc.reshape(conv_weight.shape),
        sum3,
        sume,
        norm_grads,
    )
    block_out, images_grad, *updated = pl.pallas_call(
        update_kernel,
        out_shape=[
            jax.ShapeDtypeStruct(pixel_form, BF16),
            jax.ShapeDtypeStruct(pixel_form, F32),
            *[jax.ShapeDtypeStruct(state.shape, F32) for state in held],
        ],
        in_specs=[any_space] * 25,
        out_specs=[any_space] * 20,
        scratch_shapes=[vmem(values.shape, F32) for values in (*sums, *held, *held)]
        + [vmem(pixel_form, BF16), vmem(pixel_form, F32)]
        + [dma((2, 3)), dma((23,)), dma((18,))],
        compiler_params=pltpu.CompilerParams(vmem_limit_bytes=63 * 1024 * 1024),
    )(block_out, images_grad, *sums, *held)
    by_image = lambda values: jnp.transpose(
        values.reshape(SIDE, SIDE, images.shape[0], CHANNELS), (2, 0, 1, 3)
    )
    return (
        by_image(block_out),
        by_image(images_grad),
        *updated,
    )


def solution(mesh):
    placed = (
        P(("dp", "rep"), None, None, None),
        P(("dp", "rep"), None, None, None),
        P("dp", None),
        P("dp", None),
        P("dp", None),
        P("dp", None),
        P("dp", None),
        P("dp", None),
        P("dp", None),
        P("dp", None),
        P("dp", None),
        P("dp", None),
        P("dp", None),
        P("dp", None),
        P("dp", None),
        P("dp", None),
        P("dp", None),
        P("dp"),
        P("dp"),
        P("dp"),
    )
    n_dp, n_rep = mesh.shape["dp"], mesh.shape["rep"]
    whole_tiles = n_rep == 4 and n_dp % 2 == 0 and INNER % (16 * n_dp) == 0
    return jax.shard_map(
        fused_device if whole_tiles else per_device,
        mesh=mesh,
        in_specs=placed,
        out_specs=(
            P(("dp", "rep"), None, None, None),
            P(("dp", "rep"), None, None, None),
            P("dp", None),
            P("dp", None),
            P("dp", None),
            P("dp", None),
            P("dp", None),
            P("dp", None),
            P("dp", None),
            P("dp", None),
            P("dp", None),
            P("dp", None),
            P("dp", None),
            P("dp", None),
            P("dp", None),
            P("dp", None),
            P("dp", None),
            P("dp"),
            P("dp"),
            P("dp"),
        ),
        check_vma=False,
    )
```

```python
import functools
import jax
import jax.numpy as jnp
from jax import lax
from jax.experimental import pallas as pl
from jax.experimental.pallas import tpu as pltpu
from jax.sharding import PartitionSpec as P

CHANNELS = 1024
BOTTLE = 256
INNER = 128
RADIX = 2
SIDE = 14
MICRO = 2
STEP = 10


EPSILON = 1e-05
PRECISE = lax.Precision.HIGHEST
BETA_ONE = 0.9
BETA_TWO = 0.999
ADAM_EPSILON = 1e-08
DECAY = 0.01
NORM_RATE = 0.8
ROWS = 4 * SIDE * SIDE
NORM_WIDTH = 4352


def split_params(packed):
    widths = (
        BOTTLE,
        BOTTLE,
        RADIX * BOTTLE,
        RADIX * BOTTLE,
        INNER,
        INNER,
        RADIX * BOTTLE,
        CHANNELS,
        CHANNELS,
    )
    pieces = []
    offset = 0
    for segment in widths:
        pieces.append(lax.slice_in_dim(packed, offset, offset + segment))
        offset = offset + segment
    return pieces


def silu_slope(values):
    logistic = jax.nn.sigmoid(values)
    return logistic * (1.0 + values * (1.0 - logistic))


def norm_forward(values, gain, bias, count):
    flat = values.reshape(-1, values.shape[-1])
    total, square = lax.psum((jnp.sum(flat, axis=0), jnp.sum(flat * flat, axis=0)), ("dp", "rep"))
    center = total / count
    scale = lax.rsqrt(square / count - center * center + EPSILON)
    normed = (values - center) * scale
    return (normed * gain + bias, normed, scale)


def norm_backward(upstream, normed, scale, gain, count):
    flat_up = upstream.reshape(-1, upstream.shape[-1])
    flat_norm = normed.reshape(-1, normed.shape[-1])
    bias_sum, gain_sum = lax.psum(
        (jnp.sum(flat_up, axis=0), jnp.sum(flat_up * flat_norm, axis=0)), ("dp", "rep")
    )
    downstream = gain * scale * (upstream - bias_sum / count - normed * (gain_sum / count))
    return (downstream, gain_sum, bias_sum)


def patches(active):
    padded = jnp.pad(active, ((0, 0), (1, 1), (1, 1), (0, 0), (0, 0)))
    shifted = [
        padded[:, down_step : down_step + SIDE, side_step : side_step + SIDE]
        for down_step in range(3)
        for side_step in range(3)
    ]
    return jnp.stack(shifted, axis=4)


def unpatch(columns):
    total = jnp.zeros(
        (columns.shape[0], SIDE + 2, SIDE + 2, columns.shape[3], columns.shape[5]), jnp.float32
    )
    for down_step in range(3):
        for side_step in range(3):
            piece = columns[:, :, :, :, 3 * down_step + side_step]
            total = total + jnp.pad(
                piece,
                ((0, 0), (down_step, 2 - down_step), (side_step, 2 - side_step), (0, 0), (0, 0)),
            )
    return total[:, 1 : SIDE + 1, 1 : SIDE + 1]


def adamw(param, moment, second, gradient, rate, decay):
    moment_new = BETA_ONE * moment + (1.0 - BETA_ONE) * gradient
    second_new = BETA_TWO * second + (1.0 - BETA_TWO) * gradient * gradient
    ratio = (
        moment_new
        / (1.0 - BETA_ONE**STEP)
        / (jnp.sqrt(second_new / (1.0 - BETA_TWO**STEP)) + ADAM_EPSILON)
    )
    return (param - rate * (ratio + decay * param), moment_new, second_new)


def per_device(
    images,
    out_grad,
    reduce_weight,
    reduce_moment,
    reduce_second,
    conv_weight,
    conv_moment,
    conv_second,
    squeeze_weight,
    squeeze_moment,
    squeeze_second,
    expand_weight,
    expand_moment,
    expand_second,
    project_weight,
    project_moment,
    project_second,
    norm_params,
    norm_moment,
    norm_second,
):
    bf16 = jnp.bfloat16
    low_reduce = reduce_weight.astype(bf16)
    low_conv = conv_weight.astype(bf16)
    low_squeeze = squeeze_weight.astype(bf16)
    low_expand = expand_weight.astype(bf16)
    low_project = project_weight.astype(bf16)
    low_norm = norm_params.astype(bf16)
    devices = lax.axis_size("dp") * lax.axis_size("rep")
    per_batch = images.shape[0] // MICRO
    pixel_count = float(per_batch * SIDE * SIDE * devices)
    image_count = float(per_batch * devices)
    group_in = BOTTLE // RADIX
    grad_first = jnp.zeros((CHANNELS, BOTTLE), jnp.float32)
    grad_conv = jnp.zeros((RADIX, 9 * group_in, BOTTLE), jnp.float32)
    grad_squeeze = jnp.zeros((BOTTLE, INNER), jnp.float32)
    grad_expand = jnp.zeros((INNER, RADIX * BOTTLE), jnp.float32)
    grad_last = jnp.zeros((BOTTLE, CHANNELS), jnp.float32)
    grad_norms = jnp.zeros(
        (2 * BOTTLE + 3 * RADIX * BOTTLE + 2 * INNER + 2 * CHANNELS,), jnp.float32
    )
    outputs = []
    input_grads = []
    for number in range(MICRO):
        forward_set = (
            lax.all_gather(low_reduce, "dp", axis=0, tiled=True),
            lax.all_gather(low_conv, "dp", axis=0, tiled=True),
            lax.all_gather(low_squeeze, "dp", axis=0, tiled=True),
            lax.all_gather(low_expand, "dp", axis=0, tiled=True),
            lax.all_gather(low_project, "dp", axis=0, tiled=True),
            lax.all_gather(low_norm, "dp", axis=0, tiled=True),
        )
        first, conv, squeeze, expand, last, packed = forward_set
        (
            gain_one,
            bias_one,
            gain_two,
            bias_two,
            gain_pool,
            bias_pool,
            bias_expand,
            gain_three,
            bias_three,
        ) = split_params(packed.astype(jnp.float32))
        batched = images[number * per_batch : (number + 1) * per_batch]
        cotangent = out_grad[number * per_batch : (number + 1) * per_batch]
        reduced = jnp.einsum("nhwc,cb->nhwb", batched, first, preferred_element_type=jnp.float32)
        norm_one, normed_one, scale_one = norm_forward(reduced, gain_one, bias_one, pixel_count)
        active = jax.nn.silu(norm_one).astype(bf16)
        columns = patches(active.reshape(per_batch, SIDE, SIDE, RADIX, group_in)).reshape(
            per_batch * SIDE * SIDE, RADIX, 9 * group_in
        )
        conv_grouped = conv.reshape(RADIX, 9 * group_in, BOTTLE)
        widened = jnp.einsum(
            "prk,rko->pro", columns, conv_grouped, preferred_element_type=jnp.float32
        )
        widened = widened.reshape(per_batch, SIDE, SIDE, RADIX * BOTTLE)
        norm_two, normed_two, scale_two = norm_forward(widened, gain_two, bias_two, pixel_count)
        splits = jax.nn.silu(norm_two).reshape(per_batch, SIDE, SIDE, RADIX, BOTTLE)
        pooled = jnp.sum(jnp.sum(splits, axis=3), axis=(1, 2)) / (SIDE * SIDE)
        squeeze_float = squeeze.astype(jnp.float32)
        expand_float = expand.astype(jnp.float32)
        pre_pool = jnp.dot(pooled, squeeze_float, precision=PRECISE)
        norm_pool, normed_pool, scale_pool = norm_forward(
            pre_pool, gain_pool, bias_pool, image_count
        )
        hidden = jax.nn.silu(norm_pool)
        logits = (jnp.dot(hidden, expand_float, precision=PRECISE) + bias_expand).reshape(
            per_batch, RADIX, BOTTLE
        )
        attention = jax.nn.softmax(logits, axis=1)
        mixed = jnp.sum(splits * attention[:, None, None], axis=3).astype(bf16)
        projected = jnp.einsum("nhwb,bc->nhwc", mixed, last, preferred_element_type=jnp.float32)
        norm_three, normed_three, scale_three = norm_forward(
            projected, gain_three, bias_three, pixel_count
        )
        summed = batched.astype(jnp.float32) + norm_three
        outputs.append(jax.nn.silu(summed).astype(bf16))
        backward_set = (
            lax.all_gather(low_reduce, "dp", axis=0, tiled=True),
            lax.all_gather(low_conv, "dp", axis=0, tiled=True),
            lax.all_gather(low_squeeze, "dp", axis=0, tiled=True),
            lax.all_gather(low_expand, "dp", axis=0, tiled=True),
            lax.all_gather(low_project, "dp", axis=0, tiled=True),
            lax.all_gather(low_norm, "dp", axis=0, tiled=True),
        )
        first, conv, squeeze, expand, last, packed = backward_set
        gains_back = split_params(packed.astype(jnp.float32))
        conv_grouped = conv.reshape(RADIX, 9 * group_in, BOTTLE)
        expand_float = expand.astype(jnp.float32)
        squeeze_float = squeeze.astype(jnp.float32)
        upstream = cotangent.astype(jnp.float32) * silu_slope(summed)
        d_projected, gain_three_grad, bias_three_grad = norm_backward(
            upstream, normed_three, scale_three, gains_back[7], pixel_count
        )
        d_projected_low = d_projected.astype(bf16)
        grad_last = grad_last + jnp.einsum(
            "nhwb,nhwc->bc", mixed, d_projected_low, preferred_element_type=jnp.float32
        )
        d_mixed = jnp.einsum(
            "nhwc,bc->nhwb", d_projected_low, last, preferred_element_type=jnp.float32
        )
        d_splits = d_mixed[:, :, :, None] * attention[:, None, None]
        d_attention = jnp.sum(d_mixed[:, :, :, None] * splits, axis=(1, 2))
        d_logits = attention * (
            d_attention - jnp.sum(attention * d_attention, axis=1, keepdims=True)
        )
        flat_logits = d_logits.reshape(per_batch, RADIX * BOTTLE)
        grad_expand = grad_expand + jnp.dot(hidden.T, flat_logits, precision=PRECISE)
        d_hidden = jnp.dot(flat_logits, expand_float.T, precision=PRECISE)
        d_pool_norm = d_hidden * silu_slope(norm_pool)
        pool_bias_sum, pool_gain_sum, expand_bias_sum = lax.psum(
            (
                jnp.sum(d_pool_norm, axis=0),
                jnp.sum(d_pool_norm * normed_pool, axis=0),
                jnp.sum(flat_logits, axis=0),
            ),
            ("dp", "rep"),
        )
        d_pre_pool = (
            gains_back[4]
            * scale_pool
            * (
                d_pool_norm
                - pool_bias_sum / image_count
                - normed_pool * (pool_gain_sum / image_count)
            )
        )
        grad_squeeze = grad_squeeze + jnp.dot(pooled.T, d_pre_pool, precision=PRECISE)
        d_pooled = jnp.dot(d_pre_pool, squeeze_float.T, precision=PRECISE)
        d_splits = d_splits + (d_pooled / (SIDE * SIDE))[:, None, None, None, :]
        d_norm_two = d_splits.reshape(per_batch, SIDE, SIDE, RADIX * BOTTLE) * silu_slope(norm_two)
        d_widened, gain_two_grad, bias_two_grad = norm_backward(
            d_norm_two, normed_two, scale_two, gains_back[2], pixel_count
        )
        d_widened_low = d_widened.astype(bf16).reshape(per_batch * SIDE * SIDE, RADIX, BOTTLE)
        grad_conv = grad_conv + jnp.einsum(
            "prk,pro->rko", columns, d_widened_low, preferred_element_type=jnp.float32
        )
        d_columns = jnp.einsum(
            "pro,rko->prk", d_widened_low, conv_grouped, preferred_element_type=jnp.float32
        )
        d_active = unpatch(d_columns.reshape(per_batch, SIDE, SIDE, RADIX, 9, group_in)).reshape(
            per_batch, SIDE, SIDE, BOTTLE
        )
        d_norm_one = d_active * silu_slope(norm_one)
        d_reduced, gain_one_grad, bias_one_grad = norm_backward(
            d_norm_one, normed_one, scale_one, gains_back[0], pixel_count
        )
        d_reduced_low = d_reduced.astype(bf16)
        grad_first = grad_first + jnp.einsum(
            "nhwc,nhwb->cb", batched, d_reduced_low, preferred_element_type=jnp.float32
        )
        input_grads.append(
            upstream
            + jnp.einsum("nhwb,cb->nhwc", d_reduced_low, first, preferred_element_type=jnp.float32)
        )
        grad_norms = grad_norms + jnp.concatenate(
            [
                gain_one_grad,
                bias_one_grad,
                gain_two_grad,
                bias_two_grad,
                pool_gain_sum,
                pool_bias_sum,
                expand_bias_sum,
                gain_three_grad,
                bias_three_grad,
            ]
        )
    grad_conv = grad_conv.reshape(9 * BOTTLE, BOTTLE)
    partial_value = (
        lax.psum_scatter(grad_first, "dp", scatter_dimension=0, tiled=True),
        lax.psum_scatter(grad_conv, "dp", scatter_dimension=0, tiled=True),
        lax.psum_scatter(grad_squeeze, "dp", scatter_dimension=0, tiled=True),
        lax.psum_scatter(grad_expand, "dp", scatter_dimension=0, tiled=True),
        lax.psum_scatter(grad_last, "dp", scatter_dimension=0, tiled=True),
    )
    owned = lax.psum(
        (partial_value[0], partial_value[1], partial_value[2], partial_value[3], partial_value[4]),
        "rep",
    )
    shard_length = norm_params.shape[0]
    norm_grad_owned = lax.dynamic_slice_in_dim(
        grad_norms, lax.axis_index("dp") * shard_length, shard_length
    )
    reduce_new = adamw(
        reduce_weight, reduce_moment, reduce_second, owned[0], 2.0 * CHANNELS ** (-0.5), DECAY
    )
    conv_new = adamw(
        conv_weight,
        conv_moment,
        conv_second,
        owned[1],
        2.0 * (9 * BOTTLE // RADIX) ** (-0.5),
        DECAY,
    )
    squeeze_new = adamw(
        squeeze_weight, squeeze_moment, squeeze_second, owned[2], 2.0 * BOTTLE ** (-0.5), DECAY
    )
    expand_new = adamw(
        expand_weight, expand_moment, expand_second, owned[3], 2.0 * (INNER // 8) ** (-0.5), DECAY
    )
    project_new = adamw(
        project_weight, project_moment, project_second, owned[4], 2.0 * BOTTLE ** (-0.5), DECAY
    )
    norm_new = adamw(norm_params, norm_moment, norm_second, norm_grad_owned, NORM_RATE, 0.0)
    return (
        jnp.concatenate(outputs, axis=0),
        jnp.concatenate(input_grads, axis=0),
        reduce_new[0],
        reduce_new[1],
        reduce_new[2],
        conv_new[0],
        conv_new[1],
        conv_new[2],
        squeeze_new[0],
        squeeze_new[1],
        squeeze_new[2],
        expand_new[0],
        expand_new[1],
        expand_new[2],
        project_new[0],
        project_new[1],
        project_new[2],
        norm_new[0],
        norm_new[1],
        norm_new[2],
    )


MESH = pl.DeviceIdType.MESH
PAD = 64
CHUNK = 112
F32 = jnp.float32
BF16 = jnp.bfloat16
STATS = {
    "reduced": (8, 128),
    "widened0": (8, 128),
    "widened1": (8, 128),
    "pool": (4, 128),
    "images": (16, 128),
    "projected0": (8, 256),
    "projected1": (8, 256),
    "back_projected0": (8, 256),
    "back_projected1": (8, 256),
    "back_pool": (4, 128),
    "back_widened0": (8, 128),
    "back_widened1": (16, 128),
    "back_reduced0": (8, 128),
    "back_reduced1": (8, 128),
}
DIRECT = ("reduced", "pool", "back_pool")


def sigmoid(values):
    return 0.5 * jnp.tanh(0.5 * values) + 0.5


def row_ids(width):
    return lax.broadcasted_iota(jnp.int32, (8, width), 0)


def image_sum(rows):
    return rows + pltpu.roll(rows, 4, 0)


def pair_sum(rows):
    even = row_ids(rows.shape[1]) % 2 == 0
    return rows + jnp.where(even, pltpu.roll(rows, 7, 0), pltpu.roll(rows, 1, 0))


def micro_sum(rows):
    return pair_sum(image_sum(rows))


def stack_sums(first, second):
    return jnp.where(row_ids(first.shape[1]) < 4, first, second)


def unstack_sums(stacked):
    upper = row_ids(stacked.shape[1]) < 4
    turned = pltpu.roll(stacked, 4, 0)
    return jnp.where(upper, stacked, turned), jnp.where(upper, turned, stacked)


def four_rows(first, second):
    return jnp.concatenate([first[0:1], first[2:3], second[0:1], second[2:3]], axis=0)


def from_four(rows):
    earlier = lax.rem(row_ids(rows.shape[1]), 4) < 2
    return tuple(jnp.where(earlier, rows[k : k + 1], rows[k + 1 : k + 2]) for k in (0, 2))


def fold_lanes(stacked):
    half = stacked.shape[1] // 2
    even = row_ids(half) % 2 == 0
    return jnp.where(even, stacked[:, :half], stacked[:, half:])


def unfold_lanes(folded):
    even = row_ids(folded.shape[1]) % 2 == 0
    left = jnp.where(even, folded, pltpu.roll(folded, 1, 0))
    right = jnp.where(even, pltpu.roll(folded, 7, 0), folded)
    return jnp.concatenate([left, right], axis=1)


def norm_terms(total, square, gain, bias, count):
    center = total * (1.0 / count)
    scale = lax.rsqrt(square * (1.0 / count) - center * center + EPSILON)
    slope = scale * gain
    return center, scale, slope, bias - center * slope


def back_terms(center, scale, slope, bias_sum, gain_sum, count):
    by_value = -slope * scale * (gain_sum * (1.0 / count))
    constant = -slope * (bias_sum * (1.0 / count)) - by_value * center
    return by_value, constant


def tdot(left, right):
    return lax.dot_general(left, right, (((0,), (0,)), ((), ())), preferred_element_type=F32)


def dot_t(left, right):
    return lax.dot_general(left, right, (((1,), (1,)), ((), ())), preferred_element_type=F32)


def in_parts(values, parts):
    found = []
    for _ in range(parts):
        rounded = values.astype(BF16).astype(F32)
        found.append(rounded)
        values = values - rounded
    return found


def exact_dot(left, right, transposed):
    stacked = jnp.concatenate(in_parts(left, 3), axis=0).astype(BF16)
    wide = dot_t(stacked, right) if transposed else jnp.dot(stacked, right, preferred_element_type=F32)
    return wide[0:8] + wide[8:16] + wide[16:24]


def row_dot(left, right):
    high, low = in_parts(left, 2)
    other_high, other_low = in_parts(right, 2)
    return tdot(
        jnp.concatenate([high, high, low, low], axis=0).astype(BF16),
        jnp.concatenate([other_high, other_low, other_high, other_low], axis=0).astype(BF16),
    )


def image_dot(left, right):
    return row_dot(jnp.where(row_ids(left.shape[1]) < 4, left, 0.0), right)


def block_kernel(
    n_dp,
    n_rep,
    x_hbm,
    gy_hbm,
    w1_hbm,
    wc_hbm,
    sq_hbm,
    ex_hbm,
    w3_hbm,
    np_hbm,
    bo_hbm,
    dx_hbm,
    f1_hbm,
    fc_hbm,
    f3_hbm,
    fe_hbm,
    gn_hbm,
    w1_own,
    wc_own,
    sq_own,
    ex_own,
    w3_own,
    np_own,
    gn_out,
    x4,
    gy4,
    x_v,
    gy_v,
    fw1,
    fwc,
    fpe,
    pe_own,
    np_slots,
    np_full,
    red,
    act,
    columns,
    wid,
    splits,
    mixed,
    proj,
    up,
    bo4,
    dx4,
    dproj,
    d_mixed,
    dn2,
    dwid,
    dcol,
    dn1,
    dred,
    g1,
    gc,
    g3,
    ge,
    gb,
    fix,
    back_own,
    *rest,
):
    n_ar = len(STATS)
    order = {name: k for k, name in enumerate(STATS)}
    ar_slots_a = dict(zip(STATS, rest[0:n_ar]))
    ar_slots_b = dict(zip(STATS, rest[n_ar : 2 * n_ar]))
    rest = rest[2 * n_ar :]
    r1s, ys, r2s, ks, r3s, own = (rest[6 * i : 6 * i + 6] for i in range(6))
    fs, cs = rest[36:40], rest[40:44]
    rest = rest[44:]
    local_sem, ar_send_a, ar_recv_a, ar_send_b, ar_recv_b, np_sems, ws, wr, gs, gr = rest

    dp = lax.axis_index("dp")
    rep = lax.axis_index("rep")
    core = lax.rem(rep, 2)
    half_y = lax.div(rep, 2)
    planes = n_dp // 2
    plane_size = 2 * n_rep
    plane = lax.div(dp, 2)
    in_plane = lax.rem(dp, 2) * n_rep + rep
    sibling = (dp, half_y * 2 + (1 - core))
    across = (dp, (1 - half_y) * 2 + core)
    pixels = float(SIDE * SIDE * 2 * n_dp * n_rep)
    pictures = float(2 * n_dp * n_rep)

    x = lax.rem(dp, 2)
    if planes == 4:
        upper = lax.div(plane, 2)
        other_planes = [3 - 3 * upper, 2 - upper, 1 - plane + 4 * upper]
    else:
        other_planes = [lax.rem(plane + step, planes) for step in range(1, planes)]
    flips = ((1, 1, 1), (1, 1, 0), (1, 0, 1), (1, 0, 0), (0, 1, 1), (0, 1, 0), (0, 0, 1), (0, 0, 0))

    def of_flip(z, flip):
        there = [1 - own if turn else own for own, turn in zip((x, half_y, core), flip)]
        return (z * 2 + there[0], there[1] * 2 + there[2])

    plane_peers = [of_flip(plane, flip) for flip in flips[:-1]]
    column_peers = [of_flip(z, flips[-1]) for z in other_planes]
    owner_peers = [of_flip(z, flip) for z in other_planes for flip in (flips[3], flips[7])]
    owner_peers += [of_flip(plane, flips[3])]
    all_peers = [of_flip(z, flip) for z in other_planes for flip in flips] + plane_peers
    me, everyone = dp * n_rep + rep, n_dp * n_rep
    rep_peers = [(dp, lax.rem(rep + step, n_rep)) for step in range(1, n_rep)]

    def remote(src, dst, send_sem, recv_sem, device):
        return pltpu.make_async_remote_copy(
            src_ref=src,
            dst_ref=dst,
            send_sem=send_sem,
            recv_sem=recv_sem,
            device_id=device,
            device_id_type=MESH,
        )

    def send_all(ref, send_sem, recv_sem, peers):
        for device in peers:
            remote(ref, ref, send_sem, recv_sem, device).start()

    def wait_bytes(ref, sem):
        pltpu.make_async_copy(ref, ref, sem).wait()

    def over_rows(body, init):
        def step(index, carry):
            return body(pl.multiple_of(index * CHUNK, CHUNK), carry)

        return lax.fori_loop(0, ROWS // CHUNK, step, init)

    def grouped(values):
        return values.reshape(CHUNK // 8, 8, values.shape[-1])

    def by_four(values):
        return flat(values).reshape(CHUNK // 4, 4, values.shape[-1])

    def flat(values):
        return values.reshape(CHUNK, values.shape[-1])

    own_copies = [
        pltpu.make_async_copy(source, target, local_sem.at[4 + k])
        for k, (source, target) in enumerate(
            (
                (w1_hbm, w1_own),
                (np_hbm, np_own),
                (wc_hbm, wc_own),
                (w3_hbm, w3_own),
                (sq_hbm, sq_own),
                (ex_hbm, ex_own),
            )
        )
    ]
    for copy in own_copies:
        copy.start()
    x_copy = pltpu.make_async_copy(x_hbm, x4, local_sem.at[0])
    gy_copy = pltpu.make_async_copy(gy_hbm, gy4, local_sem.at[1])
    x_copy.start()
    barrier = pltpu.get_barrier_semaphore()
    for device in all_peers:
        pl.semaphore_signal(barrier, inc=1, device_id=device, device_id_type=MESH)

    part = core * 2 + half_y
    own_copies[0].wait()
    q1 = w1_own.shape[0] // 4
    fw1[dp, core, half_y] = w1_own[pl.ds(pl.multiple_of(part * q1, q1), q1), :].astype(BF16)
    core_lanes = pl.ds(pl.multiple_of(core * 128, 128), 128)
    pe_lanes = pl.ds(pl.multiple_of(part * 384, 128), 384)

    pl.semaphore_wait(barrier, everyone - 1)

    def quarter_w1(c, y):
        return fw1.at[:, c, y]

    def quarter_wc(c, y):
        return fwc.at[:, y, :, pl.ds(pl.multiple_of(c * 128, 128), 128)]

    def quarter_pe(c, y):
        return fpe.at[:, :, pl.ds(pl.multiple_of((c * 2 + y) * 384, 128), 384)]

    quarters = (quarter_w1, quarter_wc, quarter_pe)

    def piece(which, d):
        return (
            fw1.at[d, core, half_y],
            fwc.at[d, half_y, :, core_lanes],
            fpe.at[d, :, pe_lanes],
        )[which]

    def seven(which):
        return (
            fw1.at[pl.ds(0, n_dp - 1), core, half_y],
            fwc.at[pl.ds(0, n_dp - 1), half_y, :, core_lanes],
            fpe.at[pl.ds(0, n_dp - 1), :, pe_lanes],
        )[which]

    def gather_out(which):
        send_all(piece(which, dp), ws.at[which, 0], wr.at[which, 0], owner_peers)

    def gather_turn(which):
        wait_bytes(seven(which), wr.at[which, 0])
        mine = quarters[which](core, half_y)
        remote(mine, mine, ws.at[which, 1], wr.at[which, 1], across).start()
        remote(mine, mine, ws.at[which, 2], wr.at[which, 2], sibling).start()

    def gather_hand(which):
        theirs = quarters[which](core, 1 - half_y)
        wait_bytes(theirs, wr.at[which, 1])
        remote(theirs, theirs, ws.at[which, 3], wr.at[which, 3], sibling).start()

    def gather_end(which):
        wait_bytes(quarters[which](1 - core, half_y), wr.at[which, 2])
        wait_bytes(quarters[which](1 - core, 1 - half_y), wr.at[which, 3])

    def to_rows(source, target):
        def body(index, carry):
            values = source[pl.ds(index * (CHUNK // 4), CHUNK // 4)].astype(F32)
            row = pl.multiple_of(index * CHUNK, CHUNK)
            target[pl.ds(row, CHUNK), :] = values.reshape(CHUNK, CHANNELS).astype(BF16)
            return carry

        lax.fori_loop(0, ROWS // CHUNK, body, 0)

    gather_out(0)

    own_copies[1].wait()
    shard = np_own.shape[0]
    lanes_id = lax.broadcasted_iota(jnp.int32, (8, 128), 1)
    turn = lax.rem(shard * dp, 128)
    np_rows = []
    for at in range(0, shard, 128):
        width = min(128, shard - at)
        piece_row = np_own[pl.ds(at, width)].reshape(1, width)
        if width < 128:
            piece_row = jnp.concatenate([piece_row, jnp.zeros((1, 128 - width), F32)], axis=1)
        np_rows.append(piece_row)
    np_rows.append(jnp.zeros((8 - len(np_rows), 128), F32))
    np_turned = jnp.concatenate(np_rows, axis=0).astype(BF16).astype(F32)
    np_turned = pltpu.roll(np_turned, turn, 1)
    np_slots[dp] = jnp.where(lanes_id < turn, pltpu.roll(np_turned, 1, 0), np_turned)
    send_all(np_slots.at[dp], np_sems.at[0], np_sems.at[1], owner_peers)
    own_copies[2].wait()
    qc = wc_own.shape[0] // 2
    fwc[dp, half_y, :, core_lanes] = wc_own[
        pl.ds(pl.multiple_of(half_y * qc, qc), qc), core_lanes
    ].astype(BF16)
    for copy in own_copies[3:]:
        copy.wait()
    ex_rows = ex_own.shape[0]
    pe_own[:, 0:CHANNELS] = w3_own[...].astype(BF16)
    pe_own[:, 1024:1152] = sq_own[...].astype(BF16)
    pe_own[0:ex_rows, 1152:1408] = ex_own[:, 0:256].astype(BF16)
    pe_own[ex_rows : 2 * ex_rows, 1152:1408] = ex_own[:, 256:512].astype(BF16)
    pe_own[:, 1408:1536] = jnp.zeros((2 * ex_rows, 128), BF16)
    fpe[dp, :, pe_lanes] = pe_own[:, pe_lanes]
    gy_copy.start()
    x_copy.wait()
    to_rows(x4, x_v)
    gather_turn(0)
    zero_rows = jnp.zeros((PAD, BOTTLE), F32)
    for side in range(3):
        act[side, 0:PAD, :] = zero_rows
        act[side, PAD + ROWS : 2 * PAD + ROWS, :] = zero_rows
    for lane_block in range(9):
        dcol[0:PAD, lane_block * 256 : lane_block * 256 + 256] = zero_rows
        dcol[PAD + ROWS : 2 * PAD + ROWS, lane_block * 256 : lane_block * 256 + 256] = zero_rows
    gather_hand(0)

    def sum_start(k, payload):
        if k in DIRECT:
            ar_slots_a[k][me] = payload
            send_all(ar_slots_a[k].at[me], ar_send_a.at[order[k]], ar_recv_a.at[order[k]], all_peers)
        else:
            ar_slots_a[k][in_plane] = payload
            send_all(ar_slots_a[k].at[in_plane], ar_send_a.at[order[k]], ar_recv_a.at[order[k]], plane_peers)

    def sum_slots(slots, count):
        sums = [slots[slot] for slot in range(count)]
        while len(sums) > 1:
            sums = [sums[i] + sums[i + 1] for i in range(0, len(sums), 2)]
        return sums[0]

    def sum_turn(k):
        if k in DIRECT:
            return
        wait_bytes(ar_slots_a[k].at[pl.ds(0, plane_size - 1)], ar_recv_a.at[order[k]])
        ar_slots_b[k][plane] = sum_slots(ar_slots_a[k], plane_size)
        send_all(ar_slots_b[k].at[plane], ar_send_b.at[order[k]], ar_recv_b.at[order[k]], column_peers)

    def sum_end(k):
        if k in DIRECT:
            wait_bytes(ar_slots_a[k].at[pl.ds(0, everyone - 1)], ar_recv_a.at[order[k]])
            return sum_slots(ar_slots_a[k], everyone)
        wait_bytes(ar_slots_b[k].at[pl.ds(0, planes - 1)], ar_recv_b.at[order[k]])
        return sum_slots(ar_slots_b[k], planes)

    def lanes_of(index, width):
        return pl.ds(pl.multiple_of(index * width, 128), width)

    cut = 64
    conv_rows = {1: pl.ds(0, cut), 2: pl.ds(cut, gc.shape[2] - cut)}
    grads = (g1, gc, gc, g3, ge, gb)
    turned_kinds = (0, 5)

    def half_of(which, c):
        ref = grads[which]
        if which in turned_kinds:
            return ref.at[c]
        if which in conv_rows:
            return ref.at[:, :, conv_rows[which], lanes_of(c, 128)]
        return ref.at[:, :, lanes_of(c, (512, 256)[which - 3])]

    def y_part(which, ref, y):
        if which in turned_kinds:
            return ref.at[y]
        if which < 3:
            return ref.at[:, y]
        return ref.at[:, :, lanes_of(y, (256, 128)[which - 3])]

    def quarter_of(which, c, y):
        ref = grads[which]
        if which in turned_kinds:
            return ref.at[c, y]
        if which in conv_rows:
            return ref.at[:, y, conv_rows[which], lanes_of(c, 128)]
        return ref.at[:, :, lanes_of(c * 2 + y, (256, 128)[which - 3])]

    def final_part(which, c, y):
        if which == 0:
            return fs[0].at[c, y]
        if which in conv_rows:
            return fs[1].at[y, conv_rows[which], lanes_of(c, 128)]
        return fs[which - 1].at[:, lanes_of(c * 2 + y, (256, 128)[which - 3])]

    def of_owner(which, ref, d):
        return ref.at[:, lanes_of(d, CHANNELS // n_dp)] if which in turned_kinds else ref.at[d]

    def in_blocks(which, body):
        if which in turned_kinds:
            count = 4
            rows = grads[which].shape[2] // count
            block = lambda index: pl.ds(pl.multiple_of(index * rows, rows), rows)
        else:
            count, block = n_dp, lambda index: index

        def step(index, carry):
            body(block(index))
            return carry

        lax.fori_loop(0, count, step, 0)

    def in_halves(which, body):
        if which != 0:
            return in_blocks(which, body)

        def step(index, carry):
            rows = g1.shape[2] // 4
            at = pl.ds(pl.multiple_of(lax.rem(index, 4) * rows, rows), rows)
            body((lax.div(index, 4), at))
            return carry

        lax.fori_loop(0, 8, step, 0)

    def reduce_core(which):
        source = half_of(which, 1 - core)
        if which < 4:

            def round_one(at):
                cs[which][at] = source[at].astype(BF16)

            in_halves(which, round_one)
            source = cs[which]
        remote(source, r1s[which], gs.at[which, 0], gr.at[which, 0], sibling).start()

    def reduce_y(which):
        wait_bytes(r1s[which], gr.at[which, 0])
        away = quarter_of(which, core, 1 - half_y)
        mine = quarter_of(which, core, half_y)
        there = y_part(which, r1s[which], 1 - half_y)
        here = y_part(which, r1s[which], half_y)

        def add_away(at):
            ys[which][at] = (away[at].astype(F32) + there[at].astype(F32)).astype(
                ys[which].dtype
            )

        in_blocks(which, add_away)
        remote(ys[which], r2s[which], gs.at[which, 1], gr.at[which, 1], across).start()

        def add_mine(at):
            mine[at] = (mine[at].astype(F32) + here[at].astype(F32)).astype(mine.dtype)

        in_blocks(which, add_mine)

    def reduce_owner(which):
        wait_bytes(r2s[which], gr.at[which, 1])
        mine = quarter_of(which, core, half_y)

        def add(at):
            ks[which][at] = (mine[at].astype(F32) + r2s[which][at].astype(F32)).astype(
                ks[which].dtype
            )

        in_blocks(which, add)
        for device in owner_peers:
            remote(
                of_owner(which, ks[which], device[0]),
                r3s[which].at[dp],
                gs.at[which, 2],
                gr.at[which, 2],
                device,
            ).start()
        own[which][...] = of_owner(which, mine, dp)[...].astype(F32) + of_owner(
            which, r2s[which], dp
        )[...].astype(F32)
        r3s[which][dp] = jnp.zeros(own[which].shape, r3s[which].dtype)

    def owner_total(which):
        wait_bytes(r3s[which].at[pl.ds(0, n_dp - 1)], gr.at[which, 2])
        total = own[which][...]
        for slot in range(n_dp):
            total = total + r3s[which][slot].astype(F32)
        return total

    def reduce_spread(which):
        total = owner_total(which)
        if which == 0:
            rows = pl.ds(pl.multiple_of(part * (BOTTLE // 4), BOTTLE // 4), BOTTLE // 4)
            total = total - fix[0, rows, :]
            for m in range(2):
                total = total - fix[1 + m, rows, :] * back_own[m]
        mine = final_part(which, core, half_y)
        mine[...] = total
        send_all(mine, gs.at[which, 3], gr.at[which, 3], rep_peers)

    def three_parts(which):
        if which == 0:
            return fix.at[:, pl.ds(0, BOTTLE // 4)]
        if which in conv_rows:
            return r1s[which].at[pl.ds(0, 3)]
        return fs[which - 1].at[:, pl.ds(0, 3 * (256, 128)[which - 3])]

    def reduce_end(which):
        wait_bytes(three_parts(which), gr.at[which, 3])

    gather_end(0)
    red[...] = jnp.dot(x_v[...], fw1[...].reshape(CHANNELS, BOTTLE), preferred_element_type=F32)

    def sums_of(ref, start, width):
        def body(row, carry):
            values = grouped(ref[pl.ds(row, CHUNK), start : start + width])
            return carry[0] + jnp.sum(values, axis=0), carry[1] + jnp.sum(values * values, axis=0)

        zero = jnp.zeros((8, width), F32)
        return over_rows(body, (zero, zero))

    def joined(found):
        both = [jnp.concatenate(item, axis=1) for item in zip(*found)]
        return fold_lanes(stack_sums(micro_sum(both[0]), micro_sum(both[1])))

    def both_sums(name):
        return unstack_sums(unfold_lanes(sum_end(name)))

    sum_start("reduced", joined([sums_of(red, 0, 256)]))
    gather_out(1)

    gy_copy.wait()
    to_rows(gy4, gy_v)
    wait_bytes(np_slots.at[pl.ds(0, n_dp - 1)], np_sems.at[1])
    np_full[...] = jnp.zeros(np_full.shape, F32)
    for d in range(n_dp):
        at = shard * d // 128
        np_full[at : at + 8, :] = np_full[at : at + 8, :] + np_slots[d]

    def vector(at, width):
        rows = [np_full[at // 128 + k : at // 128 + k + 1, :] for k in range(width // 128)]
        return jnp.concatenate(rows, axis=1) if len(rows) > 1 else rows[0]

    gain_one, bias_one = vector(0, 256), vector(256, 256)
    gain_two, bias_two = vector(512, 512), vector(1024, 512)
    gain_pool, bias_pool = vector(1536, 128), vector(1664, 128)
    bias_expand = vector(1792, 512)
    gain_three, bias_three = vector(2304, 1024), vector(3328, 1024)

    gather_turn(1)
    total, square = both_sums("reduced")
    center1, scale1, mul1, add1 = norm_terms(total, square, gain_one, bias_one, pixels)

    def make_active(row, carry):
        turned = grouped(red[pl.ds(row, CHUNK), :]) * mul1 + add1
        act[1, pl.ds(PAD + row, CHUNK), :] = flat(turned * sigmoid(turned))
        return carry

    over_rows(make_active, 0)
    place = lax.rem(lax.broadcasted_iota(jnp.int32, (CHUNK, BOTTLE), 0) // 4, SIDE)
    not_last = place != SIDE - 1
    not_first = place != 0

    def beside(side, row, distance, lanes=slice(0, BOTTLE)):
        near = act[side, pl.ds(PAD + row - 8, CHUNK + 16), lanes]
        return pltpu.roll(near, (CHUNK + 16 - distance) % (CHUNK + 16), 0)[8 : 8 + CHUNK]

    def shift_active(row, carry):
        act[2, pl.ds(PAD + row, CHUNK), :] = jnp.where(not_last, beside(1, row, 4), 0.0)
        act[0, pl.ds(PAD + row, CHUNK), :] = jnp.where(not_first, beside(1, row, -4), 0.0)
        return carry

    over_rows(shift_active, 0)
    gather_hand(1)
    gather_out(2)

    def make_columns(row, carry):
        for tap in range(9):
            down, side = tap // 3 - 1, tap % 3
            values = act[side, pl.ds(PAD + row + 56 * down, CHUNK), :].astype(BF16)
            columns[0, pl.ds(row, CHUNK), tap * 128 : tap * 128 + 128] = values[:, 0:128]
            columns[1, pl.ds(row, CHUNK), tap * 128 : tap * 128 + 128] = values[:, 128:256]
        return carry

    over_rows(make_columns, 0)
    gather_end(1)
    own_half = n_dp // 2

    def filters(group):
        return fwc[group * own_half : (group + 1) * own_half].reshape(9 * 128, BOTTLE)

    halves2 = (slice(0, 256), slice(256, 512))
    for group, lanes in enumerate(halves2):
        wid[:, lanes] = jnp.dot(columns[group], filters(group), preferred_element_type=F32)
        sum_start(f"widened{group}", joined([sums_of(wid, group * 256, 256)]))
    sum_turn("widened0")
    sum_turn("widened1")
    gather_turn(2)

    norm2 = []
    pooled = jnp.zeros((8, BOTTLE), F32)
    for group, lanes in enumerate(halves2):
        total, square = both_sums(f"widened{group}")
        norm2.append(norm_terms(total, square, gain_two[:, lanes], bias_two[:, lanes], pixels))
        m2, a2 = norm2[group][2:4]

        def make_splits(row, carry):
            turned = grouped(wid[pl.ds(row, CHUNK), lanes]) * m2 + a2
            values = turned * sigmoid(turned)
            splits[pl.ds(row, CHUNK), lanes] = flat(values)
            return carry + jnp.sum(values, axis=0)

        pooled = over_rows(make_splits, pooled)
        if group == 0:
            gather_hand(2)
    pooled = image_sum(pooled) * (1.0 / (SIDE * SIDE))
    gather_end(2)
    last = fpe[:, :, 0:CHANNELS].reshape(BOTTLE, CHANNELS)
    squeeze = fpe[:, :, 1024:1152].reshape(BOTTLE, INNER)
    ex_both = fpe[:, :, 1152:1408]
    expand = jnp.concatenate(
        [
            ex_both[:, 0:ex_rows].reshape(INNER, 256),
            ex_both[:, ex_rows : 2 * ex_rows].reshape(INNER, 256),
        ],
        axis=1,
    )
    pre_pool = exact_dot(pooled, squeeze, False)
    sum_start("pool", four_rows(pair_sum(pre_pool), pair_sum(pre_pool * pre_pool)))
    first_micro = lax.rem(row_ids(BOTTLE), 4) < 2

    def make_normed(row, carry):
        rows = pl.ds(row, CHUNK)
        normed = (grouped(red[rows, :]) - center1) * scale1
        dwid[rows, 0:256] = flat(jnp.where(first_micro, normed, 0.0)).astype(BF16)
        dwid[rows, 256:512] = flat(jnp.where(first_micro, 0.0, normed)).astype(BF16)
        return carry + jnp.sum(grouped(x_v[rows, :].astype(F32)), axis=0)

    image_sums = micro_sum(over_rows(make_normed, jnp.zeros((8, CHANNELS), F32)))
    sum_start(
        "images",
        jnp.concatenate(
            [
                image_sums[2 * m : 2 * m + 1, at : at + 128]
                for m in range(2)
                for at in range(0, CHANNELS, 128)
            ],
            axis=0,
        ),
    )
    normed_images = tdot(dwid[...], x_v[...]).astype(BF16)
    normed_images = normed_images.reshape(2, 2, 2, BOTTLE // 4, CHANNELS)
    for m in range(2):
        gb[:, :, m * (BOTTLE // 4) : (m + 1) * (BOTTLE // 4)] = normed_images[m]
    reduce_core(5)
    total, square = from_four(sum_end("pool"))
    center_p, scale_p, mul_p, add_p = norm_terms(total, square, gain_pool, bias_pool, pictures)
    normed_p = (pre_pool - center_p) * scale_p
    norm_p = pre_pool * mul_p + add_p
    gate_p = sigmoid(norm_p)
    hidden = norm_p * gate_p
    slope_p = gate_p * (1.0 + norm_p * (1.0 - gate_p))
    logits = exact_dot(hidden, expand, False) + bias_expand
    left, right = logits[:, 0:256], logits[:, 256:512]
    most = jnp.maximum(left, right)
    left, right = jnp.exp(left - most), jnp.exp(right - most)
    att0 = left / (left + right)
    att1 = right / (left + right)

    def make_mixed(row, carry):
        rows = pl.ds(row, CHUNK)
        values = grouped(splits[rows, 0:256]) * att0 + grouped(splits[rows, 256:512]) * att1
        mixed[rows, :] = flat(values).astype(BF16)
        return carry

    over_rows(make_mixed, 0)
    halves3 = (slice(0, 512), slice(512, 1024))
    blocks3 = [[slice(512 * h + k, 512 * h + k + 256) for k in (0, 256)] for h in range(2)]
    for half, lanes in enumerate(halves3):
        proj[:, lanes] = jnp.dot(mixed[...], last[:, lanes], preferred_element_type=F32)
        sum_start(
            f"projected{half}", joined([sums_of(proj, 512 * half + k, 256) for k in (0, 256)])
        )
    sum_turn("projected0")
    sum_turn("projected1")
    sum_turn("images")
    reduce_y(5)

    norm3 = []
    zero = jnp.zeros((8, 256), F32)
    for half, lanes in enumerate(halves3):
        total, square = both_sums(f"projected{half}")
        norm3.append(norm_terms(total, square, gain_three[:, lanes], bias_three[:, lanes], pixels))
        found = []
        for k, block in enumerate(blocks3[half]):
            c3, s3, m3, a3 = (item[:, k * 256 : k * 256 + 256] for item in norm3[half])

            def make_out(row, carry):
                rows = pl.ds(row, CHUNK)
                values = grouped(proj[rows, block])
                summed = grouped(x_v[rows, block].astype(F32)) + (values * m3 + a3)
                gate = sigmoid(summed)
                bo4[pl.ds(row // 4, CHUNK // 4), :, block] = by_four(summed * gate).astype(BF16)
                upstream = grouped(gy_v[rows, block].astype(F32)) * (
                    gate * (1.0 + summed * (1.0 - gate))
                )
                up[rows, block] = flat(upstream)
                normed = (values - c3) * s3
                return carry[0] + jnp.sum(upstream, axis=0), carry[1] + jnp.sum(
                    upstream * normed, axis=0
                )

            found.append(over_rows(make_out, (zero, zero)))
        sum_start(f"back_projected{half}", joined(found))
    bo_copy = pltpu.make_async_copy(bo4, bo_hbm, local_sem.at[2])
    bo_copy.start()

    def write_norm(at, pattern):
        at = at // 128
        both = pattern[0:1, :] + pattern[2:3, :]
        for k in range(both.shape[1] // 128):
            np_full[at + k : at + k + 1, :] = both[:, k * 128 : k * 128 + 128]

    sum_turn("back_projected0")
    sum_turn("back_projected1")
    reduce_owner(5)

    for half, lanes in enumerate(halves3):
        bias_sum, gain_sum = both_sums(f"back_projected{half}")
        write_norm(2304 + 512 * half, gain_sum)
        write_norm(3328 + 512 * half, bias_sum)
        by_value, constant = back_terms(*norm3[half][0:3], bias_sum, gain_sum, pixels)
        for k, block in enumerate(blocks3[half]):
            m3, v3, k3 = (
                item[:, k * 256 : k * 256 + 256] for item in (norm3[half][2], by_value, constant)
            )

            def make_dproj(row, carry):
                rows = pl.ds(row, CHUNK)
                values = grouped(up[rows, block]) * m3 + grouped(proj[rows, block]) * v3 + k3
                dproj[rows, block] = flat(values).astype(BF16)
                return carry

            over_rows(make_dproj, 0)
        part_mixed = dot_t(dproj[:, lanes], last[:, lanes])
        d_mixed[...] = part_mixed if half == 0 else d_mixed[...] + part_mixed

    def attend(row, carry):
        rows = pl.ds(row, CHUNK)
        values = grouped(d_mixed[rows, :])
        return (
            carry[0] + jnp.sum(values * grouped(splits[rows, 0:256]), axis=0),
            carry[1] + jnp.sum(values * grouped(splits[rows, 256:512]), axis=0),
        )

    d_att0, d_att1 = over_rows(attend, (zero, zero))
    d_att0, d_att1 = image_sum(d_att0), image_sum(d_att1)
    both = att0 * d_att0 + att1 * d_att1
    d_logits = jnp.concatenate([att0 * (d_att0 - both), att1 * (d_att1 - both)], axis=1)
    d_hidden = exact_dot(d_logits, expand, True)
    d_pool = d_hidden * slope_p
    per_micro = four_rows(pair_sum(d_pool), pair_sum(d_pool * normed_p))
    sum_start("back_pool", per_micro)
    ex_sum = pair_sum(d_logits)
    ex_sum = ex_sum + pltpu.roll(ex_sum, 2, 0)
    ex_rows_sum = ex_sum[:, 0:128]
    for k in range(1, 4):
        ex_rows_sum = jnp.where(row_ids(128) == k, ex_sum[:, k * 128 : k * 128 + 128], ex_rows_sum)

    grad_ex = image_dot(hidden, d_logits)
    grad_ex = grad_ex.reshape(n_dp, ex_rows, 512)
    ge[:, 0:ex_rows, 128:384] = grad_ex[:, :, 0:256]
    ge[:, ex_rows : 2 * ex_rows, 128:384] = grad_ex[:, :, 256:512]
    ge[:, :, 384:512] = jnp.zeros((n_dp, 2 * ex_rows, 128), F32)
    g3[...] = tdot(mixed[...], dproj[...]).reshape(g3.shape)
    reduce_core(3)
    held = []
    for group, att in ((0, att0), (1, att1)):
        lanes = halves2[group]
        c2, s2, m2, a2 = norm2[group]

        def make_dn2(row, carry):
            rows = pl.ds(row, CHUNK)
            values = grouped(wid[rows, lanes])
            turned = values * m2 + a2
            gate = sigmoid(turned)
            slope = gate * (1.0 + turned * (1.0 - gate))
            down = grouped(d_mixed[rows, :]) * att * slope
            dn2[rows, lanes] = flat(down)
            splits[rows, lanes] = flat(slope)
            normed = (values - c2) * s2
            terms = (down, down * normed, slope, slope * normed)
            return tuple(item + jnp.sum(term, axis=0) for item, term in zip(carry, terms))

        held.append([image_sum(item) for item in over_rows(make_dn2, (zero,) * 4)])
    pool_bias_sum, pool_gain_sum = from_four(sum_end("back_pool"))
    write_norm(1536, pool_gain_sum)
    write_norm(1664, pool_bias_sum)
    d_pre_pool = mul_p * (
        d_pool - pool_bias_sum * (1.0 / pictures) - normed_p * (pool_gain_sum * (1.0 / pictures))
    )
    d_pooled = exact_dot(d_pre_pool, squeeze, True) * (1.0 / (SIDE * SIDE))
    for group in range(2):
        down, down_normed, slope, slope_normed = held[group]
        payload = fold_lanes(
            stack_sums(
                pair_sum(down + d_pooled * slope), pair_sum(down_normed + d_pooled * slope_normed)
            )
        )
        if group == 1:
            payload = jnp.concatenate([payload, ex_rows_sum], axis=0)
        sum_start(f"back_widened{group}", payload)
    ge[:, :, 0:128] = image_dot(pooled, d_pre_pool).reshape(n_dp, 2 * ex_rows, 128)
    sum_turn("back_widened0")
    sum_turn("back_widened1")
    reduce_y(3)
    reduce_core(4)
    back_total = owner_total(5)
    back_own[0] = back_total[0 : BOTTLE // 4]
    back_own[1] = back_total[BOTTLE // 4 :]

    small_zero = jnp.zeros((8, 128), F32)
    for group, lanes in enumerate(halves2):
        whole = sum_end(f"back_widened{group}")
        if group == 1:
            np_full[14:18, :] = whole[8:12]
        bias_sum, gain_sum = unstack_sums(unfold_lanes(whole[0:8]))
        write_norm(512 + 256 * group, gain_sum)
        write_norm(1024 + 256 * group, bias_sum)
        m2 = norm2[group][2]
        v2, k2 = back_terms(*norm2[group][0:3], bias_sum, gain_sum, pixels)
        pooled_m2 = d_pooled * m2

        def make_dwid(row, carry):
            rows = pl.ds(row, CHUNK)
            values = grouped(dn2[rows, lanes]) * m2 + grouped(splits[rows, lanes]) * pooled_m2
            values = values + grouped(wid[rows, lanes]) * v2 + k2
            dwid[rows, lanes] = flat(values).astype(BF16)
            return carry

        over_rows(make_dwid, 0)
        gc[group * own_half : (group + 1) * own_half] = tdot(
            columns[group], dwid[:, lanes]
        ).reshape(own_half, 2, 9 * 128 // own_half // 2, BOTTLE)
    reduce_core(1)
    reduce_core(2)
    for group, lanes in enumerate(halves2):
        dcol[PAD : PAD + ROWS, group * 1152 : group * 1152 + 1152] = dot_t(
            dwid[:, lanes], filters(group)
        )
        inner = slice(group * 128, group * 128 + 128)

        def gather_taps(row, carry):
            for side in range(3):
                total = None
                for down in range(3):
                    at = group * 1152 + (3 * down + side) * 128
                    values = dcol[pl.ds(PAD + row - 56 * (down - 1), CHUNK), at : at + 128]
                    total = values if total is None else total + values
                act[side, pl.ds(PAD + row, CHUNK), inner] = total
            return carry

        over_rows(gather_taps, 0)
        c1, s1, m1, a1 = (item[:, inner] for item in (center1, scale1, mul1, add1))
        not_first1, not_last1 = not_first[:, inner], not_last[:, inner]

        def make_dn1(row, carry):
            rows = pl.ds(row, CHUNK)
            d_active = act[1, pl.ds(PAD + row, CHUNK), inner]
            d_active = d_active + jnp.where(not_first1, beside(2, row, -4, inner), 0.0)
            d_active = d_active + jnp.where(not_last1, beside(0, row, 4, inner), 0.0)
            values = grouped(red[rows, inner])
            turned = values * m1 + a1
            gate = sigmoid(turned)
            slope = gate * (1.0 + turned * (1.0 - gate))
            down = grouped(d_active) * slope
            dn1[rows, inner] = flat(down)
            mixed[rows, inner] = flat(down * m1).astype(BF16)
            normed = (values - c1) * s1
            return carry[0] + jnp.sum(down, axis=0), carry[1] + jnp.sum(down * normed, axis=0)

        bias_sum, gain_sum = over_rows(make_dn1, (small_zero, small_zero))
        sum_start(f"back_reduced{group}", stack_sums(micro_sum(bias_sum), micro_sum(gain_sum)))
        if group == 0:
            reduce_y(1)
    sum_turn("back_reduced0")
    sum_turn("back_reduced1")
    reduce_y(2)
    reduce_y(4)
    reduce_owner(3)
    g1[...] = tdot(mixed[...], x_v[...]).reshape(g1.shape)
    reduce_core(0)
    found = [unstack_sums(sum_end(f"back_reduced{group}")) for group in range(2)]
    bias_sum, gain_sum = (jnp.concatenate(item, axis=1) for item in zip(*found))
    write_norm(0, gain_sum)
    write_norm(256, bias_sum)
    by_value, constant = back_terms(center1, scale1, mul1, bias_sum, gain_sum, pixels)
    def make_dred(row, carry):
        rows = pl.ds(row, CHUNK)
        values = grouped(dn1[rows, :]) * mul1 + grouped(red[rows, :]) * by_value + constant
        dred[rows, :] = flat(values).astype(BF16)
        return carry

    over_rows(make_dred, 0)
    reduce_owner(1)
    reduce_owner(4)
    proj[...] = dot_t(dred[...], fw1[...].reshape(CHANNELS, BOTTLE))
    reduce_y(0)

    by_bias = mul1 * bias_sum * (1.0 / pixels)
    by_gain = mul1 * gain_sum * (1.0 / pixels)
    image_sums = sum_end("images")
    ids = lax.broadcasted_iota(jnp.int32, (16, 128), 0)
    own_sums = [
        jnp.sum(jnp.where(ids == m * n_dp + dp, image_sums, 0.0), axis=0, keepdims=True)
        for m in range(2)
    ]
    ids = row_ids(128)
    fix[0] = row_dot(by_bias, jnp.where(ids == 0, own_sums[0], jnp.where(ids == 2, own_sums[1], 0.0)))
    for m in range(2):
        fix[1 + m] = row_dot(by_gain, jnp.where(ids == 2 * m, 1.0, 0.0))
    reduce_spread(3)
    reduce_spread(4)

    def make_dx(row, carry):
        for start in range(0, CHANNELS, 256):
            lanes = slice(start, start + 256)
            values = up[pl.ds(row, CHUNK), lanes] + proj[pl.ds(row, CHUNK), lanes]
            dx4[pl.ds(row // 4, CHUNK // 4), :, lanes] = values.reshape(CHUNK // 4, 4, 256)
        return carry

    over_rows(make_dx, 0)
    dx_copy = pltpu.make_async_copy(dx4, dx_hbm, local_sem.at[3])
    dx_copy.start()
    norm_rows = np_full[0:8, :]
    for d in range(1, n_dp):
        at = shard * d // 128
        norm_rows = jnp.where(dp == d, np_full[at : at + 8, :], norm_rows)
    norm_rows = pltpu.roll(norm_rows, lax.rem(128 - turn, 128), 1)
    gn_out[...] = jnp.where(lanes_id < 128 - turn, norm_rows, pltpu.roll(norm_rows, 7, 0))
    reduce_owner(2)
    reduce_owner(0)
    reduce_spread(1)
    reduce_spread(2)
    reduce_spread(0)
    out_copies = [
        pltpu.make_async_copy(source, target, local_sem.at[10 + k])
        for k, (source, target) in enumerate(
            (
                (gn_out, gn_hbm),
                (fs[2], f3_hbm),
                (fs[3], fe_hbm),
                (fs[1], fc_hbm),
                (fs[0], f1_hbm),
            )
        )
    ]
    out_copies[0].start()
    for which in (3, 4, 1, 2, 0):
        reduce_end(which)
        if which != 1:
            out_copies[{3: 1, 4: 2, 2: 3, 0: 4}[which]].start()

    bo_copy.wait()
    dx_copy.wait()
    for copy in out_copies:
        copy.wait()
    for k in STATS:
        if k in DIRECT:
            wait_bytes(ar_slots_a[k].at[pl.ds(0, everyone - 1)], ar_send_a.at[order[k]])
        else:
            wait_bytes(ar_slots_a[k].at[pl.ds(0, plane_size - 1)], ar_send_a.at[order[k]])
            wait_bytes(ar_slots_b[k].at[pl.ds(0, planes - 1)], ar_send_b.at[order[k]])
    wait_bytes(np_slots.at[pl.ds(0, n_dp - 1)], np_sems.at[0])
    for which in range(3):
        wait_bytes(seven(which), ws.at[which, 0])
        for stage in range(1, 4):
            wait_bytes(quarters[which](core, half_y), ws.at[which, stage])
    for which in range(6):
        wait_bytes(r1s[which], gs.at[which, 0])
        wait_bytes(r2s[which], gs.at[which, 1])
        wait_bytes(r3s[which].at[pl.ds(0, n_dp - 1)], gs.at[which, 2])
        if which < 5:
            wait_bytes(three_parts(which), gs.at[which, 3])


def update_kernel(*refs):
    sources, targets = refs[0:25], refs[25:45]
    inputs, outs, through = refs[45:68], refs[68:86], refs[86:88]
    pass_sems, in_sems, out_sems = refs[88:91]
    fetching, passing = [], []
    half = SIDE * SIDE // 2
    for number, (which, at, count) in enumerate(((1, 0, half), (1, half, half), (0, 0, 2 * half))):
        rows = pl.ds(at, count)
        fetching.append(
            pltpu.make_async_copy(
                sources[which].at[rows], through[which].at[rows], pass_sems.at[0, number]
            )
        )
        passing.append(
            pltpu.make_async_copy(
                through[which].at[rows], targets[which].at[rows], pass_sems.at[1, number]
            )
        )
    for copy in fetching:
        copy.start()
    coming = [
        pltpu.make_async_copy(source, held, in_sems.at[k])
        for k, (source, held) in enumerate(zip(sources[2:], inputs))
    ]
    for copy in coming:
        copy.start()
    grads, states = inputs[0:5], inputs[5:23]
    going = [
        pltpu.make_async_copy(held, target, out_sems.at[k])
        for k, (held, target) in enumerate(zip(outs, targets[2:]))
    ]
    ex_rows = states[9].shape[0]
    shard = states[15].shape[0]
    fans = (CHANNELS, 9 * BOTTLE // RADIX, BOTTLE, INNER // 8, BOTTLE)
    for copy in coming[0:5]:
        copy.wait()
    found = (
        grads[0][...].T,
        grads[1][...],
        grads[3][:, 0:128],
        jnp.concatenate([grads[3][0:ex_rows, 128:384], grads[3][ex_rows:, 128:384]], axis=1),
        grads[2][...],
    )
    for order, k in enumerate((3, 2, 4, 0, 1)):
        for copy in coming[5 + 3 * k : 8 + 3 * k]:
            copy.wait()
        new = adamw(
            states[3 * k][...],
            states[3 * k + 1][...],
            states[3 * k + 2][...],
            found[k],
            2.0 * fans[k] ** (-0.5),
            DECAY,
        )
        for j in range(3):
            outs[3 * k + j][...] = new[j]
            going[3 * k + j].start()
        if order < 3:
            fetching[order].wait()
            passing[order].start()
    for copy in coming[20:23]:
        copy.wait()
    for at in range(0, shard, 128):
        width = min(128, shard - at)
        lanes = pl.ds(at, width)
        new = adamw(
            *[states[15 + j][lanes].reshape(1, width) for j in range(3)],
            grads[4][at // 128 : at // 128 + 1, 0:width],
            NORM_RATE,
            0.0,
        )
        for j in range(3):
            outs[15 + j][lanes] = new[j].reshape(width)
    for copy in going[15:18]:
        copy.start()
    for copy in passing + going:
        copy.wait()


def fused_device(
    images,
    out_grad,
    reduce_weight,
    reduce_moment,
    reduce_second,
    conv_weight,
    conv_moment,
    conv_second,
    squeeze_weight,
    squeeze_moment,
    squeeze_second,
    expand_weight,
    expand_moment,
    expand_second,
    project_weight,
    project_moment,
    project_second,
    norm_params,
    norm_moment,
    norm_second,
):
    n_dp, n_rep = lax.axis_size("dp"), lax.axis_size("rep")
    by_pixel = lambda values: jnp.transpose(values, (1, 2, 0, 3)).reshape(-1, 4, CHANNELS)
    qc = conv_weight.shape[0] // 2
    q1 = reduce_weight.shape[0] // 4
    pe = squeeze_weight.shape[0]
    vmem = pltpu.VMEM
    pixel_form = (SIDE * SIDE, 4, CHANNELS)
    scratch = [
        *[
            vmem(values.shape, F32)
            for values in (
                reduce_weight,
                conv_weight,
                squeeze_weight,
                expand_weight,
                project_weight,
                norm_params,
            )
        ],
        vmem((8, 128), F32),
        vmem(pixel_form, BF16),
        vmem(pixel_form, BF16),
        vmem((ROWS, CHANNELS), BF16),
        vmem((ROWS, CHANNELS), BF16),
        vmem((n_dp, 2, 2, q1, BOTTLE), BF16),
        vmem((n_dp, 2, qc, BOTTLE), BF16),
        vmem((n_dp, pe, 1536), BF16),
        vmem((pe, 1536), BF16),
        vmem((n_dp, 8, 128), F32),
        vmem((40, 128), F32),
        vmem((ROWS, BOTTLE), F32),
        vmem((3, ROWS + 2 * PAD, BOTTLE), F32),
        vmem((2, ROWS, 9 * 128), BF16),
        vmem((ROWS, 512), F32),
        vmem((ROWS, 512), F32),
        vmem((ROWS, BOTTLE), BF16),
        vmem((ROWS, CHANNELS), F32),
        vmem((ROWS, CHANNELS), F32),
        vmem(pixel_form, BF16),
        vmem(pixel_form, F32),
        vmem((ROWS, CHANNELS), BF16),
        vmem((ROWS, BOTTLE), F32),
        vmem((ROWS, 512), F32),
        vmem((ROWS, 512), BF16),
        vmem((ROWS + 2 * PAD, 2 * 9 * 128), F32),
        vmem((ROWS, BOTTLE), F32),
        vmem((ROWS, BOTTLE), BF16),
        vmem((2, 2, BOTTLE // 4, CHANNELS), F32),
        vmem((n_dp, 2, qc, BOTTLE), F32),
        vmem((n_dp, pe, CHANNELS), F32),
        vmem((n_dp, pe, 512), F32),
        vmem((2, 2, BOTTLE // 2, CHANNELS), BF16),
        vmem((3, BOTTLE, CHANNELS // n_dp), F32),
        vmem((2, BOTTLE // 4, CHANNELS // n_dp), F32),
    ]
    direct = n_dp * n_rep
    scratch += [
        vmem((direct if k in DIRECT else 2 * n_rep,) + shape, F32) for k, shape in STATS.items()
    ]
    scratch += [vmem((n_dp // 2,) + shape, F32) for shape in STATS.values()]
    cut = 64
    lanes1 = CHANNELS // n_dp
    half = [
        (2, BOTTLE // 4, CHANNELS),
        (n_dp, 2, cut, 128),
        (n_dp, 2, qc - cut, 128),
        (n_dp, pe, 512),
        (n_dp, pe, 256),
        (2, BOTTLE // 2, CHANNELS),
    ]
    quarter = [
        (BOTTLE // 4, CHANNELS),
        (n_dp, cut, 128),
        (n_dp, qc - cut, 128),
        (n_dp, pe, 256),
        (n_dp, pe, 128),
        (BOTTLE // 2, CHANNELS),
    ]
    final = [(2, 2, BOTTLE // 4, lanes1), (2, qc, BOTTLE), (pe, CHANNELS), (pe, 512)]
    sent = [BF16, BF16, BF16, BF16, F32, BF16]
    scratch += [vmem(shape, kind) for shape, kind in zip(half, sent)]
    scratch += [vmem(shape, kind) for shape, kind in zip(quarter, sent)] * 3
    owned = [(BOTTLE // 4, lanes1)] + [shape[1:] for shape in quarter[1:-1]]
    owned += [(BOTTLE // 2, lanes1)]
    scratch += [vmem((n_dp,) + shape, kind) for shape, kind in zip(owned, sent)]
    scratch += [vmem(shape, F32) for shape in owned]
    scratch += [vmem(shape, F32) for shape in final]
    scratch += [vmem(shape, BF16) for shape in half[0:4]]
    dma = pltpu.SemaphoreType.DMA
    scratch += [dma((15,))] + [dma((len(STATS),))] * 4 + [dma((2,))] + [dma((3, 4))] * 2 + [dma((6, 4))] * 2
    any_space = pl.BlockSpec(memory_space=pl.ANY)
    block_out, images_grad, sum1, sumc, sum3, sume, norm_grads = pl.pallas_call(
        functools.partial(block_kernel, n_dp, n_rep),
        out_shape=[
            jax.ShapeDtypeStruct(pixel_form, BF16),
            jax.ShapeDtypeStruct(pixel_form, F32),
            *[jax.ShapeDtypeStruct(shape, F32) for shape in final],
            jax.ShapeDtypeStruct((8, 128), F32),
        ],
        in_specs=[any_space] * 8,
        out_specs=[any_space] * 7,
        scratch_shapes=scratch,
        compiler_params=pltpu.CompilerParams(
            collective_id=0, has_side_effects=True, vmem_limit_bytes=63 * 1024 * 1024
        ),
    )(
        by_pixel(images),
        by_pixel(out_grad),
        reduce_weight,
        conv_weight,
        squeeze_weight,
        expand_weight,
        project_weight,
        norm_params,
    )
    states = (
        reduce_weight,
        reduce_moment,
        reduce_second,
        conv_weight,
        conv_moment,
        conv_second,
        squeeze_weight,
        squeeze_moment,
        squeeze_second,
        expand_weight,
        expand_moment,
        expand_second,
        project_weight,
        project_moment,
        project_second,
    )
    held = (*states, norm_params, norm_moment, norm_second)
    sums = (
        sum1.reshape(BOTTLE, lanes1),
        sumc.reshape(conv_weight.shape),
        sum3,
        sume,
        norm_grads,
    )
    block_out, images_grad, *updated = pl.pallas_call(
        update_kernel,
        out_shape=[
            jax.ShapeDtypeStruct(pixel_form, BF16),
            jax.ShapeDtypeStruct(pixel_form, F32),
            *[jax.ShapeDtypeStruct(state.shape, F32) for state in held],
        ],
        in_specs=[any_space] * 25,
        out_specs=[any_space] * 20,
        scratch_shapes=[vmem(values.shape, F32) for values in (*sums, *held, *held)]
        + [vmem(pixel_form, BF16), vmem(pixel_form, F32)]
        + [dma((2, 3)), dma((23,)), dma((18,))],
        compiler_params=pltpu.CompilerParams(vmem_limit_bytes=63 * 1024 * 1024),
    )(block_out, images_grad, *sums, *held)
    by_image = lambda values: jnp.transpose(
        values.reshape(SIDE, SIDE, images.shape[0], CHANNELS), (2, 0, 1, 3)
    )
    return (
        by_image(block_out),
        by_image(images_grad),
        *updated,
    )


def solution(mesh):
    placed = (
        P(("dp", "rep"), None, None, None),
        P(("dp", "rep"), None, None, None),
        P("dp", None),
        P("dp", None),
        P("dp", None),
        P("dp", None),
        P("dp", None),
        P("dp", None),
        P("dp", None),
        P("dp", None),
        P("dp", None),
        P("dp", None),
        P("dp", None),
        P("dp", None),
        P("dp", None),
        P("dp", None),
        P("dp", None),
        P("dp"),
        P("dp"),
        P("dp"),
    )
    n_dp, n_rep = mesh.shape["dp"], mesh.shape["rep"]
    whole_tiles = n_rep == 4 and n_dp % 2 == 0 and INNER % (16 * n_dp) == 0
    return jax.shard_map(
        fused_device if whole_tiles else per_device,
        mesh=mesh,
        in_specs=placed,
        out_specs=(
            P(("dp", "rep"), None, None, None),
            P(("dp", "rep"), None, None, None),
            P("dp", None),
            P("dp", None),
            P("dp", None),
            P("dp", None),
            P("dp", None),
            P("dp", None),
            P("dp", None),
            P("dp", None),
            P("dp", None),
            P("dp", None),
            P("dp", None),
            P("dp", None),
            P("dp", None),
            P("dp", None),
            P("dp", None),
            P("dp"),
            P("dp"),
            P("dp"),
        ),
        check_vma=False,
    )
```

```python
import functools
import jax
import jax.numpy as jnp
from jax import lax
from jax.experimental import pallas as pl
from jax.experimental.pallas import tpu as pltpu
from jax.sharding import PartitionSpec as P

CHANNELS = 1024
BOTTLE = 256
INNER = 128
RADIX = 2
SIDE = 14
MICRO = 2
STEP = 10


EPSILON = 1e-05
PRECISE = lax.Precision.HIGHEST
BETA_ONE = 0.9
BETA_TWO = 0.999
ADAM_EPSILON = 1e-08
DECAY = 0.01
NORM_RATE = 0.8
ROWS = 4 * SIDE * SIDE
NORM_WIDTH = 4352


def split_params(packed):
    widths = (
        BOTTLE,
        BOTTLE,
        RADIX * BOTTLE,
        RADIX * BOTTLE,
        INNER,
        INNER,
        RADIX * BOTTLE,
        CHANNELS,
        CHANNELS,
    )
    pieces = []
    offset = 0
    for segment in widths:
        pieces.append(lax.slice_in_dim(packed, offset, offset + segment))
        offset = offset + segment
    return pieces


def silu_slope(values):
    logistic = jax.nn.sigmoid(values)
    return logistic * (1.0 + values * (1.0 - logistic))


def norm_forward(values, gain, bias, count):
    flat = values.reshape(-1, values.shape[-1])
    total, square = lax.psum((jnp.sum(flat, axis=0), jnp.sum(flat * flat, axis=0)), ("dp", "rep"))
    center = total / count
    scale = lax.rsqrt(square / count - center * center + EPSILON)
    normed = (values - center) * scale
    return (normed * gain + bias, normed, scale)


def norm_backward(upstream, normed, scale, gain, count):
    flat_up = upstream.reshape(-1, upstream.shape[-1])
    flat_norm = normed.reshape(-1, normed.shape[-1])
    bias_sum, gain_sum = lax.psum(
        (jnp.sum(flat_up, axis=0), jnp.sum(flat_up * flat_norm, axis=0)), ("dp", "rep")
    )
    downstream = gain * scale * (upstream - bias_sum / count - normed * (gain_sum / count))
    return (downstream, gain_sum, bias_sum)


def patches(active):
    padded = jnp.pad(active, ((0, 0), (1, 1), (1, 1), (0, 0), (0, 0)))
    shifted = [
        padded[:, down_step : down_step + SIDE, side_step : side_step + SIDE]
        for down_step in range(3)
        for side_step in range(3)
    ]
    return jnp.stack(shifted, axis=4)


def unpatch(columns):
    total = jnp.zeros(
        (columns.shape[0], SIDE + 2, SIDE + 2, columns.shape[3], columns.shape[5]), jnp.float32
    )
    for down_step in range(3):
        for side_step in range(3):
            piece = columns[:, :, :, :, 3 * down_step + side_step]
            total = total + jnp.pad(
                piece,
                ((0, 0), (down_step, 2 - down_step), (side_step, 2 - side_step), (0, 0), (0, 0)),
            )
    return total[:, 1 : SIDE + 1, 1 : SIDE + 1]


def adamw(param, moment, second, gradient, rate, decay):
    moment_new = BETA_ONE * moment + (1.0 - BETA_ONE) * gradient
    second_new = BETA_TWO * second + (1.0 - BETA_TWO) * gradient * gradient
    ratio = (
        moment_new
        / (1.0 - BETA_ONE**STEP)
        / (jnp.sqrt(second_new / (1.0 - BETA_TWO**STEP)) + ADAM_EPSILON)
    )
    return (param - rate * (ratio + decay * param), moment_new, second_new)


def per_device(
    images,
    out_grad,
    reduce_weight,
    reduce_moment,
    reduce_second,
    conv_weight,
    conv_moment,
    conv_second,
    squeeze_weight,
    squeeze_moment,
    squeeze_second,
    expand_weight,
    expand_moment,
    expand_second,
    project_weight,
    project_moment,
    project_second,
    norm_params,
    norm_moment,
    norm_second,
):
    bf16 = jnp.bfloat16
    low_reduce = reduce_weight.astype(bf16)
    low_conv = conv_weight.astype(bf16)
    low_squeeze = squeeze_weight.astype(bf16)
    low_expand = expand_weight.astype(bf16)
    low_project = project_weight.astype(bf16)
    low_norm = norm_params.astype(bf16)
    devices = lax.axis_size("dp") * lax.axis_size("rep")
    per_batch = images.shape[0] // MICRO
    pixel_count = float(per_batch * SIDE * SIDE * devices)
    image_count = float(per_batch * devices)
    group_in = BOTTLE // RADIX
    grad_first = jnp.zeros((CHANNELS, BOTTLE), jnp.float32)
    grad_conv = jnp.zeros((RADIX, 9 * group_in, BOTTLE), jnp.float32)
    grad_squeeze = jnp.zeros((BOTTLE, INNER), jnp.float32)
    grad_expand = jnp.zeros((INNER, RADIX * BOTTLE), jnp.float32)
    grad_last = jnp.zeros((BOTTLE, CHANNELS), jnp.float32)
    grad_norms = jnp.zeros(
        (2 * BOTTLE + 3 * RADIX * BOTTLE + 2 * INNER + 2 * CHANNELS,), jnp.float32
    )
    outputs = []
    input_grads = []
    for number in range(MICRO):
        forward_set = (
            lax.all_gather(low_reduce, "dp", axis=0, tiled=True),
            lax.all_gather(low_conv, "dp", axis=0, tiled=True),
            lax.all_gather(low_squeeze, "dp", axis=0, tiled=True),
            lax.all_gather(low_expand, "dp", axis=0, tiled=True),
            lax.all_gather(low_project, "dp", axis=0, tiled=True),
            lax.all_gather(low_norm, "dp", axis=0, tiled=True),
        )
        first, conv, squeeze, expand, last, packed = forward_set
        (
            gain_one,
            bias_one,
            gain_two,
            bias_two,
            gain_pool,
            bias_pool,
            bias_expand,
            gain_three,
            bias_three,
        ) = split_params(packed.astype(jnp.float32))
        batched = images[number * per_batch : (number + 1) * per_batch]
        cotangent = out_grad[number * per_batch : (number + 1) * per_batch]
        reduced = jnp.einsum("nhwc,cb->nhwb", batched, first, preferred_element_type=jnp.float32)
        norm_one, normed_one, scale_one = norm_forward(reduced, gain_one, bias_one, pixel_count)
        active = jax.nn.silu(norm_one).astype(bf16)
        columns = patches(active.reshape(per_batch, SIDE, SIDE, RADIX, group_in)).reshape(
            per_batch * SIDE * SIDE, RADIX, 9 * group_in
        )
        conv_grouped = conv.reshape(RADIX, 9 * group_in, BOTTLE)
        widened = jnp.einsum(
            "prk,rko->pro", columns, conv_grouped, preferred_element_type=jnp.float32
        )
        widened = widened.reshape(per_batch, SIDE, SIDE, RADIX * BOTTLE)
        norm_two, normed_two, scale_two = norm_forward(widened, gain_two, bias_two, pixel_count)
        splits = jax.nn.silu(norm_two).reshape(per_batch, SIDE, SIDE, RADIX, BOTTLE)
        pooled = jnp.sum(jnp.sum(splits, axis=3), axis=(1, 2)) / (SIDE * SIDE)
        squeeze_float = squeeze.astype(jnp.float32)
        expand_float = expand.astype(jnp.float32)
        pre_pool = jnp.dot(pooled, squeeze_float, precision=PRECISE)
        norm_pool, normed_pool, scale_pool = norm_forward(
            pre_pool, gain_pool, bias_pool, image_count
        )
        hidden = jax.nn.silu(norm_pool)
        logits = (jnp.dot(hidden, expand_float, precision=PRECISE) + bias_expand).reshape(
            per_batch, RADIX, BOTTLE
        )
        attention = jax.nn.softmax(logits, axis=1)
        mixed = jnp.sum(splits * attention[:, None, None], axis=3).astype(bf16)
        projected = jnp.einsum("nhwb,bc->nhwc", mixed, last, preferred_element_type=jnp.float32)
        norm_three, normed_three, scale_three = norm_forward(
            projected, gain_three, bias_three, pixel_count
        )
        summed = batched.astype(jnp.float32) + norm_three
        outputs.append(jax.nn.silu(summed).astype(bf16))
        backward_set = (
            lax.all_gather(low_reduce, "dp", axis=0, tiled=True),
            lax.all_gather(low_conv, "dp", axis=0, tiled=True),
            lax.all_gather(low_squeeze, "dp", axis=0, tiled=True),
            lax.all_gather(low_expand, "dp", axis=0, tiled=True),
            lax.all_gather(low_project, "dp", axis=0, tiled=True),
            lax.all_gather(low_norm, "dp", axis=0, tiled=True),
        )
        first, conv, squeeze, expand, last, packed = backward_set
        gains_back = split_params(packed.astype(jnp.float32))
        conv_grouped = conv.reshape(RADIX, 9 * group_in, BOTTLE)
        expand_float = expand.astype(jnp.float32)
        squeeze_float = squeeze.astype(jnp.float32)
        upstream = cotangent.astype(jnp.float32) * silu_slope(summed)
        d_projected, gain_three_grad, bias_three_grad = norm_backward(
            upstream, normed_three, scale_three, gains_back[7], pixel_count
        )
        d_projected_low = d_projected.astype(bf16)
        grad_last = grad_last + jnp.einsum(
            "nhwb,nhwc->bc", mixed, d_projected_low, preferred_element_type=jnp.float32
        )
        d_mixed = jnp.einsum(
            "nhwc,bc->nhwb", d_projected_low, last, preferred_element_type=jnp.float32
        )
        d_splits = d_mixed[:, :, :, None] * attention[:, None, None]
        d_attention = jnp.sum(d_mixed[:, :, :, None] * splits, axis=(1, 2))
        d_logits = attention * (
            d_attention - jnp.sum(attention * d_attention, axis=1, keepdims=True)
        )
        flat_logits = d_logits.reshape(per_batch, RADIX * BOTTLE)
        grad_expand = grad_expand + jnp.dot(hidden.T, flat_logits, precision=PRECISE)
        d_hidden = jnp.dot(flat_logits, expand_float.T, precision=PRECISE)
        d_pool_norm = d_hidden * silu_slope(norm_pool)
        pool_bias_sum, pool_gain_sum, expand_bias_sum = lax.psum(
            (
                jnp.sum(d_pool_norm, axis=0),
                jnp.sum(d_pool_norm * normed_pool, axis=0),
                jnp.sum(flat_logits, axis=0),
            ),
            ("dp", "rep"),
        )
        d_pre_pool = (
            gains_back[4]
            * scale_pool
            * (
                d_pool_norm
                - pool_bias_sum / image_count
                - normed_pool * (pool_gain_sum / image_count)
            )
        )
        grad_squeeze = grad_squeeze + jnp.dot(pooled.T, d_pre_pool, precision=PRECISE)
        d_pooled = jnp.dot(d_pre_pool, squeeze_float.T, precision=PRECISE)
        d_splits = d_splits + (d_pooled / (SIDE * SIDE))[:, None, None, None, :]
        d_norm_two = d_splits.reshape(per_batch, SIDE, SIDE, RADIX * BOTTLE) * silu_slope(norm_two)
        d_widened, gain_two_grad, bias_two_grad = norm_backward(
            d_norm_two, normed_two, scale_two, gains_back[2], pixel_count
        )
        d_widened_low = d_widened.astype(bf16).reshape(per_batch * SIDE * SIDE, RADIX, BOTTLE)
        grad_conv = grad_conv + jnp.einsum(
            "prk,pro->rko", columns, d_widened_low, preferred_element_type=jnp.float32
        )
        d_columns = jnp.einsum(
            "pro,rko->prk", d_widened_low, conv_grouped, preferred_element_type=jnp.float32
        )
        d_active = unpatch(d_columns.reshape(per_batch, SIDE, SIDE, RADIX, 9, group_in)).reshape(
            per_batch, SIDE, SIDE, BOTTLE
        )
        d_norm_one = d_active * silu_slope(norm_one)
        d_reduced, gain_one_grad, bias_one_grad = norm_backward(
            d_norm_one, normed_one, scale_one, gains_back[0], pixel_count
        )
        d_reduced_low = d_reduced.astype(bf16)
        grad_first = grad_first + jnp.einsum(
            "nhwc,nhwb->cb", batched, d_reduced_low, preferred_element_type=jnp.float32
        )
        input_grads.append(
            upstream
            + jnp.einsum("nhwb,cb->nhwc", d_reduced_low, first, preferred_element_type=jnp.float32)
        )
        grad_norms = grad_norms + jnp.concatenate(
            [
                gain_one_grad,
                bias_one_grad,
                gain_two_grad,
                bias_two_grad,
                pool_gain_sum,
                pool_bias_sum,
                expand_bias_sum,
                gain_three_grad,
                bias_three_grad,
            ]
        )
    grad_conv = grad_conv.reshape(9 * BOTTLE, BOTTLE)
    partial_value = (
        lax.psum_scatter(grad_first, "dp", scatter_dimension=0, tiled=True),
        lax.psum_scatter(grad_conv, "dp", scatter_dimension=0, tiled=True),
        lax.psum_scatter(grad_squeeze, "dp", scatter_dimension=0, tiled=True),
        lax.psum_scatter(grad_expand, "dp", scatter_dimension=0, tiled=True),
        lax.psum_scatter(grad_last, "dp", scatter_dimension=0, tiled=True),
    )
    owned = lax.psum(
        (partial_value[0], partial_value[1], partial_value[2], partial_value[3], partial_value[4]),
        "rep",
    )
    shard_length = norm_params.shape[0]
    norm_grad_owned = lax.dynamic_slice_in_dim(
        grad_norms, lax.axis_index("dp") * shard_length, shard_length
    )
    reduce_new = adamw(
        reduce_weight, reduce_moment, reduce_second, owned[0], 2.0 * CHANNELS ** (-0.5), DECAY
    )
    conv_new = adamw(
        conv_weight,
        conv_moment,
        conv_second,
        owned[1],
        2.0 * (9 * BOTTLE // RADIX) ** (-0.5),
        DECAY,
    )
    squeeze_new = adamw(
        squeeze_weight, squeeze_moment, squeeze_second, owned[2], 2.0 * BOTTLE ** (-0.5), DECAY
    )
    expand_new = adamw(
        expand_weight, expand_moment, expand_second, owned[3], 2.0 * (INNER // 8) ** (-0.5), DECAY
    )
    project_new = adamw(
        project_weight, project_moment, project_second, owned[4], 2.0 * BOTTLE ** (-0.5), DECAY
    )
    norm_new = adamw(norm_params, norm_moment, norm_second, norm_grad_owned, NORM_RATE, 0.0)
    return (
        jnp.concatenate(outputs, axis=0),
        jnp.concatenate(input_grads, axis=0),
        reduce_new[0],
        reduce_new[1],
        reduce_new[2],
        conv_new[0],
        conv_new[1],
        conv_new[2],
        squeeze_new[0],
        squeeze_new[1],
        squeeze_new[2],
        expand_new[0],
        expand_new[1],
        expand_new[2],
        project_new[0],
        project_new[1],
        project_new[2],
        norm_new[0],
        norm_new[1],
        norm_new[2],
    )


MESH = pl.DeviceIdType.MESH
PAD = 64
CHUNK = 112
F32 = jnp.float32
BF16 = jnp.bfloat16
STATS = {
    "reduced": (8, 128),
    "widened0": (8, 128),
    "widened1": (8, 128),
    "pool": (4, 128),
    "images": (16, 128),
    "projected0": (8, 256),
    "projected1": (8, 256),
    "back_projected0": (8, 256),
    "back_projected1": (8, 256),
    "back_pool": (4, 128),
    "back_widened0": (8, 128),
    "back_widened1": (16, 128),
    "back_reduced0": (8, 128),
    "back_reduced1": (8, 128),
}
DIRECT = ("reduced", "pool", "back_pool")


def sigmoid(values):
    return 0.5 * jnp.tanh(0.5 * values) + 0.5


def row_ids(width):
    return lax.broadcasted_iota(jnp.int32, (8, width), 0)


def image_sum(rows):
    return rows + pltpu.roll(rows, 4, 0)


def pair_sum(rows):
    even = row_ids(rows.shape[1]) % 2 == 0
    return rows + jnp.where(even, pltpu.roll(rows, 7, 0), pltpu.roll(rows, 1, 0))


def micro_sum(rows):
    return pair_sum(image_sum(rows))


def stack_sums(first, second):
    return jnp.where(row_ids(first.shape[1]) < 4, first, second)


def unstack_sums(stacked):
    upper = row_ids(stacked.shape[1]) < 4
    turned = pltpu.roll(stacked, 4, 0)
    return jnp.where(upper, stacked, turned), jnp.where(upper, turned, stacked)


def four_rows(first, second):
    return jnp.concatenate([first[0:1], first[2:3], second[0:1], second[2:3]], axis=0)


def from_four(rows):
    earlier = lax.rem(row_ids(rows.shape[1]), 4) < 2
    return tuple(jnp.where(earlier, rows[k : k + 1], rows[k + 1 : k + 2]) for k in (0, 2))


def fold_lanes(stacked):
    half = stacked.shape[1] // 2
    even = row_ids(half) % 2 == 0
    return jnp.where(even, stacked[:, :half], stacked[:, half:])


def unfold_lanes(folded):
    even = row_ids(folded.shape[1]) % 2 == 0
    left = jnp.where(even, folded, pltpu.roll(folded, 1, 0))
    right = jnp.where(even, pltpu.roll(folded, 7, 0), folded)
    return jnp.concatenate([left, right], axis=1)


def norm_terms(total, square, gain, bias, count):
    center = total * (1.0 / count)
    scale = lax.rsqrt(square * (1.0 / count) - center * center + EPSILON)
    slope = scale * gain
    return center, scale, slope, bias - center * slope


def back_terms(center, scale, slope, bias_sum, gain_sum, count):
    by_value = -slope * scale * (gain_sum * (1.0 / count))
    constant = -slope * (bias_sum * (1.0 / count)) - by_value * center
    return by_value, constant


def tdot(left, right):
    return lax.dot_general(left, right, (((0,), (0,)), ((), ())), preferred_element_type=F32)


def dot_t(left, right):
    return lax.dot_general(left, right, (((1,), (1,)), ((), ())), preferred_element_type=F32)


def in_parts(values, parts):
    found = []
    for _ in range(parts):
        rounded = values.astype(BF16).astype(F32)
        found.append(rounded)
        values = values - rounded
    return found


def exact_dot(left, right, transposed):
    stacked = jnp.concatenate(in_parts(left, 3), axis=0).astype(BF16)
    wide = dot_t(stacked, right) if transposed else jnp.dot(stacked, right, preferred_element_type=F32)
    return wide[0:8] + wide[8:16] + wide[16:24]


def row_dot(left, right):
    high, low = in_parts(left, 2)
    other_high, other_low = in_parts(right, 2)
    return tdot(
        jnp.concatenate([high, high, low, low], axis=0).astype(BF16),
        jnp.concatenate([other_high, other_low, other_high, other_low], axis=0).astype(BF16),
    )


def image_dot(left, right):
    return row_dot(jnp.where(row_ids(left.shape[1]) < 4, left, 0.0), right)


def block_kernel(
    n_dp,
    n_rep,
    x_hbm,
    gy_hbm,
    w1_hbm,
    wc_hbm,
    sq_hbm,
    ex_hbm,
    w3_hbm,
    np_hbm,
    bo_hbm,
    dx_hbm,
    f1_hbm,
    fc_hbm,
    f3_hbm,
    fe_hbm,
    gn_hbm,
    w1_own,
    wc_own,
    sq_own,
    ex_own,
    w3_own,
    np_own,
    gn_out,
    x4,
    gy4,
    x_v,
    gy_v,
    fw1,
    fwc,
    fes,
    fw3,
    es_own,
    np_slots,
    np_full,
    red,
    act,
    columns,
    wid,
    splits,
    mixed,
    proj,
    up,
    bo4,
    dx4,
    dproj,
    d_mixed,
    dn2,
    dwid,
    dcol,
    dn1,
    dred,
    g1,
    gc,
    g3,
    ge,
    gb,
    fix,
    back_own,
    *rest,
):
    n_ar = len(STATS)
    order = {name: k for k, name in enumerate(STATS)}
    ar_slots_a = dict(zip(STATS, rest[0:n_ar]))
    ar_slots_b = dict(zip(STATS, rest[n_ar : 2 * n_ar]))
    rest = rest[2 * n_ar :]
    r1s, ys, r2s, ks, r3s, own = (rest[6 * i : 6 * i + 6] for i in range(6))
    fs, cs = rest[36:40], rest[40:44]
    rest = rest[44:]
    local_sem, ar_send_a, ar_recv_a, ar_send_b, ar_recv_b, np_sems, ws, wr, gs, gr = rest

    dp = lax.axis_index("dp")
    rep = lax.axis_index("rep")
    core = lax.rem(rep, 2)
    half_y = lax.div(rep, 2)
    planes = n_dp // 2
    plane_size = 2 * n_rep
    plane = lax.div(dp, 2)
    in_plane = lax.rem(dp, 2) * n_rep + rep
    sibling = (dp, half_y * 2 + (1 - core))
    across = (dp, (1 - half_y) * 2 + core)
    pixels = float(SIDE * SIDE * 2 * n_dp * n_rep)
    pictures = float(2 * n_dp * n_rep)

    x = lax.rem(dp, 2)
    if planes == 4:
        upper = lax.div(plane, 2)
        other_planes = [3 - 3 * upper, 2 - upper, 1 - plane + 4 * upper]
    else:
        other_planes = [lax.rem(plane + step, planes) for step in range(1, planes)]
    flips = ((1, 1, 1), (1, 1, 0), (1, 0, 1), (1, 0, 0), (0, 1, 1), (0, 1, 0), (0, 0, 1), (0, 0, 0))

    def of_flip(z, flip):
        there = [1 - own if turn else own for own, turn in zip((x, half_y, core), flip)]
        return (z * 2 + there[0], there[1] * 2 + there[2])

    plane_peers = [of_flip(plane, flip) for flip in flips[:-1]]
    column_peers = [of_flip(z, flips[-1]) for z in other_planes]
    owner_peers = [of_flip(z, flip) for z in other_planes for flip in (flips[3], flips[7])]
    owner_peers += [of_flip(plane, flips[3])]
    all_peers = [of_flip(z, flip) for z in other_planes for flip in flips] + plane_peers
    me, everyone = dp * n_rep + rep, n_dp * n_rep
    rep_peers = [(dp, lax.rem(rep + step, n_rep)) for step in range(1, n_rep)]

    def remote(src, dst, send_sem, recv_sem, device):
        return pltpu.make_async_remote_copy(
            src_ref=src,
            dst_ref=dst,
            send_sem=send_sem,
            recv_sem=recv_sem,
            device_id=device,
            device_id_type=MESH,
        )

    def send_all(ref, send_sem, recv_sem, peers):
        for device in peers:
            remote(ref, ref, send_sem, recv_sem, device).start()

    def wait_bytes(ref, sem):
        pltpu.make_async_copy(ref, ref, sem).wait()

    def over_rows(body, init):
        def step(index, carry):
            return body(pl.multiple_of(index * CHUNK, CHUNK), carry)

        return lax.fori_loop(0, ROWS // CHUNK, step, init)

    def grouped(values):
        return values.reshape(CHUNK // 8, 8, values.shape[-1])

    def by_four(values):
        return flat(values).reshape(CHUNK // 4, 4, values.shape[-1])

    def flat(values):
        return values.reshape(CHUNK, values.shape[-1])

    own_copies = [
        pltpu.make_async_copy(source, target, local_sem.at[4 + k])
        for k, (source, target) in enumerate(
            (
                (w1_hbm, w1_own),
                (np_hbm, np_own),
                (wc_hbm, wc_own),
                (w3_hbm, w3_own),
                (sq_hbm, sq_own),
                (ex_hbm, ex_own),
            )
        )
    ]
    for copy in own_copies:
        copy.start()
    x_copy = pltpu.make_async_copy(x_hbm, x4, local_sem.at[0])
    gy_copy = pltpu.make_async_copy(gy_hbm, gy4, local_sem.at[1])
    x_copy.start()
    barrier = pltpu.get_barrier_semaphore()
    for device in all_peers:
        pl.semaphore_signal(barrier, inc=1, device_id=device, device_id_type=MESH)

    part = core * 2 + half_y
    own_copies[0].wait()
    q1 = w1_own.shape[0] // 4
    fw1[dp, core, half_y] = w1_own[pl.ds(pl.multiple_of(part * q1, q1), q1), :].astype(BF16)
    core_lanes = pl.ds(pl.multiple_of(core * 128, 128), 128)
    es_lanes = pl.ds(pl.multiple_of(part * 128, 128), 128)
    w3_lanes = pl.ds(pl.multiple_of(part * 256, 128), 256)

    pl.semaphore_wait(barrier, everyone - 1)

    def quarter_w1(c, y):
        return fw1.at[:, c, y]

    def quarter_wc(c, y):
        return fwc.at[:, y, :, pl.ds(pl.multiple_of(c * 128, 128), 128)]

    def quarter_es(c, y):
        return fes.at[:, :, pl.ds(pl.multiple_of((c * 2 + y) * 128, 128), 128)]

    def quarter_w3(c, y):
        return fw3.at[:, :, pl.ds(pl.multiple_of((c * 2 + y) * 256, 128), 256)]

    quarters = (quarter_w1, quarter_wc, quarter_es, quarter_w3)

    def piece(which, d):
        return (
            fw1.at[d, core, half_y],
            fwc.at[d, half_y, :, core_lanes],
            fes.at[d, :, es_lanes],
            fw3.at[d, :, w3_lanes],
        )[which]

    def seven(which):
        return (
            fw1.at[pl.ds(0, n_dp - 1), core, half_y],
            fwc.at[pl.ds(0, n_dp - 1), half_y, :, core_lanes],
            fes.at[pl.ds(0, n_dp - 1), :, es_lanes],
            fw3.at[pl.ds(0, n_dp - 1), :, w3_lanes],
        )[which]

    def gather_out(which):
        send_all(piece(which, dp), ws.at[which, 0], wr.at[which, 0], owner_peers)

    def gather_turn(which):
        wait_bytes(seven(which), wr.at[which, 0])
        mine = quarters[which](core, half_y)
        remote(mine, mine, ws.at[which, 1], wr.at[which, 1], across).start()
        remote(mine, mine, ws.at[which, 2], wr.at[which, 2], sibling).start()

    def gather_hand(which):
        theirs = quarters[which](core, 1 - half_y)
        wait_bytes(theirs, wr.at[which, 1])
        remote(theirs, theirs, ws.at[which, 3], wr.at[which, 3], sibling).start()

    def gather_end(which):
        wait_bytes(quarters[which](1 - core, half_y), wr.at[which, 2])
        wait_bytes(quarters[which](1 - core, 1 - half_y), wr.at[which, 3])

    def to_rows(source, target):
        def body(index, carry):
            values = source[pl.ds(index * (CHUNK // 4), CHUNK // 4)].astype(F32)
            row = pl.multiple_of(index * CHUNK, CHUNK)
            target[pl.ds(row, CHUNK), :] = values.reshape(CHUNK, CHANNELS).astype(BF16)
            return carry

        lax.fori_loop(0, ROWS // CHUNK, body, 0)

    gather_out(0)

    own_copies[1].wait()
    shard = np_own.shape[0]
    lanes_id = lax.broadcasted_iota(jnp.int32, (8, 128), 1)
    turn = lax.rem(shard * dp, 128)
    np_rows = []
    for at in range(0, shard, 128):
        width = min(128, shard - at)
        piece_row = np_own[pl.ds(at, width)].reshape(1, width)
        if width < 128:
            piece_row = jnp.concatenate([piece_row, jnp.zeros((1, 128 - width), F32)], axis=1)
        np_rows.append(piece_row)
    np_rows.append(jnp.zeros((8 - len(np_rows), 128), F32))
    np_turned = jnp.concatenate(np_rows, axis=0).astype(BF16).astype(F32)
    np_turned = pltpu.roll(np_turned, turn, 1)
    np_slots[dp] = jnp.where(lanes_id < turn, pltpu.roll(np_turned, 1, 0), np_turned)
    send_all(np_slots.at[dp], np_sems.at[0], np_sems.at[1], owner_peers)
    own_copies[2].wait()
    qc = wc_own.shape[0] // 2
    fwc[dp, half_y, :, core_lanes] = wc_own[
        pl.ds(pl.multiple_of(half_y * qc, qc), qc), core_lanes
    ].astype(BF16)
    gather_out(1)
    for copy in own_copies[3:]:
        copy.wait()
    ex_rows = ex_own.shape[0]
    es_own[:, 0:128] = sq_own[...].astype(BF16)
    es_own[0:ex_rows, 128:384] = ex_own[:, 0:256].astype(BF16)
    es_own[ex_rows : 2 * ex_rows, 128:384] = ex_own[:, 256:512].astype(BF16)
    es_own[:, 384:512] = jnp.zeros((2 * ex_rows, 128), BF16)
    fes[dp, :, es_lanes] = es_own[:, es_lanes]
    gather_out(2)
    fw3[dp, :, w3_lanes] = w3_own[:, w3_lanes].astype(BF16)
    gather_out(3)
    gy_copy.start()
    x_copy.wait()
    to_rows(x4, x_v)
    gather_turn(0)
    zero_rows = jnp.zeros((PAD, BOTTLE), F32)
    for side in range(3):
        act[side, 0:PAD, :] = zero_rows
        act[side, PAD + ROWS : 2 * PAD + ROWS, :] = zero_rows
    for lane_block in range(9):
        dcol[0:PAD, lane_block * 256 : lane_block * 256 + 256] = zero_rows
        dcol[PAD + ROWS : 2 * PAD + ROWS, lane_block * 256 : lane_block * 256 + 256] = zero_rows
    gather_hand(0)

    def sum_start(k, payload):
        if k in DIRECT:
            ar_slots_a[k][me] = payload
            send_all(ar_slots_a[k].at[me], ar_send_a.at[order[k]], ar_recv_a.at[order[k]], all_peers)
        else:
            ar_slots_a[k][in_plane] = payload
            send_all(ar_slots_a[k].at[in_plane], ar_send_a.at[order[k]], ar_recv_a.at[order[k]], plane_peers)

    def sum_slots(slots, count):
        sums = [slots[slot] for slot in range(count)]
        while len(sums) > 1:
            sums = [sums[i] + sums[i + 1] for i in range(0, len(sums), 2)]
        return sums[0]

    def sum_turn(k):
        if k in DIRECT:
            return
        wait_bytes(ar_slots_a[k].at[pl.ds(0, plane_size - 1)], ar_recv_a.at[order[k]])
        ar_slots_b[k][plane] = sum_slots(ar_slots_a[k], plane_size)
        send_all(ar_slots_b[k].at[plane], ar_send_b.at[order[k]], ar_recv_b.at[order[k]], column_peers)

    def sum_end(k):
        if k in DIRECT:
            wait_bytes(ar_slots_a[k].at[pl.ds(0, everyone - 1)], ar_recv_a.at[order[k]])
            return sum_slots(ar_slots_a[k], everyone)
        wait_bytes(ar_slots_b[k].at[pl.ds(0, planes - 1)], ar_recv_b.at[order[k]])
        return sum_slots(ar_slots_b[k], planes)

    def lanes_of(index, width):
        return pl.ds(pl.multiple_of(index * width, 128), width)

    cut = 64
    conv_rows = {1: pl.ds(0, cut), 2: pl.ds(cut, gc.shape[2] - cut)}
    grads = (g1, gc, gc, g3, ge, gb)
    turned_kinds = (0, 5)

    def half_of(which, c):
        ref = grads[which]
        if which in turned_kinds:
            return ref.at[c]
        if which in conv_rows:
            return ref.at[:, :, conv_rows[which], lanes_of(c, 128)]
        return ref.at[:, :, lanes_of(c, (512, 256)[which - 3])]

    def y_part(which, ref, y):
        if which in turned_kinds:
            return ref.at[y]
        if which < 3:
            return ref.at[:, y]
        return ref.at[:, :, lanes_of(y, (256, 128)[which - 3])]

    def quarter_of(which, c, y):
        ref = grads[which]
        if which in turned_kinds:
            return ref.at[c, y]
        if which in conv_rows:
            return ref.at[:, y, conv_rows[which], lanes_of(c, 128)]
        return ref.at[:, :, lanes_of(c * 2 + y, (256, 128)[which - 3])]

    def final_part(which, c, y):
        if which == 0:
            return fs[0].at[c, y]
        if which in conv_rows:
            return fs[1].at[y, conv_rows[which], lanes_of(c, 128)]
        return fs[which - 1].at[:, lanes_of(c * 2 + y, (256, 128)[which - 3])]

    def of_owner(which, ref, d):
        return ref.at[:, lanes_of(d, CHANNELS // n_dp)] if which in turned_kinds else ref.at[d]

    def in_blocks(which, body):
        if which in turned_kinds:
            count = 4
            rows = grads[which].shape[2] // count
            block = lambda index: pl.ds(pl.multiple_of(index * rows, rows), rows)
        else:
            count, block = n_dp, lambda index: index

        def step(index, carry):
            body(block(index))
            return carry

        lax.fori_loop(0, count, step, 0)

    def in_halves(which, body):
        if which != 0:
            return in_blocks(which, body)

        def step(index, carry):
            rows = g1.shape[2] // 4
            at = pl.ds(pl.multiple_of(lax.rem(index, 4) * rows, rows), rows)
            body((lax.div(index, 4), at))
            return carry

        lax.fori_loop(0, 8, step, 0)

    def reduce_core(which):
        source = half_of(which, 1 - core)
        if which < 4:

            def round_one(at):
                cs[which][at] = source[at].astype(BF16)

            in_halves(which, round_one)
            source = cs[which]
        remote(source, r1s[which], gs.at[which, 0], gr.at[which, 0], sibling).start()

    def reduce_y(which):
        wait_bytes(r1s[which], gr.at[which, 0])
        away = quarter_of(which, core, 1 - half_y)
        mine = quarter_of(which, core, half_y)
        there = y_part(which, r1s[which], 1 - half_y)
        here = y_part(which, r1s[which], half_y)

        def add_away(at):
            ys[which][at] = (away[at].astype(F32) + there[at].astype(F32)).astype(
                ys[which].dtype
            )

        in_blocks(which, add_away)
        remote(ys[which], r2s[which], gs.at[which, 1], gr.at[which, 1], across).start()

        def add_mine(at):
            mine[at] = (mine[at].astype(F32) + here[at].astype(F32)).astype(mine.dtype)

        in_blocks(which, add_mine)

    def reduce_owner(which):
        wait_bytes(r2s[which], gr.at[which, 1])
        mine = quarter_of(which, core, half_y)

        def add(at):
            ks[which][at] = (mine[at].astype(F32) + r2s[which][at].astype(F32)).astype(
                ks[which].dtype
            )

        in_blocks(which, add)
        for device in owner_peers:
            remote(
                of_owner(which, ks[which], device[0]),
                r3s[which].at[dp],
                gs.at[which, 2],
                gr.at[which, 2],
                device,
            ).start()
        own[which][...] = of_owner(which, mine, dp)[...].astype(F32) + of_owner(
            which, r2s[which], dp
        )[...].astype(F32)
        r3s[which][dp] = jnp.zeros(own[which].shape, r3s[which].dtype)

    def owner_total(which):
        wait_bytes(r3s[which].at[pl.ds(0, n_dp - 1)], gr.at[which, 2])
        total = own[which][...]
        for slot in range(n_dp):
            total = total + r3s[which][slot].astype(F32)
        return total

    def reduce_spread(which):
        total = owner_total(which)
        if which == 0:
            rows = pl.ds(pl.multiple_of(part * (BOTTLE // 4), BOTTLE // 4), BOTTLE // 4)
            total = total - fix[0, rows, :]
            for m in range(2):
                total = total - fix[1 + m, rows, :] * back_own[m]
        mine = final_part(which, core, half_y)
        mine[...] = total
        send_all(mine, gs.at[which, 3], gr.at[which, 3], rep_peers)

    def three_parts(which):
        if which == 0:
            return fix.at[:, pl.ds(0, BOTTLE // 4)]
        if which in conv_rows:
            return r1s[which].at[pl.ds(0, 3)]
        return fs[which - 1].at[:, pl.ds(0, 3 * (256, 128)[which - 3])]

    def reduce_end(which):
        wait_bytes(three_parts(which), gr.at[which, 3])

    gather_end(0)
    red[...] = jnp.dot(x_v[...], fw1[...].reshape(CHANNELS, BOTTLE), preferred_element_type=F32)

    def sums_of(ref, start, width):
        def body(row, carry):
            values = grouped(ref[pl.ds(row, CHUNK), start : start + width])
            return carry[0] + jnp.sum(values, axis=0), carry[1] + jnp.sum(values * values, axis=0)

        zero = jnp.zeros((8, width), F32)
        return over_rows(body, (zero, zero))

    def joined(found):
        both = [jnp.concatenate(item, axis=1) for item in zip(*found)]
        return fold_lanes(stack_sums(micro_sum(both[0]), micro_sum(both[1])))

    def both_sums(name):
        return unstack_sums(unfold_lanes(sum_end(name)))

    sum_start("reduced", joined([sums_of(red, 0, 256)]))
    gather_turn(1)
    gather_turn(2)

    gy_copy.wait()
    to_rows(gy4, gy_v)
    wait_bytes(np_slots.at[pl.ds(0, n_dp - 1)], np_sems.at[1])
    np_full[...] = jnp.zeros(np_full.shape, F32)
    for d in range(n_dp):
        at = shard * d // 128
        np_full[at : at + 8, :] = np_full[at : at + 8, :] + np_slots[d]

    def vector(at, width):
        rows = [np_full[at // 128 + k : at // 128 + k + 1, :] for k in range(width // 128)]
        return jnp.concatenate(rows, axis=1) if len(rows) > 1 else rows[0]

    gain_one, bias_one = vector(0, 256), vector(256, 256)
    gain_two, bias_two = vector(512, 512), vector(1024, 512)
    gain_pool, bias_pool = vector(1536, 128), vector(1664, 128)
    bias_expand = vector(1792, 512)
    gain_three, bias_three = vector(2304, 1024), vector(3328, 1024)

    total, square = both_sums("reduced")
    center1, scale1, mul1, add1 = norm_terms(total, square, gain_one, bias_one, pixels)

    def make_active(row, carry):
        turned = grouped(red[pl.ds(row, CHUNK), :]) * mul1 + add1
        act[1, pl.ds(PAD + row, CHUNK), :] = flat(turned * sigmoid(turned))
        return carry

    over_rows(make_active, 0)
    gather_hand(1)
    gather_hand(2)
    place = lax.rem(lax.broadcasted_iota(jnp.int32, (CHUNK, BOTTLE), 0) // 4, SIDE)
    not_last = place != SIDE - 1
    not_first = place != 0

    def beside(side, row, distance, lanes=slice(0, BOTTLE)):
        near = act[side, pl.ds(PAD + row - 8, CHUNK + 16), lanes]
        return pltpu.roll(near, (CHUNK + 16 - distance) % (CHUNK + 16), 0)[8 : 8 + CHUNK]

    def shift_active(row, carry):
        act[2, pl.ds(PAD + row, CHUNK), :] = jnp.where(not_last, beside(1, row, 4), 0.0)
        act[0, pl.ds(PAD + row, CHUNK), :] = jnp.where(not_first, beside(1, row, -4), 0.0)
        return carry

    over_rows(shift_active, 0)

    def make_columns(row, carry):
        for tap in range(9):
            down, side = tap // 3 - 1, tap % 3
            values = act[side, pl.ds(PAD + row + 56 * down, CHUNK), :].astype(BF16)
            columns[0, pl.ds(row, CHUNK), tap * 128 : tap * 128 + 128] = values[:, 0:128]
            columns[1, pl.ds(row, CHUNK), tap * 128 : tap * 128 + 128] = values[:, 128:256]
        return carry

    over_rows(make_columns, 0)
    gather_end(1)
    own_half = n_dp // 2

    def filters(group):
        return fwc[group * own_half : (group + 1) * own_half].reshape(9 * 128, BOTTLE)

    halves2 = (slice(0, 256), slice(256, 512))
    for group, lanes in enumerate(halves2):
        wid[:, lanes] = jnp.dot(columns[group], filters(group), preferred_element_type=F32)
        sum_start(f"widened{group}", joined([sums_of(wid, group * 256, 256)]))
    sum_turn("widened0")
    sum_turn("widened1")
    gather_turn(3)

    norm2 = []
    pooled = jnp.zeros((8, BOTTLE), F32)
    for group, lanes in enumerate(halves2):
        total, square = both_sums(f"widened{group}")
        norm2.append(norm_terms(total, square, gain_two[:, lanes], bias_two[:, lanes], pixels))
        m2, a2 = norm2[group][2:4]

        def make_splits(row, carry):
            turned = grouped(wid[pl.ds(row, CHUNK), lanes]) * m2 + a2
            values = turned * sigmoid(turned)
            splits[pl.ds(row, CHUNK), lanes] = flat(values)
            return carry + jnp.sum(values, axis=0)

        pooled = over_rows(make_splits, pooled)
        if group == 0:
            gather_hand(3)
    pooled = image_sum(pooled) * (1.0 / (SIDE * SIDE))
    gather_end(2)
    squeeze = fes[:, :, 0:128].reshape(BOTTLE, INNER)
    ex_both = fes[:, :, 128:384]
    expand = jnp.concatenate(
        [
            ex_both[:, 0:ex_rows].reshape(INNER, 256),
            ex_both[:, ex_rows : 2 * ex_rows].reshape(INNER, 256),
        ],
        axis=1,
    )
    pre_pool = exact_dot(pooled, squeeze, False)
    sum_start("pool", four_rows(pair_sum(pre_pool), pair_sum(pre_pool * pre_pool)))
    first_micro = lax.rem(row_ids(BOTTLE), 4) < 2

    def make_normed(row, carry):
        rows = pl.ds(row, CHUNK)
        normed = (grouped(red[rows, :]) - center1) * scale1
        dwid[rows, 0:256] = flat(jnp.where(first_micro, normed, 0.0)).astype(BF16)
        dwid[rows, 256:512] = flat(jnp.where(first_micro, 0.0, normed)).astype(BF16)
        return carry + jnp.sum(grouped(x_v[rows, :].astype(F32)), axis=0)

    image_sums = micro_sum(over_rows(make_normed, jnp.zeros((8, CHANNELS), F32)))
    sum_start(
        "images",
        jnp.concatenate(
            [
                image_sums[2 * m : 2 * m + 1, at : at + 128]
                for m in range(2)
                for at in range(0, CHANNELS, 128)
            ],
            axis=0,
        ),
    )
    normed_images = tdot(dwid[...], x_v[...]).astype(BF16)
    normed_images = normed_images.reshape(2, 2, 2, BOTTLE // 4, CHANNELS)
    for m in range(2):
        gb[:, :, m * (BOTTLE // 4) : (m + 1) * (BOTTLE // 4)] = normed_images[m]
    reduce_core(5)
    total, square = from_four(sum_end("pool"))
    center_p, scale_p, mul_p, add_p = norm_terms(total, square, gain_pool, bias_pool, pictures)
    normed_p = (pre_pool - center_p) * scale_p
    norm_p = pre_pool * mul_p + add_p
    gate_p = sigmoid(norm_p)
    hidden = norm_p * gate_p
    slope_p = gate_p * (1.0 + norm_p * (1.0 - gate_p))
    logits = exact_dot(hidden, expand, False) + bias_expand
    left, right = logits[:, 0:256], logits[:, 256:512]
    most = jnp.maximum(left, right)
    left, right = jnp.exp(left - most), jnp.exp(right - most)
    att0 = left / (left + right)
    att1 = right / (left + right)

    gather_end(3)
    last = fw3[...].reshape(BOTTLE, CHANNELS)
    def make_mixed(row, carry):
        rows = pl.ds(row, CHUNK)
        values = grouped(splits[rows, 0:256]) * att0 + grouped(splits[rows, 256:512]) * att1
        mixed[rows, :] = flat(values).astype(BF16)
        return carry

    over_rows(make_mixed, 0)
    halves3 = (slice(0, 512), slice(512, 1024))
    blocks3 = [[slice(512 * h + k, 512 * h + k + 256) for k in (0, 256)] for h in range(2)]
    for half, lanes in enumerate(halves3):
        proj[:, lanes] = jnp.dot(mixed[...], last[:, lanes], preferred_element_type=F32)
        sum_start(
            f"projected{half}", joined([sums_of(proj, 512 * half + k, 256) for k in (0, 256)])
        )
    sum_turn("projected0")
    sum_turn("projected1")
    sum_turn("images")
    reduce_y(5)

    norm3 = []
    zero = jnp.zeros((8, 256), F32)
    for half, lanes in enumerate(halves3):
        total, square = both_sums(f"projected{half}")
        norm3.append(norm_terms(total, square, gain_three[:, lanes], bias_three[:, lanes], pixels))
        found = []
        for k, block in enumerate(blocks3[half]):
            c3, s3, m3, a3 = (item[:, k * 256 : k * 256 + 256] for item in norm3[half])

            def make_out(row, carry):
                rows = pl.ds(row, CHUNK)
                values = grouped(proj[rows, block])
                summed = grouped(x_v[rows, block].astype(F32)) + (values * m3 + a3)
                gate = sigmoid(summed)
                bo4[pl.ds(row // 4, CHUNK // 4), :, block] = by_four(summed * gate).astype(BF16)
                upstream = grouped(gy_v[rows, block].astype(F32)) * (
                    gate * (1.0 + summed * (1.0 - gate))
                )
                up[rows, block] = flat(upstream)
                normed = (values - c3) * s3
                return carry[0] + jnp.sum(upstream, axis=0), carry[1] + jnp.sum(
                    upstream * normed, axis=0
                )

            found.append(over_rows(make_out, (zero, zero)))
        sum_start(f"back_projected{half}", joined(found))
    bo_copy = pltpu.make_async_copy(bo4, bo_hbm, local_sem.at[2])
    bo_copy.start()

    def write_norm(at, pattern):
        at = at // 128
        both = pattern[0:1, :] + pattern[2:3, :]
        for k in range(both.shape[1] // 128):
            np_full[at + k : at + k + 1, :] = both[:, k * 128 : k * 128 + 128]

    sum_turn("back_projected0")
    sum_turn("back_projected1")
    reduce_owner(5)

    for half, lanes in enumerate(halves3):
        bias_sum, gain_sum = both_sums(f"back_projected{half}")
        write_norm(2304 + 512 * half, gain_sum)
        write_norm(3328 + 512 * half, bias_sum)
        by_value, constant = back_terms(*norm3[half][0:3], bias_sum, gain_sum, pixels)
        for k, block in enumerate(blocks3[half]):
            m3, v3, k3 = (
                item[:, k * 256 : k * 256 + 256] for item in (norm3[half][2], by_value, constant)
            )

            def make_dproj(row, carry):
                rows = pl.ds(row, CHUNK)
                values = grouped(up[rows, block]) * m3 + grouped(proj[rows, block]) * v3 + k3
                dproj[rows, block] = flat(values).astype(BF16)
                return carry

            over_rows(make_dproj, 0)
        part_mixed = dot_t(dproj[:, lanes], last[:, lanes])
        d_mixed[...] = part_mixed if half == 0 else d_mixed[...] + part_mixed

    def attend(row, carry):
        rows = pl.ds(row, CHUNK)
        values = grouped(d_mixed[rows, :])
        return (
            carry[0] + jnp.sum(values * grouped(splits[rows, 0:256]), axis=0),
            carry[1] + jnp.sum(values * grouped(splits[rows, 256:512]), axis=0),
        )

    d_att0, d_att1 = over_rows(attend, (zero, zero))
    d_att0, d_att1 = image_sum(d_att0), image_sum(d_att1)
    both = att0 * d_att0 + att1 * d_att1
    d_logits = jnp.concatenate([att0 * (d_att0 - both), att1 * (d_att1 - both)], axis=1)
    d_hidden = exact_dot(d_logits, expand, True)
    d_pool = d_hidden * slope_p
    per_micro = four_rows(pair_sum(d_pool), pair_sum(d_pool * normed_p))
    sum_start("back_pool", per_micro)
    ex_sum = pair_sum(d_logits)
    ex_sum = ex_sum + pltpu.roll(ex_sum, 2, 0)
    ex_rows_sum = ex_sum[:, 0:128]
    for k in range(1, 4):
        ex_rows_sum = jnp.where(row_ids(128) == k, ex_sum[:, k * 128 : k * 128 + 128], ex_rows_sum)

    grad_ex = image_dot(hidden, d_logits)
    grad_ex = grad_ex.reshape(n_dp, ex_rows, 512)
    ge[:, 0:ex_rows, 128:384] = grad_ex[:, :, 0:256]
    ge[:, ex_rows : 2 * ex_rows, 128:384] = grad_ex[:, :, 256:512]
    ge[:, :, 384:512] = jnp.zeros((n_dp, 2 * ex_rows, 128), F32)
    g3[...] = tdot(mixed[...], dproj[...]).reshape(g3.shape)
    reduce_core(3)
    held = []
    for group, att in ((0, att0), (1, att1)):
        lanes = halves2[group]
        c2, s2, m2, a2 = norm2[group]

        def make_dn2(row, carry):
            rows = pl.ds(row, CHUNK)
            values = grouped(wid[rows, lanes])
            turned = values * m2 + a2
            gate = sigmoid(turned)
            slope = gate * (1.0 + turned * (1.0 - gate))
            down = grouped(d_mixed[rows, :]) * att * slope
            dn2[rows, lanes] = flat(down)
            splits[rows, lanes] = flat(slope)
            normed = (values - c2) * s2
            terms = (down, down * normed, slope, slope * normed)
            return tuple(item + jnp.sum(term, axis=0) for item, term in zip(carry, terms))

        held.append([image_sum(item) for item in over_rows(make_dn2, (zero,) * 4)])
    pool_bias_sum, pool_gain_sum = from_four(sum_end("back_pool"))
    write_norm(1536, pool_gain_sum)
    write_norm(1664, pool_bias_sum)
    d_pre_pool = mul_p * (
        d_pool - pool_bias_sum * (1.0 / pictures) - normed_p * (pool_gain_sum * (1.0 / pictures))
    )
    d_pooled = exact_dot(d_pre_pool, squeeze, True) * (1.0 / (SIDE * SIDE))
    for group in range(2):
        down, down_normed, slope, slope_normed = held[group]
        payload = fold_lanes(
            stack_sums(
                pair_sum(down + d_pooled * slope), pair_sum(down_normed + d_pooled * slope_normed)
            )
        )
        if group == 1:
            payload = jnp.concatenate([payload, ex_rows_sum], axis=0)
        sum_start(f"back_widened{group}", payload)
    ge[:, :, 0:128] = image_dot(pooled, d_pre_pool).reshape(n_dp, 2 * ex_rows, 128)
    sum_turn("back_widened0")
    sum_turn("back_widened1")
    reduce_y(3)
    reduce_core(4)
    back_total = owner_total(5)
    back_own[0] = back_total[0 : BOTTLE // 4]
    back_own[1] = back_total[BOTTLE // 4 :]

    small_zero = jnp.zeros((8, 128), F32)
    for group, lanes in enumerate(halves2):
        whole = sum_end(f"back_widened{group}")
        if group == 1:
            np_full[14:18, :] = whole[8:12]
        bias_sum, gain_sum = unstack_sums(unfold_lanes(whole[0:8]))
        write_norm(512 + 256 * group, gain_sum)
        write_norm(1024 + 256 * group, bias_sum)
        m2 = norm2[group][2]
        v2, k2 = back_terms(*norm2[group][0:3], bias_sum, gain_sum, pixels)
        pooled_m2 = d_pooled * m2

        def make_dwid(row, carry):
            rows = pl.ds(row, CHUNK)
            values = grouped(dn2[rows, lanes]) * m2 + grouped(splits[rows, lanes]) * pooled_m2
            values = values + grouped(wid[rows, lanes]) * v2 + k2
            dwid[rows, lanes] = flat(values).astype(BF16)
            return carry

        over_rows(make_dwid, 0)
        gc[group * own_half : (group + 1) * own_half] = tdot(
            columns[group], dwid[:, lanes]
        ).reshape(own_half, 2, 9 * 128 // own_half // 2, BOTTLE)
    reduce_core(1)
    reduce_core(2)
    for group, lanes in enumerate(halves2):
        dcol[PAD : PAD + ROWS, group * 1152 : group * 1152 + 1152] = dot_t(
            dwid[:, lanes], filters(group)
        )
        inner = slice(group * 128, group * 128 + 128)

        def gather_taps(row, carry):
            for side in range(3):
                total = None
                for down in range(3):
                    at = group * 1152 + (3 * down + side) * 128
                    values = dcol[pl.ds(PAD + row - 56 * (down - 1), CHUNK), at : at + 128]
                    total = values if total is None else total + values
                act[side, pl.ds(PAD + row, CHUNK), inner] = total
            return carry

        over_rows(gather_taps, 0)
        c1, s1, m1, a1 = (item[:, inner] for item in (center1, scale1, mul1, add1))
        not_first1, not_last1 = not_first[:, inner], not_last[:, inner]

        def make_dn1(row, carry):
            rows = pl.ds(row, CHUNK)
            d_active = act[1, pl.ds(PAD + row, CHUNK), inner]
            d_active = d_active + jnp.where(not_first1, beside(2, row, -4, inner), 0.0)
            d_active = d_active + jnp.where(not_last1, beside(0, row, 4, inner), 0.0)
            values = grouped(red[rows, inner])
            turned = values * m1 + a1
            gate = sigmoid(turned)
            slope = gate * (1.0 + turned * (1.0 - gate))
            down = grouped(d_active) * slope
            dn1[rows, inner] = flat(down)
            mixed[rows, inner] = flat(down * m1).astype(BF16)
            normed = (values - c1) * s1
            return carry[0] + jnp.sum(down, axis=0), carry[1] + jnp.sum(down * normed, axis=0)

        bias_sum, gain_sum = over_rows(make_dn1, (small_zero, small_zero))
        sum_start(f"back_reduced{group}", stack_sums(micro_sum(bias_sum), micro_sum(gain_sum)))
        if group == 0:
            reduce_y(1)
    sum_turn("back_reduced0")
    sum_turn("back_reduced1")
    reduce_y(2)
    reduce_y(4)
    reduce_owner(3)
    g1[...] = tdot(mixed[...], x_v[...]).reshape(g1.shape)
    reduce_core(0)
    found = [unstack_sums(sum_end(f"back_reduced{group}")) for group in range(2)]
    bias_sum, gain_sum = (jnp.concatenate(item, axis=1) for item in zip(*found))
    write_norm(0, gain_sum)
    write_norm(256, bias_sum)
    by_value, constant = back_terms(center1, scale1, mul1, bias_sum, gain_sum, pixels)
    def make_dred(row, carry):
        rows = pl.ds(row, CHUNK)
        values = grouped(dn1[rows, :]) * mul1 + grouped(red[rows, :]) * by_value + constant
        dred[rows, :] = flat(values).astype(BF16)
        return carry

    over_rows(make_dred, 0)
    reduce_owner(1)
    reduce_owner(4)
    proj[...] = dot_t(dred[...], fw1[...].reshape(CHANNELS, BOTTLE))
    reduce_y(0)

    by_bias = mul1 * bias_sum * (1.0 / pixels)
    by_gain = mul1 * gain_sum * (1.0 / pixels)
    image_sums = sum_end("images")
    ids = lax.broadcasted_iota(jnp.int32, (16, 128), 0)
    own_sums = [
        jnp.sum(jnp.where(ids == m * n_dp + dp, image_sums, 0.0), axis=0, keepdims=True)
        for m in range(2)
    ]
    ids = row_ids(128)
    fix[0] = row_dot(by_bias, jnp.where(ids == 0, own_sums[0], jnp.where(ids == 2, own_sums[1], 0.0)))
    for m in range(2):
        fix[1 + m] = row_dot(by_gain, jnp.where(ids == 2 * m, 1.0, 0.0))
    reduce_spread(3)
    reduce_spread(4)

    def make_dx(row, carry):
        for start in range(0, CHANNELS, 256):
            lanes = slice(start, start + 256)
            values = up[pl.ds(row, CHUNK), lanes] + proj[pl.ds(row, CHUNK), lanes]
            dx4[pl.ds(row // 4, CHUNK // 4), :, lanes] = values.reshape(CHUNK // 4, 4, 256)
        return carry

    over_rows(make_dx, 0)
    dx_copy = pltpu.make_async_copy(dx4, dx_hbm, local_sem.at[3])
    dx_copy.start()
    norm_rows = np_full[0:8, :]
    for d in range(1, n_dp):
        at = shard * d // 128
        norm_rows = jnp.where(dp == d, np_full[at : at + 8, :], norm_rows)
    norm_rows = pltpu.roll(norm_rows, lax.rem(128 - turn, 128), 1)
    gn_out[...] = jnp.where(lanes_id < 128 - turn, norm_rows, pltpu.roll(norm_rows, 7, 0))
    reduce_owner(2)
    reduce_owner(0)
    reduce_spread(1)
    reduce_spread(2)
    reduce_spread(0)
    out_copies = [
        pltpu.make_async_copy(source, target, local_sem.at[10 + k])
        for k, (source, target) in enumerate(
            (
                (gn_out, gn_hbm),
                (fs[2], f3_hbm),
                (fs[3], fe_hbm),
                (fs[1], fc_hbm),
                (fs[0], f1_hbm),
            )
        )
    ]
    out_copies[0].start()
    for which in (3, 4, 1, 2, 0):
        reduce_end(which)
        if which != 1:
            out_copies[{3: 1, 4: 2, 2: 3, 0: 4}[which]].start()

    bo_copy.wait()
    dx_copy.wait()
    for copy in out_copies:
        copy.wait()
    for k in STATS:
        if k in DIRECT:
            wait_bytes(ar_slots_a[k].at[pl.ds(0, everyone - 1)], ar_send_a.at[order[k]])
        else:
            wait_bytes(ar_slots_a[k].at[pl.ds(0, plane_size - 1)], ar_send_a.at[order[k]])
            wait_bytes(ar_slots_b[k].at[pl.ds(0, planes - 1)], ar_send_b.at[order[k]])
    wait_bytes(np_slots.at[pl.ds(0, n_dp - 1)], np_sems.at[0])
    for which in range(4):
        wait_bytes(seven(which), ws.at[which, 0])
        for stage in range(1, 4):
            wait_bytes(quarters[which](core, half_y), ws.at[which, stage])
    for which in range(6):
        wait_bytes(r1s[which], gs.at[which, 0])
        wait_bytes(r2s[which], gs.at[which, 1])
        wait_bytes(r3s[which].at[pl.ds(0, n_dp - 1)], gs.at[which, 2])
        if which < 5:
            wait_bytes(three_parts(which), gs.at[which, 3])


def update_kernel(*refs):
    sources, targets = refs[0:25], refs[25:45]
    inputs, outs, through = refs[45:68], refs[68:86], refs[86:88]
    pass_sems, in_sems, out_sems = refs[88:91]
    fetching, passing = [], []
    half = SIDE * SIDE // 2
    for number, (which, at, count) in enumerate(((1, 0, half), (1, half, half), (0, 0, 2 * half))):
        rows = pl.ds(at, count)
        fetching.append(
            pltpu.make_async_copy(
                sources[which].at[rows], through[which].at[rows], pass_sems.at[0, number]
            )
        )
        passing.append(
            pltpu.make_async_copy(
                through[which].at[rows], targets[which].at[rows], pass_sems.at[1, number]
            )
        )
    for copy in fetching:
        copy.start()
    coming = [
        pltpu.make_async_copy(source, held, in_sems.at[k])
        for k, (source, held) in enumerate(zip(sources[2:], inputs))
    ]
    for copy in coming:
        copy.start()
    grads, states = inputs[0:5], inputs[5:23]
    going = [
        pltpu.make_async_copy(held, target, out_sems.at[k])
        for k, (held, target) in enumerate(zip(outs, targets[2:]))
    ]
    ex_rows = states[9].shape[0]
    shard = states[15].shape[0]
    fans = (CHANNELS, 9 * BOTTLE // RADIX, BOTTLE, INNER // 8, BOTTLE)
    for copy in coming[0:5]:
        copy.wait()
    found = (
        grads[0][...].T,
        grads[1][...],
        grads[3][:, 0:128],
        jnp.concatenate([grads[3][0:ex_rows, 128:384], grads[3][ex_rows:, 128:384]], axis=1),
        grads[2][...],
    )
    for order, k in enumerate((3, 2, 4, 0, 1)):
        for copy in coming[5 + 3 * k : 8 + 3 * k]:
            copy.wait()
        new = adamw(
            states[3 * k][...],
            states[3 * k + 1][...],
            states[3 * k + 2][...],
            found[k],
            2.0 * fans[k] ** (-0.5),
            DECAY,
        )
        for j in range(3):
            outs[3 * k + j][...] = new[j]
            going[3 * k + j].start()
        if order < 3:
            fetching[order].wait()
            passing[order].start()
    for copy in coming[20:23]:
        copy.wait()
    for at in range(0, shard, 128):
        width = min(128, shard - at)
        lanes = pl.ds(at, width)
        new = adamw(
            *[states[15 + j][lanes].reshape(1, width) for j in range(3)],
            grads[4][at // 128 : at // 128 + 1, 0:width],
            NORM_RATE,
            0.0,
        )
        for j in range(3):
            outs[15 + j][lanes] = new[j].reshape(width)
    for copy in going[15:18]:
        copy.start()
    for copy in passing + going:
        copy.wait()


def fused_device(
    images,
    out_grad,
    reduce_weight,
    reduce_moment,
    reduce_second,
    conv_weight,
    conv_moment,
    conv_second,
    squeeze_weight,
    squeeze_moment,
    squeeze_second,
    expand_weight,
    expand_moment,
    expand_second,
    project_weight,
    project_moment,
    project_second,
    norm_params,
    norm_moment,
    norm_second,
):
    n_dp, n_rep = lax.axis_size("dp"), lax.axis_size("rep")
    by_pixel = lambda values: jnp.transpose(values, (1, 2, 0, 3)).reshape(-1, 4, CHANNELS)
    qc = conv_weight.shape[0] // 2
    q1 = reduce_weight.shape[0] // 4
    pe = squeeze_weight.shape[0]
    vmem = pltpu.VMEM
    pixel_form = (SIDE * SIDE, 4, CHANNELS)
    scratch = [
        *[
            vmem(values.shape, F32)
            for values in (
                reduce_weight,
                conv_weight,
                squeeze_weight,
                expand_weight,
                project_weight,
                norm_params,
            )
        ],
        vmem((8, 128), F32),
        vmem(pixel_form, BF16),
        vmem(pixel_form, BF16),
        vmem((ROWS, CHANNELS), BF16),
        vmem((ROWS, CHANNELS), BF16),
        vmem((n_dp, 2, 2, q1, BOTTLE), BF16),
        vmem((n_dp, 2, qc, BOTTLE), BF16),
        vmem((n_dp, pe, 512), BF16),
        vmem((n_dp, pe, CHANNELS), BF16),
        vmem((pe, 512), BF16),
        vmem((n_dp, 8, 128), F32),
        vmem((40, 128), F32),
        vmem((ROWS, BOTTLE), F32),
        vmem((3, ROWS + 2 * PAD, BOTTLE), F32),
        vmem((2, ROWS, 9 * 128), BF16),
        vmem((ROWS, 512), F32),
        vmem((ROWS, 512), F32),
        vmem((ROWS, BOTTLE), BF16),
        vmem((ROWS, CHANNELS), F32),
        vmem((ROWS, CHANNELS), F32),
        vmem(pixel_form, BF16),
        vmem(pixel_form, F32),
        vmem((ROWS, CHANNELS), BF16),
        vmem((ROWS, BOTTLE), F32),
        vmem((ROWS, 512), F32),
        vmem((ROWS, 512), BF16),
        vmem((ROWS + 2 * PAD, 2 * 9 * 128), F32),
        vmem((ROWS, BOTTLE), F32),
        vmem((ROWS, BOTTLE), BF16),
        vmem((2, 2, BOTTLE // 4, CHANNELS), F32),
        vmem((n_dp, 2, qc, BOTTLE), F32),
        vmem((n_dp, pe, CHANNELS), F32),
        vmem((n_dp, pe, 512), F32),
        vmem((2, 2, BOTTLE // 2, CHANNELS), BF16),
        vmem((3, BOTTLE, CHANNELS // n_dp), F32),
        vmem((2, BOTTLE // 4, CHANNELS // n_dp), F32),
    ]
    direct = n_dp * n_rep
    scratch += [
        vmem((direct if k in DIRECT else 2 * n_rep,) + shape, F32) for k, shape in STATS.items()
    ]
    scratch += [vmem((n_dp // 2,) + shape, F32) for shape in STATS.values()]
    cut = 64
    lanes1 = CHANNELS // n_dp
    half = [
        (2, BOTTLE // 4, CHANNELS),
        (n_dp, 2, cut, 128),
        (n_dp, 2, qc - cut, 128),
        (n_dp, pe, 512),
        (n_dp, pe, 256),
        (2, BOTTLE // 2, CHANNELS),
    ]
    quarter = [
        (BOTTLE // 4, CHANNELS),
        (n_dp, cut, 128),
        (n_dp, qc - cut, 128),
        (n_dp, pe, 256),
        (n_dp, pe, 128),
        (BOTTLE // 2, CHANNELS),
    ]
    final = [(2, 2, BOTTLE // 4, lanes1), (2, qc, BOTTLE), (pe, CHANNELS), (pe, 512)]
    sent = [BF16, BF16, BF16, BF16, F32, BF16]
    scratch += [vmem(shape, kind) for shape, kind in zip(half, sent)]
    scratch += [vmem(shape, kind) for shape, kind in zip(quarter, sent)] * 3
    owned = [(BOTTLE // 4, lanes1)] + [shape[1:] for shape in quarter[1:-1]]
    owned += [(BOTTLE // 2, lanes1)]
    scratch += [vmem((n_dp,) + shape, kind) for shape, kind in zip(owned, sent)]
    scratch += [vmem(shape, F32) for shape in owned]
    scratch += [vmem(shape, F32) for shape in final]
    scratch += [vmem(shape, BF16) for shape in half[0:4]]
    dma = pltpu.SemaphoreType.DMA
    scratch += [dma((15,))] + [dma((len(STATS),))] * 4 + [dma((2,))] + [dma((4, 4))] * 2 + [dma((6, 4))] * 2
    any_space = pl.BlockSpec(memory_space=pl.ANY)
    block_out, images_grad, sum1, sumc, sum3, sume, norm_grads = pl.pallas_call(
        functools.partial(block_kernel, n_dp, n_rep),
        out_shape=[
            jax.ShapeDtypeStruct(pixel_form, BF16),
            jax.ShapeDtypeStruct(pixel_form, F32),
            *[jax.ShapeDtypeStruct(shape, F32) for shape in final],
            jax.ShapeDtypeStruct((8, 128), F32),
        ],
        in_specs=[any_space] * 8,
        out_specs=[any_space] * 7,
        scratch_shapes=scratch,
        compiler_params=pltpu.CompilerParams(
            collective_id=0, has_side_effects=True, vmem_limit_bytes=63 * 1024 * 1024
        ),
    )(
        by_pixel(images),
        by_pixel(out_grad),
        reduce_weight,
        conv_weight,
        squeeze_weight,
        expand_weight,
        project_weight,
        norm_params,
    )
    states = (
        reduce_weight,
        reduce_moment,
        reduce_second,
        conv_weight,
        conv_moment,
        conv_second,
        squeeze_weight,
        squeeze_moment,
        squeeze_second,
        expand_weight,
        expand_moment,
        expand_second,
        project_weight,
        project_moment,
        project_second,
    )
    held = (*states, norm_params, norm_moment, norm_second)
    sums = (
        sum1.reshape(BOTTLE, lanes1),
        sumc.reshape(conv_weight.shape),
        sum3,
        sume,
        norm_grads,
    )
    block_out, images_grad, *updated = pl.pallas_call(
        update_kernel,
        out_shape=[
            jax.ShapeDtypeStruct(pixel_form, BF16),
            jax.ShapeDtypeStruct(pixel_form, F32),
            *[jax.ShapeDtypeStruct(state.shape, F32) for state in held],
        ],
        in_specs=[any_space] * 25,
        out_specs=[any_space] * 20,
        scratch_shapes=[vmem(values.shape, F32) for values in (*sums, *held, *held)]
        + [vmem(pixel_form, BF16), vmem(pixel_form, F32)]
        + [dma((2, 3)), dma((23,)), dma((18,))],
        compiler_params=pltpu.CompilerParams(vmem_limit_bytes=63 * 1024 * 1024),
    )(block_out, images_grad, *sums, *held)
    by_image = lambda values: jnp.transpose(
        values.reshape(SIDE, SIDE, images.shape[0], CHANNELS), (2, 0, 1, 3)
    )
    return (
        by_image(block_out),
        by_image(images_grad),
        *updated,
    )


def solution(mesh):
    placed = (
        P(("dp", "rep"), None, None, None),
        P(("dp", "rep"), None, None, None),
        P("dp", None),
        P("dp", None),
        P("dp", None),
        P("dp", None),
        P("dp", None),
        P("dp", None),
        P("dp", None),
        P("dp", None),
        P("dp", None),
        P("dp", None),
        P("dp", None),
        P("dp", None),
        P("dp", None),
        P("dp", None),
        P("dp", None),
        P("dp"),
        P("dp"),
        P("dp"),
    )
    n_dp, n_rep = mesh.shape["dp"], mesh.shape["rep"]
    whole_tiles = n_rep == 4 and n_dp % 2 == 0 and INNER % (16 * n_dp) == 0
    return jax.shard_map(
        fused_device if whole_tiles else per_device,
        mesh=mesh,
        in_specs=placed,
        out_specs=(
            P(("dp", "rep"), None, None, None),
            P(("dp", "rep"), None, None, None),
            P("dp", None),
            P("dp", None),
            P("dp", None),
            P("dp", None),
            P("dp", None),
            P("dp", None),
            P("dp", None),
            P("dp", None),
            P("dp", None),
            P("dp", None),
            P("dp", None),
            P("dp", None),
            P("dp", None),
            P("dp", None),
            P("dp", None),
            P("dp"),
            P("dp"),
            P("dp"),
        ),
        check_vma=False,
    )
```

```python
import functools
import jax
import jax.numpy as jnp
from jax import lax
from jax.experimental import pallas as pl
from jax.experimental.pallas import tpu as pltpu
from jax.sharding import PartitionSpec as P

CHANNELS = 1024
BOTTLE = 256
INNER = 128
RADIX = 2
SIDE = 14
MICRO = 2
STEP = 10


EPSILON = 1e-05
PRECISE = lax.Precision.HIGHEST
BETA_ONE = 0.9
BETA_TWO = 0.999
ADAM_EPSILON = 1e-08
DECAY = 0.01
NORM_RATE = 0.8
ROWS = 4 * SIDE * SIDE
NORM_WIDTH = 4352


def split_params(packed):
    widths = (
        BOTTLE,
        BOTTLE,
        RADIX * BOTTLE,
        RADIX * BOTTLE,
        INNER,
        INNER,
        RADIX * BOTTLE,
        CHANNELS,
        CHANNELS,
    )
    pieces = []
    offset = 0
    for segment in widths:
        pieces.append(lax.slice_in_dim(packed, offset, offset + segment))
        offset = offset + segment
    return pieces


def silu_slope(values):
    logistic = jax.nn.sigmoid(values)
    return logistic * (1.0 + values * (1.0 - logistic))


def norm_forward(values, gain, bias, count):
    flat = values.reshape(-1, values.shape[-1])
    total, square = lax.psum((jnp.sum(flat, axis=0), jnp.sum(flat * flat, axis=0)), ("dp", "rep"))
    center = total / count
    scale = lax.rsqrt(square / count - center * center + EPSILON)
    normed = (values - center) * scale
    return (normed * gain + bias, normed, scale)


def norm_backward(upstream, normed, scale, gain, count):
    flat_up = upstream.reshape(-1, upstream.shape[-1])
    flat_norm = normed.reshape(-1, normed.shape[-1])
    bias_sum, gain_sum = lax.psum(
        (jnp.sum(flat_up, axis=0), jnp.sum(flat_up * flat_norm, axis=0)), ("dp", "rep")
    )
    downstream = gain * scale * (upstream - bias_sum / count - normed * (gain_sum / count))
    return (downstream, gain_sum, bias_sum)


def patches(active):
    padded = jnp.pad(active, ((0, 0), (1, 1), (1, 1), (0, 0), (0, 0)))
    shifted = [
        padded[:, down_step : down_step + SIDE, side_step : side_step + SIDE]
        for down_step in range(3)
        for side_step in range(3)
    ]
    return jnp.stack(shifted, axis=4)


def unpatch(columns):
    total = jnp.zeros(
        (columns.shape[0], SIDE + 2, SIDE + 2, columns.shape[3], columns.shape[5]), jnp.float32
    )
    for down_step in range(3):
        for side_step in range(3):
            piece = columns[:, :, :, :, 3 * down_step + side_step]
            total = total + jnp.pad(
                piece,
                ((0, 0), (down_step, 2 - down_step), (side_step, 2 - side_step), (0, 0), (0, 0)),
            )
    return total[:, 1 : SIDE + 1, 1 : SIDE + 1]


def adamw(param, moment, second, gradient, rate, decay):
    moment_new = BETA_ONE * moment + (1.0 - BETA_ONE) * gradient
    second_new = BETA_TWO * second + (1.0 - BETA_TWO) * gradient * gradient
    ratio = (
        moment_new
        / (1.0 - BETA_ONE**STEP)
        / (jnp.sqrt(second_new / (1.0 - BETA_TWO**STEP)) + ADAM_EPSILON)
    )
    return (param - rate * (ratio + decay * param), moment_new, second_new)


def per_device(
    images,
    out_grad,
    reduce_weight,
    reduce_moment,
    reduce_second,
    conv_weight,
    conv_moment,
    conv_second,
    squeeze_weight,
    squeeze_moment,
    squeeze_second,
    expand_weight,
    expand_moment,
    expand_second,
    project_weight,
    project_moment,
    project_second,
    norm_params,
    norm_moment,
    norm_second,
):
    bf16 = jnp.bfloat16
    low_reduce = reduce_weight.astype(bf16)
    low_conv = conv_weight.astype(bf16)
    low_squeeze = squeeze_weight.astype(bf16)
    low_expand = expand_weight.astype(bf16)
    low_project = project_weight.astype(bf16)
    low_norm = norm_params.astype(bf16)
    devices = lax.axis_size("dp") * lax.axis_size("rep")
    per_batch = images.shape[0] // MICRO
    pixel_count = float(per_batch * SIDE * SIDE * devices)
    image_count = float(per_batch * devices)
    group_in = BOTTLE // RADIX
    grad_first = jnp.zeros((CHANNELS, BOTTLE), jnp.float32)
    grad_conv = jnp.zeros((RADIX, 9 * group_in, BOTTLE), jnp.float32)
    grad_squeeze = jnp.zeros((BOTTLE, INNER), jnp.float32)
    grad_expand = jnp.zeros((INNER, RADIX * BOTTLE), jnp.float32)
    grad_last = jnp.zeros((BOTTLE, CHANNELS), jnp.float32)
    grad_norms = jnp.zeros(
        (2 * BOTTLE + 3 * RADIX * BOTTLE + 2 * INNER + 2 * CHANNELS,), jnp.float32
    )
    outputs = []
    input_grads = []
    for number in range(MICRO):
        forward_set = (
            lax.all_gather(low_reduce, "dp", axis=0, tiled=True),
            lax.all_gather(low_conv, "dp", axis=0, tiled=True),
            lax.all_gather(low_squeeze, "dp", axis=0, tiled=True),
            lax.all_gather(low_expand, "dp", axis=0, tiled=True),
            lax.all_gather(low_project, "dp", axis=0, tiled=True),
            lax.all_gather(low_norm, "dp", axis=0, tiled=True),
        )
        first, conv, squeeze, expand, last, packed = forward_set
        (
            gain_one,
            bias_one,
            gain_two,
            bias_two,
            gain_pool,
            bias_pool,
            bias_expand,
            gain_three,
            bias_three,
        ) = split_params(packed.astype(jnp.float32))
        batched = images[number * per_batch : (number + 1) * per_batch]
        cotangent = out_grad[number * per_batch : (number + 1) * per_batch]
        reduced = jnp.einsum("nhwc,cb->nhwb", batched, first, preferred_element_type=jnp.float32)
        norm_one, normed_one, scale_one = norm_forward(reduced, gain_one, bias_one, pixel_count)
        active = jax.nn.silu(norm_one).astype(bf16)
        columns = patches(active.reshape(per_batch, SIDE, SIDE, RADIX, group_in)).reshape(
            per_batch * SIDE * SIDE, RADIX, 9 * group_in
        )
        conv_grouped = conv.reshape(RADIX, 9 * group_in, BOTTLE)
        widened = jnp.einsum(
            "prk,rko->pro", columns, conv_grouped, preferred_element_type=jnp.float32
        )
        widened = widened.reshape(per_batch, SIDE, SIDE, RADIX * BOTTLE)
        norm_two, normed_two, scale_two = norm_forward(widened, gain_two, bias_two, pixel_count)
        splits = jax.nn.silu(norm_two).reshape(per_batch, SIDE, SIDE, RADIX, BOTTLE)
        pooled = jnp.sum(jnp.sum(splits, axis=3), axis=(1, 2)) / (SIDE * SIDE)
        squeeze_float = squeeze.astype(jnp.float32)
        expand_float = expand.astype(jnp.float32)
        pre_pool = jnp.dot(pooled, squeeze_float, precision=PRECISE)
        norm_pool, normed_pool, scale_pool = norm_forward(
            pre_pool, gain_pool, bias_pool, image_count
        )
        hidden = jax.nn.silu(norm_pool)
        logits = (jnp.dot(hidden, expand_float, precision=PRECISE) + bias_expand).reshape(
            per_batch, RADIX, BOTTLE
        )
        attention = jax.nn.softmax(logits, axis=1)
        mixed = jnp.sum(splits * attention[:, None, None], axis=3).astype(bf16)
        projected = jnp.einsum("nhwb,bc->nhwc", mixed, last, preferred_element_type=jnp.float32)
        norm_three, normed_three, scale_three = norm_forward(
            projected, gain_three, bias_three, pixel_count
        )
        summed = batched.astype(jnp.float32) + norm_three
        outputs.append(jax.nn.silu(summed).astype(bf16))
        backward_set = (
            lax.all_gather(low_reduce, "dp", axis=0, tiled=True),
            lax.all_gather(low_conv, "dp", axis=0, tiled=True),
            lax.all_gather(low_squeeze, "dp", axis=0, tiled=True),
            lax.all_gather(low_expand, "dp", axis=0, tiled=True),
            lax.all_gather(low_project, "dp", axis=0, tiled=True),
            lax.all_gather(low_norm, "dp", axis=0, tiled=True),
        )
        first, conv, squeeze, expand, last, packed = backward_set
        gains_back = split_params(packed.astype(jnp.float32))
        conv_grouped = conv.reshape(RADIX, 9 * group_in, BOTTLE)
        expand_float = expand.astype(jnp.float32)
        squeeze_float = squeeze.astype(jnp.float32)
        upstream = cotangent.astype(jnp.float32) * silu_slope(summed)
        d_projected, gain_three_grad, bias_three_grad = norm_backward(
            upstream, normed_three, scale_three, gains_back[7], pixel_count
        )
        d_projected_low = d_projected.astype(bf16)
        grad_last = grad_last + jnp.einsum(
            "nhwb,nhwc->bc", mixed, d_projected_low, preferred_element_type=jnp.float32
        )
        d_mixed = jnp.einsum(
            "nhwc,bc->nhwb", d_projected_low, last, preferred_element_type=jnp.float32
        )
        d_splits = d_mixed[:, :, :, None] * attention[:, None, None]
        d_attention = jnp.sum(d_mixed[:, :, :, None] * splits, axis=(1, 2))
        d_logits = attention * (
            d_attention - jnp.sum(attention * d_attention, axis=1, keepdims=True)
        )
        flat_logits = d_logits.reshape(per_batch, RADIX * BOTTLE)
        grad_expand = grad_expand + jnp.dot(hidden.T, flat_logits, precision=PRECISE)
        d_hidden = jnp.dot(flat_logits, expand_float.T, precision=PRECISE)
        d_pool_norm = d_hidden * silu_slope(norm_pool)
        pool_bias_sum, pool_gain_sum, expand_bias_sum = lax.psum(
            (
                jnp.sum(d_pool_norm, axis=0),
                jnp.sum(d_pool_norm * normed_pool, axis=0),
                jnp.sum(flat_logits, axis=0),
            ),
            ("dp", "rep"),
        )
        d_pre_pool = (
            gains_back[4]
            * scale_pool
            * (
                d_pool_norm
                - pool_bias_sum / image_count
                - normed_pool * (pool_gain_sum / image_count)
            )
        )
        grad_squeeze = grad_squeeze + jnp.dot(pooled.T, d_pre_pool, precision=PRECISE)
        d_pooled = jnp.dot(d_pre_pool, squeeze_float.T, precision=PRECISE)
        d_splits = d_splits + (d_pooled / (SIDE * SIDE))[:, None, None, None, :]
        d_norm_two = d_splits.reshape(per_batch, SIDE, SIDE, RADIX * BOTTLE) * silu_slope(norm_two)
        d_widened, gain_two_grad, bias_two_grad = norm_backward(
            d_norm_two, normed_two, scale_two, gains_back[2], pixel_count
        )
        d_widened_low = d_widened.astype(bf16).reshape(per_batch * SIDE * SIDE, RADIX, BOTTLE)
        grad_conv = grad_conv + jnp.einsum(
            "prk,pro->rko", columns, d_widened_low, preferred_element_type=jnp.float32
        )
        d_columns = jnp.einsum(
            "pro,rko->prk", d_widened_low, conv_grouped, preferred_element_type=jnp.float32
        )
        d_active = unpatch(d_columns.reshape(per_batch, SIDE, SIDE, RADIX, 9, group_in)).reshape(
            per_batch, SIDE, SIDE, BOTTLE
        )
        d_norm_one = d_active * silu_slope(norm_one)
        d_reduced, gain_one_grad, bias_one_grad = norm_backward(
            d_norm_one, normed_one, scale_one, gains_back[0], pixel_count
        )
        d_reduced_low = d_reduced.astype(bf16)
        grad_first = grad_first + jnp.einsum(
            "nhwc,nhwb->cb", batched, d_reduced_low, preferred_element_type=jnp.float32
        )
        input_grads.append(
            upstream
            + jnp.einsum("nhwb,cb->nhwc", d_reduced_low, first, preferred_element_type=jnp.float32)
        )
        grad_norms = grad_norms + jnp.concatenate(
            [
                gain_one_grad,
                bias_one_grad,
                gain_two_grad,
                bias_two_grad,
                pool_gain_sum,
                pool_bias_sum,
                expand_bias_sum,
                gain_three_grad,
                bias_three_grad,
            ]
        )
    grad_conv = grad_conv.reshape(9 * BOTTLE, BOTTLE)
    partial_value = (
        lax.psum_scatter(grad_first, "dp", scatter_dimension=0, tiled=True),
        lax.psum_scatter(grad_conv, "dp", scatter_dimension=0, tiled=True),
        lax.psum_scatter(grad_squeeze, "dp", scatter_dimension=0, tiled=True),
        lax.psum_scatter(grad_expand, "dp", scatter_dimension=0, tiled=True),
        lax.psum_scatter(grad_last, "dp", scatter_dimension=0, tiled=True),
    )
    owned = lax.psum(
        (partial_value[0], partial_value[1], partial_value[2], partial_value[3], partial_value[4]),
        "rep",
    )
    shard_length = norm_params.shape[0]
    norm_grad_owned = lax.dynamic_slice_in_dim(
        grad_norms, lax.axis_index("dp") * shard_length, shard_length
    )
    reduce_new = adamw(
        reduce_weight, reduce_moment, reduce_second, owned[0], 2.0 * CHANNELS ** (-0.5), DECAY
    )
    conv_new = adamw(
        conv_weight,
        conv_moment,
        conv_second,
        owned[1],
        2.0 * (9 * BOTTLE // RADIX) ** (-0.5),
        DECAY,
    )
    squeeze_new = adamw(
        squeeze_weight, squeeze_moment, squeeze_second, owned[2], 2.0 * BOTTLE ** (-0.5), DECAY
    )
    expand_new = adamw(
        expand_weight, expand_moment, expand_second, owned[3], 2.0 * (INNER // 8) ** (-0.5), DECAY
    )
    project_new = adamw(
        project_weight, project_moment, project_second, owned[4], 2.0 * BOTTLE ** (-0.5), DECAY
    )
    norm_new = adamw(norm_params, norm_moment, norm_second, norm_grad_owned, NORM_RATE, 0.0)
    return (
        jnp.concatenate(outputs, axis=0),
        jnp.concatenate(input_grads, axis=0),
        reduce_new[0],
        reduce_new[1],
        reduce_new[2],
        conv_new[0],
        conv_new[1],
        conv_new[2],
        squeeze_new[0],
        squeeze_new[1],
        squeeze_new[2],
        expand_new[0],
        expand_new[1],
        expand_new[2],
        project_new[0],
        project_new[1],
        project_new[2],
        norm_new[0],
        norm_new[1],
        norm_new[2],
    )


MESH = pl.DeviceIdType.MESH
PAD = 64
CHUNK = 112
F32 = jnp.float32
BF16 = jnp.bfloat16
STATS = {
    "reduced": (8, 128),
    "widened0": (8, 128),
    "widened1": (8, 128),
    "pool": (8, 128),
    "images": (16, 128),
    "projected0": (8, 256),
    "projected1": (8, 256),
    "back_projected0": (8, 256),
    "back_projected1": (8, 256),
    "back_pool": (8, 128),
    "back_widened0": (8, 128),
    "back_widened1": (16, 128),
    "back_reduced0": (8, 128),
    "back_reduced1": (8, 128),
}
DIRECT = ("reduced", "pool", "back_pool")


def sigmoid(values):
    return 0.5 * jnp.tanh(0.5 * values) + 0.5


def row_ids(width):
    return lax.broadcasted_iota(jnp.int32, (8, width), 0)


def image_sum(rows):
    return rows + pltpu.roll(rows, 4, 0)


def pair_sum(rows):
    even = row_ids(rows.shape[1]) % 2 == 0
    return rows + jnp.where(even, pltpu.roll(rows, 7, 0), pltpu.roll(rows, 1, 0))


def micro_sum(rows):
    return pair_sum(image_sum(rows))


def stack_sums(first, second):
    return jnp.where(row_ids(first.shape[1]) < 4, first, second)


def unstack_sums(stacked):
    upper = row_ids(stacked.shape[1]) < 4
    turned = pltpu.roll(stacked, 4, 0)
    return jnp.where(upper, stacked, turned), jnp.where(upper, turned, stacked)


def fold_lanes(stacked):
    half = stacked.shape[1] // 2
    even = row_ids(half) % 2 == 0
    return jnp.where(even, stacked[:, :half], stacked[:, half:])


def unfold_lanes(folded):
    even = row_ids(folded.shape[1]) % 2 == 0
    left = jnp.where(even, folded, pltpu.roll(folded, 1, 0))
    right = jnp.where(even, pltpu.roll(folded, 7, 0), folded)
    return jnp.concatenate([left, right], axis=1)


def norm_terms(total, square, gain, bias, count):
    center = total * (1.0 / count)
    scale = lax.rsqrt(square * (1.0 / count) - center * center + EPSILON)
    slope = scale * gain
    return center, scale, slope, bias - center * slope


def back_terms(center, scale, slope, bias_sum, gain_sum, count):
    by_value = -slope * scale * (gain_sum * (1.0 / count))
    constant = -slope * (bias_sum * (1.0 / count)) - by_value * center
    return by_value, constant


def tdot(left, right):
    return lax.dot_general(left, right, (((0,), (0,)), ((), ())), preferred_element_type=F32)


def dot_t(left, right):
    return lax.dot_general(left, right, (((1,), (1,)), ((), ())), preferred_element_type=F32)


def in_parts(values, parts):
    found = []
    for _ in range(parts):
        rounded = values.astype(BF16).astype(F32)
        found.append(rounded)
        values = values - rounded
    return found


def exact_dot(left, right, transposed):
    stacked = jnp.concatenate(in_parts(left, 3), axis=0).astype(BF16)
    wide = dot_t(stacked, right) if transposed else jnp.dot(stacked, right, preferred_element_type=F32)
    return wide[0:8] + wide[8:16] + wide[16:24]


def row_dot(left, right):
    high, low = in_parts(left, 2)
    other_high, other_low = in_parts(right, 2)
    return tdot(
        jnp.concatenate([high, high, low, low], axis=0).astype(BF16),
        jnp.concatenate([other_high, other_low, other_high, other_low], axis=0).astype(BF16),
    )


def image_dot(left, right):
    return row_dot(jnp.where(row_ids(left.shape[1]) < 4, left, 0.0), right)


def block_kernel(
    n_dp,
    n_rep,
    x_hbm,
    gy_hbm,
    w1_hbm,
    wc_hbm,
    sq_hbm,
    ex_hbm,
    w3_hbm,
    np_hbm,
    bo_hbm,
    dx_hbm,
    f1_hbm,
    fc_hbm,
    f3_hbm,
    fe_hbm,
    gn_hbm,
    w1_own,
    wc_own,
    sq_own,
    ex_own,
    w3_own,
    np_own,
    gn_out,
    x4,
    gy4,
    x_v,
    gy_v,
    fw1,
    fwc,
    fes,
    fw3,
    es_own,
    np_slots,
    np_full,
    red,
    act,
    columns,
    wid,
    splits,
    mixed,
    proj,
    up,
    bo4,
    dx4,
    dproj,
    d_mixed,
    dn2,
    dwid,
    dcol,
    dn1,
    dred,
    g1,
    gc,
    g3,
    ge,
    gb,
    fix,
    back_own,
    *rest,
):
    n_ar = len(STATS)
    order = {name: k for k, name in enumerate(STATS)}
    ar_slots_a = dict(zip(STATS, rest[0:n_ar]))
    ar_slots_b = dict(zip(STATS, rest[n_ar : 2 * n_ar]))
    rest = rest[2 * n_ar :]
    r1s, ys, r2s, ks, r3s, own = (rest[6 * i : 6 * i + 6] for i in range(6))
    fs = rest[36:40]
    rest = rest[40:]
    local_sem, ar_send_a, ar_recv_a, ar_send_b, ar_recv_b, np_sems, ws, wr, gs, gr = rest

    dp = lax.axis_index("dp")
    rep = lax.axis_index("rep")
    core = lax.rem(rep, 2)
    half_y = lax.div(rep, 2)
    planes = n_dp // 2
    plane_size = 2 * n_rep
    plane = lax.div(dp, 2)
    in_plane = lax.rem(dp, 2) * n_rep + rep
    sibling = (dp, half_y * 2 + (1 - core))
    across = (dp, (1 - half_y) * 2 + core)
    pixels = float(SIDE * SIDE * 2 * n_dp * n_rep)
    pictures = float(2 * n_dp * n_rep)

    x = lax.rem(dp, 2)
    if planes == 4:
        upper = lax.div(plane, 2)
        other_planes = [3 - 3 * upper, 2 - upper, 1 - plane + 4 * upper]
    else:
        other_planes = [lax.rem(plane + step, planes) for step in range(1, planes)]
    flips = ((1, 1, 1), (1, 1, 0), (1, 0, 1), (1, 0, 0), (0, 1, 1), (0, 1, 0), (0, 0, 1), (0, 0, 0))

    def of_flip(z, flip):
        there = [1 - own if turn else own for own, turn in zip((x, half_y, core), flip)]
        return (z * 2 + there[0], there[1] * 2 + there[2])

    plane_peers = [of_flip(plane, flip) for flip in flips[:-1]]
    column_peers = [of_flip(z, flips[-1]) for z in other_planes]
    owner_peers = [of_flip(z, flip) for z in other_planes for flip in (flips[3], flips[7])]
    owner_peers += [of_flip(plane, flips[3])]
    all_peers = [of_flip(z, flip) for z in other_planes for flip in flips] + plane_peers
    me, everyone = dp * n_rep + rep, n_dp * n_rep
    rep_peers = [(dp, lax.rem(rep + step, n_rep)) for step in range(1, n_rep)]

    def remote(src, dst, send_sem, recv_sem, device):
        return pltpu.make_async_remote_copy(
            src_ref=src,
            dst_ref=dst,
            send_sem=send_sem,
            recv_sem=recv_sem,
            device_id=device,
            device_id_type=MESH,
        )

    def send_all(ref, send_sem, recv_sem, peers):
        for device in peers:
            remote(ref, ref, send_sem, recv_sem, device).start()

    def wait_bytes(ref, sem):
        pltpu.make_async_copy(ref, ref, sem).wait()

    def over_rows(body, init):
        def step(index, carry):
            return body(pl.multiple_of(index * CHUNK, CHUNK), carry)

        return lax.fori_loop(0, ROWS // CHUNK, step, init)

    def grouped(values):
        return values.reshape(CHUNK // 8, 8, values.shape[-1])

    def by_four(values):
        return flat(values).reshape(CHUNK // 4, 4, values.shape[-1])

    def flat(values):
        return values.reshape(CHUNK, values.shape[-1])

    own_copies = [
        pltpu.make_async_copy(source, target, local_sem.at[4 + k])
        for k, (source, target) in enumerate(
            (
                (w1_hbm, w1_own),
                (np_hbm, np_own),
                (wc_hbm, wc_own),
                (w3_hbm, w3_own),
                (sq_hbm, sq_own),
                (ex_hbm, ex_own),
            )
        )
    ]
    for copy in own_copies:
        copy.start()
    x_copy = pltpu.make_async_copy(x_hbm, x4, local_sem.at[0])
    gy_copy = pltpu.make_async_copy(gy_hbm, gy4, local_sem.at[1])
    x_copy.start()
    barrier = pltpu.get_barrier_semaphore()
    for device in all_peers:
        pl.semaphore_signal(barrier, inc=1, device_id=device, device_id_type=MESH)

    part = core * 2 + half_y
    own_copies[0].wait()
    q1 = w1_own.shape[0] // 4
    fw1[dp, core, half_y] = w1_own[pl.ds(pl.multiple_of(part * q1, q1), q1), :].astype(BF16)
    core_lanes = pl.ds(pl.multiple_of(core * 128, 128), 128)
    es_lanes = pl.ds(pl.multiple_of(part * 128, 128), 128)
    w3_lanes = pl.ds(pl.multiple_of(part * 256, 128), 256)

    pl.semaphore_wait(barrier, everyone - 1)

    def quarter_w1(c, y):
        return fw1.at[:, c, y]

    def quarter_wc(c, y):
        return fwc.at[:, y, :, pl.ds(pl.multiple_of(c * 128, 128), 128)]

    def quarter_es(c, y):
        return fes.at[:, :, pl.ds(pl.multiple_of((c * 2 + y) * 128, 128), 128)]

    def quarter_w3(c, y):
        return fw3.at[:, :, pl.ds(pl.multiple_of((c * 2 + y) * 256, 128), 256)]

    quarters = (quarter_w1, quarter_wc, quarter_es, quarter_w3)

    def piece(which, d):
        return (
            fw1.at[d, core, half_y],
            fwc.at[d, half_y, :, core_lanes],
            fes.at[d, :, es_lanes],
            fw3.at[d, :, w3_lanes],
        )[which]

    def seven(which):
        return (
            fw1.at[pl.ds(0, n_dp - 1), core, half_y],
            fwc.at[pl.ds(0, n_dp - 1), half_y, :, core_lanes],
            fes.at[pl.ds(0, n_dp - 1), :, es_lanes],
            fw3.at[pl.ds(0, n_dp - 1), :, w3_lanes],
        )[which]

    def gather_out(which):
        send_all(piece(which, dp), ws.at[which, 0], wr.at[which, 0], owner_peers)

    def gather_turn(which):
        wait_bytes(seven(which), wr.at[which, 0])
        mine = quarters[which](core, half_y)
        remote(mine, mine, ws.at[which, 1], wr.at[which, 1], across).start()
        remote(mine, mine, ws.at[which, 2], wr.at[which, 2], sibling).start()

    def gather_hand(which):
        theirs = quarters[which](core, 1 - half_y)
        wait_bytes(theirs, wr.at[which, 1])
        remote(theirs, theirs, ws.at[which, 3], wr.at[which, 3], sibling).start()

    def gather_end(which):
        wait_bytes(quarters[which](1 - core, half_y), wr.at[which, 2])
        wait_bytes(quarters[which](1 - core, 1 - half_y), wr.at[which, 3])

    def to_rows(source, target):
        def body(index, carry):
            values = source[pl.ds(index * (CHUNK // 4), CHUNK // 4)].astype(F32)
            row = pl.multiple_of(index * CHUNK, CHUNK)
            target[pl.ds(row, CHUNK), :] = values.reshape(CHUNK, CHANNELS).astype(BF16)
            return carry

        lax.fori_loop(0, ROWS // CHUNK, body, 0)

    gather_out(0)

    own_copies[1].wait()
    shard = np_own.shape[0]
    lanes_id = lax.broadcasted_iota(jnp.int32, (8, 128), 1)
    turn = lax.rem(shard * dp, 128)
    np_rows = []
    for at in range(0, shard, 128):
        width = min(128, shard - at)
        piece_row = np_own[pl.ds(at, width)].reshape(1, width)
        if width < 128:
            piece_row = jnp.concatenate([piece_row, jnp.zeros((1, 128 - width), F32)], axis=1)
        np_rows.append(piece_row)
    np_rows.append(jnp.zeros((8 - len(np_rows), 128), F32))
    np_turned = jnp.concatenate(np_rows, axis=0).astype(BF16).astype(F32)
    np_turned = pltpu.roll(np_turned, turn, 1)
    np_slots[dp] = jnp.where(lanes_id < turn, pltpu.roll(np_turned, 1, 0), np_turned)
    send_all(np_slots.at[dp], np_sems.at[0], np_sems.at[1], owner_peers)
    own_copies[2].wait()
    qc = wc_own.shape[0] // 2
    fwc[dp, half_y, :, core_lanes] = wc_own[
        pl.ds(pl.multiple_of(half_y * qc, qc), qc), core_lanes
    ].astype(BF16)
    gather_out(1)
    for copy in own_copies[3:]:
        copy.wait()
    ex_rows = ex_own.shape[0]
    es_own[:, 0:128] = sq_own[...].astype(BF16)
    es_own[0:ex_rows, 128:384] = ex_own[:, 0:256].astype(BF16)
    es_own[ex_rows : 2 * ex_rows, 128:384] = ex_own[:, 256:512].astype(BF16)
    es_own[:, 384:512] = jnp.zeros((2 * ex_rows, 128), BF16)
    fes[dp, :, es_lanes] = es_own[:, es_lanes]
    gather_out(2)
    fw3[dp, :, w3_lanes] = w3_own[:, w3_lanes].astype(BF16)
    gather_out(3)
    gy_copy.start()
    x_copy.wait()
    to_rows(x4, x_v)
    gather_turn(0)
    zero_rows = jnp.zeros((PAD, BOTTLE), F32)
    for side in range(3):
        act[side, 0:PAD, :] = zero_rows
        act[side, PAD + ROWS : 2 * PAD + ROWS, :] = zero_rows
    for lane_block in range(9):
        dcol[0:PAD, lane_block * 256 : lane_block * 256 + 256] = zero_rows
        dcol[PAD + ROWS : 2 * PAD + ROWS, lane_block * 256 : lane_block * 256 + 256] = zero_rows
    gather_hand(0)
    gather_turn(1)
    gather_turn(2)

    def sum_start(k, payload):
        if k in DIRECT:
            ar_slots_a[k][me] = payload
            send_all(ar_slots_a[k].at[me], ar_send_a.at[order[k]], ar_recv_a.at[order[k]], all_peers)
        else:
            ar_slots_a[k][in_plane] = payload
            send_all(ar_slots_a[k].at[in_plane], ar_send_a.at[order[k]], ar_recv_a.at[order[k]], plane_peers)

    def sum_slots(slots, count):
        sums = [slots[slot] for slot in range(count)]
        while len(sums) > 1:
            sums = [sums[i] + sums[i + 1] for i in range(0, len(sums), 2)]
        return sums[0]

    def sum_turn(k):
        if k in DIRECT:
            return
        wait_bytes(ar_slots_a[k].at[pl.ds(0, plane_size - 1)], ar_recv_a.at[order[k]])
        ar_slots_b[k][plane] = sum_slots(ar_slots_a[k], plane_size)
        send_all(ar_slots_b[k].at[plane], ar_send_b.at[order[k]], ar_recv_b.at[order[k]], column_peers)

    def sum_end(k):
        if k in DIRECT:
            wait_bytes(ar_slots_a[k].at[pl.ds(0, everyone - 1)], ar_recv_a.at[order[k]])
            return sum_slots(ar_slots_a[k], everyone)
        wait_bytes(ar_slots_b[k].at[pl.ds(0, planes - 1)], ar_recv_b.at[order[k]])
        return sum_slots(ar_slots_b[k], planes)

    def lanes_of(index, width):
        return pl.ds(pl.multiple_of(index * width, 128), width)

    cut = 64
    conv_rows = {1: pl.ds(0, cut), 2: pl.ds(cut, gc.shape[2] - cut)}
    grads = (g1, gc, gc, g3, ge, gb)
    turned_kinds = (0, 5)

    def half_of(which, c):
        ref = grads[which]
        if which in turned_kinds:
            return ref.at[c]
        if which in conv_rows:
            return ref.at[:, :, conv_rows[which], lanes_of(c, 128)]
        return ref.at[:, :, lanes_of(c, (512, 256)[which - 3])]

    def y_part(which, ref, y):
        if which in turned_kinds:
            return ref.at[y]
        if which < 3:
            return ref.at[:, y]
        return ref.at[:, :, lanes_of(y, (256, 128)[which - 3])]

    def quarter_of(which, c, y):
        ref = grads[which]
        if which in turned_kinds:
            return ref.at[c, y]
        if which in conv_rows:
            return ref.at[:, y, conv_rows[which], lanes_of(c, 128)]
        return ref.at[:, :, lanes_of(c * 2 + y, (256, 128)[which - 3])]

    def final_part(which, c, y):
        if which == 0:
            return fs[0].at[c, y]
        if which in conv_rows:
            return fs[1].at[y, conv_rows[which], lanes_of(c, 128)]
        return fs[which - 1].at[:, lanes_of(c * 2 + y, (256, 128)[which - 3])]

    def of_owner(which, ref, d):
        return ref.at[:, lanes_of(d, CHANNELS // n_dp)] if which in turned_kinds else ref.at[d]

    def in_blocks(which, body):
        if which in turned_kinds:
            count = 4
            rows = grads[which].shape[2] // count
            block = lambda index: pl.ds(pl.multiple_of(index * rows, rows), rows)
        else:
            count, block = n_dp, lambda index: index

        def step(index, carry):
            body(block(index))
            return carry

        lax.fori_loop(0, count, step, 0)

    def reduce_core(which):
        remote(
            half_of(which, 1 - core), r1s[which], gs.at[which, 0], gr.at[which, 0], sibling
        ).start()

    def reduce_y(which):
        wait_bytes(r1s[which], gr.at[which, 0])
        away = quarter_of(which, core, 1 - half_y)
        mine = quarter_of(which, core, half_y)
        there = y_part(which, r1s[which], 1 - half_y)
        here = y_part(which, r1s[which], half_y)

        def add_away(at):
            ys[which][at] = (away[at].astype(F32) + there[at].astype(F32)).astype(
                ys[which].dtype
            )

        in_blocks(which, add_away)
        remote(ys[which], r2s[which], gs.at[which, 1], gr.at[which, 1], across).start()

        def add_mine(at):
            mine[at] = (mine[at].astype(F32) + here[at].astype(F32)).astype(mine.dtype)

        in_blocks(which, add_mine)

    def reduce_owner(which):
        wait_bytes(r2s[which], gr.at[which, 1])
        mine = quarter_of(which, core, half_y)

        def add(at):
            ks[which][at] = (mine[at].astype(F32) + r2s[which][at].astype(F32)).astype(
                ks[which].dtype
            )

        in_blocks(which, add)
        for device in owner_peers:
            remote(
                of_owner(which, ks[which], device[0]),
                r3s[which].at[dp],
                gs.at[which, 2],
                gr.at[which, 2],
                device,
            ).start()
        own[which][...] = of_owner(which, mine, dp)[...].astype(F32) + of_owner(
            which, r2s[which], dp
        )[...].astype(F32)
        r3s[which][dp] = jnp.zeros(own[which].shape, r3s[which].dtype)

    def owner_total(which):
        wait_bytes(r3s[which].at[pl.ds(0, n_dp - 1)], gr.at[which, 2])
        total = own[which][...]
        for slot in range(n_dp):
            total = total + r3s[which][slot].astype(F32)
        return total

    def reduce_spread(which):
        total = owner_total(which)
        if which == 0:
            rows = pl.ds(pl.multiple_of(part * (BOTTLE // 4), BOTTLE // 4), BOTTLE // 4)
            total = total - fix[0, rows, :]
            for m in range(2):
                total = total - fix[1 + m, rows, :] * back_own[m]
        mine = final_part(which, core, half_y)
        mine[...] = total
        send_all(mine, gs.at[which, 3], gr.at[which, 3], rep_peers)

    def three_parts(which):
        if which == 0:
            return r1s[0].at[0, :, pl.ds(0, 3 * CHANNELS // n_dp)]
        return r1s[which].at[pl.ds(0, 3), 0] if which < 3 else y_part(which, r1s[which], 0).at[pl.ds(0, 3)]

    def reduce_end(which):
        wait_bytes(three_parts(which), gr.at[which, 3])

    gather_end(0)
    red[...] = jnp.dot(x_v[...], fw1[...].reshape(CHANNELS, BOTTLE), preferred_element_type=F32)

    def sums_of(ref, start, width):
        def body(row, carry):
            values = grouped(ref[pl.ds(row, CHUNK), start : start + width])
            return carry[0] + jnp.sum(values, axis=0), carry[1] + jnp.sum(values * values, axis=0)

        zero = jnp.zeros((8, width), F32)
        return over_rows(body, (zero, zero))

    def joined(found):
        both = [jnp.concatenate(item, axis=1) for item in zip(*found)]
        return fold_lanes(stack_sums(micro_sum(both[0]), micro_sum(both[1])))

    def both_sums(name):
        return unstack_sums(unfold_lanes(sum_end(name)))

    sum_start("reduced", joined([sums_of(red, 0, 256)]))
    gather_turn(3)

    gy_copy.wait()
    to_rows(gy4, gy_v)
    wait_bytes(np_slots.at[pl.ds(0, n_dp - 1)], np_sems.at[1])
    np_full[...] = jnp.zeros(np_full.shape, F32)
    for d in range(n_dp):
        at = shard * d // 128
        np_full[at : at + 8, :] = np_full[at : at + 8, :] + np_slots[d]

    def vector(at, width):
        rows = [np_full[at // 128 + k : at // 128 + k + 1, :] for k in range(width // 128)]
        return jnp.concatenate(rows, axis=1) if len(rows) > 1 else rows[0]

    gain_one, bias_one = vector(0, 256), vector(256, 256)
    gain_two, bias_two = vector(512, 512), vector(1024, 512)
    gain_pool, bias_pool = vector(1536, 128), vector(1664, 128)
    bias_expand = vector(1792, 512)
    gain_three, bias_three = vector(2304, 1024), vector(3328, 1024)

    gather_hand(1)
    gather_hand(2)
    total, square = both_sums("reduced")
    center1, scale1, mul1, add1 = norm_terms(total, square, gain_one, bias_one, pixels)

    def make_active(row, carry):
        turned = grouped(red[pl.ds(row, CHUNK), :]) * mul1 + add1
        act[1, pl.ds(PAD + row, CHUNK), :] = flat(turned * sigmoid(turned))
        return carry

    over_rows(make_active, 0)
    gather_hand(3)
    place = lax.rem(lax.broadcasted_iota(jnp.int32, (CHUNK, BOTTLE), 0) // 4, SIDE)
    not_last = place != SIDE - 1
    not_first = place != 0

    def beside(side, row, distance, lanes=slice(0, BOTTLE)):
        near = act[side, pl.ds(PAD + row - 8, CHUNK + 16), lanes]
        return pltpu.roll(near, (CHUNK + 16 - distance) % (CHUNK + 16), 0)[8 : 8 + CHUNK]

    def shift_active(row, carry):
        act[2, pl.ds(PAD + row, CHUNK), :] = jnp.where(not_last, beside(1, row, 4), 0.0)
        act[0, pl.ds(PAD + row, CHUNK), :] = jnp.where(not_first, beside(1, row, -4), 0.0)
        return carry

    over_rows(shift_active, 0)

    def make_columns(row, carry):
        for tap in range(9):
            down, side = tap // 3 - 1, tap % 3
            values = act[side, pl.ds(PAD + row + 56 * down, CHUNK), :].astype(BF16)
            columns[0, pl.ds(row, CHUNK), tap * 128 : tap * 128 + 128] = values[:, 0:128]
            columns[1, pl.ds(row, CHUNK), tap * 128 : tap * 128 + 128] = values[:, 128:256]
        return carry

    over_rows(make_columns, 0)
    gather_end(1)
    own_half = n_dp // 2

    def filters(group):
        return fwc[group * own_half : (group + 1) * own_half].reshape(9 * 128, BOTTLE)

    halves2 = (slice(0, 256), slice(256, 512))
    for group, lanes in enumerate(halves2):
        wid[:, lanes] = jnp.dot(columns[group], filters(group), preferred_element_type=F32)
        sum_start(f"widened{group}", joined([sums_of(wid, group * 256, 256)]))
    sum_turn("widened0")
    sum_turn("widened1")

    norm2 = []
    pooled = jnp.zeros((8, BOTTLE), F32)
    for group, lanes in enumerate(halves2):
        total, square = both_sums(f"widened{group}")
        norm2.append(norm_terms(total, square, gain_two[:, lanes], bias_two[:, lanes], pixels))
        m2, a2 = norm2[group][2:4]

        def make_splits(row, carry):
            turned = grouped(wid[pl.ds(row, CHUNK), lanes]) * m2 + a2
            values = turned * sigmoid(turned)
            splits[pl.ds(row, CHUNK), lanes] = flat(values)
            return carry + jnp.sum(values, axis=0)

        pooled = over_rows(make_splits, pooled)
    pooled = image_sum(pooled) * (1.0 / (SIDE * SIDE))
    gather_end(2)
    squeeze = fes[:, :, 0:128].reshape(BOTTLE, INNER)
    ex_both = fes[:, :, 128:384]
    expand = jnp.concatenate(
        [
            ex_both[:, 0:ex_rows].reshape(INNER, 256),
            ex_both[:, ex_rows : 2 * ex_rows].reshape(INNER, 256),
        ],
        axis=1,
    )
    pre_pool = exact_dot(pooled, squeeze, False)
    sum_start("pool", stack_sums(pair_sum(pre_pool), pair_sum(pre_pool * pre_pool)))
    first_micro = lax.rem(row_ids(BOTTLE), 4) < 2

    def make_normed(row, carry):
        rows = pl.ds(row, CHUNK)
        normed = (grouped(red[rows, :]) - center1) * scale1
        dwid[rows, 0:256] = flat(jnp.where(first_micro, normed, 0.0)).astype(BF16)
        dwid[rows, 256:512] = flat(jnp.where(first_micro, 0.0, normed)).astype(BF16)
        return carry + jnp.sum(grouped(x_v[rows, :].astype(F32)), axis=0)

    image_sums = micro_sum(over_rows(make_normed, jnp.zeros((8, CHANNELS), F32)))
    sum_start(
        "images",
        jnp.concatenate(
            [
                image_sums[2 * m : 2 * m + 1, at : at + 128]
                for m in range(2)
                for at in range(0, CHANNELS, 128)
            ],
            axis=0,
        ),
    )
    normed_images = tdot(dwid[...], x_v[...]).astype(BF16)
    normed_images = normed_images.reshape(2, 2, 2, BOTTLE // 4, CHANNELS)
    for m in range(2):
        gb[:, :, m * (BOTTLE // 4) : (m + 1) * (BOTTLE // 4)] = normed_images[m]
    reduce_core(5)
    total, square = unstack_sums(sum_end("pool"))
    center_p, scale_p, mul_p, add_p = norm_terms(total, square, gain_pool, bias_pool, pictures)
    normed_p = (pre_pool - center_p) * scale_p
    norm_p = pre_pool * mul_p + add_p
    gate_p = sigmoid(norm_p)
    hidden = norm_p * gate_p
    slope_p = gate_p * (1.0 + norm_p * (1.0 - gate_p))
    logits = exact_dot(hidden, expand, False) + bias_expand
    left, right = logits[:, 0:256], logits[:, 256:512]
    most = jnp.maximum(left, right)
    left, right = jnp.exp(left - most), jnp.exp(right - most)
    att0 = left / (left + right)
    att1 = right / (left + right)

    gather_end(3)
    last = fw3[...].reshape(BOTTLE, CHANNELS)
    def make_mixed(row, carry):
        rows = pl.ds(row, CHUNK)
        values = grouped(splits[rows, 0:256]) * att0 + grouped(splits[rows, 256:512]) * att1
        mixed[rows, :] = flat(values).astype(BF16)
        return carry

    over_rows(make_mixed, 0)
    halves3 = (slice(0, 512), slice(512, 1024))
    blocks3 = [[slice(512 * h + k, 512 * h + k + 256) for k in (0, 256)] for h in range(2)]
    for half, lanes in enumerate(halves3):
        proj[:, lanes] = jnp.dot(mixed[...], last[:, lanes], preferred_element_type=F32)
        sum_start(
            f"projected{half}", joined([sums_of(proj, 512 * half + k, 256) for k in (0, 256)])
        )
    sum_turn("projected0")
    sum_turn("projected1")
    sum_turn("images")
    reduce_y(5)

    norm3 = []
    zero = jnp.zeros((8, 256), F32)
    for half, lanes in enumerate(halves3):
        total, square = both_sums(f"projected{half}")
        norm3.append(norm_terms(total, square, gain_three[:, lanes], bias_three[:, lanes], pixels))
        found = []
        for k, block in enumerate(blocks3[half]):
            c3, s3, m3, a3 = (item[:, k * 256 : k * 256 + 256] for item in norm3[half])

            def make_out(row, carry):
                rows = pl.ds(row, CHUNK)
                values = grouped(proj[rows, block])
                summed = grouped(x_v[rows, block].astype(F32)) + (values * m3 + a3)
                gate = sigmoid(summed)
                bo4[pl.ds(row // 4, CHUNK // 4), :, block] = by_four(summed * gate).astype(BF16)
                upstream = grouped(gy_v[rows, block].astype(F32)) * (
                    gate * (1.0 + summed * (1.0 - gate))
                )
                up[rows, block] = flat(upstream)
                normed = (values - c3) * s3
                return carry[0] + jnp.sum(upstream, axis=0), carry[1] + jnp.sum(
                    upstream * normed, axis=0
                )

            found.append(over_rows(make_out, (zero, zero)))
        sum_start(f"back_projected{half}", joined(found))
    bo_copy = pltpu.make_async_copy(bo4, bo_hbm, local_sem.at[2])
    bo_copy.start()

    def write_norm(at, pattern):
        at = at // 128
        both = pattern[0:1, :] + pattern[2:3, :]
        for k in range(both.shape[1] // 128):
            np_full[at + k : at + k + 1, :] = both[:, k * 128 : k * 128 + 128]

    sum_turn("back_projected0")
    sum_turn("back_projected1")
    reduce_owner(5)

    for half, lanes in enumerate(halves3):
        bias_sum, gain_sum = both_sums(f"back_projected{half}")
        write_norm(2304 + 512 * half, gain_sum)
        write_norm(3328 + 512 * half, bias_sum)
        by_value, constant = back_terms(*norm3[half][0:3], bias_sum, gain_sum, pixels)
        for k, block in enumerate(blocks3[half]):
            m3, v3, k3 = (
                item[:, k * 256 : k * 256 + 256] for item in (norm3[half][2], by_value, constant)
            )

            def make_dproj(row, carry):
                rows = pl.ds(row, CHUNK)
                values = grouped(up[rows, block]) * m3 + grouped(proj[rows, block]) * v3 + k3
                dproj[rows, block] = flat(values).astype(BF16)
                return carry

            over_rows(make_dproj, 0)
        part_mixed = dot_t(dproj[:, lanes], last[:, lanes])
        d_mixed[...] = part_mixed if half == 0 else d_mixed[...] + part_mixed

    def attend(row, carry):
        rows = pl.ds(row, CHUNK)
        values = grouped(d_mixed[rows, :])
        return (
            carry[0] + jnp.sum(values * grouped(splits[rows, 0:256]), axis=0),
            carry[1] + jnp.sum(values * grouped(splits[rows, 256:512]), axis=0),
        )

    d_att0, d_att1 = over_rows(attend, (zero, zero))
    d_att0, d_att1 = image_sum(d_att0), image_sum(d_att1)
    both = att0 * d_att0 + att1 * d_att1
    d_logits = jnp.concatenate([att0 * (d_att0 - both), att1 * (d_att1 - both)], axis=1)
    d_hidden = exact_dot(d_logits, expand, True)
    d_pool = d_hidden * slope_p
    per_micro = stack_sums(pair_sum(d_pool), pair_sum(d_pool * normed_p))
    sum_start("back_pool", per_micro)
    ex_sum = pair_sum(d_logits)
    ex_sum = ex_sum + pltpu.roll(ex_sum, 2, 0)
    ex_rows_sum = ex_sum[:, 0:128]
    for k in range(1, 4):
        ex_rows_sum = jnp.where(row_ids(128) == k, ex_sum[:, k * 128 : k * 128 + 128], ex_rows_sum)

    grad_ex = image_dot(hidden, d_logits)
    grad_ex = grad_ex.reshape(n_dp, ex_rows, 512)
    ge[:, 0:ex_rows, 128:384] = grad_ex[:, :, 0:256]
    ge[:, ex_rows : 2 * ex_rows, 128:384] = grad_ex[:, :, 256:512]
    ge[:, :, 384:512] = jnp.zeros((n_dp, 2 * ex_rows, 128), F32)
    g3[...] = tdot(mixed[...], dproj[...]).reshape(g3.shape)
    reduce_core(3)
    held = []
    for group, att in ((0, att0), (1, att1)):
        lanes = halves2[group]
        c2, s2, m2, a2 = norm2[group]

        def make_dn2(row, carry):
            rows = pl.ds(row, CHUNK)
            values = grouped(wid[rows, lanes])
            turned = values * m2 + a2
            gate = sigmoid(turned)
            slope = gate * (1.0 + turned * (1.0 - gate))
            down = grouped(d_mixed[rows, :]) * att * slope
            dn2[rows, lanes] = flat(down)
            splits[rows, lanes] = flat(slope)
            normed = (values - c2) * s2
            terms = (down, down * normed, slope, slope * normed)
            return tuple(item + jnp.sum(term, axis=0) for item, term in zip(carry, terms))

        held.append([image_sum(item) for item in over_rows(make_dn2, (zero,) * 4)])
    pool_bias_sum, pool_gain_sum = unstack_sums(sum_end("back_pool"))
    write_norm(1536, pool_gain_sum)
    write_norm(1664, pool_bias_sum)
    d_pre_pool = mul_p * (
        d_pool - pool_bias_sum * (1.0 / pictures) - normed_p * (pool_gain_sum * (1.0 / pictures))
    )
    d_pooled = exact_dot(d_pre_pool, squeeze, True) * (1.0 / (SIDE * SIDE))
    for group in range(2):
        down, down_normed, slope, slope_normed = held[group]
        payload = fold_lanes(
            stack_sums(
                pair_sum(down + d_pooled * slope), pair_sum(down_normed + d_pooled * slope_normed)
            )
        )
        if group == 1:
            payload = jnp.concatenate([payload, ex_rows_sum], axis=0)
        sum_start(f"back_widened{group}", payload)
    ge[:, :, 0:128] = image_dot(pooled, d_pre_pool).reshape(n_dp, 2 * ex_rows, 128)
    reduce_core(4)
    sum_turn("back_widened0")
    sum_turn("back_widened1")
    reduce_y(3)
    reduce_y(4)
    back_total = owner_total(5)
    back_own[0] = back_total[0 : BOTTLE // 4]
    back_own[1] = back_total[BOTTLE // 4 :]

    small_zero = jnp.zeros((8, 128), F32)
    for group, lanes in enumerate(halves2):
        whole = sum_end(f"back_widened{group}")
        if group == 1:
            np_full[14:18, :] = whole[8:12]
        bias_sum, gain_sum = unstack_sums(unfold_lanes(whole[0:8]))
        write_norm(512 + 256 * group, gain_sum)
        write_norm(1024 + 256 * group, bias_sum)
        m2 = norm2[group][2]
        v2, k2 = back_terms(*norm2[group][0:3], bias_sum, gain_sum, pixels)
        pooled_m2 = d_pooled * m2

        def make_dwid(row, carry):
            rows = pl.ds(row, CHUNK)
            values = grouped(dn2[rows, lanes]) * m2 + grouped(splits[rows, lanes]) * pooled_m2
            values = values + grouped(wid[rows, lanes]) * v2 + k2
            dwid[rows, lanes] = flat(values).astype(BF16)
            return carry

        over_rows(make_dwid, 0)
        gc[group * own_half : (group + 1) * own_half] = tdot(
            columns[group], dwid[:, lanes]
        ).reshape(own_half, 2, 9 * 128 // own_half // 2, BOTTLE)
    reduce_core(1)
    reduce_core(2)
    for group, lanes in enumerate(halves2):
        dcol[PAD : PAD + ROWS, group * 1152 : group * 1152 + 1152] = dot_t(
            dwid[:, lanes], filters(group)
        )
        inner = slice(group * 128, group * 128 + 128)

        def gather_taps(row, carry):
            for side in range(3):
                total = None
                for down in range(3):
                    at = group * 1152 + (3 * down + side) * 128
                    values = dcol[pl.ds(PAD + row - 56 * (down - 1), CHUNK), at : at + 128]
                    total = values if total is None else total + values
                act[side, pl.ds(PAD + row, CHUNK), inner] = total
            return carry

        over_rows(gather_taps, 0)
        c1, s1, m1, a1 = (item[:, inner] for item in (center1, scale1, mul1, add1))
        not_first1, not_last1 = not_first[:, inner], not_last[:, inner]

        def make_dn1(row, carry):
            rows = pl.ds(row, CHUNK)
            d_active = act[1, pl.ds(PAD + row, CHUNK), inner]
            d_active = d_active + jnp.where(not_first1, beside(2, row, -4, inner), 0.0)
            d_active = d_active + jnp.where(not_last1, beside(0, row, 4, inner), 0.0)
            values = grouped(red[rows, inner])
            turned = values * m1 + a1
            gate = sigmoid(turned)
            slope = gate * (1.0 + turned * (1.0 - gate))
            down = grouped(d_active) * slope
            dn1[rows, inner] = flat(down)
            mixed[rows, inner] = flat(down * m1).astype(BF16)
            normed = (values - c1) * s1
            return carry[0] + jnp.sum(down, axis=0), carry[1] + jnp.sum(down * normed, axis=0)

        bias_sum, gain_sum = over_rows(make_dn1, (small_zero, small_zero))
        sum_start(f"back_reduced{group}", stack_sums(micro_sum(bias_sum), micro_sum(gain_sum)))
        if group == 0:
            reduce_owner(3)
            reduce_owner(4)
            reduce_y(1)
    reduce_y(2)
    sum_turn("back_reduced0")
    sum_turn("back_reduced1")
    g1[...] = tdot(mixed[...], x_v[...]).reshape(g1.shape)
    reduce_core(0)
    reduce_owner(1)
    found = [unstack_sums(sum_end(f"back_reduced{group}")) for group in range(2)]
    bias_sum, gain_sum = (jnp.concatenate(item, axis=1) for item in zip(*found))
    write_norm(0, gain_sum)
    write_norm(256, bias_sum)
    by_value, constant = back_terms(center1, scale1, mul1, bias_sum, gain_sum, pixels)
    def make_dred(row, carry):
        rows = pl.ds(row, CHUNK)
        values = grouped(dn1[rows, :]) * mul1 + grouped(red[rows, :]) * by_value + constant
        dred[rows, :] = flat(values).astype(BF16)
        return carry

    reduce_y(0)
    over_rows(make_dred, 0)
    reduce_owner(2)
    proj[...] = dot_t(dred[...], fw1[...].reshape(CHANNELS, BOTTLE))

    by_bias = mul1 * bias_sum * (1.0 / pixels)
    by_gain = mul1 * gain_sum * (1.0 / pixels)
    image_sums = sum_end("images")
    ids = lax.broadcasted_iota(jnp.int32, (16, 128), 0)
    own_sums = [
        jnp.sum(jnp.where(ids == m * n_dp + dp, image_sums, 0.0), axis=0, keepdims=True)
        for m in range(2)
    ]
    ids = row_ids(128)
    fix[0] = row_dot(by_bias, jnp.where(ids == 0, own_sums[0], jnp.where(ids == 2, own_sums[1], 0.0)))
    for m in range(2):
        fix[1 + m] = row_dot(by_gain, jnp.where(ids == 2 * m, 1.0, 0.0))
    reduce_spread(3)
    reduce_spread(4)
    reduce_spread(1)
    reduce_owner(0)

    def make_dx(row, carry):
        for start in range(0, CHANNELS, 256):
            lanes = slice(start, start + 256)
            values = up[pl.ds(row, CHUNK), lanes] + proj[pl.ds(row, CHUNK), lanes]
            dx4[pl.ds(row // 4, CHUNK // 4), :, lanes] = values.reshape(CHUNK // 4, 4, 256)
        return carry

    over_rows(make_dx, 0)
    dx_copy = pltpu.make_async_copy(dx4, dx_hbm, local_sem.at[3])
    dx_copy.start()
    norm_rows = np_full[0:8, :]
    for d in range(1, n_dp):
        at = shard * d // 128
        norm_rows = jnp.where(dp == d, np_full[at : at + 8, :], norm_rows)
    norm_rows = pltpu.roll(norm_rows, lax.rem(128 - turn, 128), 1)
    gn_out[...] = jnp.where(lanes_id < 128 - turn, norm_rows, pltpu.roll(norm_rows, 7, 0))
    reduce_spread(2)
    reduce_spread(0)
    out_copies = [
        pltpu.make_async_copy(source, target, local_sem.at[10 + k])
        for k, (source, target) in enumerate(
            (
                (gn_out, gn_hbm),
                (fs[2], f3_hbm),
                (fs[3], fe_hbm),
                (fs[1], fc_hbm),
                (fs[0], f1_hbm),
            )
        )
    ]
    out_copies[0].start()
    for which in (3, 4, 1, 2, 0):
        reduce_end(which)
        if which != 1:
            out_copies[{3: 1, 4: 2, 2: 3, 0: 4}[which]].start()

    bo_copy.wait()
    dx_copy.wait()
    for copy in out_copies:
        copy.wait()
    for k in STATS:
        if k in DIRECT:
            wait_bytes(ar_slots_a[k].at[pl.ds(0, everyone - 1)], ar_send_a.at[order[k]])
        else:
            wait_bytes(ar_slots_a[k].at[pl.ds(0, plane_size - 1)], ar_send_a.at[order[k]])
            wait_bytes(ar_slots_b[k].at[pl.ds(0, planes - 1)], ar_send_b.at[order[k]])
    wait_bytes(np_slots.at[pl.ds(0, n_dp - 1)], np_sems.at[0])
    for which in range(4):
        wait_bytes(seven(which), ws.at[which, 0])
        for stage in range(1, 4):
            wait_bytes(quarters[which](core, half_y), ws.at[which, stage])
    for which in range(6):
        wait_bytes(r1s[which], gs.at[which, 0])
        wait_bytes(r2s[which], gs.at[which, 1])
        wait_bytes(r3s[which].at[pl.ds(0, n_dp - 1)], gs.at[which, 2])
        if which < 5:
            wait_bytes(three_parts(which), gs.at[which, 3])


def update_kernel(*refs):
    sources, targets = refs[0:25], refs[25:45]
    inputs, outs, through = refs[45:68], refs[68:86], refs[86:88]
    pass_sems, in_sems, out_sems = refs[88:91]
    fetching, passing = [], []
    half = SIDE * SIDE // 2
    for number, (which, at, count) in enumerate(((1, 0, half), (1, half, half), (0, 0, 2 * half))):
        rows = pl.ds(at, count)
        fetching.append(
            pltpu.make_async_copy(
                sources[which].at[rows], through[which].at[rows], pass_sems.at[0, number]
            )
        )
        passing.append(
            pltpu.make_async_copy(
                through[which].at[rows], targets[which].at[rows], pass_sems.at[1, number]
            )
        )
    for copy in fetching:
        copy.start()
    coming = [
        pltpu.make_async_copy(source, held, in_sems.at[k])
        for k, (source, held) in enumerate(zip(sources[2:], inputs))
    ]
    for copy in coming:
        copy.start()
    grads, states = inputs[0:5], inputs[5:23]
    going = [
        pltpu.make_async_copy(held, target, out_sems.at[k])
        for k, (held, target) in enumerate(zip(outs, targets[2:]))
    ]
    ex_rows = states[9].shape[0]
    shard = states[15].shape[0]
    fans = (CHANNELS, 9 * BOTTLE // RADIX, BOTTLE, INNER // 8, BOTTLE)
    for copy in coming[0:5]:
        copy.wait()
    found = (
        grads[0][...].T,
        grads[1][...],
        grads[3][:, 0:128],
        jnp.concatenate([grads[3][0:ex_rows, 128:384], grads[3][ex_rows:, 128:384]], axis=1),
        grads[2][...],
    )
    for order, k in enumerate((3, 2, 4, 0, 1)):
        for copy in coming[5 + 3 * k : 8 + 3 * k]:
            copy.wait()
        new = adamw(
            states[3 * k][...],
            states[3 * k + 1][...],
            states[3 * k + 2][...],
            found[k],
            2.0 * fans[k] ** (-0.5),
            DECAY,
        )
        for j in range(3):
            outs[3 * k + j][...] = new[j]
            going[3 * k + j].start()
        if order < 3:
            fetching[order].wait()
            passing[order].start()
    for copy in coming[20:23]:
        copy.wait()
    for at in range(0, shard, 128):
        width = min(128, shard - at)
        lanes = pl.ds(at, width)
        new = adamw(
            *[states[15 + j][lanes].reshape(1, width) for j in range(3)],
            grads[4][at // 128 : at // 128 + 1, 0:width],
            NORM_RATE,
            0.0,
        )
        for j in range(3):
            outs[15 + j][lanes] = new[j].reshape(width)
    for copy in going[15:18]:
        copy.start()
    for copy in passing + going:
        copy.wait()


def fused_device(
    images,
    out_grad,
    reduce_weight,
    reduce_moment,
    reduce_second,
    conv_weight,
    conv_moment,
    conv_second,
    squeeze_weight,
    squeeze_moment,
    squeeze_second,
    expand_weight,
    expand_moment,
    expand_second,
    project_weight,
    project_moment,
    project_second,
    norm_params,
    norm_moment,
    norm_second,
):
    n_dp, n_rep = lax.axis_size("dp"), lax.axis_size("rep")
    by_pixel = lambda values: jnp.transpose(values, (1, 2, 0, 3)).reshape(-1, 4, CHANNELS)
    qc = conv_weight.shape[0] // 2
    q1 = reduce_weight.shape[0] // 4
    pe = squeeze_weight.shape[0]
    vmem = pltpu.VMEM
    pixel_form = (SIDE * SIDE, 4, CHANNELS)
    scratch = [
        *[
            vmem(values.shape, F32)
            for values in (
                reduce_weight,
                conv_weight,
                squeeze_weight,
                expand_weight,
                project_weight,
                norm_params,
            )
        ],
        vmem((8, 128), F32),
        vmem(pixel_form, BF16),
        vmem(pixel_form, BF16),
        vmem((ROWS, CHANNELS), BF16),
        vmem((ROWS, CHANNELS), BF16),
        vmem((n_dp, 2, 2, q1, BOTTLE), BF16),
        vmem((n_dp, 2, qc, BOTTLE), BF16),
        vmem((n_dp, pe, 512), BF16),
        vmem((n_dp, pe, CHANNELS), BF16),
        vmem((pe, 512), BF16),
        vmem((n_dp, 8, 128), F32),
        vmem((40, 128), F32),
        vmem((ROWS, BOTTLE), F32),
        vmem((3, ROWS + 2 * PAD, BOTTLE), F32),
        vmem((2, ROWS, 9 * 128), BF16),
        vmem((ROWS, 512), F32),
        vmem((ROWS, 512), F32),
        vmem((ROWS, BOTTLE), BF16),
        vmem((ROWS, CHANNELS), F32),
        vmem((ROWS, CHANNELS), F32),
        vmem(pixel_form, BF16),
        vmem(pixel_form, F32),
        vmem((ROWS, CHANNELS), BF16),
        vmem((ROWS, BOTTLE), F32),
        vmem((ROWS, 512), F32),
        vmem((ROWS, 512), BF16),
        vmem((ROWS + 2 * PAD, 2 * 9 * 128), F32),
        vmem((ROWS, BOTTLE), F32),
        vmem((ROWS, BOTTLE), BF16),
        vmem((2, 2, BOTTLE // 4, CHANNELS), F32),
        vmem((n_dp, 2, qc, BOTTLE), F32),
        vmem((n_dp, pe, CHANNELS), F32),
        vmem((n_dp, pe, 512), F32),
        vmem((2, 2, BOTTLE // 2, CHANNELS), BF16),
        vmem((3, BOTTLE, CHANNELS // n_dp), F32),
        vmem((2, BOTTLE // 4, CHANNELS // n_dp), F32),
    ]
    direct = n_dp * n_rep
    scratch += [
        vmem((direct if k in DIRECT else 2 * n_rep,) + shape, F32) for k, shape in STATS.items()
    ]
    scratch += [vmem((n_dp // 2,) + shape, F32) for shape in STATS.values()]
    cut = 64
    lanes1 = CHANNELS // n_dp
    half = [
        (2, BOTTLE // 4, CHANNELS),
        (n_dp, 2, cut, 128),
        (n_dp, 2, qc - cut, 128),
        (n_dp, pe, 512),
        (n_dp, pe, 256),
        (2, BOTTLE // 2, CHANNELS),
    ]
    quarter = [
        (BOTTLE // 4, CHANNELS),
        (n_dp, cut, 128),
        (n_dp, qc - cut, 128),
        (n_dp, pe, 256),
        (n_dp, pe, 128),
        (BOTTLE // 2, CHANNELS),
    ]
    final = [(2, 2, BOTTLE // 4, lanes1), (2, qc, BOTTLE), (pe, CHANNELS), (pe, 512)]
    sent = [BF16, BF16, BF16, BF16, F32, BF16]
    scratch += [vmem(shape, F32) for shape in half[:-1]] + [vmem(half[-1], BF16)]
    scratch += [vmem(shape, kind) for shape, kind in zip(quarter, sent)] * 3
    owned = [(BOTTLE // 4, lanes1)] + [shape[1:] for shape in quarter[1:-1]]
    owned += [(BOTTLE // 2, lanes1)]
    scratch += [vmem((n_dp,) + shape, kind) for shape, kind in zip(owned, sent)]
    scratch += [vmem(shape, F32) for shape in owned]
    scratch += [vmem(shape, F32) for shape in final]
    dma = pltpu.SemaphoreType.DMA
    scratch += [dma((15,))] + [dma((len(STATS),))] * 4 + [dma((2,))] + [dma((4, 4))] * 2 + [dma((6, 4))] * 2
    any_space = pl.BlockSpec(memory_space=pl.ANY)
    block_out, images_grad, sum1, sumc, sum3, sume, norm_grads = pl.pallas_call(
        functools.partial(block_kernel, n_dp, n_rep),
        out_shape=[
            jax.ShapeDtypeStruct(pixel_form, BF16),
            jax.ShapeDtypeStruct(pixel_form, F32),
            *[jax.ShapeDtypeStruct(shape, F32) for shape in final],
            jax.ShapeDtypeStruct((8, 128), F32),
        ],
        in_specs=[any_space] * 8,
        out_specs=[any_space] * 7,
        scratch_shapes=scratch,
        compiler_params=pltpu.CompilerParams(
            collective_id=0, has_side_effects=True, vmem_limit_bytes=63 * 1024 * 1024
        ),
    )(
        by_pixel(images),
        by_pixel(out_grad),
        reduce_weight,
        conv_weight,
        squeeze_weight,
        expand_weight,
        project_weight,
        norm_params,
    )
    states = (
        reduce_weight,
        reduce_moment,
        reduce_second,
        conv_weight,
        conv_moment,
        conv_second,
        squeeze_weight,
        squeeze_moment,
        squeeze_second,
        expand_weight,
        expand_moment,
        expand_second,
        project_weight,
        project_moment,
        project_second,
    )
    held = (*states, norm_params, norm_moment, norm_second)
    sums = (
        sum1.reshape(BOTTLE, lanes1),
        sumc.reshape(conv_weight.shape),
        sum3,
        sume,
        norm_grads,
    )
    block_out, images_grad, *updated = pl.pallas_call(
        update_kernel,
        out_shape=[
            jax.ShapeDtypeStruct(pixel_form, BF16),
            jax.ShapeDtypeStruct(pixel_form, F32),
            *[jax.ShapeDtypeStruct(state.shape, F32) for state in held],
        ],
        in_specs=[any_space] * 25,
        out_specs=[any_space] * 20,
        scratch_shapes=[vmem(values.shape, F32) for values in (*sums, *held, *held)]
        + [vmem(pixel_form, BF16), vmem(pixel_form, F32)]
        + [dma((2, 3)), dma((23,)), dma((18,))],
        compiler_params=pltpu.CompilerParams(vmem_limit_bytes=63 * 1024 * 1024),
    )(block_out, images_grad, *sums, *held)
    by_image = lambda values: jnp.transpose(
        values.reshape(SIDE, SIDE, images.shape[0], CHANNELS), (2, 0, 1, 3)
    )
    return (
        by_image(block_out),
        by_image(images_grad),
        *updated,
    )


def solution(mesh):
    placed = (
        P(("dp", "rep"), None, None, None),
        P(("dp", "rep"), None, None, None),
        P("dp", None),
        P("dp", None),
        P("dp", None),
        P("dp", None),
        P("dp", None),
        P("dp", None),
        P("dp", None),
        P("dp", None),
        P("dp", None),
        P("dp", None),
        P("dp", None),
        P("dp", None),
        P("dp", None),
        P("dp", None),
        P("dp", None),
        P("dp"),
        P("dp"),
        P("dp"),
    )
    n_dp, n_rep = mesh.shape["dp"], mesh.shape["rep"]
    whole_tiles = n_rep == 4 and n_dp % 2 == 0 and INNER % (16 * n_dp) == 0
    return jax.shard_map(
        fused_device if whole_tiles else per_device,
        mesh=mesh,
        in_specs=placed,
        out_specs=(
            P(("dp", "rep"), None, None, None),
            P(("dp", "rep"), None, None, None),
            P("dp", None),
            P("dp", None),
            P("dp", None),
            P("dp", None),
            P("dp", None),
            P("dp", None),
            P("dp", None),
            P("dp", None),
            P("dp", None),
            P("dp", None),
            P("dp", None),
            P("dp", None),
            P("dp", None),
            P("dp", None),
            P("dp", None),
            P("dp"),
            P("dp"),
            P("dp"),
        ),
        check_vma=False,
    )
```

```python
import functools
import jax
import jax.numpy as jnp
from jax import lax
from jax.experimental import pallas as pl
from jax.experimental.pallas import tpu as pltpu
from jax.sharding import PartitionSpec as P

CHANNELS = 1024
BOTTLE = 256
INNER = 128
RADIX = 2
SIDE = 14
MICRO = 2
STEP = 10


EPSILON = 1e-05
PRECISE = lax.Precision.HIGHEST
BETA_ONE = 0.9
BETA_TWO = 0.999
ADAM_EPSILON = 1e-08
DECAY = 0.01
NORM_RATE = 0.8
ROWS = 4 * SIDE * SIDE
NORM_WIDTH = 4352


def split_params(packed):
    widths = (
        BOTTLE,
        BOTTLE,
        RADIX * BOTTLE,
        RADIX * BOTTLE,
        INNER,
        INNER,
        RADIX * BOTTLE,
        CHANNELS,
        CHANNELS,
    )
    pieces = []
    offset = 0
    for segment in widths:
        pieces.append(lax.slice_in_dim(packed, offset, offset + segment))
        offset = offset + segment
    return pieces


def silu_slope(values):
    logistic = jax.nn.sigmoid(values)
    return logistic * (1.0 + values * (1.0 - logistic))


def norm_forward(values, gain, bias, count):
    flat = values.reshape(-1, values.shape[-1])
    total, square = lax.psum((jnp.sum(flat, axis=0), jnp.sum(flat * flat, axis=0)), ("dp", "rep"))
    center = total / count
    scale = lax.rsqrt(square / count - center * center + EPSILON)
    normed = (values - center) * scale
    return (normed * gain + bias, normed, scale)


def norm_backward(upstream, normed, scale, gain, count):
    flat_up = upstream.reshape(-1, upstream.shape[-1])
    flat_norm = normed.reshape(-1, normed.shape[-1])
    bias_sum, gain_sum = lax.psum(
        (jnp.sum(flat_up, axis=0), jnp.sum(flat_up * flat_norm, axis=0)), ("dp", "rep")
    )
    downstream = gain * scale * (upstream - bias_sum / count - normed * (gain_sum / count))
    return (downstream, gain_sum, bias_sum)


def patches(active):
    padded = jnp.pad(active, ((0, 0), (1, 1), (1, 1), (0, 0), (0, 0)))
    shifted = [
        padded[:, down_step : down_step + SIDE, side_step : side_step + SIDE]
        for down_step in range(3)
        for side_step in range(3)
    ]
    return jnp.stack(shifted, axis=4)


def unpatch(columns):
    total = jnp.zeros(
        (columns.shape[0], SIDE + 2, SIDE + 2, columns.shape[3], columns.shape[5]), jnp.float32
    )
    for down_step in range(3):
        for side_step in range(3):
            piece = columns[:, :, :, :, 3 * down_step + side_step]
            total = total + jnp.pad(
                piece,
                ((0, 0), (down_step, 2 - down_step), (side_step, 2 - side_step), (0, 0), (0, 0)),
            )
    return total[:, 1 : SIDE + 1, 1 : SIDE + 1]


def adamw(param, moment, second, gradient, rate, decay):
    moment_new = BETA_ONE * moment + (1.0 - BETA_ONE) * gradient
    second_new = BETA_TWO * second + (1.0 - BETA_TWO) * gradient * gradient
    ratio = (
        moment_new
        / (1.0 - BETA_ONE**STEP)
        / (jnp.sqrt(second_new / (1.0 - BETA_TWO**STEP)) + ADAM_EPSILON)
    )
    return (param - rate * (ratio + decay * param), moment_new, second_new)


def per_device(
    images,
    out_grad,
    reduce_weight,
    reduce_moment,
    reduce_second,
    conv_weight,
    conv_moment,
    conv_second,
    squeeze_weight,
    squeeze_moment,
    squeeze_second,
    expand_weight,
    expand_moment,
    expand_second,
    project_weight,
    project_moment,
    project_second,
    norm_params,
    norm_moment,
    norm_second,
):
    bf16 = jnp.bfloat16
    low_reduce = reduce_weight.astype(bf16)
    low_conv = conv_weight.astype(bf16)
    low_squeeze = squeeze_weight.astype(bf16)
    low_expand = expand_weight.astype(bf16)
    low_project = project_weight.astype(bf16)
    low_norm = norm_params.astype(bf16)
    devices = lax.axis_size("dp") * lax.axis_size("rep")
    per_batch = images.shape[0] // MICRO
    pixel_count = float(per_batch * SIDE * SIDE * devices)
    image_count = float(per_batch * devices)
    group_in = BOTTLE // RADIX
    grad_first = jnp.zeros((CHANNELS, BOTTLE), jnp.float32)
    grad_conv = jnp.zeros((RADIX, 9 * group_in, BOTTLE), jnp.float32)
    grad_squeeze = jnp.zeros((BOTTLE, INNER), jnp.float32)
    grad_expand = jnp.zeros((INNER, RADIX * BOTTLE), jnp.float32)
    grad_last = jnp.zeros((BOTTLE, CHANNELS), jnp.float32)
    grad_norms = jnp.zeros(
        (2 * BOTTLE + 3 * RADIX * BOTTLE + 2 * INNER + 2 * CHANNELS,), jnp.float32
    )
    outputs = []
    input_grads = []
    for number in range(MICRO):
        forward_set = (
            lax.all_gather(low_reduce, "dp", axis=0, tiled=True),
            lax.all_gather(low_conv, "dp", axis=0, tiled=True),
            lax.all_gather(low_squeeze, "dp", axis=0, tiled=True),
            lax.all_gather(low_expand, "dp", axis=0, tiled=True),
            lax.all_gather(low_project, "dp", axis=0, tiled=True),
            lax.all_gather(low_norm, "dp", axis=0, tiled=True),
        )
        first, conv, squeeze, expand, last, packed = forward_set
        (
            gain_one,
            bias_one,
            gain_two,
            bias_two,
            gain_pool,
            bias_pool,
            bias_expand,
            gain_three,
            bias_three,
        ) = split_params(packed.astype(jnp.float32))
        batched = images[number * per_batch : (number + 1) * per_batch]
        cotangent = out_grad[number * per_batch : (number + 1) * per_batch]
        reduced = jnp.einsum("nhwc,cb->nhwb", batched, first, preferred_element_type=jnp.float32)
        norm_one, normed_one, scale_one = norm_forward(reduced, gain_one, bias_one, pixel_count)
        active = jax.nn.silu(norm_one).astype(bf16)
        columns = patches(active.reshape(per_batch, SIDE, SIDE, RADIX, group_in)).reshape(
            per_batch * SIDE * SIDE, RADIX, 9 * group_in
        )
        conv_grouped = conv.reshape(RADIX, 9 * group_in, BOTTLE)
        widened = jnp.einsum(
            "prk,rko->pro", columns, conv_grouped, preferred_element_type=jnp.float32
        )
        widened = widened.reshape(per_batch, SIDE, SIDE, RADIX * BOTTLE)
        norm_two, normed_two, scale_two = norm_forward(widened, gain_two, bias_two, pixel_count)
        splits = jax.nn.silu(norm_two).reshape(per_batch, SIDE, SIDE, RADIX, BOTTLE)
        pooled = jnp.sum(jnp.sum(splits, axis=3), axis=(1, 2)) / (SIDE * SIDE)
        squeeze_float = squeeze.astype(jnp.float32)
        expand_float = expand.astype(jnp.float32)
        pre_pool = jnp.dot(pooled, squeeze_float, precision=PRECISE)
        norm_pool, normed_pool, scale_pool = norm_forward(
            pre_pool, gain_pool, bias_pool, image_count
        )
        hidden = jax.nn.silu(norm_pool)
        logits = (jnp.dot(hidden, expand_float, precision=PRECISE) + bias_expand).reshape(
            per_batch, RADIX, BOTTLE
        )
        attention = jax.nn.softmax(logits, axis=1)
        mixed = jnp.sum(splits * attention[:, None, None], axis=3).astype(bf16)
        projected = jnp.einsum("nhwb,bc->nhwc", mixed, last, preferred_element_type=jnp.float32)
        norm_three, normed_three, scale_three = norm_forward(
            projected, gain_three, bias_three, pixel_count
        )
        summed = batched.astype(jnp.float32) + norm_three
        outputs.append(jax.nn.silu(summed).astype(bf16))
        backward_set = (
            lax.all_gather(low_reduce, "dp", axis=0, tiled=True),
            lax.all_gather(low_conv, "dp", axis=0, tiled=True),
            lax.all_gather(low_squeeze, "dp", axis=0, tiled=True),
            lax.all_gather(low_expand, "dp", axis=0, tiled=True),
            lax.all_gather(low_project, "dp", axis=0, tiled=True),
            lax.all_gather(low_norm, "dp", axis=0, tiled=True),
        )
        first, conv, squeeze, expand, last, packed = backward_set
        gains_back = split_params(packed.astype(jnp.float32))
        conv_grouped = conv.reshape(RADIX, 9 * group_in, BOTTLE)
        expand_float = expand.astype(jnp.float32)
        squeeze_float = squeeze.astype(jnp.float32)
        upstream = cotangent.astype(jnp.float32) * silu_slope(summed)
        d_projected, gain_three_grad, bias_three_grad = norm_backward(
            upstream, normed_three, scale_three, gains_back[7], pixel_count
        )
        d_projected_low = d_projected.astype(bf16)
        grad_last = grad_last + jnp.einsum(
            "nhwb,nhwc->bc", mixed, d_projected_low, preferred_element_type=jnp.float32
        )
        d_mixed = jnp.einsum(
            "nhwc,bc->nhwb", d_projected_low, last, preferred_element_type=jnp.float32
        )
        d_splits = d_mixed[:, :, :, None] * attention[:, None, None]
        d_attention = jnp.sum(d_mixed[:, :, :, None] * splits, axis=(1, 2))
        d_logits = attention * (
            d_attention - jnp.sum(attention * d_attention, axis=1, keepdims=True)
        )
        flat_logits = d_logits.reshape(per_batch, RADIX * BOTTLE)
        grad_expand = grad_expand + jnp.dot(hidden.T, flat_logits, precision=PRECISE)
        d_hidden = jnp.dot(flat_logits, expand_float.T, precision=PRECISE)
        d_pool_norm = d_hidden * silu_slope(norm_pool)
        pool_bias_sum, pool_gain_sum, expand_bias_sum = lax.psum(
            (
                jnp.sum(d_pool_norm, axis=0),
                jnp.sum(d_pool_norm * normed_pool, axis=0),
                jnp.sum(flat_logits, axis=0),
            ),
            ("dp", "rep"),
        )
        d_pre_pool = (
            gains_back[4]
            * scale_pool
            * (
                d_pool_norm
                - pool_bias_sum / image_count
                - normed_pool * (pool_gain_sum / image_count)
            )
        )
        grad_squeeze = grad_squeeze + jnp.dot(pooled.T, d_pre_pool, precision=PRECISE)
        d_pooled = jnp.dot(d_pre_pool, squeeze_float.T, precision=PRECISE)
        d_splits = d_splits + (d_pooled / (SIDE * SIDE))[:, None, None, None, :]
        d_norm_two = d_splits.reshape(per_batch, SIDE, SIDE, RADIX * BOTTLE) * silu_slope(norm_two)
        d_widened, gain_two_grad, bias_two_grad = norm_backward(
            d_norm_two, normed_two, scale_two, gains_back[2], pixel_count
        )
        d_widened_low = d_widened.astype(bf16).reshape(per_batch * SIDE * SIDE, RADIX, BOTTLE)
        grad_conv = grad_conv + jnp.einsum(
            "prk,pro->rko", columns, d_widened_low, preferred_element_type=jnp.float32
        )
        d_columns = jnp.einsum(
            "pro,rko->prk", d_widened_low, conv_grouped, preferred_element_type=jnp.float32
        )
        d_active = unpatch(d_columns.reshape(per_batch, SIDE, SIDE, RADIX, 9, group_in)).reshape(
            per_batch, SIDE, SIDE, BOTTLE
        )
        d_norm_one = d_active * silu_slope(norm_one)
        d_reduced, gain_one_grad, bias_one_grad = norm_backward(
            d_norm_one, normed_one, scale_one, gains_back[0], pixel_count
        )
        d_reduced_low = d_reduced.astype(bf16)
        grad_first = grad_first + jnp.einsum(
            "nhwc,nhwb->cb", batched, d_reduced_low, preferred_element_type=jnp.float32
        )
        input_grads.append(
            upstream
            + jnp.einsum("nhwb,cb->nhwc", d_reduced_low, first, preferred_element_type=jnp.float32)
        )
        grad_norms = grad_norms + jnp.concatenate(
            [
                gain_one_grad,
                bias_one_grad,
                gain_two_grad,
                bias_two_grad,
                pool_gain_sum,
                pool_bias_sum,
                expand_bias_sum,
                gain_three_grad,
                bias_three_grad,
            ]
        )
    grad_conv = grad_conv.reshape(9 * BOTTLE, BOTTLE)
    partial_value = (
        lax.psum_scatter(grad_first, "dp", scatter_dimension=0, tiled=True),
        lax.psum_scatter(grad_conv, "dp", scatter_dimension=0, tiled=True),
        lax.psum_scatter(grad_squeeze, "dp", scatter_dimension=0, tiled=True),
        lax.psum_scatter(grad_expand, "dp", scatter_dimension=0, tiled=True),
        lax.psum_scatter(grad_last, "dp", scatter_dimension=0, tiled=True),
    )
    owned = lax.psum(
        (partial_value[0], partial_value[1], partial_value[2], partial_value[3], partial_value[4]),
        "rep",
    )
    shard_length = norm_params.shape[0]
    norm_grad_owned = lax.dynamic_slice_in_dim(
        grad_norms, lax.axis_index("dp") * shard_length, shard_length
    )
    reduce_new = adamw(
        reduce_weight, reduce_moment, reduce_second, owned[0], 2.0 * CHANNELS ** (-0.5), DECAY
    )
    conv_new = adamw(
        conv_weight,
        conv_moment,
        conv_second,
        owned[1],
        2.0 * (9 * BOTTLE // RADIX) ** (-0.5),
        DECAY,
    )
    squeeze_new = adamw(
        squeeze_weight, squeeze_moment, squeeze_second, owned[2], 2.0 * BOTTLE ** (-0.5), DECAY
    )
    expand_new = adamw(
        expand_weight, expand_moment, expand_second, owned[3], 2.0 * (INNER // 8) ** (-0.5), DECAY
    )
    project_new = adamw(
        project_weight, project_moment, project_second, owned[4], 2.0 * BOTTLE ** (-0.5), DECAY
    )
    norm_new = adamw(norm_params, norm_moment, norm_second, norm_grad_owned, NORM_RATE, 0.0)
    return (
        jnp.concatenate(outputs, axis=0),
        jnp.concatenate(input_grads, axis=0),
        reduce_new[0],
        reduce_new[1],
        reduce_new[2],
        conv_new[0],
        conv_new[1],
        conv_new[2],
        squeeze_new[0],
        squeeze_new[1],
        squeeze_new[2],
        expand_new[0],
        expand_new[1],
        expand_new[2],
        project_new[0],
        project_new[1],
        project_new[2],
        norm_new[0],
        norm_new[1],
        norm_new[2],
    )


MESH = pl.DeviceIdType.MESH
PAD = 64
CHUNK = 112
F32 = jnp.float32
BF16 = jnp.bfloat16
STATS = {
    "reduced": (8, 128),
    "widened0": (8, 128),
    "widened1": (8, 128),
    "pool": (8, 128),
    "images": (16, 128),
    "projected0": (8, 256),
    "projected1": (8, 256),
    "back_projected0": (8, 256),
    "back_projected1": (8, 256),
    "back_pool": (8, 128),
    "back_widened0": (8, 128),
    "back_widened1": (16, 128),
    "back_reduced0": (8, 128),
    "back_reduced1": (8, 128),
}
DIRECT = ("reduced", "pool", "back_pool")


def sigmoid(values):
    return 0.5 * jnp.tanh(0.5 * values) + 0.5


def row_ids(width):
    return lax.broadcasted_iota(jnp.int32, (8, width), 0)


def image_sum(rows):
    return rows + pltpu.roll(rows, 4, 0)


def pair_sum(rows):
    even = row_ids(rows.shape[1]) % 2 == 0
    return rows + jnp.where(even, pltpu.roll(rows, 7, 0), pltpu.roll(rows, 1, 0))


def micro_sum(rows):
    return pair_sum(image_sum(rows))


def stack_sums(first, second):
    return jnp.where(row_ids(first.shape[1]) < 4, first, second)


def unstack_sums(stacked):
    upper = row_ids(stacked.shape[1]) < 4
    turned = pltpu.roll(stacked, 4, 0)
    return jnp.where(upper, stacked, turned), jnp.where(upper, turned, stacked)


def fold_lanes(stacked):
    half = stacked.shape[1] // 2
    even = row_ids(half) % 2 == 0
    return jnp.where(even, stacked[:, :half], stacked[:, half:])


def unfold_lanes(folded):
    even = row_ids(folded.shape[1]) % 2 == 0
    left = jnp.where(even, folded, pltpu.roll(folded, 1, 0))
    right = jnp.where(even, pltpu.roll(folded, 7, 0), folded)
    return jnp.concatenate([left, right], axis=1)


def norm_terms(total, square, gain, bias, count):
    center = total * (1.0 / count)
    scale = lax.rsqrt(square * (1.0 / count) - center * center + EPSILON)
    slope = scale * gain
    return center, scale, slope, bias - center * slope


def back_terms(center, scale, slope, bias_sum, gain_sum, count):
    by_value = -slope * scale * (gain_sum * (1.0 / count))
    constant = -slope * (bias_sum * (1.0 / count)) - by_value * center
    return by_value, constant


def tdot(left, right):
    return lax.dot_general(left, right, (((0,), (0,)), ((), ())), preferred_element_type=F32)


def dot_t(left, right):
    return lax.dot_general(left, right, (((1,), (1,)), ((), ())), preferred_element_type=F32)


def in_parts(values, parts):
    found = []
    for _ in range(parts):
        rounded = values.astype(BF16).astype(F32)
        found.append(rounded)
        values = values - rounded
    return found


def exact_dot(left, right, transposed):
    stacked = jnp.concatenate(in_parts(left, 3), axis=0).astype(BF16)
    wide = dot_t(stacked, right) if transposed else jnp.dot(stacked, right, preferred_element_type=F32)
    return wide[0:8] + wide[8:16] + wide[16:24]


def row_dot(left, right):
    high, low = in_parts(left, 2)
    other_high, other_low = in_parts(right, 2)
    return tdot(
        jnp.concatenate([high, high, low, low], axis=0).astype(BF16),
        jnp.concatenate([other_high, other_low, other_high, other_low], axis=0).astype(BF16),
    )


def image_dot(left, right):
    return row_dot(jnp.where(row_ids(left.shape[1]) < 4, left, 0.0), right)


def block_kernel(
    n_dp,
    n_rep,
    x_hbm,
    gy_hbm,
    w1_hbm,
    wc_hbm,
    sq_hbm,
    ex_hbm,
    w3_hbm,
    np_hbm,
    bo_hbm,
    dx_hbm,
    f1_hbm,
    fc_hbm,
    f3_hbm,
    fe_hbm,
    gn_hbm,
    w1_own,
    wc_own,
    sq_own,
    ex_own,
    w3_own,
    np_own,
    gn_out,
    x4,
    gy4,
    x_v,
    gy_v,
    fw1,
    fwc,
    fes,
    fw3,
    es_own,
    np_slots,
    np_full,
    red,
    act,
    columns,
    wid,
    splits,
    mixed,
    proj,
    up,
    bo4,
    dx4,
    dproj,
    d_mixed,
    dn2,
    dwid,
    dcol,
    dn1,
    dred,
    g1,
    gc,
    g3,
    ge,
    gb,
    fix,
    back_own,
    *rest,
):
    n_ar = len(STATS)
    order = {name: k for k, name in enumerate(STATS)}
    ar_slots_a = dict(zip(STATS, rest[0:n_ar]))
    ar_slots_b = dict(zip(STATS, rest[n_ar : 2 * n_ar]))
    rest = rest[2 * n_ar :]
    r1s, ys, r2s, ks, r3s, own = (rest[6 * i : 6 * i + 6] for i in range(6))
    fs = rest[36:40]
    rest = rest[40:]
    local_sem, ar_send_a, ar_recv_a, ar_send_b, ar_recv_b, np_sems, ws, wr, gs, gr = rest

    dp = lax.axis_index("dp")
    rep = lax.axis_index("rep")
    core = lax.rem(rep, 2)
    half_y = lax.div(rep, 2)
    planes = n_dp // 2
    plane_size = 2 * n_rep
    plane = lax.div(dp, 2)
    in_plane = lax.rem(dp, 2) * n_rep + rep
    sibling = (dp, half_y * 2 + (1 - core))
    across = (dp, (1 - half_y) * 2 + core)
    pixels = float(SIDE * SIDE * 2 * n_dp * n_rep)
    pictures = float(2 * n_dp * n_rep)

    x = lax.rem(dp, 2)
    if planes == 4:
        upper = lax.div(plane, 2)
        other_planes = [3 - 3 * upper, 2 - upper, 1 - plane + 4 * upper]
    else:
        other_planes = [lax.rem(plane + step, planes) for step in range(1, planes)]
    flips = ((1, 1, 1), (1, 1, 0), (1, 0, 1), (1, 0, 0), (0, 1, 1), (0, 1, 0), (0, 0, 1), (0, 0, 0))

    def of_flip(z, flip):
        there = [1 - own if turn else own for own, turn in zip((x, half_y, core), flip)]
        return (z * 2 + there[0], there[1] * 2 + there[2])

    plane_peers = [of_flip(plane, flip) for flip in flips[:-1]]
    column_peers = [of_flip(z, flips[-1]) for z in other_planes]
    owner_peers = [of_flip(z, flip) for z in other_planes for flip in (flips[3], flips[7])]
    owner_peers += [of_flip(plane, flips[3])]
    all_peers = [of_flip(z, flip) for z in other_planes for flip in flips] + plane_peers
    me, everyone = dp * n_rep + rep, n_dp * n_rep
    rep_peers = [(dp, lax.rem(rep + step, n_rep)) for step in range(1, n_rep)]

    def remote(src, dst, send_sem, recv_sem, device):
        return pltpu.make_async_remote_copy(
            src_ref=src,
            dst_ref=dst,
            send_sem=send_sem,
            recv_sem=recv_sem,
            device_id=device,
            device_id_type=MESH,
        )

    def send_all(ref, send_sem, recv_sem, peers):
        for device in peers:
            remote(ref, ref, send_sem, recv_sem, device).start()

    def wait_bytes(ref, sem):
        pltpu.make_async_copy(ref, ref, sem).wait()

    def over_rows(body, init):
        def step(index, carry):
            return body(pl.multiple_of(index * CHUNK, CHUNK), carry)

        return lax.fori_loop(0, ROWS // CHUNK, step, init)

    def grouped(values):
        return values.reshape(CHUNK // 8, 8, values.shape[-1])

    def by_four(values):
        return flat(values).reshape(CHUNK // 4, 4, values.shape[-1])

    def flat(values):
        return values.reshape(CHUNK, values.shape[-1])

    own_copies = [
        pltpu.make_async_copy(source, target, local_sem.at[4 + k])
        for k, (source, target) in enumerate(
            (
                (w1_hbm, w1_own),
                (np_hbm, np_own),
                (wc_hbm, wc_own),
                (w3_hbm, w3_own),
                (sq_hbm, sq_own),
                (ex_hbm, ex_own),
            )
        )
    ]
    for copy in own_copies:
        copy.start()
    x_copy = pltpu.make_async_copy(x_hbm, x4, local_sem.at[0])
    gy_copy = pltpu.make_async_copy(gy_hbm, gy4, local_sem.at[1])
    x_copy.start()
    barrier = pltpu.get_barrier_semaphore()
    for device in all_peers:
        pl.semaphore_signal(barrier, inc=1, device_id=device, device_id_type=MESH)

    part = core * 2 + half_y
    own_copies[0].wait()
    q1 = w1_own.shape[0] // 4
    fw1[dp, core, half_y] = w1_own[pl.ds(pl.multiple_of(part * q1, q1), q1), :].astype(BF16)
    core_lanes = pl.ds(pl.multiple_of(core * 128, 128), 128)
    es_lanes = pl.ds(pl.multiple_of(part * 128, 128), 128)
    w3_lanes = pl.ds(pl.multiple_of(part * 256, 128), 256)

    pl.semaphore_wait(barrier, everyone - 1)

    def quarter_w1(c, y):
        return fw1.at[:, c, y]

    def quarter_wc(c, y):
        return fwc.at[:, y, :, pl.ds(pl.multiple_of(c * 128, 128), 128)]

    def quarter_es(c, y):
        return fes.at[:, :, pl.ds(pl.multiple_of((c * 2 + y) * 128, 128), 128)]

    def quarter_w3(c, y):
        return fw3.at[:, :, pl.ds(pl.multiple_of((c * 2 + y) * 256, 128), 256)]

    quarters = (quarter_w1, quarter_wc, quarter_es, quarter_w3)

    def piece(which, d):
        return (
            fw1.at[d, core, half_y],
            fwc.at[d, half_y, :, core_lanes],
            fes.at[d, :, es_lanes],
            fw3.at[d, :, w3_lanes],
        )[which]

    def seven(which):
        return (
            fw1.at[pl.ds(0, n_dp - 1), core, half_y],
            fwc.at[pl.ds(0, n_dp - 1), half_y, :, core_lanes],
            fes.at[pl.ds(0, n_dp - 1), :, es_lanes],
            fw3.at[pl.ds(0, n_dp - 1), :, w3_lanes],
        )[which]

    def gather_out(which):
        send_all(piece(which, dp), ws.at[which, 0], wr.at[which, 0], owner_peers)

    def gather_turn(which):
        wait_bytes(seven(which), wr.at[which, 0])
        mine = quarters[which](core, half_y)
        remote(mine, mine, ws.at[which, 1], wr.at[which, 1], across).start()
        remote(mine, mine, ws.at[which, 2], wr.at[which, 2], sibling).start()

    def gather_hand(which):
        theirs = quarters[which](core, 1 - half_y)
        wait_bytes(theirs, wr.at[which, 1])
        remote(theirs, theirs, ws.at[which, 3], wr.at[which, 3], sibling).start()

    def gather_end(which):
        wait_bytes(quarters[which](1 - core, half_y), wr.at[which, 2])
        wait_bytes(quarters[which](1 - core, 1 - half_y), wr.at[which, 3])

    def to_rows(source, target):
        def body(index, carry):
            values = source[pl.ds(index * (CHUNK // 4), CHUNK // 4)].astype(F32)
            row = pl.multiple_of(index * CHUNK, CHUNK)
            target[pl.ds(row, CHUNK), :] = values.reshape(CHUNK, CHANNELS).astype(BF16)
            return carry

        lax.fori_loop(0, ROWS // CHUNK, body, 0)

    gather_out(0)
    own_copies[2].wait()
    qc = wc_own.shape[0] // 2
    fwc[dp, half_y, :, core_lanes] = wc_own[
        pl.ds(pl.multiple_of(half_y * qc, qc), qc), core_lanes
    ].astype(BF16)
    gather_out(1)

    own_copies[1].wait()
    shard = np_own.shape[0]
    lanes_id = lax.broadcasted_iota(jnp.int32, (8, 128), 1)
    turn = lax.rem(shard * dp, 128)
    np_rows = []
    for at in range(0, shard, 128):
        width = min(128, shard - at)
        piece_row = np_own[pl.ds(at, width)].reshape(1, width)
        if width < 128:
            piece_row = jnp.concatenate([piece_row, jnp.zeros((1, 128 - width), F32)], axis=1)
        np_rows.append(piece_row)
    np_rows.append(jnp.zeros((8 - len(np_rows), 128), F32))
    np_turned = jnp.concatenate(np_rows, axis=0).astype(BF16).astype(F32)
    np_turned = pltpu.roll(np_turned, turn, 1)
    np_slots[dp] = jnp.where(lanes_id < turn, pltpu.roll(np_turned, 1, 0), np_turned)
    send_all(np_slots.at[dp], np_sems.at[0], np_sems.at[1], owner_peers)
    for copy in own_copies[3:]:
        copy.wait()
    ex_rows = ex_own.shape[0]
    es_own[:, 0:128] = sq_own[...].astype(BF16)
    es_own[0:ex_rows, 128:384] = ex_own[:, 0:256].astype(BF16)
    es_own[ex_rows : 2 * ex_rows, 128:384] = ex_own[:, 256:512].astype(BF16)
    es_own[:, 384:512] = jnp.zeros((2 * ex_rows, 128), BF16)
    fes[dp, :, es_lanes] = es_own[:, es_lanes]
    fw3[dp, :, w3_lanes] = w3_own[:, w3_lanes].astype(BF16)
    gy_copy.start()
    x_copy.wait()
    to_rows(x4, x_v)
    gather_turn(0)
    zero_rows = jnp.zeros((PAD, BOTTLE), F32)
    for side in range(3):
        act[side, 0:PAD, :] = zero_rows
        act[side, PAD + ROWS : 2 * PAD + ROWS, :] = zero_rows
    for lane_block in range(9):
        dcol[0:PAD, lane_block * 256 : lane_block * 256 + 256] = zero_rows
        dcol[PAD + ROWS : 2 * PAD + ROWS, lane_block * 256 : lane_block * 256 + 256] = zero_rows
    gather_hand(0)
    gather_out(2)
    gather_out(3)
    gather_turn(1)

    def sum_start(k, payload):
        if k in DIRECT:
            ar_slots_a[k][me] = payload
            send_all(ar_slots_a[k].at[me], ar_send_a.at[order[k]], ar_recv_a.at[order[k]], all_peers)
        else:
            ar_slots_a[k][in_plane] = payload
            send_all(ar_slots_a[k].at[in_plane], ar_send_a.at[order[k]], ar_recv_a.at[order[k]], plane_peers)

    def sum_slots(slots, count):
        sums = [slots[slot] for slot in range(count)]
        while len(sums) > 1:
            sums = [sums[i] + sums[i + 1] for i in range(0, len(sums), 2)]
        return sums[0]

    def sum_turn(k):
        if k in DIRECT:
            return
        wait_bytes(ar_slots_a[k].at[pl.ds(0, plane_size - 1)], ar_recv_a.at[order[k]])
        ar_slots_b[k][plane] = sum_slots(ar_slots_a[k], plane_size)
        send_all(ar_slots_b[k].at[plane], ar_send_b.at[order[k]], ar_recv_b.at[order[k]], column_peers)

    def sum_end(k):
        if k in DIRECT:
            wait_bytes(ar_slots_a[k].at[pl.ds(0, everyone - 1)], ar_recv_a.at[order[k]])
            return sum_slots(ar_slots_a[k], everyone)
        wait_bytes(ar_slots_b[k].at[pl.ds(0, planes - 1)], ar_recv_b.at[order[k]])
        return sum_slots(ar_slots_b[k], planes)

    def lanes_of(index, width):
        return pl.ds(pl.multiple_of(index * width, 128), width)

    cut = 64
    conv_rows = {1: pl.ds(0, cut), 2: pl.ds(cut, gc.shape[2] - cut)}
    grads = (g1, gc, gc, g3, ge, gb)
    turned_kinds = (0, 5)

    def half_of(which, c):
        ref = grads[which]
        if which in turned_kinds:
            return ref.at[c]
        if which in conv_rows:
            return ref.at[:, :, conv_rows[which], lanes_of(c, 128)]
        return ref.at[:, :, lanes_of(c, (512, 256)[which - 3])]

    def y_part(which, ref, y):
        if which in turned_kinds:
            return ref.at[y]
        if which < 3:
            return ref.at[:, y]
        return ref.at[:, :, lanes_of(y, (256, 128)[which - 3])]

    def quarter_of(which, c, y):
        ref = grads[which]
        if which in turned_kinds:
            return ref.at[c, y]
        if which in conv_rows:
            return ref.at[:, y, conv_rows[which], lanes_of(c, 128)]
        return ref.at[:, :, lanes_of(c * 2 + y, (256, 128)[which - 3])]

    def final_part(which, c, y):
        if which == 0:
            return fs[0].at[c, y]
        if which in conv_rows:
            return fs[1].at[y, conv_rows[which], lanes_of(c, 128)]
        return fs[which - 1].at[:, lanes_of(c * 2 + y, (256, 128)[which - 3])]

    def of_owner(which, ref, d):
        return ref.at[:, lanes_of(d, CHANNELS // n_dp)] if which in turned_kinds else ref.at[d]

    def in_blocks(which, body):
        if which in turned_kinds:
            count = 4
            rows = grads[which].shape[2] // count
            block = lambda index: pl.ds(pl.multiple_of(index * rows, rows), rows)
        else:
            count, block = n_dp, lambda index: index

        def step(index, carry):
            body(block(index))
            return carry

        lax.fori_loop(0, count, step, 0)

    def reduce_core(which):
        remote(
            half_of(which, 1 - core), r1s[which], gs.at[which, 0], gr.at[which, 0], sibling
        ).start()

    def reduce_y(which):
        wait_bytes(r1s[which], gr.at[which, 0])
        away = quarter_of(which, core, 1 - half_y)
        mine = quarter_of(which, core, half_y)
        there = y_part(which, r1s[which], 1 - half_y)
        here = y_part(which, r1s[which], half_y)

        def add_away(at):
            ys[which][at] = (away[at].astype(F32) + there[at].astype(F32)).astype(
                ys[which].dtype
            )

        in_blocks(which, add_away)
        remote(ys[which], r2s[which], gs.at[which, 1], gr.at[which, 1], across).start()

        def add_mine(at):
            mine[at] = (mine[at].astype(F32) + here[at].astype(F32)).astype(mine.dtype)

        in_blocks(which, add_mine)

    def reduce_owner(which):
        wait_bytes(r2s[which], gr.at[which, 1])
        mine = quarter_of(which, core, half_y)

        def add(at):
            ks[which][at] = (mine[at].astype(F32) + r2s[which][at].astype(F32)).astype(
                ks[which].dtype
            )

        in_blocks(which, add)
        for device in owner_peers:
            remote(
                of_owner(which, ks[which], device[0]),
                r3s[which].at[dp],
                gs.at[which, 2],
                gr.at[which, 2],
                device,
            ).start()
        own[which][...] = of_owner(which, mine, dp)[...].astype(F32) + of_owner(
            which, r2s[which], dp
        )[...].astype(F32)
        r3s[which][dp] = jnp.zeros(own[which].shape, r3s[which].dtype)

    def owner_total(which):
        wait_bytes(r3s[which].at[pl.ds(0, n_dp - 1)], gr.at[which, 2])
        total = own[which][...]
        for slot in range(n_dp):
            total = total + r3s[which][slot].astype(F32)
        return total

    def reduce_spread(which):
        total = owner_total(which)
        if which == 0:
            rows = pl.ds(pl.multiple_of(part * (BOTTLE // 4), BOTTLE // 4), BOTTLE // 4)
            total = total - fix[0, rows, :]
            for m in range(2):
                total = total - fix[1 + m, rows, :] * back_own[m]
        mine = final_part(which, core, half_y)
        mine[...] = total
        send_all(mine, gs.at[which, 3], gr.at[which, 3], rep_peers)

    def three_parts(which):
        if which == 0:
            return r1s[0].at[0, :, pl.ds(0, 3 * CHANNELS // n_dp)]
        return r1s[which].at[pl.ds(0, 3), 0] if which < 3 else y_part(which, r1s[which], 0).at[pl.ds(0, 3)]

    def reduce_end(which):
        wait_bytes(three_parts(which), gr.at[which, 3])

    gather_end(0)
    red[...] = jnp.dot(x_v[...], fw1[...].reshape(CHANNELS, BOTTLE), preferred_element_type=F32)

    def sums_of(ref, start, width):
        def body(row, carry):
            values = grouped(ref[pl.ds(row, CHUNK), start : start + width])
            return carry[0] + jnp.sum(values, axis=0), carry[1] + jnp.sum(values * values, axis=0)

        zero = jnp.zeros((8, width), F32)
        return over_rows(body, (zero, zero))

    def joined(found):
        both = [jnp.concatenate(item, axis=1) for item in zip(*found)]
        return fold_lanes(stack_sums(micro_sum(both[0]), micro_sum(both[1])))

    def both_sums(name):
        return unstack_sums(unfold_lanes(sum_end(name)))

    sum_start("reduced", joined([sums_of(red, 0, 256)]))
    gather_turn(2)

    gy_copy.wait()
    to_rows(gy4, gy_v)
    wait_bytes(np_slots.at[pl.ds(0, n_dp - 1)], np_sems.at[1])
    np_full[...] = jnp.zeros(np_full.shape, F32)
    for d in range(n_dp):
        at = shard * d // 128
        np_full[at : at + 8, :] = np_full[at : at + 8, :] + np_slots[d]

    def vector(at, width):
        rows = [np_full[at // 128 + k : at // 128 + k + 1, :] for k in range(width // 128)]
        return jnp.concatenate(rows, axis=1) if len(rows) > 1 else rows[0]

    gain_one, bias_one = vector(0, 256), vector(256, 256)
    gain_two, bias_two = vector(512, 512), vector(1024, 512)
    gain_pool, bias_pool = vector(1536, 128), vector(1664, 128)
    bias_expand = vector(1792, 512)
    gain_three, bias_three = vector(2304, 1024), vector(3328, 1024)

    total, square = both_sums("reduced")
    center1, scale1, mul1, add1 = norm_terms(total, square, gain_one, bias_one, pixels)

    def make_active(row, carry):
        turned = grouped(red[pl.ds(row, CHUNK), :]) * mul1 + add1
        act[1, pl.ds(PAD + row, CHUNK), :] = flat(turned * sigmoid(turned))
        return carry

    over_rows(make_active, 0)
    gather_hand(1)
    gather_hand(2)
    gather_turn(3)
    place = lax.rem(lax.broadcasted_iota(jnp.int32, (CHUNK, BOTTLE), 0) // 4, SIDE)
    not_last = place != SIDE - 1
    not_first = place != 0

    def beside(side, row, distance, lanes=slice(0, BOTTLE)):
        near = act[side, pl.ds(PAD + row - 8, CHUNK + 16), lanes]
        return pltpu.roll(near, (CHUNK + 16 - distance) % (CHUNK + 16), 0)[8 : 8 + CHUNK]

    def shift_active(row, carry):
        act[2, pl.ds(PAD + row, CHUNK), :] = jnp.where(not_last, beside(1, row, 4), 0.0)
        act[0, pl.ds(PAD + row, CHUNK), :] = jnp.where(not_first, beside(1, row, -4), 0.0)
        return carry

    over_rows(shift_active, 0)

    def make_columns(row, carry):
        for tap in range(9):
            down, side = tap // 3 - 1, tap % 3
            values = act[side, pl.ds(PAD + row + 56 * down, CHUNK), :].astype(BF16)
            columns[0, pl.ds(row, CHUNK), tap * 128 : tap * 128 + 128] = values[:, 0:128]
            columns[1, pl.ds(row, CHUNK), tap * 128 : tap * 128 + 128] = values[:, 128:256]
        return carry

    over_rows(make_columns, 0)
    gather_end(1)
    own_half = n_dp // 2

    def filters(group):
        return fwc[group * own_half : (group + 1) * own_half].reshape(9 * 128, BOTTLE)

    halves2 = (slice(0, 256), slice(256, 512))
    for group, lanes in enumerate(halves2):
        wid[:, lanes] = jnp.dot(columns[group], filters(group), preferred_element_type=F32)
        sum_start(f"widened{group}", joined([sums_of(wid, group * 256, 256)]))
    sum_turn("widened0")
    sum_turn("widened1")
    gather_hand(3)

    norm2 = []
    pooled = jnp.zeros((8, BOTTLE), F32)
    for group, lanes in enumerate(halves2):
        total, square = both_sums(f"widened{group}")
        norm2.append(norm_terms(total, square, gain_two[:, lanes], bias_two[:, lanes], pixels))
        m2, a2 = norm2[group][2:4]

        def make_splits(row, carry):
            turned = grouped(wid[pl.ds(row, CHUNK), lanes]) * m2 + a2
            values = turned * sigmoid(turned)
            splits[pl.ds(row, CHUNK), lanes] = flat(values)
            return carry + jnp.sum(values, axis=0)

        pooled = over_rows(make_splits, pooled)
    pooled = image_sum(pooled) * (1.0 / (SIDE * SIDE))
    gather_end(2)
    squeeze = fes[:, :, 0:128].reshape(BOTTLE, INNER)
    ex_both = fes[:, :, 128:384]
    expand = jnp.concatenate(
        [
            ex_both[:, 0:ex_rows].reshape(INNER, 256),
            ex_both[:, ex_rows : 2 * ex_rows].reshape(INNER, 256),
        ],
        axis=1,
    )
    pre_pool = exact_dot(pooled, squeeze, False)
    sum_start("pool", stack_sums(pair_sum(pre_pool), pair_sum(pre_pool * pre_pool)))
    first_micro = lax.rem(row_ids(BOTTLE), 4) < 2

    def make_normed(row, carry):
        rows = pl.ds(row, CHUNK)
        normed = (grouped(red[rows, :]) - center1) * scale1
        dwid[rows, 0:256] = flat(jnp.where(first_micro, normed, 0.0)).astype(BF16)
        dwid[rows, 256:512] = flat(jnp.where(first_micro, 0.0, normed)).astype(BF16)
        return carry + jnp.sum(grouped(x_v[rows, :].astype(F32)), axis=0)

    image_sums = micro_sum(over_rows(make_normed, jnp.zeros((8, CHANNELS), F32)))
    sum_start(
        "images",
        jnp.concatenate(
            [
                image_sums[2 * m : 2 * m + 1, at : at + 128]
                for m in range(2)
                for at in range(0, CHANNELS, 128)
            ],
            axis=0,
        ),
    )
    normed_images = tdot(dwid[...], x_v[...]).astype(BF16)
    normed_images = normed_images.reshape(2, 2, 2, BOTTLE // 4, CHANNELS)
    for m in range(2):
        gb[:, :, m * (BOTTLE // 4) : (m + 1) * (BOTTLE // 4)] = normed_images[m]
    reduce_core(5)
    total, square = unstack_sums(sum_end("pool"))
    center_p, scale_p, mul_p, add_p = norm_terms(total, square, gain_pool, bias_pool, pictures)
    normed_p = (pre_pool - center_p) * scale_p
    norm_p = pre_pool * mul_p + add_p
    gate_p = sigmoid(norm_p)
    hidden = norm_p * gate_p
    slope_p = gate_p * (1.0 + norm_p * (1.0 - gate_p))
    logits = exact_dot(hidden, expand, False) + bias_expand
    left, right = logits[:, 0:256], logits[:, 256:512]
    most = jnp.maximum(left, right)
    left, right = jnp.exp(left - most), jnp.exp(right - most)
    att0 = left / (left + right)
    att1 = right / (left + right)

    gather_end(3)
    last = fw3[...].reshape(BOTTLE, CHANNELS)
    def make_mixed(row, carry):
        rows = pl.ds(row, CHUNK)
        values = grouped(splits[rows, 0:256]) * att0 + grouped(splits[rows, 256:512]) * att1
        mixed[rows, :] = flat(values).astype(BF16)
        return carry

    over_rows(make_mixed, 0)
    halves3 = (slice(0, 512), slice(512, 1024))
    blocks3 = [[slice(512 * h + k, 512 * h + k + 256) for k in (0, 256)] for h in range(2)]
    for half, lanes in enumerate(halves3):
        proj[:, lanes] = jnp.dot(mixed[...], last[:, lanes], preferred_element_type=F32)
        sum_start(
            f"projected{half}", joined([sums_of(proj, 512 * half + k, 256) for k in (0, 256)])
        )
    sum_turn("projected0")
    sum_turn("projected1")
    sum_turn("images")
    reduce_y(5)

    norm3 = []
    zero = jnp.zeros((8, 256), F32)
    for half, lanes in enumerate(halves3):
        total, square = both_sums(f"projected{half}")
        norm3.append(norm_terms(total, square, gain_three[:, lanes], bias_three[:, lanes], pixels))
        found = []
        for k, block in enumerate(blocks3[half]):
            c3, s3, m3, a3 = (item[:, k * 256 : k * 256 + 256] for item in norm3[half])

            def make_out(row, carry):
                rows = pl.ds(row, CHUNK)
                values = grouped(proj[rows, block])
                summed = grouped(x_v[rows, block].astype(F32)) + (values * m3 + a3)
                gate = sigmoid(summed)
                bo4[pl.ds(row // 4, CHUNK // 4), :, block] = by_four(summed * gate).astype(BF16)
                upstream = grouped(gy_v[rows, block].astype(F32)) * (
                    gate * (1.0 + summed * (1.0 - gate))
                )
                up[rows, block] = flat(upstream)
                normed = (values - c3) * s3
                return carry[0] + jnp.sum(upstream, axis=0), carry[1] + jnp.sum(
                    upstream * normed, axis=0
                )

            found.append(over_rows(make_out, (zero, zero)))
        sum_start(f"back_projected{half}", joined(found))
    bo_copy = pltpu.make_async_copy(bo4, bo_hbm, local_sem.at[2])
    bo_copy.start()

    def write_norm(at, pattern):
        at = at // 128
        both = pattern[0:1, :] + pattern[2:3, :]
        for k in range(both.shape[1] // 128):
            np_full[at + k : at + k + 1, :] = both[:, k * 128 : k * 128 + 128]

    sum_turn("back_projected0")
    sum_turn("back_projected1")
    reduce_owner(5)

    for half, lanes in enumerate(halves3):
        bias_sum, gain_sum = both_sums(f"back_projected{half}")
        write_norm(2304 + 512 * half, gain_sum)
        write_norm(3328 + 512 * half, bias_sum)
        by_value, constant = back_terms(*norm3[half][0:3], bias_sum, gain_sum, pixels)
        for k, block in enumerate(blocks3[half]):
            m3, v3, k3 = (
                item[:, k * 256 : k * 256 + 256] for item in (norm3[half][2], by_value, constant)
            )

            def make_dproj(row, carry):
                rows = pl.ds(row, CHUNK)
                values = grouped(up[rows, block]) * m3 + grouped(proj[rows, block]) * v3 + k3
                dproj[rows, block] = flat(values).astype(BF16)
                return carry

            over_rows(make_dproj, 0)
        part_mixed = dot_t(dproj[:, lanes], last[:, lanes])
        d_mixed[...] = part_mixed if half == 0 else d_mixed[...] + part_mixed

    def attend(row, carry):
        rows = pl.ds(row, CHUNK)
        values = grouped(d_mixed[rows, :])
        return (
            carry[0] + jnp.sum(values * grouped(splits[rows, 0:256]), axis=0),
            carry[1] + jnp.sum(values * grouped(splits[rows, 256:512]), axis=0),
        )

    d_att0, d_att1 = over_rows(attend, (zero, zero))
    d_att0, d_att1 = image_sum(d_att0), image_sum(d_att1)
    both = att0 * d_att0 + att1 * d_att1
    d_logits = jnp.concatenate([att0 * (d_att0 - both), att1 * (d_att1 - both)], axis=1)
    d_hidden = exact_dot(d_logits, expand, True)
    d_pool = d_hidden * slope_p
    per_micro = stack_sums(pair_sum(d_pool), pair_sum(d_pool * normed_p))
    sum_start("back_pool", per_micro)
    ex_sum = pair_sum(d_logits)
    ex_sum = ex_sum + pltpu.roll(ex_sum, 2, 0)
    ex_rows_sum = ex_sum[:, 0:128]
    for k in range(1, 4):
        ex_rows_sum = jnp.where(row_ids(128) == k, ex_sum[:, k * 128 : k * 128 + 128], ex_rows_sum)

    grad_ex = image_dot(hidden, d_logits)
    grad_ex = grad_ex.reshape(n_dp, ex_rows, 512)
    ge[:, 0:ex_rows, 128:384] = grad_ex[:, :, 0:256]
    ge[:, ex_rows : 2 * ex_rows, 128:384] = grad_ex[:, :, 256:512]
    ge[:, :, 384:512] = jnp.zeros((n_dp, 2 * ex_rows, 128), F32)
    g3[...] = tdot(mixed[...], dproj[...]).reshape(g3.shape)
    reduce_core(3)
    held = []
    for group, att in ((0, att0), (1, att1)):
        lanes = halves2[group]
        c2, s2, m2, a2 = norm2[group]

        def make_dn2(row, carry):
            rows = pl.ds(row, CHUNK)
            values = grouped(wid[rows, lanes])
            turned = values * m2 + a2
            gate = sigmoid(turned)
            slope = gate * (1.0 + turned * (1.0 - gate))
            down = grouped(d_mixed[rows, :]) * att * slope
            dn2[rows, lanes] = flat(down)
            splits[rows, lanes] = flat(slope)
            normed = (values - c2) * s2
            terms = (down, down * normed, slope, slope * normed)
            return tuple(item + jnp.sum(term, axis=0) for item, term in zip(carry, terms))

        held.append([image_sum(item) for item in over_rows(make_dn2, (zero,) * 4)])
    pool_bias_sum, pool_gain_sum = unstack_sums(sum_end("back_pool"))
    write_norm(1536, pool_gain_sum)
    write_norm(1664, pool_bias_sum)
    d_pre_pool = mul_p * (
        d_pool - pool_bias_sum * (1.0 / pictures) - normed_p * (pool_gain_sum * (1.0 / pictures))
    )
    d_pooled = exact_dot(d_pre_pool, squeeze, True) * (1.0 / (SIDE * SIDE))
    for group in range(2):
        down, down_normed, slope, slope_normed = held[group]
        payload = fold_lanes(
            stack_sums(
                pair_sum(down + d_pooled * slope), pair_sum(down_normed + d_pooled * slope_normed)
            )
        )
        if group == 1:
            payload = jnp.concatenate([payload, ex_rows_sum], axis=0)
        sum_start(f"back_widened{group}", payload)
    ge[:, :, 0:128] = image_dot(pooled, d_pre_pool).reshape(n_dp, 2 * ex_rows, 128)
    reduce_core(4)
    sum_turn("back_widened0")
    sum_turn("back_widened1")
    reduce_y(3)
    reduce_y(4)
    back_total = owner_total(5)
    back_own[0] = back_total[0 : BOTTLE // 4]
    back_own[1] = back_total[BOTTLE // 4 :]

    small_zero = jnp.zeros((8, 128), F32)
    for group, lanes in enumerate(halves2):
        whole = sum_end(f"back_widened{group}")
        if group == 1:
            np_full[14:18, :] = whole[8:12]
        bias_sum, gain_sum = unstack_sums(unfold_lanes(whole[0:8]))
        write_norm(512 + 256 * group, gain_sum)
        write_norm(1024 + 256 * group, bias_sum)
        m2 = norm2[group][2]
        v2, k2 = back_terms(*norm2[group][0:3], bias_sum, gain_sum, pixels)
        pooled_m2 = d_pooled * m2

        def make_dwid(row, carry):
            rows = pl.ds(row, CHUNK)
            values = grouped(dn2[rows, lanes]) * m2 + grouped(splits[rows, lanes]) * pooled_m2
            values = values + grouped(wid[rows, lanes]) * v2 + k2
            dwid[rows, lanes] = flat(values).astype(BF16)
            return carry

        over_rows(make_dwid, 0)
        gc[group * own_half : (group + 1) * own_half] = tdot(
            columns[group], dwid[:, lanes]
        ).reshape(own_half, 2, 9 * 128 // own_half // 2, BOTTLE)
    reduce_core(1)
    reduce_core(2)
    for group, lanes in enumerate(halves2):
        dcol[PAD : PAD + ROWS, group * 1152 : group * 1152 + 1152] = dot_t(
            dwid[:, lanes], filters(group)
        )
        inner = slice(group * 128, group * 128 + 128)

        def gather_taps(row, carry):
            for side in range(3):
                total = None
                for down in range(3):
                    at = group * 1152 + (3 * down + side) * 128
                    values = dcol[pl.ds(PAD + row - 56 * (down - 1), CHUNK), at : at + 128]
                    total = values if total is None else total + values
                act[side, pl.ds(PAD + row, CHUNK), inner] = total
            return carry

        over_rows(gather_taps, 0)
        c1, s1, m1, a1 = (item[:, inner] for item in (center1, scale1, mul1, add1))
        not_first1, not_last1 = not_first[:, inner], not_last[:, inner]

        def make_dn1(row, carry):
            rows = pl.ds(row, CHUNK)
            d_active = act[1, pl.ds(PAD + row, CHUNK), inner]
            d_active = d_active + jnp.where(not_first1, beside(2, row, -4, inner), 0.0)
            d_active = d_active + jnp.where(not_last1, beside(0, row, 4, inner), 0.0)
            values = grouped(red[rows, inner])
            turned = values * m1 + a1
            gate = sigmoid(turned)
            slope = gate * (1.0 + turned * (1.0 - gate))
            down = grouped(d_active) * slope
            dn1[rows, inner] = flat(down)
            mixed[rows, inner] = flat(down * m1).astype(BF16)
            normed = (values - c1) * s1
            return carry[0] + jnp.sum(down, axis=0), carry[1] + jnp.sum(down * normed, axis=0)

        bias_sum, gain_sum = over_rows(make_dn1, (small_zero, small_zero))
        sum_start(f"back_reduced{group}", stack_sums(micro_sum(bias_sum), micro_sum(gain_sum)))
        if group == 0:
            reduce_owner(3)
            reduce_owner(4)
            reduce_y(1)
    reduce_y(2)
    sum_turn("back_reduced0")
    sum_turn("back_reduced1")
    g1[...] = tdot(mixed[...], x_v[...]).reshape(g1.shape)
    reduce_core(0)
    found = [unstack_sums(sum_end(f"back_reduced{group}")) for group in range(2)]
    bias_sum, gain_sum = (jnp.concatenate(item, axis=1) for item in zip(*found))
    write_norm(0, gain_sum)
    write_norm(256, bias_sum)
    by_value, constant = back_terms(center1, scale1, mul1, bias_sum, gain_sum, pixels)
    def make_dred(row, carry):
        rows = pl.ds(row, CHUNK)
        values = grouped(dn1[rows, :]) * mul1 + grouped(red[rows, :]) * by_value + constant
        dred[rows, :] = flat(values).astype(BF16)
        return carry

    over_rows(make_dred, 0)
    reduce_owner(1)
    proj[...] = dot_t(dred[...], fw1[...].reshape(CHANNELS, BOTTLE))
    reduce_y(0)

    by_bias = mul1 * bias_sum * (1.0 / pixels)
    by_gain = mul1 * gain_sum * (1.0 / pixels)
    image_sums = sum_end("images")
    ids = lax.broadcasted_iota(jnp.int32, (16, 128), 0)
    own_sums = [
        jnp.sum(jnp.where(ids == m * n_dp + dp, image_sums, 0.0), axis=0, keepdims=True)
        for m in range(2)
    ]
    ids = row_ids(128)
    fix[0] = row_dot(by_bias, jnp.where(ids == 0, own_sums[0], jnp.where(ids == 2, own_sums[1], 0.0)))
    for m in range(2):
        fix[1 + m] = row_dot(by_gain, jnp.where(ids == 2 * m, 1.0, 0.0))
    reduce_spread(3)
    reduce_spread(4)

    def make_dx(row, carry):
        for start in range(0, CHANNELS, 256):
            lanes = slice(start, start + 256)
            values = up[pl.ds(row, CHUNK), lanes] + proj[pl.ds(row, CHUNK), lanes]
            dx4[pl.ds(row // 4, CHUNK // 4), :, lanes] = values.reshape(CHUNK // 4, 4, 256)
        return carry

    over_rows(make_dx, 0)
    dx_copy = pltpu.make_async_copy(dx4, dx_hbm, local_sem.at[3])
    dx_copy.start()
    norm_rows = np_full[0:8, :]
    for d in range(1, n_dp):
        at = shard * d // 128
        norm_rows = jnp.where(dp == d, np_full[at : at + 8, :], norm_rows)
    norm_rows = pltpu.roll(norm_rows, lax.rem(128 - turn, 128), 1)
    gn_out[...] = jnp.where(lanes_id < 128 - turn, norm_rows, pltpu.roll(norm_rows, 7, 0))
    reduce_owner(2)
    reduce_owner(0)
    reduce_spread(1)
    reduce_spread(2)
    reduce_spread(0)
    out_copies = [
        pltpu.make_async_copy(source, target, local_sem.at[10 + k])
        for k, (source, target) in enumerate(
            (
                (gn_out, gn_hbm),
                (fs[2], f3_hbm),
                (fs[3], fe_hbm),
                (fs[1], fc_hbm),
                (fs[0], f1_hbm),
            )
        )
    ]
    out_copies[0].start()
    for which in (3, 4, 1, 2, 0):
        reduce_end(which)
        if which != 1:
            out_copies[{3: 1, 4: 2, 2: 3, 0: 4}[which]].start()

    bo_copy.wait()
    dx_copy.wait()
    for copy in out_copies:
        copy.wait()
    for k in STATS:
        if k in DIRECT:
            wait_bytes(ar_slots_a[k].at[pl.ds(0, everyone - 1)], ar_send_a.at[order[k]])
        else:
            wait_bytes(ar_slots_a[k].at[pl.ds(0, plane_size - 1)], ar_send_a.at[order[k]])
            wait_bytes(ar_slots_b[k].at[pl.ds(0, planes - 1)], ar_send_b.at[order[k]])
    wait_bytes(np_slots.at[pl.ds(0, n_dp - 1)], np_sems.at[0])
    for which in range(4):
        wait_bytes(seven(which), ws.at[which, 0])
        for stage in range(1, 4):
            wait_bytes(quarters[which](core, half_y), ws.at[which, stage])
    for which in range(6):
        wait_bytes(r1s[which], gs.at[which, 0])
        wait_bytes(r2s[which], gs.at[which, 1])
        wait_bytes(r3s[which].at[pl.ds(0, n_dp - 1)], gs.at[which, 2])
        if which < 5:
            wait_bytes(three_parts(which), gs.at[which, 3])


def update_kernel(*refs):
    sources, targets = refs[0:25], refs[25:45]
    inputs, outs, through = refs[45:68], refs[68:86], refs[86:88]
    pass_sems, in_sems, out_sems = refs[88:91]
    fetching, passing = [], []
    half = SIDE * SIDE // 2
    for number, (which, at, count) in enumerate(((1, 0, half), (1, half, half), (0, 0, 2 * half))):
        rows = pl.ds(at, count)
        fetching.append(
            pltpu.make_async_copy(
                sources[which].at[rows], through[which].at[rows], pass_sems.at[0, number]
            )
        )
        passing.append(
            pltpu.make_async_copy(
                through[which].at[rows], targets[which].at[rows], pass_sems.at[1, number]
            )
        )
    for copy in fetching:
        copy.start()
    coming = [
        pltpu.make_async_copy(source, held, in_sems.at[k])
        for k, (source, held) in enumerate(zip(sources[2:], inputs))
    ]
    for copy in coming:
        copy.start()
    grads, states = inputs[0:5], inputs[5:23]
    going = [
        pltpu.make_async_copy(held, target, out_sems.at[k])
        for k, (held, target) in enumerate(zip(outs, targets[2:]))
    ]
    ex_rows = states[9].shape[0]
    shard = states[15].shape[0]
    fans = (CHANNELS, 9 * BOTTLE // RADIX, BOTTLE, INNER // 8, BOTTLE)
    for copy in coming[0:5]:
        copy.wait()
    found = (
        grads[0][...].T,
        grads[1][...],
        grads[3][:, 0:128],
        jnp.concatenate([grads[3][0:ex_rows, 128:384], grads[3][ex_rows:, 128:384]], axis=1),
        grads[2][...],
    )
    for order, k in enumerate((3, 2, 4, 0, 1)):
        for copy in coming[5 + 3 * k : 8 + 3 * k]:
            copy.wait()
        new = adamw(
            states[3 * k][...],
            states[3 * k + 1][...],
            states[3 * k + 2][...],
            found[k],
            2.0 * fans[k] ** (-0.5),
            DECAY,
        )
        for j in range(3):
            outs[3 * k + j][...] = new[j]
            going[3 * k + j].start()
        if order < 3:
            fetching[order].wait()
            passing[order].start()
    for copy in coming[20:23]:
        copy.wait()
    for at in range(0, shard, 128):
        width = min(128, shard - at)
        lanes = pl.ds(at, width)
        new = adamw(
            *[states[15 + j][lanes].reshape(1, width) for j in range(3)],
            grads[4][at // 128 : at // 128 + 1, 0:width],
            NORM_RATE,
            0.0,
        )
        for j in range(3):
            outs[15 + j][lanes] = new[j].reshape(width)
    for copy in going[15:18]:
        copy.start()
    for copy in passing + going:
        copy.wait()


def fused_device(
    images,
    out_grad,
    reduce_weight,
    reduce_moment,
    reduce_second,
    conv_weight,
    conv_moment,
    conv_second,
    squeeze_weight,
    squeeze_moment,
    squeeze_second,
    expand_weight,
    expand_moment,
    expand_second,
    project_weight,
    project_moment,
    project_second,
    norm_params,
    norm_moment,
    norm_second,
):
    n_dp, n_rep = lax.axis_size("dp"), lax.axis_size("rep")
    by_pixel = lambda values: jnp.transpose(values, (1, 2, 0, 3)).reshape(-1, 4, CHANNELS)
    qc = conv_weight.shape[0] // 2
    q1 = reduce_weight.shape[0] // 4
    pe = squeeze_weight.shape[0]
    vmem = pltpu.VMEM
    pixel_form = (SIDE * SIDE, 4, CHANNELS)
    scratch = [
        *[
            vmem(values.shape, F32)
            for values in (
                reduce_weight,
                conv_weight,
                squeeze_weight,
                expand_weight,
                project_weight,
                norm_params,
            )
        ],
        vmem((8, 128), F32),
        vmem(pixel_form, BF16),
        vmem(pixel_form, BF16),
        vmem((ROWS, CHANNELS), BF16),
        vmem((ROWS, CHANNELS), BF16),
        vmem((n_dp, 2, 2, q1, BOTTLE), BF16),
        vmem((n_dp, 2, qc, BOTTLE), BF16),
        vmem((n_dp, pe, 512), BF16),
        vmem((n_dp, pe, CHANNELS), BF16),
        vmem((pe, 512), BF16),
        vmem((n_dp, 8, 128), F32),
        vmem((40, 128), F32),
        vmem((ROWS, BOTTLE), F32),
        vmem((3, ROWS + 2 * PAD, BOTTLE), F32),
        vmem((2, ROWS, 9 * 128), BF16),
        vmem((ROWS, 512), F32),
        vmem((ROWS, 512), F32),
        vmem((ROWS, BOTTLE), BF16),
        vmem((ROWS, CHANNELS), F32),
        vmem((ROWS, CHANNELS), F32),
        vmem(pixel_form, BF16),
        vmem(pixel_form, F32),
        vmem((ROWS, CHANNELS), BF16),
        vmem((ROWS, BOTTLE), F32),
        vmem((ROWS, 512), F32),
        vmem((ROWS, 512), BF16),
        vmem((ROWS + 2 * PAD, 2 * 9 * 128), F32),
        vmem((ROWS, BOTTLE), F32),
        vmem((ROWS, BOTTLE), BF16),
        vmem((2, 2, BOTTLE // 4, CHANNELS), F32),
        vmem((n_dp, 2, qc, BOTTLE), F32),
        vmem((n_dp, pe, CHANNELS), F32),
        vmem((n_dp, pe, 512), F32),
        vmem((2, 2, BOTTLE // 2, CHANNELS), BF16),
        vmem((3, BOTTLE, CHANNELS // n_dp), F32),
        vmem((2, BOTTLE // 4, CHANNELS // n_dp), F32),
    ]
    direct = n_dp * n_rep
    scratch += [
        vmem((direct if k in DIRECT else 2 * n_rep,) + shape, F32) for k, shape in STATS.items()
    ]
    scratch += [vmem((n_dp // 2,) + shape, F32) for shape in STATS.values()]
    cut = 64
    lanes1 = CHANNELS // n_dp
    half = [
        (2, BOTTLE // 4, CHANNELS),
        (n_dp, 2, cut, 128),
        (n_dp, 2, qc - cut, 128),
        (n_dp, pe, 512),
        (n_dp, pe, 256),
        (2, BOTTLE // 2, CHANNELS),
    ]
    quarter = [
        (BOTTLE // 4, CHANNELS),
        (n_dp, cut, 128),
        (n_dp, qc - cut, 128),
        (n_dp, pe, 256),
        (n_dp, pe, 128),
        (BOTTLE // 2, CHANNELS),
    ]
    final = [(2, 2, BOTTLE // 4, lanes1), (2, qc, BOTTLE), (pe, CHANNELS), (pe, 512)]
    sent = [BF16, BF16, BF16, BF16, F32, BF16]
    scratch += [vmem(shape, F32) for shape in half[:-1]] + [vmem(half[-1], BF16)]
    scratch += [vmem(shape, kind) for shape, kind in zip(quarter, sent)] * 3
    owned = [(BOTTLE // 4, lanes1)] + [shape[1:] for shape in quarter[1:-1]]
    owned += [(BOTTLE // 2, lanes1)]
    scratch += [vmem((n_dp,) + shape, kind) for shape, kind in zip(owned, sent)]
    scratch += [vmem(shape, F32) for shape in owned]
    scratch += [vmem(shape, F32) for shape in final]
    dma = pltpu.SemaphoreType.DMA
    scratch += [dma((15,))] + [dma((len(STATS),))] * 4 + [dma((2,))] + [dma((4, 4))] * 2 + [dma((6, 4))] * 2
    any_space = pl.BlockSpec(memory_space=pl.ANY)
    block_out, images_grad, sum1, sumc, sum3, sume, norm_grads = pl.pallas_call(
        functools.partial(block_kernel, n_dp, n_rep),
        out_shape=[
            jax.ShapeDtypeStruct(pixel_form, BF16),
            jax.ShapeDtypeStruct(pixel_form, F32),
            *[jax.ShapeDtypeStruct(shape, F32) for shape in final],
            jax.ShapeDtypeStruct((8, 128), F32),
        ],
        in_specs=[any_space] * 8,
        out_specs=[any_space] * 7,
        scratch_shapes=scratch,
        compiler_params=pltpu.CompilerParams(
            collective_id=0, has_side_effects=True, vmem_limit_bytes=63 * 1024 * 1024
        ),
    )(
        by_pixel(images),
        by_pixel(out_grad),
        reduce_weight,
        conv_weight,
        squeeze_weight,
        expand_weight,
        project_weight,
        norm_params,
    )
    states = (
        reduce_weight,
        reduce_moment,
        reduce_second,
        conv_weight,
        conv_moment,
        conv_second,
        squeeze_weight,
        squeeze_moment,
        squeeze_second,
        expand_weight,
        expand_moment,
        expand_second,
        project_weight,
        project_moment,
        project_second,
    )
    held = (*states, norm_params, norm_moment, norm_second)
    sums = (
        sum1.reshape(BOTTLE, lanes1),
        sumc.reshape(conv_weight.shape),
        sum3,
        sume,
        norm_grads,
    )
    block_out, images_grad, *updated = pl.pallas_call(
        update_kernel,
        out_shape=[
            jax.ShapeDtypeStruct(pixel_form, BF16),
            jax.ShapeDtypeStruct(pixel_form, F32),
            *[jax.ShapeDtypeStruct(state.shape, F32) for state in held],
        ],
        in_specs=[any_space] * 25,
        out_specs=[any_space] * 20,
        scratch_shapes=[vmem(values.shape, F32) for values in (*sums, *held, *held)]
        + [vmem(pixel_form, BF16), vmem(pixel_form, F32)]
        + [dma((2, 3)), dma((23,)), dma((18,))],
        compiler_params=pltpu.CompilerParams(vmem_limit_bytes=63 * 1024 * 1024),
    )(block_out, images_grad, *sums, *held)
    by_image = lambda values: jnp.transpose(
        values.reshape(SIDE, SIDE, images.shape[0], CHANNELS), (2, 0, 1, 3)
    )
    return (
        by_image(block_out),
        by_image(images_grad),
        *updated,
    )


def solution(mesh):
    placed = (
        P(("dp", "rep"), None, None, None),
        P(("dp", "rep"), None, None, None),
        P("dp", None),
        P("dp", None),
        P("dp", None),
        P("dp", None),
        P("dp", None),
        P("dp", None),
        P("dp", None),
        P("dp", None),
        P("dp", None),
        P("dp", None),
        P("dp", None),
        P("dp", None),
        P("dp", None),
        P("dp", None),
        P("dp", None),
        P("dp"),
        P("dp"),
        P("dp"),
    )
    n_dp, n_rep = mesh.shape["dp"], mesh.shape["rep"]
    whole_tiles = n_rep == 4 and n_dp % 2 == 0 and INNER % (16 * n_dp) == 0
    return jax.shard_map(
        fused_device if whole_tiles else per_device,
        mesh=mesh,
        in_specs=placed,
        out_specs=(
            P(("dp", "rep"), None, None, None),
            P(("dp", "rep"), None, None, None),
            P("dp", None),
            P("dp", None),
            P("dp", None),
            P("dp", None),
            P("dp", None),
            P("dp", None),
            P("dp", None),
            P("dp", None),
            P("dp", None),
            P("dp", None),
            P("dp", None),
            P("dp", None),
            P("dp", None),
            P("dp", None),
            P("dp", None),
            P("dp"),
            P("dp"),
            P("dp"),
        ),
        check_vma=False,
    )
```

```python
import functools
import jax
import jax.numpy as jnp
from jax import lax
from jax.experimental import pallas as pl
from jax.experimental.pallas import tpu as pltpu
from jax.sharding import PartitionSpec as P

CHANNELS = 1024
BOTTLE = 256
INNER = 128
RADIX = 2
SIDE = 14
MICRO = 2
STEP = 10


EPSILON = 1e-05
PRECISE = lax.Precision.HIGHEST
BETA_ONE = 0.9
BETA_TWO = 0.999
ADAM_EPSILON = 1e-08
DECAY = 0.01
NORM_RATE = 0.8
ROWS = 4 * SIDE * SIDE
NORM_WIDTH = 4352


def split_params(packed):
    widths = (
        BOTTLE,
        BOTTLE,
        RADIX * BOTTLE,
        RADIX * BOTTLE,
        INNER,
        INNER,
        RADIX * BOTTLE,
        CHANNELS,
        CHANNELS,
    )
    pieces = []
    offset = 0
    for segment in widths:
        pieces.append(lax.slice_in_dim(packed, offset, offset + segment))
        offset = offset + segment
    return pieces


def silu_slope(values):
    logistic = jax.nn.sigmoid(values)
    return logistic * (1.0 + values * (1.0 - logistic))


def norm_forward(values, gain, bias, count):
    flat = values.reshape(-1, values.shape[-1])
    total, square = lax.psum((jnp.sum(flat, axis=0), jnp.sum(flat * flat, axis=0)), ("dp", "rep"))
    center = total / count
    scale = lax.rsqrt(square / count - center * center + EPSILON)
    normed = (values - center) * scale
    return (normed * gain + bias, normed, scale)


def norm_backward(upstream, normed, scale, gain, count):
    flat_up = upstream.reshape(-1, upstream.shape[-1])
    flat_norm = normed.reshape(-1, normed.shape[-1])
    bias_sum, gain_sum = lax.psum(
        (jnp.sum(flat_up, axis=0), jnp.sum(flat_up * flat_norm, axis=0)), ("dp", "rep")
    )
    downstream = gain * scale * (upstream - bias_sum / count - normed * (gain_sum / count))
    return (downstream, gain_sum, bias_sum)


def patches(active):
    padded = jnp.pad(active, ((0, 0), (1, 1), (1, 1), (0, 0), (0, 0)))
    shifted = [
        padded[:, down_step : down_step + SIDE, side_step : side_step + SIDE]
        for down_step in range(3)
        for side_step in range(3)
    ]
    return jnp.stack(shifted, axis=4)


def unpatch(columns):
    total = jnp.zeros(
        (columns.shape[0], SIDE + 2, SIDE + 2, columns.shape[3], columns.shape[5]), jnp.float32
    )
    for down_step in range(3):
        for side_step in range(3):
            piece = columns[:, :, :, :, 3 * down_step + side_step]
            total = total + jnp.pad(
                piece,
                ((0, 0), (down_step, 2 - down_step), (side_step, 2 - side_step), (0, 0), (0, 0)),
            )
    return total[:, 1 : SIDE + 1, 1 : SIDE + 1]


def adamw(param, moment, second, gradient, rate, decay):
    moment_new = BETA_ONE * moment + (1.0 - BETA_ONE) * gradient
    second_new = BETA_TWO * second + (1.0 - BETA_TWO) * gradient * gradient
    ratio = (
        moment_new
        / (1.0 - BETA_ONE**STEP)
        / (jnp.sqrt(second_new / (1.0 - BETA_TWO**STEP)) + ADAM_EPSILON)
    )
    return (param - rate * (ratio + decay * param), moment_new, second_new)


def per_device(
    images,
    out_grad,
    reduce_weight,
    reduce_moment,
    reduce_second,
    conv_weight,
    conv_moment,
    conv_second,
    squeeze_weight,
    squeeze_moment,
    squeeze_second,
    expand_weight,
    expand_moment,
    expand_second,
    project_weight,
    project_moment,
    project_second,
    norm_params,
    norm_moment,
    norm_second,
):
    bf16 = jnp.bfloat16
    low_reduce = reduce_weight.astype(bf16)
    low_conv = conv_weight.astype(bf16)
    low_squeeze = squeeze_weight.astype(bf16)
    low_expand = expand_weight.astype(bf16)
    low_project = project_weight.astype(bf16)
    low_norm = norm_params.astype(bf16)
    devices = lax.axis_size("dp") * lax.axis_size("rep")
    per_batch = images.shape[0] // MICRO
    pixel_count = float(per_batch * SIDE * SIDE * devices)
    image_count = float(per_batch * devices)
    group_in = BOTTLE // RADIX
    grad_first = jnp.zeros((CHANNELS, BOTTLE), jnp.float32)
    grad_conv = jnp.zeros((RADIX, 9 * group_in, BOTTLE), jnp.float32)
    grad_squeeze = jnp.zeros((BOTTLE, INNER), jnp.float32)
    grad_expand = jnp.zeros((INNER, RADIX * BOTTLE), jnp.float32)
    grad_last = jnp.zeros((BOTTLE, CHANNELS), jnp.float32)
    grad_norms = jnp.zeros(
        (2 * BOTTLE + 3 * RADIX * BOTTLE + 2 * INNER + 2 * CHANNELS,), jnp.float32
    )
    outputs = []
    input_grads = []
    for number in range(MICRO):
        forward_set = (
            lax.all_gather(low_reduce, "dp", axis=0, tiled=True),
            lax.all_gather(low_conv, "dp", axis=0, tiled=True),
            lax.all_gather(low_squeeze, "dp", axis=0, tiled=True),
            lax.all_gather(low_expand, "dp", axis=0, tiled=True),
            lax.all_gather(low_project, "dp", axis=0, tiled=True),
            lax.all_gather(low_norm, "dp", axis=0, tiled=True),
        )
        first, conv, squeeze, expand, last, packed = forward_set
        (
            gain_one,
            bias_one,
            gain_two,
            bias_two,
            gain_pool,
            bias_pool,
            bias_expand,
            gain_three,
            bias_three,
        ) = split_params(packed.astype(jnp.float32))
        batched = images[number * per_batch : (number + 1) * per_batch]
        cotangent = out_grad[number * per_batch : (number + 1) * per_batch]
        reduced = jnp.einsum("nhwc,cb->nhwb", batched, first, preferred_element_type=jnp.float32)
        norm_one, normed_one, scale_one = norm_forward(reduced, gain_one, bias_one, pixel_count)
        active = jax.nn.silu(norm_one).astype(bf16)
        columns = patches(active.reshape(per_batch, SIDE, SIDE, RADIX, group_in)).reshape(
            per_batch * SIDE * SIDE, RADIX, 9 * group_in
        )
        conv_grouped = conv.reshape(RADIX, 9 * group_in, BOTTLE)
        widened = jnp.einsum(
            "prk,rko->pro", columns, conv_grouped, preferred_element_type=jnp.float32
        )
        widened = widened.reshape(per_batch, SIDE, SIDE, RADIX * BOTTLE)
        norm_two, normed_two, scale_two = norm_forward(widened, gain_two, bias_two, pixel_count)
        splits = jax.nn.silu(norm_two).reshape(per_batch, SIDE, SIDE, RADIX, BOTTLE)
        pooled = jnp.sum(jnp.sum(splits, axis=3), axis=(1, 2)) / (SIDE * SIDE)
        squeeze_float = squeeze.astype(jnp.float32)
        expand_float = expand.astype(jnp.float32)
        pre_pool = jnp.dot(pooled, squeeze_float, precision=PRECISE)
        norm_pool, normed_pool, scale_pool = norm_forward(
            pre_pool, gain_pool, bias_pool, image_count
        )
        hidden = jax.nn.silu(norm_pool)
        logits = (jnp.dot(hidden, expand_float, precision=PRECISE) + bias_expand).reshape(
            per_batch, RADIX, BOTTLE
        )
        attention = jax.nn.softmax(logits, axis=1)
        mixed = jnp.sum(splits * attention[:, None, None], axis=3).astype(bf16)
        projected = jnp.einsum("nhwb,bc->nhwc", mixed, last, preferred_element_type=jnp.float32)
        norm_three, normed_three, scale_three = norm_forward(
            projected, gain_three, bias_three, pixel_count
        )
        summed = batched.astype(jnp.float32) + norm_three
        outputs.append(jax.nn.silu(summed).astype(bf16))
        backward_set = (
            lax.all_gather(low_reduce, "dp", axis=0, tiled=True),
            lax.all_gather(low_conv, "dp", axis=0, tiled=True),
            lax.all_gather(low_squeeze, "dp", axis=0, tiled=True),
            lax.all_gather(low_expand, "dp", axis=0, tiled=True),
            lax.all_gather(low_project, "dp", axis=0, tiled=True),
            lax.all_gather(low_norm, "dp", axis=0, tiled=True),
        )
        first, conv, squeeze, expand, last, packed = backward_set
        gains_back = split_params(packed.astype(jnp.float32))
        conv_grouped = conv.reshape(RADIX, 9 * group_in, BOTTLE)
        expand_float = expand.astype(jnp.float32)
        squeeze_float = squeeze.astype(jnp.float32)
        upstream = cotangent.astype(jnp.float32) * silu_slope(summed)
        d_projected, gain_three_grad, bias_three_grad = norm_backward(
            upstream, normed_three, scale_three, gains_back[7], pixel_count
        )
        d_projected_low = d_projected.astype(bf16)
        grad_last = grad_last + jnp.einsum(
            "nhwb,nhwc->bc", mixed, d_projected_low, preferred_element_type=jnp.float32
        )
        d_mixed = jnp.einsum(
            "nhwc,bc->nhwb", d_projected_low, last, preferred_element_type=jnp.float32
        )
        d_splits = d_mixed[:, :, :, None] * attention[:, None, None]
        d_attention = jnp.sum(d_mixed[:, :, :, None] * splits, axis=(1, 2))
        d_logits = attention * (
            d_attention - jnp.sum(attention * d_attention, axis=1, keepdims=True)
        )
        flat_logits = d_logits.reshape(per_batch, RADIX * BOTTLE)
        grad_expand = grad_expand + jnp.dot(hidden.T, flat_logits, precision=PRECISE)
        d_hidden = jnp.dot(flat_logits, expand_float.T, precision=PRECISE)
        d_pool_norm = d_hidden * silu_slope(norm_pool)
        pool_bias_sum, pool_gain_sum, expand_bias_sum = lax.psum(
            (
                jnp.sum(d_pool_norm, axis=0),
                jnp.sum(d_pool_norm * normed_pool, axis=0),
                jnp.sum(flat_logits, axis=0),
            ),
            ("dp", "rep"),
        )
        d_pre_pool = (
            gains_back[4]
            * scale_pool
            * (
                d_pool_norm
                - pool_bias_sum / image_count
                - normed_pool * (pool_gain_sum / image_count)
            )
        )
        grad_squeeze = grad_squeeze + jnp.dot(pooled.T, d_pre_pool, precision=PRECISE)
        d_pooled = jnp.dot(d_pre_pool, squeeze_float.T, precision=PRECISE)
        d_splits = d_splits + (d_pooled / (SIDE * SIDE))[:, None, None, None, :]
        d_norm_two = d_splits.reshape(per_batch, SIDE, SIDE, RADIX * BOTTLE) * silu_slope(norm_two)
        d_widened, gain_two_grad, bias_two_grad = norm_backward(
            d_norm_two, normed_two, scale_two, gains_back[2], pixel_count
        )
        d_widened_low = d_widened.astype(bf16).reshape(per_batch * SIDE * SIDE, RADIX, BOTTLE)
        grad_conv = grad_conv + jnp.einsum(
            "prk,pro->rko", columns, d_widened_low, preferred_element_type=jnp.float32
        )
        d_columns = jnp.einsum(
            "pro,rko->prk", d_widened_low, conv_grouped, preferred_element_type=jnp.float32
        )
        d_active = unpatch(d_columns.reshape(per_batch, SIDE, SIDE, RADIX, 9, group_in)).reshape(
            per_batch, SIDE, SIDE, BOTTLE
        )
        d_norm_one = d_active * silu_slope(norm_one)
        d_reduced, gain_one_grad, bias_one_grad = norm_backward(
            d_norm_one, normed_one, scale_one, gains_back[0], pixel_count
        )
        d_reduced_low = d_reduced.astype(bf16)
        grad_first = grad_first + jnp.einsum(
            "nhwc,nhwb->cb", batched, d_reduced_low, preferred_element_type=jnp.float32
        )
        input_grads.append(
            upstream
            + jnp.einsum("nhwb,cb->nhwc", d_reduced_low, first, preferred_element_type=jnp.float32)
        )
        grad_norms = grad_norms + jnp.concatenate(
            [
                gain_one_grad,
                bias_one_grad,
                gain_two_grad,
                bias_two_grad,
                pool_gain_sum,
                pool_bias_sum,
                expand_bias_sum,
                gain_three_grad,
                bias_three_grad,
            ]
        )
    grad_conv = grad_conv.reshape(9 * BOTTLE, BOTTLE)
    partial_value = (
        lax.psum_scatter(grad_first, "dp", scatter_dimension=0, tiled=True),
        lax.psum_scatter(grad_conv, "dp", scatter_dimension=0, tiled=True),
        lax.psum_scatter(grad_squeeze, "dp", scatter_dimension=0, tiled=True),
        lax.psum_scatter(grad_expand, "dp", scatter_dimension=0, tiled=True),
        lax.psum_scatter(grad_last, "dp", scatter_dimension=0, tiled=True),
    )
    owned = lax.psum(
        (partial_value[0], partial_value[1], partial_value[2], partial_value[3], partial_value[4]),
        "rep",
    )
    shard_length = norm_params.shape[0]
    norm_grad_owned = lax.dynamic_slice_in_dim(
        grad_norms, lax.axis_index("dp") * shard_length, shard_length
    )
    reduce_new = adamw(
        reduce_weight, reduce_moment, reduce_second, owned[0], 2.0 * CHANNELS ** (-0.5), DECAY
    )
    conv_new = adamw(
        conv_weight,
        conv_moment,
        conv_second,
        owned[1],
        2.0 * (9 * BOTTLE // RADIX) ** (-0.5),
        DECAY,
    )
    squeeze_new = adamw(
        squeeze_weight, squeeze_moment, squeeze_second, owned[2], 2.0 * BOTTLE ** (-0.5), DECAY
    )
    expand_new = adamw(
        expand_weight, expand_moment, expand_second, owned[3], 2.0 * (INNER // 8) ** (-0.5), DECAY
    )
    project_new = adamw(
        project_weight, project_moment, project_second, owned[4], 2.0 * BOTTLE ** (-0.5), DECAY
    )
    norm_new = adamw(norm_params, norm_moment, norm_second, norm_grad_owned, NORM_RATE, 0.0)
    return (
        jnp.concatenate(outputs, axis=0),
        jnp.concatenate(input_grads, axis=0),
        reduce_new[0],
        reduce_new[1],
        reduce_new[2],
        conv_new[0],
        conv_new[1],
        conv_new[2],
        squeeze_new[0],
        squeeze_new[1],
        squeeze_new[2],
        expand_new[0],
        expand_new[1],
        expand_new[2],
        project_new[0],
        project_new[1],
        project_new[2],
        norm_new[0],
        norm_new[1],
        norm_new[2],
    )


MESH = pl.DeviceIdType.MESH
PAD = 64
CHUNK = 112
F32 = jnp.float32
BF16 = jnp.bfloat16
STATS = {
    "reduced": (8, 128),
    "widened0": (8, 128),
    "widened1": (8, 128),
    "pool": (8, 128),
    "images": (16, 128),
    "projected0": (8, 256),
    "projected1": (8, 256),
    "back_projected0": (8, 256),
    "back_projected1": (8, 256),
    "back_pool": (8, 128),
    "back_widened0": (8, 128),
    "back_widened1": (16, 128),
    "back_reduced0": (8, 128),
    "back_reduced1": (8, 128),
}
DIRECT = ("reduced", "pool", "back_pool")


def sigmoid(values):
    return 0.5 * jnp.tanh(0.5 * values) + 0.5


def row_ids(width):
    return lax.broadcasted_iota(jnp.int32, (8, width), 0)


def image_sum(rows):
    return rows + pltpu.roll(rows, 4, 0)


def pair_sum(rows):
    even = row_ids(rows.shape[1]) % 2 == 0
    return rows + jnp.where(even, pltpu.roll(rows, 7, 0), pltpu.roll(rows, 1, 0))


def micro_sum(rows):
    return pair_sum(image_sum(rows))


def stack_sums(first, second):
    return jnp.where(row_ids(first.shape[1]) < 4, first, second)


def unstack_sums(stacked):
    upper = row_ids(stacked.shape[1]) < 4
    turned = pltpu.roll(stacked, 4, 0)
    return jnp.where(upper, stacked, turned), jnp.where(upper, turned, stacked)


def fold_lanes(stacked):
    half = stacked.shape[1] // 2
    even = row_ids(half) % 2 == 0
    return jnp.where(even, stacked[:, :half], stacked[:, half:])


def unfold_lanes(folded):
    even = row_ids(folded.shape[1]) % 2 == 0
    left = jnp.where(even, folded, pltpu.roll(folded, 1, 0))
    right = jnp.where(even, pltpu.roll(folded, 7, 0), folded)
    return jnp.concatenate([left, right], axis=1)


def norm_terms(total, square, gain, bias, count):
    center = total * (1.0 / count)
    scale = lax.rsqrt(square * (1.0 / count) - center * center + EPSILON)
    slope = scale * gain
    return center, scale, slope, bias - center * slope


def back_terms(center, scale, slope, bias_sum, gain_sum, count):
    by_value = -slope * scale * (gain_sum * (1.0 / count))
    constant = -slope * (bias_sum * (1.0 / count)) - by_value * center
    return by_value, constant


def tdot(left, right):
    return lax.dot_general(left, right, (((0,), (0,)), ((), ())), preferred_element_type=F32)


def dot_t(left, right):
    return lax.dot_general(left, right, (((1,), (1,)), ((), ())), preferred_element_type=F32)


def in_parts(values, parts):
    found = []
    for _ in range(parts):
        rounded = values.astype(BF16).astype(F32)
        found.append(rounded)
        values = values - rounded
    return found


def exact_dot(left, right, transposed):
    stacked = jnp.concatenate(in_parts(left, 3), axis=0).astype(BF16)
    wide = dot_t(stacked, right) if transposed else jnp.dot(stacked, right, preferred_element_type=F32)
    return wide[0:8] + wide[8:16] + wide[16:24]


def row_dot(left, right):
    high, low = in_parts(left, 2)
    other_high, other_low = in_parts(right, 2)
    return tdot(
        jnp.concatenate([high, high, low, low], axis=0).astype(BF16),
        jnp.concatenate([other_high, other_low, other_high, other_low], axis=0).astype(BF16),
    )


def image_dot(left, right):
    return row_dot(jnp.where(row_ids(left.shape[1]) < 4, left, 0.0), right)


def block_kernel(
    n_dp,
    n_rep,
    x_hbm,
    gy_hbm,
    w1_hbm,
    wc_hbm,
    sq_hbm,
    ex_hbm,
    w3_hbm,
    np_hbm,
    bo_hbm,
    dx_hbm,
    f1_hbm,
    fc_hbm,
    f3_hbm,
    fe_hbm,
    gn_hbm,
    w1_own,
    wc_own,
    sq_own,
    ex_own,
    w3_own,
    np_own,
    gn_out,
    x4,
    gy4,
    x_v,
    gy_v,
    fw1,
    fwc,
    fes,
    fw3,
    es_own,
    np_slots,
    np_full,
    red,
    act,
    columns,
    wid,
    splits,
    mixed,
    proj,
    up,
    bo4,
    dx4,
    dproj,
    d_mixed,
    dn2,
    dwid,
    dcol,
    dn1,
    dred,
    g1,
    gc,
    g3,
    ge,
    gb,
    fix,
    back_own,
    *rest,
):
    n_ar = len(STATS)
    order = {name: k for k, name in enumerate(STATS)}
    ar_slots_a = dict(zip(STATS, rest[0:n_ar]))
    ar_slots_b = dict(zip(STATS, rest[n_ar : 2 * n_ar]))
    rest = rest[2 * n_ar :]
    r1s, ys, r2s, ks, r3s, own = (rest[6 * i : 6 * i + 6] for i in range(6))
    fs = rest[36:40]
    rest = rest[40:]
    local_sem, ar_send_a, ar_recv_a, ar_send_b, ar_recv_b, np_sems, ws, wr, gs, gr = rest

    dp = lax.axis_index("dp")
    rep = lax.axis_index("rep")
    core = lax.rem(rep, 2)
    half_y = lax.div(rep, 2)
    planes = n_dp // 2
    plane_size = 2 * n_rep
    plane = lax.div(dp, 2)
    in_plane = lax.rem(dp, 2) * n_rep + rep
    sibling = (dp, half_y * 2 + (1 - core))
    across = (dp, (1 - half_y) * 2 + core)
    pixels = float(SIDE * SIDE * 2 * n_dp * n_rep)
    pictures = float(2 * n_dp * n_rep)

    x = lax.rem(dp, 2)
    if planes == 4:
        upper = lax.div(plane, 2)
        other_planes = [3 - 3 * upper, 2 - upper, 1 - plane + 4 * upper]
    else:
        other_planes = [lax.rem(plane + step, planes) for step in range(1, planes)]
    flips = ((1, 1, 1), (1, 1, 0), (1, 0, 1), (1, 0, 0), (0, 1, 1), (0, 1, 0), (0, 0, 1), (0, 0, 0))

    def of_flip(z, flip):
        there = [1 - own if turn else own for own, turn in zip((x, half_y, core), flip)]
        return (z * 2 + there[0], there[1] * 2 + there[2])

    plane_peers = [of_flip(plane, flip) for flip in flips[:-1]]
    column_peers = [of_flip(z, flips[-1]) for z in other_planes]
    owner_peers = [of_flip(z, flip) for z in other_planes for flip in (flips[3], flips[7])]
    owner_peers += [of_flip(plane, flips[3])]
    all_peers = [of_flip(z, flip) for z in other_planes for flip in flips] + plane_peers
    me, everyone = dp * n_rep + rep, n_dp * n_rep
    rep_peers = [(dp, lax.rem(rep + step, n_rep)) for step in range(1, n_rep)]

    def remote(src, dst, send_sem, recv_sem, device):
        return pltpu.make_async_remote_copy(
            src_ref=src,
            dst_ref=dst,
            send_sem=send_sem,
            recv_sem=recv_sem,
            device_id=device,
            device_id_type=MESH,
        )

    def send_all(ref, send_sem, recv_sem, peers):
        for device in peers:
            remote(ref, ref, send_sem, recv_sem, device).start()

    def wait_bytes(ref, sem):
        pltpu.make_async_copy(ref, ref, sem).wait()

    def over_rows(body, init):
        def step(index, carry):
            return body(pl.multiple_of(index * CHUNK, CHUNK), carry)

        return lax.fori_loop(0, ROWS // CHUNK, step, init)

    def grouped(values):
        return values.reshape(CHUNK // 8, 8, values.shape[-1])

    def by_four(values):
        return flat(values).reshape(CHUNK // 4, 4, values.shape[-1])

    def flat(values):
        return values.reshape(CHUNK, values.shape[-1])

    own_copies = [
        pltpu.make_async_copy(source, target, local_sem.at[4 + k])
        for k, (source, target) in enumerate(
            (
                (w1_hbm, w1_own),
                (np_hbm, np_own),
                (wc_hbm, wc_own),
                (w3_hbm, w3_own),
                (sq_hbm, sq_own),
                (ex_hbm, ex_own),
            )
        )
    ]
    for copy in own_copies:
        copy.start()
    x_copy = pltpu.make_async_copy(x_hbm, x4, local_sem.at[0])
    gy_copy = pltpu.make_async_copy(gy_hbm, gy4, local_sem.at[1])
    x_copy.start()
    barrier = pltpu.get_barrier_semaphore()
    for device in all_peers:
        pl.semaphore_signal(barrier, inc=1, device_id=device, device_id_type=MESH)

    part = core * 2 + half_y
    own_copies[0].wait()
    q1 = w1_own.shape[0] // 4
    fw1[dp, core, half_y] = w1_own[pl.ds(pl.multiple_of(part * q1, q1), q1), :].astype(BF16)
    core_lanes = pl.ds(pl.multiple_of(core * 128, 128), 128)
    es_lanes = pl.ds(pl.multiple_of(part * 128, 128), 128)
    w3_lanes = pl.ds(pl.multiple_of(part * 256, 128), 256)

    pl.semaphore_wait(barrier, everyone - 1)

    def quarter_w1(c, y):
        return fw1.at[:, c, y]

    def quarter_wc(c, y):
        return fwc.at[:, y, :, pl.ds(pl.multiple_of(c * 128, 128), 128)]

    def quarter_es(c, y):
        return fes.at[:, :, pl.ds(pl.multiple_of((c * 2 + y) * 128, 128), 128)]

    def quarter_w3(c, y):
        return fw3.at[:, :, pl.ds(pl.multiple_of((c * 2 + y) * 256, 128), 256)]

    quarters = (quarter_w1, quarter_wc, quarter_es, quarter_w3)

    def piece(which, d):
        return (
            fw1.at[d, core, half_y],
            fwc.at[d, half_y, :, core_lanes],
            fes.at[d, :, es_lanes],
            fw3.at[d, :, w3_lanes],
        )[which]

    def seven(which):
        return (
            fw1.at[pl.ds(0, n_dp - 1), core, half_y],
            fwc.at[pl.ds(0, n_dp - 1), half_y, :, core_lanes],
            fes.at[pl.ds(0, n_dp - 1), :, es_lanes],
            fw3.at[pl.ds(0, n_dp - 1), :, w3_lanes],
        )[which]

    def gather_out(which):
        send_all(piece(which, dp), ws.at[which, 0], wr.at[which, 0], owner_peers)

    def gather_turn(which):
        wait_bytes(seven(which), wr.at[which, 0])
        mine = quarters[which](core, half_y)
        remote(mine, mine, ws.at[which, 1], wr.at[which, 1], across).start()
        remote(mine, mine, ws.at[which, 2], wr.at[which, 2], sibling).start()

    def gather_hand(which):
        theirs = quarters[which](core, 1 - half_y)
        wait_bytes(theirs, wr.at[which, 1])
        remote(theirs, theirs, ws.at[which, 3], wr.at[which, 3], sibling).start()

    def gather_end(which):
        wait_bytes(quarters[which](1 - core, half_y), wr.at[which, 2])
        wait_bytes(quarters[which](1 - core, 1 - half_y), wr.at[which, 3])

    def to_rows(source, target):
        def body(index, carry):
            values = source[pl.ds(index * (CHUNK // 4), CHUNK // 4)].astype(F32)
            row = pl.multiple_of(index * CHUNK, CHUNK)
            target[pl.ds(row, CHUNK), :] = values.reshape(CHUNK, CHANNELS).astype(BF16)
            return carry

        lax.fori_loop(0, ROWS // CHUNK, body, 0)

    gather_out(0)
    own_copies[2].wait()
    qc = wc_own.shape[0] // 2
    fwc[dp, half_y, :, core_lanes] = wc_own[
        pl.ds(pl.multiple_of(half_y * qc, qc), qc), core_lanes
    ].astype(BF16)
    gather_out(1)

    own_copies[1].wait()
    shard = np_own.shape[0]
    lanes_id = lax.broadcasted_iota(jnp.int32, (8, 128), 1)
    turn = lax.rem(shard * dp, 128)
    np_rows = []
    for at in range(0, shard, 128):
        width = min(128, shard - at)
        piece_row = np_own[pl.ds(at, width)].reshape(1, width)
        if width < 128:
            piece_row = jnp.concatenate([piece_row, jnp.zeros((1, 128 - width), F32)], axis=1)
        np_rows.append(piece_row)
    np_rows.append(jnp.zeros((8 - len(np_rows), 128), F32))
    np_turned = jnp.concatenate(np_rows, axis=0).astype(BF16).astype(F32)
    np_turned = pltpu.roll(np_turned, turn, 1)
    np_slots[dp] = jnp.where(lanes_id < turn, pltpu.roll(np_turned, 1, 0), np_turned)
    send_all(np_slots.at[dp], np_sems.at[0], np_sems.at[1], owner_peers)
    for copy in own_copies[3:]:
        copy.wait()
    ex_rows = ex_own.shape[0]
    es_own[:, 0:128] = sq_own[...].astype(BF16)
    es_own[0:ex_rows, 128:384] = ex_own[:, 0:256].astype(BF16)
    es_own[ex_rows : 2 * ex_rows, 128:384] = ex_own[:, 256:512].astype(BF16)
    es_own[:, 384:512] = jnp.zeros((2 * ex_rows, 128), BF16)
    fes[dp, :, es_lanes] = es_own[:, es_lanes]
    fw3[dp, :, w3_lanes] = w3_own[:, w3_lanes].astype(BF16)
    gy_copy.start()
    x_copy.wait()
    to_rows(x4, x_v)
    gather_turn(0)
    zero_rows = jnp.zeros((PAD, BOTTLE), F32)
    for side in range(3):
        act[side, 0:PAD, :] = zero_rows
        act[side, PAD + ROWS : 2 * PAD + ROWS, :] = zero_rows
    for lane_block in range(9):
        dcol[0:PAD, lane_block * 256 : lane_block * 256 + 256] = zero_rows
        dcol[PAD + ROWS : 2 * PAD + ROWS, lane_block * 256 : lane_block * 256 + 256] = zero_rows
    gather_hand(0)
    gather_out(2)
    gather_out(3)
    gather_turn(1)

    def sum_start(k, payload):
        if k in DIRECT:
            ar_slots_a[k][me] = payload
            send_all(ar_slots_a[k].at[me], ar_send_a.at[order[k]], ar_recv_a.at[order[k]], all_peers)
        else:
            ar_slots_a[k][in_plane] = payload
            send_all(ar_slots_a[k].at[in_plane], ar_send_a.at[order[k]], ar_recv_a.at[order[k]], plane_peers)

    def sum_slots(slots, count):
        sums = [slots[slot] for slot in range(count)]
        while len(sums) > 1:
            sums = [sums[i] + sums[i + 1] for i in range(0, len(sums), 2)]
        return sums[0]

    def sum_turn(k):
        if k in DIRECT:
            return
        wait_bytes(ar_slots_a[k].at[pl.ds(0, plane_size - 1)], ar_recv_a.at[order[k]])
        ar_slots_b[k][plane] = sum_slots(ar_slots_a[k], plane_size)
        send_all(ar_slots_b[k].at[plane], ar_send_b.at[order[k]], ar_recv_b.at[order[k]], column_peers)

    def sum_end(k):
        if k in DIRECT:
            wait_bytes(ar_slots_a[k].at[pl.ds(0, everyone - 1)], ar_recv_a.at[order[k]])
            return sum_slots(ar_slots_a[k], everyone)
        wait_bytes(ar_slots_b[k].at[pl.ds(0, planes - 1)], ar_recv_b.at[order[k]])
        return sum_slots(ar_slots_b[k], planes)

    def lanes_of(index, width):
        return pl.ds(pl.multiple_of(index * width, 128), width)

    cut = 64
    conv_rows = {1: pl.ds(0, cut), 2: pl.ds(cut, gc.shape[2] - cut)}
    grads = (g1, gc, gc, g3, ge, gb)
    turned_kinds = (0, 5)

    def half_of(which, c):
        ref = grads[which]
        if which in turned_kinds:
            return ref.at[c]
        if which in conv_rows:
            return ref.at[:, :, conv_rows[which], lanes_of(c, 128)]
        return ref.at[:, :, lanes_of(c, (512, 256)[which - 3])]

    def y_part(which, ref, y):
        if which in turned_kinds:
            return ref.at[y]
        if which < 3:
            return ref.at[:, y]
        return ref.at[:, :, lanes_of(y, (256, 128)[which - 3])]

    def quarter_of(which, c, y):
        ref = grads[which]
        if which in turned_kinds:
            return ref.at[c, y]
        if which in conv_rows:
            return ref.at[:, y, conv_rows[which], lanes_of(c, 128)]
        return ref.at[:, :, lanes_of(c * 2 + y, (256, 128)[which - 3])]

    def final_part(which, c, y):
        if which == 0:
            return fs[0].at[c, y]
        if which in conv_rows:
            return fs[1].at[y, conv_rows[which], lanes_of(c, 128)]
        return fs[which - 1].at[:, lanes_of(c * 2 + y, (256, 128)[which - 3])]

    def of_owner(which, ref, d):
        return ref.at[:, lanes_of(d, CHANNELS // n_dp)] if which in turned_kinds else ref.at[d]

    def in_blocks(which, body):
        if which in turned_kinds:
            count = 4
            rows = grads[which].shape[2] // count
            block = lambda index: pl.ds(pl.multiple_of(index * rows, rows), rows)
        else:
            count, block = n_dp, lambda index: index

        def step(index, carry):
            body(block(index))
            return carry

        lax.fori_loop(0, count, step, 0)

    def reduce_core(which):
        remote(
            half_of(which, 1 - core), r1s[which], gs.at[which, 0], gr.at[which, 0], sibling
        ).start()

    def reduce_y(which):
        wait_bytes(r1s[which], gr.at[which, 0])
        away = quarter_of(which, core, 1 - half_y)
        mine = quarter_of(which, core, half_y)
        there = y_part(which, r1s[which], 1 - half_y)
        here = y_part(which, r1s[which], half_y)

        def add_away(at):
            ys[which][at] = (away[at].astype(F32) + there[at].astype(F32)).astype(
                ys[which].dtype
            )

        in_blocks(which, add_away)
        remote(ys[which], r2s[which], gs.at[which, 1], gr.at[which, 1], across).start()

        def add_mine(at):
            mine[at] = (mine[at].astype(F32) + here[at].astype(F32)).astype(mine.dtype)

        in_blocks(which, add_mine)

    def reduce_owner(which):
        wait_bytes(r2s[which], gr.at[which, 1])
        mine = quarter_of(which, core, half_y)

        def add(at):
            ks[which][at] = (mine[at].astype(F32) + r2s[which][at].astype(F32)).astype(
                ks[which].dtype
            )

        in_blocks(which, add)
        for device in owner_peers:
            remote(
                of_owner(which, ks[which], device[0]),
                r3s[which].at[dp],
                gs.at[which, 2],
                gr.at[which, 2],
                device,
            ).start()
        own[which][...] = of_owner(which, mine, dp)[...].astype(F32) + of_owner(
            which, r2s[which], dp
        )[...].astype(F32)
        r3s[which][dp] = jnp.zeros(own[which].shape, r3s[which].dtype)

    def owner_total(which):
        wait_bytes(r3s[which].at[pl.ds(0, n_dp - 1)], gr.at[which, 2])
        total = own[which][...]
        for slot in range(n_dp):
            total = total + r3s[which][slot].astype(F32)
        return total

    def reduce_spread(which):
        total = owner_total(which)
        if which == 0:
            rows = pl.ds(pl.multiple_of(part * (BOTTLE // 4), BOTTLE // 4), BOTTLE // 4)
            total = total - fix[0, rows, :]
            for m in range(2):
                total = total - fix[1 + m, rows, :] * back_own[m]
        mine = final_part(which, core, half_y)
        mine[...] = total
        send_all(mine, gs.at[which, 3], gr.at[which, 3], rep_peers)

    def three_parts(which):
        if which == 0:
            return r1s[0].at[0, :, pl.ds(0, 3 * CHANNELS // n_dp)]
        return r1s[which].at[pl.ds(0, 3), 0] if which < 3 else y_part(which, r1s[which], 0).at[pl.ds(0, 3)]

    def reduce_end(which):
        wait_bytes(three_parts(which), gr.at[which, 3])

    gather_end(0)
    red[...] = jnp.dot(x_v[...], fw1[...].reshape(CHANNELS, BOTTLE), preferred_element_type=F32)

    def sums_of(ref, start, width):
        def body(row, carry):
            values = grouped(ref[pl.ds(row, CHUNK), start : start + width])
            return carry[0] + jnp.sum(values, axis=0), carry[1] + jnp.sum(values * values, axis=0)

        zero = jnp.zeros((8, width), F32)
        return over_rows(body, (zero, zero))

    def joined(found):
        both = [jnp.concatenate(item, axis=1) for item in zip(*found)]
        return fold_lanes(stack_sums(micro_sum(both[0]), micro_sum(both[1])))

    def both_sums(name):
        return unstack_sums(unfold_lanes(sum_end(name)))

    sum_start("reduced", joined([sums_of(red, 0, 256)]))
    gather_turn(2)

    gy_copy.wait()
    to_rows(gy4, gy_v)
    wait_bytes(np_slots.at[pl.ds(0, n_dp - 1)], np_sems.at[1])
    np_full[...] = jnp.zeros(np_full.shape, F32)
    for d in range(n_dp):
        at = shard * d // 128
        np_full[at : at + 8, :] = np_full[at : at + 8, :] + np_slots[d]

    def vector(at, width):
        rows = [np_full[at // 128 + k : at // 128 + k + 1, :] for k in range(width // 128)]
        return jnp.concatenate(rows, axis=1) if len(rows) > 1 else rows[0]

    gain_one, bias_one = vector(0, 256), vector(256, 256)
    gain_two, bias_two = vector(512, 512), vector(1024, 512)
    gain_pool, bias_pool = vector(1536, 128), vector(1664, 128)
    bias_expand = vector(1792, 512)
    gain_three, bias_three = vector(2304, 1024), vector(3328, 1024)

    total, square = both_sums("reduced")
    center1, scale1, mul1, add1 = norm_terms(total, square, gain_one, bias_one, pixels)

    def make_active(row, carry):
        turned = grouped(red[pl.ds(row, CHUNK), :]) * mul1 + add1
        act[1, pl.ds(PAD + row, CHUNK), :] = flat(turned * sigmoid(turned))
        return carry

    over_rows(make_active, 0)
    gather_hand(1)
    gather_hand(2)
    gather_turn(3)
    place = lax.rem(lax.broadcasted_iota(jnp.int32, (CHUNK, BOTTLE), 0) // 4, SIDE)
    not_last = place != SIDE - 1
    not_first = place != 0

    def beside(side, row, distance, lanes=slice(0, BOTTLE)):
        near = act[side, pl.ds(PAD + row - 8, CHUNK + 16), lanes]
        return pltpu.roll(near, (CHUNK + 16 - distance) % (CHUNK + 16), 0)[8 : 8 + CHUNK]

    def shift_active(row, carry):
        act[2, pl.ds(PAD + row, CHUNK), :] = jnp.where(not_last, beside(1, row, 4), 0.0)
        act[0, pl.ds(PAD + row, CHUNK), :] = jnp.where(not_first, beside(1, row, -4), 0.0)
        return carry

    over_rows(shift_active, 0)

    def make_columns(row, carry):
        for tap in range(9):
            down, side = tap // 3 - 1, tap % 3
            values = act[side, pl.ds(PAD + row + 56 * down, CHUNK), :].astype(BF16)
            columns[0, pl.ds(row, CHUNK), tap * 128 : tap * 128 + 128] = values[:, 0:128]
            columns[1, pl.ds(row, CHUNK), tap * 128 : tap * 128 + 128] = values[:, 128:256]
        return carry

    over_rows(make_columns, 0)
    gather_end(1)
    own_half = n_dp // 2

    def filters(group):
        return fwc[group * own_half : (group + 1) * own_half].reshape(9 * 128, BOTTLE)

    halves2 = (slice(0, 256), slice(256, 512))
    for group, lanes in enumerate(halves2):
        wid[:, lanes] = jnp.dot(columns[group], filters(group), preferred_element_type=F32)
        sum_start(f"widened{group}", joined([sums_of(wid, group * 256, 256)]))
    sum_turn("widened0")
    sum_turn("widened1")
    gather_hand(3)

    norm2 = []
    pooled = jnp.zeros((8, BOTTLE), F32)
    for group, lanes in enumerate(halves2):
        total, square = both_sums(f"widened{group}")
        norm2.append(norm_terms(total, square, gain_two[:, lanes], bias_two[:, lanes], pixels))
        m2, a2 = norm2[group][2:4]

        def make_splits(row, carry):
            turned = grouped(wid[pl.ds(row, CHUNK), lanes]) * m2 + a2
            values = turned * sigmoid(turned)
            splits[pl.ds(row, CHUNK), lanes] = flat(values)
            return carry + jnp.sum(values, axis=0)

        pooled = over_rows(make_splits, pooled)
    pooled = image_sum(pooled) * (1.0 / (SIDE * SIDE))
    gather_end(2)
    squeeze = fes[:, :, 0:128].reshape(BOTTLE, INNER)
    ex_both = fes[:, :, 128:384]
    expand = jnp.concatenate(
        [
            ex_both[:, 0:ex_rows].reshape(INNER, 256),
            ex_both[:, ex_rows : 2 * ex_rows].reshape(INNER, 256),
        ],
        axis=1,
    )
    pre_pool = exact_dot(pooled, squeeze, False)
    sum_start("pool", stack_sums(pair_sum(pre_pool), pair_sum(pre_pool * pre_pool)))
    first_micro = lax.rem(row_ids(BOTTLE), 4) < 2

    def make_normed(row, carry):
        rows = pl.ds(row, CHUNK)
        normed = (grouped(red[rows, :]) - center1) * scale1
        dwid[rows, 0:256] = flat(jnp.where(first_micro, normed, 0.0)).astype(BF16)
        dwid[rows, 256:512] = flat(jnp.where(first_micro, 0.0, normed)).astype(BF16)
        return carry + jnp.sum(grouped(x_v[rows, :].astype(F32)), axis=0)

    image_sums = micro_sum(over_rows(make_normed, jnp.zeros((8, CHANNELS), F32)))
    sum_start(
        "images",
        jnp.concatenate(
            [
                image_sums[2 * m : 2 * m + 1, at : at + 128]
                for m in range(2)
                for at in range(0, CHANNELS, 128)
            ],
            axis=0,
        ),
    )
    normed_images = tdot(dwid[...], x_v[...]).astype(BF16)
    normed_images = normed_images.reshape(2, 2, 2, BOTTLE // 4, CHANNELS)
    for m in range(2):
        gb[:, :, m * (BOTTLE // 4) : (m + 1) * (BOTTLE // 4)] = normed_images[m]
    reduce_core(5)
    total, square = unstack_sums(sum_end("pool"))
    center_p, scale_p, mul_p, add_p = norm_terms(total, square, gain_pool, bias_pool, pictures)
    normed_p = (pre_pool - center_p) * scale_p
    norm_p = pre_pool * mul_p + add_p
    gate_p = sigmoid(norm_p)
    hidden = norm_p * gate_p
    slope_p = gate_p * (1.0 + norm_p * (1.0 - gate_p))
    logits = exact_dot(hidden, expand, False) + bias_expand
    left, right = logits[:, 0:256], logits[:, 256:512]
    most = jnp.maximum(left, right)
    left, right = jnp.exp(left - most), jnp.exp(right - most)
    att0 = left / (left + right)
    att1 = right / (left + right)

    gather_end(3)
    last = fw3[...].reshape(BOTTLE, CHANNELS)
    def make_mixed(row, carry):
        rows = pl.ds(row, CHUNK)
        values = grouped(splits[rows, 0:256]) * att0 + grouped(splits[rows, 256:512]) * att1
        mixed[rows, :] = flat(values).astype(BF16)
        return carry

    over_rows(make_mixed, 0)
    halves3 = (slice(0, 512), slice(512, 1024))
    blocks3 = [[slice(512 * h + k, 512 * h + k + 256) for k in (0, 256)] for h in range(2)]
    for half, lanes in enumerate(halves3):
        proj[:, lanes] = jnp.dot(mixed[...], last[:, lanes], preferred_element_type=F32)
        sum_start(
            f"projected{half}", joined([sums_of(proj, 512 * half + k, 256) for k in (0, 256)])
        )
    sum_turn("projected0")
    sum_turn("projected1")
    sum_turn("images")
    reduce_y(5)

    norm3 = []
    zero = jnp.zeros((8, 256), F32)
    for half, lanes in enumerate(halves3):
        total, square = both_sums(f"projected{half}")
        norm3.append(norm_terms(total, square, gain_three[:, lanes], bias_three[:, lanes], pixels))
        found = []
        for k, block in enumerate(blocks3[half]):
            c3, s3, m3, a3 = (item[:, k * 256 : k * 256 + 256] for item in norm3[half])

            def make_out(row, carry):
                rows = pl.ds(row, CHUNK)
                values = grouped(proj[rows, block])
                summed = grouped(x_v[rows, block].astype(F32)) + (values * m3 + a3)
                gate = sigmoid(summed)
                bo4[pl.ds(row // 4, CHUNK // 4), :, block] = by_four(summed * gate).astype(BF16)
                upstream = grouped(gy_v[rows, block].astype(F32)) * (
                    gate * (1.0 + summed * (1.0 - gate))
                )
                up[rows, block] = flat(upstream)
                normed = (values - c3) * s3
                return carry[0] + jnp.sum(upstream, axis=0), carry[1] + jnp.sum(
                    upstream * normed, axis=0
                )

            found.append(over_rows(make_out, (zero, zero)))
        sum_start(f"back_projected{half}", joined(found))
    bo_copy = pltpu.make_async_copy(bo4, bo_hbm, local_sem.at[2])
    bo_copy.start()

    def write_norm(at, pattern):
        at = at // 128
        both = pattern[0:1, :] + pattern[2:3, :]
        for k in range(both.shape[1] // 128):
            np_full[at + k : at + k + 1, :] = both[:, k * 128 : k * 128 + 128]

    sum_turn("back_projected0")
    sum_turn("back_projected1")
    reduce_owner(5)

    for half, lanes in enumerate(halves3):
        bias_sum, gain_sum = both_sums(f"back_projected{half}")
        write_norm(2304 + 512 * half, gain_sum)
        write_norm(3328 + 512 * half, bias_sum)
        by_value, constant = back_terms(*norm3[half][0:3], bias_sum, gain_sum, pixels)
        for k, block in enumerate(blocks3[half]):
            m3, v3, k3 = (
                item[:, k * 256 : k * 256 + 256] for item in (norm3[half][2], by_value, constant)
            )

            def make_dproj(row, carry):
                rows = pl.ds(row, CHUNK)
                values = grouped(up[rows, block]) * m3 + grouped(proj[rows, block]) * v3 + k3
                dproj[rows, block] = flat(values).astype(BF16)
                return carry

            over_rows(make_dproj, 0)
        part_mixed = dot_t(dproj[:, lanes], last[:, lanes])
        d_mixed[...] = part_mixed if half == 0 else d_mixed[...] + part_mixed

    def attend(row, carry):
        rows = pl.ds(row, CHUNK)
        values = grouped(d_mixed[rows, :])
        return (
            carry[0] + jnp.sum(values * grouped(splits[rows, 0:256]), axis=0),
            carry[1] + jnp.sum(values * grouped(splits[rows, 256:512]), axis=0),
        )

    d_att0, d_att1 = over_rows(attend, (zero, zero))
    d_att0, d_att1 = image_sum(d_att0), image_sum(d_att1)
    both = att0 * d_att0 + att1 * d_att1
    d_logits = jnp.concatenate([att0 * (d_att0 - both), att1 * (d_att1 - both)], axis=1)
    d_hidden = exact_dot(d_logits, expand, True)
    d_pool = d_hidden * slope_p
    per_micro = stack_sums(pair_sum(d_pool), pair_sum(d_pool * normed_p))
    sum_start("back_pool", per_micro)
    ex_sum = pair_sum(d_logits)
    ex_sum = ex_sum + pltpu.roll(ex_sum, 2, 0)
    ex_rows_sum = ex_sum[:, 0:128]
    for k in range(1, 4):
        ex_rows_sum = jnp.where(row_ids(128) == k, ex_sum[:, k * 128 : k * 128 + 128], ex_rows_sum)

    grad_ex = image_dot(hidden, d_logits)
    grad_ex = grad_ex.reshape(n_dp, ex_rows, 512)
    ge[:, 0:ex_rows, 128:384] = grad_ex[:, :, 0:256]
    ge[:, ex_rows : 2 * ex_rows, 128:384] = grad_ex[:, :, 256:512]
    ge[:, :, 384:512] = jnp.zeros((n_dp, 2 * ex_rows, 128), F32)
    g3[...] = tdot(mixed[...], dproj[...]).reshape(g3.shape)
    reduce_core(3)
    held = []
    for group, att in ((0, att0), (1, att1)):
        lanes = halves2[group]
        c2, s2, m2, a2 = norm2[group]

        def make_dn2(row, carry):
            rows = pl.ds(row, CHUNK)
            values = grouped(wid[rows, lanes])
            turned = values * m2 + a2
            gate = sigmoid(turned)
            slope = gate * (1.0 + turned * (1.0 - gate))
            down = grouped(d_mixed[rows, :]) * att * slope
            dn2[rows, lanes] = flat(down)
            splits[rows, lanes] = flat(slope)
            normed = (values - c2) * s2
            terms = (down, down * normed, slope, slope * normed)
            return tuple(item + jnp.sum(term, axis=0) for item, term in zip(carry, terms))

        held.append([image_sum(item) for item in over_rows(make_dn2, (zero,) * 4)])
    pool_bias_sum, pool_gain_sum = unstack_sums(sum_end("back_pool"))
    write_norm(1536, pool_gain_sum)
    write_norm(1664, pool_bias_sum)
    d_pre_pool = mul_p * (
        d_pool - pool_bias_sum * (1.0 / pictures) - normed_p * (pool_gain_sum * (1.0 / pictures))
    )
    d_pooled = exact_dot(d_pre_pool, squeeze, True) * (1.0 / (SIDE * SIDE))
    for group in range(2):
        down, down_normed, slope, slope_normed = held[group]
        payload = fold_lanes(
            stack_sums(
                pair_sum(down + d_pooled * slope), pair_sum(down_normed + d_pooled * slope_normed)
            )
        )
        if group == 1:
            payload = jnp.concatenate([payload, ex_rows_sum], axis=0)
        sum_start(f"back_widened{group}", payload)
    ge[:, :, 0:128] = image_dot(pooled, d_pre_pool).reshape(n_dp, 2 * ex_rows, 128)
    reduce_core(4)
    sum_turn("back_widened0")
    sum_turn("back_widened1")
    reduce_y(3)
    reduce_y(4)
    back_total = owner_total(5)
    back_own[0] = back_total[0 : BOTTLE // 4]
    back_own[1] = back_total[BOTTLE // 4 :]

    small_zero = jnp.zeros((8, 128), F32)
    for group, lanes in enumerate(halves2):
        whole = sum_end(f"back_widened{group}")
        if group == 1:
            np_full[14:18, :] = whole[8:12]
        bias_sum, gain_sum = unstack_sums(unfold_lanes(whole[0:8]))
        write_norm(512 + 256 * group, gain_sum)
        write_norm(1024 + 256 * group, bias_sum)
        m2 = norm2[group][2]
        v2, k2 = back_terms(*norm2[group][0:3], bias_sum, gain_sum, pixels)
        pooled_m2 = d_pooled * m2

        def make_dwid(row, carry):
            rows = pl.ds(row, CHUNK)
            values = grouped(dn2[rows, lanes]) * m2 + grouped(splits[rows, lanes]) * pooled_m2
            values = values + grouped(wid[rows, lanes]) * v2 + k2
            dwid[rows, lanes] = flat(values).astype(BF16)
            return carry

        over_rows(make_dwid, 0)
        gc[group * own_half : (group + 1) * own_half] = tdot(
            columns[group], dwid[:, lanes]
        ).reshape(own_half, 2, 9 * 128 // own_half // 2, BOTTLE)
    reduce_core(1)
    reduce_core(2)
    for group, lanes in enumerate(halves2):
        dcol[PAD : PAD + ROWS, group * 1152 : group * 1152 + 1152] = dot_t(
            dwid[:, lanes], filters(group)
        )
        inner = slice(group * 128, group * 128 + 128)

        def gather_taps(row, carry):
            for side in range(3):
                total = None
                for down in range(3):
                    at = group * 1152 + (3 * down + side) * 128
                    values = dcol[pl.ds(PAD + row - 56 * (down - 1), CHUNK), at : at + 128]
                    total = values if total is None else total + values
                act[side, pl.ds(PAD + row, CHUNK), inner] = total
            return carry

        over_rows(gather_taps, 0)
        c1, s1, m1, a1 = (item[:, inner] for item in (center1, scale1, mul1, add1))
        not_first1, not_last1 = not_first[:, inner], not_last[:, inner]

        def make_dn1(row, carry):
            rows = pl.ds(row, CHUNK)
            d_active = act[1, pl.ds(PAD + row, CHUNK), inner]
            d_active = d_active + jnp.where(not_first1, beside(2, row, -4, inner), 0.0)
            d_active = d_active + jnp.where(not_last1, beside(0, row, 4, inner), 0.0)
            values = grouped(red[rows, inner])
            turned = values * m1 + a1
            gate = sigmoid(turned)
            slope = gate * (1.0 + turned * (1.0 - gate))
            down = grouped(d_active) * slope
            dn1[rows, inner] = flat(down)
            mixed[rows, inner] = flat(down * m1).astype(BF16)
            normed = (values - c1) * s1
            return carry[0] + jnp.sum(down, axis=0), carry[1] + jnp.sum(down * normed, axis=0)

        bias_sum, gain_sum = over_rows(make_dn1, (small_zero, small_zero))
        sum_start(f"back_reduced{group}", stack_sums(micro_sum(bias_sum), micro_sum(gain_sum)))
        if group == 0:
            reduce_owner(3)
            reduce_owner(4)
    reduce_y(1)
    reduce_y(2)
    sum_turn("back_reduced0")
    g1[...] = tdot(mixed[...], x_v[...]).reshape(g1.shape)
    reduce_core(0)
    sum_turn("back_reduced1")
    reduce_owner(1)
    reduce_y(0)
    reduce_owner(2)
    found = [unstack_sums(sum_end(f"back_reduced{group}")) for group in range(2)]
    bias_sum, gain_sum = (jnp.concatenate(item, axis=1) for item in zip(*found))
    write_norm(0, gain_sum)
    write_norm(256, bias_sum)
    by_value, constant = back_terms(center1, scale1, mul1, bias_sum, gain_sum, pixels)
    def make_dred(row, carry):
        rows = pl.ds(row, CHUNK)
        values = grouped(dn1[rows, :]) * mul1 + grouped(red[rows, :]) * by_value + constant
        dred[rows, :] = flat(values).astype(BF16)
        return carry

    over_rows(make_dred, 0)
    proj[...] = dot_t(dred[...], fw1[...].reshape(CHANNELS, BOTTLE))

    by_bias = mul1 * bias_sum * (1.0 / pixels)
    by_gain = mul1 * gain_sum * (1.0 / pixels)
    image_sums = sum_end("images")
    ids = lax.broadcasted_iota(jnp.int32, (16, 128), 0)
    own_sums = [
        jnp.sum(jnp.where(ids == m * n_dp + dp, image_sums, 0.0), axis=0, keepdims=True)
        for m in range(2)
    ]
    ids = row_ids(128)
    fix[0] = row_dot(by_bias, jnp.where(ids == 0, own_sums[0], jnp.where(ids == 2, own_sums[1], 0.0)))
    for m in range(2):
        fix[1 + m] = row_dot(by_gain, jnp.where(ids == 2 * m, 1.0, 0.0))
    reduce_spread(3)
    reduce_spread(4)
    reduce_owner(0)
    reduce_spread(1)

    def make_dx(row, carry):
        for start in range(0, CHANNELS, 256):
            lanes = slice(start, start + 256)
            values = up[pl.ds(row, CHUNK), lanes] + proj[pl.ds(row, CHUNK), lanes]
            dx4[pl.ds(row // 4, CHUNK // 4), :, lanes] = values.reshape(CHUNK // 4, 4, 256)
        return carry

    over_rows(make_dx, 0)
    dx_copy = pltpu.make_async_copy(dx4, dx_hbm, local_sem.at[3])
    dx_copy.start()
    norm_rows = np_full[0:8, :]
    for d in range(1, n_dp):
        at = shard * d // 128
        norm_rows = jnp.where(dp == d, np_full[at : at + 8, :], norm_rows)
    norm_rows = pltpu.roll(norm_rows, lax.rem(128 - turn, 128), 1)
    gn_out[...] = jnp.where(lanes_id < 128 - turn, norm_rows, pltpu.roll(norm_rows, 7, 0))
    reduce_spread(2)
    reduce_spread(0)
    out_copies = [
        pltpu.make_async_copy(source, target, local_sem.at[10 + k])
        for k, (source, target) in enumerate(
            (
                (gn_out, gn_hbm),
                (fs[2], f3_hbm),
                (fs[3], fe_hbm),
                (fs[1], fc_hbm),
                (fs[0], f1_hbm),
            )
        )
    ]
    out_copies[0].start()
    for which in (3, 4, 1, 2, 0):
        reduce_end(which)
        if which != 1:
            out_copies[{3: 1, 4: 2, 2: 3, 0: 4}[which]].start()

    bo_copy.wait()
    dx_copy.wait()
    for copy in out_copies:
        copy.wait()
    for k in STATS:
        if k in DIRECT:
            wait_bytes(ar_slots_a[k].at[pl.ds(0, everyone - 1)], ar_send_a.at[order[k]])
        else:
            wait_bytes(ar_slots_a[k].at[pl.ds(0, plane_size - 1)], ar_send_a.at[order[k]])
            wait_bytes(ar_slots_b[k].at[pl.ds(0, planes - 1)], ar_send_b.at[order[k]])
    wait_bytes(np_slots.at[pl.ds(0, n_dp - 1)], np_sems.at[0])
    for which in range(4):
        wait_bytes(seven(which), ws.at[which, 0])
        for stage in range(1, 4):
            wait_bytes(quarters[which](core, half_y), ws.at[which, stage])
    for which in range(6):
        wait_bytes(r1s[which], gs.at[which, 0])
        wait_bytes(r2s[which], gs.at[which, 1])
        wait_bytes(r3s[which].at[pl.ds(0, n_dp - 1)], gs.at[which, 2])
        if which < 5:
            wait_bytes(three_parts(which), gs.at[which, 3])


def update_kernel(*refs):
    sources, targets = refs[0:25], refs[25:45]
    inputs, outs, through = refs[45:68], refs[68:86], refs[86:88]
    pass_sems, in_sems, out_sems = refs[88:91]
    fetching, passing = [], []
    half = SIDE * SIDE // 2
    for number, (which, at, count) in enumerate(((1, 0, half), (1, half, half), (0, 0, 2 * half))):
        rows = pl.ds(at, count)
        fetching.append(
            pltpu.make_async_copy(
                sources[which].at[rows], through[which].at[rows], pass_sems.at[0, number]
            )
        )
        passing.append(
            pltpu.make_async_copy(
                through[which].at[rows], targets[which].at[rows], pass_sems.at[1, number]
            )
        )
    for copy in fetching:
        copy.start()
    coming = [
        pltpu.make_async_copy(source, held, in_sems.at[k])
        for k, (source, held) in enumerate(zip(sources[2:], inputs))
    ]
    for copy in coming:
        copy.start()
    grads, states = inputs[0:5], inputs[5:23]
    going = [
        pltpu.make_async_copy(held, target, out_sems.at[k])
        for k, (held, target) in enumerate(zip(outs, targets[2:]))
    ]
    ex_rows = states[9].shape[0]
    shard = states[15].shape[0]
    fans = (CHANNELS, 9 * BOTTLE // RADIX, BOTTLE, INNER // 8, BOTTLE)
    for copy in coming[0:5]:
        copy.wait()
    found = (
        grads[0][...].T,
        grads[1][...],
        grads[3][:, 0:128],
        jnp.concatenate([grads[3][0:ex_rows, 128:384], grads[3][ex_rows:, 128:384]], axis=1),
        grads[2][...],
    )
    for order, k in enumerate((3, 2, 4, 0, 1)):
        for copy in coming[5 + 3 * k : 8 + 3 * k]:
            copy.wait()
        new = adamw(
            states[3 * k][...],
            states[3 * k + 1][...],
            states[3 * k + 2][...],
            found[k],
            2.0 * fans[k] ** (-0.5),
            DECAY,
        )
        for j in range(3):
            outs[3 * k + j][...] = new[j]
            going[3 * k + j].start()
        if order < 3:
            fetching[order].wait()
            passing[order].start()
    for copy in coming[20:23]:
        copy.wait()
    for at in range(0, shard, 128):
        width = min(128, shard - at)
        lanes = pl.ds(at, width)
        new = adamw(
            *[states[15 + j][lanes].reshape(1, width) for j in range(3)],
            grads[4][at // 128 : at // 128 + 1, 0:width],
            NORM_RATE,
            0.0,
        )
        for j in range(3):
            outs[15 + j][lanes] = new[j].reshape(width)
    for copy in going[15:18]:
        copy.start()
    for copy in passing + going:
        copy.wait()


def fused_device(
    images,
    out_grad,
    reduce_weight,
    reduce_moment,
    reduce_second,
    conv_weight,
    conv_moment,
    conv_second,
    squeeze_weight,
    squeeze_moment,
    squeeze_second,
    expand_weight,
    expand_moment,
    expand_second,
    project_weight,
    project_moment,
    project_second,
    norm_params,
    norm_moment,
    norm_second,
):
    n_dp, n_rep = lax.axis_size("dp"), lax.axis_size("rep")
    by_pixel = lambda values: jnp.transpose(values, (1, 2, 0, 3)).reshape(-1, 4, CHANNELS)
    qc = conv_weight.shape[0] // 2
    q1 = reduce_weight.shape[0] // 4
    pe = squeeze_weight.shape[0]
    vmem = pltpu.VMEM
    pixel_form = (SIDE * SIDE, 4, CHANNELS)
    scratch = [
        *[
            vmem(values.shape, F32)
            for values in (
                reduce_weight,
                conv_weight,
                squeeze_weight,
                expand_weight,
                project_weight,
                norm_params,
            )
        ],
        vmem((8, 128), F32),
        vmem(pixel_form, BF16),
        vmem(pixel_form, BF16),
        vmem((ROWS, CHANNELS), BF16),
        vmem((ROWS, CHANNELS), BF16),
        vmem((n_dp, 2, 2, q1, BOTTLE), BF16),
        vmem((n_dp, 2, qc, BOTTLE), BF16),
        vmem((n_dp, pe, 512), BF16),
        vmem((n_dp, pe, CHANNELS), BF16),
        vmem((pe, 512), BF16),
        vmem((n_dp, 8, 128), F32),
        vmem((40, 128), F32),
        vmem((ROWS, BOTTLE), F32),
        vmem((3, ROWS + 2 * PAD, BOTTLE), F32),
        vmem((2, ROWS, 9 * 128), BF16),
        vmem((ROWS, 512), F32),
        vmem((ROWS, 512), F32),
        vmem((ROWS, BOTTLE), BF16),
        vmem((ROWS, CHANNELS), F32),
        vmem((ROWS, CHANNELS), F32),
        vmem(pixel_form, BF16),
        vmem(pixel_form, F32),
        vmem((ROWS, CHANNELS), BF16),
        vmem((ROWS, BOTTLE), F32),
        vmem((ROWS, 512), F32),
        vmem((ROWS, 512), BF16),
        vmem((ROWS + 2 * PAD, 2 * 9 * 128), F32),
        vmem((ROWS, BOTTLE), F32),
        vmem((ROWS, BOTTLE), BF16),
        vmem((2, 2, BOTTLE // 4, CHANNELS), F32),
        vmem((n_dp, 2, qc, BOTTLE), F32),
        vmem((n_dp, pe, CHANNELS), F32),
        vmem((n_dp, pe, 512), F32),
        vmem((2, 2, BOTTLE // 2, CHANNELS), BF16),
        vmem((3, BOTTLE, CHANNELS // n_dp), F32),
        vmem((2, BOTTLE // 4, CHANNELS // n_dp), F32),
    ]
    direct = n_dp * n_rep
    scratch += [
        vmem((direct if k in DIRECT else 2 * n_rep,) + shape, F32) for k, shape in STATS.items()
    ]
    scratch += [vmem((n_dp // 2,) + shape, F32) for shape in STATS.values()]
    cut = 64
    lanes1 = CHANNELS // n_dp
    half = [
        (2, BOTTLE // 4, CHANNELS),
        (n_dp, 2, cut, 128),
        (n_dp, 2, qc - cut, 128),
        (n_dp, pe, 512),
        (n_dp, pe, 256),
        (2, BOTTLE // 2, CHANNELS),
    ]
    quarter = [
        (BOTTLE // 4, CHANNELS),
        (n_dp, cut, 128),
        (n_dp, qc - cut, 128),
        (n_dp, pe, 256),
        (n_dp, pe, 128),
        (BOTTLE // 2, CHANNELS),
    ]
    final = [(2, 2, BOTTLE // 4, lanes1), (2, qc, BOTTLE), (pe, CHANNELS), (pe, 512)]
    sent = [BF16, BF16, BF16, BF16, F32, BF16]
    scratch += [vmem(shape, F32) for shape in half[:-1]] + [vmem(half[-1], BF16)]
    scratch += [vmem(shape, kind) for shape, kind in zip(quarter, sent)] * 3
    owned = [(BOTTLE // 4, lanes1)] + [shape[1:] for shape in quarter[1:-1]]
    owned += [(BOTTLE // 2, lanes1)]
    scratch += [vmem((n_dp,) + shape, kind) for shape, kind in zip(owned, sent)]
    scratch += [vmem(shape, F32) for shape in owned]
    scratch += [vmem(shape, F32) for shape in final]
    dma = pltpu.SemaphoreType.DMA
    scratch += [dma((15,))] + [dma((len(STATS),))] * 4 + [dma((2,))] + [dma((4, 4))] * 2 + [dma((6, 4))] * 2
    any_space = pl.BlockSpec(memory_space=pl.ANY)
    block_out, images_grad, sum1, sumc, sum3, sume, norm_grads = pl.pallas_call(
        functools.partial(block_kernel, n_dp, n_rep),
        out_shape=[
            jax.ShapeDtypeStruct(pixel_form, BF16),
            jax.ShapeDtypeStruct(pixel_form, F32),
            *[jax.ShapeDtypeStruct(shape, F32) for shape in final],
            jax.ShapeDtypeStruct((8, 128), F32),
        ],
        in_specs=[any_space] * 8,
        out_specs=[any_space] * 7,
        scratch_shapes=scratch,
        compiler_params=pltpu.CompilerParams(
            collective_id=0, has_side_effects=True, vmem_limit_bytes=63 * 1024 * 1024
        ),
    )(
        by_pixel(images),
        by_pixel(out_grad),
        reduce_weight,
        conv_weight,
        squeeze_weight,
        expand_weight,
        project_weight,
        norm_params,
    )
    states = (
        reduce_weight,
        reduce_moment,
        reduce_second,
        conv_weight,
        conv_moment,
        conv_second,
        squeeze_weight,
        squeeze_moment,
        squeeze_second,
        expand_weight,
        expand_moment,
        expand_second,
        project_weight,
        project_moment,
        project_second,
    )
    held = (*states, norm_params, norm_moment, norm_second)
    sums = (
        sum1.reshape(BOTTLE, lanes1),
        sumc.reshape(conv_weight.shape),
        sum3,
        sume,
        norm_grads,
    )
    block_out, images_grad, *updated = pl.pallas_call(
        update_kernel,
        out_shape=[
            jax.ShapeDtypeStruct(pixel_form, BF16),
            jax.ShapeDtypeStruct(pixel_form, F32),
            *[jax.ShapeDtypeStruct(state.shape, F32) for state in held],
        ],
        in_specs=[any_space] * 25,
        out_specs=[any_space] * 20,
        scratch_shapes=[vmem(values.shape, F32) for values in (*sums, *held, *held)]
        + [vmem(pixel_form, BF16), vmem(pixel_form, F32)]
        + [dma((2, 3)), dma((23,)), dma((18,))],
        compiler_params=pltpu.CompilerParams(vmem_limit_bytes=63 * 1024 * 1024),
    )(block_out, images_grad, *sums, *held)
    by_image = lambda values: jnp.transpose(
        values.reshape(SIDE, SIDE, images.shape[0], CHANNELS), (2, 0, 1, 3)
    )
    return (
        by_image(block_out),
        by_image(images_grad),
        *updated,
    )


def solution(mesh):
    placed = (
        P(("dp", "rep"), None, None, None),
        P(("dp", "rep"), None, None, None),
        P("dp", None),
        P("dp", None),
        P("dp", None),
        P("dp", None),
        P("dp", None),
        P("dp", None),
        P("dp", None),
        P("dp", None),
        P("dp", None),
        P("dp", None),
        P("dp", None),
        P("dp", None),
        P("dp", None),
        P("dp", None),
        P("dp", None),
        P("dp"),
        P("dp"),
        P("dp"),
    )
    n_dp, n_rep = mesh.shape["dp"], mesh.shape["rep"]
    whole_tiles = n_rep == 4 and n_dp % 2 == 0 and INNER % (16 * n_dp) == 0
    return jax.shard_map(
        fused_device if whole_tiles else per_device,
        mesh=mesh,
        in_specs=placed,
        out_specs=(
            P(("dp", "rep"), None, None, None),
            P(("dp", "rep"), None, None, None),
            P("dp", None),
            P("dp", None),
            P("dp", None),
            P("dp", None),
            P("dp", None),
            P("dp", None),
            P("dp", None),
            P("dp", None),
            P("dp", None),
            P("dp", None),
            P("dp", None),
            P("dp", None),
            P("dp", None),
            P("dp", None),
            P("dp", None),
            P("dp"),
            P("dp"),
            P("dp"),
        ),
        check_vma=False,
    )
```

```python
import functools
import jax
import jax.numpy as jnp
from jax import lax
from jax.experimental import pallas as pl
from jax.experimental.pallas import tpu as pltpu
from jax.sharding import PartitionSpec as P

CHANNELS = 1024
BOTTLE = 256
INNER = 128
RADIX = 2
SIDE = 14
MICRO = 2
STEP = 10


EPSILON = 1e-05
PRECISE = lax.Precision.HIGHEST
BETA_ONE = 0.9
BETA_TWO = 0.999
ADAM_EPSILON = 1e-08
DECAY = 0.01
NORM_RATE = 0.8
ROWS = 4 * SIDE * SIDE
NORM_WIDTH = 4352


def split_params(packed):
    widths = (
        BOTTLE,
        BOTTLE,
        RADIX * BOTTLE,
        RADIX * BOTTLE,
        INNER,
        INNER,
        RADIX * BOTTLE,
        CHANNELS,
        CHANNELS,
    )
    pieces = []
    offset = 0
    for segment in widths:
        pieces.append(lax.slice_in_dim(packed, offset, offset + segment))
        offset = offset + segment
    return pieces


def silu_slope(values):
    logistic = jax.nn.sigmoid(values)
    return logistic * (1.0 + values * (1.0 - logistic))


def norm_forward(values, gain, bias, count):
    flat = values.reshape(-1, values.shape[-1])
    total, square = lax.psum((jnp.sum(flat, axis=0), jnp.sum(flat * flat, axis=0)), ("dp", "rep"))
    center = total / count
    scale = lax.rsqrt(square / count - center * center + EPSILON)
    normed = (values - center) * scale
    return (normed * gain + bias, normed, scale)


def norm_backward(upstream, normed, scale, gain, count):
    flat_up = upstream.reshape(-1, upstream.shape[-1])
    flat_norm = normed.reshape(-1, normed.shape[-1])
    bias_sum, gain_sum = lax.psum(
        (jnp.sum(flat_up, axis=0), jnp.sum(flat_up * flat_norm, axis=0)), ("dp", "rep")
    )
    downstream = gain * scale * (upstream - bias_sum / count - normed * (gain_sum / count))
    return (downstream, gain_sum, bias_sum)


def patches(active):
    padded = jnp.pad(active, ((0, 0), (1, 1), (1, 1), (0, 0), (0, 0)))
    shifted = [
        padded[:, down_step : down_step + SIDE, side_step : side_step + SIDE]
        for down_step in range(3)
        for side_step in range(3)
    ]
    return jnp.stack(shifted, axis=4)


def unpatch(columns):
    total = jnp.zeros(
        (columns.shape[0], SIDE + 2, SIDE + 2, columns.shape[3], columns.shape[5]), jnp.float32
    )
    for down_step in range(3):
        for side_step in range(3):
            piece = columns[:, :, :, :, 3 * down_step + side_step]
            total = total + jnp.pad(
                piece,
                ((0, 0), (down_step, 2 - down_step), (side_step, 2 - side_step), (0, 0), (0, 0)),
            )
    return total[:, 1 : SIDE + 1, 1 : SIDE + 1]


def adamw(param, moment, second, gradient, rate, decay):
    moment_new = BETA_ONE * moment + (1.0 - BETA_ONE) * gradient
    second_new = BETA_TWO * second + (1.0 - BETA_TWO) * gradient * gradient
    ratio = (
        moment_new
        / (1.0 - BETA_ONE**STEP)
        / (jnp.sqrt(second_new / (1.0 - BETA_TWO**STEP)) + ADAM_EPSILON)
    )
    return (param - rate * (ratio + decay * param), moment_new, second_new)


def per_device(
    images,
    out_grad,
    reduce_weight,
    reduce_moment,
    reduce_second,
    conv_weight,
    conv_moment,
    conv_second,
    squeeze_weight,
    squeeze_moment,
    squeeze_second,
    expand_weight,
    expand_moment,
    expand_second,
    project_weight,
    project_moment,
    project_second,
    norm_params,
    norm_moment,
    norm_second,
):
    bf16 = jnp.bfloat16
    low_reduce = reduce_weight.astype(bf16)
    low_conv = conv_weight.astype(bf16)
    low_squeeze = squeeze_weight.astype(bf16)
    low_expand = expand_weight.astype(bf16)
    low_project = project_weight.astype(bf16)
    low_norm = norm_params.astype(bf16)
    devices = lax.axis_size("dp") * lax.axis_size("rep")
    per_batch = images.shape[0] // MICRO
    pixel_count = float(per_batch * SIDE * SIDE * devices)
    image_count = float(per_batch * devices)
    group_in = BOTTLE // RADIX
    grad_first = jnp.zeros((CHANNELS, BOTTLE), jnp.float32)
    grad_conv = jnp.zeros((RADIX, 9 * group_in, BOTTLE), jnp.float32)
    grad_squeeze = jnp.zeros((BOTTLE, INNER), jnp.float32)
    grad_expand = jnp.zeros((INNER, RADIX * BOTTLE), jnp.float32)
    grad_last = jnp.zeros((BOTTLE, CHANNELS), jnp.float32)
    grad_norms = jnp.zeros(
        (2 * BOTTLE + 3 * RADIX * BOTTLE + 2 * INNER + 2 * CHANNELS,), jnp.float32
    )
    outputs = []
    input_grads = []
    for number in range(MICRO):
        forward_set = (
            lax.all_gather(low_reduce, "dp", axis=0, tiled=True),
            lax.all_gather(low_conv, "dp", axis=0, tiled=True),
            lax.all_gather(low_squeeze, "dp", axis=0, tiled=True),
            lax.all_gather(low_expand, "dp", axis=0, tiled=True),
            lax.all_gather(low_project, "dp", axis=0, tiled=True),
            lax.all_gather(low_norm, "dp", axis=0, tiled=True),
        )
        first, conv, squeeze, expand, last, packed = forward_set
        (
            gain_one,
            bias_one,
            gain_two,
            bias_two,
            gain_pool,
            bias_pool,
            bias_expand,
            gain_three,
            bias_three,
        ) = split_params(packed.astype(jnp.float32))
        batched = images[number * per_batch : (number + 1) * per_batch]
        cotangent = out_grad[number * per_batch : (number + 1) * per_batch]
        reduced = jnp.einsum("nhwc,cb->nhwb", batched, first, preferred_element_type=jnp.float32)
        norm_one, normed_one, scale_one = norm_forward(reduced, gain_one, bias_one, pixel_count)
        active = jax.nn.silu(norm_one).astype(bf16)
        columns = patches(active.reshape(per_batch, SIDE, SIDE, RADIX, group_in)).reshape(
            per_batch * SIDE * SIDE, RADIX, 9 * group_in
        )
        conv_grouped = conv.reshape(RADIX, 9 * group_in, BOTTLE)
        widened = jnp.einsum(
            "prk,rko->pro", columns, conv_grouped, preferred_element_type=jnp.float32
        )
        widened = widened.reshape(per_batch, SIDE, SIDE, RADIX * BOTTLE)
        norm_two, normed_two, scale_two = norm_forward(widened, gain_two, bias_two, pixel_count)
        splits = jax.nn.silu(norm_two).reshape(per_batch, SIDE, SIDE, RADIX, BOTTLE)
        pooled = jnp.sum(jnp.sum(splits, axis=3), axis=(1, 2)) / (SIDE * SIDE)
        squeeze_float = squeeze.astype(jnp.float32)
        expand_float = expand.astype(jnp.float32)
        pre_pool = jnp.dot(pooled, squeeze_float, precision=PRECISE)
        norm_pool, normed_pool, scale_pool = norm_forward(
            pre_pool, gain_pool, bias_pool, image_count
        )
        hidden = jax.nn.silu(norm_pool)
        logits = (jnp.dot(hidden, expand_float, precision=PRECISE) + bias_expand).reshape(
            per_batch, RADIX, BOTTLE
        )
        attention = jax.nn.softmax(logits, axis=1)
        mixed = jnp.sum(splits * attention[:, None, None], axis=3).astype(bf16)
        projected = jnp.einsum("nhwb,bc->nhwc", mixed, last, preferred_element_type=jnp.float32)
        norm_three, normed_three, scale_three = norm_forward(
            projected, gain_three, bias_three, pixel_count
        )
        summed = batched.astype(jnp.float32) + norm_three
        outputs.append(jax.nn.silu(summed).astype(bf16))
        backward_set = (
            lax.all_gather(low_reduce, "dp", axis=0, tiled=True),
            lax.all_gather(low_conv, "dp", axis=0, tiled=True),
            lax.all_gather(low_squeeze, "dp", axis=0, tiled=True),
            lax.all_gather(low_expand, "dp", axis=0, tiled=True),
            lax.all_gather(low_project, "dp", axis=0, tiled=True),
            lax.all_gather(low_norm, "dp", axis=0, tiled=True),
        )
        first, conv, squeeze, expand, last, packed = backward_set
        gains_back = split_params(packed.astype(jnp.float32))
        conv_grouped = conv.reshape(RADIX, 9 * group_in, BOTTLE)
        expand_float = expand.astype(jnp.float32)
        squeeze_float = squeeze.astype(jnp.float32)
        upstream = cotangent.astype(jnp.float32) * silu_slope(summed)
        d_projected, gain_three_grad, bias_three_grad = norm_backward(
            upstream, normed_three, scale_three, gains_back[7], pixel_count
        )
        d_projected_low = d_projected.astype(bf16)
        grad_last = grad_last + jnp.einsum(
            "nhwb,nhwc->bc", mixed, d_projected_low, preferred_element_type=jnp.float32
        )
        d_mixed = jnp.einsum(
            "nhwc,bc->nhwb", d_projected_low, last, preferred_element_type=jnp.float32
        )
        d_splits = d_mixed[:, :, :, None] * attention[:, None, None]
        d_attention = jnp.sum(d_mixed[:, :, :, None] * splits, axis=(1, 2))
        d_logits = attention * (
            d_attention - jnp.sum(attention * d_attention, axis=1, keepdims=True)
        )
        flat_logits = d_logits.reshape(per_batch, RADIX * BOTTLE)
        grad_expand = grad_expand + jnp.dot(hidden.T, flat_logits, precision=PRECISE)
        d_hidden = jnp.dot(flat_logits, expand_float.T, precision=PRECISE)
        d_pool_norm = d_hidden * silu_slope(norm_pool)
        pool_bias_sum, pool_gain_sum, expand_bias_sum = lax.psum(
            (
                jnp.sum(d_pool_norm, axis=0),
                jnp.sum(d_pool_norm * normed_pool, axis=0),
                jnp.sum(flat_logits, axis=0),
            ),
            ("dp", "rep"),
        )
        d_pre_pool = (
            gains_back[4]
            * scale_pool
            * (
                d_pool_norm
                - pool_bias_sum / image_count
                - normed_pool * (pool_gain_sum / image_count)
            )
        )
        grad_squeeze = grad_squeeze + jnp.dot(pooled.T, d_pre_pool, precision=PRECISE)
        d_pooled = jnp.dot(d_pre_pool, squeeze_float.T, precision=PRECISE)
        d_splits = d_splits + (d_pooled / (SIDE * SIDE))[:, None, None, None, :]
        d_norm_two = d_splits.reshape(per_batch, SIDE, SIDE, RADIX * BOTTLE) * silu_slope(norm_two)
        d_widened, gain_two_grad, bias_two_grad = norm_backward(
            d_norm_two, normed_two, scale_two, gains_back[2], pixel_count
        )
        d_widened_low = d_widened.astype(bf16).reshape(per_batch * SIDE * SIDE, RADIX, BOTTLE)
        grad_conv = grad_conv + jnp.einsum(
            "prk,pro->rko", columns, d_widened_low, preferred_element_type=jnp.float32
        )
        d_columns = jnp.einsum(
            "pro,rko->prk", d_widened_low, conv_grouped, preferred_element_type=jnp.float32
        )
        d_active = unpatch(d_columns.reshape(per_batch, SIDE, SIDE, RADIX, 9, group_in)).reshape(
            per_batch, SIDE, SIDE, BOTTLE
        )
        d_norm_one = d_active * silu_slope(norm_one)
        d_reduced, gain_one_grad, bias_one_grad = norm_backward(
            d_norm_one, normed_one, scale_one, gains_back[0], pixel_count
        )
        d_reduced_low = d_reduced.astype(bf16)
        grad_first = grad_first + jnp.einsum(
            "nhwc,nhwb->cb", batched, d_reduced_low, preferred_element_type=jnp.float32
        )
        input_grads.append(
            upstream
            + jnp.einsum("nhwb,cb->nhwc", d_reduced_low, first, preferred_element_type=jnp.float32)
        )
        grad_norms = grad_norms + jnp.concatenate(
            [
                gain_one_grad,
                bias_one_grad,
                gain_two_grad,
                bias_two_grad,
                pool_gain_sum,
                pool_bias_sum,
                expand_bias_sum,
                gain_three_grad,
                bias_three_grad,
            ]
        )
    grad_conv = grad_conv.reshape(9 * BOTTLE, BOTTLE)
    partial_value = (
        lax.psum_scatter(grad_first, "dp", scatter_dimension=0, tiled=True),
        lax.psum_scatter(grad_conv, "dp", scatter_dimension=0, tiled=True),
        lax.psum_scatter(grad_squeeze, "dp", scatter_dimension=0, tiled=True),
        lax.psum_scatter(grad_expand, "dp", scatter_dimension=0, tiled=True),
        lax.psum_scatter(grad_last, "dp", scatter_dimension=0, tiled=True),
    )
    owned = lax.psum(
        (partial_value[0], partial_value[1], partial_value[2], partial_value[3], partial_value[4]),
        "rep",
    )
    shard_length = norm_params.shape[0]
    norm_grad_owned = lax.dynamic_slice_in_dim(
        grad_norms, lax.axis_index("dp") * shard_length, shard_length
    )
    reduce_new = adamw(
        reduce_weight, reduce_moment, reduce_second, owned[0], 2.0 * CHANNELS ** (-0.5), DECAY
    )
    conv_new = adamw(
        conv_weight,
        conv_moment,
        conv_second,
        owned[1],
        2.0 * (9 * BOTTLE // RADIX) ** (-0.5),
        DECAY,
    )
    squeeze_new = adamw(
        squeeze_weight, squeeze_moment, squeeze_second, owned[2], 2.0 * BOTTLE ** (-0.5), DECAY
    )
    expand_new = adamw(
        expand_weight, expand_moment, expand_second, owned[3], 2.0 * (INNER // 8) ** (-0.5), DECAY
    )
    project_new = adamw(
        project_weight, project_moment, project_second, owned[4], 2.0 * BOTTLE ** (-0.5), DECAY
    )
    norm_new = adamw(norm_params, norm_moment, norm_second, norm_grad_owned, NORM_RATE, 0.0)
    return (
        jnp.concatenate(outputs, axis=0),
        jnp.concatenate(input_grads, axis=0),
        reduce_new[0],
        reduce_new[1],
        reduce_new[2],
        conv_new[0],
        conv_new[1],
        conv_new[2],
        squeeze_new[0],
        squeeze_new[1],
        squeeze_new[2],
        expand_new[0],
        expand_new[1],
        expand_new[2],
        project_new[0],
        project_new[1],
        project_new[2],
        norm_new[0],
        norm_new[1],
        norm_new[2],
    )


MESH = pl.DeviceIdType.MESH
PAD = 64
CHUNK = 112
F32 = jnp.float32
BF16 = jnp.bfloat16
STATS = {
    "reduced": (8, 128),
    "widened0": (8, 128),
    "widened1": (8, 128),
    "pool": (8, 128),
    "images": (16, 128),
    "projected0": (8, 256),
    "projected1": (8, 256),
    "back_projected0": (8, 256),
    "back_projected1": (8, 256),
    "back_pool": (8, 128),
    "back_widened0": (8, 128),
    "back_widened1": (16, 128),
    "back_reduced0": (8, 128),
    "back_reduced1": (8, 128),
}
DIRECT = ("reduced", "pool", "back_pool")


def sigmoid(values):
    return 0.5 * jnp.tanh(0.5 * values) + 0.5


def row_ids(width):
    return lax.broadcasted_iota(jnp.int32, (8, width), 0)


def image_sum(rows):
    return rows + pltpu.roll(rows, 4, 0)


def pair_sum(rows):
    even = row_ids(rows.shape[1]) % 2 == 0
    return rows + jnp.where(even, pltpu.roll(rows, 7, 0), pltpu.roll(rows, 1, 0))


def micro_sum(rows):
    return pair_sum(image_sum(rows))


def stack_sums(first, second):
    return jnp.where(row_ids(first.shape[1]) < 4, first, second)


def unstack_sums(stacked):
    upper = row_ids(stacked.shape[1]) < 4
    turned = pltpu.roll(stacked, 4, 0)
    return jnp.where(upper, stacked, turned), jnp.where(upper, turned, stacked)


def fold_lanes(stacked):
    half = stacked.shape[1] // 2
    even = row_ids(half) % 2 == 0
    return jnp.where(even, stacked[:, :half], stacked[:, half:])


def unfold_lanes(folded):
    even = row_ids(folded.shape[1]) % 2 == 0
    left = jnp.where(even, folded, pltpu.roll(folded, 1, 0))
    right = jnp.where(even, pltpu.roll(folded, 7, 0), folded)
    return jnp.concatenate([left, right], axis=1)


def norm_terms(total, square, gain, bias, count):
    center = total * (1.0 / count)
    scale = lax.rsqrt(square * (1.0 / count) - center * center + EPSILON)
    slope = scale * gain
    return center, scale, slope, bias - center * slope


def back_terms(center, scale, slope, bias_sum, gain_sum, count):
    by_value = -slope * scale * (gain_sum * (1.0 / count))
    constant = -slope * (bias_sum * (1.0 / count)) - by_value * center
    return by_value, constant


def tdot(left, right):
    return lax.dot_general(left, right, (((0,), (0,)), ((), ())), preferred_element_type=F32)


def dot_t(left, right):
    return lax.dot_general(left, right, (((1,), (1,)), ((), ())), preferred_element_type=F32)


def in_parts(values, parts):
    found = []
    for _ in range(parts):
        rounded = values.astype(BF16).astype(F32)
        found.append(rounded)
        values = values - rounded
    return found


def exact_dot(left, right, transposed):
    stacked = jnp.concatenate(in_parts(left, 3), axis=0).astype(BF16)
    wide = dot_t(stacked, right) if transposed else jnp.dot(stacked, right, preferred_element_type=F32)
    return wide[0:8] + wide[8:16] + wide[16:24]


def row_dot(left, right):
    high, low = in_parts(left, 2)
    other_high, other_low = in_parts(right, 2)
    return tdot(
        jnp.concatenate([high, high, low, low], axis=0).astype(BF16),
        jnp.concatenate([other_high, other_low, other_high, other_low], axis=0).astype(BF16),
    )


def image_dot(left, right):
    return row_dot(jnp.where(row_ids(left.shape[1]) < 4, left, 0.0), right)


def block_kernel(
    n_dp,
    n_rep,
    x_hbm,
    gy_hbm,
    w1_hbm,
    wc_hbm,
    sq_hbm,
    ex_hbm,
    w3_hbm,
    np_hbm,
    bo_hbm,
    dx_hbm,
    f1_hbm,
    fc_hbm,
    f3_hbm,
    fe_hbm,
    gn_hbm,
    w1_own,
    wc_own,
    sq_own,
    ex_own,
    w3_own,
    np_own,
    gn_out,
    x4,
    gy4,
    x_v,
    gy_v,
    fw1,
    fwc,
    fes,
    fw3,
    es_own,
    np_slots,
    np_full,
    red,
    act,
    columns,
    wid,
    splits,
    mixed,
    proj,
    up,
    bo4,
    dx4,
    dproj,
    d_mixed,
    dn2,
    dwid,
    dcol,
    dn1,
    dred,
    g1,
    gc,
    g3,
    ge,
    gb,
    fix,
    back_own,
    *rest,
):
    n_ar = len(STATS)
    order = {name: k for k, name in enumerate(STATS)}
    ar_slots_a = dict(zip(STATS, rest[0:n_ar]))
    ar_slots_b = dict(zip(STATS, rest[n_ar : 2 * n_ar]))
    rest = rest[2 * n_ar :]
    r1s, ys, r2s, ks, r3s, own = (rest[6 * i : 6 * i + 6] for i in range(6))
    fs = rest[36:40]
    rest = rest[40:]
    local_sem, ar_send_a, ar_recv_a, ar_send_b, ar_recv_b, np_sems, ws, wr, gs, gr = rest

    dp = lax.axis_index("dp")
    rep = lax.axis_index("rep")
    core = lax.rem(rep, 2)
    half_y = lax.div(rep, 2)
    planes = n_dp // 2
    plane_size = 2 * n_rep
    plane = lax.div(dp, 2)
    in_plane = lax.rem(dp, 2) * n_rep + rep
    sibling = (dp, half_y * 2 + (1 - core))
    across = (dp, (1 - half_y) * 2 + core)
    pixels = float(SIDE * SIDE * 2 * n_dp * n_rep)
    pictures = float(2 * n_dp * n_rep)

    x = lax.rem(dp, 2)
    if planes == 4:
        upper = lax.div(plane, 2)
        other_planes = [3 - 3 * upper, 2 - upper, 1 - plane + 4 * upper]
    else:
        other_planes = [lax.rem(plane + step, planes) for step in range(1, planes)]
    flips = ((1, 1, 1), (1, 1, 0), (1, 0, 1), (1, 0, 0), (0, 1, 1), (0, 1, 0), (0, 0, 1), (0, 0, 0))

    def of_flip(z, flip):
        there = [1 - own if turn else own for own, turn in zip((x, half_y, core), flip)]
        return (z * 2 + there[0], there[1] * 2 + there[2])

    plane_peers = [of_flip(plane, flip) for flip in flips[:-1]]
    column_peers = [of_flip(z, flips[-1]) for z in other_planes]
    owner_peers = [of_flip(z, flip) for z in other_planes for flip in (flips[3], flips[7])]
    owner_peers += [of_flip(plane, flips[3])]
    all_peers = [of_flip(z, flip) for z in other_planes for flip in flips] + plane_peers
    me, everyone = dp * n_rep + rep, n_dp * n_rep
    rep_peers = [(dp, lax.rem(rep + step, n_rep)) for step in range(1, n_rep)]

    def remote(src, dst, send_sem, recv_sem, device):
        return pltpu.make_async_remote_copy(
            src_ref=src,
            dst_ref=dst,
            send_sem=send_sem,
            recv_sem=recv_sem,
            device_id=device,
            device_id_type=MESH,
        )

    def send_all(ref, send_sem, recv_sem, peers):
        for device in peers:
            remote(ref, ref, send_sem, recv_sem, device).start()

    def wait_bytes(ref, sem):
        pltpu.make_async_copy(ref, ref, sem).wait()

    def over_rows(body, init):
        def step(index, carry):
            return body(pl.multiple_of(index * CHUNK, CHUNK), carry)

        return lax.fori_loop(0, ROWS // CHUNK, step, init)

    def grouped(values):
        return values.reshape(CHUNK // 8, 8, values.shape[-1])

    def by_four(values):
        return flat(values).reshape(CHUNK // 4, 4, values.shape[-1])

    def flat(values):
        return values.reshape(CHUNK, values.shape[-1])

    own_copies = [
        pltpu.make_async_copy(source, target, local_sem.at[4 + k])
        for k, (source, target) in enumerate(
            (
                (w1_hbm, w1_own),
                (np_hbm, np_own),
                (wc_hbm, wc_own),
                (w3_hbm, w3_own),
                (sq_hbm, sq_own),
                (ex_hbm, ex_own),
            )
        )
    ]
    for copy in own_copies:
        copy.start()
    x_copy = pltpu.make_async_copy(x_hbm, x4, local_sem.at[0])
    gy_copy = pltpu.make_async_copy(gy_hbm, gy4, local_sem.at[1])
    x_copy.start()
    barrier = pltpu.get_barrier_semaphore()
    for device in all_peers:
        pl.semaphore_signal(barrier, inc=1, device_id=device, device_id_type=MESH)

    part = core * 2 + half_y
    own_copies[0].wait()
    q1 = w1_own.shape[0] // 4
    fw1[dp, core, half_y] = w1_own[pl.ds(pl.multiple_of(part * q1, q1), q1), :].astype(BF16)
    core_lanes = pl.ds(pl.multiple_of(core * 128, 128), 128)
    es_lanes = pl.ds(pl.multiple_of(part * 128, 128), 128)
    w3_lanes = pl.ds(pl.multiple_of(part * 256, 128), 256)

    pl.semaphore_wait(barrier, everyone - 1)

    def quarter_w1(c, y):
        return fw1.at[:, c, y]

    def quarter_wc(c, y):
        return fwc.at[:, y, :, pl.ds(pl.multiple_of(c * 128, 128), 128)]

    def quarter_es(c, y):
        return fes.at[:, :, pl.ds(pl.multiple_of((c * 2 + y) * 128, 128), 128)]

    def quarter_w3(c, y):
        return fw3.at[:, :, pl.ds(pl.multiple_of((c * 2 + y) * 256, 128), 256)]

    quarters = (quarter_w1, quarter_wc, quarter_es, quarter_w3)

    def piece(which, d):
        return (
            fw1.at[d, core, half_y],
            fwc.at[d, half_y, :, core_lanes],
            fes.at[d, :, es_lanes],
            fw3.at[d, :, w3_lanes],
        )[which]

    def seven(which):
        return (
            fw1.at[pl.ds(0, n_dp - 1), core, half_y],
            fwc.at[pl.ds(0, n_dp - 1), half_y, :, core_lanes],
            fes.at[pl.ds(0, n_dp - 1), :, es_lanes],
            fw3.at[pl.ds(0, n_dp - 1), :, w3_lanes],
        )[which]

    def gather_out(which):
        send_all(piece(which, dp), ws.at[which, 0], wr.at[which, 0], owner_peers)

    def gather_turn(which):
        wait_bytes(seven(which), wr.at[which, 0])
        mine = quarters[which](core, half_y)
        remote(mine, mine, ws.at[which, 1], wr.at[which, 1], across).start()
        remote(mine, mine, ws.at[which, 2], wr.at[which, 2], sibling).start()

    def gather_hand(which):
        theirs = quarters[which](core, 1 - half_y)
        wait_bytes(theirs, wr.at[which, 1])
        remote(theirs, theirs, ws.at[which, 3], wr.at[which, 3], sibling).start()

    def gather_end(which):
        wait_bytes(quarters[which](1 - core, half_y), wr.at[which, 2])
        wait_bytes(quarters[which](1 - core, 1 - half_y), wr.at[which, 3])

    def to_rows(source, target):
        def body(index, carry):
            values = source[pl.ds(index * (CHUNK // 4), CHUNK // 4)].astype(F32)
            row = pl.multiple_of(index * CHUNK, CHUNK)
            target[pl.ds(row, CHUNK), :] = values.reshape(CHUNK, CHANNELS).astype(BF16)
            return carry

        lax.fori_loop(0, ROWS // CHUNK, body, 0)

    gather_out(0)
    own_copies[2].wait()
    qc = wc_own.shape[0] // 2
    fwc[dp, half_y, :, core_lanes] = wc_own[
        pl.ds(pl.multiple_of(half_y * qc, qc), qc), core_lanes
    ].astype(BF16)
    gather_out(1)

    own_copies[1].wait()
    shard = np_own.shape[0]
    lanes_id = lax.broadcasted_iota(jnp.int32, (8, 128), 1)
    turn = lax.rem(shard * dp, 128)
    np_rows = []
    for at in range(0, shard, 128):
        width = min(128, shard - at)
        piece_row = np_own[pl.ds(at, width)].reshape(1, width)
        if width < 128:
            piece_row = jnp.concatenate([piece_row, jnp.zeros((1, 128 - width), F32)], axis=1)
        np_rows.append(piece_row)
    np_rows.append(jnp.zeros((8 - len(np_rows), 128), F32))
    np_turned = jnp.concatenate(np_rows, axis=0).astype(BF16).astype(F32)
    np_turned = pltpu.roll(np_turned, turn, 1)
    np_slots[dp] = jnp.where(lanes_id < turn, pltpu.roll(np_turned, 1, 0), np_turned)
    send_all(np_slots.at[dp], np_sems.at[0], np_sems.at[1], owner_peers)
    for copy in own_copies[3:]:
        copy.wait()
    ex_rows = ex_own.shape[0]
    es_own[:, 0:128] = sq_own[...].astype(BF16)
    es_own[0:ex_rows, 128:384] = ex_own[:, 0:256].astype(BF16)
    es_own[ex_rows : 2 * ex_rows, 128:384] = ex_own[:, 256:512].astype(BF16)
    es_own[:, 384:512] = jnp.zeros((2 * ex_rows, 128), BF16)
    fes[dp, :, es_lanes] = es_own[:, es_lanes]
    fw3[dp, :, w3_lanes] = w3_own[:, w3_lanes].astype(BF16)
    gy_copy.start()
    x_copy.wait()
    to_rows(x4, x_v)
    gather_turn(0)
    gather_out(2)
    gather_out(3)
    zero_rows = jnp.zeros((PAD, BOTTLE), F32)
    for side in range(3):
        act[side, 0:PAD, :] = zero_rows
        act[side, PAD + ROWS : 2 * PAD + ROWS, :] = zero_rows
    for lane_block in range(9):
        dcol[0:PAD, lane_block * 256 : lane_block * 256 + 256] = zero_rows
        dcol[PAD + ROWS : 2 * PAD + ROWS, lane_block * 256 : lane_block * 256 + 256] = zero_rows
    gather_turn(1)
    gather_hand(0)

    def sum_start(k, payload):
        if k in DIRECT:
            ar_slots_a[k][me] = payload
            send_all(ar_slots_a[k].at[me], ar_send_a.at[order[k]], ar_recv_a.at[order[k]], all_peers)
        else:
            ar_slots_a[k][in_plane] = payload
            send_all(ar_slots_a[k].at[in_plane], ar_send_a.at[order[k]], ar_recv_a.at[order[k]], plane_peers)

    def sum_slots(slots, count):
        sums = [slots[slot] for slot in range(count)]
        while len(sums) > 1:
            sums = [sums[i] + sums[i + 1] for i in range(0, len(sums), 2)]
        return sums[0]

    def sum_turn(k):
        if k in DIRECT:
            return
        wait_bytes(ar_slots_a[k].at[pl.ds(0, plane_size - 1)], ar_recv_a.at[order[k]])
        ar_slots_b[k][plane] = sum_slots(ar_slots_a[k], plane_size)
        send_all(ar_slots_b[k].at[plane], ar_send_b.at[order[k]], ar_recv_b.at[order[k]], column_peers)

    def sum_end(k):
        if k in DIRECT:
            wait_bytes(ar_slots_a[k].at[pl.ds(0, everyone - 1)], ar_recv_a.at[order[k]])
            return sum_slots(ar_slots_a[k], everyone)
        wait_bytes(ar_slots_b[k].at[pl.ds(0, planes - 1)], ar_recv_b.at[order[k]])
        return sum_slots(ar_slots_b[k], planes)

    def lanes_of(index, width):
        return pl.ds(pl.multiple_of(index * width, 128), width)

    cut = 64
    conv_rows = {1: pl.ds(0, cut), 2: pl.ds(cut, gc.shape[2] - cut)}
    grads = (g1, gc, gc, g3, ge, gb)
    turned_kinds = (0, 5)

    def half_of(which, c):
        ref = grads[which]
        if which in turned_kinds:
            return ref.at[c]
        if which in conv_rows:
            return ref.at[:, :, conv_rows[which], lanes_of(c, 128)]
        return ref.at[:, :, lanes_of(c, (512, 256)[which - 3])]

    def y_part(which, ref, y):
        if which in turned_kinds:
            return ref.at[y]
        if which < 3:
            return ref.at[:, y]
        return ref.at[:, :, lanes_of(y, (256, 128)[which - 3])]

    def quarter_of(which, c, y):
        ref = grads[which]
        if which in turned_kinds:
            return ref.at[c, y]
        if which in conv_rows:
            return ref.at[:, y, conv_rows[which], lanes_of(c, 128)]
        return ref.at[:, :, lanes_of(c * 2 + y, (256, 128)[which - 3])]

    def final_part(which, c, y):
        if which == 0:
            return fs[0].at[c, y]
        if which in conv_rows:
            return fs[1].at[y, conv_rows[which], lanes_of(c, 128)]
        return fs[which - 1].at[:, lanes_of(c * 2 + y, (256, 128)[which - 3])]

    def of_owner(which, ref, d):
        return ref.at[:, lanes_of(d, CHANNELS // n_dp)] if which in turned_kinds else ref.at[d]

    def in_blocks(which, body):
        if which in turned_kinds:
            count = 4
            rows = grads[which].shape[2] // count
            block = lambda index: pl.ds(pl.multiple_of(index * rows, rows), rows)
        else:
            count, block = n_dp, lambda index: index

        def step(index, carry):
            body(block(index))
            return carry

        lax.fori_loop(0, count, step, 0)

    def reduce_core(which):
        remote(
            half_of(which, 1 - core), r1s[which], gs.at[which, 0], gr.at[which, 0], sibling
        ).start()

    def reduce_y(which):
        wait_bytes(r1s[which], gr.at[which, 0])
        away = quarter_of(which, core, 1 - half_y)
        mine = quarter_of(which, core, half_y)
        there = y_part(which, r1s[which], 1 - half_y)
        here = y_part(which, r1s[which], half_y)

        def add_away(at):
            ys[which][at] = (away[at].astype(F32) + there[at].astype(F32)).astype(
                ys[which].dtype
            )

        in_blocks(which, add_away)
        remote(ys[which], r2s[which], gs.at[which, 1], gr.at[which, 1], across).start()

        def add_mine(at):
            mine[at] = (mine[at].astype(F32) + here[at].astype(F32)).astype(mine.dtype)

        in_blocks(which, add_mine)

    def reduce_owner(which):
        wait_bytes(r2s[which], gr.at[which, 1])
        mine = quarter_of(which, core, half_y)

        def add(at):
            ks[which][at] = (mine[at].astype(F32) + r2s[which][at].astype(F32)).astype(
                ks[which].dtype
            )

        in_blocks(which, add)
        for device in owner_peers:
            remote(
                of_owner(which, ks[which], device[0]),
                r3s[which].at[dp],
                gs.at[which, 2],
                gr.at[which, 2],
                device,
            ).start()
        own[which][...] = of_owner(which, mine, dp)[...].astype(F32) + of_owner(
            which, r2s[which], dp
        )[...].astype(F32)
        r3s[which][dp] = jnp.zeros(own[which].shape, r3s[which].dtype)

    def owner_total(which):
        wait_bytes(r3s[which].at[pl.ds(0, n_dp - 1)], gr.at[which, 2])
        total = own[which][...]
        for slot in range(n_dp):
            total = total + r3s[which][slot].astype(F32)
        return total

    def reduce_spread(which):
        total = owner_total(which)
        if which == 0:
            rows = pl.ds(pl.multiple_of(part * (BOTTLE // 4), BOTTLE // 4), BOTTLE // 4)
            total = total - fix[0, rows, :]
            for m in range(2):
                total = total - fix[1 + m, rows, :] * back_own[m]
        mine = final_part(which, core, half_y)
        mine[...] = total
        send_all(mine, gs.at[which, 3], gr.at[which, 3], rep_peers)

    def three_parts(which):
        if which == 0:
            return r1s[0].at[0, :, pl.ds(0, 3 * CHANNELS // n_dp)]
        return r1s[which].at[pl.ds(0, 3), 0] if which < 3 else y_part(which, r1s[which], 0).at[pl.ds(0, 3)]

    def reduce_end(which):
        wait_bytes(three_parts(which), gr.at[which, 3])

    gather_end(0)
    red[...] = jnp.dot(x_v[...], fw1[...].reshape(CHANNELS, BOTTLE), preferred_element_type=F32)

    def sums_of(ref, start, width):
        def body(row, carry):
            values = grouped(ref[pl.ds(row, CHUNK), start : start + width])
            return carry[0] + jnp.sum(values, axis=0), carry[1] + jnp.sum(values * values, axis=0)

        zero = jnp.zeros((8, width), F32)
        return over_rows(body, (zero, zero))

    def joined(found):
        both = [jnp.concatenate(item, axis=1) for item in zip(*found)]
        return fold_lanes(stack_sums(micro_sum(both[0]), micro_sum(both[1])))

    def both_sums(name):
        return unstack_sums(unfold_lanes(sum_end(name)))

    sum_start("reduced", joined([sums_of(red, 0, 256)]))
    gather_turn(2)
    gather_turn(3)

    gy_copy.wait()
    to_rows(gy4, gy_v)
    wait_bytes(np_slots.at[pl.ds(0, n_dp - 1)], np_sems.at[1])
    np_full[...] = jnp.zeros(np_full.shape, F32)
    for d in range(n_dp):
        at = shard * d // 128
        np_full[at : at + 8, :] = np_full[at : at + 8, :] + np_slots[d]

    def vector(at, width):
        rows = [np_full[at // 128 + k : at // 128 + k + 1, :] for k in range(width // 128)]
        return jnp.concatenate(rows, axis=1) if len(rows) > 1 else rows[0]

    gain_one, bias_one = vector(0, 256), vector(256, 256)
    gain_two, bias_two = vector(512, 512), vector(1024, 512)
    gain_pool, bias_pool = vector(1536, 128), vector(1664, 128)
    bias_expand = vector(1792, 512)
    gain_three, bias_three = vector(2304, 1024), vector(3328, 1024)

    gather_hand(1)
    total, square = both_sums("reduced")
    center1, scale1, mul1, add1 = norm_terms(total, square, gain_one, bias_one, pixels)

    def make_active(row, carry):
        turned = grouped(red[pl.ds(row, CHUNK), :]) * mul1 + add1
        act[1, pl.ds(PAD + row, CHUNK), :] = flat(turned * sigmoid(turned))
        return carry

    over_rows(make_active, 0)
    gather_hand(2)
    place = lax.rem(lax.broadcasted_iota(jnp.int32, (CHUNK, BOTTLE), 0) // 4, SIDE)
    not_last = place != SIDE - 1
    not_first = place != 0

    def beside(side, row, distance, lanes=slice(0, BOTTLE)):
        near = act[side, pl.ds(PAD + row - 8, CHUNK + 16), lanes]
        return pltpu.roll(near, (CHUNK + 16 - distance) % (CHUNK + 16), 0)[8 : 8 + CHUNK]

    def shift_active(row, carry):
        act[2, pl.ds(PAD + row, CHUNK), :] = jnp.where(not_last, beside(1, row, 4), 0.0)
        act[0, pl.ds(PAD + row, CHUNK), :] = jnp.where(not_first, beside(1, row, -4), 0.0)
        return carry

    over_rows(shift_active, 0)

    def make_columns(row, carry):
        for tap in range(9):
            down, side = tap // 3 - 1, tap % 3
            values = act[side, pl.ds(PAD + row + 56 * down, CHUNK), :].astype(BF16)
            columns[0, pl.ds(row, CHUNK), tap * 128 : tap * 128 + 128] = values[:, 0:128]
            columns[1, pl.ds(row, CHUNK), tap * 128 : tap * 128 + 128] = values[:, 128:256]
        return carry

    over_rows(make_columns, 0)
    gather_end(1)
    own_half = n_dp // 2

    def filters(group):
        return fwc[group * own_half : (group + 1) * own_half].reshape(9 * 128, BOTTLE)

    halves2 = (slice(0, 256), slice(256, 512))
    for group, lanes in enumerate(halves2):
        wid[:, lanes] = jnp.dot(columns[group], filters(group), preferred_element_type=F32)
        sum_start(f"widened{group}", joined([sums_of(wid, group * 256, 256)]))
    sum_turn("widened0")
    sum_turn("widened1")
    gather_hand(3)

    norm2 = []
    pooled = jnp.zeros((8, BOTTLE), F32)
    for group, lanes in enumerate(halves2):
        total, square = both_sums(f"widened{group}")
        norm2.append(norm_terms(total, square, gain_two[:, lanes], bias_two[:, lanes], pixels))
        m2, a2 = norm2[group][2:4]

        def make_splits(row, carry):
            turned = grouped(wid[pl.ds(row, CHUNK), lanes]) * m2 + a2
            values = turned * sigmoid(turned)
            splits[pl.ds(row, CHUNK), lanes] = flat(values)
            return carry + jnp.sum(values, axis=0)

        pooled = over_rows(make_splits, pooled)
    pooled = image_sum(pooled) * (1.0 / (SIDE * SIDE))
    gather_end(2)
    squeeze = fes[:, :, 0:128].reshape(BOTTLE, INNER)
    ex_both = fes[:, :, 128:384]
    expand = jnp.concatenate(
        [
            ex_both[:, 0:ex_rows].reshape(INNER, 256),
            ex_both[:, ex_rows : 2 * ex_rows].reshape(INNER, 256),
        ],
        axis=1,
    )
    pre_pool = exact_dot(pooled, squeeze, False)
    sum_start("pool", stack_sums(pair_sum(pre_pool), pair_sum(pre_pool * pre_pool)))
    first_micro = lax.rem(row_ids(BOTTLE), 4) < 2

    def make_normed(row, carry):
        rows = pl.ds(row, CHUNK)
        normed = (grouped(red[rows, :]) - center1) * scale1
        dwid[rows, 0:256] = flat(jnp.where(first_micro, normed, 0.0)).astype(BF16)
        dwid[rows, 256:512] = flat(jnp.where(first_micro, 0.0, normed)).astype(BF16)
        return carry + jnp.sum(grouped(x_v[rows, :].astype(F32)), axis=0)

    image_sums = micro_sum(over_rows(make_normed, jnp.zeros((8, CHANNELS), F32)))
    sum_start(
        "images",
        jnp.concatenate(
            [
                image_sums[2 * m : 2 * m + 1, at : at + 128]
                for m in range(2)
                for at in range(0, CHANNELS, 128)
            ],
            axis=0,
        ),
    )
    normed_images = tdot(dwid[...], x_v[...]).astype(BF16)
    normed_images = normed_images.reshape(2, 2, 2, BOTTLE // 4, CHANNELS)
    for m in range(2):
        gb[:, :, m * (BOTTLE // 4) : (m + 1) * (BOTTLE // 4)] = normed_images[m]
    reduce_core(5)
    total, square = unstack_sums(sum_end("pool"))
    center_p, scale_p, mul_p, add_p = norm_terms(total, square, gain_pool, bias_pool, pictures)
    normed_p = (pre_pool - center_p) * scale_p
    norm_p = pre_pool * mul_p + add_p
    gate_p = sigmoid(norm_p)
    hidden = norm_p * gate_p
    slope_p = gate_p * (1.0 + norm_p * (1.0 - gate_p))
    logits = exact_dot(hidden, expand, False) + bias_expand
    left, right = logits[:, 0:256], logits[:, 256:512]
    most = jnp.maximum(left, right)
    left, right = jnp.exp(left - most), jnp.exp(right - most)
    att0 = left / (left + right)
    att1 = right / (left + right)

    gather_end(3)
    last = fw3[...].reshape(BOTTLE, CHANNELS)
    def make_mixed(row, carry):
        rows = pl.ds(row, CHUNK)
        values = grouped(splits[rows, 0:256]) * att0 + grouped(splits[rows, 256:512]) * att1
        mixed[rows, :] = flat(values).astype(BF16)
        return carry

    over_rows(make_mixed, 0)
    halves3 = (slice(0, 512), slice(512, 1024))
    blocks3 = [[slice(512 * h + k, 512 * h + k + 256) for k in (0, 256)] for h in range(2)]
    for half, lanes in enumerate(halves3):
        proj[:, lanes] = jnp.dot(mixed[...], last[:, lanes], preferred_element_type=F32)
        sum_start(
            f"projected{half}", joined([sums_of(proj, 512 * half + k, 256) for k in (0, 256)])
        )
    sum_turn("projected0")
    sum_turn("projected1")
    sum_turn("images")
    reduce_y(5)

    norm3 = []
    zero = jnp.zeros((8, 256), F32)
    for half, lanes in enumerate(halves3):
        total, square = both_sums(f"projected{half}")
        norm3.append(norm_terms(total, square, gain_three[:, lanes], bias_three[:, lanes], pixels))
        found = []
        for k, block in enumerate(blocks3[half]):
            c3, s3, m3, a3 = (item[:, k * 256 : k * 256 + 256] for item in norm3[half])

            def make_out(row, carry):
                rows = pl.ds(row, CHUNK)
                values = grouped(proj[rows, block])
                summed = grouped(x_v[rows, block].astype(F32)) + (values * m3 + a3)
                gate = sigmoid(summed)
                bo4[pl.ds(row // 4, CHUNK // 4), :, block] = by_four(summed * gate).astype(BF16)
                upstream = grouped(gy_v[rows, block].astype(F32)) * (
                    gate * (1.0 + summed * (1.0 - gate))
                )
                up[rows, block] = flat(upstream)
                normed = (values - c3) * s3
                return carry[0] + jnp.sum(upstream, axis=0), carry[1] + jnp.sum(
                    upstream * normed, axis=0
                )

            found.append(over_rows(make_out, (zero, zero)))
        sum_start(f"back_projected{half}", joined(found))
    bo_copy = pltpu.make_async_copy(bo4, bo_hbm, local_sem.at[2])
    bo_copy.start()

    def write_norm(at, pattern):
        at = at // 128
        both = pattern[0:1, :] + pattern[2:3, :]
        for k in range(both.shape[1] // 128):
            np_full[at + k : at + k + 1, :] = both[:, k * 128 : k * 128 + 128]

    sum_turn("back_projected0")
    sum_turn("back_projected1")
    reduce_owner(5)

    for half, lanes in enumerate(halves3):
        bias_sum, gain_sum = both_sums(f"back_projected{half}")
        write_norm(2304 + 512 * half, gain_sum)
        write_norm(3328 + 512 * half, bias_sum)
        by_value, constant = back_terms(*norm3[half][0:3], bias_sum, gain_sum, pixels)
        for k, block in enumerate(blocks3[half]):
            m3, v3, k3 = (
                item[:, k * 256 : k * 256 + 256] for item in (norm3[half][2], by_value, constant)
            )

            def make_dproj(row, carry):
                rows = pl.ds(row, CHUNK)
                values = grouped(up[rows, block]) * m3 + grouped(proj[rows, block]) * v3 + k3
                dproj[rows, block] = flat(values).astype(BF16)
                return carry

            over_rows(make_dproj, 0)
        part_mixed = dot_t(dproj[:, lanes], last[:, lanes])
        d_mixed[...] = part_mixed if half == 0 else d_mixed[...] + part_mixed

    def attend(row, carry):
        rows = pl.ds(row, CHUNK)
        values = grouped(d_mixed[rows, :])
        return (
            carry[0] + jnp.sum(values * grouped(splits[rows, 0:256]), axis=0),
            carry[1] + jnp.sum(values * grouped(splits[rows, 256:512]), axis=0),
        )

    d_att0, d_att1 = over_rows(attend, (zero, zero))
    d_att0, d_att1 = image_sum(d_att0), image_sum(d_att1)
    both = att0 * d_att0 + att1 * d_att1
    d_logits = jnp.concatenate([att0 * (d_att0 - both), att1 * (d_att1 - both)], axis=1)
    d_hidden = exact_dot(d_logits, expand, True)
    d_pool = d_hidden * slope_p
    per_micro = stack_sums(pair_sum(d_pool), pair_sum(d_pool * normed_p))
    sum_start("back_pool", per_micro)
    ex_sum = pair_sum(d_logits)
    ex_sum = ex_sum + pltpu.roll(ex_sum, 2, 0)
    ex_rows_sum = ex_sum[:, 0:128]
    for k in range(1, 4):
        ex_rows_sum = jnp.where(row_ids(128) == k, ex_sum[:, k * 128 : k * 128 + 128], ex_rows_sum)

    grad_ex = image_dot(hidden, d_logits)
    grad_ex = grad_ex.reshape(n_dp, ex_rows, 512)
    ge[:, 0:ex_rows, 128:384] = grad_ex[:, :, 0:256]
    ge[:, ex_rows : 2 * ex_rows, 128:384] = grad_ex[:, :, 256:512]
    ge[:, :, 384:512] = jnp.zeros((n_dp, 2 * ex_rows, 128), F32)
    g3[...] = tdot(mixed[...], dproj[...]).reshape(g3.shape)
    reduce_core(3)
    held = []
    for group, att in ((0, att0), (1, att1)):
        lanes = halves2[group]
        c2, s2, m2, a2 = norm2[group]

        def make_dn2(row, carry):
            rows = pl.ds(row, CHUNK)
            values = grouped(wid[rows, lanes])
            turned = values * m2 + a2
            gate = sigmoid(turned)
            slope = gate * (1.0 + turned * (1.0 - gate))
            down = grouped(d_mixed[rows, :]) * att * slope
            dn2[rows, lanes] = flat(down)
            splits[rows, lanes] = flat(slope)
            normed = (values - c2) * s2
            terms = (down, down * normed, slope, slope * normed)
            return tuple(item + jnp.sum(term, axis=0) for item, term in zip(carry, terms))

        held.append([image_sum(item) for item in over_rows(make_dn2, (zero,) * 4)])
    pool_bias_sum, pool_gain_sum = unstack_sums(sum_end("back_pool"))
    write_norm(1536, pool_gain_sum)
    write_norm(1664, pool_bias_sum)
    d_pre_pool = mul_p * (
        d_pool - pool_bias_sum * (1.0 / pictures) - normed_p * (pool_gain_sum * (1.0 / pictures))
    )
    d_pooled = exact_dot(d_pre_pool, squeeze, True) * (1.0 / (SIDE * SIDE))
    for group in range(2):
        down, down_normed, slope, slope_normed = held[group]
        payload = fold_lanes(
            stack_sums(
                pair_sum(down + d_pooled * slope), pair_sum(down_normed + d_pooled * slope_normed)
            )
        )
        if group == 1:
            payload = jnp.concatenate([payload, ex_rows_sum], axis=0)
        sum_start(f"back_widened{group}", payload)
    ge[:, :, 0:128] = image_dot(pooled, d_pre_pool).reshape(n_dp, 2 * ex_rows, 128)
    reduce_core(4)
    sum_turn("back_widened0")
    sum_turn("back_widened1")
    reduce_y(3)
    reduce_y(4)
    back_total = owner_total(5)
    back_own[0] = back_total[0 : BOTTLE // 4]
    back_own[1] = back_total[BOTTLE // 4 :]

    small_zero = jnp.zeros((8, 128), F32)
    for group, lanes in enumerate(halves2):
        whole = sum_end(f"back_widened{group}")
        if group == 1:
            np_full[14:18, :] = whole[8:12]
        bias_sum, gain_sum = unstack_sums(unfold_lanes(whole[0:8]))
        write_norm(512 + 256 * group, gain_sum)
        write_norm(1024 + 256 * group, bias_sum)
        m2 = norm2[group][2]
        v2, k2 = back_terms(*norm2[group][0:3], bias_sum, gain_sum, pixels)
        pooled_m2 = d_pooled * m2

        def make_dwid(row, carry):
            rows = pl.ds(row, CHUNK)
            values = grouped(dn2[rows, lanes]) * m2 + grouped(splits[rows, lanes]) * pooled_m2
            values = values + grouped(wid[rows, lanes]) * v2 + k2
            dwid[rows, lanes] = flat(values).astype(BF16)
            return carry

        over_rows(make_dwid, 0)
        gc[group * own_half : (group + 1) * own_half] = tdot(
            columns[group], dwid[:, lanes]
        ).reshape(own_half, 2, 9 * 128 // own_half // 2, BOTTLE)
    reduce_core(1)
    reduce_core(2)
    for group, lanes in enumerate(halves2):
        dcol[PAD : PAD + ROWS, group * 1152 : group * 1152 + 1152] = dot_t(
            dwid[:, lanes], filters(group)
        )
        inner = slice(group * 128, group * 128 + 128)

        def gather_taps(row, carry):
            for side in range(3):
                total = None
                for down in range(3):
                    at = group * 1152 + (3 * down + side) * 128
                    values = dcol[pl.ds(PAD + row - 56 * (down - 1), CHUNK), at : at + 128]
                    total = values if total is None else total + values
                act[side, pl.ds(PAD + row, CHUNK), inner] = total
            return carry

        over_rows(gather_taps, 0)
        c1, s1, m1, a1 = (item[:, inner] for item in (center1, scale1, mul1, add1))
        not_first1, not_last1 = not_first[:, inner], not_last[:, inner]

        def make_dn1(row, carry):
            rows = pl.ds(row, CHUNK)
            d_active = act[1, pl.ds(PAD + row, CHUNK), inner]
            d_active = d_active + jnp.where(not_first1, beside(2, row, -4, inner), 0.0)
            d_active = d_active + jnp.where(not_last1, beside(0, row, 4, inner), 0.0)
            values = grouped(red[rows, inner])
            turned = values * m1 + a1
            gate = sigmoid(turned)
            slope = gate * (1.0 + turned * (1.0 - gate))
            down = grouped(d_active) * slope
            dn1[rows, inner] = flat(down)
            mixed[rows, inner] = flat(down * m1).astype(BF16)
            normed = (values - c1) * s1
            return carry[0] + jnp.sum(down, axis=0), carry[1] + jnp.sum(down * normed, axis=0)

        bias_sum, gain_sum = over_rows(make_dn1, (small_zero, small_zero))
        sum_start(f"back_reduced{group}", stack_sums(micro_sum(bias_sum), micro_sum(gain_sum)))
        if group == 0:
            reduce_owner(3)
            reduce_owner(4)
    reduce_y(1)
    reduce_y(2)
    sum_turn("back_reduced0")
    g1[...] = tdot(mixed[...], x_v[...]).reshape(g1.shape)
    reduce_core(0)
    sum_turn("back_reduced1")
    reduce_owner(1)
    reduce_y(0)
    reduce_owner(2)
    found = [unstack_sums(sum_end(f"back_reduced{group}")) for group in range(2)]
    bias_sum, gain_sum = (jnp.concatenate(item, axis=1) for item in zip(*found))
    write_norm(0, gain_sum)
    write_norm(256, bias_sum)
    by_value, constant = back_terms(center1, scale1, mul1, bias_sum, gain_sum, pixels)
    def make_dred(row, carry):
        rows = pl.ds(row, CHUNK)
        values = grouped(dn1[rows, :]) * mul1 + grouped(red[rows, :]) * by_value + constant
        dred[rows, :] = flat(values).astype(BF16)
        return carry

    over_rows(make_dred, 0)
    proj[...] = dot_t(dred[...], fw1[...].reshape(CHANNELS, BOTTLE))

    by_bias = mul1 * bias_sum * (1.0 / pixels)
    by_gain = mul1 * gain_sum * (1.0 / pixels)
    image_sums = sum_end("images")
    ids = lax.broadcasted_iota(jnp.int32, (16, 128), 0)
    own_sums = [
        jnp.sum(jnp.where(ids == m * n_dp + dp, image_sums, 0.0), axis=0, keepdims=True)
        for m in range(2)
    ]
    ids = row_ids(128)
    fix[0] = row_dot(by_bias, jnp.where(ids == 0, own_sums[0], jnp.where(ids == 2, own_sums[1], 0.0)))
    for m in range(2):
        fix[1 + m] = row_dot(by_gain, jnp.where(ids == 2 * m, 1.0, 0.0))
    reduce_spread(3)
    reduce_spread(4)
    reduce_owner(0)
    reduce_spread(1)

    def make_dx(row, carry):
        for start in range(0, CHANNELS, 256):
            lanes = slice(start, start + 256)
            values = up[pl.ds(row, CHUNK), lanes] + proj[pl.ds(row, CHUNK), lanes]
            dx4[pl.ds(row // 4, CHUNK // 4), :, lanes] = values.reshape(CHUNK // 4, 4, 256)
        return carry

    over_rows(make_dx, 0)
    dx_copy = pltpu.make_async_copy(dx4, dx_hbm, local_sem.at[3])
    dx_copy.start()
    norm_rows = np_full[0:8, :]
    for d in range(1, n_dp):
        at = shard * d // 128
        norm_rows = jnp.where(dp == d, np_full[at : at + 8, :], norm_rows)
    norm_rows = pltpu.roll(norm_rows, lax.rem(128 - turn, 128), 1)
    gn_out[...] = jnp.where(lanes_id < 128 - turn, norm_rows, pltpu.roll(norm_rows, 7, 0))
    reduce_spread(2)
    reduce_spread(0)
    out_copies = [
        pltpu.make_async_copy(source, target, local_sem.at[10 + k])
        for k, (source, target) in enumerate(
            (
                (gn_out, gn_hbm),
                (fs[2], f3_hbm),
                (fs[3], fe_hbm),
                (fs[1], fc_hbm),
                (fs[0], f1_hbm),
            )
        )
    ]
    out_copies[0].start()
    for which in (3, 4, 1, 2, 0):
        reduce_end(which)
        if which != 1:
            out_copies[{3: 1, 4: 2, 2: 3, 0: 4}[which]].start()

    bo_copy.wait()
    dx_copy.wait()
    for copy in out_copies:
        copy.wait()
    for k in STATS:
        if k in DIRECT:
            wait_bytes(ar_slots_a[k].at[pl.ds(0, everyone - 1)], ar_send_a.at[order[k]])
        else:
            wait_bytes(ar_slots_a[k].at[pl.ds(0, plane_size - 1)], ar_send_a.at[order[k]])
            wait_bytes(ar_slots_b[k].at[pl.ds(0, planes - 1)], ar_send_b.at[order[k]])
    wait_bytes(np_slots.at[pl.ds(0, n_dp - 1)], np_sems.at[0])
    for which in range(4):
        wait_bytes(seven(which), ws.at[which, 0])
        for stage in range(1, 4):
            wait_bytes(quarters[which](core, half_y), ws.at[which, stage])
    for which in range(6):
        wait_bytes(r1s[which], gs.at[which, 0])
        wait_bytes(r2s[which], gs.at[which, 1])
        wait_bytes(r3s[which].at[pl.ds(0, n_dp - 1)], gs.at[which, 2])
        if which < 5:
            wait_bytes(three_parts(which), gs.at[which, 3])


def update_kernel(*refs):
    sources, targets = refs[0:25], refs[25:45]
    inputs, outs, through = refs[45:68], refs[68:86], refs[86:88]
    pass_sems, in_sems, out_sems = refs[88:91]
    fetching, passing = [], []
    half = SIDE * SIDE // 2
    for number, (which, at, count) in enumerate(((1, 0, half), (1, half, half), (0, 0, 2 * half))):
        rows = pl.ds(at, count)
        fetching.append(
            pltpu.make_async_copy(
                sources[which].at[rows], through[which].at[rows], pass_sems.at[0, number]
            )
        )
        passing.append(
            pltpu.make_async_copy(
                through[which].at[rows], targets[which].at[rows], pass_sems.at[1, number]
            )
        )
    for copy in fetching:
        copy.start()
    coming = [
        pltpu.make_async_copy(source, held, in_sems.at[k])
        for k, (source, held) in enumerate(zip(sources[2:], inputs))
    ]
    for copy in coming:
        copy.start()
    grads, states = inputs[0:5], inputs[5:23]
    going = [
        pltpu.make_async_copy(held, target, out_sems.at[k])
        for k, (held, target) in enumerate(zip(outs, targets[2:]))
    ]
    ex_rows = states[9].shape[0]
    shard = states[15].shape[0]
    fans = (CHANNELS, 9 * BOTTLE // RADIX, BOTTLE, INNER // 8, BOTTLE)
    for copy in coming[0:5]:
        copy.wait()
    found = (
        grads[0][...].T,
        grads[1][...],
        grads[3][:, 0:128],
        jnp.concatenate([grads[3][0:ex_rows, 128:384], grads[3][ex_rows:, 128:384]], axis=1),
        grads[2][...],
    )
    for order, k in enumerate((3, 2, 4, 0, 1)):
        for copy in coming[5 + 3 * k : 8 + 3 * k]:
            copy.wait()
        new = adamw(
            states[3 * k][...],
            states[3 * k + 1][...],
            states[3 * k + 2][...],
            found[k],
            2.0 * fans[k] ** (-0.5),
            DECAY,
        )
        for j in range(3):
            outs[3 * k + j][...] = new[j]
            going[3 * k + j].start()
        if order < 3:
            fetching[order].wait()
            passing[order].start()
    for copy in coming[20:23]:
        copy.wait()
    for at in range(0, shard, 128):
        width = min(128, shard - at)
        lanes = pl.ds(at, width)
        new = adamw(
            *[states[15 + j][lanes].reshape(1, width) for j in range(3)],
            grads[4][at // 128 : at // 128 + 1, 0:width],
            NORM_RATE,
            0.0,
        )
        for j in range(3):
            outs[15 + j][lanes] = new[j].reshape(width)
    for copy in going[15:18]:
        copy.start()
    for copy in passing + going:
        copy.wait()


def fused_device(
    images,
    out_grad,
    reduce_weight,
    reduce_moment,
    reduce_second,
    conv_weight,
    conv_moment,
    conv_second,
    squeeze_weight,
    squeeze_moment,
    squeeze_second,
    expand_weight,
    expand_moment,
    expand_second,
    project_weight,
    project_moment,
    project_second,
    norm_params,
    norm_moment,
    norm_second,
):
    n_dp, n_rep = lax.axis_size("dp"), lax.axis_size("rep")
    by_pixel = lambda values: jnp.transpose(values, (1, 2, 0, 3)).reshape(-1, 4, CHANNELS)
    qc = conv_weight.shape[0] // 2
    q1 = reduce_weight.shape[0] // 4
    pe = squeeze_weight.shape[0]
    vmem = pltpu.VMEM
    pixel_form = (SIDE * SIDE, 4, CHANNELS)
    scratch = [
        *[
            vmem(values.shape, F32)
            for values in (
                reduce_weight,
                conv_weight,
                squeeze_weight,
                expand_weight,
                project_weight,
                norm_params,
            )
        ],
        vmem((8, 128), F32),
        vmem(pixel_form, BF16),
        vmem(pixel_form, BF16),
        vmem((ROWS, CHANNELS), BF16),
        vmem((ROWS, CHANNELS), BF16),
        vmem((n_dp, 2, 2, q1, BOTTLE), BF16),
        vmem((n_dp, 2, qc, BOTTLE), BF16),
        vmem((n_dp, pe, 512), BF16),
        vmem((n_dp, pe, CHANNELS), BF16),
        vmem((pe, 512), BF16),
        vmem((n_dp, 8, 128), F32),
        vmem((40, 128), F32),
        vmem((ROWS, BOTTLE), F32),
        vmem((3, ROWS + 2 * PAD, BOTTLE), F32),
        vmem((2, ROWS, 9 * 128), BF16),
        vmem((ROWS, 512), F32),
        vmem((ROWS, 512), F32),
        vmem((ROWS, BOTTLE), BF16),
        vmem((ROWS, CHANNELS), F32),
        vmem((ROWS, CHANNELS), F32),
        vmem(pixel_form, BF16),
        vmem(pixel_form, F32),
        vmem((ROWS, CHANNELS), BF16),
        vmem((ROWS, BOTTLE), F32),
        vmem((ROWS, 512), F32),
        vmem((ROWS, 512), BF16),
        vmem((ROWS + 2 * PAD, 2 * 9 * 128), F32),
        vmem((ROWS, BOTTLE), F32),
        vmem((ROWS, BOTTLE), BF16),
        vmem((2, 2, BOTTLE // 4, CHANNELS), F32),
        vmem((n_dp, 2, qc, BOTTLE), F32),
        vmem((n_dp, pe, CHANNELS), F32),
        vmem((n_dp, pe, 512), F32),
        vmem((2, 2, BOTTLE // 2, CHANNELS), BF16),
        vmem((3, BOTTLE, CHANNELS // n_dp), F32),
        vmem((2, BOTTLE // 4, CHANNELS // n_dp), F32),
    ]
    direct = n_dp * n_rep
    scratch += [
        vmem((direct if k in DIRECT else 2 * n_rep,) + shape, F32) for k, shape in STATS.items()
    ]
    scratch += [vmem((n_dp // 2,) + shape, F32) for shape in STATS.values()]
    cut = 64
    lanes1 = CHANNELS // n_dp
    half = [
        (2, BOTTLE // 4, CHANNELS),
        (n_dp, 2, cut, 128),
        (n_dp, 2, qc - cut, 128),
        (n_dp, pe, 512),
        (n_dp, pe, 256),
        (2, BOTTLE // 2, CHANNELS),
    ]
    quarter = [
        (BOTTLE // 4, CHANNELS),
        (n_dp, cut, 128),
        (n_dp, qc - cut, 128),
        (n_dp, pe, 256),
        (n_dp, pe, 128),
        (BOTTLE // 2, CHANNELS),
    ]
    final = [(2, 2, BOTTLE // 4, lanes1), (2, qc, BOTTLE), (pe, CHANNELS), (pe, 512)]
    sent = [BF16, BF16, BF16, BF16, F32, BF16]
    scratch += [vmem(shape, F32) for shape in half[:-1]] + [vmem(half[-1], BF16)]
    scratch += [vmem(shape, kind) for shape, kind in zip(quarter, sent)] * 3
    owned = [(BOTTLE // 4, lanes1)] + [shape[1:] for shape in quarter[1:-1]]
    owned += [(BOTTLE // 2, lanes1)]
    scratch += [vmem((n_dp,) + shape, kind) for shape, kind in zip(owned, sent)]
    scratch += [vmem(shape, F32) for shape in owned]
    scratch += [vmem(shape, F32) for shape in final]
    dma = pltpu.SemaphoreType.DMA
    scratch += [dma((15,))] + [dma((len(STATS),))] * 4 + [dma((2,))] + [dma((4, 4))] * 2 + [dma((6, 4))] * 2
    any_space = pl.BlockSpec(memory_space=pl.ANY)
    block_out, images_grad, sum1, sumc, sum3, sume, norm_grads = pl.pallas_call(
        functools.partial(block_kernel, n_dp, n_rep),
        out_shape=[
            jax.ShapeDtypeStruct(pixel_form, BF16),
            jax.ShapeDtypeStruct(pixel_form, F32),
            *[jax.ShapeDtypeStruct(shape, F32) for shape in final],
            jax.ShapeDtypeStruct((8, 128), F32),
        ],
        in_specs=[any_space] * 8,
        out_specs=[any_space] * 7,
        scratch_shapes=scratch,
        compiler_params=pltpu.CompilerParams(
            collective_id=0, has_side_effects=True, vmem_limit_bytes=63 * 1024 * 1024
        ),
    )(
        by_pixel(images),
        by_pixel(out_grad),
        reduce_weight,
        conv_weight,
        squeeze_weight,
        expand_weight,
        project_weight,
        norm_params,
    )
    states = (
        reduce_weight,
        reduce_moment,
        reduce_second,
        conv_weight,
        conv_moment,
        conv_second,
        squeeze_weight,
        squeeze_moment,
        squeeze_second,
        expand_weight,
        expand_moment,
        expand_second,
        project_weight,
        project_moment,
        project_second,
    )
    held = (*states, norm_params, norm_moment, norm_second)
    sums = (
        sum1.reshape(BOTTLE, lanes1),
        sumc.reshape(conv_weight.shape),
        sum3,
        sume,
        norm_grads,
    )
    block_out, images_grad, *updated = pl.pallas_call(
        update_kernel,
        out_shape=[
            jax.ShapeDtypeStruct(pixel_form, BF16),
            jax.ShapeDtypeStruct(pixel_form, F32),
            *[jax.ShapeDtypeStruct(state.shape, F32) for state in held],
        ],
        in_specs=[any_space] * 25,
        out_specs=[any_space] * 20,
        scratch_shapes=[vmem(values.shape, F32) for values in (*sums, *held, *held)]
        + [vmem(pixel_form, BF16), vmem(pixel_form, F32)]
        + [dma((2, 3)), dma((23,)), dma((18,))],
        compiler_params=pltpu.CompilerParams(vmem_limit_bytes=63 * 1024 * 1024),
    )(block_out, images_grad, *sums, *held)
    by_image = lambda values: jnp.transpose(
        values.reshape(SIDE, SIDE, images.shape[0], CHANNELS), (2, 0, 1, 3)
    )
    return (
        by_image(block_out),
        by_image(images_grad),
        *updated,
    )


def solution(mesh):
    placed = (
        P(("dp", "rep"), None, None, None),
        P(("dp", "rep"), None, None, None),
        P("dp", None),
        P("dp", None),
        P("dp", None),
        P("dp", None),
        P("dp", None),
        P("dp", None),
        P("dp", None),
        P("dp", None),
        P("dp", None),
        P("dp", None),
        P("dp", None),
        P("dp", None),
        P("dp", None),
        P("dp", None),
        P("dp", None),
        P("dp"),
        P("dp"),
        P("dp"),
    )
    n_dp, n_rep = mesh.shape["dp"], mesh.shape["rep"]
    whole_tiles = n_rep == 4 and n_dp % 2 == 0 and INNER % (16 * n_dp) == 0
    return jax.shard_map(
        fused_device if whole_tiles else per_device,
        mesh=mesh,
        in_specs=placed,
        out_specs=(
            P(("dp", "rep"), None, None, None),
            P(("dp", "rep"), None, None, None),
            P("dp", None),
            P("dp", None),
            P("dp", None),
            P("dp", None),
            P("dp", None),
            P("dp", None),
            P("dp", None),
            P("dp", None),
            P("dp", None),
            P("dp", None),
            P("dp", None),
            P("dp", None),
            P("dp", None),
            P("dp", None),
            P("dp", None),
            P("dp"),
            P("dp"),
            P("dp"),
        ),
        check_vma=False,
    )
```

```python
import functools
import jax
import jax.numpy as jnp
from jax import lax
from jax.experimental import pallas as pl
from jax.experimental.pallas import tpu as pltpu
from jax.sharding import PartitionSpec as P

CHANNELS = 1024
BOTTLE = 256
INNER = 128
RADIX = 2
SIDE = 14
MICRO = 2
STEP = 10


EPSILON = 1e-05
PRECISE = lax.Precision.HIGHEST
BETA_ONE = 0.9
BETA_TWO = 0.999
ADAM_EPSILON = 1e-08
DECAY = 0.01
NORM_RATE = 0.8
ROWS = 4 * SIDE * SIDE
NORM_WIDTH = 4352


def split_params(packed):
    widths = (
        BOTTLE,
        BOTTLE,
        RADIX * BOTTLE,
        RADIX * BOTTLE,
        INNER,
        INNER,
        RADIX * BOTTLE,
        CHANNELS,
        CHANNELS,
    )
    pieces = []
    offset = 0
    for segment in widths:
        pieces.append(lax.slice_in_dim(packed, offset, offset + segment))
        offset = offset + segment
    return pieces


def silu_slope(values):
    logistic = jax.nn.sigmoid(values)
    return logistic * (1.0 + values * (1.0 - logistic))


def norm_forward(values, gain, bias, count):
    flat = values.reshape(-1, values.shape[-1])
    total, square = lax.psum((jnp.sum(flat, axis=0), jnp.sum(flat * flat, axis=0)), ("dp", "rep"))
    center = total / count
    scale = lax.rsqrt(square / count - center * center + EPSILON)
    normed = (values - center) * scale
    return (normed * gain + bias, normed, scale)


def norm_backward(upstream, normed, scale, gain, count):
    flat_up = upstream.reshape(-1, upstream.shape[-1])
    flat_norm = normed.reshape(-1, normed.shape[-1])
    bias_sum, gain_sum = lax.psum(
        (jnp.sum(flat_up, axis=0), jnp.sum(flat_up * flat_norm, axis=0)), ("dp", "rep")
    )
    downstream = gain * scale * (upstream - bias_sum / count - normed * (gain_sum / count))
    return (downstream, gain_sum, bias_sum)


def patches(active):
    padded = jnp.pad(active, ((0, 0), (1, 1), (1, 1), (0, 0), (0, 0)))
    shifted = [
        padded[:, down_step : down_step + SIDE, side_step : side_step + SIDE]
        for down_step in range(3)
        for side_step in range(3)
    ]
    return jnp.stack(shifted, axis=4)


def unpatch(columns):
    total = jnp.zeros(
        (columns.shape[0], SIDE + 2, SIDE + 2, columns.shape[3], columns.shape[5]), jnp.float32
    )
    for down_step in range(3):
        for side_step in range(3):
            piece = columns[:, :, :, :, 3 * down_step + side_step]
            total = total + jnp.pad(
                piece,
                ((0, 0), (down_step, 2 - down_step), (side_step, 2 - side_step), (0, 0), (0, 0)),
            )
    return total[:, 1 : SIDE + 1, 1 : SIDE + 1]


def adamw(param, moment, second, gradient, rate, decay):
    moment_new = BETA_ONE * moment + (1.0 - BETA_ONE) * gradient
    second_new = BETA_TWO * second + (1.0 - BETA_TWO) * gradient * gradient
    ratio = (
        moment_new
        / (1.0 - BETA_ONE**STEP)
        / (jnp.sqrt(second_new / (1.0 - BETA_TWO**STEP)) + ADAM_EPSILON)
    )
    return (param - rate * (ratio + decay * param), moment_new, second_new)


def per_device(
    images,
    out_grad,
    reduce_weight,
    reduce_moment,
    reduce_second,
    conv_weight,
    conv_moment,
    conv_second,
    squeeze_weight,
    squeeze_moment,
    squeeze_second,
    expand_weight,
    expand_moment,
    expand_second,
    project_weight,
    project_moment,
    project_second,
    norm_params,
    norm_moment,
    norm_second,
):
    bf16 = jnp.bfloat16
    low_reduce = reduce_weight.astype(bf16)
    low_conv = conv_weight.astype(bf16)
    low_squeeze = squeeze_weight.astype(bf16)
    low_expand = expand_weight.astype(bf16)
    low_project = project_weight.astype(bf16)
    low_norm = norm_params.astype(bf16)
    devices = lax.axis_size("dp") * lax.axis_size("rep")
    per_batch = images.shape[0] // MICRO
    pixel_count = float(per_batch * SIDE * SIDE * devices)
    image_count = float(per_batch * devices)
    group_in = BOTTLE // RADIX
    grad_first = jnp.zeros((CHANNELS, BOTTLE), jnp.float32)
    grad_conv = jnp.zeros((RADIX, 9 * group_in, BOTTLE), jnp.float32)
    grad_squeeze = jnp.zeros((BOTTLE, INNER), jnp.float32)
    grad_expand = jnp.zeros((INNER, RADIX * BOTTLE), jnp.float32)
    grad_last = jnp.zeros((BOTTLE, CHANNELS), jnp.float32)
    grad_norms = jnp.zeros(
        (2 * BOTTLE + 3 * RADIX * BOTTLE + 2 * INNER + 2 * CHANNELS,), jnp.float32
    )
    outputs = []
    input_grads = []
    for number in range(MICRO):
        forward_set = (
            lax.all_gather(low_reduce, "dp", axis=0, tiled=True),
            lax.all_gather(low_conv, "dp", axis=0, tiled=True),
            lax.all_gather(low_squeeze, "dp", axis=0, tiled=True),
            lax.all_gather(low_expand, "dp", axis=0, tiled=True),
            lax.all_gather(low_project, "dp", axis=0, tiled=True),
            lax.all_gather(low_norm, "dp", axis=0, tiled=True),
        )
        first, conv, squeeze, expand, last, packed = forward_set
        (
            gain_one,
            bias_one,
            gain_two,
            bias_two,
            gain_pool,
            bias_pool,
            bias_expand,
            gain_three,
            bias_three,
        ) = split_params(packed.astype(jnp.float32))
        batched = images[number * per_batch : (number + 1) * per_batch]
        cotangent = out_grad[number * per_batch : (number + 1) * per_batch]
        reduced = jnp.einsum("nhwc,cb->nhwb", batched, first, preferred_element_type=jnp.float32)
        norm_one, normed_one, scale_one = norm_forward(reduced, gain_one, bias_one, pixel_count)
        active = jax.nn.silu(norm_one).astype(bf16)
        columns = patches(active.reshape(per_batch, SIDE, SIDE, RADIX, group_in)).reshape(
            per_batch * SIDE * SIDE, RADIX, 9 * group_in
        )
        conv_grouped = conv.reshape(RADIX, 9 * group_in, BOTTLE)
        widened = jnp.einsum(
            "prk,rko->pro", columns, conv_grouped, preferred_element_type=jnp.float32
        )
        widened = widened.reshape(per_batch, SIDE, SIDE, RADIX * BOTTLE)
        norm_two, normed_two, scale_two = norm_forward(widened, gain_two, bias_two, pixel_count)
        splits = jax.nn.silu(norm_two).reshape(per_batch, SIDE, SIDE, RADIX, BOTTLE)
        pooled = jnp.sum(jnp.sum(splits, axis=3), axis=(1, 2)) / (SIDE * SIDE)
        squeeze_float = squeeze.astype(jnp.float32)
        expand_float = expand.astype(jnp.float32)
        pre_pool = jnp.dot(pooled, squeeze_float, precision=PRECISE)
        norm_pool, normed_pool, scale_pool = norm_forward(
            pre_pool, gain_pool, bias_pool, image_count
        )
        hidden = jax.nn.silu(norm_pool)
        logits = (jnp.dot(hidden, expand_float, precision=PRECISE) + bias_expand).reshape(
            per_batch, RADIX, BOTTLE
        )
        attention = jax.nn.softmax(logits, axis=1)
        mixed = jnp.sum(splits * attention[:, None, None], axis=3).astype(bf16)
        projected = jnp.einsum("nhwb,bc->nhwc", mixed, last, preferred_element_type=jnp.float32)
        norm_three, normed_three, scale_three = norm_forward(
            projected, gain_three, bias_three, pixel_count
        )
        summed = batched.astype(jnp.float32) + norm_three
        outputs.append(jax.nn.silu(summed).astype(bf16))
        backward_set = (
            lax.all_gather(low_reduce, "dp", axis=0, tiled=True),
            lax.all_gather(low_conv, "dp", axis=0, tiled=True),
            lax.all_gather(low_squeeze, "dp", axis=0, tiled=True),
            lax.all_gather(low_expand, "dp", axis=0, tiled=True),
            lax.all_gather(low_project, "dp", axis=0, tiled=True),
            lax.all_gather(low_norm, "dp", axis=0, tiled=True),
        )
        first, conv, squeeze, expand, last, packed = backward_set
        gains_back = split_params(packed.astype(jnp.float32))
        conv_grouped = conv.reshape(RADIX, 9 * group_in, BOTTLE)
        expand_float = expand.astype(jnp.float32)
        squeeze_float = squeeze.astype(jnp.float32)
        upstream = cotangent.astype(jnp.float32) * silu_slope(summed)
        d_projected, gain_three_grad, bias_three_grad = norm_backward(
            upstream, normed_three, scale_three, gains_back[7], pixel_count
        )
        d_projected_low = d_projected.astype(bf16)
        grad_last = grad_last + jnp.einsum(
            "nhwb,nhwc->bc", mixed, d_projected_low, preferred_element_type=jnp.float32
        )
        d_mixed = jnp.einsum(
            "nhwc,bc->nhwb", d_projected_low, last, preferred_element_type=jnp.float32
        )
        d_splits = d_mixed[:, :, :, None] * attention[:, None, None]
        d_attention = jnp.sum(d_mixed[:, :, :, None] * splits, axis=(1, 2))
        d_logits = attention * (
            d_attention - jnp.sum(attention * d_attention, axis=1, keepdims=True)
        )
        flat_logits = d_logits.reshape(per_batch, RADIX * BOTTLE)
        grad_expand = grad_expand + jnp.dot(hidden.T, flat_logits, precision=PRECISE)
        d_hidden = jnp.dot(flat_logits, expand_float.T, precision=PRECISE)
        d_pool_norm = d_hidden * silu_slope(norm_pool)
        pool_bias_sum, pool_gain_sum, expand_bias_sum = lax.psum(
            (
                jnp.sum(d_pool_norm, axis=0),
                jnp.sum(d_pool_norm * normed_pool, axis=0),
                jnp.sum(flat_logits, axis=0),
            ),
            ("dp", "rep"),
        )
        d_pre_pool = (
            gains_back[4]
            * scale_pool
            * (
                d_pool_norm
                - pool_bias_sum / image_count
                - normed_pool * (pool_gain_sum / image_count)
            )
        )
        grad_squeeze = grad_squeeze + jnp.dot(pooled.T, d_pre_pool, precision=PRECISE)
        d_pooled = jnp.dot(d_pre_pool, squeeze_float.T, precision=PRECISE)
        d_splits = d_splits + (d_pooled / (SIDE * SIDE))[:, None, None, None, :]
        d_norm_two = d_splits.reshape(per_batch, SIDE, SIDE, RADIX * BOTTLE) * silu_slope(norm_two)
        d_widened, gain_two_grad, bias_two_grad = norm_backward(
            d_norm_two, normed_two, scale_two, gains_back[2], pixel_count
        )
        d_widened_low = d_widened.astype(bf16).reshape(per_batch * SIDE * SIDE, RADIX, BOTTLE)
        grad_conv = grad_conv + jnp.einsum(
            "prk,pro->rko", columns, d_widened_low, preferred_element_type=jnp.float32
        )
        d_columns = jnp.einsum(
            "pro,rko->prk", d_widened_low, conv_grouped, preferred_element_type=jnp.float32
        )
        d_active = unpatch(d_columns.reshape(per_batch, SIDE, SIDE, RADIX, 9, group_in)).reshape(
            per_batch, SIDE, SIDE, BOTTLE
        )
        d_norm_one = d_active * silu_slope(norm_one)
        d_reduced, gain_one_grad, bias_one_grad = norm_backward(
            d_norm_one, normed_one, scale_one, gains_back[0], pixel_count
        )
        d_reduced_low = d_reduced.astype(bf16)
        grad_first = grad_first + jnp.einsum(
            "nhwc,nhwb->cb", batched, d_reduced_low, preferred_element_type=jnp.float32
        )
        input_grads.append(
            upstream
            + jnp.einsum("nhwb,cb->nhwc", d_reduced_low, first, preferred_element_type=jnp.float32)
        )
        grad_norms = grad_norms + jnp.concatenate(
            [
                gain_one_grad,
                bias_one_grad,
                gain_two_grad,
                bias_two_grad,
                pool_gain_sum,
                pool_bias_sum,
                expand_bias_sum,
                gain_three_grad,
                bias_three_grad,
            ]
        )
    grad_conv = grad_conv.reshape(9 * BOTTLE, BOTTLE)
    partial_value = (
        lax.psum_scatter(grad_first, "dp", scatter_dimension=0, tiled=True),
        lax.psum_scatter(grad_conv, "dp", scatter_dimension=0, tiled=True),
        lax.psum_scatter(grad_squeeze, "dp", scatter_dimension=0, tiled=True),
        lax.psum_scatter(grad_expand, "dp", scatter_dimension=0, tiled=True),
        lax.psum_scatter(grad_last, "dp", scatter_dimension=0, tiled=True),
    )
    owned = lax.psum(
        (partial_value[0], partial_value[1], partial_value[2], partial_value[3], partial_value[4]),
        "rep",
    )
    shard_length = norm_params.shape[0]
    norm_grad_owned = lax.dynamic_slice_in_dim(
        grad_norms, lax.axis_index("dp") * shard_length, shard_length
    )
    reduce_new = adamw(
        reduce_weight, reduce_moment, reduce_second, owned[0], 2.0 * CHANNELS ** (-0.5), DECAY
    )
    conv_new = adamw(
        conv_weight,
        conv_moment,
        conv_second,
        owned[1],
        2.0 * (9 * BOTTLE // RADIX) ** (-0.5),
        DECAY,
    )
    squeeze_new = adamw(
        squeeze_weight, squeeze_moment, squeeze_second, owned[2], 2.0 * BOTTLE ** (-0.5), DECAY
    )
    expand_new = adamw(
        expand_weight, expand_moment, expand_second, owned[3], 2.0 * (INNER // 8) ** (-0.5), DECAY
    )
    project_new = adamw(
        project_weight, project_moment, project_second, owned[4], 2.0 * BOTTLE ** (-0.5), DECAY
    )
    norm_new = adamw(norm_params, norm_moment, norm_second, norm_grad_owned, NORM_RATE, 0.0)
    return (
        jnp.concatenate(outputs, axis=0),
        jnp.concatenate(input_grads, axis=0),
        reduce_new[0],
        reduce_new[1],
        reduce_new[2],
        conv_new[0],
        conv_new[1],
        conv_new[2],
        squeeze_new[0],
        squeeze_new[1],
        squeeze_new[2],
        expand_new[0],
        expand_new[1],
        expand_new[2],
        project_new[0],
        project_new[1],
        project_new[2],
        norm_new[0],
        norm_new[1],
        norm_new[2],
    )


MESH = pl.DeviceIdType.MESH
PAD = 64
CHUNK = 112
F32 = jnp.float32
BF16 = jnp.bfloat16
STATS = {
    "reduced": (8, 128),
    "widened0": (8, 128),
    "widened1": (8, 128),
    "pool": (8, 128),
    "images": (16, 128),
    "projected0": (8, 256),
    "projected1": (8, 256),
    "back_projected0": (8, 256),
    "back_projected1": (8, 256),
    "back_pool": (8, 128),
    "back_widened0": (8, 128),
    "back_widened1": (16, 128),
    "back_reduced0": (8, 128),
    "back_reduced1": (8, 128),
}
DIRECT = ("reduced", "pool", "back_pool")


def sigmoid(values):
    return 0.5 * jnp.tanh(0.5 * values) + 0.5


def row_ids(width):
    return lax.broadcasted_iota(jnp.int32, (8, width), 0)


def image_sum(rows):
    return rows + pltpu.roll(rows, 4, 0)


def pair_sum(rows):
    even = row_ids(rows.shape[1]) % 2 == 0
    return rows + jnp.where(even, pltpu.roll(rows, 7, 0), pltpu.roll(rows, 1, 0))


def micro_sum(rows):
    return pair_sum(image_sum(rows))


def stack_sums(first, second):
    return jnp.where(row_ids(first.shape[1]) < 4, first, second)


def unstack_sums(stacked):
    upper = row_ids(stacked.shape[1]) < 4
    turned = pltpu.roll(stacked, 4, 0)
    return jnp.where(upper, stacked, turned), jnp.where(upper, turned, stacked)


def fold_lanes(stacked):
    half = stacked.shape[1] // 2
    even = row_ids(half) % 2 == 0
    return jnp.where(even, stacked[:, :half], stacked[:, half:])


def unfold_lanes(folded):
    even = row_ids(folded.shape[1]) % 2 == 0
    left = jnp.where(even, folded, pltpu.roll(folded, 1, 0))
    right = jnp.where(even, pltpu.roll(folded, 7, 0), folded)
    return jnp.concatenate([left, right], axis=1)


def norm_terms(total, square, gain, bias, count):
    center = total * (1.0 / count)
    scale = lax.rsqrt(square * (1.0 / count) - center * center + EPSILON)
    slope = scale * gain
    return center, scale, slope, bias - center * slope


def back_terms(center, scale, slope, bias_sum, gain_sum, count):
    by_value = -slope * scale * (gain_sum * (1.0 / count))
    constant = -slope * (bias_sum * (1.0 / count)) - by_value * center
    return by_value, constant


def tdot(left, right):
    return lax.dot_general(left, right, (((0,), (0,)), ((), ())), preferred_element_type=F32)


def dot_t(left, right):
    return lax.dot_general(left, right, (((1,), (1,)), ((), ())), preferred_element_type=F32)


def in_parts(values, parts):
    found = []
    for _ in range(parts):
        rounded = values.astype(BF16).astype(F32)
        found.append(rounded)
        values = values - rounded
    return found


def exact_dot(left, right, transposed):
    stacked = jnp.concatenate(in_parts(left, 3), axis=0).astype(BF16)
    wide = dot_t(stacked, right) if transposed else jnp.dot(stacked, right, preferred_element_type=F32)
    return wide[0:8] + wide[8:16] + wide[16:24]


def row_dot(left, right):
    high, low = in_parts(left, 2)
    other_high, other_low = in_parts(right, 2)
    return tdot(
        jnp.concatenate([high, high, low, low], axis=0).astype(BF16),
        jnp.concatenate([other_high, other_low, other_high, other_low], axis=0).astype(BF16),
    )


def image_dot(left, right):
    return row_dot(jnp.where(row_ids(left.shape[1]) < 4, left, 0.0), right)


def block_kernel(
    n_dp,
    n_rep,
    x_hbm,
    gy_hbm,
    w1_hbm,
    wc_hbm,
    sq_hbm,
    ex_hbm,
    w3_hbm,
    np_hbm,
    bo_hbm,
    dx_hbm,
    f1_hbm,
    fc_hbm,
    f3_hbm,
    fe_hbm,
    gn_hbm,
    w1_own,
    wc_own,
    sq_own,
    ex_own,
    w3_own,
    np_own,
    gn_out,
    x4,
    gy4,
    x_v,
    gy_v,
    fw1,
    fwc,
    fes,
    fw3,
    es_own,
    np_slots,
    np_full,
    red,
    act,
    columns,
    wid,
    splits,
    mixed,
    proj,
    up,
    bo4,
    dx4,
    dproj,
    d_mixed,
    dn2,
    dwid,
    dcol,
    dn1,
    dred,
    g1,
    gc,
    g3,
    ge,
    gb,
    fix,
    back_own,
    *rest,
):
    n_ar = len(STATS)
    order = {name: k for k, name in enumerate(STATS)}
    ar_slots_a = dict(zip(STATS, rest[0:n_ar]))
    ar_slots_b = dict(zip(STATS, rest[n_ar : 2 * n_ar]))
    rest = rest[2 * n_ar :]
    r1s, ys, r2s, ks, r3s, own = (rest[6 * i : 6 * i + 6] for i in range(6))
    fs = rest[36:40]
    rest = rest[40:]
    local_sem, ar_send_a, ar_recv_a, ar_send_b, ar_recv_b, np_sems, ws, wr, gs, gr = rest

    dp = lax.axis_index("dp")
    rep = lax.axis_index("rep")
    core = lax.rem(rep, 2)
    half_y = lax.div(rep, 2)
    planes = n_dp // 2
    plane_size = 2 * n_rep
    plane = lax.div(dp, 2)
    in_plane = lax.rem(dp, 2) * n_rep + rep
    sibling = (dp, half_y * 2 + (1 - core))
    across = (dp, (1 - half_y) * 2 + core)
    pixels = float(SIDE * SIDE * 2 * n_dp * n_rep)
    pictures = float(2 * n_dp * n_rep)

    x = lax.rem(dp, 2)
    if planes == 4:
        upper = lax.div(plane, 2)
        other_planes = [3 - 3 * upper, 2 - upper, 1 - plane + 4 * upper]
    else:
        other_planes = [lax.rem(plane + step, planes) for step in range(1, planes)]
    flips = ((1, 1, 1), (1, 1, 0), (1, 0, 1), (1, 0, 0), (0, 1, 1), (0, 1, 0), (0, 0, 1), (0, 0, 0))

    def of_flip(z, flip):
        there = [1 - own if turn else own for own, turn in zip((x, half_y, core), flip)]
        return (z * 2 + there[0], there[1] * 2 + there[2])

    plane_peers = [of_flip(plane, flip) for flip in flips[:-1]]
    column_peers = [of_flip(z, flips[-1]) for z in other_planes]
    owner_peers = [of_flip(z, flip) for z in other_planes for flip in (flips[3], flips[7])]
    owner_peers += [of_flip(plane, flips[3])]
    all_peers = [of_flip(z, flip) for z in other_planes for flip in flips] + plane_peers
    me, everyone = dp * n_rep + rep, n_dp * n_rep
    rep_peers = [(dp, lax.rem(rep + step, n_rep)) for step in range(1, n_rep)]

    def remote(src, dst, send_sem, recv_sem, device):
        return pltpu.make_async_remote_copy(
            src_ref=src,
            dst_ref=dst,
            send_sem=send_sem,
            recv_sem=recv_sem,
            device_id=device,
            device_id_type=MESH,
        )

    def send_all(ref, send_sem, recv_sem, peers):
        for device in peers:
            remote(ref, ref, send_sem, recv_sem, device).start()

    def wait_bytes(ref, sem):
        pltpu.make_async_copy(ref, ref, sem).wait()

    def over_rows(body, init):
        def step(index, carry):
            return body(pl.multiple_of(index * CHUNK, CHUNK), carry)

        return lax.fori_loop(0, ROWS // CHUNK, step, init)

    def grouped(values):
        return values.reshape(CHUNK // 8, 8, values.shape[-1])

    def by_four(values):
        return flat(values).reshape(CHUNK // 4, 4, values.shape[-1])

    def flat(values):
        return values.reshape(CHUNK, values.shape[-1])

    own_copies = [
        pltpu.make_async_copy(source, target, local_sem.at[4 + k])
        for k, (source, target) in enumerate(
            (
                (w1_hbm, w1_own),
                (np_hbm, np_own),
                (wc_hbm, wc_own),
                (w3_hbm, w3_own),
                (sq_hbm, sq_own),
                (ex_hbm, ex_own),
            )
        )
    ]
    for copy in own_copies:
        copy.start()
    x_copy = pltpu.make_async_copy(x_hbm, x4, local_sem.at[0])
    gy_copy = pltpu.make_async_copy(gy_hbm, gy4, local_sem.at[1])
    x_copy.start()
    barrier = pltpu.get_barrier_semaphore()
    for device in all_peers:
        pl.semaphore_signal(barrier, inc=1, device_id=device, device_id_type=MESH)

    part = core * 2 + half_y
    own_copies[0].wait()
    q1 = w1_own.shape[0] // 4
    fw1[dp, core, half_y] = w1_own[pl.ds(pl.multiple_of(part * q1, q1), q1), :].astype(BF16)
    core_lanes = pl.ds(pl.multiple_of(core * 128, 128), 128)
    es_lanes = pl.ds(pl.multiple_of(part * 128, 128), 128)
    w3_lanes = pl.ds(pl.multiple_of(part * 256, 128), 256)

    pl.semaphore_wait(barrier, everyone - 1)

    def quarter_w1(c, y):
        return fw1.at[:, c, y]

    def quarter_wc(c, y):
        return fwc.at[:, y, :, pl.ds(pl.multiple_of(c * 128, 128), 128)]

    def quarter_es(c, y):
        return fes.at[:, :, pl.ds(pl.multiple_of((c * 2 + y) * 128, 128), 128)]

    def quarter_w3(c, y):
        return fw3.at[:, :, pl.ds(pl.multiple_of((c * 2 + y) * 256, 128), 256)]

    quarters = (quarter_w1, quarter_wc, quarter_es, quarter_w3)

    def piece(which, d):
        return (
            fw1.at[d, core, half_y],
            fwc.at[d, half_y, :, core_lanes],
            fes.at[d, :, es_lanes],
            fw3.at[d, :, w3_lanes],
        )[which]

    def seven(which):
        return (
            fw1.at[pl.ds(0, n_dp - 1), core, half_y],
            fwc.at[pl.ds(0, n_dp - 1), half_y, :, core_lanes],
            fes.at[pl.ds(0, n_dp - 1), :, es_lanes],
            fw3.at[pl.ds(0, n_dp - 1), :, w3_lanes],
        )[which]

    def gather_out(which):
        send_all(piece(which, dp), ws.at[which, 0], wr.at[which, 0], owner_peers)

    def gather_turn(which):
        wait_bytes(seven(which), wr.at[which, 0])
        mine = quarters[which](core, half_y)
        remote(mine, mine, ws.at[which, 1], wr.at[which, 1], across).start()
        remote(mine, mine, ws.at[which, 2], wr.at[which, 2], sibling).start()

    def gather_hand(which):
        theirs = quarters[which](core, 1 - half_y)
        wait_bytes(theirs, wr.at[which, 1])
        remote(theirs, theirs, ws.at[which, 3], wr.at[which, 3], sibling).start()

    def gather_end(which):
        wait_bytes(quarters[which](1 - core, half_y), wr.at[which, 2])
        wait_bytes(quarters[which](1 - core, 1 - half_y), wr.at[which, 3])

    def to_rows(source, target):
        def body(index, carry):
            values = source[pl.ds(index * (CHUNK // 4), CHUNK // 4)].astype(F32)
            row = pl.multiple_of(index * CHUNK, CHUNK)
            target[pl.ds(row, CHUNK), :] = values.reshape(CHUNK, CHANNELS).astype(BF16)
            return carry

        lax.fori_loop(0, ROWS // CHUNK, body, 0)

    gather_out(0)
    own_copies[2].wait()
    qc = wc_own.shape[0] // 2
    fwc[dp, half_y, :, core_lanes] = wc_own[
        pl.ds(pl.multiple_of(half_y * qc, qc), qc), core_lanes
    ].astype(BF16)
    gather_out(1)

    own_copies[1].wait()
    shard = np_own.shape[0]
    lanes_id = lax.broadcasted_iota(jnp.int32, (8, 128), 1)
    turn = lax.rem(shard * dp, 128)
    np_rows = []
    for at in range(0, shard, 128):
        width = min(128, shard - at)
        piece_row = np_own[pl.ds(at, width)].reshape(1, width)
        if width < 128:
            piece_row = jnp.concatenate([piece_row, jnp.zeros((1, 128 - width), F32)], axis=1)
        np_rows.append(piece_row)
    np_rows.append(jnp.zeros((8 - len(np_rows), 128), F32))
    np_turned = jnp.concatenate(np_rows, axis=0).astype(BF16).astype(F32)
    np_turned = pltpu.roll(np_turned, turn, 1)
    np_slots[dp] = jnp.where(lanes_id < turn, pltpu.roll(np_turned, 1, 0), np_turned)
    send_all(np_slots.at[dp], np_sems.at[0], np_sems.at[1], owner_peers)
    for copy in own_copies[3:]:
        copy.wait()
    ex_rows = ex_own.shape[0]
    es_own[:, 0:128] = sq_own[...].astype(BF16)
    es_own[0:ex_rows, 128:384] = ex_own[:, 0:256].astype(BF16)
    es_own[ex_rows : 2 * ex_rows, 128:384] = ex_own[:, 256:512].astype(BF16)
    es_own[:, 384:512] = jnp.zeros((2 * ex_rows, 128), BF16)
    fes[dp, :, es_lanes] = es_own[:, es_lanes]
    fw3[dp, :, w3_lanes] = w3_own[:, w3_lanes].astype(BF16)
    gy_copy.start()
    x_copy.wait()
    to_rows(x4, x_v)
    gather_turn(0)
    zero_rows = jnp.zeros((PAD, BOTTLE), F32)
    for side in range(3):
        act[side, 0:PAD, :] = zero_rows
        act[side, PAD + ROWS : 2 * PAD + ROWS, :] = zero_rows
    for lane_block in range(9):
        dcol[0:PAD, lane_block * 256 : lane_block * 256 + 256] = zero_rows
        dcol[PAD + ROWS : 2 * PAD + ROWS, lane_block * 256 : lane_block * 256 + 256] = zero_rows
    gather_hand(0)
    gather_turn(1)

    def sum_start(k, payload):
        if k in DIRECT:
            ar_slots_a[k][me] = payload
            send_all(ar_slots_a[k].at[me], ar_send_a.at[order[k]], ar_recv_a.at[order[k]], all_peers)
        else:
            ar_slots_a[k][in_plane] = payload
            send_all(ar_slots_a[k].at[in_plane], ar_send_a.at[order[k]], ar_recv_a.at[order[k]], plane_peers)

    def sum_slots(slots, count):
        sums = [slots[slot] for slot in range(count)]
        while len(sums) > 1:
            sums = [sums[i] + sums[i + 1] for i in range(0, len(sums), 2)]
        return sums[0]

    def sum_turn(k):
        if k in DIRECT:
            return
        wait_bytes(ar_slots_a[k].at[pl.ds(0, plane_size - 1)], ar_recv_a.at[order[k]])
        ar_slots_b[k][plane] = sum_slots(ar_slots_a[k], plane_size)
        send_all(ar_slots_b[k].at[plane], ar_send_b.at[order[k]], ar_recv_b.at[order[k]], column_peers)

    def sum_end(k):
        if k in DIRECT:
            wait_bytes(ar_slots_a[k].at[pl.ds(0, everyone - 1)], ar_recv_a.at[order[k]])
            return sum_slots(ar_slots_a[k], everyone)
        wait_bytes(ar_slots_b[k].at[pl.ds(0, planes - 1)], ar_recv_b.at[order[k]])
        return sum_slots(ar_slots_b[k], planes)

    def lanes_of(index, width):
        return pl.ds(pl.multiple_of(index * width, 128), width)

    cut = 64
    conv_rows = {1: pl.ds(0, cut), 2: pl.ds(cut, gc.shape[2] - cut)}
    grads = (g1, gc, gc, g3, ge, gb)
    turned_kinds = (0, 5)

    def half_of(which, c):
        ref = grads[which]
        if which in turned_kinds:
            return ref.at[c]
        if which in conv_rows:
            return ref.at[:, :, conv_rows[which], lanes_of(c, 128)]
        return ref.at[:, :, lanes_of(c, (512, 256)[which - 3])]

    def y_part(which, ref, y):
        if which in turned_kinds:
            return ref.at[y]
        if which < 3:
            return ref.at[:, y]
        return ref.at[:, :, lanes_of(y, (256, 128)[which - 3])]

    def quarter_of(which, c, y):
        ref = grads[which]
        if which in turned_kinds:
            return ref.at[c, y]
        if which in conv_rows:
            return ref.at[:, y, conv_rows[which], lanes_of(c, 128)]
        return ref.at[:, :, lanes_of(c * 2 + y, (256, 128)[which - 3])]

    def final_part(which, c, y):
        if which == 0:
            return fs[0].at[c, y]
        if which in conv_rows:
            return fs[1].at[y, conv_rows[which], lanes_of(c, 128)]
        return fs[which - 1].at[:, lanes_of(c * 2 + y, (256, 128)[which - 3])]

    def of_owner(which, ref, d):
        return ref.at[:, lanes_of(d, CHANNELS // n_dp)] if which in turned_kinds else ref.at[d]

    def in_blocks(which, body):
        if which in turned_kinds:
            count = 4
            rows = grads[which].shape[2] // count
            block = lambda index: pl.ds(pl.multiple_of(index * rows, rows), rows)
        else:
            count, block = n_dp, lambda index: index

        def step(index, carry):
            body(block(index))
            return carry

        lax.fori_loop(0, count, step, 0)

    def reduce_core(which):
        remote(
            half_of(which, 1 - core), r1s[which], gs.at[which, 0], gr.at[which, 0], sibling
        ).start()

    def reduce_y(which):
        wait_bytes(r1s[which], gr.at[which, 0])
        away = quarter_of(which, core, 1 - half_y)
        mine = quarter_of(which, core, half_y)
        there = y_part(which, r1s[which], 1 - half_y)
        here = y_part(which, r1s[which], half_y)

        def add_away(at):
            ys[which][at] = (away[at].astype(F32) + there[at].astype(F32)).astype(
                ys[which].dtype
            )

        in_blocks(which, add_away)
        remote(ys[which], r2s[which], gs.at[which, 1], gr.at[which, 1], across).start()

        def add_mine(at):
            mine[at] = (mine[at].astype(F32) + here[at].astype(F32)).astype(mine.dtype)

        in_blocks(which, add_mine)

    def reduce_owner(which):
        wait_bytes(r2s[which], gr.at[which, 1])
        mine = quarter_of(which, core, half_y)

        def add(at):
            ks[which][at] = (mine[at].astype(F32) + r2s[which][at].astype(F32)).astype(
                ks[which].dtype
            )

        in_blocks(which, add)
        for device in owner_peers:
            remote(
                of_owner(which, ks[which], device[0]),
                r3s[which].at[dp],
                gs.at[which, 2],
                gr.at[which, 2],
                device,
            ).start()
        own[which][...] = of_owner(which, mine, dp)[...].astype(F32) + of_owner(
            which, r2s[which], dp
        )[...].astype(F32)
        r3s[which][dp] = jnp.zeros(own[which].shape, r3s[which].dtype)

    def owner_total(which):
        wait_bytes(r3s[which].at[pl.ds(0, n_dp - 1)], gr.at[which, 2])
        total = own[which][...]
        for slot in range(n_dp):
            total = total + r3s[which][slot].astype(F32)
        return total

    def reduce_spread(which):
        total = owner_total(which)
        if which == 0:
            rows = pl.ds(pl.multiple_of(part * (BOTTLE // 4), BOTTLE // 4), BOTTLE // 4)
            total = total - fix[0, rows, :]
            for m in range(2):
                total = total - fix[1 + m, rows, :] * back_own[m]
        mine = final_part(which, core, half_y)
        mine[...] = total
        send_all(mine, gs.at[which, 3], gr.at[which, 3], rep_peers)

    def three_parts(which):
        if which == 0:
            return r1s[0].at[0, :, pl.ds(0, 3 * CHANNELS // n_dp)]
        return r1s[which].at[pl.ds(0, 3), 0] if which < 3 else y_part(which, r1s[which], 0).at[pl.ds(0, 3)]

    def reduce_end(which):
        wait_bytes(three_parts(which), gr.at[which, 3])

    gather_end(0)
    red[...] = jnp.dot(x_v[...], fw1[...].reshape(CHANNELS, BOTTLE), preferred_element_type=F32)

    def sums_of(ref, start, width):
        def body(row, carry):
            values = grouped(ref[pl.ds(row, CHUNK), start : start + width])
            return carry[0] + jnp.sum(values, axis=0), carry[1] + jnp.sum(values * values, axis=0)

        zero = jnp.zeros((8, width), F32)
        return over_rows(body, (zero, zero))

    def joined(found):
        both = [jnp.concatenate(item, axis=1) for item in zip(*found)]
        return fold_lanes(stack_sums(micro_sum(both[0]), micro_sum(both[1])))

    def both_sums(name):
        return unstack_sums(unfold_lanes(sum_end(name)))

    sum_start("reduced", joined([sums_of(red, 0, 256)]))
    gather_out(2)
    gather_out(3)

    gy_copy.wait()
    to_rows(gy4, gy_v)
    wait_bytes(np_slots.at[pl.ds(0, n_dp - 1)], np_sems.at[1])
    np_full[...] = jnp.zeros(np_full.shape, F32)
    for d in range(n_dp):
        at = shard * d // 128
        np_full[at : at + 8, :] = np_full[at : at + 8, :] + np_slots[d]

    def vector(at, width):
        rows = [np_full[at // 128 + k : at // 128 + k + 1, :] for k in range(width // 128)]
        return jnp.concatenate(rows, axis=1) if len(rows) > 1 else rows[0]

    gain_one, bias_one = vector(0, 256), vector(256, 256)
    gain_two, bias_two = vector(512, 512), vector(1024, 512)
    gain_pool, bias_pool = vector(1536, 128), vector(1664, 128)
    bias_expand = vector(1792, 512)
    gain_three, bias_three = vector(2304, 1024), vector(3328, 1024)

    total, square = both_sums("reduced")
    center1, scale1, mul1, add1 = norm_terms(total, square, gain_one, bias_one, pixels)

    def make_active(row, carry):
        turned = grouped(red[pl.ds(row, CHUNK), :]) * mul1 + add1
        act[1, pl.ds(PAD + row, CHUNK), :] = flat(turned * sigmoid(turned))
        return carry

    over_rows(make_active, 0)
    gather_hand(1)
    gather_turn(2)
    gather_turn(3)
    place = lax.rem(lax.broadcasted_iota(jnp.int32, (CHUNK, BOTTLE), 0) // 4, SIDE)
    not_last = place != SIDE - 1
    not_first = place != 0

    def beside(side, row, distance, lanes=slice(0, BOTTLE)):
        near = act[side, pl.ds(PAD + row - 8, CHUNK + 16), lanes]
        return pltpu.roll(near, (CHUNK + 16 - distance) % (CHUNK + 16), 0)[8 : 8 + CHUNK]

    def shift_active(row, carry):
        act[2, pl.ds(PAD + row, CHUNK), :] = jnp.where(not_last, beside(1, row, 4), 0.0)
        act[0, pl.ds(PAD + row, CHUNK), :] = jnp.where(not_first, beside(1, row, -4), 0.0)
        return carry

    over_rows(shift_active, 0)

    def make_columns(row, carry):
        for tap in range(9):
            down, side = tap // 3 - 1, tap % 3
            values = act[side, pl.ds(PAD + row + 56 * down, CHUNK), :].astype(BF16)
            columns[0, pl.ds(row, CHUNK), tap * 128 : tap * 128 + 128] = values[:, 0:128]
            columns[1, pl.ds(row, CHUNK), tap * 128 : tap * 128 + 128] = values[:, 128:256]
        return carry

    over_rows(make_columns, 0)
    gather_end(1)
    own_half = n_dp // 2

    def filters(group):
        return fwc[group * own_half : (group + 1) * own_half].reshape(9 * 128, BOTTLE)

    halves2 = (slice(0, 256), slice(256, 512))
    for group, lanes in enumerate(halves2):
        wid[:, lanes] = jnp.dot(columns[group], filters(group), preferred_element_type=F32)
        sum_start(f"widened{group}", joined([sums_of(wid, group * 256, 256)]))
    sum_turn("widened0")
    sum_turn("widened1")
    gather_hand(2)
    gather_hand(3)

    norm2 = []
    pooled = jnp.zeros((8, BOTTLE), F32)
    for group, lanes in enumerate(halves2):
        total, square = both_sums(f"widened{group}")
        norm2.append(norm_terms(total, square, gain_two[:, lanes], bias_two[:, lanes], pixels))
        m2, a2 = norm2[group][2:4]

        def make_splits(row, carry):
            turned = grouped(wid[pl.ds(row, CHUNK), lanes]) * m2 + a2
            values = turned * sigmoid(turned)
            splits[pl.ds(row, CHUNK), lanes] = flat(values)
            return carry + jnp.sum(values, axis=0)

        pooled = over_rows(make_splits, pooled)
    pooled = image_sum(pooled) * (1.0 / (SIDE * SIDE))
    gather_end(2)
    squeeze = fes[:, :, 0:128].reshape(BOTTLE, INNER)
    ex_both = fes[:, :, 128:384]
    expand = jnp.concatenate(
        [
            ex_both[:, 0:ex_rows].reshape(INNER, 256),
            ex_both[:, ex_rows : 2 * ex_rows].reshape(INNER, 256),
        ],
        axis=1,
    )
    pre_pool = exact_dot(pooled, squeeze, False)
    sum_start("pool", stack_sums(pair_sum(pre_pool), pair_sum(pre_pool * pre_pool)))
    first_micro = lax.rem(row_ids(BOTTLE), 4) < 2

    def make_normed(row, carry):
        rows = pl.ds(row, CHUNK)
        normed = (grouped(red[rows, :]) - center1) * scale1
        dwid[rows, 0:256] = flat(jnp.where(first_micro, normed, 0.0)).astype(BF16)
        dwid[rows, 256:512] = flat(jnp.where(first_micro, 0.0, normed)).astype(BF16)
        return carry + jnp.sum(grouped(x_v[rows, :].astype(F32)), axis=0)

    image_sums = micro_sum(over_rows(make_normed, jnp.zeros((8, CHANNELS), F32)))
    sum_start(
        "images",
        jnp.concatenate(
            [
                image_sums[2 * m : 2 * m + 1, at : at + 128]
                for m in range(2)
                for at in range(0, CHANNELS, 128)
            ],
            axis=0,
        ),
    )
    normed_images = tdot(dwid[...], x_v[...]).astype(BF16)
    normed_images = normed_images.reshape(2, 2, 2, BOTTLE // 4, CHANNELS)
    for m in range(2):
        gb[:, :, m * (BOTTLE // 4) : (m + 1) * (BOTTLE // 4)] = normed_images[m]
    reduce_core(5)
    total, square = unstack_sums(sum_end("pool"))
    center_p, scale_p, mul_p, add_p = norm_terms(total, square, gain_pool, bias_pool, pictures)
    normed_p = (pre_pool - center_p) * scale_p
    norm_p = pre_pool * mul_p + add_p
    gate_p = sigmoid(norm_p)
    hidden = norm_p * gate_p
    slope_p = gate_p * (1.0 + norm_p * (1.0 - gate_p))
    logits = exact_dot(hidden, expand, False) + bias_expand
    left, right = logits[:, 0:256], logits[:, 256:512]
    most = jnp.maximum(left, right)
    left, right = jnp.exp(left - most), jnp.exp(right - most)
    att0 = left / (left + right)
    att1 = right / (left + right)

    gather_end(3)
    last = fw3[...].reshape(BOTTLE, CHANNELS)
    def make_mixed(row, carry):
        rows = pl.ds(row, CHUNK)
        values = grouped(splits[rows, 0:256]) * att0 + grouped(splits[rows, 256:512]) * att1
        mixed[rows, :] = flat(values).astype(BF16)
        return carry

    over_rows(make_mixed, 0)
    halves3 = (slice(0, 512), slice(512, 1024))
    blocks3 = [[slice(512 * h + k, 512 * h + k + 256) for k in (0, 256)] for h in range(2)]
    for half, lanes in enumerate(halves3):
        proj[:, lanes] = jnp.dot(mixed[...], last[:, lanes], preferred_element_type=F32)
        sum_start(
            f"projected{half}", joined([sums_of(proj, 512 * half + k, 256) for k in (0, 256)])
        )
    sum_turn("projected0")
    sum_turn("projected1")
    sum_turn("images")
    reduce_y(5)

    norm3 = []
    zero = jnp.zeros((8, 256), F32)
    for half, lanes in enumerate(halves3):
        total, square = both_sums(f"projected{half}")
        norm3.append(norm_terms(total, square, gain_three[:, lanes], bias_three[:, lanes], pixels))
        found = []
        for k, block in enumerate(blocks3[half]):
            c3, s3, m3, a3 = (item[:, k * 256 : k * 256 + 256] for item in norm3[half])

            def make_out(row, carry):
                rows = pl.ds(row, CHUNK)
                values = grouped(proj[rows, block])
                summed = grouped(x_v[rows, block].astype(F32)) + (values * m3 + a3)
                gate = sigmoid(summed)
                bo4[pl.ds(row // 4, CHUNK // 4), :, block] = by_four(summed * gate).astype(BF16)
                upstream = grouped(gy_v[rows, block].astype(F32)) * (
                    gate * (1.0 + summed * (1.0 - gate))
                )
                up[rows, block] = flat(upstream)
                normed = (values - c3) * s3
                return carry[0] + jnp.sum(upstream, axis=0), carry[1] + jnp.sum(
                    upstream * normed, axis=0
                )

            found.append(over_rows(make_out, (zero, zero)))
        sum_start(f"back_projected{half}", joined(found))
    bo_copy = pltpu.make_async_copy(bo4, bo_hbm, local_sem.at[2])
    bo_copy.start()

    def write_norm(at, pattern):
        at = at // 128
        both = pattern[0:1, :] + pattern[2:3, :]
        for k in range(both.shape[1] // 128):
            np_full[at + k : at + k + 1, :] = both[:, k * 128 : k * 128 + 128]

    sum_turn("back_projected0")
    sum_turn("back_projected1")
    reduce_owner(5)

    for half, lanes in enumerate(halves3):
        bias_sum, gain_sum = both_sums(f"back_projected{half}")
        write_norm(2304 + 512 * half, gain_sum)
        write_norm(3328 + 512 * half, bias_sum)
        by_value, constant = back_terms(*norm3[half][0:3], bias_sum, gain_sum, pixels)
        for k, block in enumerate(blocks3[half]):
            m3, v3, k3 = (
                item[:, k * 256 : k * 256 + 256] for item in (norm3[half][2], by_value, constant)
            )

            def make_dproj(row, carry):
                rows = pl.ds(row, CHUNK)
                values = grouped(up[rows, block]) * m3 + grouped(proj[rows, block]) * v3 + k3
                dproj[rows, block] = flat(values).astype(BF16)
                return carry

            over_rows(make_dproj, 0)
        part_mixed = dot_t(dproj[:, lanes], last[:, lanes])
        d_mixed[...] = part_mixed if half == 0 else d_mixed[...] + part_mixed

    def attend(row, carry):
        rows = pl.ds(row, CHUNK)
        values = grouped(d_mixed[rows, :])
        return (
            carry[0] + jnp.sum(values * grouped(splits[rows, 0:256]), axis=0),
            carry[1] + jnp.sum(values * grouped(splits[rows, 256:512]), axis=0),
        )

    d_att0, d_att1 = over_rows(attend, (zero, zero))
    d_att0, d_att1 = image_sum(d_att0), image_sum(d_att1)
    both = att0 * d_att0 + att1 * d_att1
    d_logits = jnp.concatenate([att0 * (d_att0 - both), att1 * (d_att1 - both)], axis=1)
    d_hidden = exact_dot(d_logits, expand, True)
    d_pool = d_hidden * slope_p
    per_micro = stack_sums(pair_sum(d_pool), pair_sum(d_pool * normed_p))
    sum_start("back_pool", per_micro)
    ex_sum = pair_sum(d_logits)
    ex_sum = ex_sum + pltpu.roll(ex_sum, 2, 0)
    ex_rows_sum = ex_sum[:, 0:128]
    for k in range(1, 4):
        ex_rows_sum = jnp.where(row_ids(128) == k, ex_sum[:, k * 128 : k * 128 + 128], ex_rows_sum)

    grad_ex = image_dot(hidden, d_logits)
    grad_ex = grad_ex.reshape(n_dp, ex_rows, 512)
    ge[:, 0:ex_rows, 128:384] = grad_ex[:, :, 0:256]
    ge[:, ex_rows : 2 * ex_rows, 128:384] = grad_ex[:, :, 256:512]
    ge[:, :, 384:512] = jnp.zeros((n_dp, 2 * ex_rows, 128), F32)
    g3[...] = tdot(mixed[...], dproj[...]).reshape(g3.shape)
    reduce_core(3)
    held = []
    for group, att in ((0, att0), (1, att1)):
        lanes = halves2[group]
        c2, s2, m2, a2 = norm2[group]

        def make_dn2(row, carry):
            rows = pl.ds(row, CHUNK)
            values = grouped(wid[rows, lanes])
            turned = values * m2 + a2
            gate = sigmoid(turned)
            slope = gate * (1.0 + turned * (1.0 - gate))
            down = grouped(d_mixed[rows, :]) * att * slope
            dn2[rows, lanes] = flat(down)
            splits[rows, lanes] = flat(slope)
            normed = (values - c2) * s2
            terms = (down, down * normed, slope, slope * normed)
            return tuple(item + jnp.sum(term, axis=0) for item, term in zip(carry, terms))

        held.append([image_sum(item) for item in over_rows(make_dn2, (zero,) * 4)])
    pool_bias_sum, pool_gain_sum = unstack_sums(sum_end("back_pool"))
    write_norm(1536, pool_gain_sum)
    write_norm(1664, pool_bias_sum)
    d_pre_pool = mul_p * (
        d_pool - pool_bias_sum * (1.0 / pictures) - normed_p * (pool_gain_sum * (1.0 / pictures))
    )
    d_pooled = exact_dot(d_pre_pool, squeeze, True) * (1.0 / (SIDE * SIDE))
    for group in range(2):
        down, down_normed, slope, slope_normed = held[group]
        payload = fold_lanes(
            stack_sums(
                pair_sum(down + d_pooled * slope), pair_sum(down_normed + d_pooled * slope_normed)
            )
        )
        if group == 1:
            payload = jnp.concatenate([payload, ex_rows_sum], axis=0)
        sum_start(f"back_widened{group}", payload)
    ge[:, :, 0:128] = image_dot(pooled, d_pre_pool).reshape(n_dp, 2 * ex_rows, 128)
    reduce_core(4)
    sum_turn("back_widened0")
    sum_turn("back_widened1")
    reduce_y(3)
    reduce_y(4)
    back_total = owner_total(5)
    back_own[0] = back_total[0 : BOTTLE // 4]
    back_own[1] = back_total[BOTTLE // 4 :]

    small_zero = jnp.zeros((8, 128), F32)
    for group, lanes in enumerate(halves2):
        whole = sum_end(f"back_widened{group}")
        if group == 1:
            np_full[14:18, :] = whole[8:12]
        bias_sum, gain_sum = unstack_sums(unfold_lanes(whole[0:8]))
        write_norm(512 + 256 * group, gain_sum)
        write_norm(1024 + 256 * group, bias_sum)
        m2 = norm2[group][2]
        v2, k2 = back_terms(*norm2[group][0:3], bias_sum, gain_sum, pixels)
        pooled_m2 = d_pooled * m2

        def make_dwid(row, carry):
            rows = pl.ds(row, CHUNK)
            values = grouped(dn2[rows, lanes]) * m2 + grouped(splits[rows, lanes]) * pooled_m2
            values = values + grouped(wid[rows, lanes]) * v2 + k2
            dwid[rows, lanes] = flat(values).astype(BF16)
            return carry

        over_rows(make_dwid, 0)
        gc[group * own_half : (group + 1) * own_half] = tdot(
            columns[group], dwid[:, lanes]
        ).reshape(own_half, 2, 9 * 128 // own_half // 2, BOTTLE)
    reduce_core(1)
    reduce_core(2)
    for group, lanes in enumerate(halves2):
        dcol[PAD : PAD + ROWS, group * 1152 : group * 1152 + 1152] = dot_t(
            dwid[:, lanes], filters(group)
        )
        inner = slice(group * 128, group * 128 + 128)

        def gather_taps(row, carry):
            for side in range(3):
                total = None
                for down in range(3):
                    at = group * 1152 + (3 * down + side) * 128
                    values = dcol[pl.ds(PAD + row - 56 * (down - 1), CHUNK), at : at + 128]
                    total = values if total is None else total + values
                act[side, pl.ds(PAD + row, CHUNK), inner] = total
            return carry

        over_rows(gather_taps, 0)
        c1, s1, m1, a1 = (item[:, inner] for item in (center1, scale1, mul1, add1))
        not_first1, not_last1 = not_first[:, inner], not_last[:, inner]

        def make_dn1(row, carry):
            rows = pl.ds(row, CHUNK)
            d_active = act[1, pl.ds(PAD + row, CHUNK), inner]
            d_active = d_active + jnp.where(not_first1, beside(2, row, -4, inner), 0.0)
            d_active = d_active + jnp.where(not_last1, beside(0, row, 4, inner), 0.0)
            values = grouped(red[rows, inner])
            turned = values * m1 + a1
            gate = sigmoid(turned)
            slope = gate * (1.0 + turned * (1.0 - gate))
            down = grouped(d_active) * slope
            dn1[rows, inner] = flat(down)
            mixed[rows, inner] = flat(down * m1).astype(BF16)
            normed = (values - c1) * s1
            return carry[0] + jnp.sum(down, axis=0), carry[1] + jnp.sum(down * normed, axis=0)

        bias_sum, gain_sum = over_rows(make_dn1, (small_zero, small_zero))
        sum_start(f"back_reduced{group}", stack_sums(micro_sum(bias_sum), micro_sum(gain_sum)))
        if group == 0:
            reduce_owner(3)
            reduce_owner(4)
    reduce_y(1)
    reduce_y(2)
    sum_turn("back_reduced0")
    g1[...] = tdot(mixed[...], x_v[...]).reshape(g1.shape)
    reduce_core(0)
    sum_turn("back_reduced1")
    reduce_owner(1)
    reduce_y(0)
    reduce_owner(2)
    found = [unstack_sums(sum_end(f"back_reduced{group}")) for group in range(2)]
    bias_sum, gain_sum = (jnp.concatenate(item, axis=1) for item in zip(*found))
    write_norm(0, gain_sum)
    write_norm(256, bias_sum)
    by_value, constant = back_terms(center1, scale1, mul1, bias_sum, gain_sum, pixels)
    def make_dred(row, carry):
        rows = pl.ds(row, CHUNK)
        values = grouped(dn1[rows, :]) * mul1 + grouped(red[rows, :]) * by_value + constant
        dred[rows, :] = flat(values).astype(BF16)
        return carry

    over_rows(make_dred, 0)
    proj[...] = dot_t(dred[...], fw1[...].reshape(CHANNELS, BOTTLE))

    by_bias = mul1 * bias_sum * (1.0 / pixels)
    by_gain = mul1 * gain_sum * (1.0 / pixels)
    image_sums = sum_end("images")
    ids = lax.broadcasted_iota(jnp.int32, (16, 128), 0)
    own_sums = [
        jnp.sum(jnp.where(ids == m * n_dp + dp, image_sums, 0.0), axis=0, keepdims=True)
        for m in range(2)
    ]
    ids = row_ids(128)
    fix[0] = row_dot(by_bias, jnp.where(ids == 0, own_sums[0], jnp.where(ids == 2, own_sums[1], 0.0)))
    for m in range(2):
        fix[1 + m] = row_dot(by_gain, jnp.where(ids == 2 * m, 1.0, 0.0))
    reduce_spread(3)
    reduce_spread(4)
    reduce_owner(0)
    reduce_spread(1)

    def make_dx(row, carry):
        for start in range(0, CHANNELS, 256):
            lanes = slice(start, start + 256)
            values = up[pl.ds(row, CHUNK), lanes] + proj[pl.ds(row, CHUNK), lanes]
            dx4[pl.ds(row // 4, CHUNK // 4), :, lanes] = values.reshape(CHUNK // 4, 4, 256)
        return carry

    over_rows(make_dx, 0)
    dx_copy = pltpu.make_async_copy(dx4, dx_hbm, local_sem.at[3])
    dx_copy.start()
    norm_rows = np_full[0:8, :]
    for d in range(1, n_dp):
        at = shard * d // 128
        norm_rows = jnp.where(dp == d, np_full[at : at + 8, :], norm_rows)
    norm_rows = pltpu.roll(norm_rows, lax.rem(128 - turn, 128), 1)
    gn_out[...] = jnp.where(lanes_id < 128 - turn, norm_rows, pltpu.roll(norm_rows, 7, 0))
    reduce_spread(2)
    reduce_spread(0)
    out_copies = [
        pltpu.make_async_copy(source, target, local_sem.at[10 + k])
        for k, (source, target) in enumerate(
            (
                (gn_out, gn_hbm),
                (fs[2], f3_hbm),
                (fs[3], fe_hbm),
                (fs[1], fc_hbm),
                (fs[0], f1_hbm),
            )
        )
    ]
    out_copies[0].start()
    for which in (3, 4, 1, 2, 0):
        reduce_end(which)
        if which != 1:
            out_copies[{3: 1, 4: 2, 2: 3, 0: 4}[which]].start()

    bo_copy.wait()
    dx_copy.wait()
    for copy in out_copies:
        copy.wait()
    for k in STATS:
        if k in DIRECT:
            wait_bytes(ar_slots_a[k].at[pl.ds(0, everyone - 1)], ar_send_a.at[order[k]])
        else:
            wait_bytes(ar_slots_a[k].at[pl.ds(0, plane_size - 1)], ar_send_a.at[order[k]])
            wait_bytes(ar_slots_b[k].at[pl.ds(0, planes - 1)], ar_send_b.at[order[k]])
    wait_bytes(np_slots.at[pl.ds(0, n_dp - 1)], np_sems.at[0])
    for which in range(4):
        wait_bytes(seven(which), ws.at[which, 0])
        for stage in range(1, 4):
            wait_bytes(quarters[which](core, half_y), ws.at[which, stage])
    for which in range(6):
        wait_bytes(r1s[which], gs.at[which, 0])
        wait_bytes(r2s[which], gs.at[which, 1])
        wait_bytes(r3s[which].at[pl.ds(0, n_dp - 1)], gs.at[which, 2])
        if which < 5:
            wait_bytes(three_parts(which), gs.at[which, 3])


def update_kernel(*refs):
    sources, targets = refs[0:25], refs[25:45]
    inputs, outs, through = refs[45:68], refs[68:86], refs[86:88]
    pass_sems, in_sems, out_sems = refs[88:91]
    fetching, passing = [], []
    half = SIDE * SIDE // 2
    for number, (which, at, count) in enumerate(((1, 0, half), (1, half, half), (0, 0, 2 * half))):
        rows = pl.ds(at, count)
        fetching.append(
            pltpu.make_async_copy(
                sources[which].at[rows], through[which].at[rows], pass_sems.at[0, number]
            )
        )
        passing.append(
            pltpu.make_async_copy(
                through[which].at[rows], targets[which].at[rows], pass_sems.at[1, number]
            )
        )
    for copy in fetching:
        copy.start()
    coming = [
        pltpu.make_async_copy(source, held, in_sems.at[k])
        for k, (source, held) in enumerate(zip(sources[2:], inputs))
    ]
    for copy in coming:
        copy.start()
    grads, states = inputs[0:5], inputs[5:23]
    going = [
        pltpu.make_async_copy(held, target, out_sems.at[k])
        for k, (held, target) in enumerate(zip(outs, targets[2:]))
    ]
    ex_rows = states[9].shape[0]
    shard = states[15].shape[0]
    fans = (CHANNELS, 9 * BOTTLE // RADIX, BOTTLE, INNER // 8, BOTTLE)
    for copy in coming[0:5]:
        copy.wait()
    found = (
        grads[0][...].T,
        grads[1][...],
        grads[3][:, 0:128],
        jnp.concatenate([grads[3][0:ex_rows, 128:384], grads[3][ex_rows:, 128:384]], axis=1),
        grads[2][...],
    )
    for order, k in enumerate((3, 2, 4, 0, 1)):
        for copy in coming[5 + 3 * k : 8 + 3 * k]:
            copy.wait()
        new = adamw(
            states[3 * k][...],
            states[3 * k + 1][...],
            states[3 * k + 2][...],
            found[k],
            2.0 * fans[k] ** (-0.5),
            DECAY,
        )
        for j in range(3):
            outs[3 * k + j][...] = new[j]
            going[3 * k + j].start()
        if order < 3:
            fetching[order].wait()
            passing[order].start()
    for copy in coming[20:23]:
        copy.wait()
    for at in range(0, shard, 128):
        width = min(128, shard - at)
        lanes = pl.ds(at, width)
        new = adamw(
            *[states[15 + j][lanes].reshape(1, width) for j in range(3)],
            grads[4][at // 128 : at // 128 + 1, 0:width],
            NORM_RATE,
            0.0,
        )
        for j in range(3):
            outs[15 + j][lanes] = new[j].reshape(width)
    for copy in going[15:18]:
        copy.start()
    for copy in passing + going:
        copy.wait()


def fused_device(
    images,
    out_grad,
    reduce_weight,
    reduce_moment,
    reduce_second,
    conv_weight,
    conv_moment,
    conv_second,
    squeeze_weight,
    squeeze_moment,
    squeeze_second,
    expand_weight,
    expand_moment,
    expand_second,
    project_weight,
    project_moment,
    project_second,
    norm_params,
    norm_moment,
    norm_second,
):
    n_dp, n_rep = lax.axis_size("dp"), lax.axis_size("rep")
    by_pixel = lambda values: jnp.transpose(values, (1, 2, 0, 3)).reshape(-1, 4, CHANNELS)
    qc = conv_weight.shape[0] // 2
    q1 = reduce_weight.shape[0] // 4
    pe = squeeze_weight.shape[0]
    vmem = pltpu.VMEM
    pixel_form = (SIDE * SIDE, 4, CHANNELS)
    scratch = [
        *[
            vmem(values.shape, F32)
            for values in (
                reduce_weight,
                conv_weight,
                squeeze_weight,
                expand_weight,
                project_weight,
                norm_params,
            )
        ],
        vmem((8, 128), F32),
        vmem(pixel_form, BF16),
        vmem(pixel_form, BF16),
        vmem((ROWS, CHANNELS), BF16),
        vmem((ROWS, CHANNELS), BF16),
        vmem((n_dp, 2, 2, q1, BOTTLE), BF16),
        vmem((n_dp, 2, qc, BOTTLE), BF16),
        vmem((n_dp, pe, 512), BF16),
        vmem((n_dp, pe, CHANNELS), BF16),
        vmem((pe, 512), BF16),
        vmem((n_dp, 8, 128), F32),
        vmem((40, 128), F32),
        vmem((ROWS, BOTTLE), F32),
        vmem((3, ROWS + 2 * PAD, BOTTLE), F32),
        vmem((2, ROWS, 9 * 128), BF16),
        vmem((ROWS, 512), F32),
        vmem((ROWS, 512), F32),
        vmem((ROWS, BOTTLE), BF16),
        vmem((ROWS, CHANNELS), F32),
        vmem((ROWS, CHANNELS), F32),
        vmem(pixel_form, BF16),
        vmem(pixel_form, F32),
        vmem((ROWS, CHANNELS), BF16),
        vmem((ROWS, BOTTLE), F32),
        vmem((ROWS, 512), F32),
        vmem((ROWS, 512), BF16),
        vmem((ROWS + 2 * PAD, 2 * 9 * 128), F32),
        vmem((ROWS, BOTTLE), F32),
        vmem((ROWS, BOTTLE), BF16),
        vmem((2, 2, BOTTLE // 4, CHANNELS), F32),
        vmem((n_dp, 2, qc, BOTTLE), F32),
        vmem((n_dp, pe, CHANNELS), F32),
        vmem((n_dp, pe, 512), F32),
        vmem((2, 2, BOTTLE // 2, CHANNELS), BF16),
        vmem((3, BOTTLE, CHANNELS // n_dp), F32),
        vmem((2, BOTTLE // 4, CHANNELS // n_dp), F32),
    ]
    direct = n_dp * n_rep
    scratch += [
        vmem((direct if k in DIRECT else 2 * n_rep,) + shape, F32) for k, shape in STATS.items()
    ]
    scratch += [vmem((n_dp // 2,) + shape, F32) for shape in STATS.values()]
    cut = 64
    lanes1 = CHANNELS // n_dp
    half = [
        (2, BOTTLE // 4, CHANNELS),
        (n_dp, 2, cut, 128),
        (n_dp, 2, qc - cut, 128),
        (n_dp, pe, 512),
        (n_dp, pe, 256),
        (2, BOTTLE // 2, CHANNELS),
    ]
    quarter = [
        (BOTTLE // 4, CHANNELS),
        (n_dp, cut, 128),
        (n_dp, qc - cut, 128),
        (n_dp, pe, 256),
        (n_dp, pe, 128),
        (BOTTLE // 2, CHANNELS),
    ]
    final = [(2, 2, BOTTLE // 4, lanes1), (2, qc, BOTTLE), (pe, CHANNELS), (pe, 512)]
    sent = [BF16, BF16, BF16, BF16, F32, BF16]
    scratch += [vmem(shape, F32) for shape in half[:-1]] + [vmem(half[-1], BF16)]
    scratch += [vmem(shape, kind) for shape, kind in zip(quarter, sent)] * 3
    owned = [(BOTTLE // 4, lanes1)] + [shape[1:] for shape in quarter[1:-1]]
    owned += [(BOTTLE // 2, lanes1)]
    scratch += [vmem((n_dp,) + shape, kind) for shape, kind in zip(owned, sent)]
    scratch += [vmem(shape, F32) for shape in owned]
    scratch += [vmem(shape, F32) for shape in final]
    dma = pltpu.SemaphoreType.DMA
    scratch += [dma((15,))] + [dma((len(STATS),))] * 4 + [dma((2,))] + [dma((4, 4))] * 2 + [dma((6, 4))] * 2
    any_space = pl.BlockSpec(memory_space=pl.ANY)
    block_out, images_grad, sum1, sumc, sum3, sume, norm_grads = pl.pallas_call(
        functools.partial(block_kernel, n_dp, n_rep),
        out_shape=[
            jax.ShapeDtypeStruct(pixel_form, BF16),
            jax.ShapeDtypeStruct(pixel_form, F32),
            *[jax.ShapeDtypeStruct(shape, F32) for shape in final],
            jax.ShapeDtypeStruct((8, 128), F32),
        ],
        in_specs=[any_space] * 8,
        out_specs=[any_space] * 7,
        scratch_shapes=scratch,
        compiler_params=pltpu.CompilerParams(
            collective_id=0, has_side_effects=True, vmem_limit_bytes=63 * 1024 * 1024
        ),
    )(
        by_pixel(images),
        by_pixel(out_grad),
        reduce_weight,
        conv_weight,
        squeeze_weight,
        expand_weight,
        project_weight,
        norm_params,
    )
    states = (
        reduce_weight,
        reduce_moment,
        reduce_second,
        conv_weight,
        conv_moment,
        conv_second,
        squeeze_weight,
        squeeze_moment,
        squeeze_second,
        expand_weight,
        expand_moment,
        expand_second,
        project_weight,
        project_moment,
        project_second,
    )
    held = (*states, norm_params, norm_moment, norm_second)
    sums = (
        sum1.reshape(BOTTLE, lanes1),
        sumc.reshape(conv_weight.shape),
        sum3,
        sume,
        norm_grads,
    )
    block_out, images_grad, *updated = pl.pallas_call(
        update_kernel,
        out_shape=[
            jax.ShapeDtypeStruct(pixel_form, BF16),
            jax.ShapeDtypeStruct(pixel_form, F32),
            *[jax.ShapeDtypeStruct(state.shape, F32) for state in held],
        ],
        in_specs=[any_space] * 25,
        out_specs=[any_space] * 20,
        scratch_shapes=[vmem(values.shape, F32) for values in (*sums, *held, *held)]
        + [vmem(pixel_form, BF16), vmem(pixel_form, F32)]
        + [dma((2, 3)), dma((23,)), dma((18,))],
        compiler_params=pltpu.CompilerParams(vmem_limit_bytes=63 * 1024 * 1024),
    )(block_out, images_grad, *sums, *held)
    by_image = lambda values: jnp.transpose(
        values.reshape(SIDE, SIDE, images.shape[0], CHANNELS), (2, 0, 1, 3)
    )
    return (
        by_image(block_out),
        by_image(images_grad),
        *updated,
    )


def solution(mesh):
    placed = (
        P(("dp", "rep"), None, None, None),
        P(("dp", "rep"), None, None, None),
        P("dp", None),
        P("dp", None),
        P("dp", None),
        P("dp", None),
        P("dp", None),
        P("dp", None),
        P("dp", None),
        P("dp", None),
        P("dp", None),
        P("dp", None),
        P("dp", None),
        P("dp", None),
        P("dp", None),
        P("dp", None),
        P("dp", None),
        P("dp"),
        P("dp"),
        P("dp"),
    )
    n_dp, n_rep = mesh.shape["dp"], mesh.shape["rep"]
    whole_tiles = n_rep == 4 and n_dp % 2 == 0 and INNER % (16 * n_dp) == 0
    return jax.shard_map(
        fused_device if whole_tiles else per_device,
        mesh=mesh,
        in_specs=placed,
        out_specs=(
            P(("dp", "rep"), None, None, None),
            P(("dp", "rep"), None, None, None),
            P("dp", None),
            P("dp", None),
            P("dp", None),
            P("dp", None),
            P("dp", None),
            P("dp", None),
            P("dp", None),
            P("dp", None),
            P("dp", None),
            P("dp", None),
            P("dp", None),
            P("dp", None),
            P("dp", None),
            P("dp", None),
            P("dp", None),
            P("dp"),
            P("dp"),
            P("dp"),
        ),
        check_vma=False,
    )
```

```python
import functools
import jax
import jax.numpy as jnp
from jax import lax
from jax.experimental import pallas as pl
from jax.experimental.pallas import tpu as pltpu
from jax.sharding import PartitionSpec as P

CHANNELS = 1024
BOTTLE = 256
INNER = 128
RADIX = 2
SIDE = 14
MICRO = 2
STEP = 10


EPSILON = 1e-05
PRECISE = lax.Precision.HIGHEST
BETA_ONE = 0.9
BETA_TWO = 0.999
ADAM_EPSILON = 1e-08
DECAY = 0.01
NORM_RATE = 0.8
ROWS = 4 * SIDE * SIDE
NORM_WIDTH = 4352


def split_params(packed):
    widths = (
        BOTTLE,
        BOTTLE,
        RADIX * BOTTLE,
        RADIX * BOTTLE,
        INNER,
        INNER,
        RADIX * BOTTLE,
        CHANNELS,
        CHANNELS,
    )
    pieces = []
    offset = 0
    for segment in widths:
        pieces.append(lax.slice_in_dim(packed, offset, offset + segment))
        offset = offset + segment
    return pieces


def silu_slope(values):
    logistic = jax.nn.sigmoid(values)
    return logistic * (1.0 + values * (1.0 - logistic))


def norm_forward(values, gain, bias, count):
    flat = values.reshape(-1, values.shape[-1])
    total, square = lax.psum((jnp.sum(flat, axis=0), jnp.sum(flat * flat, axis=0)), ("dp", "rep"))
    center = total / count
    scale = lax.rsqrt(square / count - center * center + EPSILON)
    normed = (values - center) * scale
    return (normed * gain + bias, normed, scale)


def norm_backward(upstream, normed, scale, gain, count):
    flat_up = upstream.reshape(-1, upstream.shape[-1])
    flat_norm = normed.reshape(-1, normed.shape[-1])
    bias_sum, gain_sum = lax.psum(
        (jnp.sum(flat_up, axis=0), jnp.sum(flat_up * flat_norm, axis=0)), ("dp", "rep")
    )
    downstream = gain * scale * (upstream - bias_sum / count - normed * (gain_sum / count))
    return (downstream, gain_sum, bias_sum)


def patches(active):
    padded = jnp.pad(active, ((0, 0), (1, 1), (1, 1), (0, 0), (0, 0)))
    shifted = [
        padded[:, down_step : down_step + SIDE, side_step : side_step + SIDE]
        for down_step in range(3)
        for side_step in range(3)
    ]
    return jnp.stack(shifted, axis=4)


def unpatch(columns):
    total = jnp.zeros(
        (columns.shape[0], SIDE + 2, SIDE + 2, columns.shape[3], columns.shape[5]), jnp.float32
    )
    for down_step in range(3):
        for side_step in range(3):
            piece = columns[:, :, :, :, 3 * down_step + side_step]
            total = total + jnp.pad(
                piece,
                ((0, 0), (down_step, 2 - down_step), (side_step, 2 - side_step), (0, 0), (0, 0)),
            )
    return total[:, 1 : SIDE + 1, 1 : SIDE + 1]


def adamw(param, moment, second, gradient, rate, decay):
    moment_new = BETA_ONE * moment + (1.0 - BETA_ONE) * gradient
    second_new = BETA_TWO * second + (1.0 - BETA_TWO) * gradient * gradient
    ratio = (
        moment_new
        / (1.0 - BETA_ONE**STEP)
        / (jnp.sqrt(second_new / (1.0 - BETA_TWO**STEP)) + ADAM_EPSILON)
    )
    return (param - rate * (ratio + decay * param), moment_new, second_new)


def per_device(
    images,
    out_grad,
    reduce_weight,
    reduce_moment,
    reduce_second,
    conv_weight,
    conv_moment,
    conv_second,
    squeeze_weight,
    squeeze_moment,
    squeeze_second,
    expand_weight,
    expand_moment,
    expand_second,
    project_weight,
    project_moment,
    project_second,
    norm_params,
    norm_moment,
    norm_second,
):
    bf16 = jnp.bfloat16
    low_reduce = reduce_weight.astype(bf16)
    low_conv = conv_weight.astype(bf16)
    low_squeeze = squeeze_weight.astype(bf16)
    low_expand = expand_weight.astype(bf16)
    low_project = project_weight.astype(bf16)
    low_norm = norm_params.astype(bf16)
    devices = lax.axis_size("dp") * lax.axis_size("rep")
    per_batch = images.shape[0] // MICRO
    pixel_count = float(per_batch * SIDE * SIDE * devices)
    image_count = float(per_batch * devices)
    group_in = BOTTLE // RADIX
    grad_first = jnp.zeros((CHANNELS, BOTTLE), jnp.float32)
    grad_conv = jnp.zeros((RADIX, 9 * group_in, BOTTLE), jnp.float32)
    grad_squeeze = jnp.zeros((BOTTLE, INNER), jnp.float32)
    grad_expand = jnp.zeros((INNER, RADIX * BOTTLE), jnp.float32)
    grad_last = jnp.zeros((BOTTLE, CHANNELS), jnp.float32)
    grad_norms = jnp.zeros(
        (2 * BOTTLE + 3 * RADIX * BOTTLE + 2 * INNER + 2 * CHANNELS,), jnp.float32
    )
    outputs = []
    input_grads = []
    for number in range(MICRO):
        forward_set = (
            lax.all_gather(low_reduce, "dp", axis=0, tiled=True),
            lax.all_gather(low_conv, "dp", axis=0, tiled=True),
            lax.all_gather(low_squeeze, "dp", axis=0, tiled=True),
            lax.all_gather(low_expand, "dp", axis=0, tiled=True),
            lax.all_gather(low_project, "dp", axis=0, tiled=True),
            lax.all_gather(low_norm, "dp", axis=0, tiled=True),
        )
        first, conv, squeeze, expand, last, packed = forward_set
        (
            gain_one,
            bias_one,
            gain_two,
            bias_two,
            gain_pool,
            bias_pool,
            bias_expand,
            gain_three,
            bias_three,
        ) = split_params(packed.astype(jnp.float32))
        batched = images[number * per_batch : (number + 1) * per_batch]
        cotangent = out_grad[number * per_batch : (number + 1) * per_batch]
        reduced = jnp.einsum("nhwc,cb->nhwb", batched, first, preferred_element_type=jnp.float32)
        norm_one, normed_one, scale_one = norm_forward(reduced, gain_one, bias_one, pixel_count)
        active = jax.nn.silu(norm_one).astype(bf16)
        columns = patches(active.reshape(per_batch, SIDE, SIDE, RADIX, group_in)).reshape(
            per_batch * SIDE * SIDE, RADIX, 9 * group_in
        )
        conv_grouped = conv.reshape(RADIX, 9 * group_in, BOTTLE)
        widened = jnp.einsum(
            "prk,rko->pro", columns, conv_grouped, preferred_element_type=jnp.float32
        )
        widened = widened.reshape(per_batch, SIDE, SIDE, RADIX * BOTTLE)
        norm_two, normed_two, scale_two = norm_forward(widened, gain_two, bias_two, pixel_count)
        splits = jax.nn.silu(norm_two).reshape(per_batch, SIDE, SIDE, RADIX, BOTTLE)
        pooled = jnp.sum(jnp.sum(splits, axis=3), axis=(1, 2)) / (SIDE * SIDE)
        squeeze_float = squeeze.astype(jnp.float32)
        expand_float = expand.astype(jnp.float32)
        pre_pool = jnp.dot(pooled, squeeze_float, precision=PRECISE)
        norm_pool, normed_pool, scale_pool = norm_forward(
            pre_pool, gain_pool, bias_pool, image_count
        )
        hidden = jax.nn.silu(norm_pool)
        logits = (jnp.dot(hidden, expand_float, precision=PRECISE) + bias_expand).reshape(
            per_batch, RADIX, BOTTLE
        )
        attention = jax.nn.softmax(logits, axis=1)
        mixed = jnp.sum(splits * attention[:, None, None], axis=3).astype(bf16)
        projected = jnp.einsum("nhwb,bc->nhwc", mixed, last, preferred_element_type=jnp.float32)
        norm_three, normed_three, scale_three = norm_forward(
            projected, gain_three, bias_three, pixel_count
        )
        summed = batched.astype(jnp.float32) + norm_three
        outputs.append(jax.nn.silu(summed).astype(bf16))
        backward_set = (
            lax.all_gather(low_reduce, "dp", axis=0, tiled=True),
            lax.all_gather(low_conv, "dp", axis=0, tiled=True),
            lax.all_gather(low_squeeze, "dp", axis=0, tiled=True),
            lax.all_gather(low_expand, "dp", axis=0, tiled=True),
            lax.all_gather(low_project, "dp", axis=0, tiled=True),
            lax.all_gather(low_norm, "dp", axis=0, tiled=True),
        )
        first, conv, squeeze, expand, last, packed = backward_set
        gains_back = split_params(packed.astype(jnp.float32))
        conv_grouped = conv.reshape(RADIX, 9 * group_in, BOTTLE)
        expand_float = expand.astype(jnp.float32)
        squeeze_float = squeeze.astype(jnp.float32)
        upstream = cotangent.astype(jnp.float32) * silu_slope(summed)
        d_projected, gain_three_grad, bias_three_grad = norm_backward(
            upstream, normed_three, scale_three, gains_back[7], pixel_count
        )
        d_projected_low = d_projected.astype(bf16)
        grad_last = grad_last + jnp.einsum(
            "nhwb,nhwc->bc", mixed, d_projected_low, preferred_element_type=jnp.float32
        )
        d_mixed = jnp.einsum(
            "nhwc,bc->nhwb", d_projected_low, last, preferred_element_type=jnp.float32
        )
        d_splits = d_mixed[:, :, :, None] * attention[:, None, None]
        d_attention = jnp.sum(d_mixed[:, :, :, None] * splits, axis=(1, 2))
        d_logits = attention * (
            d_attention - jnp.sum(attention * d_attention, axis=1, keepdims=True)
        )
        flat_logits = d_logits.reshape(per_batch, RADIX * BOTTLE)
        grad_expand = grad_expand + jnp.dot(hidden.T, flat_logits, precision=PRECISE)
        d_hidden = jnp.dot(flat_logits, expand_float.T, precision=PRECISE)
        d_pool_norm = d_hidden * silu_slope(norm_pool)
        pool_bias_sum, pool_gain_sum, expand_bias_sum = lax.psum(
            (
                jnp.sum(d_pool_norm, axis=0),
                jnp.sum(d_pool_norm * normed_pool, axis=0),
                jnp.sum(flat_logits, axis=0),
            ),
            ("dp", "rep"),
        )
        d_pre_pool = (
            gains_back[4]
            * scale_pool
            * (
                d_pool_norm
                - pool_bias_sum / image_count
                - normed_pool * (pool_gain_sum / image_count)
            )
        )
        grad_squeeze = grad_squeeze + jnp.dot(pooled.T, d_pre_pool, precision=PRECISE)
        d_pooled = jnp.dot(d_pre_pool, squeeze_float.T, precision=PRECISE)
        d_splits = d_splits + (d_pooled / (SIDE * SIDE))[:, None, None, None, :]
        d_norm_two = d_splits.reshape(per_batch, SIDE, SIDE, RADIX * BOTTLE) * silu_slope(norm_two)
        d_widened, gain_two_grad, bias_two_grad = norm_backward(
            d_norm_two, normed_two, scale_two, gains_back[2], pixel_count
        )
        d_widened_low = d_widened.astype(bf16).reshape(per_batch * SIDE * SIDE, RADIX, BOTTLE)
        grad_conv = grad_conv + jnp.einsum(
            "prk,pro->rko", columns, d_widened_low, preferred_element_type=jnp.float32
        )
        d_columns = jnp.einsum(
            "pro,rko->prk", d_widened_low, conv_grouped, preferred_element_type=jnp.float32
        )
        d_active = unpatch(d_columns.reshape(per_batch, SIDE, SIDE, RADIX, 9, group_in)).reshape(
            per_batch, SIDE, SIDE, BOTTLE
        )
        d_norm_one = d_active * silu_slope(norm_one)
        d_reduced, gain_one_grad, bias_one_grad = norm_backward(
            d_norm_one, normed_one, scale_one, gains_back[0], pixel_count
        )
        d_reduced_low = d_reduced.astype(bf16)
        grad_first = grad_first + jnp.einsum(
            "nhwc,nhwb->cb", batched, d_reduced_low, preferred_element_type=jnp.float32
        )
        input_grads.append(
            upstream
            + jnp.einsum("nhwb,cb->nhwc", d_reduced_low, first, preferred_element_type=jnp.float32)
        )
        grad_norms = grad_norms + jnp.concatenate(
            [
                gain_one_grad,
                bias_one_grad,
                gain_two_grad,
                bias_two_grad,
                pool_gain_sum,
                pool_bias_sum,
                expand_bias_sum,
                gain_three_grad,
                bias_three_grad,
            ]
        )
    grad_conv = grad_conv.reshape(9 * BOTTLE, BOTTLE)
    partial_value = (
        lax.psum_scatter(grad_first, "dp", scatter_dimension=0, tiled=True),
        lax.psum_scatter(grad_conv, "dp", scatter_dimension=0, tiled=True),
        lax.psum_scatter(grad_squeeze, "dp", scatter_dimension=0, tiled=True),
        lax.psum_scatter(grad_expand, "dp", scatter_dimension=0, tiled=True),
        lax.psum_scatter(grad_last, "dp", scatter_dimension=0, tiled=True),
    )
    owned = lax.psum(
        (partial_value[0], partial_value[1], partial_value[2], partial_value[3], partial_value[4]),
        "rep",
    )
    shard_length = norm_params.shape[0]
    norm_grad_owned = lax.dynamic_slice_in_dim(
        grad_norms, lax.axis_index("dp") * shard_length, shard_length
    )
    reduce_new = adamw(
        reduce_weight, reduce_moment, reduce_second, owned[0], 2.0 * CHANNELS ** (-0.5), DECAY
    )
    conv_new = adamw(
        conv_weight,
        conv_moment,
        conv_second,
        owned[1],
        2.0 * (9 * BOTTLE // RADIX) ** (-0.5),
        DECAY,
    )
    squeeze_new = adamw(
        squeeze_weight, squeeze_moment, squeeze_second, owned[2], 2.0 * BOTTLE ** (-0.5), DECAY
    )
    expand_new = adamw(
        expand_weight, expand_moment, expand_second, owned[3], 2.0 * (INNER // 8) ** (-0.5), DECAY
    )
    project_new = adamw(
        project_weight, project_moment, project_second, owned[4], 2.0 * BOTTLE ** (-0.5), DECAY
    )
    norm_new = adamw(norm_params, norm_moment, norm_second, norm_grad_owned, NORM_RATE, 0.0)
    return (
        jnp.concatenate(outputs, axis=0),
        jnp.concatenate(input_grads, axis=0),
        reduce_new[0],
        reduce_new[1],
        reduce_new[2],
        conv_new[0],
        conv_new[1],
        conv_new[2],
        squeeze_new[0],
        squeeze_new[1],
        squeeze_new[2],
        expand_new[0],
        expand_new[1],
        expand_new[2],
        project_new[0],
        project_new[1],
        project_new[2],
        norm_new[0],
        norm_new[1],
        norm_new[2],
    )


MESH = pl.DeviceIdType.MESH
PAD = 64
CHUNK = 112
F32 = jnp.float32
BF16 = jnp.bfloat16
STATS = {
    "reduced": (8, 128),
    "widened0": (8, 128),
    "widened1": (8, 128),
    "pool": (8, 128),
    "images": (16, 128),
    "projected0": (8, 256),
    "projected1": (8, 256),
    "back_projected0": (8, 256),
    "back_projected1": (8, 256),
    "back_pool": (8, 128),
    "back_widened0": (8, 128),
    "back_widened1": (16, 128),
    "back_reduced0": (8, 128),
    "back_reduced1": (8, 128),
}
DIRECT = ("reduced", "pool", "back_pool")


def sigmoid(values):
    return 0.5 * jnp.tanh(0.5 * values) + 0.5


def row_ids(width):
    return lax.broadcasted_iota(jnp.int32, (8, width), 0)


def image_sum(rows):
    return rows + pltpu.roll(rows, 4, 0)


def pair_sum(rows):
    even = row_ids(rows.shape[1]) % 2 == 0
    return rows + jnp.where(even, pltpu.roll(rows, 7, 0), pltpu.roll(rows, 1, 0))


def micro_sum(rows):
    return pair_sum(image_sum(rows))


def stack_sums(first, second):
    return jnp.where(row_ids(first.shape[1]) < 4, first, second)


def unstack_sums(stacked):
    upper = row_ids(stacked.shape[1]) < 4
    turned = pltpu.roll(stacked, 4, 0)
    return jnp.where(upper, stacked, turned), jnp.where(upper, turned, stacked)


def fold_lanes(stacked):
    half = stacked.shape[1] // 2
    even = row_ids(half) % 2 == 0
    return jnp.where(even, stacked[:, :half], stacked[:, half:])


def unfold_lanes(folded):
    even = row_ids(folded.shape[1]) % 2 == 0
    left = jnp.where(even, folded, pltpu.roll(folded, 1, 0))
    right = jnp.where(even, pltpu.roll(folded, 7, 0), folded)
    return jnp.concatenate([left, right], axis=1)


def norm_terms(total, square, gain, bias, count):
    center = total * (1.0 / count)
    scale = lax.rsqrt(square * (1.0 / count) - center * center + EPSILON)
    slope = scale * gain
    return center, scale, slope, bias - center * slope


def back_terms(center, scale, slope, bias_sum, gain_sum, count):
    by_value = -slope * scale * (gain_sum * (1.0 / count))
    constant = -slope * (bias_sum * (1.0 / count)) - by_value * center
    return by_value, constant


def tdot(left, right):
    return lax.dot_general(left, right, (((0,), (0,)), ((), ())), preferred_element_type=F32)


def dot_t(left, right):
    return lax.dot_general(left, right, (((1,), (1,)), ((), ())), preferred_element_type=F32)


def in_parts(values, parts):
    found = []
    for _ in range(parts):
        rounded = values.astype(BF16).astype(F32)
        found.append(rounded)
        values = values - rounded
    return found


def exact_dot(left, right, transposed):
    stacked = jnp.concatenate(in_parts(left, 3), axis=0).astype(BF16)
    wide = dot_t(stacked, right) if transposed else jnp.dot(stacked, right, preferred_element_type=F32)
    return wide[0:8] + wide[8:16] + wide[16:24]


def row_dot(left, right):
    high, low = in_parts(left, 2)
    other_high, other_low = in_parts(right, 2)
    return tdot(
        jnp.concatenate([high, high, low, low], axis=0).astype(BF16),
        jnp.concatenate([other_high, other_low, other_high, other_low], axis=0).astype(BF16),
    )


def image_dot(left, right):
    return row_dot(jnp.where(row_ids(left.shape[1]) < 4, left, 0.0), right)


def block_kernel(
    n_dp,
    n_rep,
    x_hbm,
    gy_hbm,
    w1_hbm,
    wc_hbm,
    sq_hbm,
    ex_hbm,
    w3_hbm,
    np_hbm,
    bo_hbm,
    dx_hbm,
    f1_hbm,
    fc_hbm,
    f3_hbm,
    fe_hbm,
    gn_hbm,
    w1_own,
    wc_own,
    sq_own,
    ex_own,
    w3_own,
    np_own,
    gn_out,
    x4,
    gy4,
    x_v,
    gy_v,
    fw1,
    fwc,
    fes,
    fw3,
    es_own,
    np_slots,
    np_full,
    red,
    act,
    columns,
    wid,
    splits,
    mixed,
    proj,
    up,
    bo4,
    dx4,
    dproj,
    d_mixed,
    dn2,
    dwid,
    dcol,
    dn1,
    dred,
    g1,
    gc,
    g3,
    ge,
    gb,
    fix,
    back_own,
    *rest,
):
    n_ar = len(STATS)
    order = {name: k for k, name in enumerate(STATS)}
    ar_slots_a = dict(zip(STATS, rest[0:n_ar]))
    ar_slots_b = dict(zip(STATS, rest[n_ar : 2 * n_ar]))
    rest = rest[2 * n_ar :]
    r1s, ys, r2s, ks, r3s, own = (rest[6 * i : 6 * i + 6] for i in range(6))
    fs = rest[36:40]
    rest = rest[40:]
    local_sem, ar_send_a, ar_recv_a, ar_send_b, ar_recv_b, np_sems, ws, wr, gs, gr = rest

    dp = lax.axis_index("dp")
    rep = lax.axis_index("rep")
    core = lax.rem(rep, 2)
    half_y = lax.div(rep, 2)
    planes = n_dp // 2
    plane_size = 2 * n_rep
    plane = lax.div(dp, 2)
    in_plane = lax.rem(dp, 2) * n_rep + rep
    sibling = (dp, half_y * 2 + (1 - core))
    across = (dp, (1 - half_y) * 2 + core)
    pixels = float(SIDE * SIDE * 2 * n_dp * n_rep)
    pictures = float(2 * n_dp * n_rep)

    x = lax.rem(dp, 2)
    if planes == 4:
        upper = lax.div(plane, 2)
        other_planes = [3 - 3 * upper, 2 - upper, 1 - plane + 4 * upper]
    else:
        other_planes = [lax.rem(plane + step, planes) for step in range(1, planes)]
    flips = ((1, 1, 1), (1, 1, 0), (1, 0, 1), (1, 0, 0), (0, 1, 1), (0, 1, 0), (0, 0, 1), (0, 0, 0))

    def of_flip(z, flip):
        there = [1 - own if turn else own for own, turn in zip((x, half_y, core), flip)]
        return (z * 2 + there[0], there[1] * 2 + there[2])

    plane_peers = [of_flip(plane, flip) for flip in flips[:-1]]
    column_peers = [of_flip(z, flips[-1]) for z in other_planes]
    owner_peers = [of_flip(z, flip) for z in other_planes for flip in (flips[3], flips[7])]
    owner_peers += [of_flip(plane, flips[3])]
    all_peers = [of_flip(z, flip) for z in other_planes for flip in flips] + plane_peers
    me, everyone = dp * n_rep + rep, n_dp * n_rep
    rep_peers = [(dp, lax.rem(rep + step, n_rep)) for step in range(1, n_rep)]

    def remote(src, dst, send_sem, recv_sem, device):
        return pltpu.make_async_remote_copy(
            src_ref=src,
            dst_ref=dst,
            send_sem=send_sem,
            recv_sem=recv_sem,
            device_id=device,
            device_id_type=MESH,
        )

    def send_all(ref, send_sem, recv_sem, peers):
        for device in peers:
            remote(ref, ref, send_sem, recv_sem, device).start()

    def wait_bytes(ref, sem):
        pltpu.make_async_copy(ref, ref, sem).wait()

    def over_rows(body, init):
        def step(index, carry):
            return body(pl.multiple_of(index * CHUNK, CHUNK), carry)

        return lax.fori_loop(0, ROWS // CHUNK, step, init)

    def grouped(values):
        return values.reshape(CHUNK // 8, 8, values.shape[-1])

    def by_four(values):
        return flat(values).reshape(CHUNK // 4, 4, values.shape[-1])

    def flat(values):
        return values.reshape(CHUNK, values.shape[-1])

    own_copies = [
        pltpu.make_async_copy(source, target, local_sem.at[4 + k])
        for k, (source, target) in enumerate(
            (
                (w1_hbm, w1_own),
                (np_hbm, np_own),
                (wc_hbm, wc_own),
                (w3_hbm, w3_own),
                (sq_hbm, sq_own),
                (ex_hbm, ex_own),
            )
        )
    ]
    for copy in own_copies:
        copy.start()
    x_copy = pltpu.make_async_copy(x_hbm, x4, local_sem.at[0])
    gy_copy = pltpu.make_async_copy(gy_hbm, gy4, local_sem.at[1])
    x_copy.start()
    barrier = pltpu.get_barrier_semaphore()
    for device in all_peers:
        pl.semaphore_signal(barrier, inc=1, device_id=device, device_id_type=MESH)

    part = core * 2 + half_y
    own_copies[0].wait()
    q1 = w1_own.shape[0] // 4
    fw1[dp, core, half_y] = w1_own[pl.ds(pl.multiple_of(part * q1, q1), q1), :].astype(BF16)
    core_lanes = pl.ds(pl.multiple_of(core * 128, 128), 128)
    es_lanes = pl.ds(pl.multiple_of(part * 128, 128), 128)
    w3_lanes = pl.ds(pl.multiple_of(part * 256, 128), 256)

    pl.semaphore_wait(barrier, everyone - 1)

    def quarter_w1(c, y):
        return fw1.at[:, c, y]

    def quarter_wc(c, y):
        return fwc.at[:, y, :, pl.ds(pl.multiple_of(c * 128, 128), 128)]

    def quarter_es(c, y):
        return fes.at[:, :, pl.ds(pl.multiple_of((c * 2 + y) * 128, 128), 128)]

    def quarter_w3(c, y):
        return fw3.at[:, :, pl.ds(pl.multiple_of((c * 2 + y) * 256, 128), 256)]

    quarters = (quarter_w1, quarter_wc, quarter_es, quarter_w3)

    def piece(which, d):
        return (
            fw1.at[d, core, half_y],
            fwc.at[d, half_y, :, core_lanes],
            fes.at[d, :, es_lanes],
            fw3.at[d, :, w3_lanes],
        )[which]

    def seven(which):
        return (
            fw1.at[pl.ds(0, n_dp - 1), core, half_y],
            fwc.at[pl.ds(0, n_dp - 1), half_y, :, core_lanes],
            fes.at[pl.ds(0, n_dp - 1), :, es_lanes],
            fw3.at[pl.ds(0, n_dp - 1), :, w3_lanes],
        )[which]

    def gather_out(which):
        send_all(piece(which, dp), ws.at[which, 0], wr.at[which, 0], owner_peers)

    def gather_turn(which):
        wait_bytes(seven(which), wr.at[which, 0])
        mine = quarters[which](core, half_y)
        remote(mine, mine, ws.at[which, 1], wr.at[which, 1], across).start()
        remote(mine, mine, ws.at[which, 2], wr.at[which, 2], sibling).start()

    def gather_hand(which):
        theirs = quarters[which](core, 1 - half_y)
        wait_bytes(theirs, wr.at[which, 1])
        remote(theirs, theirs, ws.at[which, 3], wr.at[which, 3], sibling).start()

    def gather_end(which):
        wait_bytes(quarters[which](1 - core, half_y), wr.at[which, 2])
        wait_bytes(quarters[which](1 - core, 1 - half_y), wr.at[which, 3])

    def to_rows(source, target):
        def body(index, carry):
            values = source[pl.ds(index * (CHUNK // 4), CHUNK // 4)].astype(F32)
            row = pl.multiple_of(index * CHUNK, CHUNK)
            target[pl.ds(row, CHUNK), :] = values.reshape(CHUNK, CHANNELS).astype(BF16)
            return carry

        lax.fori_loop(0, ROWS // CHUNK, body, 0)

    gather_out(0)
    own_copies[2].wait()
    qc = wc_own.shape[0] // 2
    fwc[dp, half_y, :, core_lanes] = wc_own[
        pl.ds(pl.multiple_of(half_y * qc, qc), qc), core_lanes
    ].astype(BF16)
    gather_out(1)

    own_copies[1].wait()
    shard = np_own.shape[0]
    lanes_id = lax.broadcasted_iota(jnp.int32, (8, 128), 1)
    turn = lax.rem(shard * dp, 128)
    np_rows = []
    for at in range(0, shard, 128):
        width = min(128, shard - at)
        piece_row = np_own[pl.ds(at, width)].reshape(1, width)
        if width < 128:
            piece_row = jnp.concatenate([piece_row, jnp.zeros((1, 128 - width), F32)], axis=1)
        np_rows.append(piece_row)
    np_rows.append(jnp.zeros((8 - len(np_rows), 128), F32))
    np_turned = jnp.concatenate(np_rows, axis=0).astype(BF16).astype(F32)
    np_turned = pltpu.roll(np_turned, turn, 1)
    np_slots[dp] = jnp.where(lanes_id < turn, pltpu.roll(np_turned, 1, 0), np_turned)
    send_all(np_slots.at[dp], np_sems.at[0], np_sems.at[1], owner_peers)
    for copy in own_copies[3:]:
        copy.wait()
    ex_rows = ex_own.shape[0]
    es_own[:, 0:128] = sq_own[...].astype(BF16)
    es_own[0:ex_rows, 128:384] = ex_own[:, 0:256].astype(BF16)
    es_own[ex_rows : 2 * ex_rows, 128:384] = ex_own[:, 256:512].astype(BF16)
    es_own[:, 384:512] = jnp.zeros((2 * ex_rows, 128), BF16)
    fes[dp, :, es_lanes] = es_own[:, es_lanes]
    fw3[dp, :, w3_lanes] = w3_own[:, w3_lanes].astype(BF16)
    gy_copy.start()
    x_copy.wait()
    to_rows(x4, x_v)
    gather_turn(0)
    zero_rows = jnp.zeros((PAD, BOTTLE), F32)
    for side in range(3):
        act[side, 0:PAD, :] = zero_rows
        act[side, PAD + ROWS : 2 * PAD + ROWS, :] = zero_rows
    for lane_block in range(9):
        dcol[0:PAD, lane_block * 256 : lane_block * 256 + 256] = zero_rows
        dcol[PAD + ROWS : 2 * PAD + ROWS, lane_block * 256 : lane_block * 256 + 256] = zero_rows
    gather_hand(0)
    gather_turn(1)

    def sum_start(k, payload):
        if k in DIRECT:
            ar_slots_a[k][me] = payload
            send_all(ar_slots_a[k].at[me], ar_send_a.at[order[k]], ar_recv_a.at[order[k]], all_peers)
        else:
            ar_slots_a[k][in_plane] = payload
            send_all(ar_slots_a[k].at[in_plane], ar_send_a.at[order[k]], ar_recv_a.at[order[k]], plane_peers)

    def sum_slots(slots, count):
        sums = [slots[slot] for slot in range(count)]
        while len(sums) > 1:
            sums = [sums[i] + sums[i + 1] for i in range(0, len(sums), 2)]
        return sums[0]

    def sum_turn(k):
        if k in DIRECT:
            return
        wait_bytes(ar_slots_a[k].at[pl.ds(0, plane_size - 1)], ar_recv_a.at[order[k]])
        ar_slots_b[k][plane] = sum_slots(ar_slots_a[k], plane_size)
        send_all(ar_slots_b[k].at[plane], ar_send_b.at[order[k]], ar_recv_b.at[order[k]], column_peers)

    def sum_end(k):
        if k in DIRECT:
            wait_bytes(ar_slots_a[k].at[pl.ds(0, everyone - 1)], ar_recv_a.at[order[k]])
            return sum_slots(ar_slots_a[k], everyone)
        wait_bytes(ar_slots_b[k].at[pl.ds(0, planes - 1)], ar_recv_b.at[order[k]])
        return sum_slots(ar_slots_b[k], planes)

    def lanes_of(index, width):
        return pl.ds(pl.multiple_of(index * width, 128), width)

    cut = 64
    conv_rows = {1: pl.ds(0, cut), 2: pl.ds(cut, gc.shape[2] - cut)}
    grads = (g1, gc, gc, g3, ge, gb)
    turned_kinds = (0, 5)

    def half_of(which, c):
        ref = grads[which]
        if which in turned_kinds:
            return ref.at[c]
        if which in conv_rows:
            return ref.at[:, :, conv_rows[which], lanes_of(c, 128)]
        return ref.at[:, :, lanes_of(c, (512, 256)[which - 3])]

    def y_part(which, ref, y):
        if which in turned_kinds:
            return ref.at[y]
        if which < 3:
            return ref.at[:, y]
        return ref.at[:, :, lanes_of(y, (256, 128)[which - 3])]

    def quarter_of(which, c, y):
        ref = grads[which]
        if which in turned_kinds:
            return ref.at[c, y]
        if which in conv_rows:
            return ref.at[:, y, conv_rows[which], lanes_of(c, 128)]
        return ref.at[:, :, lanes_of(c * 2 + y, (256, 128)[which - 3])]

    def final_part(which, c, y):
        if which == 0:
            return fs[0].at[c, y]
        if which in conv_rows:
            return fs[1].at[y, conv_rows[which], lanes_of(c, 128)]
        return fs[which - 1].at[:, lanes_of(c * 2 + y, (256, 128)[which - 3])]

    def of_owner(which, ref, d):
        return ref.at[:, lanes_of(d, CHANNELS // n_dp)] if which in turned_kinds else ref.at[d]

    def in_blocks(which, body):
        if which in turned_kinds:
            count = 4
            rows = grads[which].shape[2] // count
            block = lambda index: pl.ds(pl.multiple_of(index * rows, rows), rows)
        else:
            count, block = n_dp, lambda index: index

        def step(index, carry):
            body(block(index))
            return carry

        lax.fori_loop(0, count, step, 0)

    def reduce_core(which):
        remote(
            half_of(which, 1 - core), r1s[which], gs.at[which, 0], gr.at[which, 0], sibling
        ).start()

    def reduce_y(which):
        wait_bytes(r1s[which], gr.at[which, 0])
        away = quarter_of(which, core, 1 - half_y)
        mine = quarter_of(which, core, half_y)
        there = y_part(which, r1s[which], 1 - half_y)
        here = y_part(which, r1s[which], half_y)

        def add_away(at):
            ys[which][at] = (away[at].astype(F32) + there[at].astype(F32)).astype(
                ys[which].dtype
            )

        in_blocks(which, add_away)
        remote(ys[which], r2s[which], gs.at[which, 1], gr.at[which, 1], across).start()

        def add_mine(at):
            mine[at] = (mine[at].astype(F32) + here[at].astype(F32)).astype(mine.dtype)

        in_blocks(which, add_mine)

    def reduce_owner(which):
        wait_bytes(r2s[which], gr.at[which, 1])
        mine = quarter_of(which, core, half_y)

        def add(at):
            ks[which][at] = (mine[at].astype(F32) + r2s[which][at].astype(F32)).astype(
                ks[which].dtype
            )

        in_blocks(which, add)
        for device in owner_peers:
            remote(
                of_owner(which, ks[which], device[0]),
                r3s[which].at[dp],
                gs.at[which, 2],
                gr.at[which, 2],
                device,
            ).start()
        own[which][...] = of_owner(which, mine, dp)[...].astype(F32) + of_owner(
            which, r2s[which], dp
        )[...].astype(F32)
        r3s[which][dp] = jnp.zeros(own[which].shape, r3s[which].dtype)

    def owner_total(which):
        wait_bytes(r3s[which].at[pl.ds(0, n_dp - 1)], gr.at[which, 2])
        total = own[which][...]
        for slot in range(n_dp):
            total = total + r3s[which][slot].astype(F32)
        return total

    def reduce_spread(which):
        total = owner_total(which)
        if which == 0:
            rows = pl.ds(pl.multiple_of(part * (BOTTLE // 4), BOTTLE // 4), BOTTLE // 4)
            total = total - fix[0, rows, :]
            for m in range(2):
                total = total - fix[1 + m, rows, :] * back_own[m]
        mine = final_part(which, core, half_y)
        mine[...] = total
        send_all(mine, gs.at[which, 3], gr.at[which, 3], rep_peers)

    def three_parts(which):
        if which == 0:
            return r1s[0].at[0, :, pl.ds(0, 3 * CHANNELS // n_dp)]
        return r1s[which].at[pl.ds(0, 3), 0] if which < 3 else y_part(which, r1s[which], 0).at[pl.ds(0, 3)]

    def reduce_end(which):
        wait_bytes(three_parts(which), gr.at[which, 3])

    gather_end(0)
    red[...] = jnp.dot(x_v[...], fw1[...].reshape(CHANNELS, BOTTLE), preferred_element_type=F32)

    def sums_of(ref, start, width):
        def body(row, carry):
            values = grouped(ref[pl.ds(row, CHUNK), start : start + width])
            return carry[0] + jnp.sum(values, axis=0), carry[1] + jnp.sum(values * values, axis=0)

        zero = jnp.zeros((8, width), F32)
        return over_rows(body, (zero, zero))

    def joined(found):
        both = [jnp.concatenate(item, axis=1) for item in zip(*found)]
        return fold_lanes(stack_sums(micro_sum(both[0]), micro_sum(both[1])))

    def both_sums(name):
        return unstack_sums(unfold_lanes(sum_end(name)))

    sum_start("reduced", joined([sums_of(red, 0, 256)]))
    gather_out(2)
    gather_out(3)

    gy_copy.wait()
    to_rows(gy4, gy_v)
    wait_bytes(np_slots.at[pl.ds(0, n_dp - 1)], np_sems.at[1])
    np_full[...] = jnp.zeros(np_full.shape, F32)
    for d in range(n_dp):
        at = shard * d // 128
        np_full[at : at + 8, :] = np_full[at : at + 8, :] + np_slots[d]

    def vector(at, width):
        rows = [np_full[at // 128 + k : at // 128 + k + 1, :] for k in range(width // 128)]
        return jnp.concatenate(rows, axis=1) if len(rows) > 1 else rows[0]

    gain_one, bias_one = vector(0, 256), vector(256, 256)
    gain_two, bias_two = vector(512, 512), vector(1024, 512)
    gain_pool, bias_pool = vector(1536, 128), vector(1664, 128)
    bias_expand = vector(1792, 512)
    gain_three, bias_three = vector(2304, 1024), vector(3328, 1024)

    total, square = both_sums("reduced")
    center1, scale1, mul1, add1 = norm_terms(total, square, gain_one, bias_one, pixels)

    def make_active(row, carry):
        turned = grouped(red[pl.ds(row, CHUNK), :]) * mul1 + add1
        act[1, pl.ds(PAD + row, CHUNK), :] = flat(turned * sigmoid(turned))
        return carry

    over_rows(make_active, 0)
    gather_hand(1)
    gather_turn(2)
    place = lax.rem(lax.broadcasted_iota(jnp.int32, (CHUNK, BOTTLE), 0) // 4, SIDE)
    not_last = place != SIDE - 1
    not_first = place != 0

    def beside(side, row, distance, lanes=slice(0, BOTTLE)):
        near = act[side, pl.ds(PAD + row - 8, CHUNK + 16), lanes]
        return pltpu.roll(near, (CHUNK + 16 - distance) % (CHUNK + 16), 0)[8 : 8 + CHUNK]

    def shift_active(row, carry):
        act[2, pl.ds(PAD + row, CHUNK), :] = jnp.where(not_last, beside(1, row, 4), 0.0)
        act[0, pl.ds(PAD + row, CHUNK), :] = jnp.where(not_first, beside(1, row, -4), 0.0)
        return carry

    over_rows(shift_active, 0)

    def make_columns(row, carry):
        for tap in range(9):
            down, side = tap // 3 - 1, tap % 3
            values = act[side, pl.ds(PAD + row + 56 * down, CHUNK), :].astype(BF16)
            columns[0, pl.ds(row, CHUNK), tap * 128 : tap * 128 + 128] = values[:, 0:128]
            columns[1, pl.ds(row, CHUNK), tap * 128 : tap * 128 + 128] = values[:, 128:256]
        return carry

    over_rows(make_columns, 0)
    gather_end(1)
    own_half = n_dp // 2

    def filters(group):
        return fwc[group * own_half : (group + 1) * own_half].reshape(9 * 128, BOTTLE)

    halves2 = (slice(0, 256), slice(256, 512))
    for group, lanes in enumerate(halves2):
        wid[:, lanes] = jnp.dot(columns[group], filters(group), preferred_element_type=F32)
        sum_start(f"widened{group}", joined([sums_of(wid, group * 256, 256)]))
    sum_turn("widened0")
    sum_turn("widened1")
    gather_hand(2)
    gather_turn(3)

    norm2 = []
    pooled = jnp.zeros((8, BOTTLE), F32)
    for group, lanes in enumerate(halves2):
        total, square = both_sums(f"widened{group}")
        norm2.append(norm_terms(total, square, gain_two[:, lanes], bias_two[:, lanes], pixels))
        m2, a2 = norm2[group][2:4]

        def make_splits(row, carry):
            turned = grouped(wid[pl.ds(row, CHUNK), lanes]) * m2 + a2
            values = turned * sigmoid(turned)
            splits[pl.ds(row, CHUNK), lanes] = flat(values)
            return carry + jnp.sum(values, axis=0)

        pooled = over_rows(make_splits, pooled)
    pooled = image_sum(pooled) * (1.0 / (SIDE * SIDE))
    gather_end(2)
    squeeze = fes[:, :, 0:128].reshape(BOTTLE, INNER)
    ex_both = fes[:, :, 128:384]
    expand = jnp.concatenate(
        [
            ex_both[:, 0:ex_rows].reshape(INNER, 256),
            ex_both[:, ex_rows : 2 * ex_rows].reshape(INNER, 256),
        ],
        axis=1,
    )
    pre_pool = exact_dot(pooled, squeeze, False)
    sum_start("pool", stack_sums(pair_sum(pre_pool), pair_sum(pre_pool * pre_pool)))
    gather_hand(3)

    first_micro = lax.rem(row_ids(BOTTLE), 4) < 2

    def make_normed(row, carry):
        rows = pl.ds(row, CHUNK)
        normed = (grouped(red[rows, :]) - center1) * scale1
        dwid[rows, 0:256] = flat(jnp.where(first_micro, normed, 0.0)).astype(BF16)
        dwid[rows, 256:512] = flat(jnp.where(first_micro, 0.0, normed)).astype(BF16)
        return carry + jnp.sum(grouped(x_v[rows, :].astype(F32)), axis=0)

    image_sums = micro_sum(over_rows(make_normed, jnp.zeros((8, CHANNELS), F32)))
    sum_start(
        "images",
        jnp.concatenate(
            [
                image_sums[2 * m : 2 * m + 1, at : at + 128]
                for m in range(2)
                for at in range(0, CHANNELS, 128)
            ],
            axis=0,
        ),
    )
    normed_images = tdot(dwid[...], x_v[...]).astype(BF16)
    normed_images = normed_images.reshape(2, 2, 2, BOTTLE // 4, CHANNELS)
    for m in range(2):
        gb[:, :, m * (BOTTLE // 4) : (m + 1) * (BOTTLE // 4)] = normed_images[m]
    reduce_core(5)
    total, square = unstack_sums(sum_end("pool"))
    center_p, scale_p, mul_p, add_p = norm_terms(total, square, gain_pool, bias_pool, pictures)
    normed_p = (pre_pool - center_p) * scale_p
    norm_p = pre_pool * mul_p + add_p
    gate_p = sigmoid(norm_p)
    hidden = norm_p * gate_p
    slope_p = gate_p * (1.0 + norm_p * (1.0 - gate_p))
    logits = exact_dot(hidden, expand, False) + bias_expand
    left, right = logits[:, 0:256], logits[:, 256:512]
    most = jnp.maximum(left, right)
    left, right = jnp.exp(left - most), jnp.exp(right - most)
    att0 = left / (left + right)
    att1 = right / (left + right)

    gather_end(3)
    last = fw3[...].reshape(BOTTLE, CHANNELS)
    def make_mixed(row, carry):
        rows = pl.ds(row, CHUNK)
        values = grouped(splits[rows, 0:256]) * att0 + grouped(splits[rows, 256:512]) * att1
        mixed[rows, :] = flat(values).astype(BF16)
        return carry

    over_rows(make_mixed, 0)
    halves3 = (slice(0, 512), slice(512, 1024))
    blocks3 = [[slice(512 * h + k, 512 * h + k + 256) for k in (0, 256)] for h in range(2)]
    for half, lanes in enumerate(halves3):
        proj[:, lanes] = jnp.dot(mixed[...], last[:, lanes], preferred_element_type=F32)
        sum_start(
            f"projected{half}", joined([sums_of(proj, 512 * half + k, 256) for k in (0, 256)])
        )
    sum_turn("projected0")
    sum_turn("projected1")
    sum_turn("images")
    reduce_y(5)

    norm3 = []
    zero = jnp.zeros((8, 256), F32)
    for half, lanes in enumerate(halves3):
        total, square = both_sums(f"projected{half}")
        norm3.append(norm_terms(total, square, gain_three[:, lanes], bias_three[:, lanes], pixels))
        found = []
        for k, block in enumerate(blocks3[half]):
            c3, s3, m3, a3 = (item[:, k * 256 : k * 256 + 256] for item in norm3[half])

            def make_out(row, carry):
                rows = pl.ds(row, CHUNK)
                values = grouped(proj[rows, block])
                summed = grouped(x_v[rows, block].astype(F32)) + (values * m3 + a3)
                gate = sigmoid(summed)
                bo4[pl.ds(row // 4, CHUNK // 4), :, block] = by_four(summed * gate).astype(BF16)
                upstream = grouped(gy_v[rows, block].astype(F32)) * (
                    gate * (1.0 + summed * (1.0 - gate))
                )
                up[rows, block] = flat(upstream)
                normed = (values - c3) * s3
                return carry[0] + jnp.sum(upstream, axis=0), carry[1] + jnp.sum(
                    upstream * normed, axis=0
                )

            found.append(over_rows(make_out, (zero, zero)))
        sum_start(f"back_projected{half}", joined(found))
    bo_copy = pltpu.make_async_copy(bo4, bo_hbm, local_sem.at[2])
    bo_copy.start()

    def write_norm(at, pattern):
        at = at // 128
        both = pattern[0:1, :] + pattern[2:3, :]
        for k in range(both.shape[1] // 128):
            np_full[at + k : at + k + 1, :] = both[:, k * 128 : k * 128 + 128]

    sum_turn("back_projected0")
    sum_turn("back_projected1")
    reduce_owner(5)

    for half, lanes in enumerate(halves3):
        bias_sum, gain_sum = both_sums(f"back_projected{half}")
        write_norm(2304 + 512 * half, gain_sum)
        write_norm(3328 + 512 * half, bias_sum)
        by_value, constant = back_terms(*norm3[half][0:3], bias_sum, gain_sum, pixels)
        for k, block in enumerate(blocks3[half]):
            m3, v3, k3 = (
                item[:, k * 256 : k * 256 + 256] for item in (norm3[half][2], by_value, constant)
            )

            def make_dproj(row, carry):
                rows = pl.ds(row, CHUNK)
                values = grouped(up[rows, block]) * m3 + grouped(proj[rows, block]) * v3 + k3
                dproj[rows, block] = flat(values).astype(BF16)
                return carry

            over_rows(make_dproj, 0)
        part_mixed = dot_t(dproj[:, lanes], last[:, lanes])
        d_mixed[...] = part_mixed if half == 0 else d_mixed[...] + part_mixed

    def attend(row, carry):
        rows = pl.ds(row, CHUNK)
        values = grouped(d_mixed[rows, :])
        return (
            carry[0] + jnp.sum(values * grouped(splits[rows, 0:256]), axis=0),
            carry[1] + jnp.sum(values * grouped(splits[rows, 256:512]), axis=0),
        )

    d_att0, d_att1 = over_rows(attend, (zero, zero))
    d_att0, d_att1 = image_sum(d_att0), image_sum(d_att1)
    both = att0 * d_att0 + att1 * d_att1
    d_logits = jnp.concatenate([att0 * (d_att0 - both), att1 * (d_att1 - both)], axis=1)
    d_hidden = exact_dot(d_logits, expand, True)
    d_pool = d_hidden * slope_p
    per_micro = stack_sums(pair_sum(d_pool), pair_sum(d_pool * normed_p))
    sum_start("back_pool", per_micro)
    ex_sum = pair_sum(d_logits)
    ex_sum = ex_sum + pltpu.roll(ex_sum, 2, 0)
    ex_rows_sum = ex_sum[:, 0:128]
    for k in range(1, 4):
        ex_rows_sum = jnp.where(row_ids(128) == k, ex_sum[:, k * 128 : k * 128 + 128], ex_rows_sum)

    grad_ex = image_dot(hidden, d_logits)
    grad_ex = grad_ex.reshape(n_dp, ex_rows, 512)
    ge[:, 0:ex_rows, 128:384] = grad_ex[:, :, 0:256]
    ge[:, ex_rows : 2 * ex_rows, 128:384] = grad_ex[:, :, 256:512]
    ge[:, :, 384:512] = jnp.zeros((n_dp, 2 * ex_rows, 128), F32)
    g3[...] = tdot(mixed[...], dproj[...]).reshape(g3.shape)
    reduce_core(3)
    held = []
    for group, att in ((0, att0), (1, att1)):
        lanes = halves2[group]
        c2, s2, m2, a2 = norm2[group]

        def make_dn2(row, carry):
            rows = pl.ds(row, CHUNK)
            values = grouped(wid[rows, lanes])
            turned = values * m2 + a2
            gate = sigmoid(turned)
            slope = gate * (1.0 + turned * (1.0 - gate))
            down = grouped(d_mixed[rows, :]) * att * slope
            dn2[rows, lanes] = flat(down)
            splits[rows, lanes] = flat(slope)
            normed = (values - c2) * s2
            terms = (down, down * normed, slope, slope * normed)
            return tuple(item + jnp.sum(term, axis=0) for item, term in zip(carry, terms))

        held.append([image_sum(item) for item in over_rows(make_dn2, (zero,) * 4)])
    pool_bias_sum, pool_gain_sum = unstack_sums(sum_end("back_pool"))
    write_norm(1536, pool_gain_sum)
    write_norm(1664, pool_bias_sum)
    d_pre_pool = mul_p * (
        d_pool - pool_bias_sum * (1.0 / pictures) - normed_p * (pool_gain_sum * (1.0 / pictures))
    )
    d_pooled = exact_dot(d_pre_pool, squeeze, True) * (1.0 / (SIDE * SIDE))
    for group in range(2):
        down, down_normed, slope, slope_normed = held[group]
        payload = fold_lanes(
            stack_sums(
                pair_sum(down + d_pooled * slope), pair_sum(down_normed + d_pooled * slope_normed)
            )
        )
        if group == 1:
            payload = jnp.concatenate([payload, ex_rows_sum], axis=0)
        sum_start(f"back_widened{group}", payload)
    ge[:, :, 0:128] = image_dot(pooled, d_pre_pool).reshape(n_dp, 2 * ex_rows, 128)
    reduce_core(4)
    sum_turn("back_widened0")
    sum_turn("back_widened1")
    reduce_y(3)
    reduce_y(4)
    back_total = owner_total(5)
    back_own[0] = back_total[0 : BOTTLE // 4]
    back_own[1] = back_total[BOTTLE // 4 :]

    small_zero = jnp.zeros((8, 128), F32)
    for group, lanes in enumerate(halves2):
        whole = sum_end(f"back_widened{group}")
        if group == 1:
            np_full[14:18, :] = whole[8:12]
        bias_sum, gain_sum = unstack_sums(unfold_lanes(whole[0:8]))
        write_norm(512 + 256 * group, gain_sum)
        write_norm(1024 + 256 * group, bias_sum)
        m2 = norm2[group][2]
        v2, k2 = back_terms(*norm2[group][0:3], bias_sum, gain_sum, pixels)
        pooled_m2 = d_pooled * m2

        def make_dwid(row, carry):
            rows = pl.ds(row, CHUNK)
            values = grouped(dn2[rows, lanes]) * m2 + grouped(splits[rows, lanes]) * pooled_m2
            values = values + grouped(wid[rows, lanes]) * v2 + k2
            dwid[rows, lanes] = flat(values).astype(BF16)
            return carry

        over_rows(make_dwid, 0)
        gc[group * own_half : (group + 1) * own_half] = tdot(
            columns[group], dwid[:, lanes]
        ).reshape(own_half, 2, 9 * 128 // own_half // 2, BOTTLE)
    reduce_core(1)
    reduce_core(2)
    for group, lanes in enumerate(halves2):
        dcol[PAD : PAD + ROWS, group * 1152 : group * 1152 + 1152] = dot_t(
            dwid[:, lanes], filters(group)
        )
        inner = slice(group * 128, group * 128 + 128)

        def gather_taps(row, carry):
            for side in range(3):
                total = None
                for down in range(3):
                    at = group * 1152 + (3 * down + side) * 128
                    values = dcol[pl.ds(PAD + row - 56 * (down - 1), CHUNK), at : at + 128]
                    total = values if total is None else total + values
                act[side, pl.ds(PAD + row, CHUNK), inner] = total
            return carry

        over_rows(gather_taps, 0)
        c1, s1, m1, a1 = (item[:, inner] for item in (center1, scale1, mul1, add1))
        not_first1, not_last1 = not_first[:, inner], not_last[:, inner]

        def make_dn1(row, carry):
            rows = pl.ds(row, CHUNK)
            d_active = act[1, pl.ds(PAD + row, CHUNK), inner]
            d_active = d_active + jnp.where(not_first1, beside(2, row, -4, inner), 0.0)
            d_active = d_active + jnp.where(not_last1, beside(0, row, 4, inner), 0.0)
            values = grouped(red[rows, inner])
            turned = values * m1 + a1
            gate = sigmoid(turned)
            slope = gate * (1.0 + turned * (1.0 - gate))
            down = grouped(d_active) * slope
            dn1[rows, inner] = flat(down)
            mixed[rows, inner] = flat(down * m1).astype(BF16)
            normed = (values - c1) * s1
            return carry[0] + jnp.sum(down, axis=0), carry[1] + jnp.sum(down * normed, axis=0)

        bias_sum, gain_sum = over_rows(make_dn1, (small_zero, small_zero))
        sum_start(f"back_reduced{group}", stack_sums(micro_sum(bias_sum), micro_sum(gain_sum)))
        if group == 0:
            reduce_owner(3)
            reduce_owner(4)
    reduce_y(1)
    reduce_y(2)
    sum_turn("back_reduced0")
    g1[...] = tdot(mixed[...], x_v[...]).reshape(g1.shape)
    reduce_core(0)
    sum_turn("back_reduced1")
    reduce_owner(1)
    reduce_y(0)
    reduce_owner(2)
    found = [unstack_sums(sum_end(f"back_reduced{group}")) for group in range(2)]
    bias_sum, gain_sum = (jnp.concatenate(item, axis=1) for item in zip(*found))
    write_norm(0, gain_sum)
    write_norm(256, bias_sum)
    by_value, constant = back_terms(center1, scale1, mul1, bias_sum, gain_sum, pixels)
    def make_dred(row, carry):
        rows = pl.ds(row, CHUNK)
        values = grouped(dn1[rows, :]) * mul1 + grouped(red[rows, :]) * by_value + constant
        dred[rows, :] = flat(values).astype(BF16)
        return carry

    over_rows(make_dred, 0)
    proj[...] = dot_t(dred[...], fw1[...].reshape(CHANNELS, BOTTLE))

    by_bias = mul1 * bias_sum * (1.0 / pixels)
    by_gain = mul1 * gain_sum * (1.0 / pixels)
    image_sums = sum_end("images")
    ids = lax.broadcasted_iota(jnp.int32, (16, 128), 0)
    own_sums = [
        jnp.sum(jnp.where(ids == m * n_dp + dp, image_sums, 0.0), axis=0, keepdims=True)
        for m in range(2)
    ]
    ids = row_ids(128)
    fix[0] = row_dot(by_bias, jnp.where(ids == 0, own_sums[0], jnp.where(ids == 2, own_sums[1], 0.0)))
    for m in range(2):
        fix[1 + m] = row_dot(by_gain, jnp.where(ids == 2 * m, 1.0, 0.0))
    reduce_spread(3)
    reduce_spread(4)
    reduce_owner(0)
    reduce_spread(1)

    def make_dx(row, carry):
        for start in range(0, CHANNELS, 256):
            lanes = slice(start, start + 256)
            values = up[pl.ds(row, CHUNK), lanes] + proj[pl.ds(row, CHUNK), lanes]
            dx4[pl.ds(row // 4, CHUNK // 4), :, lanes] = values.reshape(CHUNK // 4, 4, 256)
        return carry

    over_rows(make_dx, 0)
    dx_copy = pltpu.make_async_copy(dx4, dx_hbm, local_sem.at[3])
    dx_copy.start()
    norm_rows = np_full[0:8, :]
    for d in range(1, n_dp):
        at = shard * d // 128
        norm_rows = jnp.where(dp == d, np_full[at : at + 8, :], norm_rows)
    norm_rows = pltpu.roll(norm_rows, lax.rem(128 - turn, 128), 1)
    gn_out[...] = jnp.where(lanes_id < 128 - turn, norm_rows, pltpu.roll(norm_rows, 7, 0))
    reduce_spread(2)
    reduce_spread(0)
    out_copies = [
        pltpu.make_async_copy(source, target, local_sem.at[10 + k])
        for k, (source, target) in enumerate(
            (
                (gn_out, gn_hbm),
                (fs[2], f3_hbm),
                (fs[3], fe_hbm),
                (fs[1], fc_hbm),
                (fs[0], f1_hbm),
            )
        )
    ]
    out_copies[0].start()
    for which in (3, 4, 1, 2, 0):
        reduce_end(which)
        if which != 1:
            out_copies[{3: 1, 4: 2, 2: 3, 0: 4}[which]].start()

    bo_copy.wait()
    dx_copy.wait()
    for copy in out_copies:
        copy.wait()
    for k in STATS:
        if k in DIRECT:
            wait_bytes(ar_slots_a[k].at[pl.ds(0, everyone - 1)], ar_send_a.at[order[k]])
        else:
            wait_bytes(ar_slots_a[k].at[pl.ds(0, plane_size - 1)], ar_send_a.at[order[k]])
            wait_bytes(ar_slots_b[k].at[pl.ds(0, planes - 1)], ar_send_b.at[order[k]])
    wait_bytes(np_slots.at[pl.ds(0, n_dp - 1)], np_sems.at[0])
    for which in range(4):
        wait_bytes(seven(which), ws.at[which, 0])
        for stage in range(1, 4):
            wait_bytes(quarters[which](core, half_y), ws.at[which, stage])
    for which in range(6):
        wait_bytes(r1s[which], gs.at[which, 0])
        wait_bytes(r2s[which], gs.at[which, 1])
        wait_bytes(r3s[which].at[pl.ds(0, n_dp - 1)], gs.at[which, 2])
        if which < 5:
            wait_bytes(three_parts(which), gs.at[which, 3])


def update_kernel(*refs):
    sources, targets = refs[0:25], refs[25:45]
    inputs, outs, through = refs[45:68], refs[68:86], refs[86:88]
    pass_sems, in_sems, out_sems = refs[88:91]
    fetching, passing = [], []
    half = SIDE * SIDE // 2
    for number, (which, at, count) in enumerate(((1, 0, half), (1, half, half), (0, 0, 2 * half))):
        rows = pl.ds(at, count)
        fetching.append(
            pltpu.make_async_copy(
                sources[which].at[rows], through[which].at[rows], pass_sems.at[0, number]
            )
        )
        passing.append(
            pltpu.make_async_copy(
                through[which].at[rows], targets[which].at[rows], pass_sems.at[1, number]
            )
        )
    for copy in fetching:
        copy.start()
    coming = [
        pltpu.make_async_copy(source, held, in_sems.at[k])
        for k, (source, held) in enumerate(zip(sources[2:], inputs))
    ]
    for copy in coming:
        copy.start()
    grads, states = inputs[0:5], inputs[5:23]
    going = [
        pltpu.make_async_copy(held, target, out_sems.at[k])
        for k, (held, target) in enumerate(zip(outs, targets[2:]))
    ]
    ex_rows = states[9].shape[0]
    shard = states[15].shape[0]
    fans = (CHANNELS, 9 * BOTTLE // RADIX, BOTTLE, INNER // 8, BOTTLE)
    for copy in coming[0:5]:
        copy.wait()
    found = (
        grads[0][...].T,
        grads[1][...],
        grads[3][:, 0:128],
        jnp.concatenate([grads[3][0:ex_rows, 128:384], grads[3][ex_rows:, 128:384]], axis=1),
        grads[2][...],
    )
    for order, k in enumerate((3, 2, 4, 0, 1)):
        for copy in coming[5 + 3 * k : 8 + 3 * k]:
            copy.wait()
        new = adamw(
            states[3 * k][...],
            states[3 * k + 1][...],
            states[3 * k + 2][...],
            found[k],
            2.0 * fans[k] ** (-0.5),
            DECAY,
        )
        for j in range(3):
            outs[3 * k + j][...] = new[j]
            going[3 * k + j].start()
        if order < 3:
            fetching[order].wait()
            passing[order].start()
    for copy in coming[20:23]:
        copy.wait()
    for at in range(0, shard, 128):
        width = min(128, shard - at)
        lanes = pl.ds(at, width)
        new = adamw(
            *[states[15 + j][lanes].reshape(1, width) for j in range(3)],
            grads[4][at // 128 : at // 128 + 1, 0:width],
            NORM_RATE,
            0.0,
        )
        for j in range(3):
            outs[15 + j][lanes] = new[j].reshape(width)
    for copy in going[15:18]:
        copy.start()
    for copy in passing + going:
        copy.wait()


def fused_device(
    images,
    out_grad,
    reduce_weight,
    reduce_moment,
    reduce_second,
    conv_weight,
    conv_moment,
    conv_second,
    squeeze_weight,
    squeeze_moment,
    squeeze_second,
    expand_weight,
    expand_moment,
    expand_second,
    project_weight,
    project_moment,
    project_second,
    norm_params,
    norm_moment,
    norm_second,
):
    n_dp, n_rep = lax.axis_size("dp"), lax.axis_size("rep")
    by_pixel = lambda values: jnp.transpose(values, (1, 2, 0, 3)).reshape(-1, 4, CHANNELS)
    qc = conv_weight.shape[0] // 2
    q1 = reduce_weight.shape[0] // 4
    pe = squeeze_weight.shape[0]
    vmem = pltpu.VMEM
    pixel_form = (SIDE * SIDE, 4, CHANNELS)
    scratch = [
        *[
            vmem(values.shape, F32)
            for values in (
                reduce_weight,
                conv_weight,
                squeeze_weight,
                expand_weight,
                project_weight,
                norm_params,
            )
        ],
        vmem((8, 128), F32),
        vmem(pixel_form, BF16),
        vmem(pixel_form, BF16),
        vmem((ROWS, CHANNELS), BF16),
        vmem((ROWS, CHANNELS), BF16),
        vmem((n_dp, 2, 2, q1, BOTTLE), BF16),
        vmem((n_dp, 2, qc, BOTTLE), BF16),
        vmem((n_dp, pe, 512), BF16),
        vmem((n_dp, pe, CHANNELS), BF16),
        vmem((pe, 512), BF16),
        vmem((n_dp, 8, 128), F32),
        vmem((40, 128), F32),
        vmem((ROWS, BOTTLE), F32),
        vmem((3, ROWS + 2 * PAD, BOTTLE), F32),
        vmem((2, ROWS, 9 * 128), BF16),
        vmem((ROWS, 512), F32),
        vmem((ROWS, 512), F32),
        vmem((ROWS, BOTTLE), BF16),
        vmem((ROWS, CHANNELS), F32),
        vmem((ROWS, CHANNELS), F32),
        vmem(pixel_form, BF16),
        vmem(pixel_form, F32),
        vmem((ROWS, CHANNELS), BF16),
        vmem((ROWS, BOTTLE), F32),
        vmem((ROWS, 512), F32),
        vmem((ROWS, 512), BF16),
        vmem((ROWS + 2 * PAD, 2 * 9 * 128), F32),
        vmem((ROWS, BOTTLE), F32),
        vmem((ROWS, BOTTLE), BF16),
        vmem((2, 2, BOTTLE // 4, CHANNELS), F32),
        vmem((n_dp, 2, qc, BOTTLE), F32),
        vmem((n_dp, pe, CHANNELS), F32),
        vmem((n_dp, pe, 512), F32),
        vmem((2, 2, BOTTLE // 2, CHANNELS), BF16),
        vmem((3, BOTTLE, CHANNELS // n_dp), F32),
        vmem((2, BOTTLE // 4, CHANNELS // n_dp), F32),
    ]
    direct = n_dp * n_rep
    scratch += [
        vmem((direct if k in DIRECT else 2 * n_rep,) + shape, F32) for k, shape in STATS.items()
    ]
    scratch += [vmem((n_dp // 2,) + shape, F32) for shape in STATS.values()]
    cut = 64
    lanes1 = CHANNELS // n_dp
    half = [
        (2, BOTTLE // 4, CHANNELS),
        (n_dp, 2, cut, 128),
        (n_dp, 2, qc - cut, 128),
        (n_dp, pe, 512),
        (n_dp, pe, 256),
        (2, BOTTLE // 2, CHANNELS),
    ]
    quarter = [
        (BOTTLE // 4, CHANNELS),
        (n_dp, cut, 128),
        (n_dp, qc - cut, 128),
        (n_dp, pe, 256),
        (n_dp, pe, 128),
        (BOTTLE // 2, CHANNELS),
    ]
    final = [(2, 2, BOTTLE // 4, lanes1), (2, qc, BOTTLE), (pe, CHANNELS), (pe, 512)]
    sent = [BF16, BF16, BF16, BF16, F32, BF16]
    scratch += [vmem(shape, F32) for shape in half[:-1]] + [vmem(half[-1], BF16)]
    scratch += [vmem(shape, kind) for shape, kind in zip(quarter, sent)] * 3
    owned = [(BOTTLE // 4, lanes1)] + [shape[1:] for shape in quarter[1:-1]]
    owned += [(BOTTLE // 2, lanes1)]
    scratch += [vmem((n_dp,) + shape, kind) for shape, kind in zip(owned, sent)]
    scratch += [vmem(shape, F32) for shape in owned]
    scratch += [vmem(shape, F32) for shape in final]
    dma = pltpu.SemaphoreType.DMA
    scratch += [dma((15,))] + [dma((len(STATS),))] * 4 + [dma((2,))] + [dma((4, 4))] * 2 + [dma((6, 4))] * 2
    any_space = pl.BlockSpec(memory_space=pl.ANY)
    block_out, images_grad, sum1, sumc, sum3, sume, norm_grads = pl.pallas_call(
        functools.partial(block_kernel, n_dp, n_rep),
        out_shape=[
            jax.ShapeDtypeStruct(pixel_form, BF16),
            jax.ShapeDtypeStruct(pixel_form, F32),
            *[jax.ShapeDtypeStruct(shape, F32) for shape in final],
            jax.ShapeDtypeStruct((8, 128), F32),
        ],
        in_specs=[any_space] * 8,
        out_specs=[any_space] * 7,
        scratch_shapes=scratch,
        compiler_params=pltpu.CompilerParams(
            collective_id=0, has_side_effects=True, vmem_limit_bytes=63 * 1024 * 1024
        ),
    )(
        by_pixel(images),
        by_pixel(out_grad),
        reduce_weight,
        conv_weight,
        squeeze_weight,
        expand_weight,
        project_weight,
        norm_params,
    )
    states = (
        reduce_weight,
        reduce_moment,
        reduce_second,
        conv_weight,
        conv_moment,
        conv_second,
        squeeze_weight,
        squeeze_moment,
        squeeze_second,
        expand_weight,
        expand_moment,
        expand_second,
        project_weight,
        project_moment,
        project_second,
    )
    held = (*states, norm_params, norm_moment, norm_second)
    sums = (
        sum1.reshape(BOTTLE, lanes1),
        sumc.reshape(conv_weight.shape),
        sum3,
        sume,
        norm_grads,
    )
    block_out, images_grad, *updated = pl.pallas_call(
        update_kernel,
        out_shape=[
            jax.ShapeDtypeStruct(pixel_form, BF16),
            jax.ShapeDtypeStruct(pixel_form, F32),
            *[jax.ShapeDtypeStruct(state.shape, F32) for state in held],
        ],
        in_specs=[any_space] * 25,
        out_specs=[any_space] * 20,
        scratch_shapes=[vmem(values.shape, F32) for values in (*sums, *held, *held)]
        + [vmem(pixel_form, BF16), vmem(pixel_form, F32)]
        + [dma((2, 3)), dma((23,)), dma((18,))],
        compiler_params=pltpu.CompilerParams(vmem_limit_bytes=63 * 1024 * 1024),
    )(block_out, images_grad, *sums, *held)
    by_image = lambda values: jnp.transpose(
        values.reshape(SIDE, SIDE, images.shape[0], CHANNELS), (2, 0, 1, 3)
    )
    return (
        by_image(block_out),
        by_image(images_grad),
        *updated,
    )


def solution(mesh):
    placed = (
        P(("dp", "rep"), None, None, None),
        P(("dp", "rep"), None, None, None),
        P("dp", None),
        P("dp", None),
        P("dp", None),
        P("dp", None),
        P("dp", None),
        P("dp", None),
        P("dp", None),
        P("dp", None),
        P("dp", None),
        P("dp", None),
        P("dp", None),
        P("dp", None),
        P("dp", None),
        P("dp", None),
        P("dp", None),
        P("dp"),
        P("dp"),
        P("dp"),
    )
    n_dp, n_rep = mesh.shape["dp"], mesh.shape["rep"]
    whole_tiles = n_rep == 4 and n_dp % 2 == 0 and INNER % (16 * n_dp) == 0
    return jax.shard_map(
        fused_device if whole_tiles else per_device,
        mesh=mesh,
        in_specs=placed,
        out_specs=(
            P(("dp", "rep"), None, None, None),
            P(("dp", "rep"), None, None, None),
            P("dp", None),
            P("dp", None),
            P("dp", None),
            P("dp", None),
            P("dp", None),
            P("dp", None),
            P("dp", None),
            P("dp", None),
            P("dp", None),
            P("dp", None),
            P("dp", None),
            P("dp", None),
            P("dp", None),
            P("dp", None),
            P("dp", None),
            P("dp"),
            P("dp"),
            P("dp"),
        ),
        check_vma=False,
    )
```
